128 devices in a mesh: dp: 32 (over x, z, y_hi), tensor: 4 (over y_lo, core).
Axes of the slice: x: 4, y: 4 (y_hi: 2, y_lo: 2; y = y_hi * 2 + y_lo), z: 4, core: 2. Of those that a mesh axis runs over, the one named last changes fastest.
Arguments:
- hidden_in: bfloat16 [32768, 1024], P(('dp', 'tensor')), may hold values from -6 to 6
- out_grad: bfloat16 [32768, 1024], P(('dp', 'tensor')), may hold values from -6 to 6
- attn_gain: bfloat16 [1024], P('dp'), may hold values from 0.5 to 1.5
- query_weight: bfloat16 [1024, 1024], P('dp', 'tensor'), may hold values from -0.1875 to 0.1875
- key_weight: bfloat16 [1024, 512], P('dp', 'tensor'), may hold values from -0.1875 to 0.1875
- value_weight: bfloat16 [1024, 512], P('dp', 'tensor'), may hold values from -0.1875 to 0.1875
- output_weight: bfloat16 [1024, 1024], P('dp', 'tensor'), may hold values from -1.5 to 1.5
- moe_gain: bfloat16 [1024], P('dp'), may hold values from 0.5 to 1.5
- router_weight: bfloat16 [1024, 32], P('dp'), may hold values from -0.09375 to 0.09375
- expert_gate: bfloat16 [32, 1024, 512], P(None, 'dp', 'tensor'), may hold values from -0.1875 to 0.1875
- expert_up: bfloat16 [32, 1024, 512], P(None, 'dp', 'tensor'), may hold values from -0.1875 to 0.1875
- expert_down: bfloat16 [32, 1024, 512], P(None, 'dp', 'tensor'), may hold values from -1 to 1
- expert_ids: int32 [32768, 8], P(('dp', 'tensor')), may hold values from 0 to 31, all different within a row; in each aligned block of 1024 rows (0 to 1023, 1024 to 2047, ...) at most 320 rows name the same one
- segment_ids: int32 [32768], P(('dp', 'tensor')), may hold values from 0 to 3, as said below
Outputs:
- block_out: bfloat16 [32768, 1024], P(('dp', 'tensor'))
- hidden_grad: float32 [32768, 1024], P(('dp', 'tensor'))
- attn_gain_grad: float32 [1024], P('dp')
- query_grad: float32 [1024, 1024], P('dp', 'tensor')
- key_grad: float32 [1024, 512], P('dp', 'tensor')
- value_grad: float32 [1024, 512], P('dp', 'tensor')
- output_grad: float32 [1024, 1024], P('dp', 'tensor')
- moe_gain_grad: float32 [1024], P('dp')
- router_grad: float32 [1024, 32], P('dp')
- expert_gate_grad: float32 [32, 1024, 512], P(None, 'dp', 'tensor')
- expert_up_grad: float32 [32, 1024, 512], P(None, 'dp', 'tensor')
- expert_down_grad: float32 [32, 1024, 512], P(None, 'dp', 'tensor')
The draws below stay inside these ranges and needn't reach their ends.
Inputs may be any that keep to these rules, and one draw needn't show every extreme that they name: `expert_ids`: each row names 8 different experts. Within the rows of one sequence no expert is named by more than 320 rows, and in some sequence some expert is named by exactly 320. `segment_ids`: each sequence of 1024 tokens holds four documents numbered 0, 1, 2, 3, never falling, each of one token or more; document 1 begins in the first quarter of its sequence and ends in the last quarter.
All inputs are finite; a program needn't handle non-finite values.
Results may differ from the reference program's by a relative error of at most 0.028.
Values may be sent and summed in bfloat16 or wider, within the bound.
A program may use at most 320 MiB of HBM per device.

```python
import math
import jax
import jax.numpy as jnp
import numpy as np
from jax import lax

D = 1024
H = 16
KV = 8
HD = 64
FF = 512
E = 32
TOPK = 8
SEQ_LEN = 1024
TOKENS = 32768
CAP = 320


def draw_segment_ids(key, part):
    key = jax.random.fold_in(key, 11)
    length = SEQ_LEN
    sequences = TOKENS // SEQ_LEN
    first_key, second_key, third_key = jax.random.split(key, 3)
    opening = jax.random.randint(first_key, (sequences,), 1, length // 8 + 1)
    closing = length - length // 8 - jax.random.randint(second_key, (sequences,), 0, length // 16 + 1)
    last_start = closing + 1 + jax.random.randint(third_key, (sequences,), 0, length - closing - 1)
    positions = jnp.arange(length)[None, :]
    numbers = (positions >= opening[:, None]).astype(jnp.int32) + (positions >= closing[:, None]).astype(jnp.int32) + (positions >= last_start[:, None]).astype(jnp.int32)
    return numbers.reshape(TOKENS).astype(jnp.int32)


def block_scale(own_key, extent, cuts, low, high):
    gain = 1.0
    for position, blocks in cuts:
        draws = jax.random.uniform(jax.random.fold_in(jax.random.fold_in(own_key, 6), position), (blocks,), jnp.float32, low / len(cuts), high / len(cuts))
        gain = gain * jnp.repeat(jnp.exp(draws), extent[position] // blocks).reshape((-1,) + (1,) * (len(extent) - 1 - position))
    return gain


def assign_block(own_key, own, number, rows, count, top, most, slope):
    order = jax.random.permutation(own_key, count)
    crowded, ordinary = load_shares(count, rows * top, most, slope, True), load_shares(count, rows * top, most, slope, False)
    places = jnp.arange(count)

    def named(sizes, turn):
        used = int((sizes > 0).sum())
        fixed = max(1, used // 4)
        moved = fixed + (places - fixed + turn * (used - fixed)) % max(1, count - fixed)
        return jnp.zeros((count,), jnp.int32).at[order[jnp.where(places < fixed, places, moved)]].set(jnp.asarray(sizes, jnp.int32))

    sizes = jnp.where(number % 4 == 0, named(crowded, number // 4), named(ordinary, number - number // 4 - 1))
    mixed = jax.random.permutation(jax.random.fold_in(own, 3), count)
    source_of, receiver = mixed[0:count // 2 * 2:2], mixed[1:count // 2 * 2:2]
    slack = jnp.minimum(sizes[source_of] - 1, most - sizes[receiver]) // 2
    slack = jnp.where((source_of == order[0]) | (receiver == order[0]) | (sizes[receiver] == 0), 0, jnp.maximum(slack, 0))
    moved = jax.random.randint(jax.random.fold_in(own, 4), (count // 2,), 0, 1 << 20) % (slack + 1)
    sizes = sizes.at[source_of].add(-moved).at[receiver].add(moved)
    labels = jnp.searchsorted(jnp.cumsum(sizes), jnp.arange(rows * top), side="right").astype(jnp.int32)
    listing = labels.reshape(top, rows).T
    listing = listing[jax.random.permutation(jax.random.fold_in(own, 1), rows)]
    turn = jax.random.randint(jax.random.fold_in(own, 2), (rows, 1), 0, top)
    return jnp.take_along_axis(listing, (jnp.arange(top)[None, :] + turn) % top, axis=1)


def load_shares(number_of, total, most, slope, full):
    loads = [(1 << 20) // math.isqrt(grade ** slope) + 1 for grade in range(1, number_of + 1)]
    largest = most if full else min(most, max(-(-total // number_of), total * loads[0] // sum(loads)))
    least = 1 if total - largest >= number_of - 1 else 0
    given, surplus = [largest] + [least] * (number_of - 1), total - largest - least * (number_of - 1)
    while surplus > 0:
        candidates = [i for i in range(1, number_of) if given[i] < largest] or [i for i in range(1, number_of) if given[i] < most]
        whole, budget = sum([loads[i] for i in candidates]), surplus
        for i in candidates:
            extra = min(most - given[i], max(1, budget * loads[i] // whole), surplus)
            given[i] = given[i] + extra
            surplus = surplus - extra
    return np.array(given)


def centred(own_key, dims, spread, bound, cuts=(), kind=jnp.bfloat16):
    factor_of = block_scale(own_key, dims, cuts, -0.22, 0.18) if cuts else 1.0
    entries = jax.random.normal(own_key, dims, jnp.float32) * spread * factor_of
    return jnp.minimum(jnp.maximum(entries, -bound), bound).astype(kind)


def setup_inputs(seed: int = 0) -> dict:
    streams_of = jax.random.split(jax.random.key(seed), 15)
    hidden_in = centred(streams_of[0], (TOKENS, D), 1.0, 6.0, ((0, 128),))
    out_grad = centred(streams_of[1], (TOKENS, D), 1.0, 6.0, ((0, 128),))
    attn_gain = jnp.clip(1.0 + 0.1 * jax.random.normal(streams_of[2], (D,), jnp.float32), 0.5, 1.5).astype(jnp.bfloat16)
    query_weight = centred(streams_of[3], (D, H * HD), D ** -0.5, 0.1875, ((0, 32), (1, 4)))
    key_weight = centred(streams_of[4], (D, KV * HD), D ** -0.5, 0.1875, ((0, 32), (1, 4)))
    value_weight = centred(streams_of[5], (D, KV * HD), D ** -0.5, 0.1875, ((0, 32), (1, 4)))
    output_weight = centred(streams_of[6], (D, H * HD), (H * HD // 64) ** -0.5, 1.5, ((0, 32), (1, 4)))
    moe_gain = jnp.clip(1.0 + 0.1 * jax.random.normal(streams_of[7], (D,), jnp.float32), 0.5, 1.5).astype(jnp.bfloat16)
    router_weight = centred(streams_of[8], (D, E), (4 * D) ** -0.5, 0.09375, ((0, 32),))
    expert_gate = centred(streams_of[9], (E, D, FF), D ** -0.5, 0.1875, ((1, 32), (2, 4)))
    expert_up = centred(streams_of[10], (E, D, FF), D ** -0.5, 0.1875, ((1, 32), (2, 4)))
    expert_down = centred(streams_of[11], (E, D, FF), (FF // 16) ** -0.5, 1.0, ((1, 32), (2, 4)))
    expert_ids_keys = jax.random.split(jax.random.fold_in(streams_of[12], 1), TOKENS // SEQ_LEN)
    expert_ids_turns = jax.random.permutation(jax.random.fold_in(streams_of[12], 3), TOKENS // SEQ_LEN)
    expert_ids = jax.vmap(lambda own, number: assign_block(jax.random.fold_in(streams_of[12], 2), own, number, SEQ_LEN, E, TOPK, CAP, 1))(expert_ids_keys, expert_ids_turns).reshape((TOKENS, TOPK))
    segment_ids = draw_segment_ids(jax.random.fold_in(streams_of[14], 71), 0)
    return dict(hidden_in=hidden_in, out_grad=out_grad, attn_gain=attn_gain, query_weight=query_weight, key_weight=key_weight, value_weight=value_weight, output_weight=output_weight, moe_gain=moe_gain, router_weight=router_weight, expert_gate=expert_gate, expert_up=expert_up, expert_down=expert_down, expert_ids=expert_ids, segment_ids=segment_ids)


@jax.custom_vjp
def low(v):
    return lax.optimization_barrier(v.astype(jnp.bfloat16)).astype(jnp.float32)

@jax.custom_vjp
def low_back(v):
    return v

def low_keep(v):
    return (low(v), None)

def low_pass(kept, grad):
    return (grad,)

def back_keep(v):
    return (v, None)

def back_low(kept, grad):
    return (low(grad),)
low.defvjp(low_keep, low_pass)
low_back.defvjp(back_keep, back_low)
epsilon = 1e-06
masked_score = -1e+30
highest = lax.Precision.HIGHEST

def matmul(operand, matrix):
    return jnp.dot(operand, matrix, precision=highest, preferred_element_type=jnp.float32)

def rms_scale(values):
    return lax.rsqrt(lax.optimization_barrier(jnp.mean(values * values, axis=-1, keepdims=True)) + epsilon)

def rotary_tables(length):
    half_dim = HD // 2
    inverse = 10000.0 ** (-(jnp.arange(half_dim).astype(jnp.float32) * 2.0) / HD)
    angles = jnp.arange(length).astype(jnp.float32)[:, None] * inverse[None, :]
    return (jnp.cos(angles)[:, None, :], jnp.sin(angles)[:, None, :])

def rotate(values, cosine_table, sine_table):
    half_dim = HD // 2
    leading = values[..., :half_dim]
    trailing = values[..., half_dim:]
    return jnp.concatenate([leading * cosine_table - trailing * sine_table, trailing * cosine_table + leading * sine_table], axis=-1)

def expert_slots(routes):
    flat_ids = routes.reshape(-1).astype(jnp.int32)
    assignments = flat_ids.shape[0]
    sorted_order = jnp.argsort(flat_ids, stable=True).astype(jnp.int32)
    picked = (flat_ids[:, None] == jnp.arange(E).astype(jnp.int32)[None, :]).astype(jnp.int32)
    counts = lax.optimization_barrier(jnp.sum(picked, axis=0)).astype(jnp.int32)
    starts = (jnp.cumsum(counts) - counts).astype(jnp.int32)
    sorted_ids = flat_ids[sorted_order]
    slot_sorted = jnp.arange(assignments).astype(jnp.int32) - starts[sorted_ids]
    slot_ranks = jnp.zeros((assignments,), jnp.int32).at[sorted_order].set(slot_sorted)
    return (flat_ids * CAP + slot_ranks).astype(jnp.int32)

def sequence_forward(hidden, segments, routes, weights):
    attn_gain, query_weight, key_weight, value_weight, output_weight, moe_gain, router_weight, expert_gate, expert_up, expert_down = weights
    length = hidden.shape[0]
    group_size = H // KV
    normed = low(hidden * rms_scale(hidden) * attn_gain)
    cosine_table, sine_table = rotary_tables(length)
    queries = low_back(matmul(normed, query_weight)).reshape(length, H, HD)
    queries = low(rotate(queries, cosine_table, sine_table)).reshape(length, KV, group_size, HD)
    key_rot = low_back(matmul(normed, key_weight)).reshape(length, KV, HD)
    key_rot = low(rotate(key_rot, cosine_table, sine_table))
    values = low(low_back(matmul(normed, value_weight))).reshape(length, KV, HD)
    block_rows = min(512, length)
    block_count = length // block_rows
    positions = jnp.arange(length).astype(jnp.int32)

    def attend(pieces):
        query_block, segment_block, position_block = pieces
        scores = jnp.einsum('qgrd,kgd->grqk', query_block, key_rot, precision=highest) * HD ** (-0.5)
        scores = low_back(scores)
        allowed = (segment_block[:, None] == segments[None, :]) & (position_block[:, None] >= positions[None, :])
        scores = jnp.where(allowed, scores, masked_score)
        row_max = lax.optimization_barrier(jnp.max(scores, axis=-1, keepdims=True))
        exponent = jnp.exp(scores - row_max)
        softmax_out = exponent / lax.optimization_barrier(jnp.sum(exponent, axis=-1, keepdims=True))
        context = jnp.einsum('grqk,kgd->qgrd', low(softmax_out), values, precision=highest)
        return context.reshape(block_rows, H * HD)
    contexts = lax.map(jax.checkpoint(attend), (queries.reshape(block_count, block_rows, KV, group_size, HD), segments.reshape(block_count, block_rows), positions.reshape(block_count, block_rows)))
    context = low(low_back(contexts.reshape(length, H * HD)))
    attention_out = low_back(matmul(context, output_weight.T))
    middle = hidden + attention_out
    normed_moe = low(middle * rms_scale(middle) * moe_gain)
    logits = low_back(matmul(normed_moe, router_weight))
    chosen = jnp.take_along_axis(logits, routes, axis=1)
    gating = jax.nn.softmax(chosen, axis=-1)
    destination = expert_slots(routes)
    owners = (jnp.arange(length * TOPK) // TOPK).astype(jnp.int32)
    source = jnp.full((E * CAP,), length, jnp.int32).at[destination].set(owners)
    expert_in = jnp.take(normed_moe, source, axis=0, mode='fill', fill_value=0.0).reshape(E, CAP, D)
    gate_pre = low_back(jnp.einsum('ecd,edf->ecf', expert_in, expert_gate, precision=highest))
    up_pre = low_back(jnp.einsum('ecd,edf->ecf', expert_in, expert_up, precision=highest))
    activation = low(jax.nn.silu(gate_pre) * up_pre)
    expert_out = low_back(jnp.einsum('ecf,edf->ecd', activation, expert_down, precision=highest))
    picked_rows = expert_out.reshape(E * CAP, D)[destination].reshape(length, TOPK, D)
    mixture = lax.optimization_barrier(jnp.sum(gating[:, :, None] * picked_rows, axis=1))
    return middle + mixture

def reference(hidden_in, out_grad, attn_gain, query_weight, key_weight, value_weight, output_weight, moe_gain, router_weight, expert_gate, expert_up, expert_down, expert_ids, segment_ids):
    weights = tuple((weight_in.astype(jnp.float32) for weight_in in (attn_gain, query_weight, key_weight, value_weight, output_weight, moe_gain, router_weight, expert_gate, expert_up, expert_down)))
    sequences = TOKENS // SEQ_LEN
    per_step = max(1, min(sequences, 4096 // SEQ_LEN))
    steps_count = sequences // per_step

    def shaped(source_array, trailing):
        return source_array.reshape((steps_count, per_step, SEQ_LEN) + trailing)
    inputs = (shaped(hidden_in.astype(jnp.float32), (D,)), shaped(out_grad.astype(jnp.float32), (D,)), shaped(segment_ids, ()), shaped(expert_ids, (TOPK,)))

    def group_step(totals, pieces):
        hidden_part, grad_part, segment_part, route_part = pieces

        def forward(hidden_arg, weight_arg):
            return jax.vmap(sequence_forward, in_axes=(0, 0, 0, None))(hidden_arg, segment_part, route_part, weight_arg)
        output, pullback = jax.vjp(forward, hidden_part, weights)
        hidden_grad, weight_grads = pullback(grad_part)
        totals = jax.tree.map(lambda running, update: running + update, totals, weight_grads)
        return (totals, (output.astype(jnp.bfloat16), hidden_grad))
    zero_grads = jax.tree.map(jnp.zeros_like, weights)
    totals, (output, hidden_grad) = lax.scan(group_step, zero_grads, inputs)
    return (output.reshape(TOKENS, D), hidden_grad.reshape(TOKENS, D), totals[0], totals[1], totals[2], totals[3], totals[4], totals[5], totals[6], totals[7], totals[8], totals[9])
```

```python
import functools

import jax
import jax.numpy as jnp
import numpy as np
from jax import lax
from jax.experimental import pallas as pl
from jax.experimental.pallas import tpu as pltpu
from jax.sharding import Mesh
from jax.sharding import PartitionSpec as P

D = 1024
HD = 64
E = 32
SEQ = 1024
LOCAL = 256
HEADS = 4
QUAD = 4
FF = 128
F = QUAD * FF
EPS = 1e-06
MASKED = -1e30
BLOCK = 256
TOKENS = 2048
STEPS = 4

DP = ("x", "z", "yh")
TENSOR = ("yl", "core")
RING = ("yh", "yl", "core")
PLANE = ("x", "z")
ALL = ("x", "z", "yh", "yl", "core")

F32 = jnp.float32
BF = jnp.bfloat16
LAST = (((1,), (1,)), ((), ()))
MIB = 1024 * 1024
MESH = pl.DeviceIdType.MESH
SMALL = 896


def mm(a, b):
    return jnp.dot(a, b, preferred_element_type=F32)


def mm_last(a, b):
    return lax.dot_general(a, b, LAST, preferred_element_type=F32)


class Place:
    def __init__(self):
        self.x = lax.axis_index("x")
        self.z = lax.axis_index("z")
        self.yh = lax.axis_index("yh")
        self.yl = lax.axis_index("yl")
        self.core = lax.axis_index("core")
        self.y = self.yh * 2 + self.yl

    def chip(self, k):
        return lax.rem(self.y + k, 4)

    def ring(self, k):
        chip = self.chip(k)
        return {"yh": chip // 2, "yl": lax.rem(chip, 2)}

    def along(self, axis, k):
        return {axis: lax.rem(getattr(self, axis) + k, 4)}

    def sibling(self):
        return {"core": 1 - self.core}

    def partner(self):
        return {"yl": 1 - self.yl}

    def diagonal(self):
        return {"yl": 1 - self.yl, "core": 1 - self.core}

    def opposite(self):
        return {"yh": 1 - self.yh}


def greet(devices):
    barrier = pltpu.get_barrier_semaphore()
    for device in devices:
        pl.semaphore_signal(barrier, inc=1, device_id=device, device_id_type=MESH)
    pl.semaphore_wait(barrier, len(devices))


def push(src, dst, send, recv, i, device):
    copy = pltpu.make_async_remote_copy(
        src_ref=src, dst_ref=dst, send_sem=send.at[i], recv_sem=recv.at[i],
        device_id=device, device_id_type=MESH,
    )
    copy.start()
    return copy


def keep(src, dst, sem):
    copy = pltpu.make_async_copy(src, dst, sem)
    copy.start()
    return copy


class RingGather:
    def __init__(self, at, own, out, send, recv, here, base=0):
        self.at, self.out, self.send, self.recv, self.base = at, out, send, recv, base
        self.half = own.shape[0] // 2
        me = out.at[self.slot(0)]
        self.kept = keep(own, me, here)
        self.copies = {}
        self.go(1, own, me, at.ring(1))
        self.go(2, own, me, at.ring(3))
        self.go(0, own, me, at.sibling())

    def slot(self, k):
        return self.at.chip(k) * 2 + self.at.core

    def go(self, i, src, dst, device):
        self.copies[i] = push(src, dst, self.send, self.recv, self.base + i, device)

    def pass_on(self, i, view, device):
        self.go(i, view, view, device)

    def forward(self):
        lo, hi = pl.ds(0, self.half), pl.ds(self.half, self.half)
        self.copies[1].wait_recv()
        self.pass_on(3, self.out.at[self.slot(3), lo], self.at.ring(1))
        self.pass_on(4, self.out.at[self.slot(3)], self.at.sibling())
        self.copies[2].wait_recv()
        self.pass_on(5, self.out.at[self.slot(1), hi], self.at.ring(3))
        self.pass_on(6, self.out.at[self.slot(1)], self.at.sibling())

    def forward_far(self):
        lo, hi = pl.ds(0, self.half), pl.ds(self.half, self.half)
        self.copies[3].wait_recv()
        self.pass_on(7, self.out.at[self.slot(2), lo], self.at.sibling())
        self.copies[5].wait_recv()
        self.pass_on(8, self.out.at[self.slot(2), hi], self.at.sibling())

    def finish(self):
        for i in (0, 4, 6, 7, 8):
            self.copies[i].wait_recv()
        for i in range(9):
            self.copies[i].wait_send()
        self.kept.wait()


def gather_ring_kernel(count, *refs):
    owns, outs = refs[:count], refs[count : 2 * count]
    send, recv, here = refs[2 * count :]
    at = Place()
    greet([at.sibling(), at.ring(1), at.ring(3)])
    gathers = [
        RingGather(at, own, out, send, recv, here.at[i], 9 * i)
        for i, (own, out) in enumerate(zip(owns, outs))
    ]
    for gather in gathers:
        gather.forward()
    for gather in gathers:
        gather.forward_far()
    for gather in gathers:
        gather.finish()


def gather_ring(owns, ident):
    count = len(owns)
    hbm = pl.BlockSpec(memory_space=pl.ANY)
    outs = pl.pallas_call(
        functools.partial(gather_ring_kernel, count),
        in_specs=[hbm] * count,
        out_specs=[hbm] * count,
        out_shape=[jax.ShapeDtypeStruct((8, *own.shape), own.dtype) for own in owns],
        scratch_shapes=[
            pltpu.SemaphoreType.DMA((9 * count,)),
            pltpu.SemaphoreType.DMA((9 * count,)),
            pltpu.SemaphoreType.DMA((count,)),
        ],
        compiler_params=pltpu.CompilerParams(collective_id=ident, has_side_effects=True),
        name="gather_ring",
    )(*owns)
    return [out.reshape(-1, out.shape[-1]) for out in outs]


class PairGather:
    def __init__(self, at, own, out, send, recv, here, base, pieces):
        self.at, self.out, self.send, self.recv, self.base = at, out, send, recv, base
        size = own.shape[0] // pieces
        self.parts = [pl.ds(i * size, size) for i in range(pieces)]
        me = at.yl * 2 + at.core
        self.other = (1 - at.yl) * 2 + at.core
        self.kept = keep(own, out.at[me], here)
        self.far = [
            push(own.at[part], out.at[me, part], send, recv, base + 1 + i, at.partner())
            for i, part in enumerate(self.parts)
        ]
        self.near = [push(own, out.at[me], send, recv, base, at.sibling())]

    def forward(self):
        for i, part in enumerate(self.parts):
            self.far[i].wait_recv()
            view = self.out.at[self.other, part]
            index = self.base + 1 + len(self.parts) + i
            self.near.append(push(view, view, self.send, self.recv, index, self.at.sibling()))

    def finish(self):
        for copy in self.near:
            copy.wait_recv()
        for copy in (*self.far, *self.near):
            copy.wait_send()
        self.kept.wait()


PIECES = 4


def gather_pair_kernel(own, out, send, recv, here):
    at = Place()
    greet([at.sibling(), at.partner()])
    gather = PairGather(at, own, out, send, recv, here, 0, PIECES)
    gather.forward()
    gather.finish()


def gather_pair(own, ident):
    hbm = pl.BlockSpec(memory_space=pl.ANY)
    out = pl.pallas_call(
        gather_pair_kernel,
        in_specs=[hbm],
        out_specs=hbm,
        out_shape=jax.ShapeDtypeStruct((4, *own.shape), own.dtype),
        scratch_shapes=[
            pltpu.SemaphoreType.DMA((1 + 2 * PIECES,)),
            pltpu.SemaphoreType.DMA((1 + 2 * PIECES,)),
            pltpu.SemaphoreType.DMA,
        ],
        compiler_params=pltpu.CompilerParams(collective_id=ident, has_side_effects=True),
        name="gather_pair",
    )(own)
    return out.reshape(-1, own.shape[1])


def startup_kernel(hidden, segment, small, hidden_all, segment_all, small_all, send, recv, here):
    at = Place()
    greet(
        [
            at.sibling(), at.partner(), at.diagonal(), at.opposite(),
            at.along("z", 1), at.along("z", 3), at.along("x", 1), at.along("x", 3),
        ]
    )
    rank = at.yl * 2 + at.core
    first = (at.x * 4 + at.z) * 2
    mine = small_all.at[first + at.yh]
    shared = keep(small, mine, here.at[0])
    to_opposite = push(small, mine, send, recv, 0, at.opposite())
    gather = PairGather(at, hidden, hidden_all, send, recv, here.at[1], 12, PIECES)
    seg_here = keep(segment, segment_all.at[rank], here.at[2])
    seg_copies = [
        push(segment, segment_all.at[rank], send, recv, 9 + i, device)
        for i, device in enumerate((at.sibling(), at.partner(), at.diagonal()))
    ]
    copies = [to_opposite]

    def ring(axis, base, view, step, low, high):
        up = push(view(0), view(0), send, recv, base, at.along(axis, 1))
        down = push(view(0), view(0), send, recv, base + 1, at.along(axis, 3))
        up.wait_recv()
        far_up = push(low(3), low(3), send, recv, base + 2, at.along(axis, 1))
        down.wait_recv()
        far_down = push(high(1), high(1), send, recv, base + 3, at.along(axis, 3))
        far_up.wait_recv()
        far_down.wait_recv()
        copies.extend([up, down, far_up, far_down])

    shared.wait()
    to_opposite.wait_recv()
    z_at = lambda k: (at.x * 4 + lax.rem(at.z + k, 4)) * 2
    ring(
        "z", 1, lambda k: small_all.at[pl.ds(z_at(k), 2)], 2,
        lambda k: small_all.at[pl.ds(z_at(k), 1)],
        lambda k: small_all.at[pl.ds(z_at(k) + 1, 1)],
    )
    gather.forward()
    x_at = lambda k: lax.rem(at.x + k, 4) * 8
    ring(
        "x", 5, lambda k: small_all.at[pl.ds(x_at(k), 8)], 8,
        lambda k: small_all.at[pl.ds(x_at(k), 4)],
        lambda k: small_all.at[pl.ds(x_at(k) + 4, 4)],
    )
    gather.finish()
    seg_here.wait()
    for copy in seg_copies:
        copy.wait_recv()
    for copy in (*copies, *seg_copies):
        copy.wait_send()


def startup(hidden, segment, small, ident):
    hbm = pl.BlockSpec(memory_space=pl.ANY)
    sems = 12 + 1 + 2 * PIECES
    hidden_all, segment_all, small_all = pl.pallas_call(
        startup_kernel,
        in_specs=[hbm] * 3,
        out_specs=[hbm] * 3,
        out_shape=[
            jax.ShapeDtypeStruct((4, *hidden.shape), hidden.dtype),
            jax.ShapeDtypeStruct((4, *segment.shape), segment.dtype),
            jax.ShapeDtypeStruct((32, *small.shape), small.dtype),
        ],
        scratch_shapes=[
            pltpu.SemaphoreType.DMA((sems,)),
            pltpu.SemaphoreType.DMA((sems,)),
            pltpu.SemaphoreType.DMA((3,)),
        ],
        compiler_params=pltpu.CompilerParams(collective_id=ident, has_side_effects=True),
        name="startup",
    )(hidden, segment, small)
    return hidden_all.reshape(SEQ, D), segment_all, small_all.reshape(D, SMALL)


def scatter_ring_kernel(
    part, out, near, half_a, half_b, full_up, full_down, to_far, to_up, to_down, send, recv
):
    at = Place()
    greet([at.sibling(), at.ring(1), at.ring(3)])
    half = out.shape[0] // 2
    lo, hi = pl.ds(0, half), pl.ds(half, half)
    near_copies = {
        k: push(part.at[at.chip(k) * 2 + 1 - at.core], near.at[k], send, recv, k, at.sibling())
        for k in (2, 1, 3, 0)
    }

    def chip_sum(k):
        near_copies[k].wait_recv()
        return part[at.chip(k) * 2 + at.core].astype(F32) + near[k].astype(F32)

    to_far[...] = chip_sum(2).astype(BF)
    far_up = push(to_far.at[lo], half_a, send, recv, 4, at.ring(1))
    far_down = push(to_far.at[hi], half_b, send, recv, 5, at.ring(3))
    total = chip_sum(1)
    far_up.wait_recv()
    to_up[lo, :] = (total[:half] + half_a[...].astype(F32)).astype(BF)
    to_up[hi, :] = total[half:].astype(BF)
    up = push(to_up, full_up, send, recv, 6, at.ring(1))
    total = chip_sum(3)
    far_down.wait_recv()
    to_down[lo, :] = total[:half].astype(BF)
    to_down[hi, :] = (total[half:] + half_b[...].astype(F32)).astype(BF)
    down = push(to_down, full_down, send, recv, 7, at.ring(3))
    out[...] = chip_sum(0)
    up.wait_recv()
    out[...] += full_up[...].astype(F32)
    down.wait_recv()
    out[...] += full_down[...].astype(F32)
    for copy in (*near_copies.values(), far_up, far_down, up, down):
        copy.wait_send()


def scatter_ring(part, ident):
    vmem = pl.BlockSpec(memory_space=pltpu.VMEM)
    rows, columns = part.shape[0] // 8, part.shape[1]
    block, half = pltpu.VMEM((rows, columns), BF), pltpu.VMEM((rows // 2, columns), BF)
    return pl.pallas_call(
        scatter_ring_kernel,
        in_specs=[vmem],
        out_specs=vmem,
        out_shape=jax.ShapeDtypeStruct((rows, columns), F32),
        scratch_shapes=[
            pltpu.VMEM((4, rows, columns), BF), half, half, block, block, block, block, block,
            pltpu.SemaphoreType.DMA((8,)),
            pltpu.SemaphoreType.DMA((8,)),
        ],
        compiler_params=pltpu.CompilerParams(
            collective_id=ident, has_side_effects=True, vmem_limit_bytes=32 * MIB
        ),
        name="scatter_ring",
    )(part.reshape(8, rows, columns))


def scatter_pair_kernel(part, out, near, far, to_far, send, recv):
    at = Place()
    greet([at.sibling(), at.partner()])
    size = out.shape[0] // PIECES
    parts = [pl.ds(i * size, size) for i in range(PIECES)]
    other, own = (1 - at.yl) * 2, at.yl * 2
    first = [
        push(part.at[other + 1 - at.core, rows], near.at[1, rows], send, recv, i, at.sibling())
        for i, rows in enumerate(parts)
    ]
    second = push(part.at[own + 1 - at.core], near.at[0], send, recv, PIECES, at.sibling())
    sent = []
    for i, rows in enumerate(parts):
        first[i].wait_recv()
        total = part[other + at.core, rows, :].astype(F32) + near[1, rows, :].astype(F32)
        to_far[rows, :] = total.astype(BF)
        index = PIECES + 1 + i
        sent.append(push(to_far.at[rows], far.at[rows], send, recv, index, at.partner()))
    second.wait_recv()
    out[...] = part[own + at.core].astype(F32) + near[0].astype(F32)
    for i, rows in enumerate(parts):
        sent[i].wait_recv()
        out[rows, :] += far[rows, :].astype(F32)
    for copy in (*first, second, *sent):
        copy.wait_send()


def scatter_pair(part, ident):
    vmem = pl.BlockSpec(memory_space=pltpu.VMEM)
    rows, columns = part.shape[0] // 4, part.shape[1]
    block = pltpu.VMEM((rows, columns), BF)
    return pl.pallas_call(
        scatter_pair_kernel,
        in_specs=[vmem],
        out_specs=vmem,
        out_shape=jax.ShapeDtypeStruct((rows, columns), F32),
        scratch_shapes=[
            pltpu.VMEM((2, rows, columns), BF), block, block,
            pltpu.SemaphoreType.DMA((1 + 2 * PIECES,)),
            pltpu.SemaphoreType.DMA((1 + 2 * PIECES,)),
        ],
        compiler_params=pltpu.CompilerParams(
            collective_id=ident, has_side_effects=True, vmem_limit_bytes=32 * MIB
        ),
        name="scatter_pair",
    )(part.reshape(4, rows, columns))


def rotary_tables():
    half = HD // 2
    inverse = (10000.0 ** (-(np.arange(half, dtype=np.float64) * 2.0) / HD)).astype(np.float32)
    angles = np.arange(SEQ, dtype=np.float32)[:, None] * inverse[None, :]
    cosine, sine = np.cos(angles), np.sin(angles)
    wide_cosine = np.concatenate([cosine] * 4, axis=1)
    wide_sine = np.concatenate([-sine, sine] * 2, axis=1)
    return wide_cosine.astype(np.float32), wide_sine.astype(np.float32)


def swapped(values):
    lane = lax.broadcasted_iota(jnp.int32, values.shape, 1)
    low = (lane % HD) < HD // 2
    return jnp.where(low, pltpu.roll(values, 96, 1), pltpu.roll(values, 32, 1))


def rotated(values, cosine, sine):
    return values * cosine + swapped(values) * sine


def bias_block(key_segment, query_segment, first, rows):
    key_at = lax.broadcasted_iota(jnp.int32, (rows, BLOCK), 0)
    query_at = lax.broadcasted_iota(jnp.int32, (rows, BLOCK), 1) + first
    allowed = (key_segment == query_segment) & (key_at <= query_at)
    return jnp.where(allowed, 0.0, MASKED)


def attention_forward_kernel(
    hidden, gain, weights, cosine, sine, seg_column, seg_row, out_grad,
    part, normed, query, key, value, context_t, log_total, out_grad_all,
    bias, send, recv, here,
):
    at = Place()
    greet([at.sibling(), at.ring(1), at.ring(3)])
    gather = RingGather(at, out_grad, out_grad_all, send, recv, here)
    for block in range(SEQ // BLOCK):
        rows = slice(block * BLOCK, (block + 1) * BLOCK)
        values = hidden[rows, :].astype(F32)
        scale = lax.rsqrt(jnp.mean(values * values, axis=-1, keepdims=True) + EPS)
        normed[rows, :] = (values * scale * gain[...]).astype(BF)
    for half in range(2):
        columns = slice(half * 128, half * 128 + 128)
        pre = mm(normed[...], weights[:, columns])
        query[:, columns] = (rotated(pre, cosine[...], sine[...]) * 0.125).astype(BF)
    key_pre = mm(normed[...], weights[:, 256:384])
    key[...] = rotated(key_pre, cosine[...], sine[...]).astype(BF)
    value_pre = mm(normed[...], weights[:, 384:512])
    value[...] = value_pre.astype(BF)
    value_t = value_pre.T.astype(BF)
    for block in range(SEQ // BLOCK):
        first, end = block * BLOCK, (block + 1) * BLOCK
        bias[:end, :] = bias_block(seg_column[:end, :], seg_row[:, first:end], first, end)
        for head in range(HEADS):
            kv = slice((head // 2) * HD, (head // 2) * HD + HD)
            own = slice(head * HD, head * HD + HD)
            scores = mm_last(key[:end, kv], query[first:end, own]) + bias[:end, :]
            top = jnp.max(scores, axis=0, keepdims=True)
            powers = jnp.exp(scores - top)
            total = jnp.sum(powers, axis=0, keepdims=True)
            share = (powers * (1.0 / total)).astype(BF)
            context_t[own, first:end] = mm(value_t[kv, :end], share).astype(BF)
            log_total[head : head + 1, first:end] = top + jnp.log(total)
        if block == 2:
            gather.forward()
    gather.forward_far()
    context = context_t[...].T
    for block in range(SEQ // BLOCK):
        rows = slice(block * BLOCK, (block + 1) * BLOCK)
        part[rows, :] = mm_last(context[rows, :], weights[:, 512:768]).astype(BF)
    gather.finish()


def attention_forward(hidden, gain, weights, tables, seg_column, seg_row, out_grad, ident):
    vmem = pl.BlockSpec(memory_space=pltpu.VMEM)
    hbm = pl.BlockSpec(memory_space=pl.ANY)
    return pl.pallas_call(
        attention_forward_kernel,
        in_specs=[vmem] * 7 + [hbm],
        out_specs=[vmem] * 7 + [hbm],
        out_shape=[
            jax.ShapeDtypeStruct((SEQ, D), BF),
            jax.ShapeDtypeStruct((SEQ, D), BF),
            jax.ShapeDtypeStruct((SEQ, HEADS * HD), BF),
            jax.ShapeDtypeStruct((SEQ, 128), BF),
            jax.ShapeDtypeStruct((SEQ, 128), BF),
            jax.ShapeDtypeStruct((HEADS * HD, SEQ), BF),
            jax.ShapeDtypeStruct((8, SEQ), F32),
            jax.ShapeDtypeStruct((8, *out_grad.shape), BF),
        ],
        scratch_shapes=[
            pltpu.VMEM((SEQ, BLOCK), F32),
            pltpu.SemaphoreType.DMA((9,)),
            pltpu.SemaphoreType.DMA((9,)),
            pltpu.SemaphoreType.DMA,
        ],
        compiler_params=pltpu.CompilerParams(
            collective_id=ident, has_side_effects=True, vmem_limit_bytes=56 * MIB
        ),
        name="attention_forward",
    )(hidden, gain, weights, *tables, seg_column, seg_row, out_grad)


def attention_backward_kernel(
    dattn, normed, weights, cosine, sine, seg_column, seg_row,
    query, key, value, context_t, log_total,
    dn1, grads, bias, dcontext, dquery_t, dkey, dvalue, dall, dall_t,
):
    dcontext[...] = mm(dattn[...], weights[:, 512:768]).astype(BF)
    output_grad_t = mm(context_t[...], dattn[...])
    grads[:, 512:768] = output_grad_t.T.astype(BF)
    key_t = key[...].astype(F32).T.astype(BF)
    dkey[...] = jnp.zeros_like(dkey)
    dvalue[...] = jnp.zeros_like(dvalue)
    for block in range(SEQ // BLOCK):
        first, end = block * BLOCK, (block + 1) * BLOCK
        bias[:end, :] = bias_block(seg_column[:end, :], seg_row[:, first:end], first, end)
        for head in range(HEADS):
            kv = slice((head // 2) * HD, (head // 2) * HD + HD)
            own = slice(head * HD, head * HD + HD)
            query_block = query[first:end, own]
            dcontext_block = dcontext[first:end, own]
            scores = mm_last(key[:end, kv], query_block) + bias[:end, :]
            share = jnp.exp(scores - log_total[head : head + 1, first:end])
            dshare = mm_last(value[:end, kv], dcontext_block)
            centre = jnp.sum(share * dshare, axis=0, keepdims=True)
            dscore = (share * (dshare - centre)).astype(BF)
            dquery_t[own, first:end] = mm(key_t[kv, :end], dscore) * 0.125
            dkey[:end, kv] += mm(dscore, query_block)
            dvalue[:end, kv] += mm(share.astype(BF), dcontext_block)
    turn = -sine[...]
    for half in range(2):
        rows = slice(half * 128, half * 128 + 128)
        piece = rotated(dquery_t[rows, :].T, cosine[...], turn)
        dall[:, rows] = piece.astype(BF)
        dall_t[rows, :] = piece.T.astype(BF)
    piece = rotated(dkey[...], cosine[...], turn)
    dall[:, 256:384] = piece.astype(BF)
    dall_t[256:384, :] = piece.T.astype(BF)
    dall[:, 384:512] = dvalue[...].astype(BF)
    dall_t[384:512, :] = dvalue[...].T.astype(BF)
    grads[:, 0:512] = mm(dall_t[...], normed[...]).T.astype(BF)
    for block in range(SEQ // BLOCK):
        rows = slice(block * BLOCK, (block + 1) * BLOCK)
        dn1[rows, :] = mm_last(dall[rows, :], weights[:, 0:512]).astype(BF)


def attention_backward(dattn, normed, weights, tables, seg_column, seg_row, kept):
    vmem = pl.BlockSpec(memory_space=pltpu.VMEM)
    return pl.pallas_call(
        attention_backward_kernel,
        in_specs=[vmem] * 12,
        out_specs=[vmem] * 2,
        out_shape=[
            jax.ShapeDtypeStruct((SEQ, D), BF),
            jax.ShapeDtypeStruct((D, 768), BF),
        ],
        scratch_shapes=[
            pltpu.VMEM((SEQ, BLOCK), F32),
            pltpu.VMEM((SEQ, HEADS * HD), BF),
            pltpu.VMEM((HEADS * HD, SEQ), F32),
            pltpu.VMEM((SEQ, 128), F32),
            pltpu.VMEM((SEQ, 128), F32),
            pltpu.VMEM((SEQ, 512), BF),
            pltpu.VMEM((512, SEQ), BF),
        ],
        compiler_params=pltpu.CompilerParams(vmem_limit_bytes=56 * MIB),
        name="attention_backward",
    )(dattn, normed, weights, *tables, seg_column, seg_row, *kept)


def experts_kernel(
    x_in, d_in, gating, weights, y_out, dx_out, dgate, grads,
    x, d, xt, dt, y, dx, hidden, load, store,
):
    step = pl.program_id(0)
    rows_at_once = 512
    blocks = TOKENS // rows_at_once
    lane = lax.broadcasted_iota(jnp.int32, (rows_at_once, 128), 1)
    own_first = lax.axis_index("yh") * 16 + step * QUAD

    def rows_of(block):
        return pl.ds(pl.multiple_of(block * rows_at_once, rows_at_once), rows_at_once)

    def loads(block):
        rows = rows_of(block)
        return (
            pltpu.make_async_copy(x_in.at[rows], x.at[rows], load.at[block, 0]),
            pltpu.make_async_copy(d_in.at[rows], d.at[rows], load.at[block, 1]),
        )

    def stores(block):
        rows = rows_of(block)
        return (
            pltpu.make_async_copy(x.at[rows], y_out.at[rows], store.at[block, 0]),
            pltpu.make_async_copy(d.at[rows], dx_out.at[rows], store.at[block, 1]),
        )

    @pl.when(step == 0)
    def _():
        for block in range(blocks):
            for copy in loads(block):
                copy.start()
        dgate[...] = jnp.zeros_like(dgate)

    def tokens_block(block, carry):
        rows = rows_of(block)

        @pl.when(step == 0)
        def _():
            for copy in loads(block):
                copy.wait()
            xt[:, rows] = x[rows, :].T
            dt[:, rows] = d[rows, :].T
            y[rows, :] = jnp.zeros((rows_at_once, D), F32)
            dx[rows, :] = jnp.zeros((rows_at_once, D), F32)

        both = mm(x[rows, :], weights[:, 0 : 2 * F])
        gate, up = both[:, :F], both[:, F:]
        dact = mm(d[rows, :], weights[:, 2 * F :])
        turned = pltpu.roll(gating[rows, :], lax.rem(128 - own_first, 128), 1)
        factor = jnp.concatenate(
            [jnp.broadcast_to(turned[:, i : i + 1], (rows_at_once, FF)) for i in range(QUAD)],
            axis=1,
        )
        q = 1.0 / (1.0 + jnp.exp(-gate))
        silu = gate * q
        act = silu * up
        product = act * dact
        sums = dgate[rows, :]
        for i in range(QUAD):
            own = jnp.sum(product[:, i * FF : (i + 1) * FF], axis=1, keepdims=True)
            sums = jnp.where(lane == own_first + i, own, sums)
        dgate[rows, :] = sums
        dact = dact * factor
        hidden[rows, 0:F] = (dact * up * (q + silu * (1.0 - q))).astype(BF)
        hidden[rows, F : 2 * F] = (dact * silu).astype(BF)
        hidden[rows, 2 * F :] = (act * factor).astype(BF)
        y[rows, :] += mm_last(hidden[rows, 2 * F :], weights[:, 2 * F :])
        dx[rows, :] += mm_last(hidden[rows, 0 : 2 * F], weights[:, 0 : 2 * F])

        @pl.when(step == STEPS - 1)
        def _():
            x[rows, :] = y[rows, :].astype(BF)
            d[rows, :] = dx[rows, :].astype(BF)
            for copy in stores(block):
                copy.start()

        return carry

    lax.fori_loop(0, blocks, tokens_block, 0)

    def grads_block(block, carry):
        rows = pl.ds(pl.multiple_of(block * 512, 512), 512)
        grads[rows, 0 : 2 * F] = mm(xt[rows, :], hidden[:, 0 : 2 * F]).astype(BF)
        grads[rows, 2 * F :] = mm(dt[rows, :], hidden[:, 2 * F :]).astype(BF)
        return carry

    lax.fori_loop(0, D // 512, grads_block, 0)

    @pl.when(step == STEPS - 1)
    def _():
        for block in range(blocks):
            for copy in stores(block):
                copy.wait()


def experts(x, d, gating, weights):
    hbm = pl.BlockSpec(memory_space=pl.ANY)
    whole = pl.BlockSpec((TOKENS, 128), lambda step: (0, 0), pipeline_mode=pl.Buffered(1))
    column = pl.BlockSpec((D, 3 * F), lambda step: (0, step))
    return pl.pallas_call(
        experts_kernel,
        grid=(STEPS,),
        in_specs=[hbm, hbm, whole, column],
        out_specs=[hbm, hbm, whole, column],
        out_shape=[
            jax.ShapeDtypeStruct((TOKENS, D), BF),
            jax.ShapeDtypeStruct((TOKENS, D), BF),
            jax.ShapeDtypeStruct((TOKENS, 128), F32),
            jax.ShapeDtypeStruct((D, STEPS * 3 * F), BF),
        ],
        scratch_shapes=[
            pltpu.VMEM((TOKENS, D), BF),
            pltpu.VMEM((TOKENS, D), BF),
            pltpu.VMEM((D, TOKENS), BF),
            pltpu.VMEM((D, TOKENS), BF),
            pltpu.VMEM((TOKENS, D), F32),
            pltpu.VMEM((TOKENS, D), F32),
            pltpu.VMEM((TOKENS, 3 * F), BF),
            pltpu.SemaphoreType.DMA((TOKENS // 512, 2)),
            pltpu.SemaphoreType.DMA((TOKENS // 512, 2)),
        ],
        compiler_params=pltpu.CompilerParams(vmem_limit_bytes=62 * MIB),
        name="experts",
    )(x, d, gating, weights)


def from_everyone(value, axes):
    count = lax.axis_size(axes)
    shown = jnp.broadcast_to(value[None], (count, *value.shape))
    return lax.all_to_all(shown, axes, 0, 0, tiled=True)


def arrived(value, axes):
    count = lax.axis_size(axes)
    tiles = value.reshape(count, -1, *value.shape[1:])
    return lax.all_to_all(tiles, axes, 0, 0, tiled=True)


def summed(value, axes):
    return jnp.sum(arrived(value, axes).astype(F32), axis=0)


def norm_scale(values):
    return lax.rsqrt(jnp.mean(values * values, axis=-1, keepdims=True) + EPS)


def norm_grad(values, gain, dnormed):
    scale = norm_scale(values)
    unit = values * scale
    weighted = dnormed * gain
    dvalues = scale * (weighted - unit * jnp.mean(weighted * unit, axis=-1, keepdims=True))
    return dvalues, jnp.sum(dnormed * unit, axis=0)


def packed_experts(expert_gate, expert_up, expert_down):
    shares = jnp.stack([expert_gate, expert_up, expert_down])
    shares = shares.reshape(3, 2, STEPS, QUAD, 32, FF)
    return shares.transpose(1, 4, 2, 0, 3, 5).reshape(2, 32, STEPS * 3 * F)


def unpacked_experts(tiles):
    tiles = tiles.reshape(2, 32, STEPS, 3, QUAD, FF).transpose(3, 0, 2, 4, 1, 5)
    tiles = tiles.reshape(3, E, 32, FF).astype(F32)
    return tiles[0], tiles[1], tiles[2]


def on_device(
    hidden_in, out_grad, attn_gain, query_weight, key_weight, value_weight, output_weight,
    moe_gain, router_weight, expert_gate, expert_up, expert_down, expert_ids, segment_ids,
):
    halves = packed_experts(expert_gate, expert_up, expert_down)
    halves = lax.all_to_all(halves, "yh", 0, 0, tiled=True)
    expert_weights = lax.all_gather(
        halves.reshape(64, STEPS * 3 * F), PLANE, axis=0, tiled=True
    )
    small = jnp.concatenate(
        [
            query_weight, key_weight, value_weight, output_weight,
            router_weight, attn_gain[:, None], moe_gain[:, None], jnp.zeros((32, 94), BF),
        ],
        axis=1,
    )
    segment = jnp.pad(segment_ids.reshape(2, 128), ((0, 6), (0, 0)))
    hidden_all, segment_all, small = startup(hidden_in, segment, small, 0)
    router = small[:, 768:800]
    attn_gain_all = small[:, 800].astype(F32)
    moe_gain_all = small[:, 801].astype(F32)
    tables = tuple(jnp.asarray(t) for t in rotary_tables())
    segments = segment_all[:, :2].reshape(SEQ)
    seg_column, seg_row = segments[:, None], segments[None, :]

    part, normed_all, *kept, d = attention_forward(
        hidden_all, attn_gain_all[None, :], small, tables, seg_column, seg_row, out_grad, 1
    )
    d = d.reshape(TOKENS, D)
    hidden = hidden_in.astype(F32)
    middle = hidden + scatter_pair(part, 2)
    normed_moe = (middle * norm_scale(middle) * moe_gain_all).astype(BF)
    logits = mm(normed_moe, router)
    named = jnp.any(
        expert_ids[:, :, None] == jnp.arange(E, dtype=jnp.int32)[None, None, :], axis=1
    )
    top = jnp.max(jnp.where(named, logits, -jnp.inf), axis=-1, keepdims=True)
    powers = jnp.where(named, jnp.exp(logits - top), 0.0)
    gating = powers / jnp.sum(powers, axis=-1, keepdims=True)

    x, gating_all = gather_ring([normed_moe, jnp.pad(gating, ((0, 0), (0, 96)))], 3)
    y, dx, dgate, expert_grads = experts(x, d, gating_all, expert_weights)
    expert_grads = lax.psum_scatter(expert_grads, PLANE, scatter_dimension=0, tiled=True)

    sums = scatter_ring(jnp.concatenate([dx, dgate.astype(BF)], axis=1), 4)
    dgate = sums[:, D : D + E]
    dchosen = gating * (dgate - jnp.sum(gating * dgate, axis=-1, keepdims=True))
    dlogits = dchosen.astype(BF)
    dnormed_moe = sums[:, :D] + mm_last(dlogits, router)
    dmiddle, moe_gain_part = norm_grad(middle, moe_gain_all, dnormed_moe)
    dmiddle = dmiddle + out_grad.astype(F32)
    dattn = gather_pair(dmiddle.astype(BF), 5)
    block_out = (middle + summed(y, RING)).astype(BF)
    router_part = lax.dot_general(
        normed_moe, dlogits, (((0,), (0,)), ((), ())), preferred_element_type=F32
    )
    rest = jnp.concatenate(
        [router_part, moe_gain_part[:, None], jnp.zeros((D, 95), F32)], axis=1
    )
    rest = lax.psum_scatter(rest.astype(BF), PLANE, scatter_dimension=0, tiled=True)
    rest = rest.reshape(2, 1, 32, 128)
    rest = jnp.broadcast_to(rest, (2, 4, 32, 128)).reshape(8, 32, 128)
    rest = jnp.sum(lax.all_to_all(rest, RING, 0, 0, tiled=True).astype(F32), axis=0)

    dn1, attention_grads = attention_backward(
        dattn, normed_all, small, tables, seg_column, seg_row, kept
    )
    attention_grads = lax.psum_scatter(attention_grads, PLANE, scatter_dimension=0, tiled=True)
    dhidden, _ = norm_grad(hidden, attn_gain_all, scatter_pair(dn1, 6))
    hidden_grad = dmiddle + dhidden

    expert_grads = unpacked_experts(
        lax.all_to_all(expert_grads.reshape(2, 32, STEPS * 3 * F), "yh", 0, 0, tiled=True)
    )
    attention_grads = lax.all_to_all(attention_grads.reshape(2, 32, 768), "yh", 0, 0, tiled=True)
    attention_grads = jnp.sum(attention_grads.astype(F32), axis=0)
    own_weights = jnp.concatenate([query_weight, key_weight, value_weight], axis=1)
    attn_gain_grad = jnp.sum(own_weights.astype(F32) * attention_grads[:, :512], axis=1)
    attn_gain_grad = jnp.sum(from_everyone(attn_gain_grad[None], TENSOR), axis=(0, 1))
    return (
        block_out,
        hidden_grad,
        attn_gain_grad / attn_gain.astype(F32),
        attention_grads[:, 0:256],
        attention_grads[:, 256:384],
        attention_grads[:, 384:512],
        attention_grads[:, 512:768],
        rest[:, 32],
        rest[:, :32],
        *expert_grads,
    )


def solution(mesh):
    fine = Mesh(np.asarray(mesh.devices).reshape(4, 4, 2, 2, 2), ALL)
    return jax.shard_map(
        on_device,
        mesh=fine,
        in_specs=(
            P(ALL, None),
            P(ALL, None),
            P(DP),
            P(DP, TENSOR),
            P(DP, TENSOR),
            P(DP, TENSOR),
            P(DP, TENSOR),
            P(DP),
            P(DP, None),
            P(None, DP, TENSOR),
            P(None, DP, TENSOR),
            P(None, DP, TENSOR),
            P(ALL, None),
            P(ALL),
        ),
        out_specs=(
            P(ALL, None),
            P(ALL, None),
            P(DP),
            P(DP, TENSOR),
            P(DP, TENSOR),
            P(DP, TENSOR),
            P(DP, TENSOR),
            P(DP),
            P(DP, None),
            P(None, DP, TENSOR),
            P(None, DP, TENSOR),
            P(None, DP, TENSOR),
        ),
        check_vma=False,
    )
```

```python
import functools

import jax
import jax.numpy as jnp
import numpy as np
from jax import lax
from jax.experimental import pallas as pl
from jax.experimental.pallas import tpu as pltpu
from jax.sharding import Mesh
from jax.sharding import PartitionSpec as P

D = 1024
HD = 64
E = 32
SEQ = 1024
LOCAL = 256
HEADS = 4
QUAD = 4
FF = 128
F = QUAD * FF
EPS = 1e-06
MASKED = -1e30
BLOCK = 256
TOKENS = 2048
STEPS = 4

DP = ("x", "z", "yh")
TENSOR = ("yl", "core")
RING = ("yh", "yl", "core")
PLANE = ("x", "z")
ALL = ("x", "z", "yh", "yl", "core")

F32 = jnp.float32
BF = jnp.bfloat16
LAST = (((1,), (1,)), ((), ()))
MIB = 1024 * 1024
MESH = pl.DeviceIdType.MESH
SMALL = 896


def mm(a, b):
    return jnp.dot(a, b, preferred_element_type=F32)


def mm_last(a, b):
    return lax.dot_general(a, b, LAST, preferred_element_type=F32)


class Place:
    def __init__(self):
        self.x = lax.axis_index("x")
        self.z = lax.axis_index("z")
        self.yh = lax.axis_index("yh")
        self.yl = lax.axis_index("yl")
        self.core = lax.axis_index("core")
        self.y = self.yh * 2 + self.yl

    def chip(self, k):
        return lax.rem(self.y + k, 4)

    def ring(self, k):
        chip = self.chip(k)
        return {"yh": chip // 2, "yl": lax.rem(chip, 2)}

    def along(self, axis, k):
        return {axis: lax.rem(getattr(self, axis) + k, 4)}

    def sibling(self):
        return {"core": 1 - self.core}

    def partner(self):
        return {"yl": 1 - self.yl}

    def diagonal(self):
        return {"yl": 1 - self.yl, "core": 1 - self.core}

    def opposite(self):
        return {"yh": 1 - self.yh}


def greet(devices):
    barrier = pltpu.get_barrier_semaphore()
    for device in devices:
        pl.semaphore_signal(barrier, inc=1, device_id=device, device_id_type=MESH)
    pl.semaphore_wait(barrier, len(devices))


def push(src, dst, send, recv, i, device):
    copy = pltpu.make_async_remote_copy(
        src_ref=src, dst_ref=dst, send_sem=send.at[i], recv_sem=recv.at[i],
        device_id=device, device_id_type=MESH,
    )
    copy.start()
    return copy


def keep(src, dst, sem):
    copy = pltpu.make_async_copy(src, dst, sem)
    copy.start()
    return copy


class RingGather:
    def __init__(self, at, own, out, send, recv, here, base=0):
        self.at, self.out, self.send, self.recv, self.base = at, out, send, recv, base
        self.half = own.shape[0] // 2
        me = out.at[self.slot(0)]
        self.kept = keep(own, me, here)
        self.copies = {}
        self.go(1, own, me, at.ring(1))
        self.go(2, own, me, at.ring(3))
        self.go(0, own, me, at.sibling())

    def slot(self, k):
        return self.at.chip(k) * 2 + self.at.core

    def go(self, i, src, dst, device):
        self.copies[i] = push(src, dst, self.send, self.recv, self.base + i, device)

    def pass_on(self, i, view, device):
        self.go(i, view, view, device)

    def forward(self):
        lo, hi = pl.ds(0, self.half), pl.ds(self.half, self.half)
        self.copies[1].wait_recv()
        self.pass_on(3, self.out.at[self.slot(3), lo], self.at.ring(1))
        self.pass_on(4, self.out.at[self.slot(3)], self.at.sibling())
        self.copies[2].wait_recv()
        self.pass_on(5, self.out.at[self.slot(1), hi], self.at.ring(3))
        self.pass_on(6, self.out.at[self.slot(1)], self.at.sibling())

    def forward_far(self):
        lo, hi = pl.ds(0, self.half), pl.ds(self.half, self.half)
        self.copies[3].wait_recv()
        self.pass_on(7, self.out.at[self.slot(2), lo], self.at.sibling())
        self.copies[5].wait_recv()
        self.pass_on(8, self.out.at[self.slot(2), hi], self.at.sibling())

    def finish(self):
        for i in (0, 4, 6, 7, 8):
            self.copies[i].wait_recv()
        for i in range(9):
            self.copies[i].wait_send()
        self.kept.wait()


def gather_ring_kernel(count, *refs):
    owns, outs = refs[:count], refs[count : 2 * count]
    send, recv, here = refs[2 * count :]
    at = Place()
    greet([at.sibling(), at.ring(1), at.ring(3)])
    gathers = [
        RingGather(at, own, out, send, recv, here.at[i], 9 * i)
        for i, (own, out) in enumerate(zip(owns, outs))
    ]
    for gather in gathers:
        gather.forward()
    for gather in gathers:
        gather.forward_far()
    for gather in gathers:
        gather.finish()


def gather_ring(owns, ident):
    count = len(owns)
    hbm = pl.BlockSpec(memory_space=pl.ANY)
    outs = pl.pallas_call(
        functools.partial(gather_ring_kernel, count),
        in_specs=[hbm] * count,
        out_specs=[hbm] * count,
        out_shape=[jax.ShapeDtypeStruct((8, *own.shape), own.dtype) for own in owns],
        scratch_shapes=[
            pltpu.SemaphoreType.DMA((9 * count,)),
            pltpu.SemaphoreType.DMA((9 * count,)),
            pltpu.SemaphoreType.DMA((count,)),
        ],
        compiler_params=pltpu.CompilerParams(collective_id=ident, has_side_effects=True),
        name="gather_ring",
    )(*owns)
    return [out.reshape(-1, out.shape[-1]) for out in outs]


class PairGather:
    def __init__(self, at, own, out, send, recv, here, base, pieces):
        self.at, self.out, self.send, self.recv, self.base = at, out, send, recv, base
        size = own.shape[0] // pieces
        self.parts = [pl.ds(i * size, size) for i in range(pieces)]
        me = at.yl * 2 + at.core
        self.other = (1 - at.yl) * 2 + at.core
        self.kept = keep(own, out.at[me], here)
        self.far = [
            push(own.at[part], out.at[me, part], send, recv, base + 1 + i, at.partner())
            for i, part in enumerate(self.parts)
        ]
        self.near = [push(own, out.at[me], send, recv, base, at.sibling())]

    def forward(self):
        for i, part in enumerate(self.parts):
            self.far[i].wait_recv()
            view = self.out.at[self.other, part]
            index = self.base + 1 + len(self.parts) + i
            self.near.append(push(view, view, self.send, self.recv, index, self.at.sibling()))

    def finish(self):
        for copy in self.near:
            copy.wait_recv()
        for copy in (*self.far, *self.near):
            copy.wait_send()
        self.kept.wait()


PIECES = 4


def gather_pair_kernel(own, out, send, recv, here):
    at = Place()
    greet([at.sibling(), at.partner()])
    gather = PairGather(at, own, out, send, recv, here, 0, PIECES)
    gather.forward()
    gather.finish()


def gather_pair(own, ident):
    hbm = pl.BlockSpec(memory_space=pl.ANY)
    out = pl.pallas_call(
        gather_pair_kernel,
        in_specs=[hbm],
        out_specs=hbm,
        out_shape=jax.ShapeDtypeStruct((4, *own.shape), own.dtype),
        scratch_shapes=[
            pltpu.SemaphoreType.DMA((1 + 2 * PIECES,)),
            pltpu.SemaphoreType.DMA((1 + 2 * PIECES,)),
            pltpu.SemaphoreType.DMA,
        ],
        compiler_params=pltpu.CompilerParams(collective_id=ident, has_side_effects=True),
        name="gather_pair",
    )(own)
    return out.reshape(-1, own.shape[1])


def startup_kernel(hidden, segment, small, hidden_all, segment_all, small_all, send, recv, here):
    at = Place()
    greet(
        [
            at.sibling(), at.partner(), at.diagonal(), at.opposite(),
            at.along("z", 1), at.along("z", 3), at.along("x", 1), at.along("x", 3),
        ]
    )
    rank = at.yl * 2 + at.core
    first = (at.x * 4 + at.z) * 2
    mine = small_all.at[first + at.yh]
    shared = keep(small, mine, here.at[0])
    to_opposite = push(small, mine, send, recv, 0, at.opposite())
    gather = PairGather(at, hidden, hidden_all, send, recv, here.at[1], 12, PIECES)
    seg_here = keep(segment, segment_all.at[rank], here.at[2])
    seg_copies = [
        push(segment, segment_all.at[rank], send, recv, 9 + i, device)
        for i, device in enumerate((at.sibling(), at.partner(), at.diagonal()))
    ]
    copies = [to_opposite]

    def ring(axis, base, view, step, low, high):
        up = push(view(0), view(0), send, recv, base, at.along(axis, 1))
        down = push(view(0), view(0), send, recv, base + 1, at.along(axis, 3))
        up.wait_recv()
        far_up = push(low(3), low(3), send, recv, base + 2, at.along(axis, 1))
        down.wait_recv()
        far_down = push(high(1), high(1), send, recv, base + 3, at.along(axis, 3))
        far_up.wait_recv()
        far_down.wait_recv()
        copies.extend([up, down, far_up, far_down])

    shared.wait()
    to_opposite.wait_recv()
    z_at = lambda k: (at.x * 4 + lax.rem(at.z + k, 4)) * 2
    ring(
        "z", 1, lambda k: small_all.at[pl.ds(z_at(k), 2)], 2,
        lambda k: small_all.at[pl.ds(z_at(k), 1)],
        lambda k: small_all.at[pl.ds(z_at(k) + 1, 1)],
    )
    gather.forward()
    x_at = lambda k: lax.rem(at.x + k, 4) * 8
    ring(
        "x", 5, lambda k: small_all.at[pl.ds(x_at(k), 8)], 8,
        lambda k: small_all.at[pl.ds(x_at(k), 4)],
        lambda k: small_all.at[pl.ds(x_at(k) + 4, 4)],
    )
    gather.finish()
    seg_here.wait()
    for copy in seg_copies:
        copy.wait_recv()
    for copy in (*copies, *seg_copies):
        copy.wait_send()


def startup(hidden, segment, small, ident):
    hbm = pl.BlockSpec(memory_space=pl.ANY)
    sems = 12 + 1 + 2 * PIECES
    hidden_all, segment_all, small_all = pl.pallas_call(
        startup_kernel,
        in_specs=[hbm] * 3,
        out_specs=[hbm] * 3,
        out_shape=[
            jax.ShapeDtypeStruct((4, *hidden.shape), hidden.dtype),
            jax.ShapeDtypeStruct((4, *segment.shape), segment.dtype),
            jax.ShapeDtypeStruct((32, *small.shape), small.dtype),
        ],
        scratch_shapes=[
            pltpu.SemaphoreType.DMA((sems,)),
            pltpu.SemaphoreType.DMA((sems,)),
            pltpu.SemaphoreType.DMA((3,)),
        ],
        compiler_params=pltpu.CompilerParams(collective_id=ident, has_side_effects=True),
        name="startup",
    )(hidden, segment, small)
    return hidden_all.reshape(SEQ, D), segment_all, small_all.reshape(D, SMALL)


class RingScatter:
    def __init__(self, at, part, scratch, send, recv, base=0):
        self.at, self.part, self.send, self.recv, self.base = at, part, send, recv, base
        (
            self.near, self.half_a, self.half_b, self.full_up, self.full_down,
            self.to_far, self.to_up, self.to_down,
        ) = scratch
        self.half = self.half_a.shape[0]
        self.lo, self.hi = pl.ds(0, self.half), pl.ds(self.half, self.half)
        self.copies = {
            k: self.go(
                k, part.at[at.chip(k) * 2 + 1 - at.core], self.near.at[k], at.sibling()
            )
            for k in (2, 1, 3, 0)
        }

    def go(self, i, src, dst, device):
        return push(src, dst, self.send, self.recv, self.base + i, device)

    def chip_sum(self, k):
        self.copies[k].wait_recv()
        own = self.part[self.at.chip(k) * 2 + self.at.core]
        return own.astype(F32) + self.near[k].astype(F32)

    def far(self):
        self.to_far[...] = self.chip_sum(2).astype(BF)
        self.copies[4] = self.go(4, self.to_far.at[self.lo], self.half_a, self.at.ring(1))
        self.copies[5] = self.go(5, self.to_far.at[self.hi], self.half_b, self.at.ring(3))

    def sides(self):
        total = self.chip_sum(1)
        self.copies[4].wait_recv()
        self.to_up[self.lo, :] = (total[: self.half] + self.half_a[...].astype(F32)).astype(BF)
        self.to_up[self.hi, :] = total[self.half :].astype(BF)
        self.copies[6] = self.go(6, self.to_up, self.full_up, self.at.ring(1))
        total = self.chip_sum(3)
        self.copies[5].wait_recv()
        self.to_down[self.lo, :] = total[: self.half].astype(BF)
        self.to_down[self.hi, :] = (total[self.half :] + self.half_b[...].astype(F32)).astype(BF)
        self.copies[7] = self.go(7, self.to_down, self.full_down, self.at.ring(3))

    def finish(self, out):
        out[...] = self.chip_sum(0)
        self.copies[6].wait_recv()
        out[...] += self.full_up[...].astype(F32)
        self.copies[7].wait_recv()
        out[...] += self.full_down[...].astype(F32)
        for copy in self.copies.values():
            copy.wait_send()


def ring_scratch(rows, columns):
    block, half = pltpu.VMEM((rows, columns), BF), pltpu.VMEM((rows // 2, columns), BF)
    return [pltpu.VMEM((4, rows, columns), BF), half, half, block, block, block, block, block]


def scatter_ring_kernel(part, out, *refs):
    at = Place()
    greet([at.sibling(), at.ring(1), at.ring(3)])
    scatter = RingScatter(at, part, refs[:8], *refs[8:])
    scatter.far()
    scatter.sides()
    scatter.finish(out)


def scatter_ring(part, ident):
    vmem = pl.BlockSpec(memory_space=pltpu.VMEM)
    rows, columns = part.shape[0] // 8, part.shape[1]
    return pl.pallas_call(
        scatter_ring_kernel,
        in_specs=[vmem],
        out_specs=vmem,
        out_shape=jax.ShapeDtypeStruct((rows, columns), F32),
        scratch_shapes=[
            *ring_scratch(rows, columns),
            pltpu.SemaphoreType.DMA((8,)),
            pltpu.SemaphoreType.DMA((8,)),
        ],
        compiler_params=pltpu.CompilerParams(
            collective_id=ident, has_side_effects=True, vmem_limit_bytes=32 * MIB
        ),
        name="scatter_ring",
    )(part.reshape(8, rows, columns))


class PairScatter:
    def __init__(self, at, part, scratch, send, recv):
        self.at, self.part, self.send, self.recv = at, part, send, recv
        self.near, self.far_rows, self.to_far = scratch
        size = self.to_far.shape[0] // PIECES
        self.parts = [pl.ds(i * size, size) for i in range(PIECES)]
        self.other, self.own = (1 - at.yl) * 2, at.yl * 2
        self.first = [
            push(
                part.at[self.other + 1 - at.core, rows], self.near.at[1, rows],
                send, recv, i, at.sibling(),
            )
            for i, rows in enumerate(self.parts)
        ]
        self.second = push(
            part.at[self.own + 1 - at.core], self.near.at[0], send, recv, PIECES, at.sibling()
        )

    def forward(self):
        at = self.at
        self.sent = []
        for i, rows in enumerate(self.parts):
            self.first[i].wait_recv()
            own = self.part[self.other + at.core, rows, :].astype(F32)
            self.to_far[rows, :] = (own + self.near[1, rows, :].astype(F32)).astype(BF)
            self.sent.append(
                push(
                    self.to_far.at[rows], self.far_rows.at[rows], self.send, self.recv,
                    PIECES + 1 + i, at.partner(),
                )
            )

    def finish(self, out):
        self.second.wait_recv()
        out[...] = self.part[self.own + self.at.core].astype(F32) + self.near[0].astype(F32)
        for i, rows in enumerate(self.parts):
            self.sent[i].wait_recv()
            out[rows, :] += self.far_rows[rows, :].astype(F32)
        for copy in (*self.first, self.second, *self.sent):
            copy.wait_send()


def pair_scratch(rows, columns):
    block = pltpu.VMEM((rows, columns), BF)
    return [pltpu.VMEM((2, rows, columns), BF), block, block]


def scatter_pair_kernel(part, out, *refs):
    at = Place()
    greet([at.sibling(), at.partner()])
    scatter = PairScatter(at, part, refs[:3], *refs[3:])
    scatter.forward()
    scatter.finish(out)


def scatter_pair(part, ident):
    vmem = pl.BlockSpec(memory_space=pltpu.VMEM)
    rows, columns = part.shape[0] // 4, part.shape[1]
    return pl.pallas_call(
        scatter_pair_kernel,
        in_specs=[vmem],
        out_specs=vmem,
        out_shape=jax.ShapeDtypeStruct((rows, columns), F32),
        scratch_shapes=[
            *pair_scratch(rows, columns),
            pltpu.SemaphoreType.DMA((1 + 2 * PIECES,)),
            pltpu.SemaphoreType.DMA((1 + 2 * PIECES,)),
        ],
        compiler_params=pltpu.CompilerParams(
            collective_id=ident, has_side_effects=True, vmem_limit_bytes=32 * MIB
        ),
        name="scatter_pair",
    )(part.reshape(4, rows, columns))


class AxisScatter:
    def __init__(self, at, axis, part, scratch, send, recv, base):
        self.at, self.axis, self.part, self.base = at, axis, part, base
        self.send, self.recv = send, recv
        self.half_a, self.half_b, self.up, self.down, self.to_up, self.to_down = scratch
        self.half = part.shape[1] // 2
        lo, hi = pl.ds(0, self.half), pl.ds(self.half, self.half)
        far = part.at[self.to(2)]
        self.far_up = self.go(0, far.at[lo], self.half_a, 1)
        self.far_down = self.go(1, far.at[hi], self.half_b, 3)

    def to(self, k):
        return self.at.along(self.axis, k)[self.axis]

    def go(self, i, src, dst, k):
        return push(src, dst, self.send, self.recv, self.base + i, self.at.along(self.axis, k))

    def sides(self):
        h = self.half
        self.far_up.wait_recv()
        block = self.part[self.to(1)]
        self.to_up[:h] = (block[:h].astype(F32) + self.half_a[...].astype(F32)).astype(BF)
        self.to_up[h:] = block[h:]
        self.sent_up = self.go(2, self.to_up, self.up, 1)
        self.far_down.wait_recv()
        block = self.part[self.to(3)]
        self.to_down[:h] = block[:h]
        self.to_down[h:] = (block[h:].astype(F32) + self.half_b[...].astype(F32)).astype(BF)
        self.sent_down = self.go(3, self.to_down, self.down, 3)

    def finish(self):
        total = self.part[self.to(0)].astype(F32)
        self.sent_up.wait_recv()
        self.sent_down.wait_recv()
        total = total + self.up[...].astype(F32) + self.down[...].astype(F32)
        for copy in (self.far_up, self.far_down, self.sent_up, self.sent_down):
            copy.wait_send()
        return total


def axis_scratch(*block):
    half = (block[0] // 2, *block[1:])
    return [pltpu.VMEM(half, BF)] * 2 + [pltpu.VMEM(block, BF)] * 4


def final_kernel(
    part, grads, weights, dn1, attention, rest,
    over_z, over_y, from_opposite, share, shares, *refs,
):
    at = Place()
    greet(
        [
            at.sibling(), at.partner(), at.diagonal(), at.opposite(),
            at.along("z", 1), at.along("z", 3), at.along("x", 1), at.along("x", 3),
        ]
    )
    pair_refs, x_refs, z_refs = refs[:3], refs[3:9], refs[9:15]
    send, recv = refs[15:]
    base = 1 + 2 * PIECES
    x_scatter = AxisScatter(at, "x", grads, x_refs, send, recv, base)
    pair = PairScatter(at, part, pair_refs, send, recv)
    pair.forward()
    x_scatter.sides()
    over_z[...] = x_scatter.finish().astype(BF).reshape(over_z.shape)
    z_scatter = AxisScatter(at, "z", over_z, z_refs, send, recv, base + 4)
    z_scatter.sides()
    over_y[...] = z_scatter.finish().astype(BF)
    swap = push(over_y.at[1 - at.yh], from_opposite, send, recv, base + 8, at.opposite())
    swap.wait_recv()
    total = over_y[at.yh].astype(F32) + from_opposite[...].astype(F32)
    attention[...] = total[:, :768]
    gain_part = jnp.sum(total[:, :512] * weights[...].astype(F32), axis=1, keepdims=True)
    lane = lax.broadcasted_iota(jnp.int32, (32, 128), 1)
    share[...] = jnp.where(lane == 33, gain_part, total[:, 768:])
    copies = [
        push(share, shares.at[i], send, recv, base + 9 + i, device)
        for i, device in enumerate((at.sibling(), at.partner(), at.diagonal()))
    ]
    pair.finish(dn1)
    rest[...] = share[...]
    for i, copy in enumerate(copies):
        copy.wait_recv()
        rest[...] += shares[i]
    for copy in (swap, *copies):
        copy.wait_send()


def final(part, grads, weights, ident):
    vmem = pl.BlockSpec(memory_space=pltpu.VMEM)
    width = grads.shape[1]
    sems = 1 + 2 * PIECES + 12
    return pl.pallas_call(
        final_kernel,
        in_specs=[vmem] * 3,
        out_specs=[vmem] * 3,
        out_shape=[
            jax.ShapeDtypeStruct((LOCAL, D), F32),
            jax.ShapeDtypeStruct((32, 768), F32),
            jax.ShapeDtypeStruct((32, 128), F32),
        ],
        scratch_shapes=[
            pltpu.VMEM((4, 2, 32, width), BF),
            pltpu.VMEM((2, 32, width), BF),
            pltpu.VMEM((32, width), BF),
            pltpu.VMEM((32, 128), F32),
            pltpu.VMEM((3, 32, 128), F32),
            *pair_scratch(LOCAL, D),
            *axis_scratch(8, 32, width),
            *axis_scratch(2, 32, width),
            pltpu.SemaphoreType.DMA((sems,)),
            pltpu.SemaphoreType.DMA((sems,)),
        ],
        compiler_params=pltpu.CompilerParams(
            collective_id=ident, has_side_effects=True, vmem_limit_bytes=32 * MIB
        ),
        name="final",
    )(part.reshape(4, LOCAL, D), grads.reshape(4, 8, 32, width), weights)


def swap_kernel(halves, out, send, recv, here):
    at = Place()
    greet([at.opposite()])
    kept = keep(halves.at[at.yh], out.at[at.yh], here)
    parts = [pl.ds(i * 8, 8) for i in range(4)]
    copies = [
        push(halves.at[1 - at.yh, rows], out.at[at.yh, rows], send, recv, i, at.opposite())
        for i, rows in enumerate(parts)
    ]
    kept.wait()
    for copy in copies:
        copy.wait()


def swap_halves(halves, ident):
    hbm = pl.BlockSpec(memory_space=pl.ANY)
    return pl.pallas_call(
        swap_kernel,
        in_specs=[hbm],
        out_specs=hbm,
        out_shape=jax.ShapeDtypeStruct(halves.shape, halves.dtype),
        scratch_shapes=[
            pltpu.SemaphoreType.DMA((4,)),
            pltpu.SemaphoreType.DMA((4,)),
            pltpu.SemaphoreType.DMA,
        ],
        compiler_params=pltpu.CompilerParams(collective_id=ident, has_side_effects=True),
        name="swap_halves",
    )(halves)


def rotary_tables():
    half = HD // 2
    inverse = (10000.0 ** (-(np.arange(half, dtype=np.float64) * 2.0) / HD)).astype(np.float32)
    angles = np.arange(SEQ, dtype=np.float32)[:, None] * inverse[None, :]
    cosine, sine = np.cos(angles), np.sin(angles)
    wide_cosine = np.concatenate([cosine] * 4, axis=1)
    wide_sine = np.concatenate([-sine, sine] * 2, axis=1)
    return wide_cosine.astype(np.float32), wide_sine.astype(np.float32)


def swapped(values):
    lane = lax.broadcasted_iota(jnp.int32, values.shape, 1)
    low = (lane % HD) < HD // 2
    return jnp.where(low, pltpu.roll(values, 96, 1), pltpu.roll(values, 32, 1))


def rotated(values, cosine, sine):
    return values * cosine + swapped(values) * sine


def bias_block(key_segment, query_segment, first, rows):
    key_at = lax.broadcasted_iota(jnp.int32, (rows, BLOCK), 0)
    query_at = lax.broadcasted_iota(jnp.int32, (rows, BLOCK), 1) + first
    allowed = (key_segment == query_segment) & (key_at <= query_at)
    return jnp.where(allowed, 0.0, MASKED)


def attention_forward_kernel(
    hidden, gain, weights, cosine, sine, seg_column, seg_row, out_grad,
    part, normed, query, key, value, context_t, log_total, out_grad_all,
    bias, send, recv, here,
):
    at = Place()
    greet([at.sibling(), at.ring(1), at.ring(3)])
    gather = RingGather(at, out_grad, out_grad_all, send, recv, here)
    for block in range(SEQ // BLOCK):
        rows = slice(block * BLOCK, (block + 1) * BLOCK)
        values = hidden[rows, :].astype(F32)
        scale = lax.rsqrt(jnp.mean(values * values, axis=-1, keepdims=True) + EPS)
        normed[rows, :] = (values * scale * gain[...]).astype(BF)
    for half in range(2):
        columns = slice(half * 128, half * 128 + 128)
        pre = mm(normed[...], weights[:, columns])
        query[:, columns] = (rotated(pre, cosine[...], sine[...]) * 0.125).astype(BF)
    key_pre = mm(normed[...], weights[:, 256:384])
    key[...] = rotated(key_pre, cosine[...], sine[...]).astype(BF)
    value_pre = mm(normed[...], weights[:, 384:512])
    value[...] = value_pre.astype(BF)
    value_t = value_pre.T.astype(BF)
    for block in range(SEQ // BLOCK):
        first, end = block * BLOCK, (block + 1) * BLOCK
        bias[:end, :] = bias_block(seg_column[:end, :], seg_row[:, first:end], first, end)
        for head in range(HEADS):
            kv = slice((head // 2) * HD, (head // 2) * HD + HD)
            own = slice(head * HD, head * HD + HD)
            scores = mm_last(key[:end, kv], query[first:end, own]) + bias[:end, :]
            top = jnp.max(scores, axis=0, keepdims=True)
            powers = jnp.exp(scores - top)
            total = jnp.sum(powers, axis=0, keepdims=True)
            share = (powers * (1.0 / total)).astype(BF)
            context_t[own, first:end] = mm(value_t[kv, :end], share).astype(BF)
            log_total[head : head + 1, first:end] = top + jnp.log(total)
        if block == 2:
            gather.forward()
    gather.forward_far()
    context = context_t[...].T
    for block in range(SEQ // BLOCK):
        rows = slice(block * BLOCK, (block + 1) * BLOCK)
        part[rows, :] = mm_last(context[rows, :], weights[:, 512:768]).astype(BF)
    gather.finish()


def attention_forward(hidden, gain, weights, tables, seg_column, seg_row, out_grad, ident):
    vmem = pl.BlockSpec(memory_space=pltpu.VMEM)
    hbm = pl.BlockSpec(memory_space=pl.ANY)
    return pl.pallas_call(
        attention_forward_kernel,
        in_specs=[vmem] * 7 + [hbm],
        out_specs=[vmem] * 7 + [hbm],
        out_shape=[
            jax.ShapeDtypeStruct((SEQ, D), BF),
            jax.ShapeDtypeStruct((SEQ, D), BF),
            jax.ShapeDtypeStruct((SEQ, HEADS * HD), BF),
            jax.ShapeDtypeStruct((SEQ, 128), BF),
            jax.ShapeDtypeStruct((SEQ, 128), BF),
            jax.ShapeDtypeStruct((HEADS * HD, SEQ), BF),
            jax.ShapeDtypeStruct((8, SEQ), F32),
            jax.ShapeDtypeStruct((8, *out_grad.shape), BF),
        ],
        scratch_shapes=[
            pltpu.VMEM((SEQ, BLOCK), F32),
            pltpu.SemaphoreType.DMA((9,)),
            pltpu.SemaphoreType.DMA((9,)),
            pltpu.SemaphoreType.DMA,
        ],
        compiler_params=pltpu.CompilerParams(
            collective_id=ident, has_side_effects=True, vmem_limit_bytes=56 * MIB
        ),
        name="attention_forward",
    )(hidden, gain, weights, *tables, seg_column, seg_row, out_grad)


def attention_backward_kernel(
    dattn, normed, weights, cosine, sine, seg_column, seg_row,
    query, key, value, context_t, log_total, rest, y_part,
    dn1, grads, y, bias, dcontext, dquery_t, dkey, dvalue, dall, dall_t, *refs,
):
    at = Place()
    greet([at.sibling(), at.ring(1), at.ring(3)])
    scatter = RingScatter(at, y_part, refs[:8], *refs[8:])
    grads[:, 768:] = rest[...]
    dcontext[...] = mm(dattn[...], weights[:, 512:768]).astype(BF)
    output_grad_t = mm(context_t[...], dattn[...])
    grads[:, 512:768] = output_grad_t.T.astype(BF)
    key_t = key[...].astype(F32).T.astype(BF)
    dkey[...] = jnp.zeros_like(dkey)
    dvalue[...] = jnp.zeros_like(dvalue)
    for block in range(SEQ // BLOCK):
        first, end = block * BLOCK, (block + 1) * BLOCK
        bias[:end, :] = bias_block(seg_column[:end, :], seg_row[:, first:end], first, end)
        for head in range(HEADS):
            kv = slice((head // 2) * HD, (head // 2) * HD + HD)
            own = slice(head * HD, head * HD + HD)
            query_block = query[first:end, own]
            dcontext_block = dcontext[first:end, own]
            scores = mm_last(key[:end, kv], query_block) + bias[:end, :]
            share = jnp.exp(scores - log_total[head : head + 1, first:end])
            dshare = mm_last(value[:end, kv], dcontext_block)
            centre = jnp.sum(share * dshare, axis=0, keepdims=True)
            dscore = (share * (dshare - centre)).astype(BF)
            dquery_t[own, first:end] = mm(key_t[kv, :end], dscore) * 0.125
            dkey[:end, kv] += mm(dscore, query_block)
            dvalue[:end, kv] += mm(share.astype(BF), dcontext_block)
        if block == 0:
            scatter.far()
        if block == 2:
            scatter.sides()
    turn = -sine[...]
    for half in range(2):
        rows = slice(half * 128, half * 128 + 128)
        piece = rotated(dquery_t[rows, :].T, cosine[...], turn)
        dall[:, rows] = piece.astype(BF)
        dall_t[rows, :] = piece.T.astype(BF)
    piece = rotated(dkey[...], cosine[...], turn)
    dall[:, 256:384] = piece.astype(BF)
    dall_t[256:384, :] = piece.T.astype(BF)
    dall[:, 384:512] = dvalue[...].astype(BF)
    dall_t[384:512, :] = dvalue[...].T.astype(BF)
    grads[:, 0:512] = mm(dall_t[...], normed[...]).T.astype(BF)
    for block in range(SEQ // BLOCK):
        rows = slice(block * BLOCK, (block + 1) * BLOCK)
        dn1[rows, :] = mm_last(dall[rows, :], weights[:, 0:512]).astype(BF)
    scatter.finish(y)


def attention_backward(
    dattn, normed, weights, tables, seg_column, seg_row, kept, rest, y_part, ident
):
    vmem = pl.BlockSpec(memory_space=pltpu.VMEM)
    return pl.pallas_call(
        attention_backward_kernel,
        in_specs=[vmem] * 14,
        out_specs=[vmem] * 3,
        out_shape=[
            jax.ShapeDtypeStruct((SEQ, D), BF),
            jax.ShapeDtypeStruct((D, SMALL), BF),
            jax.ShapeDtypeStruct((LOCAL, D), F32),
        ],
        scratch_shapes=[
            pltpu.VMEM((SEQ, BLOCK), F32),
            pltpu.VMEM((SEQ, HEADS * HD), BF),
            pltpu.VMEM((HEADS * HD, SEQ), F32),
            pltpu.VMEM((SEQ, 128), F32),
            pltpu.VMEM((SEQ, 128), F32),
            pltpu.VMEM((SEQ, 512), BF),
            pltpu.VMEM((512, SEQ), BF),
            *ring_scratch(LOCAL, D),
            pltpu.SemaphoreType.DMA((8,)),
            pltpu.SemaphoreType.DMA((8,)),
        ],
        compiler_params=pltpu.CompilerParams(
            collective_id=ident, has_side_effects=True, vmem_limit_bytes=56 * MIB
        ),
        name="attention_backward",
    )(
        dattn, normed, weights, *tables, seg_column, seg_row, *kept, rest,
        y_part.reshape(8, LOCAL, D),
    )


def experts_kernel(
    x_in, d_in, gating, weights, y_out, dx_out, dgate, grads,
    x, d, xt, dt, y, dx, hidden, load, store,
):
    step = pl.program_id(0)
    rows_at_once = 512
    blocks = TOKENS // rows_at_once
    lane = lax.broadcasted_iota(jnp.int32, (rows_at_once, 128), 1)
    own_first = lax.axis_index("yh") * 16 + step * QUAD

    def rows_of(block):
        return pl.ds(pl.multiple_of(block * rows_at_once, rows_at_once), rows_at_once)

    def loads(block):
        rows = rows_of(block)
        return (
            pltpu.make_async_copy(x_in.at[rows], x.at[rows], load.at[block, 0]),
            pltpu.make_async_copy(d_in.at[rows], d.at[rows], load.at[block, 1]),
        )

    def stores(block):
        rows = rows_of(block)
        return (
            pltpu.make_async_copy(x.at[rows], y_out.at[rows], store.at[block, 0]),
            pltpu.make_async_copy(d.at[rows], dx_out.at[rows], store.at[block, 1]),
        )

    @pl.when(step == 0)
    def _():
        for block in range(blocks):
            for copy in loads(block):
                copy.start()
        dgate[...] = jnp.zeros_like(dgate)

    def tokens_block(block, carry):
        rows = rows_of(block)

        @pl.when(step == 0)
        def _():
            for copy in loads(block):
                copy.wait()
            xt[:, rows] = x[rows, :].T
            dt[:, rows] = d[rows, :].T
            y[rows, :] = jnp.zeros((rows_at_once, D), F32)
            dx[rows, :] = jnp.zeros((rows_at_once, D), F32)

        both = mm(x[rows, :], weights[:, 0 : 2 * F])
        gate, up = both[:, :F], both[:, F:]
        dact = mm(d[rows, :], weights[:, 2 * F :])
        turned = pltpu.roll(gating[rows, :], lax.rem(128 - own_first, 128), 1)
        factor = jnp.concatenate(
            [jnp.broadcast_to(turned[:, i : i + 1], (rows_at_once, FF)) for i in range(QUAD)],
            axis=1,
        )
        q = 1.0 / (1.0 + jnp.exp(-gate))
        silu = gate * q
        act = silu * up
        product = act * dact
        sums = dgate[rows, :]
        for i in range(QUAD):
            own = jnp.sum(product[:, i * FF : (i + 1) * FF], axis=1, keepdims=True)
            sums = jnp.where(lane == own_first + i, own, sums)
        dgate[rows, :] = sums
        dact = dact * factor
        hidden[rows, 0:F] = (dact * up * (q + silu * (1.0 - q))).astype(BF)
        hidden[rows, F : 2 * F] = (dact * silu).astype(BF)
        hidden[rows, 2 * F :] = (act * factor).astype(BF)
        y[rows, :] += mm_last(hidden[rows, 2 * F :], weights[:, 2 * F :])
        dx[rows, :] += mm_last(hidden[rows, 0 : 2 * F], weights[:, 0 : 2 * F])

        @pl.when(step == STEPS - 1)
        def _():
            x[rows, :] = y[rows, :].astype(BF)
            d[rows, :] = dx[rows, :].astype(BF)
            for copy in stores(block):
                copy.start()

        return carry

    lax.fori_loop(0, blocks, tokens_block, 0)

    def grads_block(block, carry):
        rows = pl.ds(pl.multiple_of(block * 512, 512), 512)
        grads[rows, 0 : 2 * F] = mm(xt[rows, :], hidden[:, 0 : 2 * F]).astype(BF)
        grads[rows, 2 * F :] = mm(dt[rows, :], hidden[:, 2 * F :]).astype(BF)
        return carry

    lax.fori_loop(0, D // 512, grads_block, 0)

    @pl.when(step == STEPS - 1)
    def _():
        for block in range(blocks):
            for copy in stores(block):
                copy.wait()


def experts(x, d, gating, weights):
    hbm = pl.BlockSpec(memory_space=pl.ANY)
    whole = pl.BlockSpec((TOKENS, 128), lambda step: (0, 0), pipeline_mode=pl.Buffered(1))
    column = pl.BlockSpec((D, 3 * F), lambda step: (0, step))
    return pl.pallas_call(
        experts_kernel,
        grid=(STEPS,),
        in_specs=[hbm, hbm, whole, column],
        out_specs=[hbm, hbm, whole, column],
        out_shape=[
            jax.ShapeDtypeStruct((TOKENS, D), BF),
            jax.ShapeDtypeStruct((TOKENS, D), BF),
            jax.ShapeDtypeStruct((TOKENS, 128), F32),
            jax.ShapeDtypeStruct((D, STEPS * 3 * F), BF),
        ],
        scratch_shapes=[
            pltpu.VMEM((TOKENS, D), BF),
            pltpu.VMEM((TOKENS, D), BF),
            pltpu.VMEM((D, TOKENS), BF),
            pltpu.VMEM((D, TOKENS), BF),
            pltpu.VMEM((TOKENS, D), F32),
            pltpu.VMEM((TOKENS, D), F32),
            pltpu.VMEM((TOKENS, 3 * F), BF),
            pltpu.SemaphoreType.DMA((TOKENS // 512, 2)),
            pltpu.SemaphoreType.DMA((TOKENS // 512, 2)),
        ],
        compiler_params=pltpu.CompilerParams(vmem_limit_bytes=62 * MIB),
        name="experts",
    )(x, d, gating, weights)


def norm_scale(values):
    return lax.rsqrt(jnp.mean(values * values, axis=-1, keepdims=True) + EPS)


def norm_grad(values, gain, dnormed):
    scale = norm_scale(values)
    unit = values * scale
    weighted = dnormed * gain
    dvalues = scale * (weighted - unit * jnp.mean(weighted * unit, axis=-1, keepdims=True))
    return dvalues, jnp.sum(dnormed * unit, axis=0)


def packed_experts(expert_gate, expert_up, expert_down):
    shares = jnp.stack([expert_gate, expert_up, expert_down])
    shares = shares.reshape(3, 2, STEPS, QUAD, 32, FF)
    return shares.transpose(1, 4, 2, 0, 3, 5).reshape(2, 32, STEPS * 3 * F)


def unpacked_experts(tiles):
    tiles = tiles.reshape(2, 32, STEPS, 3, QUAD, FF).transpose(3, 0, 2, 4, 1, 5)
    tiles = tiles.reshape(3, E, 32, FF).astype(F32)
    return tiles[0], tiles[1], tiles[2]


def on_device(
    hidden_in, out_grad, attn_gain, query_weight, key_weight, value_weight, output_weight,
    moe_gain, router_weight, expert_gate, expert_up, expert_down, expert_ids, segment_ids,
):
    halves = packed_experts(expert_gate, expert_up, expert_down)
    halves = swap_halves(halves, 7)
    expert_weights = lax.all_gather(
        halves.reshape(64, STEPS * 3 * F), PLANE, axis=0, tiled=True
    )
    small = jnp.concatenate(
        [
            query_weight, key_weight, value_weight, output_weight,
            router_weight, attn_gain[:, None], moe_gain[:, None], jnp.zeros((32, 94), BF),
        ],
        axis=1,
    )
    segment = jnp.pad(segment_ids.reshape(2, 128), ((0, 6), (0, 0)))
    hidden_all, segment_all, small = startup(hidden_in, segment, small, 0)
    router = small[:, 768:800]
    attn_gain_all = small[:, 800].astype(F32)
    moe_gain_all = small[:, 801].astype(F32)
    tables = tuple(jnp.asarray(t) for t in rotary_tables())
    segments = segment_all[:, :2].reshape(SEQ)
    seg_column, seg_row = segments[:, None], segments[None, :]

    part, normed_all, *kept, d = attention_forward(
        hidden_all, attn_gain_all[None, :], small, tables, seg_column, seg_row, out_grad, 1
    )
    d = d.reshape(TOKENS, D)
    hidden = hidden_in.astype(F32)
    middle = hidden + scatter_pair(part, 2)
    normed_moe = (middle * norm_scale(middle) * moe_gain_all).astype(BF)
    logits = mm(normed_moe, router)
    named = jnp.any(
        expert_ids[:, :, None] == jnp.arange(E, dtype=jnp.int32)[None, None, :], axis=1
    )
    top = jnp.max(jnp.where(named, logits, -jnp.inf), axis=-1, keepdims=True)
    powers = jnp.where(named, jnp.exp(logits - top), 0.0)
    gating = powers / jnp.sum(powers, axis=-1, keepdims=True)

    x, gating_all = gather_ring([normed_moe, jnp.pad(gating, ((0, 0), (0, 96)))], 3)
    y, dx, dgate, expert_grads = experts(x, d, gating_all, expert_weights)
    expert_grads = lax.psum_scatter(expert_grads, PLANE, scatter_dimension=0, tiled=True)

    sums = scatter_ring(jnp.concatenate([dx, dgate.astype(BF)], axis=1), 4)
    dgate = sums[:, D : D + E]
    dchosen = gating * (dgate - jnp.sum(gating * dgate, axis=-1, keepdims=True))
    dlogits = dchosen.astype(BF)
    dnormed_moe = sums[:, :D] + mm_last(dlogits, router)
    dmiddle, moe_gain_part = norm_grad(middle, moe_gain_all, dnormed_moe)
    dmiddle = dmiddle + out_grad.astype(F32)
    dattn = gather_pair(dmiddle.astype(BF), 5)
    router_part = lax.dot_general(
        normed_moe, dlogits, (((0,), (0,)), ((), ())), preferred_element_type=F32
    )
    rest = jnp.concatenate(
        [router_part, moe_gain_part[:, None], jnp.zeros((D, 95), F32)], axis=1
    )
    dn1, grads, y = attention_backward(
        dattn, normed_all, small, tables, seg_column, seg_row, kept, rest.astype(BF), y, 8
    )
    block_out = (middle + y).astype(BF)
    own_weights = jnp.concatenate([query_weight, key_weight, value_weight], axis=1)
    dn1, attention_grads, rest = final(dn1, grads, own_weights, 6)
    dhidden, _ = norm_grad(hidden, attn_gain_all, dn1)
    hidden_grad = dmiddle + dhidden
    expert_grads = unpacked_experts(
        swap_halves(expert_grads.reshape(2, 32, STEPS * 3 * F), 9)
    )
    return (
        block_out,
        hidden_grad,
        rest[:, 33] / attn_gain.astype(F32),
        attention_grads[:, 0:256],
        attention_grads[:, 256:384],
        attention_grads[:, 384:512],
        attention_grads[:, 512:768],
        rest[:, 32],
        rest[:, :32],
        *expert_grads,
    )


def solution(mesh):
    fine = Mesh(np.asarray(mesh.devices).reshape(4, 4, 2, 2, 2), ALL)
    return jax.shard_map(
        on_device,
        mesh=fine,
        in_specs=(
            P(ALL, None),
            P(ALL, None),
            P(DP),
            P(DP, TENSOR),
            P(DP, TENSOR),
            P(DP, TENSOR),
            P(DP, TENSOR),
            P(DP),
            P(DP, None),
            P(None, DP, TENSOR),
            P(None, DP, TENSOR),
            P(None, DP, TENSOR),
            P(ALL, None),
            P(ALL),
        ),
        out_specs=(
            P(ALL, None),
            P(ALL, None),
            P(DP),
            P(DP, TENSOR),
            P(DP, TENSOR),
            P(DP, TENSOR),
            P(DP, TENSOR),
            P(DP),
            P(DP, None),
            P(None, DP, TENSOR),
            P(None, DP, TENSOR),
            P(None, DP, TENSOR),
        ),
        check_vma=False,
    )
```

```python
import jax
import jax.numpy as jnp
import numpy as np
from jax import lax
from jax.experimental import pallas as pl
from jax.experimental.pallas import tpu as pltpu
from jax.sharding import Mesh
from jax.sharding import PartitionSpec as P

D = 1024
HD = 64
E = 32
SEQ = 1024
LOCAL = 256
HEADS = 4
QUAD = 4
FF = 128
F = QUAD * FF
EPS = 1e-06
MASKED = -1e30
BLOCK = 256
TOKENS = 2048
STEPS = 4

DP = ("x", "z", "yh")
TENSOR = ("yl", "core")
RING = ("yh", "yl", "core")
PLANE = ("x", "z")
ALL = ("x", "z", "yh", "yl", "core")

F32 = jnp.float32
BF = jnp.bfloat16
LAST = (((1,), (1,)), ((), ()))
MIB = 1024 * 1024
MESH = pl.DeviceIdType.MESH
SMALL = 896


def mm(a, b):
    return jnp.dot(a, b, preferred_element_type=F32)


def mm_last(a, b):
    return lax.dot_general(a, b, LAST, preferred_element_type=F32)


class Place:
    def __init__(self):
        self.x = lax.axis_index("x")
        self.z = lax.axis_index("z")
        self.yh = lax.axis_index("yh")
        self.yl = lax.axis_index("yl")
        self.core = lax.axis_index("core")
        self.y = self.yh * 2 + self.yl

    def chip(self, k):
        return lax.rem(self.y + k, 4)

    def ring(self, k):
        chip = self.chip(k)
        return {"yh": chip // 2, "yl": lax.rem(chip, 2)}

    def along(self, axis, k):
        return {axis: lax.rem(getattr(self, axis) + k, 4)}

    def sibling(self):
        return {"core": 1 - self.core}

    def partner(self):
        return {"yl": 1 - self.yl}

    def diagonal(self):
        return {"yl": 1 - self.yl, "core": 1 - self.core}

    def opposite(self):
        return {"yh": 1 - self.yh}


def greet(devices):
    barrier = pltpu.get_barrier_semaphore()
    for device in devices:
        pl.semaphore_signal(barrier, inc=1, device_id=device, device_id_type=MESH)
    pl.semaphore_wait(barrier, len(devices))


def remote(src, dst, send, recv, i, device):
    return pltpu.make_async_remote_copy(
        src_ref=src, dst_ref=dst, send_sem=send.at[i], recv_sem=recv.at[i],
        device_id=device, device_id_type=MESH,
    )


def push(src, dst, send, recv, i, device):
    copy = remote(src, dst, send, recv, i, device)
    copy.start()
    return copy


def keep(src, dst, sem):
    copy = pltpu.make_async_copy(src, dst, sem)
    copy.start()
    return copy


class RingGather:
    def __init__(self, at, own, out, send, recv, here, base=0):
        self.at, self.own, self.out, self.base = at, own, out, base
        self.send, self.recv, self.here = send, recv, here
        half = own.shape[0] // 2
        lo, hi = pl.ds(0, half), pl.ds(half, half)
        me, before, behind, across = (out.at[self.slot(k)] for k in (0, 3, 1, 2))
        near, up, down = at.sibling(), at.ring(1), at.ring(3)
        self.plan = [
            (own, me, near),
            (own, me, up),
            (own, me, down),
            (before.at[lo], before.at[lo], up),
            (before, before, near),
            (behind.at[hi], behind.at[hi], down),
            (behind, behind, near),
            (across.at[lo], across.at[lo], near),
            (across.at[hi], across.at[hi], near),
        ]

    def slot(self, k):
        return self.at.chip(k) * 2 + self.at.core

    def copy(self, i):
        src, dst, device = self.plan[i]
        return remote(src, dst, self.send, self.recv, self.base + i, device)

    def kept(self):
        return pltpu.make_async_copy(self.own, self.out.at[self.slot(0)], self.here)

    def begin(self):
        self.kept().start()
        for i in (1, 2, 0):
            self.copy(i).start()

    def forward_before(self):
        self.copy(1).wait_recv()
        self.copy(3).start()
        self.copy(4).start()

    def forward_behind(self):
        self.copy(2).wait_recv()
        self.copy(5).start()
        self.copy(6).start()

    def forward_across(self):
        self.copy(3).wait_recv()
        self.copy(7).start()
        self.copy(5).wait_recv()
        self.copy(8).start()

    def sent(self):
        for i in range(9):
            self.copy(i).wait_send()


class PairGather:
    def __init__(self, at, own, out, send, recv, here, base, pieces):
        self.at, self.out, self.send, self.recv, self.base = at, out, send, recv, base
        size = own.shape[0] // pieces
        self.parts = [pl.ds(i * size, size) for i in range(pieces)]
        me = at.yl * 2 + at.core
        self.other = (1 - at.yl) * 2 + at.core
        self.kept = keep(own, out.at[me], here)
        self.far = [
            push(own.at[part], out.at[me, part], send, recv, base + 1 + i, at.partner())
            for i, part in enumerate(self.parts)
        ]
        self.near = [push(own, out.at[me], send, recv, base, at.sibling())]

    def forward(self):
        for i, part in enumerate(self.parts):
            self.far[i].wait_recv()
            view = self.out.at[self.other, part]
            index = self.base + 1 + len(self.parts) + i
            self.near.append(push(view, view, self.send, self.recv, index, self.at.sibling()))

    def finish(self):
        for copy in self.near:
            copy.wait_recv()
        for copy in (*self.far, *self.near):
            copy.wait_send()
        self.kept.wait()


PIECES = 4


class AxisGather:
    def __init__(self, at, axis, view, send, recv, base):
        self.up, self.down = at.along(axis, 1), at.along(axis, 3)
        self.view, self.send, self.recv, self.base = view, send, recv, base

    def go(self, i, view, device):
        return push(view, view, self.send, self.recv, self.base + i, device)

    def begin(self):
        self.first = [
            self.go(0, self.view(0, "all"), self.up), self.go(1, self.view(0, "all"), self.down),
        ]

    def finish(self):
        self.first[0].wait_recv()
        far_up = self.go(2, self.view(3, "low"), self.up)
        self.first[1].wait_recv()
        far_down = self.go(3, self.view(1, "high"), self.down)
        far_up.wait_recv()
        far_down.wait_recv()
        for copy in (*self.first, far_up, far_down):
            copy.wait_send()


def halves_of(ref, first, size):
    spans = {"all": (0, size), "low": (0, size // 2), "high": (size // 2, size // 2)}
    return lambda part: ref.at[pl.ds(first + spans[part][0], spans[part][1])]


def first_kernel(gate, up, down, small, experts_all, small_all, send, recv, here):
    at = Place()
    greet([at.opposite(), at.along("z", 1), at.along("z", 3)])
    own_rows = pl.ds(at.yh * 32, 32)
    first = (at.x * 4 + at.z) * 2
    mine = small_all.at[at.z * 2 + at.yh]
    small_kept = keep(small, mine, here.at[3])
    copies = [push(small, mine, send, recv, 0, at.opposite())]
    kept = []
    for i, share in enumerate((gate, up, down)):
        dst = experts_all.at[i, :, own_rows]
        copies.append(
            push(share.at[pl.ds((1 - at.yh) * 16, 16)], dst, send, recv, 1 + i, at.opposite())
        )
        kept.append(keep(share.at[pl.ds(at.yh * 16, 16)], dst, here.at[i]))
    small_kept.wait()
    copies[0].wait_recv()
    over_z = AxisGather(
        at, "z", lambda k, part: halves_of(small_all, lax.rem(at.z + k, 4) * 2, 2)(part),
        send, recv, 4,
    )
    over_z.begin()
    over_z.finish()
    for copy in copies[1:]:
        copy.wait_recv()
    for copy in copies:
        copy.wait_send()
    for copy in kept:
        copy.wait()


def first_exchange(gate, up, down, small, ident):
    hbm = pl.BlockSpec(memory_space=pl.ANY)
    return pl.pallas_call(
        first_kernel,
        in_specs=[hbm] * 4,
        out_specs=[hbm] * 2,
        out_shape=[
            jax.ShapeDtypeStruct((3, 16, 64, FF), BF),
            jax.ShapeDtypeStruct((8, 32, SMALL), BF),
        ],
        scratch_shapes=[
            pltpu.SemaphoreType.DMA((8,)),
            pltpu.SemaphoreType.DMA((8,)),
            pltpu.SemaphoreType.DMA((4,)),
        ],
        compiler_params=pltpu.CompilerParams(collective_id=ident, has_side_effects=True),
        name="first_exchange",
    )(gate, up, down, small)


def startup_kernel(
    hidden, segment, out_grad, small, hidden_all, segment_all, out_grad_all, small_all,
    send, recv, here,
):
    at = Place()
    greet(
        [
            at.sibling(), at.partner(), at.diagonal(), at.ring(1), at.ring(3),
            at.along("x", 1), at.along("x", 3),
        ]
    )
    rank = at.yl * 2 + at.core
    pair = PairGather(at, hidden, hidden_all, send, recv, here.at[0], 0, PIECES)
    base = 1 + 2 * PIECES
    seg_here = keep(segment, segment_all.at[rank], here.at[1])
    copies = [
        push(segment, segment_all.at[rank], send, recv, base + i, device)
        for i, device in enumerate((at.sibling(), at.partner(), at.diagonal()))
    ]
    small_kept = keep(small, small_all.at[pl.ds(at.x * 8, 8)], here.at[2])
    small_kept.wait()
    over_x = AxisGather(
        at, "x", lambda k, part: halves_of(small_all, lax.rem(at.x + k, 4) * 8, 8)(part),
        send, recv, base + 3,
    )
    over_x.begin()
    ring = RingGather(at, out_grad, out_grad_all, send, recv, here.at[3], base + 7)
    ring.begin()
    pair.forward()
    over_x.finish()
    ring.forward_before()
    ring.forward_behind()
    pair.finish()
    seg_here.wait()
    for copy in copies:
        copy.wait_recv()
    ring.forward_across()
    for i in (0, 4, 6, 7, 8):
        ring.copy(i).wait_recv()
    ring.sent()
    ring.kept().wait()
    for copy in copies:
        copy.wait_send()


def startup(hidden, segment, out_grad, small, ident):
    hbm = pl.BlockSpec(memory_space=pl.ANY)
    sems = 1 + 2 * PIECES + 3 + 4 + 9
    hidden_all, segment_all, out_grad_all, small_all = pl.pallas_call(
        startup_kernel,
        in_specs=[hbm] * 4,
        out_specs=[hbm] * 4,
        out_shape=[
            jax.ShapeDtypeStruct((4, *hidden.shape), hidden.dtype),
            jax.ShapeDtypeStruct((4, *segment.shape), segment.dtype),
            jax.ShapeDtypeStruct((8, *out_grad.shape), out_grad.dtype),
            jax.ShapeDtypeStruct((32, 32, SMALL), small.dtype),
        ],
        scratch_shapes=[
            pltpu.SemaphoreType.DMA((sems,)),
            pltpu.SemaphoreType.DMA((sems,)),
            pltpu.SemaphoreType.DMA((4,)),
        ],
        compiler_params=pltpu.CompilerParams(collective_id=ident, has_side_effects=True),
        name="startup",
    )(hidden, segment, out_grad, small)
    return hidden_all.reshape(SEQ, D), segment_all, out_grad_all, small_all.reshape(D, SMALL)


class RingScatter:
    def __init__(self, at, part, scratch, send, recv, base=0):
        self.at, self.part, self.send, self.recv, self.base = at, part, send, recv, base
        near, half_a, half_b, self.full_up, self.full_down = scratch[:5]
        to_far, to_up, to_down = scratch[5:] or [
            part.at[at.chip(k) * 2 + at.core] for k in (2, 1, 3)
        ]
        self.near, self.half_a, self.half_b = near, half_a, half_b
        self.to_far, self.to_up, self.to_down = to_far, to_up, to_down
        self.half = half_a.shape[0]
        self.lo, self.hi = pl.ds(0, self.half), pl.ds(self.half, self.half)
        up, down = at.ring(1), at.ring(3)
        self.plan = {
            k: (part.at[at.chip(k) * 2 + 1 - at.core], near.at[k], at.sibling()) for k in range(4)
        }
        self.plan[4] = (to_far.at[self.lo], half_a, up)
        self.plan[5] = (to_far.at[self.hi], half_b, down)
        self.plan[6] = (to_up, self.full_up, up)
        self.plan[7] = (to_down, self.full_down, down)

    def copy(self, i):
        src, dst, device = self.plan[i]
        return remote(src, dst, self.send, self.recv, self.base + i, device)

    def chip_sum(self, k):
        self.copy(k).wait_recv()
        own = self.part[self.at.chip(k) * 2 + self.at.core]
        return own.astype(F32) + self.near[k].astype(F32)

    def far(self):
        self.to_far[...] = self.chip_sum(2).astype(BF)
        self.copy(4).start()
        self.copy(5).start()

    def up_side(self):
        total = self.chip_sum(1)
        self.copy(4).wait_recv()
        self.to_up[self.lo, :] = (total[: self.half] + self.half_a[...].astype(F32)).astype(BF)
        self.to_up[self.hi, :] = total[self.half :].astype(BF)
        self.copy(6).start()

    def down_side(self):
        total = self.chip_sum(3)
        self.copy(5).wait_recv()
        self.to_down[self.lo, :] = total[: self.half].astype(BF)
        self.to_down[self.hi, :] = (total[self.half :] + self.half_b[...].astype(F32)).astype(BF)
        self.copy(7).start()

    def finish(self, out):
        out[...] = self.chip_sum(0)
        self.copy(6).wait_recv()
        out[...] += self.full_up[...].astype(F32)
        self.copy(7).wait_recv()
        out[...] += self.full_down[...].astype(F32)
        for i in range(8):
            self.copy(i).wait_send()


def ring_scratch(rows, columns, own_sends=True):
    block, half = pltpu.VMEM((rows, columns), BF), pltpu.VMEM((rows // 2, columns), BF)
    scratch = [pltpu.VMEM((4, rows, columns), BF), half, half, block, block]
    return scratch + [block] * 3 if own_sends else scratch


class PairScatter:
    def __init__(self, at, part, scratch, send, recv):
        self.at, self.part, self.send, self.recv = at, part, send, recv
        self.near, self.far_rows, self.to_far = scratch
        size = self.to_far.shape[0] // PIECES
        self.parts = [pl.ds(i * size, size) for i in range(PIECES)]
        self.other, self.own = (1 - at.yl) * 2, at.yl * 2
        self.first = [
            push(
                part.at[self.other + 1 - at.core, rows], self.near.at[1, rows],
                send, recv, i, at.sibling(),
            )
            for i, rows in enumerate(self.parts)
        ]
        self.second = push(
            part.at[self.own + 1 - at.core], self.near.at[0], send, recv, PIECES, at.sibling()
        )

    def forward(self):
        at = self.at
        self.sent = []
        for i, rows in enumerate(self.parts):
            self.first[i].wait_recv()
            own = self.part[self.other + at.core, rows, :].astype(F32)
            self.to_far[rows, :] = (own + self.near[1, rows, :].astype(F32)).astype(BF)
            self.sent.append(
                push(
                    self.to_far.at[rows], self.far_rows.at[rows], self.send, self.recv,
                    PIECES + 1 + i, at.partner(),
                )
            )

    def finish(self, out):
        self.second.wait_recv()
        out[...] = self.part[self.own + self.at.core].astype(F32) + self.near[0].astype(F32)
        for i, rows in enumerate(self.parts):
            self.sent[i].wait_recv()
            out[rows, :] += self.far_rows[rows, :].astype(F32)
        for copy in (*self.first, self.second, *self.sent):
            copy.wait_send()


def pair_scratch(rows, columns):
    block = pltpu.VMEM((rows, columns), BF)
    return [pltpu.VMEM((2, rows, columns), BF), block, block]


def gain_rows(small):
    return small[:, 768:896].astype(F32).T[32:40, :]


def column_of(row):
    return jnp.broadcast_to(row, (8, row.shape[1])).T[:, 0:1]


def middle_kernel(part, hidden, small, named, middle, normed, gating, *refs):
    at = Place()
    greet([at.sibling(), at.partner()])
    scatter = PairScatter(at, part, refs[:3], *refs[3:])
    gains = gain_rows(small)
    scatter.forward()
    scatter.finish(middle)
    values = middle[...] + hidden[...].astype(F32)
    middle[...] = values
    scale = lax.rsqrt(jnp.mean(values * values, axis=-1, keepdims=True) + EPS)
    normed[...] = (values * scale * gains[1:2, :]).astype(BF)
    chosen = named[...] > 0.0
    logits = jnp.where(chosen, mm(normed[...], small[:, 768:896]), MASKED)
    powers = jnp.where(chosen, jnp.exp(logits - jnp.max(logits, axis=-1, keepdims=True)), 0.0)
    gating[...] = powers / jnp.sum(powers, axis=-1, keepdims=True)


def middle_of(part, hidden, small, named, ident):
    vmem = pl.BlockSpec(memory_space=pltpu.VMEM)
    return pl.pallas_call(
        middle_kernel,
        in_specs=[vmem] * 4,
        out_specs=[vmem] * 3,
        out_shape=[
            jax.ShapeDtypeStruct((LOCAL, D), F32),
            jax.ShapeDtypeStruct((LOCAL, D), BF),
            jax.ShapeDtypeStruct((LOCAL, 128), F32),
        ],
        scratch_shapes=[
            *pair_scratch(LOCAL, D),
            pltpu.SemaphoreType.DMA((1 + 2 * PIECES,)),
            pltpu.SemaphoreType.DMA((1 + 2 * PIECES,)),
        ],
        compiler_params=pltpu.CompilerParams(
            collective_id=ident, has_side_effects=True, vmem_limit_bytes=40 * MIB
        ),
        name="middle",
    )(part.reshape(4, LOCAL, D), hidden, small, named)


def dmiddle_kernel(
    dx, dgate, gating, middle, normed, out_grad, small, dattn_all, dmiddle, rest,
    dattn, send, recv, here,
):
    at = Place()
    greet([at.sibling(), at.partner()])
    gain = gain_rows(small)[1:2, :]
    share = gating[...]
    dchosen = share * (dgate[...] - jnp.sum(share * dgate[...], axis=-1, keepdims=True))
    dlogits = dchosen.astype(BF)
    dnormed = dx[...] + mm_last(dlogits, small[:, 768:896])
    values = middle[...]
    scale = lax.rsqrt(jnp.mean(values * values, axis=-1, keepdims=True) + EPS)
    unit = values * scale
    weighted = dnormed * gain
    inner = jnp.mean(weighted * unit, axis=-1, keepdims=True)
    total = out_grad[...].astype(F32) + scale * (weighted - unit * inner)
    dmiddle[...] = total
    dattn[...] = total.astype(BF)
    gather = PairGather(at, dattn, dattn_all, send, recv, here, 0, PIECES)
    router_part = mm(normed[...].T, dlogits)
    gain_part = column_of(jnp.sum(dnormed * unit, axis=0, keepdims=True))
    lane = lax.broadcasted_iota(jnp.int32, (D, 128), 1)
    rest[...] = jnp.where(lane == 32, gain_part, router_part).astype(BF)
    gather.forward()
    gather.finish()


def dmiddle_of(dx, dgate, gating, middle, normed, out_grad, small, ident):
    vmem = pl.BlockSpec(memory_space=pltpu.VMEM)
    dattn, dmiddle, rest = pl.pallas_call(
        dmiddle_kernel,
        in_specs=[vmem] * 7,
        out_specs=[vmem] * 3,
        out_shape=[
            jax.ShapeDtypeStruct((4, LOCAL, D), BF),
            jax.ShapeDtypeStruct((LOCAL, D), F32),
            jax.ShapeDtypeStruct((D, 128), BF),
        ],
        scratch_shapes=[
            pltpu.VMEM((LOCAL, D), BF),
            pltpu.SemaphoreType.DMA((1 + 2 * PIECES,)),
            pltpu.SemaphoreType.DMA((1 + 2 * PIECES,)),
            pltpu.SemaphoreType.DMA,
        ],
        compiler_params=pltpu.CompilerParams(
            collective_id=ident, has_side_effects=True, vmem_limit_bytes=40 * MIB
        ),
        name="dmiddle",
    )(dx, dgate, gating, middle, normed, out_grad, small)
    return dattn.reshape(SEQ, D), dmiddle, rest


class AxisScatter:
    def __init__(self, at, axis, part, scratch, send, recv, base):
        self.at, self.axis, self.part, self.base = at, axis, part, base
        self.send, self.recv = send, recv
        self.half_a, self.half_b, self.up, self.down, self.to_up, self.to_down = scratch
        self.half = part.shape[1] // 2
        lo, hi = pl.ds(0, self.half), pl.ds(self.half, self.half)
        far = part.at[self.to(2)]
        self.far_up = self.go(0, far.at[lo], self.half_a, 1)
        self.far_down = self.go(1, far.at[hi], self.half_b, 3)

    def to(self, k):
        return self.at.along(self.axis, k)[self.axis]

    def go(self, i, src, dst, k):
        return push(src, dst, self.send, self.recv, self.base + i, self.at.along(self.axis, k))

    def sides(self):
        h = self.half
        self.far_up.wait_recv()
        block = self.part[self.to(1)]
        self.to_up[:h] = (block[:h].astype(F32) + self.half_a[...].astype(F32)).astype(BF)
        self.to_up[h:] = block[h:]
        self.sent_up = self.go(2, self.to_up, self.up, 1)
        self.far_down.wait_recv()
        block = self.part[self.to(3)]
        self.to_down[:h] = block[:h]
        self.to_down[h:] = (block[h:].astype(F32) + self.half_b[...].astype(F32)).astype(BF)
        self.sent_down = self.go(3, self.to_down, self.down, 3)

    def finish(self):
        total = self.part[self.to(0)].astype(F32)
        self.sent_up.wait_recv()
        self.sent_down.wait_recv()
        total = total + self.up[...].astype(F32) + self.down[...].astype(F32)
        for copy in (self.far_up, self.far_down, self.sent_up, self.sent_down):
            copy.wait_send()
        return total


def axis_scratch(*block):
    half = (block[0] // 2, *block[1:])
    return [pltpu.VMEM(half, BF)] * 2 + [pltpu.VMEM(block, BF)] * 4


def final_kernel(
    part, grads, weights, dn1, attention, rest,
    over_z, over_y, from_opposite, share, shares, *refs,
):
    at = Place()
    greet(
        [
            at.sibling(), at.partner(), at.diagonal(), at.opposite(),
            at.along("z", 1), at.along("z", 3), at.along("x", 1), at.along("x", 3),
        ]
    )
    pair_refs, x_refs, z_refs = refs[:3], refs[3:9], refs[9:15]
    send, recv = refs[15:]
    base = 1 + 2 * PIECES
    x_scatter = AxisScatter(at, "x", grads, x_refs, send, recv, base)
    pair = PairScatter(at, part, pair_refs, send, recv)
    pair.forward()
    x_scatter.sides()
    over_z[...] = x_scatter.finish().astype(BF).reshape(over_z.shape)
    z_scatter = AxisScatter(at, "z", over_z, z_refs, send, recv, base + 4)
    z_scatter.sides()
    over_y[...] = z_scatter.finish().astype(BF)
    swap = push(over_y.at[1 - at.yh], from_opposite, send, recv, base + 8, at.opposite())
    swap.wait_recv()
    total = over_y[at.yh].astype(F32) + from_opposite[...].astype(F32)
    attention[...] = total[:, :768]
    gain_part = jnp.sum(total[:, :512] * weights[...].astype(F32), axis=1, keepdims=True)
    lane = lax.broadcasted_iota(jnp.int32, (32, 128), 1)
    share[...] = jnp.where(lane == 33, gain_part, total[:, 768:])
    copies = [
        push(share, shares.at[i], send, recv, base + 9 + i, device)
        for i, device in enumerate((at.sibling(), at.partner(), at.diagonal()))
    ]
    pair.finish(dn1)
    rest[...] = share[...]
    for i, copy in enumerate(copies):
        copy.wait_recv()
        rest[...] += shares[i]
    for copy in (swap, *copies):
        copy.wait_send()


def final(part, grads, weights, ident):
    vmem = pl.BlockSpec(memory_space=pltpu.VMEM)
    width = grads.shape[1]
    sems = 1 + 2 * PIECES + 12
    return pl.pallas_call(
        final_kernel,
        in_specs=[vmem] * 3,
        out_specs=[vmem] * 3,
        out_shape=[
            jax.ShapeDtypeStruct((LOCAL, D), F32),
            jax.ShapeDtypeStruct((32, 768), F32),
            jax.ShapeDtypeStruct((32, 128), F32),
        ],
        scratch_shapes=[
            pltpu.VMEM((4, 2, 32, width), BF),
            pltpu.VMEM((2, 32, width), BF),
            pltpu.VMEM((32, width), BF),
            pltpu.VMEM((32, 128), F32),
            pltpu.VMEM((3, 32, 128), F32),
            *pair_scratch(LOCAL, D),
            *axis_scratch(8, 32, width),
            *axis_scratch(2, 32, width),
            pltpu.SemaphoreType.DMA((sems,)),
            pltpu.SemaphoreType.DMA((sems,)),
        ],
        compiler_params=pltpu.CompilerParams(
            collective_id=ident, has_side_effects=True, vmem_limit_bytes=32 * MIB
        ),
        name="final",
    )(part.reshape(4, LOCAL, D), grads.reshape(4, 8, 32, width), weights)


def last_kernel(grads, gate, up, down, send, recv, here):
    at = Place()
    greet([at.opposite()])
    half = pl.ds(at.yh * 16, 16)
    kept, copies = [], []
    for i, out in enumerate((gate, up, down)):
        theirs = grads.at[i, :, pl.ds((1 - at.yh) * 32, 32)]
        copies.append(push(theirs, out.at[half], send, recv, i, at.opposite()))
        kept.append(keep(grads.at[i, :, pl.ds(at.yh * 32, 32)], out.at[half], here.at[i]))
    for copy in (*copies, *kept):
        copy.wait()


def last_exchange(grads, ident):
    hbm = pl.BlockSpec(memory_space=pl.ANY)
    return pl.pallas_call(
        last_kernel,
        in_specs=[hbm],
        out_specs=[hbm] * 3,
        out_shape=[jax.ShapeDtypeStruct((E, 32, FF), BF)] * 3,
        scratch_shapes=[
            pltpu.SemaphoreType.DMA((3,)),
            pltpu.SemaphoreType.DMA((3,)),
            pltpu.SemaphoreType.DMA((3,)),
        ],
        compiler_params=pltpu.CompilerParams(collective_id=ident, has_side_effects=True),
        name="last_exchange",
    )(grads)


def rotary_tables():
    half = HD // 2
    inverse = (10000.0 ** (-(np.arange(half, dtype=np.float64) * 2.0) / HD)).astype(np.float32)
    angles = np.arange(SEQ, dtype=np.float32)[:, None] * inverse[None, :]
    cosine, sine = np.cos(angles), np.sin(angles)
    wide_cosine = np.concatenate([cosine] * 4, axis=1)
    wide_sine = np.concatenate([-sine, sine] * 2, axis=1)
    return wide_cosine.astype(np.float32), wide_sine.astype(np.float32)


def swapped(values):
    lane = lax.broadcasted_iota(jnp.int32, values.shape, 1)
    low = (lane % HD) < HD // 2
    return jnp.where(low, pltpu.roll(values, 96, 1), pltpu.roll(values, 32, 1))


def rotated(values, cosine, sine):
    return values * cosine + swapped(values) * sine


def bias_block(key_segment, query_segment, first, rows):
    key_at = lax.broadcasted_iota(jnp.int32, (rows, BLOCK), 0)
    query_at = lax.broadcasted_iota(jnp.int32, (rows, BLOCK), 1) + first
    allowed = (key_segment == query_segment) & (key_at <= query_at)
    return jnp.where(allowed, 0.0, MASKED)


def segment_row(segments):
    return jnp.concatenate(
        [segments[rank, i : i + 1, :] for rank in range(4) for i in range(2)], axis=1
    ).astype(F32)


def attention_forward_kernel(
    hidden, weights, cosine, sine, segments,
    part, normed, query, key, value, context_t, log_total, bias,
):
    gain = gain_rows(weights)[0:1, :]
    seg_row = segment_row(segments)
    seg_column = column_of(seg_row)
    for block in range(SEQ // BLOCK):
        rows = slice(block * BLOCK, (block + 1) * BLOCK)
        values = hidden[rows, :].astype(F32)
        scale = lax.rsqrt(jnp.mean(values * values, axis=-1, keepdims=True) + EPS)
        normed[rows, :] = (values * scale * gain).astype(BF)
    for half in range(2):
        columns = slice(half * 128, half * 128 + 128)
        pre = mm(normed[...], weights[:, columns])
        query[:, columns] = (rotated(pre, cosine[...], sine[...]) * 0.125).astype(BF)
    key_pre = mm(normed[...], weights[:, 256:384])
    key[...] = rotated(key_pre, cosine[...], sine[...]).astype(BF)
    value_pre = mm(normed[...], weights[:, 384:512])
    value[...] = value_pre.astype(BF)
    value_t = value_pre.T.astype(BF)
    for block in range(SEQ // BLOCK):
        first, end = block * BLOCK, (block + 1) * BLOCK
        bias[:end, :] = bias_block(seg_column[:end, :], seg_row[:, first:end], first, end)
        for head in range(HEADS):
            kv = slice((head // 2) * HD, (head // 2) * HD + HD)
            own = slice(head * HD, head * HD + HD)
            scores = mm_last(key[:end, kv], query[first:end, own]) + bias[:end, :]
            top = jnp.max(scores, axis=0, keepdims=True)
            powers = jnp.exp(scores - top)
            total = jnp.sum(powers, axis=0, keepdims=True)
            share = (powers * (1.0 / total)).astype(BF)
            context_t[own, first:end] = mm(value_t[kv, :end], share).astype(BF)
            log_total[head : head + 1, first:end] = top + jnp.log(total)
    context = context_t[...].T
    for block in range(SEQ // BLOCK):
        rows = slice(block * BLOCK, (block + 1) * BLOCK)
        part[rows, :] = mm_last(context[rows, :], weights[:, 512:768]).astype(BF)


def attention_forward(hidden, weights, tables, segments):
    vmem = pl.BlockSpec(memory_space=pltpu.VMEM)
    return pl.pallas_call(
        attention_forward_kernel,
        in_specs=[vmem] * 5,
        out_specs=[vmem] * 7,
        out_shape=[
            jax.ShapeDtypeStruct((SEQ, D), BF),
            jax.ShapeDtypeStruct((SEQ, D), BF),
            jax.ShapeDtypeStruct((SEQ, HEADS * HD), BF),
            jax.ShapeDtypeStruct((SEQ, 128), BF),
            jax.ShapeDtypeStruct((SEQ, 128), BF),
            jax.ShapeDtypeStruct((HEADS * HD, SEQ), BF),
            jax.ShapeDtypeStruct((8, SEQ), F32),
        ],
        scratch_shapes=[pltpu.VMEM((SEQ, BLOCK), F32)],
        compiler_params=pltpu.CompilerParams(vmem_limit_bytes=56 * MIB),
        name="attention_forward",
    )(hidden, weights, *tables, segments)


def attention_backward_kernel(
    dattn, normed, weights, cosine, sine, segments,
    query, key, value, context_t, log_total, rest, y_part,
    dn1, grads, y, bias, dcontext, dquery_t, dkey, dvalue, dall, dall_t, *refs,
):
    at = Place()
    greet([at.sibling(), at.ring(1), at.ring(3)])
    scatter = RingScatter(at, y_part, refs[:8], *refs[8:])
    for k in (2, 1, 3, 0):
        scatter.copy(k).start()
    seg_row = segment_row(segments)
    seg_column = column_of(seg_row)
    grads[:, 768:] = rest[...]
    dcontext[...] = mm(dattn[...], weights[:, 512:768]).astype(BF)
    scatter.far()
    output_grad_t = mm(context_t[...], dattn[...])
    grads[:, 512:768] = output_grad_t.T.astype(BF)
    key_t = key[...].astype(F32).T.astype(BF)
    dkey[...] = jnp.zeros_like(dkey)
    dvalue[...] = jnp.zeros_like(dvalue)
    for block in range(SEQ // BLOCK):
        first, end = block * BLOCK, (block + 1) * BLOCK
        bias[:end, :] = bias_block(seg_column[:end, :], seg_row[:, first:end], first, end)
        for head in range(HEADS):
            kv = slice((head // 2) * HD, (head // 2) * HD + HD)
            own = slice(head * HD, head * HD + HD)
            query_block = query[first:end, own]
            dcontext_block = dcontext[first:end, own]
            scores = mm_last(key[:end, kv], query_block) + bias[:end, :]
            share = jnp.exp(scores - log_total[head : head + 1, first:end])
            dshare = mm_last(value[:end, kv], dcontext_block)
            centre = jnp.sum(share * dshare, axis=0, keepdims=True)
            dscore = (share * (dshare - centre)).astype(BF)
            dquery_t[own, first:end] = mm(key_t[kv, :end], dscore) * 0.125
            dkey[:end, kv] += mm(dscore, query_block)
            dvalue[:end, kv] += mm(share.astype(BF), dcontext_block)
        if block == 1:
            scatter.up_side()
            scatter.down_side()
    turn = -sine[...]
    for half in range(2):
        rows = slice(half * 128, half * 128 + 128)
        piece = rotated(dquery_t[rows, :].T, cosine[...], turn)
        dall[:, rows] = piece.astype(BF)
        dall_t[rows, :] = piece.T.astype(BF)
    piece = rotated(dkey[...], cosine[...], turn)
    dall[:, 256:384] = piece.astype(BF)
    dall_t[256:384, :] = piece.T.astype(BF)
    dall[:, 384:512] = dvalue[...].astype(BF)
    dall_t[384:512, :] = dvalue[...].T.astype(BF)
    grads[:, 0:512] = mm(dall_t[...], normed[...]).T.astype(BF)
    for block in range(SEQ // BLOCK):
        rows = slice(block * BLOCK, (block + 1) * BLOCK)
        dn1[rows, :] = mm_last(dall[rows, :], weights[:, 0:512]).astype(BF)
    scatter.finish(y)


def attention_backward(
    dattn, normed, weights, tables, segments, kept, rest, y_part, ident
):
    vmem = pl.BlockSpec(memory_space=pltpu.VMEM)
    return pl.pallas_call(
        attention_backward_kernel,
        in_specs=[vmem] * 13,
        out_specs=[vmem] * 3,
        out_shape=[
            jax.ShapeDtypeStruct((SEQ, D), BF),
            jax.ShapeDtypeStruct((D, SMALL), BF),
            jax.ShapeDtypeStruct((LOCAL, D), F32),
        ],
        scratch_shapes=[
            pltpu.VMEM((SEQ, BLOCK), F32),
            pltpu.VMEM((SEQ, HEADS * HD), BF),
            pltpu.VMEM((HEADS * HD, SEQ), F32),
            pltpu.VMEM((SEQ, 128), F32),
            pltpu.VMEM((SEQ, 128), F32),
            pltpu.VMEM((SEQ, 512), BF),
            pltpu.VMEM((512, SEQ), BF),
            *ring_scratch(LOCAL, D),
            pltpu.SemaphoreType.DMA((8,)),
            pltpu.SemaphoreType.DMA((8,)),
        ],
        compiler_params=pltpu.CompilerParams(
            collective_id=ident, has_side_effects=True, vmem_limit_bytes=56 * MIB
        ),
        name="attention_backward",
    )(
        dattn, normed, weights, *tables, segments, *kept, rest, y_part,
    )


def experts_kernel(
    x_in, gate_in, d_in, weights, y_out, dx_out, dgate_out, grads,
    x, d, xt, dt, y, dx, gating, dgate, dgate_part, hidden, w, *refs,
):
    dx_scratch, dgate_scratch = refs[:5], refs[5:10]
    send, recv, here, load, store, fetch = refs[10:]
    at = Place()
    step = pl.program_id(0)
    opening, closing = step == 0, step == STEPS - 1
    rows_at_once = 2 * LOCAL
    lane = lax.broadcasted_iota(jnp.int32, (rows_at_once, 128), 1)
    own_first = at.yh * 16 + step * QUAD
    x_gather = RingGather(at, x_in, x, send, recv, here.at[0], 0)
    gate_gather = RingGather(at, gate_in, gating, send, recv, here.at[1], 9)
    gathers = (x_gather, gate_gather)
    scatters = (
        RingScatter(at, d, dx_scratch, send, recv, 18),
        RingScatter(at, dgate_part, dgate_scratch, send, recv, 26),
    )

    def fetches(number):
        return [
            pltpu.make_async_copy(
                weights.at[g, number * QUAD + i],
                w.at[:, pl.ds((g * QUAD + i) * FF, FF)],
                fetch.at[g * QUAD + i],
            )
            for g in range(3)
            for i in range(QUAD)
        ]

    def d_load(chip):
        two = pl.ds(chip * 2, 2)
        return pltpu.make_async_copy(d_in.at[two], d.at[two], load.at[chip])

    def y_store(chip):
        two = pl.ds(chip * 2, 2)
        return pltpu.make_async_copy(x.at[two], y_out.at[two], store.at[chip])

    @pl.when(opening)
    def _():
        greet([at.sibling(), at.ring(1), at.ring(3)])
        for gather in gathers:
            gather.begin()
        for copy in fetches(step):
            copy.start()
        for chip in range(4):
            d_load(chip).start()

    for copy in fetches(step):
        copy.wait()

    def arrive(turn):
        @pl.when(turn == 0)
        def _():
            for gather in gathers:
                gather.kept().wait()
                gather.copy(0).wait_recv()

        @pl.when(turn == 1)
        def _():
            for gather in gathers:
                gather.forward_before()
                gather.forward_behind()
            for gather in gathers:
                gather.copy(4).wait_recv()

        @pl.when(turn == 2)
        def _():
            for gather in gathers:
                gather.forward_across()
            for gather in gathers:
                gather.copy(6).wait_recv()

        @pl.when(turn == 3)
        def _():
            for gather in gathers:
                gather.copy(7).wait_recv()
                gather.copy(8).wait_recv()

    def leave(turn):
        @pl.when(turn == 0)
        def _():
            for scatter in scatters:
                scatter.copy(2).start()

        @pl.when(turn == 1)
        def _():
            for scatter in scatters:
                scatter.copy(1).start()
                scatter.far()

        @pl.when(turn == 2)
        def _():
            for scatter in scatters:
                scatter.copy(3).start()
                scatter.up_side()

        @pl.when(turn == 3)
        def _():
            for scatter in scatters:
                scatter.copy(0).start()
                scatter.down_side()

    def tokens_block(turn, carry):
        inward = jnp.where(turn == 0, 0, jnp.where(turn == 1, 3, turn - 1))
        outward = jnp.where(turn == 0, 2, jnp.where(turn == 3, 0, turn * 2 - 1))
        chip = at.chip(jnp.where(closing, outward, inward))
        two = pl.ds(chip * 2, 2)
        rows = pl.ds(pl.multiple_of(chip * rows_at_once, rows_at_once), rows_at_once)

        @pl.when(opening)
        def _():
            arrive(turn)
            d_load(chip).wait()
            xt[:, rows] = x[two].reshape(rows_at_once, D).T
            dt[:, rows] = d[two].reshape(rows_at_once, D).T
            y[rows, :] = jnp.zeros((rows_at_once, D), F32)
            dx[rows, :] = jnp.zeros((rows_at_once, D), F32)
            dgate[rows, :] = jnp.zeros((rows_at_once, 128), F32)

        both = mm(x[two].reshape(rows_at_once, D), w[:, 0 : 2 * F])
        gate, up = both[:, :F], both[:, F:]
        dact = mm(d[two].reshape(rows_at_once, D), w[:, 2 * F :])
        shares = gating[two].reshape(rows_at_once, 128)
        turned = pltpu.roll(shares, lax.rem(128 - own_first, 128), 1)
        factor = jnp.concatenate(
            [jnp.broadcast_to(turned[:, i : i + 1], (rows_at_once, FF)) for i in range(QUAD)],
            axis=1,
        )
        q = 1.0 / (1.0 + jnp.exp(-gate))
        silu = gate * q
        act = silu * up
        product = act * dact
        sums = dgate[rows, :]
        for i in range(QUAD):
            own = jnp.sum(product[:, i * FF : (i + 1) * FF], axis=1, keepdims=True)
            sums = jnp.where(lane == own_first + i, own, sums)
        dgate[rows, :] = sums
        dact = dact * factor
        hidden[rows, 0:F] = (dact * up * (q + silu * (1.0 - q))).astype(BF)
        hidden[rows, F : 2 * F] = (dact * silu).astype(BF)
        hidden[rows, 2 * F :] = (act * factor).astype(BF)
        y[rows, :] += mm_last(hidden[rows, 2 * F :], w[:, 2 * F :])
        dx[rows, :] += mm_last(hidden[rows, 0 : 2 * F], w[:, 0 : 2 * F])

        @pl.when(closing)
        def _():
            x[two] = y[rows, :].astype(BF).reshape(2, LOCAL, D)
            d[two] = dx[rows, :].astype(BF).reshape(2, LOCAL, D)
            dgate_part[two] = dgate[rows, :].astype(BF).reshape(2, LOCAL, 128)
            y_store(chip).start()
            leave(turn)

        return carry

    lax.fori_loop(0, 4, tokens_block, 0)

    @pl.when(step < STEPS - 1)
    def _():
        for copy in fetches(step + 1):
            copy.start()

    @pl.when(opening)
    def _():
        for gather in gathers:
            gather.sent()

    def grads_block(block, carry):
        rows = pl.ds(pl.multiple_of(block * 512, 512), 512)
        both = mm(xt[rows, :], hidden[:, 0 : 2 * F]).astype(BF)
        for g in range(2):
            for i in range(QUAD):
                first = (g * QUAD + i) * FF
                grads[g, i, rows, :] = both[:, first : first + FF]
        down = mm(dt[rows, :], hidden[:, 2 * F :]).astype(BF)
        for i in range(QUAD):
            grads[2, i, rows, :] = down[:, i * FF : (i + 1) * FF]
        return carry

    lax.fori_loop(0, D // 512, grads_block, 0)

    @pl.when(closing)
    def _():
        scatters[0].finish(dx_out)
        scatters[1].finish(dgate_out)
        for chip in range(4):
            y_store(chip).wait()


def experts(x, gating, d, weights, ident):
    hbm = pl.BlockSpec(memory_space=pl.ANY)

    def whole(rows, columns):
        return pl.BlockSpec((rows, columns), lambda step: (0, 0), pipeline_mode=pl.Buffered(1))

    return pl.pallas_call(
        experts_kernel,
        grid=(STEPS,),
        in_specs=[hbm] * 4,
        out_specs=[
            hbm,
            whole(LOCAL, D),
            whole(LOCAL, 128),
            pl.BlockSpec(
                (3, QUAD, D, FF), lambda step: (0, step, 0, 0), pipeline_mode=pl.Buffered(1)
            ),
        ],
        out_shape=[
            jax.ShapeDtypeStruct((8, LOCAL, D), BF),
            jax.ShapeDtypeStruct((LOCAL, D), F32),
            jax.ShapeDtypeStruct((LOCAL, 128), F32),
            jax.ShapeDtypeStruct((3, STEPS * QUAD, D, FF), BF),
        ],
        scratch_shapes=[
            pltpu.VMEM((8, LOCAL, D), BF),
            pltpu.VMEM((8, LOCAL, D), BF),
            pltpu.VMEM((D, TOKENS), BF),
            pltpu.VMEM((D, TOKENS), BF),
            pltpu.VMEM((TOKENS, D), F32),
            pltpu.VMEM((TOKENS, D), F32),
            pltpu.VMEM((8, LOCAL, 128), F32),
            pltpu.VMEM((TOKENS, 128), F32),
            pltpu.VMEM((8, LOCAL, 128), BF),
            pltpu.VMEM((TOKENS, 3 * F), BF),
            pltpu.VMEM((D, 3 * F), BF),
            *ring_scratch(LOCAL, D, False),
            *ring_scratch(LOCAL, 128, False),
            pltpu.SemaphoreType.DMA((34,)),
            pltpu.SemaphoreType.DMA((34,)),
            pltpu.SemaphoreType.DMA((2,)),
            pltpu.SemaphoreType.DMA((4,)),
            pltpu.SemaphoreType.DMA((4,)),
            pltpu.SemaphoreType.DMA((3 * QUAD,)),
        ],
        compiler_params=pltpu.CompilerParams(
            collective_id=ident, has_side_effects=True, vmem_limit_bytes=63 * MIB
        ),
        name="experts",
    )(x, gating, d, weights)


def norm_scale(values):
    return lax.rsqrt(jnp.mean(values * values, axis=-1, keepdims=True) + EPS)


def norm_grad(values, gain, dnormed):
    scale = norm_scale(values)
    unit = values * scale
    weighted = dnormed * gain
    dvalues = scale * (weighted - unit * jnp.mean(weighted * unit, axis=-1, keepdims=True))
    return dvalues


def on_device(
    hidden_in, out_grad, attn_gain, query_weight, key_weight, value_weight, output_weight,
    moe_gain, router_weight, expert_gate, expert_up, expert_down, expert_ids, segment_ids,
):
    small = jnp.concatenate(
        [
            query_weight, key_weight, value_weight, output_weight,
            router_weight, attn_gain[:, None], moe_gain[:, None], jnp.zeros((32, 94), BF),
        ],
        axis=1,
    )
    expert_weights, small = first_exchange(expert_gate, expert_up, expert_down, small, 0)
    expert_weights = lax.all_gather(expert_weights, PLANE, axis=2, tiled=True)
    segment = jnp.pad(segment_ids.reshape(2, 128), ((0, 6), (0, 0)))
    hidden_all, segments, d, small = startup(hidden_in, segment, out_grad, small, 1)
    tables = tuple(jnp.asarray(t) for t in rotary_tables())
    named = jnp.any(
        expert_ids[:, :, None] == jnp.arange(128, dtype=jnp.int32)[None, None, :], axis=1
    ).astype(F32)

    part, normed_all, *kept = attention_forward(hidden_all, small, tables, segments)
    middle, normed_moe, gating = middle_of(part, hidden_in, small, named, 2)
    y, dx, dgate, expert_grads = experts(normed_moe, gating, d, expert_weights, 3)
    expert_grads = lax.psum_scatter(expert_grads, PLANE, scatter_dimension=2, tiled=True)
    dattn, dmiddle, rest = dmiddle_of(dx, dgate, gating, middle, normed_moe, out_grad, small, 4)
    dn1, grads, y = attention_backward(
        dattn, normed_all, small, tables, segments, kept, rest, y, 5
    )
    block_out = (middle + y).astype(BF)
    own_weights = jnp.concatenate([query_weight, key_weight, value_weight], axis=1)
    dn1, attention_grads, rest = final(dn1, grads, own_weights, 6)
    hidden = hidden_in.astype(F32)
    dhidden = norm_grad(hidden, small[:, 800].astype(F32), dn1)
    hidden_grad = dmiddle + dhidden
    expert_grads = [share.astype(F32) for share in last_exchange(expert_grads, 7)]
    return (
        block_out,
        hidden_grad,
        rest[:, 33] / attn_gain.astype(F32),
        attention_grads[:, 0:256],
        attention_grads[:, 256:384],
        attention_grads[:, 384:512],
        attention_grads[:, 512:768],
        rest[:, 32],
        rest[:, :32],
        *expert_grads,
    )


def solution(mesh):
    fine = Mesh(np.asarray(mesh.devices).reshape(4, 4, 2, 2, 2), ALL)
    return jax.shard_map(
        on_device,
        mesh=fine,
        in_specs=(
            P(ALL, None),
            P(ALL, None),
            P(DP),
            P(DP, TENSOR),
            P(DP, TENSOR),
            P(DP, TENSOR),
            P(DP, TENSOR),
            P(DP),
            P(DP, None),
            P(None, DP, TENSOR),
            P(None, DP, TENSOR),
            P(None, DP, TENSOR),
            P(ALL, None),
            P(ALL),
        ),
        out_specs=(
            P(ALL, None),
            P(ALL, None),
            P(DP),
            P(DP, TENSOR),
            P(DP, TENSOR),
            P(DP, TENSOR),
            P(DP, TENSOR),
            P(DP),
            P(DP, None),
            P(None, DP, TENSOR),
            P(None, DP, TENSOR),
            P(None, DP, TENSOR),
        ),
        check_vma=False,
    )
```

```python
import jax
import jax.numpy as jnp
import numpy as np
from jax import lax
from jax.experimental import pallas as pl
from jax.experimental.pallas import tpu as pltpu
from jax.sharding import Mesh
from jax.sharding import PartitionSpec as P

D = 1024
HD = 64
E = 32
SEQ = 1024
LOCAL = 256
HEADS = 4
QUAD = 4
FF = 128
F = QUAD * FF
EPS = 1e-06
MASKED = -1e30
BLOCK = 256
TOKENS = 2048
STEPS = 4

DP = ("x", "z", "yh")
TENSOR = ("yl", "core")
RING = ("yh", "yl", "core")
PLANE = ("x", "z")
ALL = ("x", "z", "yh", "yl", "core")

F32 = jnp.float32
BF = jnp.bfloat16
LAST = (((1,), (1,)), ((), ()))
MIB = 1024 * 1024
MESH = pl.DeviceIdType.MESH
SMALL = 896


def mm(a, b):
    return jnp.dot(a, b, preferred_element_type=F32)


def mm_last(a, b):
    return lax.dot_general(a, b, LAST, preferred_element_type=F32)


class Place:
    def __init__(self):
        self.x = lax.axis_index("x")
        self.z = lax.axis_index("z")
        self.yh = lax.axis_index("yh")
        self.yl = lax.axis_index("yl")
        self.core = lax.axis_index("core")
        self.y = self.yh * 2 + self.yl

    def chip(self, k):
        return lax.rem(self.y + k, 4)

    def ring(self, k):
        chip = self.chip(k)
        return {"yh": chip // 2, "yl": lax.rem(chip, 2)}

    def along(self, axis, k):
        return {axis: lax.rem(getattr(self, axis) + k, 4)}

    def sibling(self):
        return {"core": 1 - self.core}

    def partner(self):
        return {"yl": 1 - self.yl}

    def diagonal(self):
        return {"yl": 1 - self.yl, "core": 1 - self.core}

    def opposite(self):
        return {"yh": 1 - self.yh}


def greet(devices):
    barrier = pltpu.get_barrier_semaphore()
    for device in devices:
        pl.semaphore_signal(barrier, inc=1, device_id=device, device_id_type=MESH)
    pl.semaphore_wait(barrier, len(devices))


def remote(src, dst, send, recv, i, device):
    return pltpu.make_async_remote_copy(
        src_ref=src, dst_ref=dst, send_sem=send.at[i], recv_sem=recv.at[i],
        device_id=device, device_id_type=MESH,
    )


def push(src, dst, send, recv, i, device):
    copy = remote(src, dst, send, recv, i, device)
    copy.start()
    return copy


def keep(src, dst, sem):
    copy = pltpu.make_async_copy(src, dst, sem)
    copy.start()
    return copy


class RingGather:
    def __init__(self, at, own, out, send, recv, here, base=0):
        self.at, self.own, self.out, self.base = at, own, out, base
        self.send, self.recv, self.here = send, recv, here
        half = own.shape[0] // 2
        lo, hi = pl.ds(0, half), pl.ds(half, half)
        me, before, behind, across = (out.at[self.slot(k)] for k in (0, 3, 1, 2))
        near, up, down = at.sibling(), at.ring(1), at.ring(3)
        self.plan = [
            (own, me, near),
            (own, me, up),
            (own, me, down),
            (before.at[lo], before.at[lo], up),
            (before, before, near),
            (behind.at[hi], behind.at[hi], down),
            (behind, behind, near),
            (across.at[lo], across.at[lo], near),
            (across.at[hi], across.at[hi], near),
        ]

    def slot(self, k):
        return self.at.chip(k) * 2 + self.at.core

    def copy(self, i):
        src, dst, device = self.plan[i]
        return remote(src, dst, self.send, self.recv, self.base + i, device)

    def kept(self):
        return pltpu.make_async_copy(self.own, self.out.at[self.slot(0)], self.here)

    def begin(self):
        self.kept().start()
        for i in (1, 2, 0):
            self.copy(i).start()

    def forward_before(self):
        self.copy(1).wait_recv()
        self.copy(3).start()
        self.copy(4).start()

    def forward_behind(self):
        self.copy(2).wait_recv()
        self.copy(5).start()
        self.copy(6).start()

    def forward_across(self):
        self.copy(3).wait_recv()
        self.copy(7).start()
        self.copy(5).wait_recv()
        self.copy(8).start()

    def sent(self):
        for i in range(9):
            self.copy(i).wait_send()


class PairGather:
    def __init__(self, at, own, out, send, recv, here, base, pieces):
        self.at, self.out, self.send, self.recv, self.base = at, out, send, recv, base
        size = own.shape[0] // pieces
        self.parts = [pl.ds(i * size, size) for i in range(pieces)]
        me = at.yl * 2 + at.core
        self.other = (1 - at.yl) * 2 + at.core
        self.kept = keep(own, out.at[me], here)
        self.far = [
            push(own.at[part], out.at[me, part], send, recv, base + 1 + i, at.partner())
            for i, part in enumerate(self.parts)
        ]
        self.near = [push(own, out.at[me], send, recv, base, at.sibling())]

    def forward(self):
        for i, part in enumerate(self.parts):
            self.far[i].wait_recv()
            view = self.out.at[self.other, part]
            index = self.base + 1 + len(self.parts) + i
            self.near.append(push(view, view, self.send, self.recv, index, self.at.sibling()))

    def finish(self):
        for copy in self.near:
            copy.wait_recv()
        for copy in (*self.far, *self.near):
            copy.wait_send()
        self.kept.wait()


PIECES = 4


class AxisGather:
    def __init__(self, at, axis, view, send, recv, base):
        self.up, self.down = at.along(axis, 1), at.along(axis, 3)
        self.view, self.send, self.recv, self.base = view, send, recv, base

    def go(self, i, view, device):
        return push(view, view, self.send, self.recv, self.base + i, device)

    def begin(self):
        self.first = [
            self.go(0, self.view(0, "all"), self.up), self.go(1, self.view(0, "all"), self.down),
        ]

    def forward(self):
        self.first[0].wait_recv()
        self.far = [self.go(2, self.view(3, "low"), self.up)]
        self.first[1].wait_recv()
        self.far.append(self.go(3, self.view(1, "high"), self.down))

    def finish(self):
        for copy in self.far:
            copy.wait_recv()
        for copy in (*self.first, *self.far):
            copy.wait_send()


def halves_of(ref, first, size):
    spans = {"all": (0, size), "low": (0, size // 2), "high": (size // 2, size // 2)}
    return lambda part: ref.at[pl.ds(first + spans[part][0], spans[part][1])]


class QuadGather:
    COPIES = 16

    def __init__(self, at, own, out, send, recv, here, base=0):
        self.own, self.out, self.here = own, out, here
        self.at, self.send, self.recv, self.base = at, send, recv, base
        low, high, whole = pl.ds(0, 32), pl.ds(32, 32), pl.ds(0, 64)
        first, second = pl.ds(0, 2), pl.ds(2, 2)

        def z_of(k):
            return lax.rem(at.z + k, 4)

        def x_of(k):
            return lax.rem(at.x + k, 4)

        views = (
            ("z", lambda k, rows: out.at[:, first, at.x, z_of(k), rows]),
            ("x", lambda k, rows: out.at[:, second, x_of(k), at.z, rows]),
            ("x", lambda k, rows: out.at[:, first, x_of(k), :, rows]),
            ("z", lambda k, rows: out.at[:, second, :, z_of(k), rows]),
        )
        self.plan = []
        for stage in (views[:2], views[2:]):
            for axis, view in stage:
                self.plan.append((view(0, whole), at.along(axis, 1)))
                self.plan.append((view(0, whole), at.along(axis, 3)))
            for axis, view in stage:
                self.plan.append((view(3, low), at.along(axis, 1)))
                self.plan.append((view(1, high), at.along(axis, 3)))

    def copy(self, i):
        view, device = self.plan[i]
        return remote(view, view, self.send, self.recv, self.base + i, device)

    def kept(self):
        return pltpu.make_async_copy(
            self.own, self.out.at[:, :, self.at.x, self.at.z], self.here
        )

    def begin(self):
        self.kept().start()
        self.kept().wait()
        for i in range(4):
            self.copy(i).start()

    def forward(self, stage):
        for i in range(4):
            self.copy(8 * stage + i).wait_recv()
            self.copy(8 * stage + 4 + i).start()

    def turn(self):
        for i in range(4, 8):
            self.copy(i).wait_recv()
        for i in range(8, 12):
            self.copy(i).start()

    def finish(self):
        for i in range(12, 16):
            self.copy(i).wait_recv()
        for i in range(16):
            self.copy(i).wait_send()


QUAD_SHAPE = jax.ShapeDtypeStruct((3, QUAD, 4, 4, 64, FF), BF)


def startup_kernel(
    hidden, segment, out_grad, gate, up, down, small,
    hidden_all, segment_all, out_grad_all, small_all, shares, quad, send, recv, here,
):
    at = Place()
    greet(
        [
            at.sibling(), at.partner(), at.diagonal(), at.opposite(), at.ring(1), at.ring(3),
            at.along("x", 1), at.along("x", 3), at.along("z", 1), at.along("z", 3),
        ]
    )
    rank = at.yl * 2 + at.core
    own_rows = pl.ds(at.yh * 32, 32)
    own_slot = (at.x * 4 + at.z) * 2
    mine = small_all.at[own_slot + at.yh]
    small_kept = keep(small, mine, here.at[0])
    copies = [push(small, mine, send, recv, 0, at.opposite())]
    swaps, kept = [], []
    for number, (first, count) in enumerate(((0, QUAD), (QUAD, 3 * QUAD))):
        for i, share in enumerate((gate, up, down)):
            dst = shares.at[i, pl.ds(first, count), own_rows]
            theirs = share.at[pl.ds((1 - at.yh) * 16 + first, count)]
            index = 1 + 3 * number + i
            swaps.append(push(theirs, dst, send, recv, index, at.opposite()))
            own = share.at[pl.ds(at.yh * 16 + first, count)]
            kept.append(keep(own, dst, here.at[index]))
    pair = PairGather(at, hidden, hidden_all, send, recv, here.at[7], 7, PIECES)
    base = 8 + 2 * PIECES
    seg_here = keep(segment, segment_all.at[rank], here.at[8])
    copies.extend(
        push(segment, segment_all.at[rank], send, recv, base + i, device)
        for i, device in enumerate((at.sibling(), at.partner(), at.diagonal()))
    )
    over_z = AxisGather(
        at, "z",
        lambda k, part: halves_of(small_all, (at.x * 4 + lax.rem(at.z + k, 4)) * 2, 2)(part),
        send, recv, base + 3,
    )
    over_x = AxisGather(
        at, "x", lambda k, part: halves_of(small_all, lax.rem(at.x + k, 4) * 8, 8)(part),
        send, recv, base + 7,
    )
    ring = RingGather(at, out_grad, out_grad_all, send, recv, here.at[9], base + 11)
    experts = QuadGather(
        at, shares.at[:, pl.ds(0, QUAD)], quad, send, recv, here.at[10], base + 20
    )
    small_kept.wait()
    copies[0].wait_recv()
    over_z.begin()
    for swap, own in zip(swaps[:3], kept[:3]):
        swap.wait_recv()
        own.wait()
    over_z.forward()
    experts.begin()
    over_z.finish()
    over_x.begin()
    pair.forward()
    ring.begin()
    experts.forward(0)
    over_x.forward()
    experts.turn()
    pair.finish()
    over_x.finish()
    experts.forward(1)
    ring.forward_before()
    ring.forward_behind()
    experts.finish()
    ring.forward_across()
    seg_here.wait()
    for copy in copies[1:]:
        copy.wait_recv()
    for copy in swaps[3:]:
        copy.wait_recv()
    for copy in kept[3:]:
        copy.wait()
    for i in (0, 4, 6, 7, 8):
        ring.copy(i).wait_recv()
    ring.sent()
    ring.kept().wait()
    for copy in (*copies, *swaps):
        copy.wait_send()


def startup(hidden, segment, out_grad, shares, small, ident):
    hbm = pl.BlockSpec(memory_space=pl.ANY)
    sems = 8 + 2 * PIECES + 20 + QuadGather.COPIES
    hidden_all, segment_all, out_grad_all, small_all, shares, quad = pl.pallas_call(
        startup_kernel,
        in_specs=[hbm] * 7,
        out_specs=[hbm] * 6,
        out_shape=[
            jax.ShapeDtypeStruct((4, *hidden.shape), hidden.dtype),
            jax.ShapeDtypeStruct((4, *segment.shape), segment.dtype),
            jax.ShapeDtypeStruct((8, *out_grad.shape), out_grad.dtype),
            jax.ShapeDtypeStruct((32, 32, SMALL), small.dtype),
            jax.ShapeDtypeStruct((3, 16, 64, FF), BF),
            QUAD_SHAPE,
        ],
        scratch_shapes=[
            pltpu.SemaphoreType.DMA((sems,)),
            pltpu.SemaphoreType.DMA((sems,)),
            pltpu.SemaphoreType.DMA((11,)),
        ],
        compiler_params=pltpu.CompilerParams(collective_id=ident, has_side_effects=True),
        name="startup",
    )(hidden, segment, out_grad, *shares, small)
    hidden_all, small_all = hidden_all.reshape(SEQ, D), small_all.reshape(D, SMALL)
    return hidden_all, segment_all, out_grad_all, small_all, shares, quad


class RingScatter:
    def __init__(self, at, part, scratch, send, recv, base=0):
        self.at, self.part, self.send, self.recv, self.base = at, part, send, recv, base
        near, half_a, half_b, self.full_up, self.full_down = scratch[:5]
        to_far, to_up, to_down = scratch[5:] or [
            part.at[at.chip(k) * 2 + at.core] for k in (2, 1, 3)
        ]
        self.near, self.half_a, self.half_b = near, half_a, half_b
        self.to_far, self.to_up, self.to_down = to_far, to_up, to_down
        self.half = half_a.shape[0]
        self.lo, self.hi = pl.ds(0, self.half), pl.ds(self.half, self.half)
        up, down = at.ring(1), at.ring(3)
        self.plan = {
            k: (part.at[at.chip(k) * 2 + 1 - at.core], near.at[k], at.sibling()) for k in range(4)
        }
        self.plan[4] = (to_far.at[self.lo], half_a, up)
        self.plan[5] = (to_far.at[self.hi], half_b, down)
        self.plan[6] = (to_up, self.full_up, up)
        self.plan[7] = (to_down, self.full_down, down)

    def copy(self, i):
        src, dst, device = self.plan[i]
        return remote(src, dst, self.send, self.recv, self.base + i, device)

    def chip_sum(self, k):
        self.copy(k).wait_recv()
        own = self.part[self.at.chip(k) * 2 + self.at.core]
        return own.astype(F32) + self.near[k].astype(F32)

    def far(self):
        self.to_far[...] = self.chip_sum(2).astype(BF)
        self.copy(4).start()
        self.copy(5).start()

    def up_side(self):
        total = self.chip_sum(1)
        self.copy(4).wait_recv()
        self.to_up[self.lo, :] = (total[: self.half] + self.half_a[...].astype(F32)).astype(BF)
        self.to_up[self.hi, :] = total[self.half :].astype(BF)
        self.copy(6).start()

    def down_side(self):
        total = self.chip_sum(3)
        self.copy(5).wait_recv()
        self.to_down[self.lo, :] = total[: self.half].astype(BF)
        self.to_down[self.hi, :] = (total[self.half :] + self.half_b[...].astype(F32)).astype(BF)
        self.copy(7).start()

    def finish(self, out):
        out[...] = self.chip_sum(0)
        self.copy(6).wait_recv()
        out[...] += self.full_up[...].astype(F32)
        self.copy(7).wait_recv()
        out[...] += self.full_down[...].astype(F32)
        for i in range(8):
            self.copy(i).wait_send()


def ring_scratch(rows, columns, own_sends=True):
    block, half = pltpu.VMEM((rows, columns), BF), pltpu.VMEM((rows // 2, columns), BF)
    scratch = [pltpu.VMEM((4, rows, columns), BF), half, half, block, block]
    return scratch + [block] * 3 if own_sends else scratch


class PairScatter:
    def __init__(self, at, part, scratch, send, recv):
        self.at, self.part, self.send, self.recv = at, part, send, recv
        self.near, self.far_rows, self.to_far = scratch
        size = self.to_far.shape[0] // PIECES
        self.parts = [pl.ds(i * size, size) for i in range(PIECES)]
        self.other, self.own = (1 - at.yl) * 2, at.yl * 2
        self.first = [
            push(
                part.at[self.other + 1 - at.core, rows], self.near.at[1, rows],
                send, recv, i, at.sibling(),
            )
            for i, rows in enumerate(self.parts)
        ]
        self.second = push(
            part.at[self.own + 1 - at.core], self.near.at[0], send, recv, PIECES, at.sibling()
        )

    def forward(self):
        at = self.at
        self.sent = []
        for i, rows in enumerate(self.parts):
            self.first[i].wait_recv()
            own = self.part[self.other + at.core, rows, :].astype(F32)
            self.to_far[rows, :] = (own + self.near[1, rows, :].astype(F32)).astype(BF)
            self.sent.append(
                push(
                    self.to_far.at[rows], self.far_rows.at[rows], self.send, self.recv,
                    PIECES + 1 + i, at.partner(),
                )
            )

    def finish(self, out):
        self.second.wait_recv()
        out[...] = self.part[self.own + self.at.core].astype(F32) + self.near[0].astype(F32)
        for i, rows in enumerate(self.parts):
            self.sent[i].wait_recv()
            out[rows, :] += self.far_rows[rows, :].astype(F32)
        for copy in (*self.first, self.second, *self.sent):
            copy.wait_send()


def pair_scratch(rows, columns):
    block = pltpu.VMEM((rows, columns), BF)
    return [pltpu.VMEM((2, rows, columns), BF), block, block]


def gain_rows(small):
    return small[:, 768:896].astype(F32).T[32:40, :]


def column_of(row):
    return jnp.broadcast_to(row, (8, row.shape[1])).T[:, 0:1]


def middle_kernel(part, hidden, small, named, shares, middle, normed, gating, quad, *refs):
    at = Place()
    greet(
        [
            at.sibling(), at.partner(),
            at.along("x", 1), at.along("x", 3), at.along("z", 1), at.along("z", 3),
        ]
    )
    scatter = PairScatter(at, part, refs[:3], *refs[3:5])
    experts = QuadGather(at, shares.at[:, pl.ds(2 * QUAD, QUAD)], quad, *refs[5:])
    experts.begin()
    gains = gain_rows(small)
    scatter.forward()
    experts.forward(0)
    experts.turn()
    scatter.finish(middle)
    values = middle[...] + hidden[...].astype(F32)
    middle[...] = values
    scale = lax.rsqrt(jnp.mean(values * values, axis=-1, keepdims=True) + EPS)
    normed[...] = (values * scale * gains[1:2, :]).astype(BF)
    chosen = named[...] > 0.0
    logits = jnp.where(chosen, mm(normed[...], small[:, 768:896]), MASKED)
    powers = jnp.where(chosen, jnp.exp(logits - jnp.max(logits, axis=-1, keepdims=True)), 0.0)
    gating[...] = powers / jnp.sum(powers, axis=-1, keepdims=True)
    experts.forward(1)
    experts.finish()


def middle_of(part, hidden, small, named, shares, ident):
    vmem = pl.BlockSpec(memory_space=pltpu.VMEM)
    hbm = pl.BlockSpec(memory_space=pl.ANY)
    return pl.pallas_call(
        middle_kernel,
        in_specs=[vmem] * 4 + [hbm],
        out_specs=[vmem] * 3 + [hbm],
        out_shape=[
            jax.ShapeDtypeStruct((LOCAL, D), F32),
            jax.ShapeDtypeStruct((LOCAL, D), BF),
            jax.ShapeDtypeStruct((LOCAL, 128), F32),
            QUAD_SHAPE,
        ],
        scratch_shapes=[
            *pair_scratch(LOCAL, D),
            pltpu.SemaphoreType.DMA((1 + 2 * PIECES,)),
            pltpu.SemaphoreType.DMA((1 + 2 * PIECES,)),
            *quad_sems(),
        ],
        compiler_params=pltpu.CompilerParams(
            collective_id=ident, has_side_effects=True, vmem_limit_bytes=40 * MIB
        ),
        name="middle",
    )(part.reshape(4, LOCAL, D), hidden, small, named, shares)


def dmiddle_kernel(
    dx, dgate, gating, middle, normed, out_grad, small, dattn_all, dmiddle, rest,
    dattn, send, recv, here,
):
    at = Place()
    greet([at.sibling(), at.partner()])
    gain = gain_rows(small)[1:2, :]
    share = gating[...]
    dchosen = share * (dgate[...] - jnp.sum(share * dgate[...], axis=-1, keepdims=True))
    dlogits = dchosen.astype(BF)
    dnormed = dx[...] + mm_last(dlogits, small[:, 768:896])
    values = middle[...]
    scale = lax.rsqrt(jnp.mean(values * values, axis=-1, keepdims=True) + EPS)
    unit = values * scale
    weighted = dnormed * gain
    inner = jnp.mean(weighted * unit, axis=-1, keepdims=True)
    total = out_grad[...].astype(F32) + scale * (weighted - unit * inner)
    dmiddle[...] = total
    dattn[...] = total.astype(BF)
    gather = PairGather(at, dattn, dattn_all, send, recv, here, 0, PIECES)
    router_part = mm(normed[...].T, dlogits)
    gain_part = column_of(jnp.sum(dnormed * unit, axis=0, keepdims=True))
    lane = lax.broadcasted_iota(jnp.int32, (D, 128), 1)
    rest[...] = jnp.where(lane == 32, gain_part, router_part).astype(BF)
    gather.forward()
    gather.finish()


def dmiddle_of(dx, dgate, gating, middle, normed, out_grad, small, ident):
    vmem = pl.BlockSpec(memory_space=pltpu.VMEM)
    dattn, dmiddle, rest = pl.pallas_call(
        dmiddle_kernel,
        in_specs=[vmem] * 7,
        out_specs=[vmem] * 3,
        out_shape=[
            jax.ShapeDtypeStruct((4, LOCAL, D), BF),
            jax.ShapeDtypeStruct((LOCAL, D), F32),
            jax.ShapeDtypeStruct((D, 128), BF),
        ],
        scratch_shapes=[
            pltpu.VMEM((LOCAL, D), BF),
            pltpu.SemaphoreType.DMA((1 + 2 * PIECES,)),
            pltpu.SemaphoreType.DMA((1 + 2 * PIECES,)),
            pltpu.SemaphoreType.DMA,
        ],
        compiler_params=pltpu.CompilerParams(
            collective_id=ident, has_side_effects=True, vmem_limit_bytes=40 * MIB
        ),
        name="dmiddle",
    )(dx, dgate, gating, middle, normed, out_grad, small)
    return dattn.reshape(SEQ, D), dmiddle, rest


class AxisScatter:
    def __init__(self, at, axis, part, scratch, send, recv, base):
        self.at, self.axis, self.part, self.base = at, axis, part, base
        self.send, self.recv = send, recv
        self.half_a, self.half_b, self.up, self.down, self.to_up, self.to_down = scratch
        self.half = part.shape[1] // 2
        lo, hi = pl.ds(0, self.half), pl.ds(self.half, self.half)
        far = part.at[self.to(2)]
        self.far_up = self.go(0, far.at[lo], self.half_a, 1)
        self.far_down = self.go(1, far.at[hi], self.half_b, 3)

    def to(self, k):
        return self.at.along(self.axis, k)[self.axis]

    def go(self, i, src, dst, k):
        return push(src, dst, self.send, self.recv, self.base + i, self.at.along(self.axis, k))

    def sides(self):
        h = self.half
        self.far_up.wait_recv()
        block = self.part[self.to(1)]
        self.to_up[:h] = (block[:h].astype(F32) + self.half_a[...].astype(F32)).astype(BF)
        self.to_up[h:] = block[h:]
        self.sent_up = self.go(2, self.to_up, self.up, 1)
        self.far_down.wait_recv()
        block = self.part[self.to(3)]
        self.to_down[:h] = block[:h]
        self.to_down[h:] = (block[h:].astype(F32) + self.half_b[...].astype(F32)).astype(BF)
        self.sent_down = self.go(3, self.to_down, self.down, 3)

    def finish(self):
        total = self.part[self.to(0)].astype(F32)
        self.sent_up.wait_recv()
        self.sent_down.wait_recv()
        total = total + self.up[...].astype(F32) + self.down[...].astype(F32)
        for copy in (self.far_up, self.far_down, self.sent_up, self.sent_down):
            copy.wait_send()
        return total


def axis_scratch(*block):
    half = (block[0] // 2, *block[1:])
    return [pltpu.VMEM(half, BF)] * 2 + [pltpu.VMEM(block, BF)] * 4


def final_kernel(
    part, grads, weights, dn1, attention, rest,
    over_z, over_y, from_opposite, share, shares, *refs,
):
    at = Place()
    greet(
        [
            at.sibling(), at.partner(), at.diagonal(), at.opposite(),
            at.along("z", 1), at.along("z", 3), at.along("x", 1), at.along("x", 3),
        ]
    )
    pair_refs, x_refs, z_refs = refs[:3], refs[3:9], refs[9:15]
    send, recv = refs[15:]
    base = 1 + 2 * PIECES
    x_scatter = AxisScatter(at, "x", grads, x_refs, send, recv, base)
    pair = PairScatter(at, part, pair_refs, send, recv)
    pair.forward()
    x_scatter.sides()
    over_z[...] = x_scatter.finish().astype(BF).reshape(over_z.shape)
    z_scatter = AxisScatter(at, "z", over_z, z_refs, send, recv, base + 4)
    z_scatter.sides()
    over_y[...] = z_scatter.finish().astype(BF)
    swap = push(over_y.at[1 - at.yh], from_opposite, send, recv, base + 8, at.opposite())
    swap.wait_recv()
    total = over_y[at.yh].astype(F32) + from_opposite[...].astype(F32)
    attention[...] = total[:, :768]
    gain_part = jnp.sum(total[:, :512] * weights[...].astype(F32), axis=1, keepdims=True)
    lane = lax.broadcasted_iota(jnp.int32, (32, 128), 1)
    share[...] = jnp.where(lane == 33, gain_part, total[:, 768:])
    copies = [
        push(share, shares.at[i], send, recv, base + 9 + i, device)
        for i, device in enumerate((at.sibling(), at.partner(), at.diagonal()))
    ]
    pair.finish(dn1)
    rest[...] = share[...]
    for i, copy in enumerate(copies):
        copy.wait_recv()
        rest[...] += shares[i]
    for copy in (swap, *copies):
        copy.wait_send()


def final(part, grads, weights, ident):
    vmem = pl.BlockSpec(memory_space=pltpu.VMEM)
    width = grads.shape[1]
    sems = 1 + 2 * PIECES + 12
    return pl.pallas_call(
        final_kernel,
        in_specs=[vmem] * 3,
        out_specs=[vmem] * 3,
        out_shape=[
            jax.ShapeDtypeStruct((LOCAL, D), F32),
            jax.ShapeDtypeStruct((32, 768), F32),
            jax.ShapeDtypeStruct((32, 128), F32),
        ],
        scratch_shapes=[
            pltpu.VMEM((4, 2, 32, width), BF),
            pltpu.VMEM((2, 32, width), BF),
            pltpu.VMEM((32, width), BF),
            pltpu.VMEM((32, 128), F32),
            pltpu.VMEM((3, 32, 128), F32),
            *pair_scratch(LOCAL, D),
            *axis_scratch(8, 32, width),
            *axis_scratch(2, 32, width),
            pltpu.SemaphoreType.DMA((sems,)),
            pltpu.SemaphoreType.DMA((sems,)),
        ],
        compiler_params=pltpu.CompilerParams(
            collective_id=ident, has_side_effects=True, vmem_limit_bytes=32 * MIB
        ),
        name="final",
    )(part.reshape(4, LOCAL, D), grads.reshape(4, 8, 32, width), weights)


def last_kernel(grads, gate, up, down, send, recv, here):
    at = Place()
    greet([at.opposite()])
    half = pl.ds(at.yh * 16, 16)
    kept, copies = [], []
    for i, out in enumerate((gate, up, down)):
        theirs = grads.at[i, :, pl.ds((1 - at.yh) * 32, 32)]
        copies.append(push(theirs, out.at[half], send, recv, i, at.opposite()))
        kept.append(keep(grads.at[i, :, pl.ds(at.yh * 32, 32)], out.at[half], here.at[i]))
    for copy in (*copies, *kept):
        copy.wait()


def last_exchange(grads, ident):
    hbm = pl.BlockSpec(memory_space=pl.ANY)
    return pl.pallas_call(
        last_kernel,
        in_specs=[hbm],
        out_specs=[hbm] * 3,
        out_shape=[jax.ShapeDtypeStruct((E, 32, FF), BF)] * 3,
        scratch_shapes=[
            pltpu.SemaphoreType.DMA((3,)),
            pltpu.SemaphoreType.DMA((3,)),
            pltpu.SemaphoreType.DMA((3,)),
        ],
        compiler_params=pltpu.CompilerParams(collective_id=ident, has_side_effects=True),
        name="last_exchange",
    )(grads)


def rotary_tables():
    half = HD // 2
    inverse = (10000.0 ** (-(np.arange(half, dtype=np.float64) * 2.0) / HD)).astype(np.float32)
    angles = np.arange(SEQ, dtype=np.float32)[:, None] * inverse[None, :]
    cosine, sine = np.cos(angles), np.sin(angles)
    wide_cosine = np.concatenate([cosine] * 4, axis=1)
    wide_sine = np.concatenate([-sine, sine] * 2, axis=1)
    return wide_cosine.astype(np.float32), wide_sine.astype(np.float32)


def swapped(values):
    lane = lax.broadcasted_iota(jnp.int32, values.shape, 1)
    low = (lane % HD) < HD // 2
    return jnp.where(low, pltpu.roll(values, 96, 1), pltpu.roll(values, 32, 1))


def rotated(values, cosine, sine):
    return values * cosine + swapped(values) * sine


def bias_block(key_segment, query_segment, first, rows):
    key_at = lax.broadcasted_iota(jnp.int32, (rows, BLOCK), 0)
    query_at = lax.broadcasted_iota(jnp.int32, (rows, BLOCK), 1) + first
    allowed = (key_segment == query_segment) & (key_at <= query_at)
    return jnp.where(allowed, 0.0, MASKED)


def segment_row(segments):
    return jnp.concatenate(
        [segments[rank, i : i + 1, :] for rank in range(4) for i in range(2)], axis=1
    ).astype(F32)


def attention_forward_kernel(
    hidden, weights, cosine, sine, segments, shares,
    part, normed, query, key, value, context_t, log_total, quad, bias, send, recv, here,
):
    at = Place()
    greet([at.along("x", 1), at.along("x", 3), at.along("z", 1), at.along("z", 3)])
    experts = QuadGather(at, shares.at[:, pl.ds(QUAD, QUAD)], quad, send, recv, here)
    experts.begin()
    gain = gain_rows(weights)[0:1, :]
    seg_row = segment_row(segments)
    seg_column = column_of(seg_row)
    for block in range(SEQ // BLOCK):
        rows = slice(block * BLOCK, (block + 1) * BLOCK)
        values = hidden[rows, :].astype(F32)
        scale = lax.rsqrt(jnp.mean(values * values, axis=-1, keepdims=True) + EPS)
        normed[rows, :] = (values * scale * gain).astype(BF)
    for half in range(2):
        columns = slice(half * 128, half * 128 + 128)
        pre = mm(normed[...], weights[:, columns])
        query[:, columns] = (rotated(pre, cosine[...], sine[...]) * 0.125).astype(BF)
    key_pre = mm(normed[...], weights[:, 256:384])
    key[...] = rotated(key_pre, cosine[...], sine[...]).astype(BF)
    value_pre = mm(normed[...], weights[:, 384:512])
    value[...] = value_pre.astype(BF)
    value_t = value_pre.T.astype(BF)
    for block in range(SEQ // BLOCK):
        first, end = block * BLOCK, (block + 1) * BLOCK
        bias[:end, :] = bias_block(seg_column[:end, :], seg_row[:, first:end], first, end)
        for head in range(HEADS):
            kv = slice((head // 2) * HD, (head // 2) * HD + HD)
            own = slice(head * HD, head * HD + HD)
            scores = mm_last(key[:end, kv], query[first:end, own]) + bias[:end, :]
            top = jnp.max(scores, axis=0, keepdims=True)
            powers = jnp.exp(scores - top)
            total = jnp.sum(powers, axis=0, keepdims=True)
            share = (powers * (1.0 / total)).astype(BF)
            context_t[own, first:end] = mm(value_t[kv, :end], share).astype(BF)
            log_total[head : head + 1, first:end] = top + jnp.log(total)
        if block == 0:
            experts.forward(0)
        if block == 1:
            experts.turn()
    experts.forward(1)
    context = context_t[...].T
    for block in range(SEQ // BLOCK):
        rows = slice(block * BLOCK, (block + 1) * BLOCK)
        part[rows, :] = mm_last(context[rows, :], weights[:, 512:768]).astype(BF)
    experts.finish()


def quad_sems():
    return [
        pltpu.SemaphoreType.DMA((QuadGather.COPIES,)),
        pltpu.SemaphoreType.DMA((QuadGather.COPIES,)),
        pltpu.SemaphoreType.DMA,
    ]


def attention_forward(hidden, weights, tables, segments, shares, ident):
    vmem = pl.BlockSpec(memory_space=pltpu.VMEM)
    hbm = pl.BlockSpec(memory_space=pl.ANY)
    return pl.pallas_call(
        attention_forward_kernel,
        in_specs=[vmem] * 5 + [hbm],
        out_specs=[vmem] * 7 + [hbm],
        out_shape=[
            jax.ShapeDtypeStruct((SEQ, D), BF),
            jax.ShapeDtypeStruct((SEQ, D), BF),
            jax.ShapeDtypeStruct((SEQ, HEADS * HD), BF),
            jax.ShapeDtypeStruct((SEQ, 128), BF),
            jax.ShapeDtypeStruct((SEQ, 128), BF),
            jax.ShapeDtypeStruct((HEADS * HD, SEQ), BF),
            jax.ShapeDtypeStruct((8, SEQ), F32),
            QUAD_SHAPE,
        ],
        scratch_shapes=[pltpu.VMEM((SEQ, BLOCK), F32), *quad_sems()],
        compiler_params=pltpu.CompilerParams(
            collective_id=ident, has_side_effects=True, vmem_limit_bytes=56 * MIB
        ),
        name="attention_forward",
    )(hidden, weights, *tables, segments, shares)


def attention_backward_kernel(
    dattn, normed, weights, cosine, sine, segments,
    query, key, value, context_t, log_total, rest, y_part,
    dn1, grads, y, bias, dcontext, dquery_t, dkey, dvalue, dall, dall_t, *refs,
):
    at = Place()
    greet([at.sibling(), at.ring(1), at.ring(3)])
    scatter = RingScatter(at, y_part, refs[:8], *refs[8:])
    for k in (2, 1, 3, 0):
        scatter.copy(k).start()
    seg_row = segment_row(segments)
    seg_column = column_of(seg_row)
    grads[:, 768:] = rest[...]
    dcontext[...] = mm(dattn[...], weights[:, 512:768]).astype(BF)
    scatter.far()
    output_grad_t = mm(context_t[...], dattn[...])
    grads[:, 512:768] = output_grad_t.T.astype(BF)
    key_t = key[...].astype(F32).T.astype(BF)
    dkey[...] = jnp.zeros_like(dkey)
    dvalue[...] = jnp.zeros_like(dvalue)
    for block in range(SEQ // BLOCK):
        first, end = block * BLOCK, (block + 1) * BLOCK
        bias[:end, :] = bias_block(seg_column[:end, :], seg_row[:, first:end], first, end)
        for head in range(HEADS):
            kv = slice((head // 2) * HD, (head // 2) * HD + HD)
            own = slice(head * HD, head * HD + HD)
            query_block = query[first:end, own]
            dcontext_block = dcontext[first:end, own]
            scores = mm_last(key[:end, kv], query_block) + bias[:end, :]
            share = jnp.exp(scores - log_total[head : head + 1, first:end])
            dshare = mm_last(value[:end, kv], dcontext_block)
            centre = jnp.sum(share * dshare, axis=0, keepdims=True)
            dscore = (share * (dshare - centre)).astype(BF)
            dquery_t[own, first:end] = mm(key_t[kv, :end], dscore) * 0.125
            dkey[:end, kv] += mm(dscore, query_block)
            dvalue[:end, kv] += mm(share.astype(BF), dcontext_block)
        if block == 1:
            scatter.up_side()
            scatter.down_side()
    turn = -sine[...]
    for half in range(2):
        rows = slice(half * 128, half * 128 + 128)
        piece = rotated(dquery_t[rows, :].T, cosine[...], turn)
        dall[:, rows] = piece.astype(BF)
        dall_t[rows, :] = piece.T.astype(BF)
    piece = rotated(dkey[...], cosine[...], turn)
    dall[:, 256:384] = piece.astype(BF)
    dall_t[256:384, :] = piece.T.astype(BF)
    dall[:, 384:512] = dvalue[...].astype(BF)
    dall_t[384:512, :] = dvalue[...].T.astype(BF)
    grads[:, 0:512] = mm(dall_t[...], normed[...]).T.astype(BF)
    for block in range(SEQ // BLOCK):
        rows = slice(block * BLOCK, (block + 1) * BLOCK)
        dn1[rows, :] = mm_last(dall[rows, :], weights[:, 0:512]).astype(BF)
    scatter.finish(y)


def attention_backward(
    dattn, normed, weights, tables, segments, kept, rest, y_part, ident
):
    vmem = pl.BlockSpec(memory_space=pltpu.VMEM)
    return pl.pallas_call(
        attention_backward_kernel,
        in_specs=[vmem] * 13,
        out_specs=[vmem] * 3,
        out_shape=[
            jax.ShapeDtypeStruct((SEQ, D), BF),
            jax.ShapeDtypeStruct((D, SMALL), BF),
            jax.ShapeDtypeStruct((LOCAL, D), F32),
        ],
        scratch_shapes=[
            pltpu.VMEM((SEQ, BLOCK), F32),
            pltpu.VMEM((SEQ, HEADS * HD), BF),
            pltpu.VMEM((HEADS * HD, SEQ), F32),
            pltpu.VMEM((SEQ, 128), F32),
            pltpu.VMEM((SEQ, 128), F32),
            pltpu.VMEM((SEQ, 512), BF),
            pltpu.VMEM((512, SEQ), BF),
            *ring_scratch(LOCAL, D),
            pltpu.SemaphoreType.DMA((8,)),
            pltpu.SemaphoreType.DMA((8,)),
        ],
        compiler_params=pltpu.CompilerParams(
            collective_id=ident, has_side_effects=True, vmem_limit_bytes=56 * MIB
        ),
        name="attention_backward",
    )(
        dattn, normed, weights, *tables, segments, *kept, rest, y_part,
    )


def experts_kernel(
    x_in, gate_in, d_in, quad_0, quad_1, quad_2, shares,
    y_out, dx_out, dgate_out, grads, quad_3,
    x, d, xt, dt, y, dx, gating, dgate, dgate_part, hidden, w, *refs,
):
    dx_scratch, dgate_scratch = refs[:5], refs[5:10]
    send, recv, here, load, store, fetch = refs[10:16]
    at = Place()
    step = pl.program_id(0)
    opening, closing = step == 0, step == STEPS - 1
    rows_at_once = 2 * LOCAL
    lane = lax.broadcasted_iota(jnp.int32, (LOCAL, 128), 1)
    own_first = at.yh * 16 + step * QUAD
    x_gather = RingGather(at, x_in, x, send, recv, here.at[0], 0)
    gate_gather = RingGather(at, gate_in, gating, send, recv, here.at[1], 9)
    gathers = (x_gather, gate_gather)
    scatters = (
        RingScatter(at, d, dx_scratch, send, recv, 18),
        RingScatter(at, dgate_part, dgate_scratch, send, recv, 26),
    )

    last_quad = QuadGather(at, shares.at[:, pl.ds(3 * QUAD, QUAD)], quad_3, *refs[16:])

    def fetches(quad):
        return [
            pltpu.make_async_copy(
                quad.at[g, i], w.at[:, :, :, pl.ds((g * QUAD + i) * FF, FF)],
                fetch.at[g * QUAD + i],
            )
            for g in range(3)
            for i in range(QUAD)
        ]

    def d_load(chip):
        two = pl.ds(chip * 2, 2)
        return pltpu.make_async_copy(d_in.at[two], d.at[two], load.at[chip])

    def y_store(chip):
        two = pl.ds(chip * 2, 2)
        return pltpu.make_async_copy(x.at[two], y_out.at[two], store.at[chip])

    @pl.when(opening)
    def _():
        greet(
            [
                at.sibling(), at.ring(1), at.ring(3),
                at.along("x", 1), at.along("x", 3), at.along("z", 1), at.along("z", 3),
            ]
        )
        for gather in gathers:
            gather.begin()
        for copy in fetches(quad_0):
            copy.start()
        last_quad.begin()
        for chip in range(4):
            d_load(chip).start()

    for copy in fetches(quad_0):
        copy.wait()

    def arrive(turn):
        @pl.when(turn == 0)
        def _():
            for gather in gathers:
                gather.kept().wait()
                gather.copy(0).wait_recv()

        @pl.when(turn == 1)
        def _():
            for gather in gathers:
                gather.forward_before()
                gather.forward_behind()
            for gather in gathers:
                gather.copy(4).wait_recv()
            last_quad.forward(0)

        @pl.when(turn == 2)
        def _():
            for gather in gathers:
                gather.forward_across()
            for gather in gathers:
                gather.copy(6).wait_recv()
            last_quad.turn()

        @pl.when(turn == 3)
        def _():
            for gather in gathers:
                gather.copy(7).wait_recv()
                gather.copy(8).wait_recv()
            last_quad.forward(1)

    def leave(turn):
        @pl.when(turn == 0)
        def _():
            for scatter in scatters:
                scatter.copy(2).start()

        @pl.when(turn == 1)
        def _():
            for scatter in scatters:
                scatter.copy(1).start()
                scatter.far()

        @pl.when(turn == 2)
        def _():
            for scatter in scatters:
                scatter.copy(3).start()
                scatter.up_side()

        @pl.when(turn == 3)
        def _():
            for scatter in scatters:
                scatter.copy(0).start()
                scatter.down_side()

    def tokens_block(turn, carry):
        inward = jnp.where(turn == 0, 0, jnp.where(turn == 1, 3, turn - 1))
        outward = jnp.where(turn == 0, 2, jnp.where(turn == 3, 0, turn * 2 - 1))
        chip = at.chip(jnp.where(closing, outward, inward))
        two = pl.ds(chip * 2, 2)
        rows = pl.ds(pl.multiple_of(chip * rows_at_once, rows_at_once), rows_at_once)

        @pl.when(opening)
        def _():
            arrive(turn)
            d_load(chip).wait()
            xt[:, rows] = x[two].reshape(rows_at_once, D).T
            dt[:, rows] = d[two].reshape(rows_at_once, D).T
            y[rows, :] = jnp.zeros((rows_at_once, D), F32)
            dx[rows, :] = jnp.zeros((rows_at_once, D), F32)
            dgate[rows, :] = jnp.zeros((rows_at_once, 128), F32)

        gate_up = w[:, :, :, 0 : 2 * F].reshape(D, 2 * F)
        down = w[:, :, :, 2 * F :].reshape(D, F)
        for core in range(2):
            slot = chip * 2 + core
            part = pl.ds(pl.multiple_of(slot * LOCAL, LOCAL), LOCAL)
            both = mm(x[slot], gate_up)
            gate, up = both[:, :F], both[:, F:]
            dact = mm(d[slot], down)
            turned = pltpu.roll(gating[slot], lax.rem(128 - own_first, 128), 1)
            factor = jnp.concatenate(
                [jnp.broadcast_to(turned[:, i : i + 1], (LOCAL, FF)) for i in range(QUAD)],
                axis=1,
            )
            q = 1.0 / (1.0 + jnp.exp(-gate))
            silu = gate * q
            act = silu * up
            product = act * dact
            sums = dgate[part, :]
            for i in range(QUAD):
                own = jnp.sum(product[:, i * FF : (i + 1) * FF], axis=1, keepdims=True)
                sums = jnp.where(lane == own_first + i, own, sums)
            dgate[part, :] = sums
            dact = dact * factor
            hidden[part, 0:F] = (dact * up * (q + silu * (1.0 - q))).astype(BF)
            hidden[part, F : 2 * F] = (dact * silu).astype(BF)
            hidden[part, 2 * F :] = (act * factor).astype(BF)
        y[rows, :] += mm_last(hidden[rows, 2 * F :], down)
        dx[rows, :] += mm_last(hidden[rows, 0 : 2 * F], gate_up)

        @pl.when(closing)
        def _():
            x[two] = y[rows, :].astype(BF).reshape(2, LOCAL, D)
            d[two] = dx[rows, :].astype(BF).reshape(2, LOCAL, D)
            dgate_part[two] = dgate[rows, :].astype(BF).reshape(2, LOCAL, 128)
            y_store(chip).start()
            leave(turn)

        return carry

    lax.fori_loop(0, 4, tokens_block, 0)

    for number, quad in enumerate((quad_1, quad_2, quad_3)):

        @pl.when(step == number)
        def _():
            for copy in fetches(quad):
                copy.start()

    @pl.when(opening)
    def _():
        for gather in gathers:
            gather.sent()
        last_quad.finish()

    def grads_block(block, carry):
        rows = pl.ds(pl.multiple_of(block * 512, 512), 512)
        both = mm(xt[rows, :], hidden[:, 0 : 2 * F]).astype(BF)
        for g in range(2):
            for i in range(QUAD):
                first = (g * QUAD + i) * FF
                grads[g, i, rows, :] = both[:, first : first + FF]
        down = mm(dt[rows, :], hidden[:, 2 * F :]).astype(BF)
        for i in range(QUAD):
            grads[2, i, rows, :] = down[:, i * FF : (i + 1) * FF]
        return carry

    lax.fori_loop(0, D // 512, grads_block, 0)

    @pl.when(closing)
    def _():
        scatters[0].finish(dx_out)
        scatters[1].finish(dgate_out)
        for chip in range(4):
            y_store(chip).wait()


def experts(x, gating, d, quads, shares, ident):
    hbm = pl.BlockSpec(memory_space=pl.ANY)

    def whole(rows, columns):
        return pl.BlockSpec((rows, columns), lambda step: (0, 0), pipeline_mode=pl.Buffered(1))

    return pl.pallas_call(
        experts_kernel,
        grid=(STEPS,),
        in_specs=[hbm] * 7,
        out_specs=[
            hbm,
            whole(LOCAL, D),
            whole(LOCAL, 128),
            pl.BlockSpec(
                (3, QUAD, D, FF), lambda step: (0, step, 0, 0), pipeline_mode=pl.Buffered(1)
            ),
            hbm,
        ],
        out_shape=[
            jax.ShapeDtypeStruct((8, LOCAL, D), BF),
            jax.ShapeDtypeStruct((LOCAL, D), F32),
            jax.ShapeDtypeStruct((LOCAL, 128), F32),
            jax.ShapeDtypeStruct((3, STEPS * QUAD, D, FF), BF),
            QUAD_SHAPE,
        ],
        scratch_shapes=[
            pltpu.VMEM((8, LOCAL, D), BF),
            pltpu.VMEM((8, LOCAL, D), BF),
            pltpu.VMEM((D, TOKENS), BF),
            pltpu.VMEM((D, TOKENS), BF),
            pltpu.VMEM((TOKENS, D), F32),
            pltpu.VMEM((TOKENS, D), F32),
            pltpu.VMEM((8, LOCAL, 128), F32),
            pltpu.VMEM((TOKENS, 128), F32),
            pltpu.VMEM((8, LOCAL, 128), BF),
            pltpu.VMEM((TOKENS, 3 * F), BF),
            pltpu.VMEM((4, 4, 64, 3 * F), BF),
            *ring_scratch(LOCAL, D, False),
            *ring_scratch(LOCAL, 128, False),
            pltpu.SemaphoreType.DMA((34,)),
            pltpu.SemaphoreType.DMA((34,)),
            pltpu.SemaphoreType.DMA((2,)),
            pltpu.SemaphoreType.DMA((4,)),
            pltpu.SemaphoreType.DMA((4,)),
            pltpu.SemaphoreType.DMA((3 * QUAD,)),
            *quad_sems(),
        ],
        compiler_params=pltpu.CompilerParams(
            collective_id=ident, has_side_effects=True, vmem_limit_bytes=63 * MIB
        ),
        name="experts",
    )(x, gating, d, *quads, shares)[:4]


def norm_scale(values):
    return lax.rsqrt(jnp.mean(values * values, axis=-1, keepdims=True) + EPS)


def norm_grad(values, gain, dnormed):
    scale = norm_scale(values)
    unit = values * scale
    weighted = dnormed * gain
    dvalues = scale * (weighted - unit * jnp.mean(weighted * unit, axis=-1, keepdims=True))
    return dvalues


def on_device(
    hidden_in, out_grad, attn_gain, query_weight, key_weight, value_weight, output_weight,
    moe_gain, router_weight, expert_gate, expert_up, expert_down, expert_ids, segment_ids,
):
    small = jnp.concatenate(
        [
            query_weight, key_weight, value_weight, output_weight,
            router_weight, attn_gain[:, None], moe_gain[:, None], jnp.zeros((32, 94), BF),
        ],
        axis=1,
    )
    segment = jnp.pad(segment_ids.reshape(2, 128), ((0, 6), (0, 0)))
    hidden_all, segments, d, small, shares, quad_0 = startup(
        hidden_in, segment, out_grad, (expert_gate, expert_up, expert_down), small, 0
    )
    tables = tuple(jnp.asarray(t) for t in rotary_tables())
    named = jnp.any(
        expert_ids[:, :, None] == jnp.arange(128, dtype=jnp.int32)[None, None, :], axis=1
    ).astype(F32)

    part, normed_all, *kept, quad_1 = attention_forward(
        hidden_all, small, tables, segments, shares, 1
    )
    middle, normed_moe, gating, quad_2 = middle_of(part, hidden_in, small, named, shares, 2)
    y, dx, dgate, expert_grads = experts(
        normed_moe, gating, d, (quad_0, quad_1, quad_2), shares, 3
    )
    expert_grads = lax.psum_scatter(expert_grads, PLANE, scatter_dimension=2, tiled=True)
    dattn, dmiddle, rest = dmiddle_of(dx, dgate, gating, middle, normed_moe, out_grad, small, 4)
    dn1, grads, y = attention_backward(
        dattn, normed_all, small, tables, segments, kept, rest, y, 5
    )
    block_out = (middle + y).astype(BF)
    weights = jnp.concatenate([query_weight, key_weight, value_weight], axis=1)
    dn1, attention_grads, rest = final(dn1, grads, weights, 6)
    hidden = hidden_in.astype(F32)
    dhidden = norm_grad(hidden, small[:, 800].astype(F32), dn1)
    hidden_grad = dmiddle + dhidden
    expert_grads = [share.astype(F32) for share in last_exchange(expert_grads, 7)]
    return (
        block_out,
        hidden_grad,
        rest[:, 33] / attn_gain.astype(F32),
        attention_grads[:, 0:256],
        attention_grads[:, 256:384],
        attention_grads[:, 384:512],
        attention_grads[:, 512:768],
        rest[:, 32],
        rest[:, :32],
        *expert_grads,
    )


def solution(mesh):
    fine = Mesh(np.asarray(mesh.devices).reshape(4, 4, 2, 2, 2), ALL)
    return jax.shard_map(
        on_device,
        mesh=fine,
        in_specs=(
            P(ALL, None),
            P(ALL, None),
            P(DP),
            P(DP, TENSOR),
            P(DP, TENSOR),
            P(DP, TENSOR),
            P(DP, TENSOR),
            P(DP),
            P(DP, None),
            P(None, DP, TENSOR),
            P(None, DP, TENSOR),
            P(None, DP, TENSOR),
            P(ALL, None),
            P(ALL),
        ),
        out_specs=(
            P(ALL, None),
            P(ALL, None),
            P(DP),
            P(DP, TENSOR),
            P(DP, TENSOR),
            P(DP, TENSOR),
            P(DP, TENSOR),
            P(DP),
            P(DP, None),
            P(None, DP, TENSOR),
            P(None, DP, TENSOR),
            P(None, DP, TENSOR),
        ),
        check_vma=False,
    )
```

```python
import jax
import jax.numpy as jnp
import numpy as np
from jax import lax
from jax.experimental import pallas as pl
from jax.experimental.pallas import tpu as pltpu
from jax.sharding import Mesh
from jax.sharding import PartitionSpec as P

D = 1024
HD = 64
E = 32
SEQ = 1024
LOCAL = 256
HEADS = 4
QUAD = 4
FF = 128
F = QUAD * FF
EPS = 1e-06
MASKED = -1e30
BLOCK = 256
TOKENS = 2048
STEPS = 4

DP = ("x", "z", "yh")
TENSOR = ("yl", "core")
RING = ("yh", "yl", "core")
PLANE = ("x", "z")
ALL = ("x", "z", "yh", "yl", "core")

F32 = jnp.float32
BF = jnp.bfloat16
LAST = (((1,), (1,)), ((), ()))
MIB = 1024 * 1024
MESH = pl.DeviceIdType.MESH
SMALL = 896


def mm(a, b):
    return jnp.dot(a, b, preferred_element_type=F32)


def mm_last(a, b):
    return lax.dot_general(a, b, LAST, preferred_element_type=F32)


class Place:
    def __init__(self):
        self.x = lax.axis_index("x")
        self.z = lax.axis_index("z")
        self.yh = lax.axis_index("yh")
        self.yl = lax.axis_index("yl")
        self.core = lax.axis_index("core")
        self.y = self.yh * 2 + self.yl

    def chip(self, k):
        return lax.rem(self.y + k, 4)

    def ring(self, k):
        chip = self.chip(k)
        return {"yh": chip // 2, "yl": lax.rem(chip, 2)}

    def along(self, axis, k):
        return {axis: lax.rem(getattr(self, axis) + k, 4)}

    def sibling(self):
        return {"core": 1 - self.core}

    def partner(self):
        return {"yl": 1 - self.yl}

    def diagonal(self):
        return {"yl": 1 - self.yl, "core": 1 - self.core}

    def opposite(self):
        return {"yh": 1 - self.yh}


def greet(devices):
    barrier = pltpu.get_barrier_semaphore()
    for device in devices:
        pl.semaphore_signal(barrier, inc=1, device_id=device, device_id_type=MESH)
    pl.semaphore_wait(barrier, len(devices))


def remote(src, dst, send, recv, i, device):
    return pltpu.make_async_remote_copy(
        src_ref=src, dst_ref=dst, send_sem=send.at[i], recv_sem=recv.at[i],
        device_id=device, device_id_type=MESH,
    )


def push(src, dst, send, recv, i, device):
    copy = remote(src, dst, send, recv, i, device)
    copy.start()
    return copy


def keep(src, dst, sem):
    copy = pltpu.make_async_copy(src, dst, sem)
    copy.start()
    return copy


class RingGather:
    def __init__(self, at, own, out, send, recv, here, base=0):
        self.at, self.own, self.out, self.base = at, own, out, base
        self.send, self.recv, self.here = send, recv, here
        half = own.shape[0] // 2
        lo, hi = pl.ds(0, half), pl.ds(half, half)
        me, before, behind, across = (out.at[self.slot(k)] for k in (0, 3, 1, 2))
        near, up, down = at.sibling(), at.ring(1), at.ring(3)
        self.plan = [
            (own, me, near),
            (own, me, up),
            (own, me, down),
            (before.at[lo], before.at[lo], up),
            (before, before, near),
            (behind.at[hi], behind.at[hi], down),
            (behind, behind, near),
            (across.at[lo], across.at[lo], near),
            (across.at[hi], across.at[hi], near),
        ]

    def slot(self, k):
        return self.at.chip(k) * 2 + self.at.core

    def copy(self, i):
        src, dst, device = self.plan[i]
        return remote(src, dst, self.send, self.recv, self.base + i, device)

    def kept(self):
        return pltpu.make_async_copy(self.own, self.out.at[self.slot(0)], self.here)

    def begin(self):
        self.kept().start()
        for i in (1, 2, 0):
            self.copy(i).start()

    def forward_before(self):
        self.copy(1).wait_recv()
        self.copy(3).start()
        self.copy(4).start()

    def forward_behind(self):
        self.copy(2).wait_recv()
        self.copy(5).start()
        self.copy(6).start()

    def forward_across(self):
        self.copy(3).wait_recv()
        self.copy(7).start()
        self.copy(5).wait_recv()
        self.copy(8).start()

    def sent(self):
        for i in range(9):
            self.copy(i).wait_send()


class PairGather:
    def __init__(self, at, own, out, send, recv, here, base, pieces):
        self.at, self.out, self.send, self.recv, self.base = at, out, send, recv, base
        size = own.shape[0] // pieces
        self.parts = [pl.ds(i * size, size) for i in range(pieces)]
        me = at.yl * 2 + at.core
        self.other = (1 - at.yl) * 2 + at.core
        self.kept = keep(own, out.at[me], here)
        self.far = [
            push(own.at[part], out.at[me, part], send, recv, base + 1 + i, at.partner())
            for i, part in enumerate(self.parts)
        ]
        self.near = [push(own, out.at[me], send, recv, base, at.sibling())]

    def forward(self):
        for i, part in enumerate(self.parts):
            self.far[i].wait_recv()
            view = self.out.at[self.other, part]
            index = self.base + 1 + len(self.parts) + i
            self.near.append(push(view, view, self.send, self.recv, index, self.at.sibling()))

    def finish(self):
        for copy in self.near:
            copy.wait_recv()
        for copy in (*self.far, *self.near):
            copy.wait_send()
        self.kept.wait()


PIECES = 4


class AxisGather:
    def __init__(self, at, axis, view, send, recv, base):
        self.up, self.down = at.along(axis, 1), at.along(axis, 3)
        self.view, self.send, self.recv, self.base = view, send, recv, base

    def go(self, i, view, device):
        return push(view, view, self.send, self.recv, self.base + i, device)

    def begin(self):
        self.first = [
            self.go(0, self.view(0, "all"), self.up), self.go(1, self.view(0, "all"), self.down),
        ]

    def forward(self):
        self.first[0].wait_recv()
        self.far = [self.go(2, self.view(3, "low"), self.up)]
        self.first[1].wait_recv()
        self.far.append(self.go(3, self.view(1, "high"), self.down))

    def finish(self):
        for copy in self.far:
            copy.wait_recv()
        for copy in (*self.first, *self.far):
            copy.wait_send()


def halves_of(ref, first, size):
    spans = {"all": (0, size), "low": (0, size // 2), "high": (size // 2, size // 2)}
    return lambda part: ref.at[pl.ds(first + spans[part][0], spans[part][1])]


class QuadGather:
    COPIES = 16

    def __init__(self, at, own, out, send, recv, here, base=0):
        self.own, self.out, self.here = own, out, here
        self.at, self.send, self.recv, self.base = at, send, recv, base
        low, high, whole = pl.ds(0, 32), pl.ds(32, 32), pl.ds(0, 64)
        first, second = pl.ds(0, 2), pl.ds(2, 2)

        def z_of(k):
            return lax.rem(at.z + k, 4)

        def x_of(k):
            return lax.rem(at.x + k, 4)

        views = (
            ("z", lambda k, rows: out.at[:, first, at.x, z_of(k), rows]),
            ("x", lambda k, rows: out.at[:, second, x_of(k), at.z, rows]),
            ("x", lambda k, rows: out.at[:, first, x_of(k), :, rows]),
            ("z", lambda k, rows: out.at[:, second, :, z_of(k), rows]),
        )
        self.plan = []
        for stage in (views[:2], views[2:]):
            for axis, view in stage:
                self.plan.append((view(0, whole), at.along(axis, 1)))
                self.plan.append((view(0, whole), at.along(axis, 3)))
            for axis, view in stage:
                self.plan.append((view(3, low), at.along(axis, 1)))
                self.plan.append((view(1, high), at.along(axis, 3)))

    def copy(self, i):
        view, device = self.plan[i]
        return remote(view, view, self.send, self.recv, self.base + i, device)

    def kept(self):
        return pltpu.make_async_copy(
            self.own, self.out.at[:, :, self.at.x, self.at.z], self.here
        )

    def begin(self):
        self.kept().start()
        self.kept().wait()
        for i in range(4):
            self.copy(i).start()

    def forward(self, stage):
        for i in range(4):
            self.copy(8 * stage + i).wait_recv()
            self.copy(8 * stage + 4 + i).start()

    def turn(self):
        for i in range(4, 8):
            self.copy(i).wait_recv()
        for i in range(8, 12):
            self.copy(i).start()

    def finish(self):
        for i in range(12, 16):
            self.copy(i).wait_recv()
        for i in range(16):
            self.copy(i).wait_send()


QUAD_SHAPE = jax.ShapeDtypeStruct((3, QUAD, 4, 4, 64, FF), BF)


def startup_kernel(
    hidden, segment, small, hidden_all, segment_all, small_all, send, recv, here
):
    at = Place()
    greet(
        [
            at.sibling(), at.partner(), at.diagonal(), at.opposite(),
            at.along("x", 1), at.along("x", 3), at.along("z", 1), at.along("z", 3),
        ]
    )
    rank = at.yl * 2 + at.core
    mine = small_all.at[(at.x * 4 + at.z) * 2 + at.yh]
    small_kept = keep(small, mine, here.at[0])
    copies = [push(small, mine, send, recv, 0, at.opposite())]
    copies.extend(
        push(segment, segment_all.at[rank], send, recv, 1 + i, device)
        for i, device in enumerate((at.sibling(), at.partner(), at.diagonal()))
    )
    pair = PairGather(at, hidden, hidden_all, send, recv, here.at[1], 12, PIECES)
    seg_here = keep(segment, segment_all.at[rank], here.at[2])
    over_z = AxisGather(
        at, "z",
        lambda k, part: halves_of(small_all, (at.x * 4 + lax.rem(at.z + k, 4)) * 2, 2)(part),
        send, recv, 4,
    )
    over_x = AxisGather(
        at, "x", lambda k, part: halves_of(small_all, lax.rem(at.x + k, 4) * 8, 8)(part),
        send, recv, 8,
    )
    small_kept.wait()
    copies[0].wait_recv()
    over_z.begin()
    over_z.forward()
    over_z.finish()
    over_x.begin()
    pair.forward()
    over_x.forward()
    pair.finish()
    seg_here.wait()
    for copy in copies[1:]:
        copy.wait_recv()
    over_x.finish()
    for copy in copies:
        copy.wait_send()


def startup(hidden, segment, small, ident):
    hbm = pl.BlockSpec(memory_space=pl.ANY)
    sems = 12 + 1 + 2 * PIECES
    hidden_all, segment_all, small_all = pl.pallas_call(
        startup_kernel,
        in_specs=[hbm] * 3,
        out_specs=[hbm] * 3,
        out_shape=[
            jax.ShapeDtypeStruct((4, *hidden.shape), hidden.dtype),
            jax.ShapeDtypeStruct((4, *segment.shape), segment.dtype),
            jax.ShapeDtypeStruct((32, 32, SMALL), small.dtype),
        ],
        scratch_shapes=[
            pltpu.SemaphoreType.DMA((sems,)),
            pltpu.SemaphoreType.DMA((sems,)),
            pltpu.SemaphoreType.DMA((3,)),
        ],
        compiler_params=pltpu.CompilerParams(collective_id=ident, has_side_effects=True),
        name="startup",
    )(hidden, segment, small)
    return hidden_all.reshape(SEQ, D), segment_all, small_all.reshape(D, SMALL)


class RingScatter:
    def __init__(self, at, part, scratch, send, recv, base=0):
        self.at, self.part, self.send, self.recv, self.base = at, part, send, recv, base
        near, half_a, half_b, self.full_up, self.full_down = scratch[:5]
        to_far, to_up, to_down = scratch[5:] or [
            part.at[at.chip(k) * 2 + at.core] for k in (2, 1, 3)
        ]
        self.near, self.half_a, self.half_b = near, half_a, half_b
        self.to_far, self.to_up, self.to_down = to_far, to_up, to_down
        self.half = half_a.shape[0]
        self.lo, self.hi = pl.ds(0, self.half), pl.ds(self.half, self.half)
        up, down = at.ring(1), at.ring(3)
        self.plan = {
            k: (part.at[at.chip(k) * 2 + 1 - at.core], near.at[k], at.sibling()) for k in range(4)
        }
        self.plan[4] = (to_far.at[self.lo], half_a, up)
        self.plan[5] = (to_far.at[self.hi], half_b, down)
        self.plan[6] = (to_up, self.full_up, up)
        self.plan[7] = (to_down, self.full_down, down)

    def copy(self, i):
        src, dst, device = self.plan[i]
        return remote(src, dst, self.send, self.recv, self.base + i, device)

    def chip_sum(self, k):
        self.copy(k).wait_recv()
        own = self.part[self.at.chip(k) * 2 + self.at.core]
        return own.astype(F32) + self.near[k].astype(F32)

    def far(self):
        self.to_far[...] = self.chip_sum(2).astype(BF)
        self.copy(4).start()
        self.copy(5).start()

    def up_side(self):
        total = self.chip_sum(1)
        self.copy(4).wait_recv()
        self.to_up[self.lo, :] = (total[: self.half] + self.half_a[...].astype(F32)).astype(BF)
        self.to_up[self.hi, :] = total[self.half :].astype(BF)
        self.copy(6).start()

    def down_side(self):
        total = self.chip_sum(3)
        self.copy(5).wait_recv()
        self.to_down[self.lo, :] = total[: self.half].astype(BF)
        self.to_down[self.hi, :] = (total[self.half :] + self.half_b[...].astype(F32)).astype(BF)
        self.copy(7).start()

    def finish(self, out):
        out[...] = self.chip_sum(0)
        self.copy(6).wait_recv()
        out[...] += self.full_up[...].astype(F32)
        self.copy(7).wait_recv()
        out[...] += self.full_down[...].astype(F32)
        for i in range(8):
            self.copy(i).wait_send()


def ring_scratch(rows, columns, own_sends=True):
    block, half = pltpu.VMEM((rows, columns), BF), pltpu.VMEM((rows // 2, columns), BF)
    scratch = [pltpu.VMEM((4, rows, columns), BF), half, half, block, block]
    return scratch + [block] * 3 if own_sends else scratch


class PairScatter:
    def __init__(self, at, part, scratch, send, recv, base=0):
        self.at, self.part, self.send, self.recv, self.base = at, part, send, recv, base
        self.near, self.far_rows, self.to_far = scratch
        size = self.to_far.shape[0] // PIECES
        self.parts = [pl.ds(i * size, size) for i in range(PIECES)]
        self.other, self.own = (1 - at.yl) * 2, at.yl * 2

    def go(self, i, src, dst, device):
        return push(src, dst, self.send, self.recv, self.base + i, device)

    def begin_far(self):
        slot = self.other + 1 - self.at.core
        self.first = [
            self.go(i, self.part.at[slot, rows], self.near.at[1, rows], self.at.sibling())
            for i, rows in enumerate(self.parts)
        ]

    def begin_own(self):
        slot = self.own + 1 - self.at.core
        self.second = self.go(PIECES, self.part.at[slot], self.near.at[0], self.at.sibling())

    def forward(self):
        self.sent = []
        for i, rows in enumerate(self.parts):
            self.first[i].wait_recv()
            own = self.part[self.other + self.at.core, rows, :].astype(F32)
            self.to_far[rows, :] = (own + self.near[1, rows, :].astype(F32)).astype(BF)
            far = self.far_rows.at[rows]
            self.sent.append(self.go(PIECES + 1 + i, self.to_far.at[rows], far, self.at.partner()))

    def finish(self, out):
        self.second.wait_recv()
        out[...] = self.part[self.own + self.at.core].astype(F32) + self.near[0].astype(F32)
        for i, rows in enumerate(self.parts):
            self.sent[i].wait_recv()
            out[rows, :] += self.far_rows[rows, :].astype(F32)
        for copy in (*self.first, self.second, *self.sent):
            copy.wait_send()


def pair_scratch(rows, columns):
    block = pltpu.VMEM((rows, columns), BF)
    return [pltpu.VMEM((2, rows, columns), BF), block, block]


def gain_rows(small):
    return small[:, 768:896].astype(F32).T[32:40, :]


def column_of(row):
    return jnp.broadcast_to(row, (8, row.shape[1])).T[:, 0:1]


class AxisScatter:
    def __init__(self, at, axis, part, scratch, send, recv, base):
        self.at, self.axis, self.part, self.base = at, axis, part, base
        self.send, self.recv = send, recv
        self.half_a, self.half_b, self.up, self.down, self.to_up, self.to_down = scratch
        self.half = part.shape[1] // 2
        lo, hi = pl.ds(0, self.half), pl.ds(self.half, self.half)
        far = part.at[self.to(2)]
        self.far_up = self.go(0, far.at[lo], self.half_a, 1)
        self.far_down = self.go(1, far.at[hi], self.half_b, 3)

    def to(self, k):
        return self.at.along(self.axis, k)[self.axis]

    def go(self, i, src, dst, k):
        return push(src, dst, self.send, self.recv, self.base + i, self.at.along(self.axis, k))

    def sides(self):
        h = self.half
        self.far_up.wait_recv()
        block = self.part[self.to(1)]
        self.to_up[:h] = (block[:h].astype(F32) + self.half_a[...].astype(F32)).astype(BF)
        self.to_up[h:] = block[h:]
        self.sent_up = self.go(2, self.to_up, self.up, 1)
        self.far_down.wait_recv()
        block = self.part[self.to(3)]
        self.to_down[:h] = block[:h]
        self.to_down[h:] = (block[h:].astype(F32) + self.half_b[...].astype(F32)).astype(BF)
        self.sent_down = self.go(3, self.to_down, self.down, 3)

    def finish(self):
        total = self.part[self.to(0)].astype(F32)
        self.sent_up.wait_recv()
        self.sent_down.wait_recv()
        total = total + self.up[...].astype(F32) + self.down[...].astype(F32)
        for copy in (self.far_up, self.far_down, self.sent_up, self.sent_down):
            copy.wait_send()
        return total


def axis_scratch(*block):
    half = (block[0] // 2, *block[1:])
    return [pltpu.VMEM(half, BF)] * 2 + [pltpu.VMEM(block, BF)] * 4


def final_kernel(
    part, grads, weights, dn1, attention, rest,
    over_z, over_y, from_opposite, share, shares, *refs,
):
    at = Place()
    greet(
        [
            at.sibling(), at.partner(), at.diagonal(), at.opposite(),
            at.along("z", 1), at.along("z", 3), at.along("x", 1), at.along("x", 3),
        ]
    )
    pair_refs, x_refs, z_refs = refs[:3], refs[3:9], refs[9:15]
    send, recv = refs[15:]
    base = 1 + 2 * PIECES
    x_scatter = AxisScatter(at, "x", grads, x_refs, send, recv, base)
    pair = PairScatter(at, part, pair_refs, send, recv)
    pair.begin_far()
    pair.begin_own()
    pair.forward()
    x_scatter.sides()
    over_z[...] = x_scatter.finish().astype(BF).reshape(over_z.shape)
    z_scatter = AxisScatter(at, "z", over_z, z_refs, send, recv, base + 4)
    z_scatter.sides()
    over_y[...] = z_scatter.finish().astype(BF)
    swap = push(over_y.at[1 - at.yh], from_opposite, send, recv, base + 8, at.opposite())
    swap.wait_recv()
    total = over_y[at.yh].astype(F32) + from_opposite[...].astype(F32)
    attention[...] = total[:, :768]
    gain_part = jnp.sum(total[:, :512] * weights[...].astype(F32), axis=1, keepdims=True)
    lane = lax.broadcasted_iota(jnp.int32, (32, 128), 1)
    share[...] = jnp.where(lane == 33, gain_part, total[:, 768:])
    copies = [
        push(share, shares.at[i], send, recv, base + 9 + i, device)
        for i, device in enumerate((at.sibling(), at.partner(), at.diagonal()))
    ]
    pair.finish(dn1)
    rest[...] = share[...]
    for i, copy in enumerate(copies):
        copy.wait_recv()
        rest[...] += shares[i]
    for copy in (swap, *copies):
        copy.wait_send()


def final(part, grads, weights, ident):
    vmem = pl.BlockSpec(memory_space=pltpu.VMEM)
    width = grads.shape[1]
    sems = 1 + 2 * PIECES + 12
    return pl.pallas_call(
        final_kernel,
        in_specs=[vmem] * 3,
        out_specs=[vmem] * 3,
        out_shape=[
            jax.ShapeDtypeStruct((LOCAL, D), F32),
            jax.ShapeDtypeStruct((32, 768), F32),
            jax.ShapeDtypeStruct((32, 128), F32),
        ],
        scratch_shapes=[
            pltpu.VMEM((4, 2, 32, width), BF),
            pltpu.VMEM((2, 32, width), BF),
            pltpu.VMEM((32, width), BF),
            pltpu.VMEM((32, 128), F32),
            pltpu.VMEM((3, 32, 128), F32),
            *pair_scratch(LOCAL, D),
            *axis_scratch(8, 32, width),
            *axis_scratch(2, 32, width),
            pltpu.SemaphoreType.DMA((sems,)),
            pltpu.SemaphoreType.DMA((sems,)),
        ],
        compiler_params=pltpu.CompilerParams(
            collective_id=ident, has_side_effects=True, vmem_limit_bytes=32 * MIB
        ),
        name="final",
    )(part.reshape(4, LOCAL, D), grads.reshape(4, 8, 32, width), weights)


def last_kernel(grads, gate, up, down, send, recv, here):
    at = Place()
    greet([at.opposite()])
    half = pl.ds(at.yh * 16, 16)
    kept, copies = [], []
    for i, out in enumerate((gate, up, down)):
        theirs = grads.at[i, :, pl.ds((1 - at.yh) * 32, 32)]
        copies.append(push(theirs, out.at[half], send, recv, i, at.opposite()))
        kept.append(keep(grads.at[i, :, pl.ds(at.yh * 32, 32)], out.at[half], here.at[i]))
    for copy in (*copies, *kept):
        copy.wait()


def last_exchange(grads, ident):
    hbm = pl.BlockSpec(memory_space=pl.ANY)
    return pl.pallas_call(
        last_kernel,
        in_specs=[hbm],
        out_specs=[hbm] * 3,
        out_shape=[jax.ShapeDtypeStruct((E, 32, FF), BF)] * 3,
        scratch_shapes=[
            pltpu.SemaphoreType.DMA((3,)),
            pltpu.SemaphoreType.DMA((3,)),
            pltpu.SemaphoreType.DMA((3,)),
        ],
        compiler_params=pltpu.CompilerParams(collective_id=ident, has_side_effects=True),
        name="last_exchange",
    )(grads)


def rotary_tables():
    half = HD // 2
    inverse = (10000.0 ** (-(np.arange(half, dtype=np.float64) * 2.0) / HD)).astype(np.float32)
    angles = np.arange(SEQ, dtype=np.float32)[:, None] * inverse[None, :]
    cosine, sine = np.cos(angles), np.sin(angles)
    wide_cosine = np.concatenate([cosine] * 4, axis=1)
    wide_sine = np.concatenate([-sine, sine] * 2, axis=1)
    return wide_cosine.astype(np.float32), wide_sine.astype(np.float32)


def swapped(values):
    lane = lax.broadcasted_iota(jnp.int32, values.shape, 1)
    low = (lane % HD) < HD // 2
    return jnp.where(low, pltpu.roll(values, 96, 1), pltpu.roll(values, 32, 1))


def rotated(values, cosine, sine):
    return values * cosine + swapped(values) * sine


def bias_block(key_segment, query_segment, first, rows):
    key_at = lax.broadcasted_iota(jnp.int32, (rows, BLOCK), 0)
    query_at = lax.broadcasted_iota(jnp.int32, (rows, BLOCK), 1) + first
    allowed = (key_segment == query_segment) & (key_at <= query_at)
    return jnp.where(allowed, 0.0, MASKED)


def segment_row(segments):
    return jnp.concatenate(
        [segments[rank, i : i + 1, :] for rank in range(4) for i in range(2)], axis=1
    ).astype(F32)


def gain_rows(small):
    return small[:, 768:896].astype(F32).T[32:40, :]


def column_of(row):
    return jnp.broadcast_to(row, (8, row.shape[1])).T[:, 0:1]


def front_kernel(
    hidden, weights, cosine, sine, segments, own_hidden, named, gate, up, down, out_grad,
    normed, query, key, value, context_t, log_total, middle, normed_moe, gating,
    shares, quad, out_grad_all, bias, part, context, *refs,
):
    pair_refs = refs[:3]
    send, recv, here = refs[3:]
    at = Place()
    greet(
        [
            at.sibling(), at.partner(), at.opposite(), at.ring(1), at.ring(3),
            at.along("x", 1), at.along("x", 3), at.along("z", 1), at.along("z", 3),
        ]
    )
    own_rows = pl.ds(at.yh * 32, 32)
    swaps, kept = [], []
    for number, (first, count) in enumerate(((0, QUAD), (QUAD, 3 * QUAD))):
        for i, share in enumerate((gate, up, down)):
            dst = shares.at[i, pl.ds(first, count), own_rows]
            theirs = share.at[pl.ds((1 - at.yh) * 16 + first, count)]
            index = 3 * number + i
            swaps.append(push(theirs, dst, send, recv, index, at.opposite()))
            own = share.at[pl.ds(at.yh * 16 + first, count)]
            kept.append(keep(own, dst, here.at[index]))
    ring = RingGather(at, out_grad, out_grad_all, send, recv, here.at[6], 6)
    ring.begin()
    experts = QuadGather(at, shares.at[:, pl.ds(0, QUAD)], quad, send, recv, here.at[7], 15)
    scatter = PairScatter(at, part, pair_refs, send, recv, 15 + QuadGather.COPIES)

    gains = gain_rows(weights)
    seg_row = segment_row(segments)
    seg_column = column_of(seg_row)
    for block in range(SEQ // BLOCK):
        rows = slice(block * BLOCK, (block + 1) * BLOCK)
        values = hidden[rows, :].astype(F32)
        scale = lax.rsqrt(jnp.mean(values * values, axis=-1, keepdims=True) + EPS)
        normed[rows, :] = (values * scale * gains[0:1, :]).astype(BF)
    for half in range(2):
        columns = slice(half * 128, half * 128 + 128)
        pre = mm(normed[...], weights[:, columns])
        query[:, columns] = (rotated(pre, cosine[...], sine[...]) * 0.125).astype(BF)
    key_pre = mm(normed[...], weights[:, 256:384])
    key[...] = rotated(key_pre, cosine[...], sine[...]).astype(BF)
    value_pre = mm(normed[...], weights[:, 384:512])
    value[...] = value_pre.astype(BF)
    value_t = value_pre.T.astype(BF)
    for swap, own in zip(swaps[:3], kept[:3]):
        swap.wait_recv()
        own.wait()
    experts.begin()
    for block in range(SEQ // BLOCK):
        first, end = block * BLOCK, (block + 1) * BLOCK
        bias[:end, :] = bias_block(seg_column[:end, :], seg_row[:, first:end], first, end)
        for head in range(HEADS):
            kv = slice((head // 2) * HD, (head // 2) * HD + HD)
            own = slice(head * HD, head * HD + HD)
            scores = mm_last(key[:end, kv], query[first:end, own]) + bias[:end, :]
            top = jnp.max(scores, axis=0, keepdims=True)
            powers = jnp.exp(scores - top)
            total = jnp.sum(powers, axis=0, keepdims=True)
            share = (powers * (1.0 / total)).astype(BF)
            context_t[own, first:end] = mm(value_t[kv, :end], share).astype(BF)
            log_total[head : head + 1, first:end] = top + jnp.log(total)
        if block == 1:
            ring.forward_before()
            ring.forward_behind()
        if block == 2:
            experts.forward(0)
    experts.turn()
    context[...] = context_t[...].T

    def project(slot):
        rows = pl.ds(pl.multiple_of(slot * LOCAL, LOCAL), LOCAL)
        part[slot] = mm_last(context[rows, :], weights[:, 512:768]).astype(BF)

    project(scatter.other + 1 - at.core)
    scatter.begin_far()
    project(scatter.other + at.core)
    project(scatter.own + 1 - at.core)
    scatter.begin_own()
    project(scatter.own + at.core)
    scatter.forward()
    ring.forward_across()
    experts.forward(1)
    scatter.finish(middle)
    values = middle[...] + own_hidden[...].astype(F32)
    middle[...] = values
    scale = lax.rsqrt(jnp.mean(values * values, axis=-1, keepdims=True) + EPS)
    normed_moe[...] = (values * scale * gains[1:2, :]).astype(BF)
    chosen = named[...] > 0.0
    logits = jnp.where(chosen, mm(normed_moe[...], weights[:, 768:896]), MASKED)
    powers = jnp.where(chosen, jnp.exp(logits - jnp.max(logits, axis=-1, keepdims=True)), 0.0)
    gating[...] = powers / jnp.sum(powers, axis=-1, keepdims=True)
    for swap, own in zip(swaps[3:], kept[3:]):
        swap.wait_recv()
        own.wait()
    for swap in swaps:
        swap.wait_send()
    for i in (0, 4, 6, 7, 8):
        ring.copy(i).wait_recv()
    ring.sent()
    ring.kept().wait()
    experts.finish()


def front(hidden, weights, tables, segments, own_hidden, named, shares, out_grad, ident):
    vmem = pl.BlockSpec(memory_space=pltpu.VMEM)
    hbm = pl.BlockSpec(memory_space=pl.ANY)
    sems = 15 + QuadGather.COPIES + 1 + 2 * PIECES
    return pl.pallas_call(
        front_kernel,
        in_specs=[vmem] * 7 + [hbm] * 4,
        out_specs=[vmem] * 9 + [hbm] * 3,
        out_shape=[
            jax.ShapeDtypeStruct((SEQ, D), BF),
            jax.ShapeDtypeStruct((SEQ, HEADS * HD), BF),
            jax.ShapeDtypeStruct((SEQ, 128), BF),
            jax.ShapeDtypeStruct((SEQ, 128), BF),
            jax.ShapeDtypeStruct((HEADS * HD, SEQ), BF),
            jax.ShapeDtypeStruct((8, SEQ), F32),
            jax.ShapeDtypeStruct((LOCAL, D), F32),
            jax.ShapeDtypeStruct((LOCAL, D), BF),
            jax.ShapeDtypeStruct((LOCAL, 128), F32),
            jax.ShapeDtypeStruct((3, 16, 64, FF), BF),
            QUAD_SHAPE,
            jax.ShapeDtypeStruct((8, LOCAL, D), BF),
        ],
        scratch_shapes=[
            pltpu.VMEM((SEQ, BLOCK), F32),
            pltpu.VMEM((4, LOCAL, D), BF),
            pltpu.VMEM((SEQ, HEADS * HD), BF),
            *pair_scratch(LOCAL, D),
            pltpu.SemaphoreType.DMA((sems,)),
            pltpu.SemaphoreType.DMA((sems,)),
            pltpu.SemaphoreType.DMA((8,)),
        ],
        compiler_params=pltpu.CompilerParams(
            collective_id=ident, has_side_effects=True, vmem_limit_bytes=56 * MIB
        ),
        name="front",
    )(hidden, weights, *tables, segments, own_hidden, named, *shares, out_grad)


def back_kernel(
    dx, dgate, gating, middle, normed_moe, out_grad, y_part,
    normed, weights, cosine, sine, segments, query, key, value, context_t, log_total,
    dmiddle, dn1, grads, block_out,
    bias, dcontext, dquery_t, dkey, dvalue, dall, dall_t, dattn_own, dattn_all, y_sum, *refs,
):
    ring_refs = refs[:8]
    send, recv, here = refs[8:]
    at = Place()
    greet([at.sibling(), at.partner(), at.ring(1), at.ring(3)])
    gain = gain_rows(weights)[1:2, :]
    chosen = gating[...]
    dchosen = chosen * (dgate[...] - jnp.sum(chosen * dgate[...], axis=-1, keepdims=True))
    dlogits = dchosen.astype(BF)
    dnormed = dx[...] + mm_last(dlogits, weights[:, 768:896])
    values = middle[...]
    scale = lax.rsqrt(jnp.mean(values * values, axis=-1, keepdims=True) + EPS)
    unit = values * scale
    weighted = dnormed * gain
    inner = jnp.mean(weighted * unit, axis=-1, keepdims=True)
    total = out_grad[...].astype(F32) + scale * (weighted - unit * inner)
    dmiddle[...] = total
    dattn_own[...] = total.astype(BF)
    gather = PairGather(at, dattn_own, dattn_all, send, recv, here, 8, PIECES)
    scatter = RingScatter(at, y_part, ring_refs, send, recv)
    for k in (2, 1, 3, 0):
        scatter.copy(k).start()
    router_part = mm(normed_moe[...].T, dlogits)
    gain_part = column_of(jnp.sum(dnormed * unit, axis=0, keepdims=True))
    lane = lax.broadcasted_iota(jnp.int32, (D, 128), 1)
    grads[:, 768:] = jnp.where(lane == 32, gain_part, router_part).astype(BF)
    seg_row = segment_row(segments)
    seg_column = column_of(seg_row)
    gather.forward()
    scatter.far()
    gather.finish()
    dattn = dattn_all[...].reshape(SEQ, D)
    dcontext[...] = mm(dattn, weights[:, 512:768]).astype(BF)
    output_grad_t = mm(context_t[...], dattn)
    grads[:, 512:768] = output_grad_t.T.astype(BF)
    key_t = key[...].astype(F32).T.astype(BF)
    dkey[...] = jnp.zeros_like(dkey)
    dvalue[...] = jnp.zeros_like(dvalue)
    for block in range(SEQ // BLOCK):
        first, end = block * BLOCK, (block + 1) * BLOCK
        bias[:end, :] = bias_block(seg_column[:end, :], seg_row[:, first:end], first, end)
        for head in range(HEADS):
            kv = slice((head // 2) * HD, (head // 2) * HD + HD)
            own = slice(head * HD, head * HD + HD)
            query_block = query[first:end, own]
            dcontext_block = dcontext[first:end, own]
            scores = mm_last(key[:end, kv], query_block) + bias[:end, :]
            share = jnp.exp(scores - log_total[head : head + 1, first:end])
            dshare = mm_last(value[:end, kv], dcontext_block)
            centre = jnp.sum(share * dshare, axis=0, keepdims=True)
            dscore = (share * (dshare - centre)).astype(BF)
            dquery_t[own, first:end] = mm(key_t[kv, :end], dscore) * 0.125
            dkey[:end, kv] += mm(dscore, query_block)
            dvalue[:end, kv] += mm(share.astype(BF), dcontext_block)
        if block == 0:
            scatter.up_side()
            scatter.down_side()
    turn = -sine[...]
    for half in range(2):
        rows = slice(half * 128, half * 128 + 128)
        piece = rotated(dquery_t[rows, :].T, cosine[...], turn)
        dall[:, rows] = piece.astype(BF)
        dall_t[rows, :] = piece.T.astype(BF)
    piece = rotated(dkey[...], cosine[...], turn)
    dall[:, 256:384] = piece.astype(BF)
    dall_t[256:384, :] = piece.T.astype(BF)
    dall[:, 384:512] = dvalue[...].astype(BF)
    dall_t[384:512, :] = dvalue[...].T.astype(BF)
    grads[:, 0:512] = mm(dall_t[...], normed[...]).T.astype(BF)
    for block in range(SEQ // BLOCK):
        rows = slice(block * BLOCK, (block + 1) * BLOCK)
        dn1[rows, :] = mm_last(dall[rows, :], weights[:, 0:512]).astype(BF)
    scatter.finish(y_sum)
    block_out[...] = (y_sum[...] + middle[...]).astype(BF)


def back(
    dx, dgate, gating, middle, normed_moe, out_grad, y_part,
    normed, weights, tables, segments, kept, ident,
):
    vmem = pl.BlockSpec(memory_space=pltpu.VMEM)
    sems = 8 + 1 + 2 * PIECES
    return pl.pallas_call(
        back_kernel,
        in_specs=[vmem] * 17,
        out_specs=[vmem] * 4,
        out_shape=[
            jax.ShapeDtypeStruct((LOCAL, D), F32),
            jax.ShapeDtypeStruct((SEQ, D), BF),
            jax.ShapeDtypeStruct((D, SMALL), BF),
            jax.ShapeDtypeStruct((LOCAL, D), BF),
        ],
        scratch_shapes=[
            pltpu.VMEM((SEQ, BLOCK), F32),
            pltpu.VMEM((SEQ, HEADS * HD), BF),
            pltpu.VMEM((HEADS * HD, SEQ), F32),
            pltpu.VMEM((SEQ, 128), F32),
            pltpu.VMEM((SEQ, 128), F32),
            pltpu.VMEM((SEQ, 512), BF),
            pltpu.VMEM((512, SEQ), BF),
            pltpu.VMEM((LOCAL, D), BF),
            pltpu.VMEM((4, LOCAL, D), BF),
            pltpu.VMEM((LOCAL, D), F32),
            *ring_scratch(LOCAL, D),
            pltpu.SemaphoreType.DMA((sems,)),
            pltpu.SemaphoreType.DMA((sems,)),
            pltpu.SemaphoreType.DMA,
        ],
        compiler_params=pltpu.CompilerParams(
            collective_id=ident, has_side_effects=True, vmem_limit_bytes=58 * MIB
        ),
        name="back",
    )(
        dx, dgate, gating, middle, normed_moe, out_grad, y_part,
        normed, weights, *tables, segments, *kept,
    )


def experts_kernel(
    x_in, gate_in, d_in, quad_0, shares,
    y_out, dx_out, dgate_out, grads, quad_1, quad_2, quad_3,
    x, d, xt, dt, y, dx, gating, dgate, dgate_part, hidden, w, *refs,
):
    dx_scratch, dgate_scratch = refs[:5], refs[5:10]
    send, recv, here, load, store, fetch = refs[10:16]
    at = Place()
    step = pl.program_id(0)
    opening, closing = step == 0, step == STEPS - 1
    rows_at_once = 2 * LOCAL
    lane = lax.broadcasted_iota(jnp.int32, (LOCAL, 128), 1)
    own_first = at.yh * 16 + step * QUAD
    x_gather = RingGather(at, x_in, x, send, recv, here.at[0], 0)
    gate_gather = RingGather(at, gate_in, gating, send, recv, here.at[1], 9)
    gathers = (x_gather, gate_gather)
    scatters = (
        RingScatter(at, d, dx_scratch, send, recv, 18),
        RingScatter(at, dgate_part, dgate_scratch, send, recv, 26),
    )

    quads = [
        QuadGather(
            at, shares.at[:, pl.ds((i + 1) * QUAD, QUAD)], quad, *refs[16:18],
            refs[18].at[i], QuadGather.COPIES * i,
        )
        for i, quad in enumerate((quad_1, quad_2, quad_3))
    ]

    def ride(condition, what):
        for i, quad in enumerate(quads):

            @pl.when(condition & (step == i))
            def _():
                what(quad)

    def fetches(quad):
        return [
            pltpu.make_async_copy(
                quad.at[g, i], w.at[:, :, :, pl.ds((g * QUAD + i) * FF, FF)],
                fetch.at[g * QUAD + i],
            )
            for g in range(3)
            for i in range(QUAD)
        ]

    def d_load(chip):
        two = pl.ds(chip * 2, 2)
        return pltpu.make_async_copy(d_in.at[two], d.at[two], load.at[chip])

    def y_store(chip):
        two = pl.ds(chip * 2, 2)
        return pltpu.make_async_copy(x.at[two], y_out.at[two], store.at[chip])

    @pl.when(opening)
    def _():
        greet(
            [
                at.sibling(), at.ring(1), at.ring(3),
                at.along("x", 1), at.along("x", 3), at.along("z", 1), at.along("z", 3),
            ]
        )
        for gather in gathers:
            gather.begin()
        for copy in fetches(quad_0):
            copy.start()
        for chip in range(4):
            d_load(chip).start()

    for copy in fetches(quad_0):
        copy.wait()

    ride(step < STEPS, lambda quad: quad.begin())

    def arrive(turn):
        @pl.when(turn == 0)
        def _():
            for gather in gathers:
                gather.kept().wait()
                gather.copy(0).wait_recv()

        @pl.when(turn == 1)
        def _():
            for gather in gathers:
                gather.forward_before()
                gather.forward_behind()
            for gather in gathers:
                gather.copy(4).wait_recv()

        @pl.when(turn == 2)
        def _():
            for gather in gathers:
                gather.forward_across()
            for gather in gathers:
                gather.copy(6).wait_recv()

        @pl.when(turn == 3)
        def _():
            for gather in gathers:
                gather.copy(7).wait_recv()
                gather.copy(8).wait_recv()

    def leave(turn):
        @pl.when(turn == 0)
        def _():
            for scatter in scatters:
                scatter.copy(2).start()

        @pl.when(turn == 1)
        def _():
            for scatter in scatters:
                scatter.copy(1).start()
                scatter.far()

        @pl.when(turn == 2)
        def _():
            for scatter in scatters:
                scatter.copy(3).start()
                scatter.up_side()

        @pl.when(turn == 3)
        def _():
            for scatter in scatters:
                scatter.copy(0).start()
                scatter.down_side()

    def tokens_block(turn, carry):
        inward = jnp.where(turn == 0, 0, jnp.where(turn == 1, 3, turn - 1))
        outward = jnp.where(turn == 0, 2, jnp.where(turn == 3, 0, turn * 2 - 1))
        chip = at.chip(jnp.where(closing, outward, inward))
        two = pl.ds(chip * 2, 2)
        rows = pl.ds(pl.multiple_of(chip * rows_at_once, rows_at_once), rows_at_once)

        @pl.when(opening)
        def _():
            arrive(turn)
            d_load(chip).wait()
            xt[:, rows] = x[two].reshape(rows_at_once, D).T
            dt[:, rows] = d[two].reshape(rows_at_once, D).T
            y[rows, :] = jnp.zeros((rows_at_once, D), F32)
            dx[rows, :] = jnp.zeros((rows_at_once, D), F32)
            dgate[rows, :] = jnp.zeros((rows_at_once, 128), F32)

        ride(turn == 1, lambda quad: quad.forward(0))
        ride(turn == 2, lambda quad: quad.turn())
        ride(turn == 3, lambda quad: quad.forward(1))
        gate_up = w[:, :, :, 0 : 2 * F].reshape(D, 2 * F)
        down = w[:, :, :, 2 * F :].reshape(D, F)
        for core in range(2):
            slot = chip * 2 + core
            part = pl.ds(pl.multiple_of(slot * LOCAL, LOCAL), LOCAL)
            both = mm(x[slot], gate_up)
            gate, up = both[:, :F], both[:, F:]
            dact = mm(d[slot], down)
            turned = pltpu.roll(gating[slot], lax.rem(128 - own_first, 128), 1)
            factor = jnp.concatenate(
                [jnp.broadcast_to(turned[:, i : i + 1], (LOCAL, FF)) for i in range(QUAD)],
                axis=1,
            )
            q = 1.0 / (1.0 + jnp.exp(-gate))
            silu = gate * q
            act = silu * up
            product = act * dact
            sums = dgate[part, :]
            for i in range(QUAD):
                own = jnp.sum(product[:, i * FF : (i + 1) * FF], axis=1, keepdims=True)
                sums = jnp.where(lane == own_first + i, own, sums)
            dgate[part, :] = sums
            dact = dact * factor
            hidden[part, 0:F] = (dact * up * (q + silu * (1.0 - q))).astype(BF)
            hidden[part, F : 2 * F] = (dact * silu).astype(BF)
            hidden[part, 2 * F :] = (act * factor).astype(BF)
        y[rows, :] += mm_last(hidden[rows, 2 * F :], down)
        dx[rows, :] += mm_last(hidden[rows, 0 : 2 * F], gate_up)

        @pl.when(closing)
        def _():
            x[two] = y[rows, :].astype(BF).reshape(2, LOCAL, D)
            d[two] = dx[rows, :].astype(BF).reshape(2, LOCAL, D)
            dgate_part[two] = dgate[rows, :].astype(BF).reshape(2, LOCAL, 128)
            y_store(chip).start()
            leave(turn)

        return carry

    lax.fori_loop(0, 4, tokens_block, 0)

    ride(step < STEPS, lambda quad: quad.finish())
    for number, quad in enumerate((quad_1, quad_2, quad_3)):

        @pl.when(step == number)
        def _():
            for copy in fetches(quad):
                copy.start()

    @pl.when(opening)
    def _():
        for gather in gathers:
            gather.sent()

    def grads_block(block, carry):
        rows = pl.ds(pl.multiple_of(block * 512, 512), 512)
        both = mm(xt[rows, :], hidden[:, 0 : 2 * F]).astype(BF)
        for g in range(2):
            for i in range(QUAD):
                first = (g * QUAD + i) * FF
                grads[g, i, rows, :] = both[:, first : first + FF]
        down = mm(dt[rows, :], hidden[:, 2 * F :]).astype(BF)
        for i in range(QUAD):
            grads[2, i, rows, :] = down[:, i * FF : (i + 1) * FF]
        return carry

    lax.fori_loop(0, D // 512, grads_block, 0)

    @pl.when(closing)
    def _():
        scatters[0].finish(dx_out)
        scatters[1].finish(dgate_out)
        for chip in range(4):
            y_store(chip).wait()


def experts(x, gating, d, quad, shares, ident):
    hbm = pl.BlockSpec(memory_space=pl.ANY)

    def whole(rows, columns):
        return pl.BlockSpec((rows, columns), lambda step: (0, 0), pipeline_mode=pl.Buffered(1))

    return pl.pallas_call(
        experts_kernel,
        grid=(STEPS,),
        in_specs=[hbm] * 5,
        out_specs=[
            hbm,
            whole(LOCAL, D),
            whole(LOCAL, 128),
            pl.BlockSpec(
                (3, QUAD, D, FF), lambda step: (0, step, 0, 0), pipeline_mode=pl.Buffered(1)
            ),
            *[hbm] * 3,
        ],
        out_shape=[
            jax.ShapeDtypeStruct((8, LOCAL, D), BF),
            jax.ShapeDtypeStruct((LOCAL, D), F32),
            jax.ShapeDtypeStruct((LOCAL, 128), F32),
            jax.ShapeDtypeStruct((3, STEPS * QUAD, D, FF), BF),
            *[QUAD_SHAPE] * 3,
        ],
        scratch_shapes=[
            pltpu.VMEM((8, LOCAL, D), BF),
            pltpu.VMEM((8, LOCAL, D), BF),
            pltpu.VMEM((D, TOKENS), BF),
            pltpu.VMEM((D, TOKENS), BF),
            pltpu.VMEM((TOKENS, D), F32),
            pltpu.VMEM((TOKENS, D), F32),
            pltpu.VMEM((8, LOCAL, 128), F32),
            pltpu.VMEM((TOKENS, 128), F32),
            pltpu.VMEM((8, LOCAL, 128), BF),
            pltpu.VMEM((TOKENS, 3 * F), BF),
            pltpu.VMEM((4, 4, 64, 3 * F), BF),
            *ring_scratch(LOCAL, D, False),
            *ring_scratch(LOCAL, 128, False),
            pltpu.SemaphoreType.DMA((34,)),
            pltpu.SemaphoreType.DMA((34,)),
            pltpu.SemaphoreType.DMA((2,)),
            pltpu.SemaphoreType.DMA((4,)),
            pltpu.SemaphoreType.DMA((4,)),
            pltpu.SemaphoreType.DMA((3 * QUAD,)),
            pltpu.SemaphoreType.DMA((3 * QuadGather.COPIES,)),
            pltpu.SemaphoreType.DMA((3 * QuadGather.COPIES,)),
            pltpu.SemaphoreType.DMA((3,)),
        ],
        compiler_params=pltpu.CompilerParams(
            collective_id=ident, has_side_effects=True, vmem_limit_bytes=63 * MIB
        ),
        name="experts",
    )(x, gating, d, quad, shares)[:4]


def norm_scale(values):
    return lax.rsqrt(jnp.mean(values * values, axis=-1, keepdims=True) + EPS)


def norm_grad(values, gain, dnormed):
    scale = norm_scale(values)
    unit = values * scale
    weighted = dnormed * gain
    dvalues = scale * (weighted - unit * jnp.mean(weighted * unit, axis=-1, keepdims=True))
    return dvalues


def on_device(
    hidden_in, out_grad, attn_gain, query_weight, key_weight, value_weight, output_weight,
    moe_gain, router_weight, expert_gate, expert_up, expert_down, expert_ids, segment_ids,
):
    small = jnp.concatenate(
        [
            query_weight, key_weight, value_weight, output_weight,
            router_weight, attn_gain[:, None], moe_gain[:, None], jnp.zeros((32, 94), BF),
        ],
        axis=1,
    )
    segment = jnp.pad(segment_ids.reshape(2, 128), ((0, 6), (0, 0)))
    hidden_all, segments, small = startup(hidden_in, segment, small, 0)
    tables = tuple(jnp.asarray(t) for t in rotary_tables())
    named = jnp.any(
        expert_ids[:, :, None] == jnp.arange(128, dtype=jnp.int32)[None, None, :], axis=1
    ).astype(F32)

    own_shares = (expert_gate, expert_up, expert_down)
    normed, *kept, middle, normed_moe, gating, shares, quad, d = front(
        hidden_all, small, tables, segments, hidden_in, named, own_shares, out_grad, 1
    )
    y, dx, dgate, expert_grads = experts(normed_moe, gating, d, quad, shares, 3)
    expert_grads = lax.psum_scatter(expert_grads, PLANE, scatter_dimension=2, tiled=True)
    dmiddle, dn1, grads, block_out = back(
        dx, dgate, gating, middle, normed_moe, out_grad, y,
        normed, small, tables, segments, kept, 5,
    )
    weights = jnp.concatenate([query_weight, key_weight, value_weight], axis=1)
    dn1, attention_grads, rest = final(dn1, grads, weights, 6)
    hidden = hidden_in.astype(F32)
    dhidden = norm_grad(hidden, small[:, 800].astype(F32), dn1)
    hidden_grad = dmiddle + dhidden
    expert_grads = [share.astype(F32) for share in last_exchange(expert_grads, 7)]
    return (
        block_out,
        hidden_grad,
        rest[:, 33] / attn_gain.astype(F32),
        attention_grads[:, 0:256],
        attention_grads[:, 256:384],
        attention_grads[:, 384:512],
        attention_grads[:, 512:768],
        rest[:, 32],
        rest[:, :32],
        *expert_grads,
    )


def solution(mesh):
    fine = Mesh(np.asarray(mesh.devices).reshape(4, 4, 2, 2, 2), ALL)
    return jax.shard_map(
        on_device,
        mesh=fine,
        in_specs=(
            P(ALL, None),
            P(ALL, None),
            P(DP),
            P(DP, TENSOR),
            P(DP, TENSOR),
            P(DP, TENSOR),
            P(DP, TENSOR),
            P(DP),
            P(DP, None),
            P(None, DP, TENSOR),
            P(None, DP, TENSOR),
            P(None, DP, TENSOR),
            P(ALL, None),
            P(ALL),
        ),
        out_specs=(
            P(ALL, None),
            P(ALL, None),
            P(DP),
            P(DP, TENSOR),
            P(DP, TENSOR),
            P(DP, TENSOR),
            P(DP, TENSOR),
            P(DP),
            P(DP, None),
            P(None, DP, TENSOR),
            P(None, DP, TENSOR),
            P(None, DP, TENSOR),
        ),
        check_vma=False,
    )
```

```python
import jax
import jax.numpy as jnp
import numpy as np
from jax import lax
from jax.experimental import pallas as pl
from jax.experimental.pallas import tpu as pltpu
from jax.sharding import Mesh
from jax.sharding import PartitionSpec as P

D = 1024
HD = 64
E = 32
SEQ = 1024
LOCAL = 256
HEADS = 4
QUAD = 4
FF = 128
F = QUAD * FF
EPS = 1e-06
MASKED = -1e30
BLOCK = 256
TOKENS = 2048
STEPS = 4

DP = ("x", "z", "yh")
TENSOR = ("yl", "core")
RING = ("yh", "yl", "core")
PLANE = ("x", "z")
ALL = ("x", "z", "yh", "yl", "core")

F32 = jnp.float32
BF = jnp.bfloat16
LAST = (((1,), (1,)), ((), ()))
MIB = 1024 * 1024
MESH = pl.DeviceIdType.MESH
SMALL = 896


def mm(a, b):
    return jnp.dot(a, b, preferred_element_type=F32)


def mm_last(a, b):
    return lax.dot_general(a, b, LAST, preferred_element_type=F32)


class Place:
    def __init__(self):
        self.x = lax.axis_index("x")
        self.z = lax.axis_index("z")
        self.yh = lax.axis_index("yh")
        self.yl = lax.axis_index("yl")
        self.core = lax.axis_index("core")
        self.y = self.yh * 2 + self.yl

    def chip(self, k):
        return lax.rem(self.y + k, 4)

    def ring(self, k):
        chip = self.chip(k)
        return {"yh": chip // 2, "yl": lax.rem(chip, 2)}

    def along(self, axis, k):
        return {axis: lax.rem(getattr(self, axis) + k, 4)}

    def sibling(self):
        return {"core": 1 - self.core}

    def partner(self):
        return {"yl": 1 - self.yl}

    def diagonal(self):
        return {"yl": 1 - self.yl, "core": 1 - self.core}

    def opposite(self):
        return {"yh": 1 - self.yh}


def greet(devices):
    barrier = pltpu.get_barrier_semaphore()
    for device in devices:
        pl.semaphore_signal(barrier, inc=1, device_id=device, device_id_type=MESH)
    pl.semaphore_wait(barrier, len(devices))


def remote(src, dst, send, recv, i, device):
    return pltpu.make_async_remote_copy(
        src_ref=src, dst_ref=dst, send_sem=send.at[i], recv_sem=recv.at[i],
        device_id=device, device_id_type=MESH,
    )


def push(src, dst, send, recv, i, device):
    copy = remote(src, dst, send, recv, i, device)
    copy.start()
    return copy


def keep(src, dst, sem):
    copy = pltpu.make_async_copy(src, dst, sem)
    copy.start()
    return copy


class RingGather:
    def __init__(self, at, own, out, send, recv, here, base=0):
        self.at, self.own, self.out, self.base = at, own, out, base
        self.send, self.recv, self.here = send, recv, here
        half = own.shape[0] // 2
        lo, hi = pl.ds(0, half), pl.ds(half, half)
        me, before, behind, across = (out.at[self.slot(k)] for k in (0, 3, 1, 2))
        near, up, down = at.sibling(), at.ring(1), at.ring(3)
        self.plan = [
            (own, me, near),
            (own, me, up),
            (own, me, down),
            (before.at[lo], before.at[lo], up),
            (before, before, near),
            (behind.at[hi], behind.at[hi], down),
            (behind, behind, near),
            (across.at[lo], across.at[lo], near),
            (across.at[hi], across.at[hi], near),
        ]

    def slot(self, k):
        return self.at.chip(k) * 2 + self.at.core

    def copy(self, i):
        src, dst, device = self.plan[i]
        return remote(src, dst, self.send, self.recv, self.base + i, device)

    def kept(self):
        return pltpu.make_async_copy(self.own, self.out.at[self.slot(0)], self.here)

    def begin(self):
        self.kept().start()
        for i in (1, 2, 0):
            self.copy(i).start()

    def forward_before(self):
        self.copy(1).wait_recv()
        self.copy(3).start()
        self.copy(4).start()

    def forward_behind(self):
        self.copy(2).wait_recv()
        self.copy(5).start()
        self.copy(6).start()

    def forward_across(self):
        self.copy(3).wait_recv()
        self.copy(7).start()
        self.copy(5).wait_recv()
        self.copy(8).start()

    def sent(self):
        for i in range(9):
            self.copy(i).wait_send()


class PairGather:
    def __init__(self, at, own, out, send, recv, here, base, pieces):
        self.at, self.out, self.send, self.recv, self.base = at, out, send, recv, base
        size = own.shape[0] // pieces
        self.parts = [pl.ds(i * size, size) for i in range(pieces)]
        me = at.yl * 2 + at.core
        self.other = (1 - at.yl) * 2 + at.core
        self.kept = keep(own, out.at[me], here)
        self.far = [
            push(own.at[part], out.at[me, part], send, recv, base + 1 + i, at.partner())
            for i, part in enumerate(self.parts)
        ]
        self.near = [push(own, out.at[me], send, recv, base, at.sibling())]

    def forward(self):
        for i, part in enumerate(self.parts):
            self.far[i].wait_recv()
            view = self.out.at[self.other, part]
            index = self.base + 1 + len(self.parts) + i
            self.near.append(push(view, view, self.send, self.recv, index, self.at.sibling()))

    def finish(self):
        for copy in self.near:
            copy.wait_recv()
        for copy in (*self.far, *self.near):
            copy.wait_send()
        self.kept.wait()


PIECES = 4


class AxisGather:
    def __init__(self, at, axis, view, send, recv, base):
        self.up, self.down = at.along(axis, 1), at.along(axis, 3)
        self.view, self.send, self.recv, self.base = view, send, recv, base

    def go(self, i, view, device):
        return push(view, view, self.send, self.recv, self.base + i, device)

    def begin(self):
        self.first = [
            self.go(0, self.view(0, "all"), self.up), self.go(1, self.view(0, "all"), self.down),
        ]

    def forward(self):
        self.first[0].wait_recv()
        self.far = [self.go(2, self.view(3, "low"), self.up)]
        self.first[1].wait_recv()
        self.far.append(self.go(3, self.view(1, "high"), self.down))

    def finish(self):
        for copy in self.far:
            copy.wait_recv()
        for copy in (*self.first, *self.far):
            copy.wait_send()


def halves_of(ref, first, size):
    spans = {"all": (0, size), "low": (0, size // 2), "high": (size // 2, size // 2)}
    return lambda part: ref.at[pl.ds(first + spans[part][0], spans[part][1])]


class LineGather:
    COPIES = 8

    def __init__(self, at, own, over_z, over_x, send, recv, here, base=0):
        self.send, self.recv, self.here, self.base = send, recv, here, base
        low, high, whole = pl.ds(0, 32), pl.ds(32, 32), pl.ds(0, 64)
        first, second = own.at[:, :, pl.ds(0, 2)], own.at[:, :, pl.ds(2, 2)]

        def z_line(k, rows):
            return over_z.at[:, :, :, lax.rem(at.z + k, 4), rows]

        def x_line(k, rows):
            return over_x.at[:, :, :, lax.rem(at.x + k, 4), rows]

        self.own = [(first, z_line(0, whole)), (second, x_line(0, whole))]
        self.plan = []
        for (mine, slot), axis in zip(self.own, ("z", "x")):
            self.plan.append((mine, slot, at.along(axis, 1)))
            self.plan.append((mine, slot, at.along(axis, 3)))
        for line, axis in ((z_line, "z"), (x_line, "x")):
            self.plan.append((line(3, low), line(3, low), at.along(axis, 1)))
            self.plan.append((line(1, high), line(1, high), at.along(axis, 3)))

    def copy(self, i):
        src, dst, device = self.plan[i]
        return remote(src, dst, self.send, self.recv, self.base + i, device)

    def begin(self):
        for i in range(4):
            self.copy(i).start()
        self.kept = [keep(src, dst, self.here.at[i]) for i, (src, dst) in enumerate(self.own)]

    def forward(self):
        for i in range(4):
            self.copy(i).wait_recv()
            self.copy(4 + i).start()

    def finish(self):
        for i in range(4, 8):
            self.copy(i).wait_recv()
        for i in range(8):
            self.copy(i).wait_send()
        for copy in self.kept:
            copy.wait()


class QuadGather:
    COPIES = 8

    def __init__(self, at, number, over_z, over_x, out, send, recv, here, base=0):
        self.send, self.recv, self.here, self.base = send, recv, here, base
        low, high, whole = pl.ds(0, 32), pl.ds(32, 32), pl.ds(0, 64)
        first, second = pl.ds(0, 2), pl.ds(2, 2)

        def planes(k, rows):
            return out.at[:, first, lax.rem(at.x + k, 4), :, rows]

        def lines(k, rows):
            return out.at[:, second, :, lax.rem(at.z + k, 4), rows]

        self.own = [
            (over_z.at[:, number], planes(0, whole)), (over_x.at[:, number], lines(0, whole)),
        ]
        self.plan = []
        for (mine, slot), axis in zip(self.own, ("x", "z")):
            self.plan.append((mine, slot, at.along(axis, 1)))
            self.plan.append((mine, slot, at.along(axis, 3)))
        for view, axis in ((planes, "x"), (lines, "z")):
            self.plan.append((view(3, low), view(3, low), at.along(axis, 1)))
            self.plan.append((view(1, high), view(1, high), at.along(axis, 3)))

    def copy(self, i):
        src, dst, device = self.plan[i]
        return remote(src, dst, self.send, self.recv, self.base + i, device)

    def kept(self, i):
        src, dst = self.own[i]
        return pltpu.make_async_copy(src, dst, self.here.at[i])

    def begin(self):
        for i in range(4):
            self.copy(i).start()
        for i in range(2):
            self.kept(i).start()

    def forward(self):
        for i in range(4):
            self.copy(i).wait_recv()
            self.copy(4 + i).start()

    def finish(self):
        for i in range(4, 8):
            self.copy(i).wait_recv()
        for i in range(8):
            self.copy(i).wait_send()
        for i in range(2):
            self.kept(i).wait()


LINE_SHAPE = jax.ShapeDtypeStruct((3, STEPS, 2, 4, 64, FF), BF)
QUAD_SHAPE = jax.ShapeDtypeStruct((3, QUAD, 4, 4, 64, FF), BF)


def startup_kernel(
    hidden, segment, small, gate, up, down,
    hidden_all, segment_all, small_all, shares, over_z_line, over_x_line, send, recv, here,
):
    at = Place()
    greet(
        [
            at.sibling(), at.partner(), at.diagonal(), at.opposite(),
            at.along("x", 1), at.along("x", 3), at.along("z", 1), at.along("z", 3),
        ]
    )
    rank = at.yl * 2 + at.core
    mine = small_all.at[(at.x * 4 + at.z) * 2 + at.yh]
    small_kept = keep(small, mine, here.at[0])
    copies = [push(small, mine, send, recv, 0, at.opposite())]
    own_rows = pl.ds(at.yh * 32, 32)
    swaps, swaps_kept = [], []
    base = 13 + 2 * PIECES
    for i, share in enumerate((gate, up, down)):
        dst = shares.at[i, :, :, own_rows]
        theirs = share.at[pl.ds((1 - at.yh) * STEPS, STEPS)]
        swaps.append(push(theirs, dst, send, recv, base + i, at.opposite()))
        own = share.at[pl.ds(at.yh * STEPS, STEPS)]
        swaps_kept.append(keep(own, dst, here.at[3 + i]))
    experts = LineGather(
        at, shares, over_z_line, over_x_line, send, recv, here.at[pl.ds(6, 2)], base + 3
    )
    copies.extend(
        push(segment, segment_all.at[rank], send, recv, 1 + i, device)
        for i, device in enumerate((at.sibling(), at.partner(), at.diagonal()))
    )
    pair = PairGather(at, hidden, hidden_all, send, recv, here.at[1], 12, PIECES)
    seg_here = keep(segment, segment_all.at[rank], here.at[2])
    over_z = AxisGather(
        at, "z",
        lambda k, part: halves_of(small_all, (at.x * 4 + lax.rem(at.z + k, 4)) * 2, 2)(part),
        send, recv, 4,
    )
    over_x = AxisGather(
        at, "x", lambda k, part: halves_of(small_all, lax.rem(at.x + k, 4) * 8, 8)(part),
        send, recv, 8,
    )
    small_kept.wait()
    copies[0].wait_recv()
    over_z.begin()
    over_z.forward()
    over_z.finish()
    over_x.begin()
    pair.forward()
    for swap, own in zip(swaps, swaps_kept):
        swap.wait_recv()
        own.wait()
    experts.begin()
    over_x.forward()
    experts.forward()
    pair.finish()
    seg_here.wait()
    for copy in copies[1:]:
        copy.wait_recv()
    over_x.finish()
    experts.finish()
    for copy in (*copies, *swaps):
        copy.wait_send()


def startup(hidden, segment, small, shares, ident):
    hbm = pl.BlockSpec(memory_space=pl.ANY)
    sems = 13 + 2 * PIECES + 3 + LineGather.COPIES
    shares = [share.reshape(2 * STEPS, QUAD, 32, FF) for share in shares]
    hidden_all, segment_all, small_all, _, over_z, over_x = pl.pallas_call(
        startup_kernel,
        in_specs=[hbm] * 6,
        out_specs=[hbm] * 6,
        out_shape=[
            jax.ShapeDtypeStruct((4, *hidden.shape), hidden.dtype),
            jax.ShapeDtypeStruct((4, *segment.shape), segment.dtype),
            jax.ShapeDtypeStruct((32, 32, SMALL), small.dtype),
            jax.ShapeDtypeStruct((3, STEPS, QUAD, 64, FF), BF),
            LINE_SHAPE,
            LINE_SHAPE,
        ],
        scratch_shapes=[
            pltpu.SemaphoreType.DMA((sems,)),
            pltpu.SemaphoreType.DMA((sems,)),
            pltpu.SemaphoreType.DMA((8,)),
        ],
        compiler_params=pltpu.CompilerParams(collective_id=ident, has_side_effects=True),
        name="startup",
    )(hidden, segment, small, *shares)
    hidden_all, small_all = hidden_all.reshape(SEQ, D), small_all.reshape(D, SMALL)
    return hidden_all, segment_all, small_all, over_z, over_x


class RingScatter:
    def __init__(self, at, part, scratch, send, recv, base=0):
        self.at, self.part, self.send, self.recv, self.base = at, part, send, recv, base
        near, half_a, half_b, self.full_up, self.full_down = scratch[:5]
        to_far, to_up, to_down = scratch[5:] or [
            part.at[at.chip(k) * 2 + at.core] for k in (2, 1, 3)
        ]
        self.near, self.half_a, self.half_b = near, half_a, half_b
        self.to_far, self.to_up, self.to_down = to_far, to_up, to_down
        self.half = half_a.shape[0]
        self.lo, self.hi = pl.ds(0, self.half), pl.ds(self.half, self.half)
        up, down = at.ring(1), at.ring(3)
        self.plan = {
            k: (part.at[at.chip(k) * 2 + 1 - at.core], near.at[k], at.sibling()) for k in range(4)
        }
        self.plan[4] = (to_far.at[self.lo], half_a, up)
        self.plan[5] = (to_far.at[self.hi], half_b, down)
        self.plan[6] = (to_up, self.full_up, up)
        self.plan[7] = (to_down, self.full_down, down)

    def copy(self, i):
        src, dst, device = self.plan[i]
        return remote(src, dst, self.send, self.recv, self.base + i, device)

    def chip_sum(self, k):
        self.copy(k).wait_recv()
        own = self.part[self.at.chip(k) * 2 + self.at.core]
        return own.astype(F32) + self.near[k].astype(F32)

    def far(self):
        self.to_far[...] = self.chip_sum(2).astype(BF)
        self.copy(4).start()
        self.copy(5).start()

    def up_side(self):
        total = self.chip_sum(1)
        self.copy(4).wait_recv()
        self.to_up[self.lo, :] = (total[: self.half] + self.half_a[...].astype(F32)).astype(BF)
        self.to_up[self.hi, :] = total[self.half :].astype(BF)
        self.copy(6).start()

    def down_side(self):
        total = self.chip_sum(3)
        self.copy(5).wait_recv()
        self.to_down[self.lo, :] = total[: self.half].astype(BF)
        self.to_down[self.hi, :] = (total[self.half :] + self.half_b[...].astype(F32)).astype(BF)
        self.copy(7).start()

    def finish(self, out):
        out[...] = self.chip_sum(0)
        self.copy(6).wait_recv()
        out[...] += self.full_up[...].astype(F32)
        self.copy(7).wait_recv()
        out[...] += self.full_down[...].astype(F32)
        for i in range(8):
            self.copy(i).wait_send()


def ring_scratch(rows, columns, own_sends=True):
    block, half = pltpu.VMEM((rows, columns), BF), pltpu.VMEM((rows // 2, columns), BF)
    scratch = [pltpu.VMEM((4, rows, columns), BF), half, half, block, block]
    return scratch + [block] * 3 if own_sends else scratch


class PairScatter:
    def __init__(self, at, part, scratch, send, recv, base=0):
        self.at, self.part, self.send, self.recv, self.base = at, part, send, recv, base
        self.near, self.far_rows, self.to_far = scratch
        size = self.to_far.shape[0] // PIECES
        self.parts = [pl.ds(i * size, size) for i in range(PIECES)]
        self.other, self.own = (1 - at.yl) * 2, at.yl * 2

    def go(self, i, src, dst, device):
        return push(src, dst, self.send, self.recv, self.base + i, device)

    def begin_far(self):
        slot = self.other + 1 - self.at.core
        self.first = [
            self.go(i, self.part.at[slot, rows], self.near.at[1, rows], self.at.sibling())
            for i, rows in enumerate(self.parts)
        ]

    def begin_own(self):
        slot = self.own + 1 - self.at.core
        self.second = self.go(PIECES, self.part.at[slot], self.near.at[0], self.at.sibling())

    def forward(self):
        self.sent = []
        for i, rows in enumerate(self.parts):
            self.first[i].wait_recv()
            own = self.part[self.other + self.at.core, rows, :].astype(F32)
            self.to_far[rows, :] = (own + self.near[1, rows, :].astype(F32)).astype(BF)
            far = self.far_rows.at[rows]
            self.sent.append(self.go(PIECES + 1 + i, self.to_far.at[rows], far, self.at.partner()))

    def finish(self, out):
        self.second.wait_recv()
        out[...] = self.part[self.own + self.at.core].astype(F32) + self.near[0].astype(F32)
        for i, rows in enumerate(self.parts):
            self.sent[i].wait_recv()
            out[rows, :] += self.far_rows[rows, :].astype(F32)
        for copy in (*self.first, self.second, *self.sent):
            copy.wait_send()


def pair_scratch(rows, columns):
    block = pltpu.VMEM((rows, columns), BF)
    return [pltpu.VMEM((2, rows, columns), BF), block, block]


class DirectScatter:
    def __init__(self, at, axis, blocks, landed, send, recv, base):
        self.blocks, self.landed = blocks, landed
        self.copies = [
            push(blocks(k), landed.at[k - 1], send, recv, base + k - 1, at.along(axis, k))
            for k in (2, 1, 3)
        ]

    def total(self):
        value = self.blocks(0)[...].astype(F32)
        for copy, k in zip(self.copies, (2, 1, 3)):
            copy.wait_recv()
            value = value + self.landed[k - 1].astype(F32)
        return value

    def sent(self):
        for copy in self.copies:
            copy.wait_send()


SPLIT = 384


def final_kernel(
    part, grads, weights, dn1, attention, rest,
    a_1, b_1, a_half, b_half, a_2, b_2, over_y, from_opposite, share, shares, *refs,
):
    at = Place()
    greet(
        [
            at.sibling(), at.partner(), at.diagonal(), at.opposite(),
            *[at.along(axis, k) for axis in ("x", "z") for k in (1, 2, 3)],
        ]
    )
    pair_refs = refs[:3]
    send, recv = refs[3:]
    base = 1 + 2 * PIECES
    width = grads.shape[-1]
    a, b = pl.ds(0, SPLIT), pl.ds(SPLIT, width - SPLIT)

    def x_of(k):
        return lax.rem(at.x + k, 4)

    def z_of(k):
        return lax.rem(at.z + k, 4)

    first_a = DirectScatter(
        at, "x", lambda k: grads.at[x_of(k), :, :, a], a_1, send, recv, base
    )
    first_b = DirectScatter(
        at, "z", lambda k: grads.at[:, z_of(k), :, b], b_1, send, recv, base + 3
    )
    pair = PairScatter(at, part, pair_refs, send, recv)
    pair.begin_far()
    pair.begin_own()
    pair.forward()
    a_half[...] = first_a.total().astype(BF)
    second_a = DirectScatter(
        at, "z", lambda k: a_half.at[z_of(k)], a_2, send, recv, base + 6
    )
    b_half[...] = first_b.total().astype(BF)
    second_b = DirectScatter(
        at, "x", lambda k: b_half.at[x_of(k)], b_2, send, recv, base + 9
    )
    over_y[:, a] = second_a.total().astype(BF)
    over_y[:, b] = second_b.total().astype(BF)
    theirs = pl.ds(pl.multiple_of((1 - at.yh) * 32, 32), 32)
    own = pl.ds(pl.multiple_of(at.yh * 32, 32), 32)
    swap = push(over_y.at[theirs], from_opposite, send, recv, base + 12, at.opposite())
    swap.wait_recv()
    total = over_y[own, :].astype(F32) + from_opposite[...].astype(F32)
    attention[...] = total[:, :768]
    gain_part = jnp.sum(total[:, :512] * weights[...].astype(F32), axis=1, keepdims=True)
    lane = lax.broadcasted_iota(jnp.int32, (32, 128), 1)
    share[...] = jnp.where(lane == 33, gain_part, total[:, 768:])
    copies = [
        push(share, shares.at[i], send, recv, base + 13 + i, device)
        for i, device in enumerate((at.sibling(), at.partner(), at.diagonal()))
    ]
    pair.finish(dn1)
    rest[...] = share[...]
    for i, copy in enumerate(copies):
        copy.wait_recv()
        rest[...] += shares[i]
    for copy in (swap, *copies):
        copy.wait_send()
    for scatter in (first_a, first_b, second_a, second_b):
        scatter.sent()


def final(part, grads, weights, ident):
    vmem = pl.BlockSpec(memory_space=pltpu.VMEM)
    width = grads.shape[1]
    sems = 1 + 2 * PIECES + 16
    return pl.pallas_call(
        final_kernel,
        in_specs=[vmem] * 3,
        out_specs=[vmem] * 3,
        out_shape=[
            jax.ShapeDtypeStruct((LOCAL, D), F32),
            jax.ShapeDtypeStruct((32, 768), F32),
            jax.ShapeDtypeStruct((32, 128), F32),
        ],
        scratch_shapes=[
            pltpu.VMEM((3, 4, 64, SPLIT), BF),
            pltpu.VMEM((3, 4, 64, width - SPLIT), BF),
            pltpu.VMEM((4, 64, SPLIT), BF),
            pltpu.VMEM((4, 64, width - SPLIT), BF),
            pltpu.VMEM((3, 64, SPLIT), BF),
            pltpu.VMEM((3, 64, width - SPLIT), BF),
            pltpu.VMEM((64, width), BF),
            pltpu.VMEM((32, width), BF),
            pltpu.VMEM((32, 128), F32),
            pltpu.VMEM((3, 32, 128), F32),
            *pair_scratch(LOCAL, D),
            pltpu.SemaphoreType.DMA((sems,)),
            pltpu.SemaphoreType.DMA((sems,)),
        ],
        compiler_params=pltpu.CompilerParams(
            collective_id=ident, has_side_effects=True, vmem_limit_bytes=32 * MIB
        ),
        name="final",
    )(part.reshape(4, LOCAL, D), grads.reshape(4, 4, 64, width), weights)


def last_kernel(grads, gate, up, down, send, recv, here):
    at = Place()
    greet([at.opposite()])
    half = pl.ds(at.yh * 16, 16)
    kept, copies = [], []
    for i, out in enumerate((gate, up, down)):
        theirs = grads.at[i, :, pl.ds((1 - at.yh) * 32, 32)]
        copies.append(push(theirs, out.at[half], send, recv, i, at.opposite()))
        kept.append(keep(grads.at[i, :, pl.ds(at.yh * 32, 32)], out.at[half], here.at[i]))
    for copy in (*copies, *kept):
        copy.wait()


def last_exchange(grads, ident):
    hbm = pl.BlockSpec(memory_space=pl.ANY)
    return pl.pallas_call(
        last_kernel,
        in_specs=[hbm],
        out_specs=[hbm] * 3,
        out_shape=[jax.ShapeDtypeStruct((E, 32, FF), BF)] * 3,
        scratch_shapes=[
            pltpu.SemaphoreType.DMA((3,)),
            pltpu.SemaphoreType.DMA((3,)),
            pltpu.SemaphoreType.DMA((3,)),
        ],
        compiler_params=pltpu.CompilerParams(collective_id=ident, has_side_effects=True),
        name="last_exchange",
    )(grads)


def rotary_tables():
    half = HD // 2
    inverse = (10000.0 ** (-(np.arange(half, dtype=np.float64) * 2.0) / HD)).astype(np.float32)
    angles = np.arange(SEQ, dtype=np.float32)[:, None] * inverse[None, :]
    cosine, sine = np.cos(angles), np.sin(angles)
    wide_cosine = np.concatenate([cosine] * 4, axis=1)
    wide_sine = np.concatenate([-sine, sine] * 2, axis=1)
    return wide_cosine.astype(np.float32), wide_sine.astype(np.float32)


def swapped(values):
    lane = lax.broadcasted_iota(jnp.int32, values.shape, 1)
    low = (lane % HD) < HD // 2
    return jnp.where(low, pltpu.roll(values, 96, 1), pltpu.roll(values, 32, 1))


def rotated(values, cosine, sine):
    return values * cosine + swapped(values) * sine


def bias_block(key_segment, query_segment, first, rows):
    key_at = lax.broadcasted_iota(jnp.int32, (rows, BLOCK), 0)
    query_at = lax.broadcasted_iota(jnp.int32, (rows, BLOCK), 1) + first
    allowed = (key_segment == query_segment) & (key_at <= query_at)
    return jnp.where(allowed, 0.0, MASKED)


def segment_row(segments):
    return jnp.concatenate(
        [segments[rank, i : i + 1, :] for rank in range(4) for i in range(2)], axis=1
    ).astype(F32)


def gain_rows(small):
    return small[:, 768:896].astype(F32).T[32:40, :]


def column_of(row):
    return jnp.broadcast_to(row, (8, row.shape[1])).T[:, 0:1]


def front_kernel(
    hidden, weights, cosine, sine, segments, own_hidden, named, out_grad, over_z, over_x,
    normed, query, key, value, context_t, log_total, middle, normed_moe, gating,
    quad_0, quad_1, out_grad_all, bias, part, context, *refs,
):
    pair_refs = refs[:3]
    send, recv, here = refs[3:]
    at = Place()
    greet(
        [
            at.sibling(), at.partner(), at.ring(1), at.ring(3),
            at.along("x", 1), at.along("x", 3), at.along("z", 1), at.along("z", 3),
        ]
    )
    ring = RingGather(at, out_grad, out_grad_all, send, recv, here.at[0], 0)
    quads = [
        QuadGather(
            at, i, over_z, over_x, quad, send, recv, here.at[pl.ds(1 + 2 * i, 2)],
            9 + QuadGather.COPIES * i,
        )
        for i, quad in enumerate((quad_0, quad_1))
    ]
    scatter = PairScatter(at, part, pair_refs, send, recv, 9 + 2 * QuadGather.COPIES)
    ring.begin()
    quads[0].begin()

    gains = gain_rows(weights)
    seg_row = segment_row(segments)
    seg_column = column_of(seg_row)
    for block in range(SEQ // BLOCK):
        rows = slice(block * BLOCK, (block + 1) * BLOCK)
        values = hidden[rows, :].astype(F32)
        scale = lax.rsqrt(jnp.mean(values * values, axis=-1, keepdims=True) + EPS)
        normed[rows, :] = (values * scale * gains[0:1, :]).astype(BF)
    for half in range(2):
        columns = slice(half * 128, half * 128 + 128)
        pre = mm(normed[...], weights[:, columns])
        query[:, columns] = (rotated(pre, cosine[...], sine[...]) * 0.125).astype(BF)
    key_pre = mm(normed[...], weights[:, 256:384])
    key[...] = rotated(key_pre, cosine[...], sine[...]).astype(BF)
    value_pre = mm(normed[...], weights[:, 384:512])
    value[...] = value_pre.astype(BF)
    value_t = value_pre.T.astype(BF)
    for block in range(SEQ // BLOCK):
        first, end = block * BLOCK, (block + 1) * BLOCK
        bias[:end, :] = bias_block(seg_column[:end, :], seg_row[:, first:end], first, end)
        for head in range(HEADS):
            kv = slice((head // 2) * HD, (head // 2) * HD + HD)
            own = slice(head * HD, head * HD + HD)
            scores = mm_last(key[:end, kv], query[first:end, own]) + bias[:end, :]
            top = jnp.max(scores, axis=0, keepdims=True)
            powers = jnp.exp(scores - top)
            total = jnp.sum(powers, axis=0, keepdims=True)
            share = (powers * (1.0 / total)).astype(BF)
            context_t[own, first:end] = mm(value_t[kv, :end], share).astype(BF)
            log_total[head : head + 1, first:end] = top + jnp.log(total)
        if block == 1:
            quads[0].forward()
            quads[1].begin()
        if block == 2:
            ring.forward_before()
            ring.forward_behind()
    context[...] = context_t[...].T

    def project(slot):
        rows = pl.ds(pl.multiple_of(slot * LOCAL, LOCAL), LOCAL)
        part[slot] = mm_last(context[rows, :], weights[:, 512:768]).astype(BF)

    project(scatter.other + 1 - at.core)
    scatter.begin_far()
    project(scatter.other + at.core)
    project(scatter.own + 1 - at.core)
    scatter.begin_own()
    project(scatter.own + at.core)
    scatter.forward()
    quads[1].forward()
    ring.forward_across()
    scatter.finish(middle)
    values = middle[...] + own_hidden[...].astype(F32)
    middle[...] = values
    scale = lax.rsqrt(jnp.mean(values * values, axis=-1, keepdims=True) + EPS)
    normed_moe[...] = (values * scale * gains[1:2, :]).astype(BF)
    chosen = named[...] > 0.0
    logits = jnp.where(chosen, mm(normed_moe[...], weights[:, 768:896]), MASKED)
    powers = jnp.where(chosen, jnp.exp(logits - jnp.max(logits, axis=-1, keepdims=True)), 0.0)
    gating[...] = powers / jnp.sum(powers, axis=-1, keepdims=True)
    for i in (0, 4, 6, 7, 8):
        ring.copy(i).wait_recv()
    ring.sent()
    ring.kept().wait()
    for quad in quads:
        quad.finish()


def front(hidden, weights, tables, segments, own_hidden, named, out_grad, lines, ident):
    vmem = pl.BlockSpec(memory_space=pltpu.VMEM)
    hbm = pl.BlockSpec(memory_space=pl.ANY)
    sems = 9 + 2 * QuadGather.COPIES + 1 + 2 * PIECES
    return pl.pallas_call(
        front_kernel,
        in_specs=[vmem] * 7 + [hbm] * 3,
        out_specs=[vmem] * 9 + [hbm] * 3,
        out_shape=[
            jax.ShapeDtypeStruct((SEQ, D), BF),
            jax.ShapeDtypeStruct((SEQ, HEADS * HD), BF),
            jax.ShapeDtypeStruct((SEQ, 128), BF),
            jax.ShapeDtypeStruct((SEQ, 128), BF),
            jax.ShapeDtypeStruct((HEADS * HD, SEQ), BF),
            jax.ShapeDtypeStruct((8, SEQ), F32),
            jax.ShapeDtypeStruct((LOCAL, D), F32),
            jax.ShapeDtypeStruct((LOCAL, D), BF),
            jax.ShapeDtypeStruct((LOCAL, 128), F32),
            QUAD_SHAPE,
            QUAD_SHAPE,
            jax.ShapeDtypeStruct((8, LOCAL, D), BF),
        ],
        scratch_shapes=[
            pltpu.VMEM((SEQ, BLOCK), F32),
            pltpu.VMEM((4, LOCAL, D), BF),
            pltpu.VMEM((SEQ, HEADS * HD), BF),
            *pair_scratch(LOCAL, D),
            pltpu.SemaphoreType.DMA((sems,)),
            pltpu.SemaphoreType.DMA((sems,)),
            pltpu.SemaphoreType.DMA((5,)),
        ],
        compiler_params=pltpu.CompilerParams(
            collective_id=ident, has_side_effects=True, vmem_limit_bytes=56 * MIB
        ),
        name="front",
    )(hidden, weights, *tables, segments, own_hidden, named, out_grad, *lines)


def back_kernel(
    dx, dgate, gating, middle, normed_moe, out_grad, y_part,
    normed, weights, cosine, sine, segments, query, key, value, context_t, log_total,
    dmiddle, dn1, grads, block_out,
    bias, dcontext, dquery_t, dkey, dvalue, dall, dall_t, dattn_own, dattn_all, y_sum, *refs,
):
    ring_refs = refs[:8]
    send, recv, here = refs[8:]
    at = Place()
    greet([at.sibling(), at.partner(), at.ring(1), at.ring(3)])
    gain = gain_rows(weights)[1:2, :]
    chosen = gating[...]
    dchosen = chosen * (dgate[...] - jnp.sum(chosen * dgate[...], axis=-1, keepdims=True))
    dlogits = dchosen.astype(BF)
    dnormed = dx[...] + mm_last(dlogits, weights[:, 768:896])
    values = middle[...]
    scale = lax.rsqrt(jnp.mean(values * values, axis=-1, keepdims=True) + EPS)
    unit = values * scale
    weighted = dnormed * gain
    inner = jnp.mean(weighted * unit, axis=-1, keepdims=True)
    total = out_grad[...].astype(F32) + scale * (weighted - unit * inner)
    dmiddle[...] = total
    dattn_own[...] = total.astype(BF)
    gather = PairGather(at, dattn_own, dattn_all, send, recv, here, 8, PIECES)
    scatter = RingScatter(at, y_part, ring_refs, send, recv)
    for k in (2, 1, 3, 0):
        scatter.copy(k).start()
    router_part = mm(normed_moe[...].T, dlogits)
    gain_part = column_of(jnp.sum(dnormed * unit, axis=0, keepdims=True))
    lane = lax.broadcasted_iota(jnp.int32, (D, 128), 1)
    grads[:, 768:] = jnp.where(lane == 32, gain_part, router_part).astype(BF)
    seg_row = segment_row(segments)
    seg_column = column_of(seg_row)
    gather.forward()
    scatter.far()
    gather.finish()
    dattn = dattn_all[...].reshape(SEQ, D)
    dcontext[...] = mm(dattn, weights[:, 512:768]).astype(BF)
    output_grad_t = mm(context_t[...], dattn)
    grads[:, 512:768] = output_grad_t.T.astype(BF)
    key_t = key[...].astype(F32).T.astype(BF)
    dkey[...] = jnp.zeros_like(dkey)
    dvalue[...] = jnp.zeros_like(dvalue)
    for block in range(SEQ // BLOCK):
        first, end = block * BLOCK, (block + 1) * BLOCK
        bias[:end, :] = bias_block(seg_column[:end, :], seg_row[:, first:end], first, end)
        for head in range(HEADS):
            kv = slice((head // 2) * HD, (head // 2) * HD + HD)
            own = slice(head * HD, head * HD + HD)
            query_block = query[first:end, own]
            dcontext_block = dcontext[first:end, own]
            scores = mm_last(key[:end, kv], query_block) + bias[:end, :]
            share = jnp.exp(scores - log_total[head : head + 1, first:end])
            dshare = mm_last(value[:end, kv], dcontext_block)
            centre = jnp.sum(share * dshare, axis=0, keepdims=True)
            dscore = (share * (dshare - centre)).astype(BF)
            dquery_t[own, first:end] = mm(key_t[kv, :end], dscore) * 0.125
            dkey[:end, kv] += mm(dscore, query_block)
            dvalue[:end, kv] += mm(share.astype(BF), dcontext_block)
        if block == 0:
            scatter.up_side()
            scatter.down_side()
    turn = -sine[...]
    for half in range(2):
        rows = slice(half * 128, half * 128 + 128)
        piece = rotated(dquery_t[rows, :].T, cosine[...], turn)
        dall[:, rows] = piece.astype(BF)
        dall_t[rows, :] = piece.T.astype(BF)
    piece = rotated(dkey[...], cosine[...], turn)
    dall[:, 256:384] = piece.astype(BF)
    dall_t[256:384, :] = piece.T.astype(BF)
    dall[:, 384:512] = dvalue[...].astype(BF)
    dall_t[384:512, :] = dvalue[...].T.astype(BF)
    grads[:, 0:512] = mm(dall_t[...], normed[...]).T.astype(BF)
    for block in range(SEQ // BLOCK):
        rows = slice(block * BLOCK, (block + 1) * BLOCK)
        dn1[rows, :] = mm_last(dall[rows, :], weights[:, 0:512]).astype(BF)
    scatter.finish(y_sum)
    block_out[...] = (y_sum[...] + middle[...]).astype(BF)


def back(
    dx, dgate, gating, middle, normed_moe, out_grad, y_part,
    normed, weights, tables, segments, kept, ident,
):
    vmem = pl.BlockSpec(memory_space=pltpu.VMEM)
    sems = 8 + 1 + 2 * PIECES
    return pl.pallas_call(
        back_kernel,
        in_specs=[vmem] * 17,
        out_specs=[vmem] * 4,
        out_shape=[
            jax.ShapeDtypeStruct((LOCAL, D), F32),
            jax.ShapeDtypeStruct((SEQ, D), BF),
            jax.ShapeDtypeStruct((D, SMALL), BF),
            jax.ShapeDtypeStruct((LOCAL, D), BF),
        ],
        scratch_shapes=[
            pltpu.VMEM((SEQ, BLOCK), F32),
            pltpu.VMEM((SEQ, HEADS * HD), BF),
            pltpu.VMEM((HEADS * HD, SEQ), F32),
            pltpu.VMEM((SEQ, 128), F32),
            pltpu.VMEM((SEQ, 128), F32),
            pltpu.VMEM((SEQ, 512), BF),
            pltpu.VMEM((512, SEQ), BF),
            pltpu.VMEM((LOCAL, D), BF),
            pltpu.VMEM((4, LOCAL, D), BF),
            pltpu.VMEM((LOCAL, D), F32),
            *ring_scratch(LOCAL, D),
            pltpu.SemaphoreType.DMA((sems,)),
            pltpu.SemaphoreType.DMA((sems,)),
            pltpu.SemaphoreType.DMA,
        ],
        compiler_params=pltpu.CompilerParams(
            collective_id=ident, has_side_effects=True, vmem_limit_bytes=58 * MIB
        ),
        name="back",
    )(
        dx, dgate, gating, middle, normed_moe, out_grad, y_part,
        normed, weights, *tables, segments, *kept,
    )


def experts_kernel(
    x_in, gate_in, d_in, quad_0, quad_1, over_z, over_x,
    y_out, dx_out, dgate_out, grads, quad_2, quad_3,
    x, d, xt, dt, y, dx, gating, dgate, dgate_part, hidden, w, *refs,
):
    dx_scratch, dgate_scratch = refs[:5], refs[5:10]
    send, recv, here, load, store, fetch = refs[10:16]
    at = Place()
    step = pl.program_id(0)
    opening, closing = step == 0, step == STEPS - 1
    rows_at_once = 2 * LOCAL
    lane = lax.broadcasted_iota(jnp.int32, (LOCAL, 128), 1)
    own_first = at.yh * 16 + step * QUAD
    x_gather = RingGather(at, x_in, x, send, recv, here.at[0], 0)
    gate_gather = RingGather(at, gate_in, gating, send, recv, here.at[1], 9)
    gathers = (x_gather, gate_gather)
    scatters = (
        RingScatter(at, d, dx_scratch, send, recv, 18),
        RingScatter(at, dgate_part, dgate_scratch, send, recv, 26),
    )

    quads = [
        QuadGather(
            at, 2 + i, over_z, over_x, quad, *refs[16:18], refs[18].at[pl.ds(2 * i, 2)],
            QuadGather.COPIES * i,
        )
        for i, quad in enumerate((quad_2, quad_3))
    ]

    def ride(condition, what):
        for i, quad in enumerate(quads):

            @pl.when(condition & (step == i))
            def _():
                what(quad)

    def fetches(quad):
        return [
            pltpu.make_async_copy(
                quad.at[g, i], w.at[:, :, :, pl.ds((g * QUAD + i) * FF, FF)],
                fetch.at[g * QUAD + i],
            )
            for g in range(3)
            for i in range(QUAD)
        ]

    def d_load(chip):
        two = pl.ds(chip * 2, 2)
        return pltpu.make_async_copy(d_in.at[two], d.at[two], load.at[chip])

    def y_store(chip):
        two = pl.ds(chip * 2, 2)
        return pltpu.make_async_copy(x.at[two], y_out.at[two], store.at[chip])

    @pl.when(opening)
    def _():
        greet(
            [
                at.sibling(), at.ring(1), at.ring(3),
                at.along("x", 1), at.along("x", 3), at.along("z", 1), at.along("z", 3),
            ]
        )
        for gather in gathers:
            gather.begin()
        for copy in fetches(quad_0):
            copy.start()
        for chip in range(4):
            d_load(chip).start()

    for copy in fetches(quad_0):
        copy.wait()

    ride(step < STEPS, lambda quad: quad.begin())

    def arrive(turn):
        @pl.when(turn == 0)
        def _():
            for gather in gathers:
                gather.kept().wait()
                gather.copy(0).wait_recv()

        @pl.when(turn == 1)
        def _():
            for gather in gathers:
                gather.forward_before()
                gather.forward_behind()
            for gather in gathers:
                gather.copy(4).wait_recv()

        @pl.when(turn == 2)
        def _():
            for gather in gathers:
                gather.forward_across()
            for gather in gathers:
                gather.copy(6).wait_recv()

        @pl.when(turn == 3)
        def _():
            for gather in gathers:
                gather.copy(7).wait_recv()
                gather.copy(8).wait_recv()

    def leave(turn):
        @pl.when(turn == 0)
        def _():
            for scatter in scatters:
                scatter.copy(2).start()

        @pl.when(turn == 1)
        def _():
            for scatter in scatters:
                scatter.copy(1).start()
                scatter.far()

        @pl.when(turn == 2)
        def _():
            for scatter in scatters:
                scatter.copy(3).start()
                scatter.up_side()

        @pl.when(turn == 3)
        def _():
            for scatter in scatters:
                scatter.copy(0).start()
                scatter.down_side()

    def tokens_block(turn, carry):
        inward = jnp.where(turn == 0, 0, jnp.where(turn == 1, 3, turn - 1))
        outward = jnp.where(turn == 0, 2, jnp.where(turn == 3, 0, turn * 2 - 1))
        chip = at.chip(jnp.where(closing, outward, inward))
        two = pl.ds(chip * 2, 2)
        rows = pl.ds(pl.multiple_of(chip * rows_at_once, rows_at_once), rows_at_once)

        @pl.when(opening)
        def _():
            arrive(turn)
            d_load(chip).wait()
            xt[:, rows] = x[two].reshape(rows_at_once, D).T
            dt[:, rows] = d[two].reshape(rows_at_once, D).T
            y[rows, :] = jnp.zeros((rows_at_once, D), F32)
            dx[rows, :] = jnp.zeros((rows_at_once, D), F32)
            dgate[rows, :] = jnp.zeros((rows_at_once, 128), F32)

        ride(turn == 3, lambda quad: quad.forward())
        gate_up = w[:, :, :, 0 : 2 * F].reshape(D, 2 * F)
        down = w[:, :, :, 2 * F :].reshape(D, F)
        for core in range(2):
            slot = chip * 2 + core
            part = pl.ds(pl.multiple_of(slot * LOCAL, LOCAL), LOCAL)
            both = mm(x[slot], gate_up)
            gate, up = both[:, :F], both[:, F:]
            dact = mm(d[slot], down)
            turned = pltpu.roll(gating[slot], lax.rem(128 - own_first, 128), 1)
            factor = jnp.concatenate(
                [jnp.broadcast_to(turned[:, i : i + 1], (LOCAL, FF)) for i in range(QUAD)],
                axis=1,
            )
            q = 1.0 / (1.0 + jnp.exp(-gate))
            silu = gate * q
            act = silu * up
            product = act * dact
            sums = dgate[part, :]
            for i in range(QUAD):
                own = jnp.sum(product[:, i * FF : (i + 1) * FF], axis=1, keepdims=True)
                sums = jnp.where(lane == own_first + i, own, sums)
            dgate[part, :] = sums
            dact = dact * factor
            hidden[part, 0:F] = (dact * up * (q + silu * (1.0 - q))).astype(BF)
            hidden[part, F : 2 * F] = (dact * silu).astype(BF)
            hidden[part, 2 * F :] = (act * factor).astype(BF)
        y[rows, :] += mm_last(hidden[rows, 2 * F :], down)
        dx[rows, :] += mm_last(hidden[rows, 0 : 2 * F], gate_up)

        @pl.when(closing)
        def _():
            x[two] = y[rows, :].astype(BF).reshape(2, LOCAL, D)
            d[two] = dx[rows, :].astype(BF).reshape(2, LOCAL, D)
            dgate_part[two] = dgate[rows, :].astype(BF).reshape(2, LOCAL, 128)
            y_store(chip).start()
            leave(turn)

        return carry

    lax.fori_loop(0, 4, tokens_block, 0)

    for number, quad in enumerate((quad_1, quad_2, quad_3)):

        @pl.when(step == number)
        def _():
            for copy in fetches(quad):
                copy.start()

    @pl.when(opening)
    def _():
        for gather in gathers:
            gather.sent()

    def grads_block(block, carry):
        rows = pl.ds(pl.multiple_of(block * 512, 512), 512)
        both = mm(xt[rows, :], hidden[:, 0 : 2 * F]).astype(BF)
        for g in range(2):
            for i in range(QUAD):
                first = (g * QUAD + i) * FF
                grads[g, i, rows, :] = both[:, first : first + FF]
        down = mm(dt[rows, :], hidden[:, 2 * F :]).astype(BF)
        for i in range(QUAD):
            grads[2, i, rows, :] = down[:, i * FF : (i + 1) * FF]
        return carry

    lax.fori_loop(0, D // 512, grads_block, 0)
    ride(step < STEPS, lambda quad: quad.finish())

    @pl.when(closing)
    def _():
        scatters[0].finish(dx_out)
        scatters[1].finish(dgate_out)
        for chip in range(4):
            y_store(chip).wait()


def experts(x, gating, d, quads, lines, ident):
    hbm = pl.BlockSpec(memory_space=pl.ANY)

    def whole(rows, columns):
        return pl.BlockSpec((rows, columns), lambda step: (0, 0), pipeline_mode=pl.Buffered(1))

    return pl.pallas_call(
        experts_kernel,
        grid=(STEPS,),
        in_specs=[hbm] * 7,
        out_specs=[
            hbm,
            whole(LOCAL, D),
            whole(LOCAL, 128),
            pl.BlockSpec(
                (3, QUAD, D, FF), lambda step: (0, step, 0, 0), pipeline_mode=pl.Buffered(1)
            ),
            *[hbm] * 2,
        ],
        out_shape=[
            jax.ShapeDtypeStruct((8, LOCAL, D), BF),
            jax.ShapeDtypeStruct((LOCAL, D), F32),
            jax.ShapeDtypeStruct((LOCAL, 128), F32),
            jax.ShapeDtypeStruct((3, STEPS * QUAD, D, FF), BF),
            *[QUAD_SHAPE] * 2,
        ],
        scratch_shapes=[
            pltpu.VMEM((8, LOCAL, D), BF),
            pltpu.VMEM((8, LOCAL, D), BF),
            pltpu.VMEM((D, TOKENS), BF),
            pltpu.VMEM((D, TOKENS), BF),
            pltpu.VMEM((TOKENS, D), F32),
            pltpu.VMEM((TOKENS, D), F32),
            pltpu.VMEM((8, LOCAL, 128), F32),
            pltpu.VMEM((TOKENS, 128), F32),
            pltpu.VMEM((8, LOCAL, 128), BF),
            pltpu.VMEM((TOKENS, 3 * F), BF),
            pltpu.VMEM((4, 4, 64, 3 * F), BF),
            *ring_scratch(LOCAL, D, False),
            *ring_scratch(LOCAL, 128, False),
            pltpu.SemaphoreType.DMA((34,)),
            pltpu.SemaphoreType.DMA((34,)),
            pltpu.SemaphoreType.DMA((2,)),
            pltpu.SemaphoreType.DMA((4,)),
            pltpu.SemaphoreType.DMA((4,)),
            pltpu.SemaphoreType.DMA((3 * QUAD,)),
            pltpu.SemaphoreType.DMA((2 * QuadGather.COPIES,)),
            pltpu.SemaphoreType.DMA((2 * QuadGather.COPIES,)),
            pltpu.SemaphoreType.DMA((4,)),
        ],
        compiler_params=pltpu.CompilerParams(
            collective_id=ident, has_side_effects=True, vmem_limit_bytes=63 * MIB
        ),
        name="experts",
    )(x, gating, d, *quads, *lines)[:4]


def norm_scale(values):
    return lax.rsqrt(jnp.mean(values * values, axis=-1, keepdims=True) + EPS)


def norm_grad(values, gain, dnormed):
    scale = norm_scale(values)
    unit = values * scale
    weighted = dnormed * gain
    dvalues = scale * (weighted - unit * jnp.mean(weighted * unit, axis=-1, keepdims=True))
    return dvalues


def on_device(
    hidden_in, out_grad, attn_gain, query_weight, key_weight, value_weight, output_weight,
    moe_gain, router_weight, expert_gate, expert_up, expert_down, expert_ids, segment_ids,
):
    small = jnp.concatenate(
        [
            query_weight, key_weight, value_weight, output_weight,
            router_weight, attn_gain[:, None], moe_gain[:, None], jnp.zeros((32, 94), BF),
        ],
        axis=1,
    )
    segment = jnp.pad(segment_ids.reshape(2, 128), ((0, 6), (0, 0)))
    own_shares = (expert_gate, expert_up, expert_down)
    hidden_all, segments, small, *lines = startup(hidden_in, segment, small, own_shares, 0)
    tables = tuple(jnp.asarray(t) for t in rotary_tables())
    named = jnp.any(
        expert_ids[:, :, None] == jnp.arange(128, dtype=jnp.int32)[None, None, :], axis=1
    ).astype(F32)

    normed, *kept, middle, normed_moe, gating, quad_0, quad_1, d = front(
        hidden_all, small, tables, segments, hidden_in, named, out_grad, lines, 1
    )
    y, dx, dgate, expert_grads = experts(
        normed_moe, gating, d, (quad_0, quad_1), lines, 3
    )
    expert_grads = lax.psum_scatter(expert_grads, PLANE, scatter_dimension=2, tiled=True)
    dmiddle, dn1, grads, block_out = back(
        dx, dgate, gating, middle, normed_moe, out_grad, y,
        normed, small, tables, segments, kept, 5,
    )
    weights = jnp.concatenate([query_weight, key_weight, value_weight], axis=1)
    dn1, attention_grads, rest = final(dn1, grads, weights, 6)
    hidden = hidden_in.astype(F32)
    dhidden = norm_grad(hidden, small[:, 800].astype(F32), dn1)
    hidden_grad = dmiddle + dhidden
    expert_grads = [share.astype(F32) for share in last_exchange(expert_grads, 7)]
    return (
        block_out,
        hidden_grad,
        rest[:, 33] / attn_gain.astype(F32),
        attention_grads[:, 0:256],
        attention_grads[:, 256:384],
        attention_grads[:, 384:512],
        attention_grads[:, 512:768],
        rest[:, 32],
        rest[:, :32],
        *expert_grads,
    )


def solution(mesh):
    fine = Mesh(np.asarray(mesh.devices).reshape(4, 4, 2, 2, 2), ALL)
    return jax.shard_map(
        on_device,
        mesh=fine,
        in_specs=(
            P(ALL, None),
            P(ALL, None),
            P(DP),
            P(DP, TENSOR),
            P(DP, TENSOR),
            P(DP, TENSOR),
            P(DP, TENSOR),
            P(DP),
            P(DP, None),
            P(None, DP, TENSOR),
            P(None, DP, TENSOR),
            P(None, DP, TENSOR),
            P(ALL, None),
            P(ALL),
        ),
        out_specs=(
            P(ALL, None),
            P(ALL, None),
            P(DP),
            P(DP, TENSOR),
            P(DP, TENSOR),
            P(DP, TENSOR),
            P(DP, TENSOR),
            P(DP),
            P(DP, None),
            P(None, DP, TENSOR),
            P(None, DP, TENSOR),
            P(None, DP, TENSOR),
        ),
        check_vma=False,
    )
```

```python
import jax
import jax.numpy as jnp
import numpy as np
from jax import lax
from jax.experimental import pallas as pl
from jax.experimental.pallas import tpu as pltpu
from jax.sharding import Mesh
from jax.sharding import PartitionSpec as P

D = 1024
HD = 64
E = 32
SEQ = 1024
LOCAL = 256
HEADS = 4
QUAD = 4
FF = 128
F = QUAD * FF
EPS = 1e-06
MASKED = -1e30
BLOCK = 256
TOKENS = 2048
STEPS = 4

DP = ("x", "z", "yh")
TENSOR = ("yl", "core")
RING = ("yh", "yl", "core")
PLANE = ("x", "z")
ALL = ("x", "z", "yh", "yl", "core")

F32 = jnp.float32
BF = jnp.bfloat16
LAST = (((1,), (1,)), ((), ()))
MIB = 1024 * 1024
MESH = pl.DeviceIdType.MESH
SMALL = 896


def mm(a, b):
    return jnp.dot(a, b, preferred_element_type=F32)


def mm_last(a, b):
    return lax.dot_general(a, b, LAST, preferred_element_type=F32)


class Place:
    def __init__(self):
        self.x = lax.axis_index("x")
        self.z = lax.axis_index("z")
        self.yh = lax.axis_index("yh")
        self.yl = lax.axis_index("yl")
        self.core = lax.axis_index("core")
        self.y = self.yh * 2 + self.yl

    def chip(self, k):
        return lax.rem(self.y + k, 4)

    def ring(self, k):
        chip = self.chip(k)
        return {"yh": chip // 2, "yl": lax.rem(chip, 2)}

    def along(self, axis, k):
        return {axis: lax.rem(getattr(self, axis) + k, 4)}

    def sibling(self):
        return {"core": 1 - self.core}

    def partner(self):
        return {"yl": 1 - self.yl}

    def diagonal(self):
        return {"yl": 1 - self.yl, "core": 1 - self.core}

    def opposite(self):
        return {"yh": 1 - self.yh}


def greet(devices):
    barrier = pltpu.get_barrier_semaphore()
    for device in devices:
        pl.semaphore_signal(barrier, inc=1, device_id=device, device_id_type=MESH)
    pl.semaphore_wait(barrier, len(devices))


def remote(src, dst, send, recv, i, device):
    return pltpu.make_async_remote_copy(
        src_ref=src, dst_ref=dst, send_sem=send.at[i], recv_sem=recv.at[i],
        device_id=device, device_id_type=MESH,
    )


def push(src, dst, send, recv, i, device):
    copy = remote(src, dst, send, recv, i, device)
    copy.start()
    return copy


def keep(src, dst, sem):
    copy = pltpu.make_async_copy(src, dst, sem)
    copy.start()
    return copy


class RingGather:
    def __init__(self, at, own, out, send, recv, here, base=0):
        self.at, self.own, self.out, self.base = at, own, out, base
        self.send, self.recv, self.here = send, recv, here
        half = own.shape[0] // 2
        lo, hi = pl.ds(0, half), pl.ds(half, half)
        me, before, behind, across = (out.at[self.slot(k)] for k in (0, 3, 1, 2))
        near, up, down = at.sibling(), at.ring(1), at.ring(3)
        self.plan = [
            (own, me, near),
            (own, me, up),
            (own, me, down),
            (before.at[lo], before.at[lo], up),
            (before, before, near),
            (behind.at[hi], behind.at[hi], down),
            (behind, behind, near),
            (across.at[lo], across.at[lo], near),
            (across.at[hi], across.at[hi], near),
        ]

    def slot(self, k):
        return self.at.chip(k) * 2 + self.at.core

    def copy(self, i):
        src, dst, device = self.plan[i]
        return remote(src, dst, self.send, self.recv, self.base + i, device)

    def kept(self):
        return pltpu.make_async_copy(self.own, self.out.at[self.slot(0)], self.here)

    def begin(self):
        self.kept().start()
        for i in (1, 2, 0):
            self.copy(i).start()

    def forward_before(self):
        self.copy(1).wait_recv()
        self.copy(3).start()
        self.copy(4).start()

    def forward_behind(self):
        self.copy(2).wait_recv()
        self.copy(5).start()
        self.copy(6).start()

    def forward_across(self):
        self.copy(3).wait_recv()
        self.copy(7).start()
        self.copy(5).wait_recv()
        self.copy(8).start()

    def sent(self):
        for i in range(9):
            self.copy(i).wait_send()


class PairGather:
    def __init__(self, at, own, out, send, recv, here, base, pieces):
        self.at, self.out, self.send, self.recv, self.base = at, out, send, recv, base
        size = own.shape[0] // pieces
        self.parts = [pl.ds(i * size, size) for i in range(pieces)]
        me = at.yl * 2 + at.core
        self.other = (1 - at.yl) * 2 + at.core
        self.kept = keep(own, out.at[me], here)
        self.far = [
            push(own.at[part], out.at[me, part], send, recv, base + 1 + i, at.partner())
            for i, part in enumerate(self.parts)
        ]
        self.near = [push(own, out.at[me], send, recv, base, at.sibling())]

    def forward(self):
        for i, part in enumerate(self.parts):
            self.far[i].wait_recv()
            view = self.out.at[self.other, part]
            index = self.base + 1 + len(self.parts) + i
            self.near.append(push(view, view, self.send, self.recv, index, self.at.sibling()))

    def finish(self):
        for copy in self.near:
            copy.wait_recv()
        for copy in (*self.far, *self.near):
            copy.wait_send()
        self.kept.wait()


PIECES = 4


class AxisGather:
    def __init__(self, at, axis, view, send, recv, base):
        self.up, self.down = at.along(axis, 1), at.along(axis, 3)
        self.view, self.send, self.recv, self.base = view, send, recv, base

    def go(self, i, view, device):
        return push(view, view, self.send, self.recv, self.base + i, device)

    def begin(self):
        self.first = [
            self.go(0, self.view(0, "all"), self.up), self.go(1, self.view(0, "all"), self.down),
        ]

    def forward(self):
        self.first[0].wait_recv()
        self.far = [self.go(2, self.view(3, "low"), self.up)]
        self.first[1].wait_recv()
        self.far.append(self.go(3, self.view(1, "high"), self.down))

    def finish(self):
        for copy in self.far:
            copy.wait_recv()
        for copy in (*self.first, *self.far):
            copy.wait_send()


def halves_of(ref, first, size):
    spans = {"all": (0, size), "low": (0, size // 2), "high": (size // 2, size // 2)}
    return lambda part: ref.at[pl.ds(first + spans[part][0], spans[part][1])]


class SpreadOut:
    COPIES = 8

    def __init__(self, at, rings, send, recv, here, base=0):
        self.send, self.recv, self.here, self.base = send, recv, here, base
        self.own = [(own, slot(0)) for _, own, slot, _ in rings]
        self.plan = []
        for axis, own, slot, _ in rings:
            self.plan.append((own, slot(0), at.along(axis, 1)))
            self.plan.append((own, slot(0), at.along(axis, 3)))
        for axis, _, slot, half in rings:
            low, high = (slot(3).at[pl.ds(0, half)], slot(1).at[pl.ds(half, half)])
            self.plan.append((low, low, at.along(axis, 1)))
            self.plan.append((high, high, at.along(axis, 3)))

    def copy(self, i):
        src, dst, device = self.plan[i]
        return remote(src, dst, self.send, self.recv, self.base + i, device)

    def kept(self, i):
        src, dst = self.own[i]
        return pltpu.make_async_copy(src, dst, self.here.at[i])

    def begin(self):
        for i in range(4):
            self.copy(i).start()
        for i in range(2):
            self.kept(i).start()

    def forward(self):
        for i in range(4):
            self.copy(i).wait_recv()
            self.copy(4 + i).start()

    def finish(self):
        for i in range(4, 8):
            self.copy(i).wait_recv()
        for i in range(8):
            self.copy(i).wait_send()
        for i in range(2):
            self.kept(i).wait()


def ring_slots(out, place):
    return lambda k: out.at[lax.rem(place + k, 4)]


def first_gather(at, own_a, own_b, over_z, over_x, *sems):
    rings = (
        ("z", own_a, ring_slots(over_z, at.z), 1), ("x", own_b, ring_slots(over_x, at.x), 1),
    )
    return SpreadOut(at, rings, *sems)


def second_gather(at, number, over_z, over_x, quad_a, quad_b, *sems):
    rings = (
        ("x", over_z.at[:, :, number], ring_slots(quad_a, at.x), 2),
        ("z", over_x.at[:, :, number], ring_slots(quad_b, at.z), 2),
    )
    return SpreadOut(at, rings, *sems)


SHARE_SHAPE = jax.ShapeDtypeStruct((2, STEPS, 3, 2, 32, FF), BF)
LINE_SHAPE = jax.ShapeDtypeStruct((4, 2, STEPS, 3, 2, 32, FF), BF)
QUAD_SHAPE = jax.ShapeDtypeStruct((4, 4, 2, 3, 2, 32, FF), BF)


def startup_kernel(
    hidden, segment, small, gate, up, down,
    hidden_all, segment_all, small_all, share_a, share_b, over_z_line, over_x_line,
    send, recv, here,
):
    at = Place()
    greet(
        [
            at.sibling(), at.partner(), at.diagonal(), at.opposite(),
            at.along("x", 1), at.along("x", 3), at.along("z", 1), at.along("z", 3),
        ]
    )
    rank = at.yl * 2 + at.core
    mine = small_all.at[(at.x * 4 + at.z) * 2 + at.yh]
    small_kept = keep(small, mine, here.at[0])
    copies = [push(small, mine, send, recv, 0, at.opposite())]
    swaps, swaps_kept = [], []
    base = 13 + 2 * PIECES
    for i, share in enumerate((gate, up, down)):
        for j, out in enumerate((share_a, share_b)):
            dst, two = out.at[at.yh, :, i], pl.ds(2 * j, 2)
            theirs = share.at[pl.ds((1 - at.yh) * STEPS, STEPS), two]
            index = 2 * i + j
            swaps.append(push(theirs, dst, send, recv, base + index, at.opposite()))
            own = share.at[pl.ds(at.yh * STEPS, STEPS), two]
            swaps_kept.append(keep(own, dst, here.at[3 + index]))
    experts = first_gather(
        at, share_a, share_b, over_z_line, over_x_line, send, recv, here.at[pl.ds(9, 2)], base + 6
    )
    copies.extend(
        push(segment, segment_all.at[rank], send, recv, 1 + i, device)
        for i, device in enumerate((at.sibling(), at.partner(), at.diagonal()))
    )
    pair = PairGather(at, hidden, hidden_all, send, recv, here.at[1], 12, PIECES)
    seg_here = keep(segment, segment_all.at[rank], here.at[2])
    over_z = AxisGather(
        at, "z",
        lambda k, part: halves_of(small_all, (at.x * 4 + lax.rem(at.z + k, 4)) * 2, 2)(part),
        send, recv, 4,
    )
    over_x = AxisGather(
        at, "x", lambda k, part: halves_of(small_all, lax.rem(at.x + k, 4) * 8, 8)(part),
        send, recv, 8,
    )
    small_kept.wait()
    copies[0].wait_recv()
    over_z.begin()
    over_z.forward()
    over_z.finish()
    over_x.begin()
    pair.forward()
    for swap, own in zip(swaps, swaps_kept):
        swap.wait_recv()
        own.wait()
    experts.begin()
    over_x.forward()
    experts.forward()
    pair.finish()
    seg_here.wait()
    for copy in copies[1:]:
        copy.wait_recv()
    over_x.finish()
    experts.finish()
    for copy in (*copies, *swaps):
        copy.wait_send()


def startup(hidden, segment, small, shares, ident):
    hbm = pl.BlockSpec(memory_space=pl.ANY)
    sems = 13 + 2 * PIECES + 6 + SpreadOut.COPIES
    shares = [share.reshape(2 * STEPS, QUAD, 32, FF) for share in shares]
    hidden_all, segment_all, small_all, _, _, over_z, over_x = pl.pallas_call(
        startup_kernel,
        in_specs=[hbm] * 6,
        out_specs=[hbm] * 7,
        out_shape=[
            jax.ShapeDtypeStruct((4, *hidden.shape), hidden.dtype),
            jax.ShapeDtypeStruct((4, *segment.shape), segment.dtype),
            jax.ShapeDtypeStruct((32, 32, SMALL), small.dtype),
            SHARE_SHAPE,
            SHARE_SHAPE,
            LINE_SHAPE,
            LINE_SHAPE,
        ],
        scratch_shapes=[
            pltpu.SemaphoreType.DMA((sems,)),
            pltpu.SemaphoreType.DMA((sems,)),
            pltpu.SemaphoreType.DMA((11,)),
        ],
        compiler_params=pltpu.CompilerParams(collective_id=ident, has_side_effects=True),
        name="startup",
    )(hidden, segment, small, *shares)
    hidden_all, small_all = hidden_all.reshape(SEQ, D), small_all.reshape(D, SMALL)
    return hidden_all, segment_all, small_all, over_z, over_x


class RingScatter:
    def __init__(self, at, part, scratch, send, recv, base=0):
        self.at, self.part, self.send, self.recv, self.base = at, part, send, recv, base
        near, half_a, half_b, self.full_up, self.full_down = scratch[:5]
        to_far, to_up, to_down = scratch[5:] or [
            part.at[at.chip(k) * 2 + at.core] for k in (2, 1, 3)
        ]
        self.near, self.half_a, self.half_b = near, half_a, half_b
        self.to_far, self.to_up, self.to_down = to_far, to_up, to_down
        self.half = half_a.shape[0]
        self.lo, self.hi = pl.ds(0, self.half), pl.ds(self.half, self.half)
        up, down = at.ring(1), at.ring(3)
        self.plan = {
            k: (part.at[at.chip(k) * 2 + 1 - at.core], near.at[k], at.sibling()) for k in range(4)
        }
        self.plan[4] = (to_far.at[self.lo], half_a, up)
        self.plan[5] = (to_far.at[self.hi], half_b, down)
        self.plan[6] = (to_up, self.full_up, up)
        self.plan[7] = (to_down, self.full_down, down)

    def copy(self, i):
        src, dst, device = self.plan[i]
        return remote(src, dst, self.send, self.recv, self.base + i, device)

    def chip_sum(self, k):
        self.copy(k).wait_recv()
        own = self.part[self.at.chip(k) * 2 + self.at.core]
        return own.astype(F32) + self.near[k].astype(F32)

    def far(self):
        self.to_far[...] = self.chip_sum(2).astype(BF)
        self.copy(4).start()
        self.copy(5).start()

    def up_side(self):
        total = self.chip_sum(1)
        self.copy(4).wait_recv()
        self.to_up[self.lo, :] = (total[: self.half] + self.half_a[...].astype(F32)).astype(BF)
        self.to_up[self.hi, :] = total[self.half :].astype(BF)
        self.copy(6).start()

    def down_side(self):
        total = self.chip_sum(3)
        self.copy(5).wait_recv()
        self.to_down[self.lo, :] = total[: self.half].astype(BF)
        self.to_down[self.hi, :] = (total[self.half :] + self.half_b[...].astype(F32)).astype(BF)
        self.copy(7).start()

    def finish(self, out):
        out[...] = self.chip_sum(0)
        self.copy(6).wait_recv()
        out[...] += self.full_up[...].astype(F32)
        self.copy(7).wait_recv()
        out[...] += self.full_down[...].astype(F32)
        for i in range(8):
            self.copy(i).wait_send()


def ring_scratch(rows, columns, own_sends=True):
    block, half = pltpu.VMEM((rows, columns), BF), pltpu.VMEM((rows // 2, columns), BF)
    scratch = [pltpu.VMEM((4, rows, columns), BF), half, half, block, block]
    return scratch + [block] * 3 if own_sends else scratch


class PairScatter:
    def __init__(self, at, part, scratch, send, recv, base=0):
        self.at, self.part, self.send, self.recv, self.base = at, part, send, recv, base
        self.near, self.far_rows, self.to_far = scratch
        size = self.to_far.shape[0] // PIECES
        self.parts = [pl.ds(i * size, size) for i in range(PIECES)]
        self.other, self.own = (1 - at.yl) * 2, at.yl * 2

    def go(self, i, src, dst, device):
        return push(src, dst, self.send, self.recv, self.base + i, device)

    def begin_far(self):
        slot = self.other + 1 - self.at.core
        self.first = [
            self.go(i, self.part.at[slot, rows], self.near.at[1, rows], self.at.sibling())
            for i, rows in enumerate(self.parts)
        ]

    def begin_own(self):
        slot = self.own + 1 - self.at.core
        self.second = self.go(PIECES, self.part.at[slot], self.near.at[0], self.at.sibling())

    def forward(self):
        self.sent = []
        for i, rows in enumerate(self.parts):
            self.first[i].wait_recv()
            own = self.part[self.other + self.at.core, rows, :].astype(F32)
            self.to_far[rows, :] = (own + self.near[1, rows, :].astype(F32)).astype(BF)
            far = self.far_rows.at[rows]
            self.sent.append(self.go(PIECES + 1 + i, self.to_far.at[rows], far, self.at.partner()))

    def finish(self, out):
        self.second.wait_recv()
        out[...] = self.part[self.own + self.at.core].astype(F32) + self.near[0].astype(F32)
        for i, rows in enumerate(self.parts):
            self.sent[i].wait_recv()
            out[rows, :] += self.far_rows[rows, :].astype(F32)
        for copy in (*self.first, self.second, *self.sent):
            copy.wait_send()


def pair_scratch(rows, columns):
    block = pltpu.VMEM((rows, columns), BF)
    return [pltpu.VMEM((2, rows, columns), BF), block, block]


class DirectScatter:
    def __init__(self, at, axis, blocks, landed, send, recv, base):
        self.blocks, self.landed = blocks, landed
        self.copies = [
            push(blocks(k), landed.at[k - 1], send, recv, base + k - 1, at.along(axis, k))
            for k in (2, 1, 3)
        ]

    def total(self):
        value = self.blocks(0)[...].astype(F32)
        for copy, k in zip(self.copies, (2, 1, 3)):
            copy.wait_recv()
            value = value + self.landed[k - 1].astype(F32)
        return value

    def sent(self):
        for copy in self.copies:
            copy.wait_send()


SPLIT = 384


def final_kernel(
    part, grads, weights, dn1, attention, rest,
    a_1, b_1, a_half, b_half, a_2, b_2, over_y, from_opposite, share, shares, *refs,
):
    at = Place()
    greet(
        [
            at.sibling(), at.partner(), at.diagonal(), at.opposite(),
            *[at.along(axis, k) for axis in ("x", "z") for k in (1, 2, 3)],
        ]
    )
    pair_refs = refs[:3]
    send, recv = refs[3:]
    base = 1 + 2 * PIECES
    width = grads.shape[-1]
    a, b = pl.ds(0, SPLIT), pl.ds(SPLIT, width - SPLIT)

    def x_of(k):
        return lax.rem(at.x + k, 4)

    def z_of(k):
        return lax.rem(at.z + k, 4)

    first_a = DirectScatter(
        at, "x", lambda k: grads.at[x_of(k), :, :, a], a_1, send, recv, base
    )
    first_b = DirectScatter(
        at, "z", lambda k: grads.at[:, z_of(k), :, b], b_1, send, recv, base + 3
    )
    pair = PairScatter(at, part, pair_refs, send, recv)
    pair.begin_far()
    pair.begin_own()
    pair.forward()
    a_half[...] = first_a.total().astype(BF)
    second_a = DirectScatter(
        at, "z", lambda k: a_half.at[z_of(k)], a_2, send, recv, base + 6
    )
    b_half[...] = first_b.total().astype(BF)
    second_b = DirectScatter(
        at, "x", lambda k: b_half.at[x_of(k)], b_2, send, recv, base + 9
    )
    over_y[:, a] = second_a.total().astype(BF)
    over_y[:, b] = second_b.total().astype(BF)
    theirs = pl.ds(pl.multiple_of((1 - at.yh) * 32, 32), 32)
    own = pl.ds(pl.multiple_of(at.yh * 32, 32), 32)
    swap = push(over_y.at[theirs], from_opposite, send, recv, base + 12, at.opposite())
    swap.wait_recv()
    total = over_y[own, :].astype(F32) + from_opposite[...].astype(F32)
    attention[...] = total[:, :768]
    gain_part = jnp.sum(total[:, :512] * weights[...].astype(F32), axis=1, keepdims=True)
    lane = lax.broadcasted_iota(jnp.int32, (32, 128), 1)
    share[...] = jnp.where(lane == 33, gain_part, total[:, 768:])
    copies = [
        push(share, shares.at[i], send, recv, base + 13 + i, device)
        for i, device in enumerate((at.sibling(), at.partner(), at.diagonal()))
    ]
    pair.finish(dn1)
    rest[...] = share[...]
    for i, copy in enumerate(copies):
        copy.wait_recv()
        rest[...] += shares[i]
    for copy in (swap, *copies):
        copy.wait_send()
    for scatter in (first_a, first_b, second_a, second_b):
        scatter.sent()


def final(part, grads, weights, ident):
    vmem = pl.BlockSpec(memory_space=pltpu.VMEM)
    width = grads.shape[1]
    sems = 1 + 2 * PIECES + 16
    return pl.pallas_call(
        final_kernel,
        in_specs=[vmem] * 3,
        out_specs=[vmem] * 3,
        out_shape=[
            jax.ShapeDtypeStruct((LOCAL, D), F32),
            jax.ShapeDtypeStruct((32, 768), F32),
            jax.ShapeDtypeStruct((32, 128), F32),
        ],
        scratch_shapes=[
            pltpu.VMEM((3, 4, 64, SPLIT), BF),
            pltpu.VMEM((3, 4, 64, width - SPLIT), BF),
            pltpu.VMEM((4, 64, SPLIT), BF),
            pltpu.VMEM((4, 64, width - SPLIT), BF),
            pltpu.VMEM((3, 64, SPLIT), BF),
            pltpu.VMEM((3, 64, width - SPLIT), BF),
            pltpu.VMEM((64, width), BF),
            pltpu.VMEM((32, width), BF),
            pltpu.VMEM((32, 128), F32),
            pltpu.VMEM((3, 32, 128), F32),
            *pair_scratch(LOCAL, D),
            pltpu.SemaphoreType.DMA((sems,)),
            pltpu.SemaphoreType.DMA((sems,)),
        ],
        compiler_params=pltpu.CompilerParams(
            collective_id=ident, has_side_effects=True, vmem_limit_bytes=32 * MIB
        ),
        name="final",
    )(part.reshape(4, LOCAL, D), grads.reshape(4, 4, 64, width), weights)


def last_kernel(grads, gate, up, down, send, recv, here):
    at = Place()
    greet([at.opposite()])
    half = pl.ds(at.yh * 16, 16)
    kept, copies = [], []
    for i, out in enumerate((gate, up, down)):
        theirs = grads.at[1 - at.yh, i]
        copies.append(push(theirs, out.at[half], send, recv, i, at.opposite()))
        kept.append(keep(grads.at[at.yh, i], out.at[half], here.at[i]))
    for copy in (*copies, *kept):
        copy.wait()


def last_exchange(grads, ident):
    hbm = pl.BlockSpec(memory_space=pl.ANY)
    return pl.pallas_call(
        last_kernel,
        in_specs=[hbm],
        out_specs=[hbm] * 3,
        out_shape=[jax.ShapeDtypeStruct((E, 32, FF), BF)] * 3,
        scratch_shapes=[
            pltpu.SemaphoreType.DMA((3,)),
            pltpu.SemaphoreType.DMA((3,)),
            pltpu.SemaphoreType.DMA((3,)),
        ],
        compiler_params=pltpu.CompilerParams(collective_id=ident, has_side_effects=True),
        name="last_exchange",
    )(grads)


def rotary_tables():
    half = HD // 2
    inverse = (10000.0 ** (-(np.arange(half, dtype=np.float64) * 2.0) / HD)).astype(np.float32)
    angles = np.arange(SEQ, dtype=np.float32)[:, None] * inverse[None, :]
    cosine, sine = np.cos(angles), np.sin(angles)
    wide_cosine = np.concatenate([cosine] * 4, axis=1)
    wide_sine = np.concatenate([-sine, sine] * 2, axis=1)
    return wide_cosine.astype(np.float32), wide_sine.astype(np.float32)


def swapped(values):
    lane = lax.broadcasted_iota(jnp.int32, values.shape, 1)
    low = (lane % HD) < HD // 2
    return jnp.where(low, pltpu.roll(values, 96, 1), pltpu.roll(values, 32, 1))


def rotated(values, cosine, sine):
    return values * cosine + swapped(values) * sine


def bias_block(key_segment, query_segment, first, rows):
    key_at = lax.broadcasted_iota(jnp.int32, (rows, BLOCK), 0)
    query_at = lax.broadcasted_iota(jnp.int32, (rows, BLOCK), 1) + first
    allowed = (key_segment == query_segment) & (key_at <= query_at)
    return jnp.where(allowed, 0.0, MASKED)


def segment_row(segments):
    return jnp.concatenate(
        [segments[rank, i : i + 1, :] for rank in range(4) for i in range(2)], axis=1
    ).astype(F32)


def gain_rows(small):
    return small[:, 768:896].astype(F32).T[32:40, :]


def column_of(row):
    return jnp.broadcast_to(row, (8, row.shape[1])).T[:, 0:1]


def front_kernel(
    hidden, weights, cosine, sine, segments, own_hidden, named, out_grad, over_z, over_x,
    normed, query, key, value, context_t, log_total, middle, normed_moe, gating,
    quad_0a, quad_0b, quad_1a, quad_1b, out_grad_all, bias, part, context, *refs,
):
    pair_refs = refs[:3]
    send, recv, here = refs[3:]
    at = Place()
    greet(
        [
            at.sibling(), at.partner(), at.ring(1), at.ring(3),
            at.along("x", 1), at.along("x", 3), at.along("z", 1), at.along("z", 3),
        ]
    )
    ring = RingGather(at, out_grad, out_grad_all, send, recv, here.at[0], 0)
    quads = [
        second_gather(
            at, i, over_z, over_x, *quad, send, recv, here.at[pl.ds(1 + 2 * i, 2)],
            9 + SpreadOut.COPIES * i,
        )
        for i, quad in enumerate(((quad_0a, quad_0b), (quad_1a, quad_1b)))
    ]
    scatter = PairScatter(at, part, pair_refs, send, recv, 9 + 2 * SpreadOut.COPIES)
    ring.begin()
    quads[0].begin()

    gains = gain_rows(weights)
    seg_row = segment_row(segments)
    seg_column = column_of(seg_row)
    for block in range(SEQ // BLOCK):
        rows = slice(block * BLOCK, (block + 1) * BLOCK)
        values = hidden[rows, :].astype(F32)
        scale = lax.rsqrt(jnp.mean(values * values, axis=-1, keepdims=True) + EPS)
        normed[rows, :] = (values * scale * gains[0:1, :]).astype(BF)
    for half in range(2):
        columns = slice(half * 128, half * 128 + 128)
        pre = mm(normed[...], weights[:, columns])
        query[:, columns] = (rotated(pre, cosine[...], sine[...]) * 0.125).astype(BF)
    key_pre = mm(normed[...], weights[:, 256:384])
    key[...] = rotated(key_pre, cosine[...], sine[...]).astype(BF)
    value_pre = mm(normed[...], weights[:, 384:512])
    value[...] = value_pre.astype(BF)
    value_t = value_pre.T.astype(BF)
    for block in range(SEQ // BLOCK):
        first, end = block * BLOCK, (block + 1) * BLOCK
        bias[:end, :] = bias_block(seg_column[:end, :], seg_row[:, first:end], first, end)
        for head in range(HEADS):
            kv = slice((head // 2) * HD, (head // 2) * HD + HD)
            own = slice(head * HD, head * HD + HD)
            scores = mm_last(key[:end, kv], query[first:end, own]) + bias[:end, :]
            top = jnp.max(scores, axis=0, keepdims=True)
            powers = jnp.exp(scores - top)
            total = jnp.sum(powers, axis=0, keepdims=True)
            share = (powers * (1.0 / total)).astype(BF)
            context_t[own, first:end] = mm(value_t[kv, :end], share).astype(BF)
            log_total[head : head + 1, first:end] = top + jnp.log(total)
        if block == 1:
            quads[0].forward()
            quads[1].begin()
        if block == 2:
            ring.forward_before()
            ring.forward_behind()
    context[...] = context_t[...].T

    def project(slot):
        rows = pl.ds(pl.multiple_of(slot * LOCAL, LOCAL), LOCAL)
        part[slot] = mm_last(context[rows, :], weights[:, 512:768]).astype(BF)

    project(scatter.other + 1 - at.core)
    scatter.begin_far()
    project(scatter.other + at.core)
    project(scatter.own + 1 - at.core)
    scatter.begin_own()
    project(scatter.own + at.core)
    scatter.forward()
    quads[1].forward()
    ring.forward_across()
    scatter.finish(middle)
    values = middle[...] + own_hidden[...].astype(F32)
    middle[...] = values
    scale = lax.rsqrt(jnp.mean(values * values, axis=-1, keepdims=True) + EPS)
    normed_moe[...] = (values * scale * gains[1:2, :]).astype(BF)
    chosen = named[...] > 0.0
    logits = jnp.where(chosen, mm(normed_moe[...], weights[:, 768:896]), MASKED)
    powers = jnp.where(chosen, jnp.exp(logits - jnp.max(logits, axis=-1, keepdims=True)), 0.0)
    gating[...] = powers / jnp.sum(powers, axis=-1, keepdims=True)
    for i in (0, 4, 6, 7, 8):
        ring.copy(i).wait_recv()
    ring.sent()
    ring.kept().wait()
    for quad in quads:
        quad.finish()


def front(hidden, weights, tables, segments, own_hidden, named, out_grad, lines, ident):
    vmem = pl.BlockSpec(memory_space=pltpu.VMEM)
    hbm = pl.BlockSpec(memory_space=pl.ANY)
    sems = 9 + 2 * SpreadOut.COPIES + 1 + 2 * PIECES
    return pl.pallas_call(
        front_kernel,
        in_specs=[vmem] * 7 + [hbm] * 3,
        out_specs=[vmem] * 9 + [hbm] * 5,
        out_shape=[
            jax.ShapeDtypeStruct((SEQ, D), BF),
            jax.ShapeDtypeStruct((SEQ, HEADS * HD), BF),
            jax.ShapeDtypeStruct((SEQ, 128), BF),
            jax.ShapeDtypeStruct((SEQ, 128), BF),
            jax.ShapeDtypeStruct((HEADS * HD, SEQ), BF),
            jax.ShapeDtypeStruct((8, SEQ), F32),
            jax.ShapeDtypeStruct((LOCAL, D), F32),
            jax.ShapeDtypeStruct((LOCAL, D), BF),
            jax.ShapeDtypeStruct((LOCAL, 128), F32),
            *[QUAD_SHAPE] * 4,
            jax.ShapeDtypeStruct((8, LOCAL, D), BF),
        ],
        scratch_shapes=[
            pltpu.VMEM((SEQ, BLOCK), F32),
            pltpu.VMEM((4, LOCAL, D), BF),
            pltpu.VMEM((SEQ, HEADS * HD), BF),
            *pair_scratch(LOCAL, D),
            pltpu.SemaphoreType.DMA((sems,)),
            pltpu.SemaphoreType.DMA((sems,)),
            pltpu.SemaphoreType.DMA((5,)),
        ],
        compiler_params=pltpu.CompilerParams(
            collective_id=ident, has_side_effects=True, vmem_limit_bytes=56 * MIB
        ),
        name="front",
    )(hidden, weights, *tables, segments, own_hidden, named, out_grad, *lines)


def back_kernel(
    dx, dgate, gating, middle, normed_moe, out_grad, y_part,
    normed, weights, cosine, sine, segments, query, key, value, context_t, log_total,
    dmiddle, dn1, grads, block_out,
    bias, dcontext, dquery_t, dkey, dvalue, dall, dall_t, dattn_own, dattn_all, y_sum, *refs,
):
    ring_refs = refs[:8]
    send, recv, here = refs[8:]
    at = Place()
    greet([at.sibling(), at.partner(), at.ring(1), at.ring(3)])
    gain = gain_rows(weights)[1:2, :]
    chosen = gating[...]
    dchosen = chosen * (dgate[...] - jnp.sum(chosen * dgate[...], axis=-1, keepdims=True))
    dlogits = dchosen.astype(BF)
    dnormed = dx[...] + mm_last(dlogits, weights[:, 768:896])
    values = middle[...]
    scale = lax.rsqrt(jnp.mean(values * values, axis=-1, keepdims=True) + EPS)
    unit = values * scale
    weighted = dnormed * gain
    inner = jnp.mean(weighted * unit, axis=-1, keepdims=True)
    total = out_grad[...].astype(F32) + scale * (weighted - unit * inner)
    dmiddle[...] = total
    dattn_own[...] = total.astype(BF)
    gather = PairGather(at, dattn_own, dattn_all, send, recv, here, 8, PIECES)
    scatter = RingScatter(at, y_part, ring_refs, send, recv)
    for k in (2, 1, 3, 0):
        scatter.copy(k).start()
    router_part = mm(normed_moe[...].T, dlogits)
    gain_part = column_of(jnp.sum(dnormed * unit, axis=0, keepdims=True))
    lane = lax.broadcasted_iota(jnp.int32, (D, 128), 1)
    grads[:, 768:] = jnp.where(lane == 32, gain_part, router_part).astype(BF)
    seg_row = segment_row(segments)
    seg_column = column_of(seg_row)
    gather.forward()
    scatter.far()
    gather.finish()
    dattn = dattn_all[...].reshape(SEQ, D)
    dcontext[...] = mm(dattn, weights[:, 512:768]).astype(BF)
    output_grad_t = mm(context_t[...], dattn)
    grads[:, 512:768] = output_grad_t.T.astype(BF)
    key_t = key[...].astype(F32).T.astype(BF)
    dkey[...] = jnp.zeros_like(dkey)
    dvalue[...] = jnp.zeros_like(dvalue)
    for block in range(SEQ // BLOCK):
        first, end = block * BLOCK, (block + 1) * BLOCK
        bias[:end, :] = bias_block(seg_column[:end, :], seg_row[:, first:end], first, end)
        for head in range(HEADS):
            kv = slice((head // 2) * HD, (head // 2) * HD + HD)
            own = slice(head * HD, head * HD + HD)
            query_block = query[first:end, own]
            dcontext_block = dcontext[first:end, own]
            scores = mm_last(key[:end, kv], query_block) + bias[:end, :]
            share = jnp.exp(scores - log_total[head : head + 1, first:end])
            dshare = mm_last(value[:end, kv], dcontext_block)
            centre = jnp.sum(share * dshare, axis=0, keepdims=True)
            dscore = (share * (dshare - centre)).astype(BF)
            dquery_t[own, first:end] = mm(key_t[kv, :end], dscore) * 0.125
            dkey[:end, kv] += mm(dscore, query_block)
            dvalue[:end, kv] += mm(share.astype(BF), dcontext_block)
        if block == 0:
            scatter.up_side()
            scatter.down_side()
    turn = -sine[...]
    for half in range(2):
        rows = slice(half * 128, half * 128 + 128)
        piece = rotated(dquery_t[rows, :].T, cosine[...], turn)
        dall[:, rows] = piece.astype(BF)
        dall_t[rows, :] = piece.T.astype(BF)
    piece = rotated(dkey[...], cosine[...], turn)
    dall[:, 256:384] = piece.astype(BF)
    dall_t[256:384, :] = piece.T.astype(BF)
    dall[:, 384:512] = dvalue[...].astype(BF)
    dall_t[384:512, :] = dvalue[...].T.astype(BF)
    grads[:, 0:512] = mm(dall_t[...], normed[...]).T.astype(BF)
    for block in range(SEQ // BLOCK):
        rows = slice(block * BLOCK, (block + 1) * BLOCK)
        dn1[rows, :] = mm_last(dall[rows, :], weights[:, 0:512]).astype(BF)
    scatter.finish(y_sum)
    block_out[...] = (y_sum[...] + middle[...]).astype(BF)


def back(
    dx, dgate, gating, middle, normed_moe, out_grad, y_part,
    normed, weights, tables, segments, kept, ident,
):
    vmem = pl.BlockSpec(memory_space=pltpu.VMEM)
    sems = 8 + 1 + 2 * PIECES
    return pl.pallas_call(
        back_kernel,
        in_specs=[vmem] * 17,
        out_specs=[vmem] * 4,
        out_shape=[
            jax.ShapeDtypeStruct((LOCAL, D), F32),
            jax.ShapeDtypeStruct((SEQ, D), BF),
            jax.ShapeDtypeStruct((D, SMALL), BF),
            jax.ShapeDtypeStruct((LOCAL, D), BF),
        ],
        scratch_shapes=[
            pltpu.VMEM((SEQ, BLOCK), F32),
            pltpu.VMEM((SEQ, HEADS * HD), BF),
            pltpu.VMEM((HEADS * HD, SEQ), F32),
            pltpu.VMEM((SEQ, 128), F32),
            pltpu.VMEM((SEQ, 128), F32),
            pltpu.VMEM((SEQ, 512), BF),
            pltpu.VMEM((512, SEQ), BF),
            pltpu.VMEM((LOCAL, D), BF),
            pltpu.VMEM((4, LOCAL, D), BF),
            pltpu.VMEM((LOCAL, D), F32),
            *ring_scratch(LOCAL, D),
            pltpu.SemaphoreType.DMA((sems,)),
            pltpu.SemaphoreType.DMA((sems,)),
            pltpu.SemaphoreType.DMA,
        ],
        compiler_params=pltpu.CompilerParams(
            collective_id=ident, has_side_effects=True, vmem_limit_bytes=58 * MIB
        ),
        name="back",
    )(
        dx, dgate, gating, middle, normed_moe, out_grad, y_part,
        normed, weights, *tables, segments, *kept,
    )


def experts_kernel(
    x_in, gate_in, d_in, quad_0a, quad_0b, quad_1a, quad_1b, over_z, over_x,
    y_out, dx_out, dgate_out, grads, quad_2a, quad_2b, quad_3a, quad_3b,
    x, d, xt, dt, y, dx, gating, dgate, dgate_part, hidden, w, *refs,
):
    dx_scratch, dgate_scratch = refs[:5], refs[5:10]
    send, recv, here, load, store, fetch = refs[10:16]
    at = Place()
    step = pl.program_id(0)
    opening, closing = step == 0, step == STEPS - 1
    rows_at_once = 2 * LOCAL
    lane = lax.broadcasted_iota(jnp.int32, (LOCAL, 128), 1)
    own_first = at.yh * 16 + step * QUAD
    x_gather = RingGather(at, x_in, x, send, recv, here.at[0], 0)
    gate_gather = RingGather(at, gate_in, gating, send, recv, here.at[1], 9)
    gathers = (x_gather, gate_gather)
    scatters = (
        RingScatter(at, d, dx_scratch, send, recv, 18),
        RingScatter(at, dgate_part, dgate_scratch, send, recv, 26),
    )

    quads = [
        second_gather(
            at, 2 + i, over_z, over_x, *quad, *refs[16:18], refs[18].at[pl.ds(2 * i, 2)],
            SpreadOut.COPIES * i,
        )
        for i, quad in enumerate(((quad_2a, quad_2b), (quad_3a, quad_3b)))
    ]

    def ride(condition, what):
        for i, quad in enumerate(quads):

            @pl.when(condition & (step == i))
            def _():
                what(quad)

    def fetches(quad_a, quad_b):
        copies = []
        for g in range(3):
            for i in range(QUAD):
                columns = pl.ds((g * QUAD + i) * FF, FF)
                if i < 2:
                    parts = [(quad_a.at[:, :, :, g, i], w.at[:, :, :, :, columns])]
                else:
                    parts = [
                        (quad_b.at[:, x_at, :, g, i - 2], w.at[x_at, :, :, :, columns])
                        for x_at in range(4)
                    ]
                for part in parts:
                    copies.append(pltpu.make_async_copy(*part, fetch.at[len(copies)]))
        return copies

    def d_load(chip):
        two = pl.ds(chip * 2, 2)
        return pltpu.make_async_copy(d_in.at[two], d.at[two], load.at[chip])

    def y_store(chip):
        two = pl.ds(chip * 2, 2)
        return pltpu.make_async_copy(x.at[two], y_out.at[two], store.at[chip])

    @pl.when(opening)
    def _():
        greet(
            [
                at.sibling(), at.ring(1), at.ring(3),
                at.along("x", 1), at.along("x", 3), at.along("z", 1), at.along("z", 3),
            ]
        )
        for gather in gathers:
            gather.begin()
        for copy in fetches(quad_0a, quad_0b):
            copy.start()
        for chip in range(4):
            d_load(chip).start()

    for copy in fetches(quad_0a, quad_0b):
        copy.wait()

    ride(step < STEPS, lambda quad: quad.begin())

    def arrive(turn):
        @pl.when(turn == 0)
        def _():
            for gather in gathers:
                gather.kept().wait()
                gather.copy(0).wait_recv()

        @pl.when(turn == 1)
        def _():
            for gather in gathers:
                gather.forward_before()
                gather.forward_behind()
            for gather in gathers:
                gather.copy(4).wait_recv()

        @pl.when(turn == 2)
        def _():
            for gather in gathers:
                gather.forward_across()
            for gather in gathers:
                gather.copy(6).wait_recv()

        @pl.when(turn == 3)
        def _():
            for gather in gathers:
                gather.copy(7).wait_recv()
                gather.copy(8).wait_recv()

    def leave(turn):
        @pl.when(turn == 0)
        def _():
            for scatter in scatters:
                scatter.copy(2).start()

        @pl.when(turn == 1)
        def _():
            for scatter in scatters:
                scatter.copy(1).start()
                scatter.far()

        @pl.when(turn == 2)
        def _():
            for scatter in scatters:
                scatter.copy(3).start()
                scatter.up_side()

        @pl.when(turn == 3)
        def _():
            for scatter in scatters:
                scatter.copy(0).start()
                scatter.down_side()

    def tokens_block(turn, carry):
        inward = jnp.where(turn == 0, 0, jnp.where(turn == 1, 3, turn - 1))
        outward = jnp.where(turn == 0, 2, jnp.where(turn == 3, 0, turn * 2 - 1))
        chip = at.chip(jnp.where(closing, outward, inward))
        two = pl.ds(chip * 2, 2)
        rows = pl.ds(pl.multiple_of(chip * rows_at_once, rows_at_once), rows_at_once)

        @pl.when(opening)
        def _():
            arrive(turn)
            d_load(chip).wait()
            xt[:, rows] = x[two].reshape(rows_at_once, D).T
            dt[:, rows] = d[two].reshape(rows_at_once, D).T
            y[rows, :] = jnp.zeros((rows_at_once, D), F32)
            dx[rows, :] = jnp.zeros((rows_at_once, D), F32)
            dgate[rows, :] = jnp.zeros((rows_at_once, 128), F32)

        ride(turn == 3, lambda quad: quad.forward())
        gate_up = w[:, :, :, :, 0 : 2 * F].reshape(D, 2 * F)
        down = w[:, :, :, :, 2 * F :].reshape(D, F)
        for core in range(2):
            slot = chip * 2 + core
            part = pl.ds(pl.multiple_of(slot * LOCAL, LOCAL), LOCAL)
            both = mm(x[slot], gate_up)
            gate, up = both[:, :F], both[:, F:]
            dact = mm(d[slot], down)
            turned = pltpu.roll(gating[slot], lax.rem(128 - own_first, 128), 1)
            factor = jnp.concatenate(
                [jnp.broadcast_to(turned[:, i : i + 1], (LOCAL, FF)) for i in range(QUAD)],
                axis=1,
            )
            q = 1.0 / (1.0 + jnp.exp(-gate))
            silu = gate * q
            act = silu * up
            product = act * dact
            sums = dgate[part, :]
            for i in range(QUAD):
                own = jnp.sum(product[:, i * FF : (i + 1) * FF], axis=1, keepdims=True)
                sums = jnp.where(lane == own_first + i, own, sums)
            dgate[part, :] = sums
            dact = dact * factor
            hidden[part, 0:F] = (dact * up * (q + silu * (1.0 - q))).astype(BF)
            hidden[part, F : 2 * F] = (dact * silu).astype(BF)
            hidden[part, 2 * F :] = (act * factor).astype(BF)
        y[rows, :] += mm_last(hidden[rows, 2 * F :], down)
        dx[rows, :] += mm_last(hidden[rows, 0 : 2 * F], gate_up)

        @pl.when(closing)
        def _():
            x[two] = y[rows, :].astype(BF).reshape(2, LOCAL, D)
            d[two] = dx[rows, :].astype(BF).reshape(2, LOCAL, D)
            dgate_part[two] = dgate[rows, :].astype(BF).reshape(2, LOCAL, 128)
            y_store(chip).start()
            leave(turn)

        return carry

    lax.fori_loop(0, 4, tokens_block, 0)

    later = ((quad_1a, quad_1b), (quad_2a, quad_2b), (quad_3a, quad_3b))
    for number, quad in enumerate(later):

        @pl.when(step == number)
        def _():
            for copy in fetches(*quad):
                copy.start()

    @pl.when(opening)
    def _():
        for gather in gathers:
            gather.sent()

    def grads_block(block, carry):
        rows = pl.ds(pl.multiple_of(block * 512, 512), 512)
        into = pl.ds(pl.multiple_of(block * 256, 256), 256)

        def put(g, value):
            value = value.astype(BF).reshape(8, 2, 32, value.shape[1])
            for h in range(2):
                half = value[:, h].reshape(256, value.shape[-1])
                for i in range(half.shape[1] // FF):
                    columns = slice(i * FF, (i + 1) * FF)
                    grads[h, g + i // QUAD, i % QUAD, into, :] = half[:, columns]

        put(0, mm(xt[rows, :], hidden[:, 0 : 2 * F]))
        put(2, mm(dt[rows, :], hidden[:, 2 * F :]))
        return carry

    lax.fori_loop(0, D // 512, grads_block, 0)
    ride(step < STEPS, lambda quad: quad.finish())

    @pl.when(closing)
    def _():
        scatters[0].finish(dx_out)
        scatters[1].finish(dgate_out)
        for chip in range(4):
            y_store(chip).wait()


def experts(x, gating, d, quads, lines, ident):
    hbm = pl.BlockSpec(memory_space=pl.ANY)

    def whole(rows, columns):
        return pl.BlockSpec((rows, columns), lambda step: (0, 0), pipeline_mode=pl.Buffered(1))

    return pl.pallas_call(
        experts_kernel,
        grid=(STEPS,),
        in_specs=[hbm] * 9,
        out_specs=[
            hbm,
            whole(LOCAL, D),
            whole(LOCAL, 128),
            pl.BlockSpec(
                (2, 3, QUAD, D // 2, FF), lambda step: (0, 0, step, 0, 0),
                pipeline_mode=pl.Buffered(1),
            ),
            *[hbm] * 4,
        ],
        out_shape=[
            jax.ShapeDtypeStruct((8, LOCAL, D), BF),
            jax.ShapeDtypeStruct((LOCAL, D), F32),
            jax.ShapeDtypeStruct((LOCAL, 128), F32),
            jax.ShapeDtypeStruct((2, 3, STEPS * QUAD, D // 2, FF), BF),
            *[QUAD_SHAPE] * 4,
        ],
        scratch_shapes=[
            pltpu.VMEM((8, LOCAL, D), BF),
            pltpu.VMEM((8, LOCAL, D), BF),
            pltpu.VMEM((D, TOKENS), BF),
            pltpu.VMEM((D, TOKENS), BF),
            pltpu.VMEM((TOKENS, D), F32),
            pltpu.VMEM((TOKENS, D), F32),
            pltpu.VMEM((8, LOCAL, 128), F32),
            pltpu.VMEM((TOKENS, 128), F32),
            pltpu.VMEM((8, LOCAL, 128), BF),
            pltpu.VMEM((TOKENS, 3 * F), BF),
            pltpu.VMEM((4, 4, 2, 32, 3 * F), BF),
            *ring_scratch(LOCAL, D, False),
            *ring_scratch(LOCAL, 128, False),
            pltpu.SemaphoreType.DMA((34,)),
            pltpu.SemaphoreType.DMA((34,)),
            pltpu.SemaphoreType.DMA((2,)),
            pltpu.SemaphoreType.DMA((4,)),
            pltpu.SemaphoreType.DMA((4,)),
            pltpu.SemaphoreType.DMA((30,)),
            pltpu.SemaphoreType.DMA((2 * SpreadOut.COPIES,)),
            pltpu.SemaphoreType.DMA((2 * SpreadOut.COPIES,)),
            pltpu.SemaphoreType.DMA((4,)),
        ],
        compiler_params=pltpu.CompilerParams(
            collective_id=ident, has_side_effects=True, vmem_limit_bytes=63 * MIB
        ),
        name="experts",
    )(x, gating, d, *quads, *lines)[:4]


def norm_scale(values):
    return lax.rsqrt(jnp.mean(values * values, axis=-1, keepdims=True) + EPS)


def norm_grad(values, gain, dnormed):
    scale = norm_scale(values)
    unit = values * scale
    weighted = dnormed * gain
    dvalues = scale * (weighted - unit * jnp.mean(weighted * unit, axis=-1, keepdims=True))
    return dvalues


def on_device(
    hidden_in, out_grad, attn_gain, query_weight, key_weight, value_weight, output_weight,
    moe_gain, router_weight, expert_gate, expert_up, expert_down, expert_ids, segment_ids,
):
    small = jnp.concatenate(
        [
            query_weight, key_weight, value_weight, output_weight,
            router_weight, attn_gain[:, None], moe_gain[:, None], jnp.zeros((32, 94), BF),
        ],
        axis=1,
    )
    segment = jnp.pad(segment_ids.reshape(2, 128), ((0, 6), (0, 0)))
    own_shares = (expert_gate, expert_up, expert_down)
    hidden_all, segments, small, *lines = startup(hidden_in, segment, small, own_shares, 0)
    tables = tuple(jnp.asarray(t) for t in rotary_tables())
    named = jnp.any(
        expert_ids[:, :, None] == jnp.arange(128, dtype=jnp.int32)[None, None, :], axis=1
    ).astype(F32)

    normed, *more, d = front(
        hidden_all, small, tables, segments, hidden_in, named, out_grad, lines, 1
    )
    kept, (middle, normed_moe, gating), quads = more[:5], more[5:8], more[8:]
    y, dx, dgate, expert_grads = experts(normed_moe, gating, d, quads, lines, 3)
    expert_grads = lax.psum_scatter(expert_grads, PLANE, scatter_dimension=3, tiled=True)
    dmiddle, dn1, grads, block_out = back(
        dx, dgate, gating, middle, normed_moe, out_grad, y,
        normed, small, tables, segments, kept, 5,
    )
    weights = jnp.concatenate([query_weight, key_weight, value_weight], axis=1)
    dn1, attention_grads, rest = final(dn1, grads, weights, 6)
    hidden = hidden_in.astype(F32)
    dhidden = norm_grad(hidden, small[:, 800].astype(F32), dn1)
    hidden_grad = dmiddle + dhidden
    expert_grads = [share.astype(F32) for share in last_exchange(expert_grads, 7)]
    return (
        block_out,
        hidden_grad,
        rest[:, 33] / attn_gain.astype(F32),
        attention_grads[:, 0:256],
        attention_grads[:, 256:384],
        attention_grads[:, 384:512],
        attention_grads[:, 512:768],
        rest[:, 32],
        rest[:, :32],
        *expert_grads,
    )


def solution(mesh):
    fine = Mesh(np.asarray(mesh.devices).reshape(4, 4, 2, 2, 2), ALL)
    return jax.shard_map(
        on_device,
        mesh=fine,
        in_specs=(
            P(ALL, None),
            P(ALL, None),
            P(DP),
            P(DP, TENSOR),
            P(DP, TENSOR),
            P(DP, TENSOR),
            P(DP, TENSOR),
            P(DP),
            P(DP, None),
            P(None, DP, TENSOR),
            P(None, DP, TENSOR),
            P(None, DP, TENSOR),
            P(ALL, None),
            P(ALL),
        ),
        out_specs=(
            P(ALL, None),
            P(ALL, None),
            P(DP),
            P(DP, TENSOR),
            P(DP, TENSOR),
            P(DP, TENSOR),
            P(DP, TENSOR),
            P(DP),
            P(DP, None),
            P(None, DP, TENSOR),
            P(None, DP, TENSOR),
            P(None, DP, TENSOR),
        ),
        check_vma=False,
    )
```

```python
import jax
import jax.numpy as jnp
import numpy as np
from jax import lax
from jax.experimental import pallas as pl
from jax.experimental.pallas import tpu as pltpu
from jax.sharding import Mesh
from jax.sharding import PartitionSpec as P

D = 1024
HD = 64
E = 32
SEQ = 1024
LOCAL = 256
HEADS = 4
QUAD = 4
FF = 128
F = QUAD * FF
EPS = 1e-06
MASKED = -1e30
BLOCK = 256
TOKENS = 2048
STEPS = 4

DP = ("x", "z", "yh")
TENSOR = ("yl", "core")
RING = ("yh", "yl", "core")
PLANE = ("x", "z")
ALL = ("x", "z", "yh", "yl", "core")

F32 = jnp.float32
BF = jnp.bfloat16
LAST = (((1,), (1,)), ((), ()))
MIB = 1024 * 1024
MESH = pl.DeviceIdType.MESH
SMALL = 896


def mm(a, b):
    return jnp.dot(a, b, preferred_element_type=F32)


def mm_last(a, b):
    return lax.dot_general(a, b, LAST, preferred_element_type=F32)


class Place:
    def __init__(self):
        self.x = lax.axis_index("x")
        self.z = lax.axis_index("z")
        self.yh = lax.axis_index("yh")
        self.yl = lax.axis_index("yl")
        self.core = lax.axis_index("core")
        self.y = self.yh * 2 + self.yl

    def chip(self, k):
        return lax.rem(self.y + k, 4)

    def ring(self, k):
        chip = self.chip(k)
        return {"yh": chip // 2, "yl": lax.rem(chip, 2)}

    def along(self, axis, k):
        return {axis: lax.rem(getattr(self, axis) + k, 4)}

    def sibling(self):
        return {"core": 1 - self.core}

    def partner(self):
        return {"yl": 1 - self.yl}

    def diagonal(self):
        return {"yl": 1 - self.yl, "core": 1 - self.core}

    def opposite(self):
        return {"yh": 1 - self.yh}


def greet(devices):
    barrier = pltpu.get_barrier_semaphore()
    for device in devices:
        pl.semaphore_signal(barrier, inc=1, device_id=device, device_id_type=MESH)
    pl.semaphore_wait(barrier, len(devices))


def remote(src, dst, send, recv, i, device):
    return pltpu.make_async_remote_copy(
        src_ref=src, dst_ref=dst, send_sem=send.at[i], recv_sem=recv.at[i],
        device_id=device, device_id_type=MESH,
    )


def push(src, dst, send, recv, i, device):
    copy = remote(src, dst, send, recv, i, device)
    copy.start()
    return copy


def keep(src, dst, sem):
    copy = pltpu.make_async_copy(src, dst, sem)
    copy.start()
    return copy


class RingGather:
    def __init__(self, at, own, out, send, recv, here, base=0):
        self.at, self.own, self.out, self.base = at, own, out, base
        self.send, self.recv, self.here = send, recv, here
        half = own.shape[0] // 2
        lo, hi = pl.ds(0, half), pl.ds(half, half)
        me, before, behind, across = (out.at[self.slot(k)] for k in (0, 3, 1, 2))
        near, up, down = at.sibling(), at.ring(1), at.ring(3)
        self.plan = [
            (own, me, near),
            (own, me, up),
            (own, me, down),
            (before.at[lo], before.at[lo], up),
            (before, before, near),
            (behind.at[hi], behind.at[hi], down),
            (behind, behind, near),
            (across.at[lo], across.at[lo], near),
            (across.at[hi], across.at[hi], near),
        ]

    def slot(self, k):
        return self.at.chip(k) * 2 + self.at.core

    def copy(self, i):
        src, dst, device = self.plan[i]
        return remote(src, dst, self.send, self.recv, self.base + i, device)

    def kept(self):
        return pltpu.make_async_copy(self.own, self.out.at[self.slot(0)], self.here)

    def begin(self):
        self.kept().start()
        for i in (1, 2, 0):
            self.copy(i).start()

    def forward_before(self):
        self.copy(1).wait_recv()
        self.copy(3).start()
        self.copy(4).start()

    def forward_behind(self):
        self.copy(2).wait_recv()
        self.copy(5).start()
        self.copy(6).start()

    def forward_across(self):
        self.copy(3).wait_recv()
        self.copy(7).start()
        self.copy(5).wait_recv()
        self.copy(8).start()

    def sent(self):
        for i in range(9):
            self.copy(i).wait_send()


class PairGather:
    def __init__(self, at, own, out, send, recv, here, base, pieces):
        self.at, self.out, self.send, self.recv, self.base = at, out, send, recv, base
        size = own.shape[0] // pieces
        self.parts = [pl.ds(i * size, size) for i in range(pieces)]
        me = at.yl * 2 + at.core
        self.other = (1 - at.yl) * 2 + at.core
        self.kept = keep(own, out.at[me], here)
        self.far = [
            push(own.at[part], out.at[me, part], send, recv, base + 1 + i, at.partner())
            for i, part in enumerate(self.parts)
        ]
        self.near = [push(own, out.at[me], send, recv, base, at.sibling())]

    def forward(self):
        for i, part in enumerate(self.parts):
            self.far[i].wait_recv()
            view = self.out.at[self.other, part]
            index = self.base + 1 + len(self.parts) + i
            self.near.append(push(view, view, self.send, self.recv, index, self.at.sibling()))

    def finish(self):
        for copy in self.near:
            copy.wait_recv()
        for copy in (*self.far, *self.near):
            copy.wait_send()
        self.kept.wait()


PIECES = 4


class AxisGather:
    def __init__(self, at, axis, view, send, recv, base):
        self.up, self.down = at.along(axis, 1), at.along(axis, 3)
        self.view, self.send, self.recv, self.base = view, send, recv, base

    def go(self, i, view, device):
        return push(view, view, self.send, self.recv, self.base + i, device)

    def begin(self):
        self.first = [
            self.go(0, self.view(0, "all"), self.up), self.go(1, self.view(0, "all"), self.down),
        ]

    def forward(self):
        self.first[0].wait_recv()
        self.far = [self.go(2, self.view(3, "low"), self.up)]
        self.first[1].wait_recv()
        self.far.append(self.go(3, self.view(1, "high"), self.down))

    def finish(self):
        for copy in self.far:
            copy.wait_recv()
        for copy in (*self.first, *self.far):
            copy.wait_send()


def halves_of(ref, first, size):
    spans = {"all": (0, size), "low": (0, size // 2), "high": (size // 2, size // 2)}
    return lambda part: ref.at[pl.ds(first + spans[part][0], spans[part][1])]


class SpreadOut:
    COPIES = 8

    def __init__(self, at, rings, send, recv, here, base=0, through=None):
        self.send, self.recv, self.here, self.base = send, recv, here, base
        self.through = through
        self.own = [(own, slot(0)) for _, own, slot, _ in rings]
        self.plan = []
        for axis, own, slot, _ in rings:
            self.plan.append((own, slot(0), at.along(axis, 1)))
            self.plan.append((own, slot(0), at.along(axis, 3)))
        for axis, _, slot, half in rings:
            low, high = (slot(3).at[pl.ds(0, half)], slot(1).at[pl.ds(half, half)])
            self.plan.append((low, low, at.along(axis, 1)))
            self.plan.append((high, high, at.along(axis, 3)))

    def copy(self, i):
        src, dst, device = self.plan[i]
        return remote(src, dst, self.send, self.recv, self.base + i, device)

    def loaded(self, i):
        return pltpu.make_async_copy(self.own[i][0], self.through.at[i], self.here.at[i])

    def kept(self, i):
        src, dst = self.own[i]
        src = src if self.through is None else self.through.at[i]
        return pltpu.make_async_copy(src, dst, self.here.at[2 + i])

    def begin(self):
        for i in range(4):
            self.copy(i).start()
        for i in range(2):
            (self.kept(i) if self.through is None else self.loaded(i)).start()

    def forward(self):
        for i in range(4):
            self.copy(i).wait_recv()
            self.copy(4 + i).start()
        if self.through is not None:
            for i in range(2):
                self.loaded(i).wait()
                self.kept(i).start()

    def finish(self):
        for i in range(4, 8):
            self.copy(i).wait_recv()
        for i in range(8):
            self.copy(i).wait_send()
        for i in range(2):
            self.kept(i).wait()


def ring_slots(out, place):
    return lambda k: out.at[lax.rem(place + k, 4)]


def first_gather(at, own_a, own_b, over_z, over_x, *sems):
    rings = (
        ("z", own_a, ring_slots(over_z, at.z), 1), ("x", own_b, ring_slots(over_x, at.x), 1),
    )
    return SpreadOut(at, rings, *sems)


def second_gather(at, number, over_z, over_x, quad_a, quad_b, *sems):
    rings = (
        ("x", over_z.at[:, :, number], ring_slots(quad_a, at.x), 2),
        ("z", over_x.at[:, :, number], ring_slots(quad_b, at.z), 2),
    )
    return SpreadOut(at, rings, *sems)


SHARE_SHAPE = (2, STEPS, 3, 2, 32, FF)
BLOCK_SHAPE = (4, 2, 3, 2, 32, FF)
LINE_SHAPE = jax.ShapeDtypeStruct((4, 2, STEPS, 3, 2, 32, FF), BF)
QUAD_SHAPE = jax.ShapeDtypeStruct((4, 4, 2, 3, 2, 32, FF), BF)


def startup_kernel(
    hidden, segment, small, gate, up, down,
    hidden_all, segment_all, small_all, over_z_line, over_x_line,
    share_a, share_b, send, recv, here,
):
    at = Place()
    greet(
        [
            at.sibling(), at.partner(), at.diagonal(), at.opposite(),
            at.along("x", 1), at.along("x", 3), at.along("z", 1), at.along("z", 3),
        ]
    )
    rank = at.yl * 2 + at.core
    mine = small_all.at[(at.x * 4 + at.z) * 2 + at.yh]
    small_kept = keep(small, mine, here.at[0])
    copies = [push(small, mine, send, recv, 0, at.opposite())]
    swaps, swaps_kept = [], []
    base = 13 + 2 * PIECES
    for i, share in enumerate((gate, up, down)):
        for j, out in enumerate((share_a, share_b)):
            dst, two = out.at[at.yh, :, i], pl.ds(2 * j, 2)
            theirs = share.at[pl.ds((1 - at.yh) * STEPS, STEPS), two]
            index = 2 * i + j
            swaps.append(push(theirs, dst, send, recv, base + index, at.opposite()))
            own = share.at[pl.ds(at.yh * STEPS, STEPS), two]
            swaps_kept.append(keep(own, dst, here.at[3 + index]))
    experts = first_gather(
        at, share_a, share_b, over_z_line, over_x_line, send, recv, here.at[pl.ds(9, 4)], base + 6
    )
    copies.extend(
        push(segment, segment_all.at[rank], send, recv, 1 + i, device)
        for i, device in enumerate((at.sibling(), at.partner(), at.diagonal()))
    )
    pair = PairGather(at, hidden, hidden_all, send, recv, here.at[1], 12, PIECES)
    seg_here = keep(segment, segment_all.at[rank], here.at[2])
    over_z = AxisGather(
        at, "z",
        lambda k, part: halves_of(small_all, (at.x * 4 + lax.rem(at.z + k, 4)) * 2, 2)(part),
        send, recv, 4,
    )
    over_x = AxisGather(
        at, "x", lambda k, part: halves_of(small_all, lax.rem(at.x + k, 4) * 8, 8)(part),
        send, recv, 8,
    )
    small_kept.wait()
    copies[0].wait_recv()
    over_z.begin()
    over_z.forward()
    over_z.finish()
    over_x.begin()
    pair.forward()
    for swap, own in zip(swaps, swaps_kept):
        swap.wait_recv()
        own.wait()
    experts.begin()
    over_x.forward()
    experts.forward()
    pair.finish()
    seg_here.wait()
    for copy in copies[1:]:
        copy.wait_recv()
    over_x.finish()
    experts.finish()
    for copy in (*copies, *swaps):
        copy.wait_send()


def startup(hidden, segment, small, shares, ident):
    hbm = pl.BlockSpec(memory_space=pl.ANY)
    sems = 13 + 2 * PIECES + 6 + SpreadOut.COPIES
    shares = [share.reshape(2 * STEPS, QUAD, 32, FF) for share in shares]
    vmem = pl.BlockSpec(memory_space=pltpu.VMEM)
    hidden_all, segment_all, small_all, over_z, over_x = pl.pallas_call(
        startup_kernel,
        in_specs=[vmem] * 3 + [hbm] * 3,
        out_specs=[hbm] * 5,
        out_shape=[
            jax.ShapeDtypeStruct((4, *hidden.shape), hidden.dtype),
            jax.ShapeDtypeStruct((4, *segment.shape), segment.dtype),
            jax.ShapeDtypeStruct((32, 32, SMALL), small.dtype),
            LINE_SHAPE,
            LINE_SHAPE,
        ],
        scratch_shapes=[
            pltpu.VMEM(SHARE_SHAPE, BF),
            pltpu.VMEM(SHARE_SHAPE, BF),
            pltpu.SemaphoreType.DMA((sems,)),
            pltpu.SemaphoreType.DMA((sems,)),
            pltpu.SemaphoreType.DMA((13,)),
        ],
        compiler_params=pltpu.CompilerParams(collective_id=ident, has_side_effects=True),
        name="startup",
    )(hidden, segment, small, *shares)
    hidden_all, small_all = hidden_all.reshape(SEQ, D), small_all.reshape(D, SMALL)
    return hidden_all, segment_all, small_all, over_z, over_x


class RingScatter:
    def __init__(self, at, part, scratch, send, recv, base=0):
        self.at, self.part, self.send, self.recv, self.base = at, part, send, recv, base
        near, half_a, half_b, self.full_up, self.full_down = scratch[:5]
        to_far, to_up, to_down = scratch[5:] or [
            part.at[at.chip(k) * 2 + at.core] for k in (2, 1, 3)
        ]
        self.near, self.half_a, self.half_b = near, half_a, half_b
        self.to_far, self.to_up, self.to_down = to_far, to_up, to_down
        self.half = half_a.shape[0]
        self.lo, self.hi = pl.ds(0, self.half), pl.ds(self.half, self.half)
        up, down = at.ring(1), at.ring(3)
        self.plan = {
            k: (part.at[at.chip(k) * 2 + 1 - at.core], near.at[k], at.sibling()) for k in range(4)
        }
        self.plan[4] = (to_far.at[self.lo], half_a, up)
        self.plan[5] = (to_far.at[self.hi], half_b, down)
        self.plan[6] = (to_up, self.full_up, up)
        self.plan[7] = (to_down, self.full_down, down)

    def copy(self, i):
        src, dst, device = self.plan[i]
        return remote(src, dst, self.send, self.recv, self.base + i, device)

    def chip_sum(self, k):
        self.copy(k).wait_recv()
        own = self.part[self.at.chip(k) * 2 + self.at.core]
        return own.astype(F32) + self.near[k].astype(F32)

    def far(self):
        self.to_far[...] = self.chip_sum(2).astype(BF)
        self.copy(4).start()
        self.copy(5).start()

    def up_side(self):
        total = self.chip_sum(1)
        self.copy(4).wait_recv()
        self.to_up[self.lo, :] = (total[: self.half] + self.half_a[...].astype(F32)).astype(BF)
        self.to_up[self.hi, :] = total[self.half :].astype(BF)
        self.copy(6).start()

    def down_side(self):
        total = self.chip_sum(3)
        self.copy(5).wait_recv()
        self.to_down[self.lo, :] = total[: self.half].astype(BF)
        self.to_down[self.hi, :] = (total[self.half :] + self.half_b[...].astype(F32)).astype(BF)
        self.copy(7).start()

    def finish(self, out):
        out[...] = self.chip_sum(0)
        self.copy(6).wait_recv()
        out[...] += self.full_up[...].astype(F32)
        self.copy(7).wait_recv()
        out[...] += self.full_down[...].astype(F32)
        for i in range(8):
            self.copy(i).wait_send()


def ring_scratch(rows, columns, own_sends=True):
    block, half = pltpu.VMEM((rows, columns), BF), pltpu.VMEM((rows // 2, columns), BF)
    scratch = [pltpu.VMEM((4, rows, columns), BF), half, half, block, block]
    return scratch + [block] * 3 if own_sends else scratch


class PairScatter:
    def __init__(self, at, part, scratch, send, recv, base=0):
        self.at, self.part, self.send, self.recv, self.base = at, part, send, recv, base
        self.near, self.far_rows, self.to_far = scratch
        size = self.to_far.shape[0] // PIECES
        self.parts = [pl.ds(i * size, size) for i in range(PIECES)]
        self.other, self.own = (1 - at.yl) * 2, at.yl * 2

    def go(self, i, src, dst, device):
        return push(src, dst, self.send, self.recv, self.base + i, device)

    def begin_far(self):
        slot = self.other + 1 - self.at.core
        self.first = [
            self.go(i, self.part.at[slot, rows], self.near.at[1, rows], self.at.sibling())
            for i, rows in enumerate(self.parts)
        ]

    def begin_own(self):
        slot = self.own + 1 - self.at.core
        self.second = self.go(PIECES, self.part.at[slot], self.near.at[0], self.at.sibling())

    def forward(self):
        self.sent = []
        for i, rows in enumerate(self.parts):
            self.first[i].wait_recv()
            own = self.part[self.other + self.at.core, rows, :].astype(F32)
            self.to_far[rows, :] = (own + self.near[1, rows, :].astype(F32)).astype(BF)
            far = self.far_rows.at[rows]
            self.sent.append(self.go(PIECES + 1 + i, self.to_far.at[rows], far, self.at.partner()))

    def finish(self, out):
        self.second.wait_recv()
        out[...] = self.part[self.own + self.at.core].astype(F32) + self.near[0].astype(F32)
        for i, rows in enumerate(self.parts):
            self.sent[i].wait_recv()
            out[rows, :] += self.far_rows[rows, :].astype(F32)
        for copy in (*self.first, self.second, *self.sent):
            copy.wait_send()


def pair_scratch(rows, columns):
    block = pltpu.VMEM((rows, columns), BF)
    return [pltpu.VMEM((2, rows, columns), BF), block, block]


class DirectScatter:
    def __init__(self, at, axis, blocks, landed, send, recv, base):
        self.blocks, self.landed = blocks, landed
        self.copies = [
            push(blocks(k), landed.at[k - 1], send, recv, base + k - 1, at.along(axis, k))
            for k in (2, 1, 3)
        ]

    def total(self):
        value = self.blocks(0)[...].astype(F32)
        for copy, k in zip(self.copies, (2, 1, 3)):
            copy.wait_recv()
            value = value + self.landed[k - 1].astype(F32)
        return value

    def sent(self):
        for copy in self.copies:
            copy.wait_send()


SPLIT = 384


def final_kernel(
    part, grads, weights, dn1, attention, rest,
    a_1, b_1, a_half, b_half, a_2, b_2, over_y, from_opposite, share, shares, *refs,
):
    at = Place()
    greet(
        [
            at.sibling(), at.partner(), at.diagonal(), at.opposite(),
            *[at.along(axis, k) for axis in ("x", "z") for k in (1, 2, 3)],
        ]
    )
    pair_refs = refs[:3]
    send, recv = refs[3:]
    base = 1 + 2 * PIECES
    width = grads.shape[-1]
    a, b = pl.ds(0, SPLIT), pl.ds(SPLIT, width - SPLIT)

    def x_of(k):
        return lax.rem(at.x + k, 4)

    def z_of(k):
        return lax.rem(at.z + k, 4)

    first_a = DirectScatter(
        at, "x", lambda k: grads.at[x_of(k), :, :, a], a_1, send, recv, base
    )
    first_b = DirectScatter(
        at, "z", lambda k: grads.at[:, z_of(k), :, b], b_1, send, recv, base + 3
    )
    pair = PairScatter(at, part, pair_refs, send, recv)
    pair.begin_far()
    pair.begin_own()
    pair.forward()
    a_half[...] = first_a.total().astype(BF)
    second_a = DirectScatter(
        at, "z", lambda k: a_half.at[z_of(k)], a_2, send, recv, base + 6
    )
    b_half[...] = first_b.total().astype(BF)
    second_b = DirectScatter(
        at, "x", lambda k: b_half.at[x_of(k)], b_2, send, recv, base + 9
    )
    over_y[:, a] = second_a.total().astype(BF)
    over_y[:, b] = second_b.total().astype(BF)
    theirs = pl.ds(pl.multiple_of((1 - at.yh) * 32, 32), 32)
    own = pl.ds(pl.multiple_of(at.yh * 32, 32), 32)
    swap = push(over_y.at[theirs], from_opposite, send, recv, base + 12, at.opposite())
    swap.wait_recv()
    total = over_y[own, :].astype(F32) + from_opposite[...].astype(F32)
    attention[...] = total[:, :768]
    gain_part = jnp.sum(total[:, :512] * weights[...].astype(F32), axis=1, keepdims=True)
    lane = lax.broadcasted_iota(jnp.int32, (32, 128), 1)
    share[...] = jnp.where(lane == 33, gain_part, total[:, 768:])
    copies = [
        push(share, shares.at[i], send, recv, base + 13 + i, device)
        for i, device in enumerate((at.sibling(), at.partner(), at.diagonal()))
    ]
    pair.finish(dn1)
    rest[...] = share[...]
    for i, copy in enumerate(copies):
        copy.wait_recv()
        rest[...] += shares[i]
    for copy in (swap, *copies):
        copy.wait_send()
    for scatter in (first_a, first_b, second_a, second_b):
        scatter.sent()


def final(part, grads, weights, ident):
    vmem = pl.BlockSpec(memory_space=pltpu.VMEM)
    width = grads.shape[1]
    sems = 1 + 2 * PIECES + 16
    return pl.pallas_call(
        final_kernel,
        in_specs=[vmem] * 3,
        out_specs=[vmem] * 3,
        out_shape=[
            jax.ShapeDtypeStruct((LOCAL, D), F32),
            jax.ShapeDtypeStruct((32, 768), F32),
            jax.ShapeDtypeStruct((32, 128), F32),
        ],
        scratch_shapes=[
            pltpu.VMEM((3, 4, 64, SPLIT), BF),
            pltpu.VMEM((3, 4, 64, width - SPLIT), BF),
            pltpu.VMEM((4, 64, SPLIT), BF),
            pltpu.VMEM((4, 64, width - SPLIT), BF),
            pltpu.VMEM((3, 64, SPLIT), BF),
            pltpu.VMEM((3, 64, width - SPLIT), BF),
            pltpu.VMEM((64, width), BF),
            pltpu.VMEM((32, width), BF),
            pltpu.VMEM((32, 128), F32),
            pltpu.VMEM((3, 32, 128), F32),
            *pair_scratch(LOCAL, D),
            pltpu.SemaphoreType.DMA((sems,)),
            pltpu.SemaphoreType.DMA((sems,)),
        ],
        compiler_params=pltpu.CompilerParams(
            collective_id=ident, has_side_effects=True, vmem_limit_bytes=32 * MIB
        ),
        name="final",
    )(part.reshape(4, LOCAL, D), grads.reshape(4, 4, 64, width), weights)


def last_kernel(grads, gate, up, down, landed, send, recv):
    at = Place()
    greet([at.opposite()])
    copies = [
        push(grads.at[1 - at.yh, i], landed.at[i], send, recv, i, at.opposite()) for i in range(3)
    ]
    own, theirs = pl.ds(at.yh * 16, 16), pl.ds((1 - at.yh) * 16, 16)
    for i, out in enumerate((gate, up, down)):
        out[own] = grads[at.yh, i].astype(F32)
    for i, out in enumerate((gate, up, down)):
        copies[i].wait()
        out[theirs] = landed[i].astype(F32)


def last_exchange(grads, ident):
    vmem = pl.BlockSpec(memory_space=pltpu.VMEM)
    return pl.pallas_call(
        last_kernel,
        in_specs=[vmem],
        out_specs=[vmem] * 3,
        out_shape=[jax.ShapeDtypeStruct((E, 32, FF), F32)] * 3,
        scratch_shapes=[
            pltpu.VMEM((3, 16, 32, FF), BF),
            pltpu.SemaphoreType.DMA((3,)),
            pltpu.SemaphoreType.DMA((3,)),
        ],
        compiler_params=pltpu.CompilerParams(
            collective_id=ident, has_side_effects=True, vmem_limit_bytes=32 * MIB
        ),
        name="last_exchange",
    )(grads)


def rotary_tables():
    half = HD // 2
    inverse = (10000.0 ** (-(np.arange(half, dtype=np.float64) * 2.0) / HD)).astype(np.float32)
    angles = np.arange(SEQ, dtype=np.float32)[:, None] * inverse[None, :]
    cosine, sine = np.cos(angles), np.sin(angles)
    wide_cosine = np.concatenate([cosine] * 4, axis=1)
    wide_sine = np.concatenate([-sine, sine] * 2, axis=1)
    return wide_cosine.astype(np.float32), wide_sine.astype(np.float32)


def swapped(values):
    lane = lax.broadcasted_iota(jnp.int32, values.shape, 1)
    low = (lane % HD) < HD // 2
    return jnp.where(low, pltpu.roll(values, 96, 1), pltpu.roll(values, 32, 1))


def rotated(values, cosine, sine):
    return values * cosine + swapped(values) * sine


def bias_block(key_segment, query_segment, first, rows):
    key_at = lax.broadcasted_iota(jnp.int32, (rows, BLOCK), 0)
    query_at = lax.broadcasted_iota(jnp.int32, (rows, BLOCK), 1) + first
    allowed = (key_segment == query_segment) & (key_at <= query_at)
    return jnp.where(allowed, 0.0, MASKED)


def segment_row(segments):
    return jnp.concatenate(
        [segments[rank, i : i + 1, :] for rank in range(4) for i in range(2)], axis=1
    ).astype(F32)


def gain_rows(small):
    return small[:, 768:896].astype(F32).T[32:40, :]


def column_of(row):
    return jnp.broadcast_to(row, (8, row.shape[1])).T[:, 0:1]


def front_kernel(
    hidden, weights, cosine, sine, segments, own_hidden, named, out_grad, over_z, over_x,
    normed, query, key, value, context_t, log_total, middle, normed_moe, gating,
    quad_0a, quad_0b, quad_1a, quad_1b, out_grad_all, bias, part, context, through, *refs,
):
    pair_refs = refs[:3]
    send, recv, here = refs[3:]
    at = Place()
    greet(
        [
            at.sibling(), at.partner(), at.ring(1), at.ring(3),
            at.along("x", 1), at.along("x", 3), at.along("z", 1), at.along("z", 3),
        ]
    )
    ring = RingGather(at, out_grad, out_grad_all, send, recv, here.at[0], 0)
    quads = [
        second_gather(
            at, i, over_z, over_x, *quad, send, recv, here.at[pl.ds(1 + 4 * i, 4)],
            9 + SpreadOut.COPIES * i, through.at[i],
        )
        for i, quad in enumerate(((quad_0a, quad_0b), (quad_1a, quad_1b)))
    ]
    scatter = PairScatter(at, part, pair_refs, send, recv, 9 + 2 * SpreadOut.COPIES)
    ring.begin()
    quads[0].begin()

    gains = gain_rows(weights)
    seg_row = segment_row(segments)
    seg_column = column_of(seg_row)
    for block in range(SEQ // BLOCK):
        rows = slice(block * BLOCK, (block + 1) * BLOCK)
        values = hidden[rows, :].astype(F32)
        scale = lax.rsqrt(jnp.mean(values * values, axis=-1, keepdims=True) + EPS)
        normed[rows, :] = (values * scale * gains[0:1, :]).astype(BF)
    for half in range(2):
        columns = slice(half * 128, half * 128 + 128)
        pre = mm(normed[...], weights[:, columns])
        query[:, columns] = (rotated(pre, cosine[...], sine[...]) * 0.125).astype(BF)
    key_pre = mm(normed[...], weights[:, 256:384])
    key[...] = rotated(key_pre, cosine[...], sine[...]).astype(BF)
    value_pre = mm(normed[...], weights[:, 384:512])
    value[...] = value_pre.astype(BF)
    value_t = value_pre.T.astype(BF)
    for block in range(SEQ // BLOCK):
        first, end = block * BLOCK, (block + 1) * BLOCK
        bias[:end, :] = bias_block(seg_column[:end, :], seg_row[:, first:end], first, end)
        for head in range(HEADS):
            kv = slice((head // 2) * HD, (head // 2) * HD + HD)
            own = slice(head * HD, head * HD + HD)
            scores = mm_last(key[:end, kv], query[first:end, own]) + bias[:end, :]
            top = jnp.max(scores, axis=0, keepdims=True)
            powers = jnp.exp(scores - top)
            total = jnp.sum(powers, axis=0, keepdims=True)
            share = (powers * (1.0 / total)).astype(BF)
            context_t[own, first:end] = mm(value_t[kv, :end], share).astype(BF)
            log_total[head : head + 1, first:end] = top + jnp.log(total)
        if block == 1:
            quads[0].forward()
            quads[1].begin()
        if block == 2:
            ring.forward_before()
            ring.forward_behind()
    context[...] = context_t[...].T

    def project(slot):
        rows = pl.ds(pl.multiple_of(slot * LOCAL, LOCAL), LOCAL)
        part[slot] = mm_last(context[rows, :], weights[:, 512:768]).astype(BF)

    project(scatter.other + 1 - at.core)
    scatter.begin_far()
    project(scatter.other + at.core)
    project(scatter.own + 1 - at.core)
    scatter.begin_own()
    project(scatter.own + at.core)
    scatter.forward()
    quads[1].forward()
    ring.forward_across()
    scatter.finish(middle)
    values = middle[...] + own_hidden[...].astype(F32)
    middle[...] = values
    scale = lax.rsqrt(jnp.mean(values * values, axis=-1, keepdims=True) + EPS)
    normed_moe[...] = (values * scale * gains[1:2, :]).astype(BF)
    chosen = named[...] > 0.0
    logits = jnp.where(chosen, mm(normed_moe[...], weights[:, 768:896]), MASKED)
    powers = jnp.where(chosen, jnp.exp(logits - jnp.max(logits, axis=-1, keepdims=True)), 0.0)
    gating[...] = powers / jnp.sum(powers, axis=-1, keepdims=True)
    for i in (0, 4, 6, 7, 8):
        ring.copy(i).wait_recv()
    ring.sent()
    ring.kept().wait()
    for quad in quads:
        quad.finish()


def front(hidden, weights, tables, segments, own_hidden, named, out_grad, lines, ident):
    vmem = pl.BlockSpec(memory_space=pltpu.VMEM)
    hbm = pl.BlockSpec(memory_space=pl.ANY)
    sems = 9 + 2 * SpreadOut.COPIES + 1 + 2 * PIECES
    return pl.pallas_call(
        front_kernel,
        in_specs=[vmem] * 8 + [hbm] * 2,
        out_specs=[vmem] * 9 + [hbm] * 5,
        out_shape=[
            jax.ShapeDtypeStruct((SEQ, D), BF),
            jax.ShapeDtypeStruct((SEQ, HEADS * HD), BF),
            jax.ShapeDtypeStruct((SEQ, 128), BF),
            jax.ShapeDtypeStruct((SEQ, 128), BF),
            jax.ShapeDtypeStruct((HEADS * HD, SEQ), BF),
            jax.ShapeDtypeStruct((8, SEQ), F32),
            jax.ShapeDtypeStruct((LOCAL, D), F32),
            jax.ShapeDtypeStruct((LOCAL, D), BF),
            jax.ShapeDtypeStruct((LOCAL, 128), F32),
            *[QUAD_SHAPE] * 4,
            jax.ShapeDtypeStruct((8, LOCAL, D), BF),
        ],
        scratch_shapes=[
            pltpu.VMEM((SEQ, BLOCK), F32),
            pltpu.VMEM((4, LOCAL, D), BF),
            pltpu.VMEM((SEQ, HEADS * HD), BF),
            pltpu.VMEM((2, 2, *BLOCK_SHAPE), BF),
            *pair_scratch(LOCAL, D),
            pltpu.SemaphoreType.DMA((sems,)),
            pltpu.SemaphoreType.DMA((sems,)),
            pltpu.SemaphoreType.DMA((9,)),
        ],
        compiler_params=pltpu.CompilerParams(
            collective_id=ident, has_side_effects=True, vmem_limit_bytes=56 * MIB
        ),
        name="front",
    )(hidden, weights, *tables, segments, own_hidden, named, out_grad, *lines)


def back_kernel(
    dx, dgate, gating, middle, normed_moe, out_grad, y_part,
    normed, weights, cosine, sine, segments, query, key, value, context_t, log_total,
    dmiddle, dn1, grads, block_out,
    bias, dcontext, dquery_t, dkey, dvalue, dall, dall_t, dattn_own, dattn_all, y_sum, *refs,
):
    ring_refs = refs[:8]
    send, recv, here = refs[8:]
    at = Place()
    greet([at.sibling(), at.partner(), at.ring(1), at.ring(3)])
    gain = gain_rows(weights)[1:2, :]
    chosen = gating[...]
    dchosen = chosen * (dgate[...] - jnp.sum(chosen * dgate[...], axis=-1, keepdims=True))
    dlogits = dchosen.astype(BF)
    dnormed = dx[...] + mm_last(dlogits, weights[:, 768:896])
    values = middle[...]
    scale = lax.rsqrt(jnp.mean(values * values, axis=-1, keepdims=True) + EPS)
    unit = values * scale
    weighted = dnormed * gain
    inner = jnp.mean(weighted * unit, axis=-1, keepdims=True)
    total = out_grad[...].astype(F32) + scale * (weighted - unit * inner)
    dmiddle[...] = total
    dattn_own[...] = total.astype(BF)
    gather = PairGather(at, dattn_own, dattn_all, send, recv, here, 8, PIECES)
    scatter = RingScatter(at, y_part, ring_refs, send, recv)
    for k in (2, 1, 3, 0):
        scatter.copy(k).start()
    router_part = mm(normed_moe[...].T, dlogits)
    gain_part = column_of(jnp.sum(dnormed * unit, axis=0, keepdims=True))
    lane = lax.broadcasted_iota(jnp.int32, (D, 128), 1)
    grads[:, 768:] = jnp.where(lane == 32, gain_part, router_part).astype(BF)
    seg_row = segment_row(segments)
    seg_column = column_of(seg_row)
    gather.forward()
    scatter.far()
    gather.finish()
    dattn = dattn_all[...].reshape(SEQ, D)
    dcontext[...] = mm(dattn, weights[:, 512:768]).astype(BF)
    output_grad_t = mm(context_t[...], dattn)
    grads[:, 512:768] = output_grad_t.T.astype(BF)
    key_t = key[...].astype(F32).T.astype(BF)
    dkey[...] = jnp.zeros_like(dkey)
    dvalue[...] = jnp.zeros_like(dvalue)
    for block in range(SEQ // BLOCK):
        first, end = block * BLOCK, (block + 1) * BLOCK
        bias[:end, :] = bias_block(seg_column[:end, :], seg_row[:, first:end], first, end)
        for head in range(HEADS):
            kv = slice((head // 2) * HD, (head // 2) * HD + HD)
            own = slice(head * HD, head * HD + HD)
            query_block = query[first:end, own]
            dcontext_block = dcontext[first:end, own]
            scores = mm_last(key[:end, kv], query_block) + bias[:end, :]
            share = jnp.exp(scores - log_total[head : head + 1, first:end])
            dshare = mm_last(value[:end, kv], dcontext_block)
            centre = jnp.sum(share * dshare, axis=0, keepdims=True)
            dscore = (share * (dshare - centre)).astype(BF)
            dquery_t[own, first:end] = mm(key_t[kv, :end], dscore) * 0.125
            dkey[:end, kv] += mm(dscore, query_block)
            dvalue[:end, kv] += mm(share.astype(BF), dcontext_block)
        if block == 0:
            scatter.up_side()
            scatter.down_side()
    turn = -sine[...]
    for half in range(2):
        rows = slice(half * 128, half * 128 + 128)
        piece = rotated(dquery_t[rows, :].T, cosine[...], turn)
        dall[:, rows] = piece.astype(BF)
        dall_t[rows, :] = piece.T.astype(BF)
    piece = rotated(dkey[...], cosine[...], turn)
    dall[:, 256:384] = piece.astype(BF)
    dall_t[256:384, :] = piece.T.astype(BF)
    dall[:, 384:512] = dvalue[...].astype(BF)
    dall_t[384:512, :] = dvalue[...].T.astype(BF)
    grads[:, 0:512] = mm(dall_t[...], normed[...]).T.astype(BF)
    for block in range(SEQ // BLOCK):
        rows = slice(block * BLOCK, (block + 1) * BLOCK)
        dn1[rows, :] = mm_last(dall[rows, :], weights[:, 0:512]).astype(BF)
    scatter.finish(y_sum)
    block_out[...] = (y_sum[...] + middle[...]).astype(BF)


def back(
    dx, dgate, gating, middle, normed_moe, out_grad, y_part,
    normed, weights, tables, segments, kept, ident,
):
    vmem = pl.BlockSpec(memory_space=pltpu.VMEM)
    sems = 8 + 1 + 2 * PIECES
    return pl.pallas_call(
        back_kernel,
        in_specs=[vmem] * 17,
        out_specs=[vmem] * 4,
        out_shape=[
            jax.ShapeDtypeStruct((LOCAL, D), F32),
            jax.ShapeDtypeStruct((SEQ, D), BF),
            jax.ShapeDtypeStruct((D, SMALL), BF),
            jax.ShapeDtypeStruct((LOCAL, D), BF),
        ],
        scratch_shapes=[
            pltpu.VMEM((SEQ, BLOCK), F32),
            pltpu.VMEM((SEQ, HEADS * HD), BF),
            pltpu.VMEM((HEADS * HD, SEQ), F32),
            pltpu.VMEM((SEQ, 128), F32),
            pltpu.VMEM((SEQ, 128), F32),
            pltpu.VMEM((SEQ, 512), BF),
            pltpu.VMEM((512, SEQ), BF),
            pltpu.VMEM((LOCAL, D), BF),
            pltpu.VMEM((4, LOCAL, D), BF),
            pltpu.VMEM((LOCAL, D), F32),
            *ring_scratch(LOCAL, D),
            pltpu.SemaphoreType.DMA((sems,)),
            pltpu.SemaphoreType.DMA((sems,)),
            pltpu.SemaphoreType.DMA,
        ],
        compiler_params=pltpu.CompilerParams(
            collective_id=ident, has_side_effects=True, vmem_limit_bytes=58 * MIB
        ),
        name="back",
    )(
        dx, dgate, gating, middle, normed_moe, out_grad, y_part,
        normed, weights, *tables, segments, *kept,
    )


def experts_kernel(
    x_in, gate_in, d_in, quad_0a, quad_0b, quad_1a, quad_1b, over_z, over_x,
    y_out, dx_out, dgate_out, grads, quad_2a, quad_2b, quad_3a, quad_3b,
    x, d, xt, dt, y, dx, gating, dgate, dgate_part, hidden, w, *refs,
):
    dx_scratch, dgate_scratch = refs[:5], refs[5:10]
    send, recv, here, load, store, fetch = refs[10:16]
    at = Place()
    step = pl.program_id(0)
    opening, closing = step == 0, step == STEPS - 1
    rows_at_once = 2 * LOCAL
    lane = lax.broadcasted_iota(jnp.int32, (LOCAL, 128), 1)
    own_first = at.yh * 16 + step * QUAD
    x_gather = RingGather(at, x_in, x, send, recv, here.at[0], 0)
    gate_gather = RingGather(at, gate_in, gating, send, recv, here.at[1], 9)
    gathers = (x_gather, gate_gather)
    scatters = (
        RingScatter(at, d, dx_scratch, send, recv, 18),
        RingScatter(at, dgate_part, dgate_scratch, send, recv, 26),
    )

    quads = [
        second_gather(
            at, 2 + i, over_z, over_x, *quad, *refs[16:18], refs[18].at[pl.ds(4 * i, 4)],
            SpreadOut.COPIES * i, refs[19],
        )
        for i, quad in enumerate(((quad_2a, quad_2b), (quad_3a, quad_3b)))
    ]

    def ride(condition, what):
        for i, quad in enumerate(quads):

            @pl.when(condition & (step == i))
            def _():
                what(quad)

    def fetches(quad_a, quad_b):
        copies = []
        for g in range(3):
            for i in range(QUAD):
                columns = pl.ds((g * QUAD + i) * FF, FF)
                if i < 2:
                    parts = [(quad_a.at[:, :, :, g, i], w.at[:, :, :, :, columns])]
                else:
                    parts = [
                        (quad_b.at[:, x_at, :, g, i - 2], w.at[x_at, :, :, :, columns])
                        for x_at in range(4)
                    ]
                for part in parts:
                    copies.append(pltpu.make_async_copy(*part, fetch.at[len(copies)]))
        return copies

    def d_load(chip):
        two = pl.ds(chip * 2, 2)
        return pltpu.make_async_copy(d_in.at[two], d.at[two], load.at[chip])

    def y_store(chip):
        two = pl.ds(chip * 2, 2)
        return pltpu.make_async_copy(x.at[two], y_out.at[two], store.at[chip])

    @pl.when(opening)
    def _():
        greet(
            [
                at.sibling(), at.ring(1), at.ring(3),
                at.along("x", 1), at.along("x", 3), at.along("z", 1), at.along("z", 3),
            ]
        )
        for gather in gathers:
            gather.begin()
        for copy in fetches(quad_0a, quad_0b):
            copy.start()
        for chip in range(4):
            d_load(chip).start()

    for copy in fetches(quad_0a, quad_0b):
        copy.wait()

    ride(step < STEPS, lambda quad: quad.begin())

    def arrive(turn):
        @pl.when(turn == 0)
        def _():
            for gather in gathers:
                gather.kept().wait()
                gather.copy(0).wait_recv()

        @pl.when(turn == 1)
        def _():
            for gather in gathers:
                gather.forward_before()
                gather.forward_behind()
            for gather in gathers:
                gather.copy(4).wait_recv()

        @pl.when(turn == 2)
        def _():
            for gather in gathers:
                gather.forward_across()
            for gather in gathers:
                gather.copy(6).wait_recv()

        @pl.when(turn == 3)
        def _():
            for gather in gathers:
                gather.copy(7).wait_recv()
                gather.copy(8).wait_recv()

    def leave(turn):
        @pl.when(turn == 0)
        def _():
            for scatter in scatters:
                scatter.copy(2).start()

        @pl.when(turn == 1)
        def _():
            for scatter in scatters:
                scatter.copy(1).start()
                scatter.far()

        @pl.when(turn == 2)
        def _():
            for scatter in scatters:
                scatter.copy(3).start()
                scatter.up_side()

        @pl.when(turn == 3)
        def _():
            for scatter in scatters:
                scatter.copy(0).start()
                scatter.down_side()

    def tokens_block(turn, carry):
        inward = jnp.where(turn == 0, 0, jnp.where(turn == 1, 3, turn - 1))
        outward = jnp.where(turn == 0, 2, jnp.where(turn == 3, 0, turn * 2 - 1))
        chip = at.chip(jnp.where(closing, outward, inward))
        two = pl.ds(chip * 2, 2)
        rows = pl.ds(pl.multiple_of(chip * rows_at_once, rows_at_once), rows_at_once)

        @pl.when(opening)
        def _():
            arrive(turn)
            d_load(chip).wait()
            xt[:, rows] = x[two].reshape(rows_at_once, D).T
            dt[:, rows] = d[two].reshape(rows_at_once, D).T
            y[rows, :] = jnp.zeros((rows_at_once, D), F32)
            dx[rows, :] = jnp.zeros((rows_at_once, D), F32)
            dgate[rows, :] = jnp.zeros((rows_at_once, 128), F32)

        ride(turn == 3, lambda quad: quad.forward())
        gate_up = w[:, :, :, :, 0 : 2 * F].reshape(D, 2 * F)
        down = w[:, :, :, :, 2 * F :].reshape(D, F)
        for core in range(2):
            slot = chip * 2 + core
            part = pl.ds(pl.multiple_of(slot * LOCAL, LOCAL), LOCAL)
            both = mm(x[slot], gate_up)
            gate, up = both[:, :F], both[:, F:]
            dact = mm(d[slot], down)
            turned = pltpu.roll(gating[slot], lax.rem(128 - own_first, 128), 1)
            factor = jnp.concatenate(
                [jnp.broadcast_to(turned[:, i : i + 1], (LOCAL, FF)) for i in range(QUAD)],
                axis=1,
            )
            q = 1.0 / (1.0 + jnp.exp(-gate))
            silu = gate * q
            act = silu * up
            product = act * dact
            sums = dgate[part, :]
            for i in range(QUAD):
                own = jnp.sum(product[:, i * FF : (i + 1) * FF], axis=1, keepdims=True)
                sums = jnp.where(lane == own_first + i, own, sums)
            dgate[part, :] = sums
            dact = dact * factor
            hidden[part, 0:F] = (dact * up * (q + silu * (1.0 - q))).astype(BF)
            hidden[part, F : 2 * F] = (dact * silu).astype(BF)
            hidden[part, 2 * F :] = (act * factor).astype(BF)
        y[rows, :] += mm_last(hidden[rows, 2 * F :], down)
        dx[rows, :] += mm_last(hidden[rows, 0 : 2 * F], gate_up)

        @pl.when(closing)
        def _():
            x[two] = y[rows, :].astype(BF).reshape(2, LOCAL, D)
            d[two] = dx[rows, :].astype(BF).reshape(2, LOCAL, D)
            dgate_part[two] = dgate[rows, :].astype(BF).reshape(2, LOCAL, 128)
            y_store(chip).start()
            leave(turn)

        return carry

    lax.fori_loop(0, 4, tokens_block, 0)

    later = ((quad_1a, quad_1b), (quad_2a, quad_2b), (quad_3a, quad_3b))
    for number, quad in enumerate(later):

        @pl.when(step == number)
        def _():
            for copy in fetches(*quad):
                copy.start()

    @pl.when(opening)
    def _():
        for gather in gathers:
            gather.sent()

    def grads_block(block, carry):
        rows = pl.ds(pl.multiple_of(block * 512, 512), 512)
        into = pl.ds(pl.multiple_of(block * 256, 256), 256)

        def put(g, value):
            value = value.astype(BF).reshape(8, 2, 32, value.shape[1])
            for h in range(2):
                half = value[:, h].reshape(256, value.shape[-1])
                for i in range(half.shape[1] // FF):
                    columns = slice(i * FF, (i + 1) * FF)
                    grads[h, g + i // QUAD, i % QUAD, into, :] = half[:, columns]

        put(0, mm(xt[rows, :], hidden[:, 0 : 2 * F]))
        put(2, mm(dt[rows, :], hidden[:, 2 * F :]))
        return carry

    lax.fori_loop(0, D // 512, grads_block, 0)
    ride(step < STEPS, lambda quad: quad.finish())

    @pl.when(closing)
    def _():
        scatters[0].finish(dx_out)
        scatters[1].finish(dgate_out)
        for chip in range(4):
            y_store(chip).wait()


def experts(x, gating, d, quads, lines, ident):
    hbm = pl.BlockSpec(memory_space=pl.ANY)

    def whole(rows, columns):
        return pl.BlockSpec((rows, columns), lambda step: (0, 0), pipeline_mode=pl.Buffered(1))

    return pl.pallas_call(
        experts_kernel,
        grid=(STEPS,),
        in_specs=[hbm] * 9,
        out_specs=[
            hbm,
            whole(LOCAL, D),
            whole(LOCAL, 128),
            pl.BlockSpec(
                (2, 3, QUAD, D // 2, FF), lambda step: (0, 0, step, 0, 0),
                pipeline_mode=pl.Buffered(1),
            ),
            *[hbm] * 4,
        ],
        out_shape=[
            jax.ShapeDtypeStruct((8, LOCAL, D), BF),
            jax.ShapeDtypeStruct((LOCAL, D), F32),
            jax.ShapeDtypeStruct((LOCAL, 128), F32),
            jax.ShapeDtypeStruct((2, 3, STEPS * QUAD, D // 2, FF), BF),
            *[QUAD_SHAPE] * 4,
        ],
        scratch_shapes=[
            pltpu.VMEM((8, LOCAL, D), BF),
            pltpu.VMEM((8, LOCAL, D), BF),
            pltpu.VMEM((D, TOKENS), BF),
            pltpu.VMEM((D, TOKENS), BF),
            pltpu.VMEM((TOKENS, D), F32),
            pltpu.VMEM((TOKENS, D), F32),
            pltpu.VMEM((8, LOCAL, 128), F32),
            pltpu.VMEM((TOKENS, 128), F32),
            pltpu.VMEM((8, LOCAL, 128), BF),
            pltpu.VMEM((TOKENS, 3 * F), BF),
            pltpu.VMEM((4, 4, 2, 32, 3 * F), BF),
            *ring_scratch(LOCAL, D, False),
            *ring_scratch(LOCAL, 128, False),
            pltpu.SemaphoreType.DMA((34,)),
            pltpu.SemaphoreType.DMA((34,)),
            pltpu.SemaphoreType.DMA((2,)),
            pltpu.SemaphoreType.DMA((4,)),
            pltpu.SemaphoreType.DMA((4,)),
            pltpu.SemaphoreType.DMA((30,)),
            pltpu.SemaphoreType.DMA((2 * SpreadOut.COPIES,)),
            pltpu.SemaphoreType.DMA((2 * SpreadOut.COPIES,)),
            pltpu.SemaphoreType.DMA((8,)),
            pltpu.VMEM((2, *BLOCK_SHAPE), BF),
        ],
        compiler_params=pltpu.CompilerParams(
            collective_id=ident, has_side_effects=True, vmem_limit_bytes=63 * MIB
        ),
        name="experts",
    )(x, gating, d, *quads, *lines)[:4]


def norm_scale(values):
    return lax.rsqrt(jnp.mean(values * values, axis=-1, keepdims=True) + EPS)


def norm_grad(values, gain, dnormed):
    scale = norm_scale(values)
    unit = values * scale
    weighted = dnormed * gain
    dvalues = scale * (weighted - unit * jnp.mean(weighted * unit, axis=-1, keepdims=True))
    return dvalues


def on_device(
    hidden_in, out_grad, attn_gain, query_weight, key_weight, value_weight, output_weight,
    moe_gain, router_weight, expert_gate, expert_up, expert_down, expert_ids, segment_ids,
):
    small = jnp.concatenate(
        [
            query_weight, key_weight, value_weight, output_weight,
            router_weight, attn_gain[:, None], moe_gain[:, None], jnp.zeros((32, 94), BF),
        ],
        axis=1,
    )
    segment = jnp.pad(segment_ids.reshape(2, 128), ((0, 6), (0, 0)))
    own_shares = (expert_gate, expert_up, expert_down)
    hidden_all, segments, small, *lines = startup(hidden_in, segment, small, own_shares, 0)
    tables = tuple(jnp.asarray(t) for t in rotary_tables())
    named = jnp.any(
        expert_ids[:, :, None] == jnp.arange(128, dtype=jnp.int32)[None, None, :], axis=1
    ).astype(F32)

    normed, *more, d = front(
        hidden_all, small, tables, segments, hidden_in, named, out_grad, lines, 1
    )
    kept, (middle, normed_moe, gating), quads = more[:5], more[5:8], more[8:]
    y, dx, dgate, expert_grads = experts(normed_moe, gating, d, quads, lines, 3)
    expert_grads = lax.psum_scatter(expert_grads, PLANE, scatter_dimension=3, tiled=True)
    dmiddle, dn1, grads, block_out = back(
        dx, dgate, gating, middle, normed_moe, out_grad, y,
        normed, small, tables, segments, kept, 5,
    )
    weights = jnp.concatenate([query_weight, key_weight, value_weight], axis=1)
    dn1, attention_grads, rest = final(dn1, grads, weights, 6)
    hidden = hidden_in.astype(F32)
    dhidden = norm_grad(hidden, small[:, 800].astype(F32), dn1)
    hidden_grad = dmiddle + dhidden
    expert_grads = last_exchange(expert_grads, 7)
    return (
        block_out,
        hidden_grad,
        rest[:, 33] / attn_gain.astype(F32),
        attention_grads[:, 0:256],
        attention_grads[:, 256:384],
        attention_grads[:, 384:512],
        attention_grads[:, 512:768],
        rest[:, 32],
        rest[:, :32],
        *expert_grads,
    )


def solution(mesh):
    fine = Mesh(np.asarray(mesh.devices).reshape(4, 4, 2, 2, 2), ALL)
    return jax.shard_map(
        on_device,
        mesh=fine,
        in_specs=(
            P(ALL, None),
            P(ALL, None),
            P(DP),
            P(DP, TENSOR),
            P(DP, TENSOR),
            P(DP, TENSOR),
            P(DP, TENSOR),
            P(DP),
            P(DP, None),
            P(None, DP, TENSOR),
            P(None, DP, TENSOR),
            P(None, DP, TENSOR),
            P(ALL, None),
            P(ALL),
        ),
        out_specs=(
            P(ALL, None),
            P(ALL, None),
            P(DP),
            P(DP, TENSOR),
            P(DP, TENSOR),
            P(DP, TENSOR),
            P(DP, TENSOR),
            P(DP),
            P(DP, None),
            P(None, DP, TENSOR),
            P(None, DP, TENSOR),
            P(None, DP, TENSOR),
        ),
        check_vma=False,
    )
```

```python
import jax
import jax.numpy as jnp
import numpy as np
from jax import lax
from jax.experimental import pallas as pl
from jax.experimental.pallas import tpu as pltpu
from jax.sharding import Mesh
from jax.sharding import PartitionSpec as P

D = 1024
HD = 64
E = 32
SEQ = 1024
LOCAL = 256
HEADS = 4
QUAD = 4
FF = 128
F = QUAD * FF
EPS = 1e-06
MASKED = -1e30
BLOCK = 256
TOKENS = 2048
STEPS = 4

DP = ("x", "z", "yh")
TENSOR = ("yl", "core")
RING = ("yh", "yl", "core")
PLANE = ("x", "z")
ALL = ("x", "z", "yh", "yl", "core")

F32 = jnp.float32
BF = jnp.bfloat16
LAST = (((1,), (1,)), ((), ()))
MIB = 1024 * 1024
MESH = pl.DeviceIdType.MESH
SMALL = 896


def mm(a, b):
    return jnp.dot(a, b, preferred_element_type=F32)


def mm_last(a, b):
    return lax.dot_general(a, b, LAST, preferred_element_type=F32)


class Place:
    def __init__(self):
        self.x = lax.axis_index("x")
        self.z = lax.axis_index("z")
        self.yh = lax.axis_index("yh")
        self.yl = lax.axis_index("yl")
        self.core = lax.axis_index("core")
        self.y = self.yh * 2 + self.yl

    def chip(self, k):
        return lax.rem(self.y + k, 4)

    def ring(self, k):
        chip = self.chip(k)
        return {"yh": chip // 2, "yl": lax.rem(chip, 2)}

    def along(self, axis, k):
        return {axis: lax.rem(getattr(self, axis) + k, 4)}

    def sibling(self):
        return {"core": 1 - self.core}

    def partner(self):
        return {"yl": 1 - self.yl}

    def diagonal(self):
        return {"yl": 1 - self.yl, "core": 1 - self.core}

    def opposite(self):
        return {"yh": 1 - self.yh}


def greet(devices):
    barrier = pltpu.get_barrier_semaphore()
    for device in devices:
        pl.semaphore_signal(barrier, inc=1, device_id=device, device_id_type=MESH)
    pl.semaphore_wait(barrier, len(devices))


def remote(src, dst, send, recv, i, device):
    return pltpu.make_async_remote_copy(
        src_ref=src, dst_ref=dst, send_sem=send.at[i], recv_sem=recv.at[i],
        device_id=device, device_id_type=MESH,
    )


def push(src, dst, send, recv, i, device):
    copy = remote(src, dst, send, recv, i, device)
    copy.start()
    return copy


def keep(src, dst, sem):
    copy = pltpu.make_async_copy(src, dst, sem)
    copy.start()
    return copy


class RingGather:
    def __init__(self, at, own, out, send, recv, here, base=0):
        self.at, self.own, self.out, self.base = at, own, out, base
        self.send, self.recv, self.here = send, recv, here
        half = own.shape[0] // 2
        lo, hi = pl.ds(0, half), pl.ds(half, half)
        me, before, behind, across = (out.at[self.slot(k)] for k in (0, 3, 1, 2))
        near, up, down = at.sibling(), at.ring(1), at.ring(3)
        self.plan = [
            (own, me, near),
            (own, me, up),
            (own, me, down),
            (before.at[lo], before.at[lo], up),
            (before, before, near),
            (behind.at[hi], behind.at[hi], down),
            (behind, behind, near),
            (across.at[lo], across.at[lo], near),
            (across.at[hi], across.at[hi], near),
        ]

    def slot(self, k):
        return self.at.chip(k) * 2 + self.at.core

    def copy(self, i):
        src, dst, device = self.plan[i]
        return remote(src, dst, self.send, self.recv, self.base + i, device)

    def kept(self):
        return pltpu.make_async_copy(self.own, self.out.at[self.slot(0)], self.here)

    def begin(self):
        self.kept().start()
        for i in (1, 2, 0):
            self.copy(i).start()

    def forward_before(self):
        self.copy(1).wait_recv()
        self.copy(3).start()
        self.copy(4).start()

    def forward_behind(self):
        self.copy(2).wait_recv()
        self.copy(5).start()
        self.copy(6).start()

    def forward_across(self):
        self.copy(3).wait_recv()
        self.copy(7).start()
        self.copy(5).wait_recv()
        self.copy(8).start()

    def sent(self):
        for i in range(9):
            self.copy(i).wait_send()


class PairGather:
    def __init__(self, at, own, out, send, recv, here, base, pieces):
        self.at, self.out, self.send, self.recv, self.base = at, out, send, recv, base
        size = own.shape[0] // pieces
        self.parts = [pl.ds(i * size, size) for i in range(pieces)]
        me = at.yl * 2 + at.core
        self.other = (1 - at.yl) * 2 + at.core
        self.kept = keep(own, out.at[me], here)
        self.far = [
            push(own.at[part], out.at[me, part], send, recv, base + 1 + i, at.partner())
            for i, part in enumerate(self.parts)
        ]
        self.near = [push(own, out.at[me], send, recv, base, at.sibling())]

    def forward(self):
        for i, part in enumerate(self.parts):
            self.far[i].wait_recv()
            view = self.out.at[self.other, part]
            index = self.base + 1 + len(self.parts) + i
            self.near.append(push(view, view, self.send, self.recv, index, self.at.sibling()))

    def finish(self):
        for copy in self.near:
            copy.wait_recv()
        for copy in (*self.far, *self.near):
            copy.wait_send()
        self.kept.wait()


PIECES = 4


class AxisGather:
    def __init__(self, at, axis, view, send, recv, base):
        self.up, self.down = at.along(axis, 1), at.along(axis, 3)
        self.view, self.send, self.recv, self.base = view, send, recv, base

    def go(self, i, view, device):
        return push(view, view, self.send, self.recv, self.base + i, device)

    def begin(self):
        self.first = [
            self.go(0, self.view(0, "all"), self.up), self.go(1, self.view(0, "all"), self.down),
        ]

    def forward(self):
        self.first[0].wait_recv()
        self.far = [self.go(2, self.view(3, "low"), self.up)]
        self.first[1].wait_recv()
        self.far.append(self.go(3, self.view(1, "high"), self.down))

    def finish(self):
        for copy in self.far:
            copy.wait_recv()
        for copy in (*self.first, *self.far):
            copy.wait_send()


def halves_of(ref, first, size):
    spans = {"all": (0, size), "low": (0, size // 2), "high": (size // 2, size // 2)}
    return lambda part: ref.at[pl.ds(first + spans[part][0], spans[part][1])]


class SpreadOut:
    COPIES = 8

    def __init__(self, at, rings, send, recv, here, base=0, through=None):
        self.send, self.recv, self.here, self.base = send, recv, here, base
        self.through = through
        self.own = [(own, slot(0)) for _, own, slot, _ in rings]
        self.plan = []
        for axis, own, slot, _ in rings:
            self.plan.append((own, slot(0), at.along(axis, 1)))
            self.plan.append((own, slot(0), at.along(axis, 3)))
        for axis, _, slot, half in rings:
            low, high = (slot(3).at[pl.ds(0, half)], slot(1).at[pl.ds(half, half)])
            self.plan.append((low, low, at.along(axis, 1)))
            self.plan.append((high, high, at.along(axis, 3)))

    def copy(self, i):
        src, dst, device = self.plan[i]
        return remote(src, dst, self.send, self.recv, self.base + i, device)

    def loaded(self, i):
        return pltpu.make_async_copy(self.own[i][0], self.through.at[i], self.here.at[i])

    def kept(self, i):
        src, dst = self.own[i]
        src = src if self.through is None else self.through.at[i]
        return pltpu.make_async_copy(src, dst, self.here.at[2 + i])

    def begin(self):
        for i in range(4):
            self.copy(i).start()
        for i in range(2):
            (self.kept(i) if self.through is None else self.loaded(i)).start()

    def forward(self):
        for i in range(4):
            self.copy(i).wait_recv()
            self.copy(4 + i).start()
        if self.through is not None:
            for i in range(2):
                self.loaded(i).wait()
                self.kept(i).start()

    def finish(self):
        for i in range(4, 8):
            self.copy(i).wait_recv()
        for i in range(8):
            self.copy(i).wait_send()
        for i in range(2):
            self.kept(i).wait()


def ring_slots(out, place):
    return lambda k: out.at[lax.rem(place + k, 4)]


def first_gather(at, own_a, own_b, over_z, over_x, *sems):
    rings = (
        ("z", own_a, ring_slots(over_z, at.z), 1), ("x", own_b, ring_slots(over_x, at.x), 1),
    )
    return SpreadOut(at, rings, *sems)


def second_gather(at, number, over_z, over_x, quad_a, quad_b, *sems):
    rings = (
        ("x", over_z.at[:, :, number], ring_slots(quad_a, at.x), 2),
        ("z", over_x.at[:, :, number], ring_slots(quad_b, at.z), 2),
    )
    return SpreadOut(at, rings, *sems)


SHARE_SHAPE = (2, STEPS, 3, 2, 32, FF)
BLOCK_SHAPE = (4, 2, 3, 2, 32, FF)
LINE_SHAPE = jax.ShapeDtypeStruct((4, 2, STEPS, 3, 2, 32, FF), BF)
QUAD_SHAPE = jax.ShapeDtypeStruct((4, 4, 2, 3, 2, 32, FF), BF)
GRADS_SHAPE = jax.ShapeDtypeStruct((4, 4, 2, STEPS, 3, 2, 32, FF), BF)
SUMS_SHAPE = jax.ShapeDtypeStruct((4, 2, STEPS, 3, 2, 32, FF), BF)


class RingSum:
    COPIES = 6

    def __init__(self, at, axis, part, scratch, send, recv, load, base=0, first=0):
        half_a, half_b, up, down, to_up, to_down, own = scratch
        self.half_a, self.half_b, self.up, self.down = half_a, half_b, up, down
        self.to_up, self.to_down, self.own = to_up, to_down, own
        self.send, self.recv, self.base = send, recv, base
        size = half_a.shape[0]
        lo, hi = pl.ds(0, size), pl.ds(size, size)
        place = {"x": at.x, "z": at.z}[axis]
        here, above, across, below = (part.at[lax.rem(place + k, 4)] for k in range(4))
        upper, lower = at.along(axis, 1), at.along(axis, 3)
        self.plan = [
            (across.at[lo], half_a, upper),
            (across.at[hi], half_b, lower),
            (above.at[hi], up.at[hi], upper),
            (below.at[lo], down.at[lo], lower),
            (to_up, up.at[lo], upper),
            (to_down, down.at[hi], lower),
        ]
        self.loads = [
            pltpu.make_async_copy(src, dst, load.at[first + i])
            for i, (src, dst) in enumerate(
                ((above.at[lo], to_up), (below.at[hi], to_down), (here, own))
            )
        ]

    def copy(self, i):
        src, dst, device = self.plan[i]
        return remote(src, dst, self.send, self.recv, self.base + i, device)

    def begin(self):
        for i in range(4):
            self.copy(i).start()
        for load in self.loads:
            load.start()

    def middle(self):
        for i, (total, landed) in enumerate(
            ((self.to_up, self.half_a), (self.to_down, self.half_b))
        ):
            self.loads[i].wait()
            self.copy(i).wait_recv()
            rows = total.shape[1]

            def add(at, carry, total=total, landed=landed, rows=rows):
                i, j = at // rows, lax.rem(at, rows)
                total[i, j] = (total[i, j].astype(F32) + landed[i, j].astype(F32)).astype(BF)
                return carry

            lax.fori_loop(0, total.shape[0] * rows, add, 0)
            self.copy(4 + i).start()

    def finish(self, out):
        self.loads[2].wait()
        for i in range(2, 6):
            self.copy(i).wait_recv()
        rows = out.shape[1]

        def add(at, carry):
            i, j = at // rows, lax.rem(at, rows)
            total = self.own[i, j].astype(F32) + self.up[i, j].astype(F32)
            out[i, j] = (total + self.down[i, j].astype(F32)).astype(out.dtype)
            return carry

        lax.fori_loop(0, out.shape[0] * rows, add, 0)
        for i in range(6):
            self.copy(i).wait_send()


def sum_scratch(block):
    half, whole = pltpu.VMEM((block[0] // 2, *block[1:]), BF), pltpu.VMEM(block, BF)
    return [half, half, whole, whole, half, half, whole]


def startup_kernel(
    hidden, segment, small, gate, up, down,
    hidden_all, segment_all, small_all, over_z_line, over_x_line,
    share_a, share_b, send, recv, here,
):
    at = Place()
    greet(
        [
            at.sibling(), at.partner(), at.diagonal(), at.opposite(),
            at.along("x", 1), at.along("x", 3), at.along("z", 1), at.along("z", 3),
        ]
    )
    rank = at.yl * 2 + at.core
    mine = small_all.at[(at.x * 4 + at.z) * 2 + at.yh]
    small_kept = keep(small, mine, here.at[0])
    copies = [push(small, mine, send, recv, 0, at.opposite())]
    swaps, swaps_kept = [], []
    base = 13 + 2 * PIECES
    for i, share in enumerate((gate, up, down)):
        for j, out in enumerate((share_a, share_b)):
            dst, two = out.at[at.yh, :, i], pl.ds(2 * j, 2)
            theirs = share.at[pl.ds((1 - at.yh) * STEPS, STEPS), two]
            index = 2 * i + j
            swaps.append(push(theirs, dst, send, recv, base + index, at.opposite()))
            own = share.at[pl.ds(at.yh * STEPS, STEPS), two]
            swaps_kept.append(keep(own, dst, here.at[3 + index]))
    experts = first_gather(
        at, share_a, share_b, over_z_line, over_x_line, send, recv, here.at[pl.ds(9, 4)], base + 6
    )
    copies.extend(
        push(segment, segment_all.at[rank], send, recv, 1 + i, device)
        for i, device in enumerate((at.sibling(), at.partner(), at.diagonal()))
    )
    pair = PairGather(at, hidden, hidden_all, send, recv, here.at[1], 12, PIECES)
    seg_here = keep(segment, segment_all.at[rank], here.at[2])
    over_z = AxisGather(
        at, "z",
        lambda k, part: halves_of(small_all, (at.x * 4 + lax.rem(at.z + k, 4)) * 2, 2)(part),
        send, recv, 4,
    )
    over_x = AxisGather(
        at, "x", lambda k, part: halves_of(small_all, lax.rem(at.x + k, 4) * 8, 8)(part),
        send, recv, 8,
    )
    small_kept.wait()
    copies[0].wait_recv()
    over_z.begin()
    over_z.forward()
    over_z.finish()
    over_x.begin()
    pair.forward()
    for swap, own in zip(swaps, swaps_kept):
        swap.wait_recv()
        own.wait()
    experts.begin()
    over_x.forward()
    experts.forward()
    pair.finish()
    seg_here.wait()
    for copy in copies[1:]:
        copy.wait_recv()
    over_x.finish()
    experts.finish()
    for copy in (*copies, *swaps):
        copy.wait_send()


def startup(hidden, segment, small, shares, ident):
    hbm = pl.BlockSpec(memory_space=pl.ANY)
    sems = 13 + 2 * PIECES + 6 + SpreadOut.COPIES
    shares = [share.reshape(2 * STEPS, QUAD, 32, FF) for share in shares]
    vmem = pl.BlockSpec(memory_space=pltpu.VMEM)
    hidden_all, segment_all, small_all, over_z, over_x = pl.pallas_call(
        startup_kernel,
        in_specs=[vmem] * 3 + [hbm] * 3,
        out_specs=[hbm] * 5,
        out_shape=[
            jax.ShapeDtypeStruct((4, *hidden.shape), hidden.dtype),
            jax.ShapeDtypeStruct((4, *segment.shape), segment.dtype),
            jax.ShapeDtypeStruct((32, 32, SMALL), small.dtype),
            LINE_SHAPE,
            LINE_SHAPE,
        ],
        scratch_shapes=[
            pltpu.VMEM(SHARE_SHAPE, BF),
            pltpu.VMEM(SHARE_SHAPE, BF),
            pltpu.SemaphoreType.DMA((sems,)),
            pltpu.SemaphoreType.DMA((sems,)),
            pltpu.SemaphoreType.DMA((13,)),
        ],
        compiler_params=pltpu.CompilerParams(collective_id=ident, has_side_effects=True),
        name="startup",
    )(hidden, segment, small, *shares)
    hidden_all, small_all = hidden_all.reshape(SEQ, D), small_all.reshape(D, SMALL)
    return hidden_all, segment_all, small_all, over_z, over_x


class RingScatter:
    def __init__(self, at, part, scratch, send, recv, base=0):
        self.at, self.part, self.send, self.recv, self.base = at, part, send, recv, base
        near, half_a, half_b, self.full_up, self.full_down = scratch[:5]
        to_far, to_up, to_down = scratch[5:] or [
            part.at[at.chip(k) * 2 + at.core] for k in (2, 1, 3)
        ]
        self.near, self.half_a, self.half_b = near, half_a, half_b
        self.to_far, self.to_up, self.to_down = to_far, to_up, to_down
        self.half = half_a.shape[0]
        self.lo, self.hi = pl.ds(0, self.half), pl.ds(self.half, self.half)
        up, down = at.ring(1), at.ring(3)
        self.plan = {
            k: (part.at[at.chip(k) * 2 + 1 - at.core], near.at[k], at.sibling()) for k in range(4)
        }
        self.plan[4] = (to_far.at[self.lo], half_a, up)
        self.plan[5] = (to_far.at[self.hi], half_b, down)
        self.plan[6] = (to_up, self.full_up, up)
        self.plan[7] = (to_down, self.full_down, down)

    def copy(self, i):
        src, dst, device = self.plan[i]
        return remote(src, dst, self.send, self.recv, self.base + i, device)

    def chip_sum(self, k):
        self.copy(k).wait_recv()
        own = self.part[self.at.chip(k) * 2 + self.at.core]
        return own.astype(F32) + self.near[k].astype(F32)

    def far(self):
        self.to_far[...] = self.chip_sum(2).astype(BF)
        self.copy(4).start()
        self.copy(5).start()

    def up_side(self):
        total = self.chip_sum(1)
        self.copy(4).wait_recv()
        self.to_up[self.lo, :] = (total[: self.half] + self.half_a[...].astype(F32)).astype(BF)
        self.to_up[self.hi, :] = total[self.half :].astype(BF)
        self.copy(6).start()

    def down_side(self):
        total = self.chip_sum(3)
        self.copy(5).wait_recv()
        self.to_down[self.lo, :] = total[: self.half].astype(BF)
        self.to_down[self.hi, :] = (total[self.half :] + self.half_b[...].astype(F32)).astype(BF)
        self.copy(7).start()

    def finish(self, out):
        out[...] = self.chip_sum(0)
        self.copy(6).wait_recv()
        out[...] += self.full_up[...].astype(F32)
        self.copy(7).wait_recv()
        out[...] += self.full_down[...].astype(F32)
        for i in range(8):
            self.copy(i).wait_send()


def ring_scratch(rows, columns, own_sends=True):
    block, half = pltpu.VMEM((rows, columns), BF), pltpu.VMEM((rows // 2, columns), BF)
    scratch = [pltpu.VMEM((4, rows, columns), BF), half, half, block, block]
    return scratch + [block] * 3 if own_sends else scratch


class PairScatter:
    def __init__(self, at, part, scratch, send, recv, base=0):
        self.at, self.part, self.send, self.recv, self.base = at, part, send, recv, base
        self.near, self.far_rows, self.to_far = scratch
        size = self.to_far.shape[0] // PIECES
        self.parts = [pl.ds(i * size, size) for i in range(PIECES)]
        self.other, self.own = (1 - at.yl) * 2, at.yl * 2

    def go(self, i, src, dst, device):
        return push(src, dst, self.send, self.recv, self.base + i, device)

    def begin_far(self):
        slot = self.other + 1 - self.at.core
        self.first = [
            self.go(i, self.part.at[slot, rows], self.near.at[1, rows], self.at.sibling())
            for i, rows in enumerate(self.parts)
        ]

    def begin_own(self):
        slot = self.own + 1 - self.at.core
        self.second = self.go(PIECES, self.part.at[slot], self.near.at[0], self.at.sibling())

    def forward(self):
        self.sent = []
        for i, rows in enumerate(self.parts):
            self.first[i].wait_recv()
            own = self.part[self.other + self.at.core, rows, :].astype(F32)
            self.to_far[rows, :] = (own + self.near[1, rows, :].astype(F32)).astype(BF)
            far = self.far_rows.at[rows]
            self.sent.append(self.go(PIECES + 1 + i, self.to_far.at[rows], far, self.at.partner()))

    def finish(self, out):
        self.second.wait_recv()
        out[...] = self.part[self.own + self.at.core].astype(F32) + self.near[0].astype(F32)
        for i, rows in enumerate(self.parts):
            self.sent[i].wait_recv()
            out[rows, :] += self.far_rows[rows, :].astype(F32)
        for copy in (*self.first, self.second, *self.sent):
            copy.wait_send()


def pair_scratch(rows, columns):
    block = pltpu.VMEM((rows, columns), BF)
    return [pltpu.VMEM((2, rows, columns), BF), block, block]


class DirectScatter:
    def __init__(self, at, axis, blocks, landed, send, recv, base):
        self.blocks, self.landed = blocks, landed
        self.copies = [
            push(blocks(k), landed.at[k - 1], send, recv, base + k - 1, at.along(axis, k))
            for k in (2, 1, 3)
        ]

    def total(self):
        value = self.blocks(0)[...].astype(F32)
        for copy, k in zip(self.copies, (2, 1, 3)):
            copy.wait_recv()
            value = value + self.landed[k - 1].astype(F32)
        return value

    def sent(self):
        for copy in self.copies:
            copy.wait_send()


SPLIT = 384


def final_kernel(
    part, grads, weights, sum_a, sum_b, dn1, attention, rest, gate, up, down,
    a_1, b_1, a_half, b_half, a_2, b_2, over_y, from_opposite, share, shares, *refs,
):
    at = Place()
    greet(
        [
            at.sibling(), at.partner(), at.diagonal(), at.opposite(),
            *[at.along(axis, k) for axis in ("x", "z") for k in (1, 2, 3)],
        ]
    )
    pair_refs = refs[:3]
    total_a, total_b, land_a, land_b = refs[17:21]
    send, recv, load = refs[21:]
    base = 1 + 2 * PIECES
    after = base + 18
    width = grads.shape[-1]
    a, b = pl.ds(0, SPLIT), pl.ds(SPLIT, width - SPLIT)

    def x_of(k):
        return lax.rem(at.x + k, 4)

    def z_of(k):
        return lax.rem(at.z + k, 4)

    first_a = DirectScatter(
        at, "x", lambda k: grads.at[x_of(k), :, :, a], a_1, send, recv, base
    )
    first_b = DirectScatter(
        at, "z", lambda k: grads.at[:, z_of(k), :, b], b_1, send, recv, base + 3
    )
    sums = [
        RingSum(at, "z", sum_a, refs[3:10], send, recv, load, after),
        RingSum(at, "x", sum_b, refs[10:17], send, recv, load, after + RingSum.COPIES, 3),
    ]
    for each in sums:
        each.begin()
    pair = PairScatter(at, part, pair_refs, send, recv)
    pair.begin_far()
    pair.begin_own()
    pair.forward()
    a_half[...] = first_a.total().astype(BF)
    second_a = DirectScatter(
        at, "z", lambda k: a_half.at[z_of(k)], a_2, send, recv, base + 6
    )
    b_half[...] = first_b.total().astype(BF)
    second_b = DirectScatter(
        at, "x", lambda k: b_half.at[x_of(k)], b_2, send, recv, base + 9
    )
    for each in sums:
        each.middle()
    over_y[:, a] = second_a.total().astype(BF)
    over_y[:, b] = second_b.total().astype(BF)
    theirs = pl.ds(pl.multiple_of((1 - at.yh) * 32, 32), 32)
    own = pl.ds(pl.multiple_of(at.yh * 32, 32), 32)
    swap = push(over_y.at[theirs], from_opposite, send, recv, base + 12, at.opposite())
    lands = []
    for i, (each, out, land) in enumerate(
        zip(sums, (total_a, total_b), (land_a, land_b))
    ):
        each.finish(out)
        lands.append(
            push(out.at[1 - at.yh], land, send, recv, base + 16 + i, at.opposite())
        )
    swap.wait_recv()
    total = over_y[own, :].astype(F32) + from_opposite[...].astype(F32)
    attention[...] = total[:, :768]
    gain_part = jnp.sum(total[:, :512] * weights[...].astype(F32), axis=1, keepdims=True)
    lane = lax.broadcasted_iota(jnp.int32, (32, 128), 1)
    share[...] = jnp.where(lane == 33, gain_part, total[:, 768:])
    copies = [
        push(share, shares.at[i], send, recv, base + 13 + i, device)
        for i, device in enumerate((at.sibling(), at.partner(), at.diagonal()))
    ]
    pair.finish(dn1)
    mine, theirs = pl.ds(at.yh * STEPS, STEPS), pl.ds((1 - at.yh) * STEPS, STEPS)
    for j, value in enumerate((total_a, total_b)):
        for i, out in enumerate((gate, up, down)):
            out[mine, 2 * j : 2 * j + 2] = value[at.yh, :, i].astype(F32)
    rest[...] = share[...]
    for i, copy in enumerate(copies):
        copy.wait_recv()
        rest[...] += shares[i]
    for j, (copy, land) in enumerate(zip(lands, (land_a, land_b))):
        copy.wait_recv()
        for i, out in enumerate((gate, up, down)):
            out[theirs, 2 * j : 2 * j + 2] = land[:, i].astype(F32)
    for copy in (swap, *copies, *lands):
        copy.wait_send()
    for scatter in (first_a, first_b, second_a, second_b):
        scatter.sent()


def final(part, grads, weights, sums, ident):
    vmem = pl.BlockSpec(memory_space=pltpu.VMEM)
    hbm = pl.BlockSpec(memory_space=pl.ANY)
    width = grads.shape[1]
    sems = 1 + 2 * PIECES + 18 + 2 * RingSum.COPIES
    block = SUMS_SHAPE.shape[1:]
    return pl.pallas_call(
        final_kernel,
        in_specs=[vmem] * 3 + [hbm] * 2,
        out_specs=[vmem] * 6,
        out_shape=[
            jax.ShapeDtypeStruct((LOCAL, D), F32),
            jax.ShapeDtypeStruct((32, 768), F32),
            jax.ShapeDtypeStruct((32, 128), F32),
            *[jax.ShapeDtypeStruct((2 * STEPS, QUAD, 32, FF), F32)] * 3,
        ],
        scratch_shapes=[
            pltpu.VMEM((3, 4, 64, SPLIT), BF),
            pltpu.VMEM((3, 4, 64, width - SPLIT), BF),
            pltpu.VMEM((4, 64, SPLIT), BF),
            pltpu.VMEM((4, 64, width - SPLIT), BF),
            pltpu.VMEM((3, 64, SPLIT), BF),
            pltpu.VMEM((3, 64, width - SPLIT), BF),
            pltpu.VMEM((64, width), BF),
            pltpu.VMEM((32, width), BF),
            pltpu.VMEM((32, 128), F32),
            pltpu.VMEM((3, 32, 128), F32),
            *pair_scratch(LOCAL, D),
            *sum_scratch(block),
            *sum_scratch(block),
            *[pltpu.VMEM(block, BF)] * 2,
            *[pltpu.VMEM(block[1:], BF)] * 2,
            pltpu.SemaphoreType.DMA((sems,)),
            pltpu.SemaphoreType.DMA((sems,)),
            pltpu.SemaphoreType.DMA((6,)),
        ],
        compiler_params=pltpu.CompilerParams(
            collective_id=ident, has_side_effects=True, vmem_limit_bytes=48 * MIB
        ),
        name="final",
    )(part.reshape(4, LOCAL, D), grads.reshape(4, 4, 64, width), weights, *sums)


def rotary_tables():
    half = HD // 2
    inverse = (10000.0 ** (-(np.arange(half, dtype=np.float64) * 2.0) / HD)).astype(np.float32)
    angles = np.arange(SEQ, dtype=np.float32)[:, None] * inverse[None, :]
    cosine, sine = np.cos(angles), np.sin(angles)
    wide_cosine = np.concatenate([cosine] * 4, axis=1)
    wide_sine = np.concatenate([-sine, sine] * 2, axis=1)
    return wide_cosine.astype(np.float32), wide_sine.astype(np.float32)


def swapped(values):
    lane = lax.broadcasted_iota(jnp.int32, values.shape, 1)
    low = (lane % HD) < HD // 2
    return jnp.where(low, pltpu.roll(values, 96, 1), pltpu.roll(values, 32, 1))


def rotated(values, cosine, sine):
    return values * cosine + swapped(values) * sine


def bias_block(key_segment, query_segment, first, rows):
    key_at = lax.broadcasted_iota(jnp.int32, (rows, BLOCK), 0)
    query_at = lax.broadcasted_iota(jnp.int32, (rows, BLOCK), 1) + first
    allowed = (key_segment == query_segment) & (key_at <= query_at)
    return jnp.where(allowed, 0.0, MASKED)


def segment_row(segments):
    return jnp.concatenate(
        [segments[rank, i : i + 1, :] for rank in range(4) for i in range(2)], axis=1
    ).astype(F32)


def gain_rows(small):
    return small[:, 768:896].astype(F32).T[32:40, :]


def column_of(row):
    return jnp.broadcast_to(row, (8, row.shape[1])).T[:, 0:1]


def front_kernel(
    hidden, weights, cosine, sine, segments, own_hidden, named, out_grad, over_z, over_x,
    normed, query, key, value, context_t, log_total, middle, normed_moe, gating,
    quad_0a, quad_0b, quad_1a, quad_1b, out_grad_all, bias, part, context, through, *refs,
):
    pair_refs = refs[:3]
    send, recv, here = refs[3:]
    at = Place()
    greet(
        [
            at.sibling(), at.partner(), at.ring(1), at.ring(3),
            at.along("x", 1), at.along("x", 3), at.along("z", 1), at.along("z", 3),
        ]
    )
    ring = RingGather(at, out_grad, out_grad_all, send, recv, here.at[0], 0)
    quads = [
        second_gather(
            at, i, over_z, over_x, *quad, send, recv, here.at[pl.ds(1 + 4 * i, 4)],
            9 + SpreadOut.COPIES * i, through.at[i],
        )
        for i, quad in enumerate(((quad_0a, quad_0b), (quad_1a, quad_1b)))
    ]
    scatter = PairScatter(at, part, pair_refs, send, recv, 9 + 2 * SpreadOut.COPIES)
    ring.begin()
    quads[0].begin()

    gains = gain_rows(weights)
    seg_row = segment_row(segments)
    seg_column = column_of(seg_row)
    for block in range(SEQ // BLOCK):
        rows = slice(block * BLOCK, (block + 1) * BLOCK)
        values = hidden[rows, :].astype(F32)
        scale = lax.rsqrt(jnp.mean(values * values, axis=-1, keepdims=True) + EPS)
        normed[rows, :] = (values * scale * gains[0:1, :]).astype(BF)
    for half in range(2):
        columns = slice(half * 128, half * 128 + 128)
        pre = mm(normed[...], weights[:, columns])
        query[:, columns] = (rotated(pre, cosine[...], sine[...]) * 0.125).astype(BF)
    key_pre = mm(normed[...], weights[:, 256:384])
    key[...] = rotated(key_pre, cosine[...], sine[...]).astype(BF)
    value_pre = mm(normed[...], weights[:, 384:512])
    value[...] = value_pre.astype(BF)
    value_t = value_pre.T.astype(BF)
    for block in range(SEQ // BLOCK):
        first, end = block * BLOCK, (block + 1) * BLOCK
        bias[:end, :] = bias_block(seg_column[:end, :], seg_row[:, first:end], first, end)
        for head in range(HEADS):
            kv = slice((head // 2) * HD, (head // 2) * HD + HD)
            own = slice(head * HD, head * HD + HD)
            scores = mm_last(key[:end, kv], query[first:end, own]) + bias[:end, :]
            top = jnp.max(scores, axis=0, keepdims=True)
            powers = jnp.exp(scores - top)
            total = jnp.sum(powers, axis=0, keepdims=True)
            share = (powers * (1.0 / total)).astype(BF)
            context_t[own, first:end] = mm(value_t[kv, :end], share).astype(BF)
            log_total[head : head + 1, first:end] = top + jnp.log(total)
        if block == 1:
            quads[0].forward()
            quads[1].begin()
        if block == 2:
            ring.forward_before()
            ring.forward_behind()
    context[...] = context_t[...].T

    def project(slot):
        rows = pl.ds(pl.multiple_of(slot * LOCAL, LOCAL), LOCAL)
        part[slot] = mm_last(context[rows, :], weights[:, 512:768]).astype(BF)

    project(scatter.other + 1 - at.core)
    scatter.begin_far()
    project(scatter.other + at.core)
    project(scatter.own + 1 - at.core)
    scatter.begin_own()
    project(scatter.own + at.core)
    scatter.forward()
    quads[1].forward()
    ring.forward_across()
    scatter.finish(middle)
    values = middle[...] + own_hidden[...].astype(F32)
    middle[...] = values
    scale = lax.rsqrt(jnp.mean(values * values, axis=-1, keepdims=True) + EPS)
    normed_moe[...] = (values * scale * gains[1:2, :]).astype(BF)
    chosen = named[...] > 0.0
    logits = jnp.where(chosen, mm(normed_moe[...], weights[:, 768:896]), MASKED)
    powers = jnp.where(chosen, jnp.exp(logits - jnp.max(logits, axis=-1, keepdims=True)), 0.0)
    gating[...] = powers / jnp.sum(powers, axis=-1, keepdims=True)
    for i in (0, 4, 6, 7, 8):
        ring.copy(i).wait_recv()
    ring.sent()
    ring.kept().wait()
    for quad in quads:
        quad.finish()


def front(hidden, weights, tables, segments, own_hidden, named, out_grad, lines, ident):
    vmem = pl.BlockSpec(memory_space=pltpu.VMEM)
    hbm = pl.BlockSpec(memory_space=pl.ANY)
    sems = 9 + 2 * SpreadOut.COPIES + 1 + 2 * PIECES
    return pl.pallas_call(
        front_kernel,
        in_specs=[vmem] * 8 + [hbm] * 2,
        out_specs=[vmem] * 9 + [hbm] * 5,
        out_shape=[
            jax.ShapeDtypeStruct((SEQ, D), BF),
            jax.ShapeDtypeStruct((SEQ, HEADS * HD), BF),
            jax.ShapeDtypeStruct((SEQ, 128), BF),
            jax.ShapeDtypeStruct((SEQ, 128), BF),
            jax.ShapeDtypeStruct((HEADS * HD, SEQ), BF),
            jax.ShapeDtypeStruct((8, SEQ), F32),
            jax.ShapeDtypeStruct((LOCAL, D), F32),
            jax.ShapeDtypeStruct((LOCAL, D), BF),
            jax.ShapeDtypeStruct((LOCAL, 128), F32),
            *[QUAD_SHAPE] * 4,
            jax.ShapeDtypeStruct((8, LOCAL, D), BF),
        ],
        scratch_shapes=[
            pltpu.VMEM((SEQ, BLOCK), F32),
            pltpu.VMEM((4, LOCAL, D), BF),
            pltpu.VMEM((SEQ, HEADS * HD), BF),
            pltpu.VMEM((2, 2, *BLOCK_SHAPE), BF),
            *pair_scratch(LOCAL, D),
            pltpu.SemaphoreType.DMA((sems,)),
            pltpu.SemaphoreType.DMA((sems,)),
            pltpu.SemaphoreType.DMA((9,)),
        ],
        compiler_params=pltpu.CompilerParams(
            collective_id=ident, has_side_effects=True, vmem_limit_bytes=56 * MIB
        ),
        name="front",
    )(hidden, weights, *tables, segments, own_hidden, named, out_grad, *lines)


def back_kernel(
    dx, dgate, gating, middle, normed_moe, out_grad, y_part,
    normed, weights, cosine, sine, segments, query, key, value, context_t, log_total,
    expert_a, expert_b, dmiddle, dn1, grads, block_out, sum_a, sum_b,
    bias, dcontext, dquery_t, dkey, dvalue, dall, dall_t, dattn_own, dattn_all, y_sum, *refs,
):
    ring_refs = refs[:8]
    send, recv, here, load = refs[22:]
    at = Place()
    greet(
        [
            at.sibling(), at.partner(), at.ring(1), at.ring(3),
            at.along("x", 1), at.along("x", 3), at.along("z", 1), at.along("z", 3),
        ]
    )
    base = 9 + 2 * PIECES
    sums = [
        RingSum(at, "x", expert_a, refs[8:15], send, recv, load, base),
        RingSum(at, "z", expert_b, refs[15:22], send, recv, load, base + RingSum.COPIES, 3),
    ]
    for each in sums:
        each.begin()
    gain = gain_rows(weights)[1:2, :]
    chosen = gating[...]
    dchosen = chosen * (dgate[...] - jnp.sum(chosen * dgate[...], axis=-1, keepdims=True))
    dlogits = dchosen.astype(BF)
    dnormed = dx[...] + mm_last(dlogits, weights[:, 768:896])
    values = middle[...]
    scale = lax.rsqrt(jnp.mean(values * values, axis=-1, keepdims=True) + EPS)
    unit = values * scale
    weighted = dnormed * gain
    inner = jnp.mean(weighted * unit, axis=-1, keepdims=True)
    total = out_grad[...].astype(F32) + scale * (weighted - unit * inner)
    dmiddle[...] = total
    dattn_own[...] = total.astype(BF)
    gather = PairGather(at, dattn_own, dattn_all, send, recv, here, 8, PIECES)
    scatter = RingScatter(at, y_part, ring_refs, send, recv)
    for k in (2, 1, 3, 0):
        scatter.copy(k).start()
    router_part = mm(normed_moe[...].T, dlogits)
    gain_part = column_of(jnp.sum(dnormed * unit, axis=0, keepdims=True))
    lane = lax.broadcasted_iota(jnp.int32, (D, 128), 1)
    grads[:, 768:] = jnp.where(lane == 32, gain_part, router_part).astype(BF)
    seg_row = segment_row(segments)
    seg_column = column_of(seg_row)
    gather.forward()
    scatter.far()
    gather.finish()
    dattn = dattn_all[...].reshape(SEQ, D)
    dcontext[...] = mm(dattn, weights[:, 512:768]).astype(BF)
    output_grad_t = mm(context_t[...], dattn)
    grads[:, 512:768] = output_grad_t.T.astype(BF)
    key_t = key[...].astype(F32).T.astype(BF)
    dkey[...] = jnp.zeros_like(dkey)
    dvalue[...] = jnp.zeros_like(dvalue)
    for block in range(SEQ // BLOCK):
        first, end = block * BLOCK, (block + 1) * BLOCK
        bias[:end, :] = bias_block(seg_column[:end, :], seg_row[:, first:end], first, end)
        for head in range(HEADS):
            kv = slice((head // 2) * HD, (head // 2) * HD + HD)
            own = slice(head * HD, head * HD + HD)
            query_block = query[first:end, own]
            dcontext_block = dcontext[first:end, own]
            scores = mm_last(key[:end, kv], query_block) + bias[:end, :]
            share = jnp.exp(scores - log_total[head : head + 1, first:end])
            dshare = mm_last(value[:end, kv], dcontext_block)
            centre = jnp.sum(share * dshare, axis=0, keepdims=True)
            dscore = (share * (dshare - centre)).astype(BF)
            dquery_t[own, first:end] = mm(key_t[kv, :end], dscore) * 0.125
            dkey[:end, kv] += mm(dscore, query_block)
            dvalue[:end, kv] += mm(share.astype(BF), dcontext_block)
        if block == 0:
            scatter.up_side()
            scatter.down_side()
        if block == 2:
            for each in sums:
                each.middle()
    turn = -sine[...]
    for half in range(2):
        rows = slice(half * 128, half * 128 + 128)
        piece = rotated(dquery_t[rows, :].T, cosine[...], turn)
        dall[:, rows] = piece.astype(BF)
        dall_t[rows, :] = piece.T.astype(BF)
    piece = rotated(dkey[...], cosine[...], turn)
    dall[:, 256:384] = piece.astype(BF)
    dall_t[256:384, :] = piece.T.astype(BF)
    dall[:, 384:512] = dvalue[...].astype(BF)
    dall_t[384:512, :] = dvalue[...].T.astype(BF)
    grads[:, 0:512] = mm(dall_t[...], normed[...]).T.astype(BF)
    for block in range(SEQ // BLOCK):
        rows = slice(block * BLOCK, (block + 1) * BLOCK)
        dn1[rows, :] = mm_last(dall[rows, :], weights[:, 0:512]).astype(BF)
    scatter.finish(y_sum)
    block_out[...] = (y_sum[...] + middle[...]).astype(BF)
    for each, out in zip(sums, (sum_a, sum_b)):
        each.finish(out)


def back(
    dx, dgate, gating, middle, normed_moe, out_grad, y_part,
    normed, weights, tables, segments, kept, expert_grads, ident,
):
    vmem = pl.BlockSpec(memory_space=pltpu.VMEM)
    hbm = pl.BlockSpec(memory_space=pl.ANY)
    sems = 9 + 2 * PIECES + 2 * RingSum.COPIES
    return pl.pallas_call(
        back_kernel,
        in_specs=[vmem] * 17 + [hbm] * 2,
        out_specs=[vmem] * 6,
        out_shape=[
            jax.ShapeDtypeStruct((LOCAL, D), F32),
            jax.ShapeDtypeStruct((SEQ, D), BF),
            jax.ShapeDtypeStruct((D, SMALL), BF),
            jax.ShapeDtypeStruct((LOCAL, D), BF),
            SUMS_SHAPE,
            SUMS_SHAPE,
        ],
        scratch_shapes=[
            pltpu.VMEM((SEQ, BLOCK), F32),
            pltpu.VMEM((SEQ, HEADS * HD), BF),
            pltpu.VMEM((HEADS * HD, SEQ), F32),
            pltpu.VMEM((SEQ, 128), F32),
            pltpu.VMEM((SEQ, 128), F32),
            pltpu.VMEM((SEQ, 512), BF),
            pltpu.VMEM((512, SEQ), BF),
            pltpu.VMEM((LOCAL, D), BF),
            pltpu.VMEM((4, LOCAL, D), BF),
            pltpu.VMEM((LOCAL, D), F32),
            *ring_scratch(LOCAL, D),
            *sum_scratch(SUMS_SHAPE.shape),
            *sum_scratch(SUMS_SHAPE.shape),
            pltpu.SemaphoreType.DMA((sems,)),
            pltpu.SemaphoreType.DMA((sems,)),
            pltpu.SemaphoreType.DMA,
            pltpu.SemaphoreType.DMA((6,)),
        ],
        compiler_params=pltpu.CompilerParams(
            collective_id=ident, has_side_effects=True, vmem_limit_bytes=62 * MIB
        ),
        name="back",
    )(
        dx, dgate, gating, middle, normed_moe, out_grad, y_part,
        normed, weights, *tables, segments, *kept, *expert_grads,
    )


def experts_kernel(
    x_in, gate_in, d_in, quad_0a, quad_0b, quad_1a, quad_1b, over_z, over_x,
    y_out, dx_out, dgate_out, grads_a, grads_b, quad_2a, quad_2b, quad_3a, quad_3b,
    x, d, xt, dt, y, dx, gating, dgate, dgate_part, hidden, w, *refs,
):
    dx_scratch, dgate_scratch = refs[:5], refs[5:10]
    send, recv, here, load, store, fetch = refs[10:16]
    at = Place()
    step = pl.program_id(0)
    opening, closing = step == 0, step == STEPS - 1
    rows_at_once = 2 * LOCAL
    lane = lax.broadcasted_iota(jnp.int32, (LOCAL, 128), 1)
    own_first = at.yh * 16 + step * QUAD
    x_gather = RingGather(at, x_in, x, send, recv, here.at[0], 0)
    gate_gather = RingGather(at, gate_in, gating, send, recv, here.at[1], 9)
    gathers = (x_gather, gate_gather)
    scatters = (
        RingScatter(at, d, dx_scratch, send, recv, 18),
        RingScatter(at, dgate_part, dgate_scratch, send, recv, 26),
    )

    quads = [
        second_gather(
            at, 2 + i, over_z, over_x, *quad, *refs[16:18], refs[18].at[pl.ds(4 * i, 4)],
            SpreadOut.COPIES * i, refs[19],
        )
        for i, quad in enumerate(((quad_2a, quad_2b), (quad_3a, quad_3b)))
    ]

    def ride(condition, what):
        for i, quad in enumerate(quads):

            @pl.when(condition & (step == i))
            def _():
                what(quad)

    def fetches(quad_a, quad_b):
        copies = []
        for g in range(3):
            for i in range(QUAD):
                columns = pl.ds((g * QUAD + i) * FF, FF)
                if i < 2:
                    parts = [(quad_a.at[:, :, :, g, i], w.at[:, :, :, :, columns])]
                else:
                    parts = [
                        (quad_b.at[:, x_at, :, g, i - 2], w.at[x_at, :, :, :, columns])
                        for x_at in range(4)
                    ]
                for part in parts:
                    copies.append(pltpu.make_async_copy(*part, fetch.at[len(copies)]))
        return copies

    def d_load(chip):
        two = pl.ds(chip * 2, 2)
        return pltpu.make_async_copy(d_in.at[two], d.at[two], load.at[chip])

    def y_store(chip):
        two = pl.ds(chip * 2, 2)
        return pltpu.make_async_copy(x.at[two], y_out.at[two], store.at[chip])

    @pl.when(opening)
    def _():
        greet(
            [
                at.sibling(), at.ring(1), at.ring(3),
                at.along("x", 1), at.along("x", 3), at.along("z", 1), at.along("z", 3),
            ]
        )
        for gather in gathers:
            gather.begin()
        for copy in fetches(quad_0a, quad_0b):
            copy.start()
        for chip in range(4):
            d_load(chip).start()

    for copy in fetches(quad_0a, quad_0b):
        copy.wait()

    ride(step < STEPS, lambda quad: quad.begin())

    def arrive(turn):
        @pl.when(turn == 0)
        def _():
            for gather in gathers:
                gather.kept().wait()
                gather.copy(0).wait_recv()

        @pl.when(turn == 1)
        def _():
            for gather in gathers:
                gather.forward_before()
                gather.forward_behind()
            for gather in gathers:
                gather.copy(4).wait_recv()

        @pl.when(turn == 2)
        def _():
            for gather in gathers:
                gather.forward_across()
            for gather in gathers:
                gather.copy(6).wait_recv()

        @pl.when(turn == 3)
        def _():
            for gather in gathers:
                gather.copy(7).wait_recv()
                gather.copy(8).wait_recv()

    def leave(turn):
        @pl.when(turn == 0)
        def _():
            for scatter in scatters:
                scatter.copy(2).start()

        @pl.when(turn == 1)
        def _():
            for scatter in scatters:
                scatter.copy(1).start()
                scatter.far()

        @pl.when(turn == 2)
        def _():
            for scatter in scatters:
                scatter.copy(3).start()
                scatter.up_side()

        @pl.when(turn == 3)
        def _():
            for scatter in scatters:
                scatter.copy(0).start()
                scatter.down_side()

    def tokens_block(turn, carry):
        inward = jnp.where(turn == 0, 0, jnp.where(turn == 1, 3, turn - 1))
        outward = jnp.where(turn == 0, 2, jnp.where(turn == 3, 0, turn * 2 - 1))
        chip = at.chip(jnp.where(closing, outward, inward))
        two = pl.ds(chip * 2, 2)
        rows = pl.ds(pl.multiple_of(chip * rows_at_once, rows_at_once), rows_at_once)

        @pl.when(opening)
        def _():
            arrive(turn)
            d_load(chip).wait()
            xt[:, rows] = x[two].reshape(rows_at_once, D).T
            dt[:, rows] = d[two].reshape(rows_at_once, D).T
            y[rows, :] = jnp.zeros((rows_at_once, D), F32)
            dx[rows, :] = jnp.zeros((rows_at_once, D), F32)
            dgate[rows, :] = jnp.zeros((rows_at_once, 128), F32)

        ride(turn == 3, lambda quad: quad.forward())
        gate_up = w[:, :, :, :, 0 : 2 * F].reshape(D, 2 * F)
        down = w[:, :, :, :, 2 * F :].reshape(D, F)
        for core in range(2):
            slot = chip * 2 + core
            part = pl.ds(pl.multiple_of(slot * LOCAL, LOCAL), LOCAL)
            both = mm(x[slot], gate_up)
            gate, up = both[:, :F], both[:, F:]
            dact = mm(d[slot], down)
            turned = pltpu.roll(gating[slot], lax.rem(128 - own_first, 128), 1)
            factor = jnp.concatenate(
                [jnp.broadcast_to(turned[:, i : i + 1], (LOCAL, FF)) for i in range(QUAD)],
                axis=1,
            )
            q = 1.0 / (1.0 + jnp.exp(-gate))
            silu = gate * q
            act = silu * up
            product = act * dact
            sums = dgate[part, :]
            for i in range(QUAD):
                own = jnp.sum(product[:, i * FF : (i + 1) * FF], axis=1, keepdims=True)
                sums = jnp.where(lane == own_first + i, own, sums)
            dgate[part, :] = sums
            dact = dact * factor
            hidden[part, 0:F] = (dact * up * (q + silu * (1.0 - q))).astype(BF)
            hidden[part, F : 2 * F] = (dact * silu).astype(BF)
            hidden[part, 2 * F :] = (act * factor).astype(BF)
        y[rows, :] += mm_last(hidden[rows, 2 * F :], down)
        dx[rows, :] += mm_last(hidden[rows, 0 : 2 * F], gate_up)

        @pl.when(closing)
        def _():
            x[two] = y[rows, :].astype(BF).reshape(2, LOCAL, D)
            d[two] = dx[rows, :].astype(BF).reshape(2, LOCAL, D)
            dgate_part[two] = dgate[rows, :].astype(BF).reshape(2, LOCAL, 128)
            y_store(chip).start()
            leave(turn)

        return carry

    lax.fori_loop(0, 4, tokens_block, 0)

    later = ((quad_1a, quad_1b), (quad_2a, quad_2b), (quad_3a, quad_3b))
    for number, quad in enumerate(later):

        @pl.when(step == number)
        def _():
            for copy in fetches(*quad):
                copy.start()

    @pl.when(opening)
    def _():
        for gather in gathers:
            gather.sent()

    def grads_block(block, carry):
        rows = pl.ds(pl.multiple_of(block * 512, 512), 512)

        def put(g, value):
            value = value.astype(BF).reshape(2, 4, 2, 32, value.shape[1])
            for j in range(value.shape[-1] // FF):
                piece = value[..., j * FF : (j + 1) * FF]
                group, i = g + j // QUAD, j % QUAD
                for x_at in range(2):
                    if i < 2:
                        grads_a[block * 2 + x_at, :, :, 0, group, i] = piece[x_at]
                    else:
                        grads_b[:, block * 2 + x_at, :, 0, group, i - 2] = piece[x_at]

        put(0, mm(xt[rows, :], hidden[:, 0 : 2 * F]))
        put(2, mm(dt[rows, :], hidden[:, 2 * F :]))
        return carry

    lax.fori_loop(0, D // 512, grads_block, 0)
    ride(step < STEPS, lambda quad: quad.finish())

    @pl.when(closing)
    def _():
        scatters[0].finish(dx_out)
        scatters[1].finish(dgate_out)
        for chip in range(4):
            y_store(chip).wait()


def experts(x, gating, d, quads, lines, ident):
    hbm = pl.BlockSpec(memory_space=pl.ANY)

    def whole(rows, columns):
        return pl.BlockSpec((rows, columns), lambda step: (0, 0), pipeline_mode=pl.Buffered(1))

    each_step = pl.BlockSpec(
        (4, 4, 2, 1, 3, 2, 32, FF),
        lambda step: (0, 0, 0, step, 0, 0, 0, 0),
        pipeline_mode=pl.Buffered(1),
    )
    return pl.pallas_call(
        experts_kernel,
        grid=(STEPS,),
        in_specs=[hbm] * 9,
        out_specs=[
            hbm,
            whole(LOCAL, D),
            whole(LOCAL, 128),
            each_step,
            each_step,
            *[hbm] * 4,
        ],
        out_shape=[
            jax.ShapeDtypeStruct((8, LOCAL, D), BF),
            jax.ShapeDtypeStruct((LOCAL, D), F32),
            jax.ShapeDtypeStruct((LOCAL, 128), F32),
            GRADS_SHAPE,
            GRADS_SHAPE,
            *[QUAD_SHAPE] * 4,
        ],
        scratch_shapes=[
            pltpu.VMEM((8, LOCAL, D), BF),
            pltpu.VMEM((8, LOCAL, D), BF),
            pltpu.VMEM((D, TOKENS), BF),
            pltpu.VMEM((D, TOKENS), BF),
            pltpu.VMEM((TOKENS, D), F32),
            pltpu.VMEM((TOKENS, D), F32),
            pltpu.VMEM((8, LOCAL, 128), F32),
            pltpu.VMEM((TOKENS, 128), F32),
            pltpu.VMEM((8, LOCAL, 128), BF),
            pltpu.VMEM((TOKENS, 3 * F), BF),
            pltpu.VMEM((4, 4, 2, 32, 3 * F), BF),
            *ring_scratch(LOCAL, D, False),
            *ring_scratch(LOCAL, 128, False),
            pltpu.SemaphoreType.DMA((34,)),
            pltpu.SemaphoreType.DMA((34,)),
            pltpu.SemaphoreType.DMA((2,)),
            pltpu.SemaphoreType.DMA((4,)),
            pltpu.SemaphoreType.DMA((4,)),
            pltpu.SemaphoreType.DMA((30,)),
            pltpu.SemaphoreType.DMA((2 * SpreadOut.COPIES,)),
            pltpu.SemaphoreType.DMA((2 * SpreadOut.COPIES,)),
            pltpu.SemaphoreType.DMA((8,)),
            pltpu.VMEM((2, *BLOCK_SHAPE), BF),
        ],
        compiler_params=pltpu.CompilerParams(
            collective_id=ident, has_side_effects=True, vmem_limit_bytes=63 * MIB
        ),
        name="experts",
    )(x, gating, d, *quads, *lines)[:5]


def norm_scale(values):
    return lax.rsqrt(jnp.mean(values * values, axis=-1, keepdims=True) + EPS)


def norm_grad(values, gain, dnormed):
    scale = norm_scale(values)
    unit = values * scale
    weighted = dnormed * gain
    dvalues = scale * (weighted - unit * jnp.mean(weighted * unit, axis=-1, keepdims=True))
    return dvalues


def on_device(
    hidden_in, out_grad, attn_gain, query_weight, key_weight, value_weight, output_weight,
    moe_gain, router_weight, expert_gate, expert_up, expert_down, expert_ids, segment_ids,
):
    small = jnp.concatenate(
        [
            query_weight, key_weight, value_weight, output_weight,
            router_weight, attn_gain[:, None], moe_gain[:, None], jnp.zeros((32, 94), BF),
        ],
        axis=1,
    )
    segment = jnp.pad(segment_ids.reshape(2, 128), ((0, 6), (0, 0)))
    own_shares = (expert_gate, expert_up, expert_down)
    hidden_all, segments, small, *lines = startup(hidden_in, segment, small, own_shares, 0)
    tables = tuple(jnp.asarray(t) for t in rotary_tables())
    named = jnp.any(
        expert_ids[:, :, None] == jnp.arange(128, dtype=jnp.int32)[None, None, :], axis=1
    ).astype(F32)

    normed, *more, d = front(
        hidden_all, small, tables, segments, hidden_in, named, out_grad, lines, 1
    )
    kept, (middle, normed_moe, gating), quads = more[:5], more[5:8], more[8:]
    y, dx, dgate, *expert_grads = experts(normed_moe, gating, d, quads, lines, 3)
    dmiddle, dn1, grads, block_out, *sums = back(
        dx, dgate, gating, middle, normed_moe, out_grad, y,
        normed, small, tables, segments, kept, expert_grads, 5,
    )
    weights = jnp.concatenate([query_weight, key_weight, value_weight], axis=1)
    dn1, attention_grads, rest, *expert_grads = final(dn1, grads, weights, sums, 6)
    hidden = hidden_in.astype(F32)
    dhidden = norm_grad(hidden, small[:, 800].astype(F32), dn1)
    hidden_grad = dmiddle + dhidden
    expert_grads = [share.reshape(E, 32, FF) for share in expert_grads]
    return (
        block_out,
        hidden_grad,
        rest[:, 33] / attn_gain.astype(F32),
        attention_grads[:, 0:256],
        attention_grads[:, 256:384],
        attention_grads[:, 384:512],
        attention_grads[:, 512:768],
        rest[:, 32],
        rest[:, :32],
        *expert_grads,
    )


def solution(mesh):
    fine = Mesh(np.asarray(mesh.devices).reshape(4, 4, 2, 2, 2), ALL)
    return jax.shard_map(
        on_device,
        mesh=fine,
        in_specs=(
            P(ALL, None),
            P(ALL, None),
            P(DP),
            P(DP, TENSOR),
            P(DP, TENSOR),
            P(DP, TENSOR),
            P(DP, TENSOR),
            P(DP),
            P(DP, None),
            P(None, DP, TENSOR),
            P(None, DP, TENSOR),
            P(None, DP, TENSOR),
            P(ALL, None),
            P(ALL),
        ),
        out_specs=(
            P(ALL, None),
            P(ALL, None),
            P(DP),
            P(DP, TENSOR),
            P(DP, TENSOR),
            P(DP, TENSOR),
            P(DP, TENSOR),
            P(DP),
            P(DP, None),
            P(None, DP, TENSOR),
            P(None, DP, TENSOR),
            P(None, DP, TENSOR),
        ),
        check_vma=False,
    )
```

```python
import jax
import jax.numpy as jnp
import numpy as np
from jax import lax
from jax.experimental import pallas as pl
from jax.experimental.pallas import tpu as pltpu
from jax.sharding import Mesh
from jax.sharding import PartitionSpec as P

D = 1024
HD = 64
E = 32
SEQ = 1024
LOCAL = 256
HEADS = 4
QUAD = 4
FF = 128
F = QUAD * FF
EPS = 1e-06
TOPK = 8
MASKED = -1e30
BLOCK = 256
TOKENS = 2048
STEPS = 4

DP = ("x", "z", "yh")
TENSOR = ("yl", "core")
RING = ("yh", "yl", "core")
PLANE = ("x", "z")
ALL = ("x", "z", "yh", "yl", "core")

F32 = jnp.float32
BF = jnp.bfloat16
LAST = (((1,), (1,)), ((), ()))
MIB = 1024 * 1024
MESH = pl.DeviceIdType.MESH
SMALL = 896


def mm(a, b):
    return jnp.dot(a, b, preferred_element_type=F32)


def mm_last(a, b):
    return lax.dot_general(a, b, LAST, preferred_element_type=F32)


class Place:
    def __init__(self):
        self.x = lax.axis_index("x")
        self.z = lax.axis_index("z")
        self.yh = lax.axis_index("yh")
        self.yl = lax.axis_index("yl")
        self.core = lax.axis_index("core")
        self.y = self.yh * 2 + self.yl

    def chip(self, k):
        return lax.rem(self.y + k, 4)

    def ring(self, k):
        chip = self.chip(k)
        return {"yh": chip // 2, "yl": lax.rem(chip, 2)}

    def along(self, axis, k):
        return {axis: lax.rem(getattr(self, axis) + k, 4)}

    def sibling(self):
        return {"core": 1 - self.core}

    def partner(self):
        return {"yl": 1 - self.yl}

    def diagonal(self):
        return {"yl": 1 - self.yl, "core": 1 - self.core}

    def opposite(self):
        return {"yh": 1 - self.yh}


def greet(devices):
    barrier = pltpu.get_barrier_semaphore()
    for device in devices:
        pl.semaphore_signal(barrier, inc=1, device_id=device, device_id_type=MESH)
    pl.semaphore_wait(barrier, len(devices))


def remote(src, dst, send, recv, i, device):
    return pltpu.make_async_remote_copy(
        src_ref=src, dst_ref=dst, send_sem=send.at[i], recv_sem=recv.at[i],
        device_id=device, device_id_type=MESH,
    )


def push(src, dst, send, recv, i, device):
    copy = remote(src, dst, send, recv, i, device)
    copy.start()
    return copy


def keep(src, dst, sem):
    copy = pltpu.make_async_copy(src, dst, sem)
    copy.start()
    return copy


class RingGather:
    def __init__(self, at, own, out, send, recv, here, base=0):
        self.at, self.own, self.out, self.base = at, own, out, base
        self.send, self.recv, self.here = send, recv, here
        half = own.shape[0] // 2
        lo, hi = pl.ds(0, half), pl.ds(half, half)
        me, before, behind, across = (out.at[self.slot(k)] for k in (0, 3, 1, 2))
        near, up, down = at.sibling(), at.ring(1), at.ring(3)
        self.plan = [
            (own, me, near),
            (own, me, up),
            (own, me, down),
            (before.at[lo], before.at[lo], up),
            (before, before, near),
            (behind.at[hi], behind.at[hi], down),
            (behind, behind, near),
            (across.at[lo], across.at[lo], near),
            (across.at[hi], across.at[hi], near),
        ]

    def slot(self, k):
        return self.at.chip(k) * 2 + self.at.core

    def copy(self, i):
        src, dst, device = self.plan[i]
        return remote(src, dst, self.send, self.recv, self.base + i, device)

    def kept(self):
        return pltpu.make_async_copy(self.own, self.out.at[self.slot(0)], self.here)

    def begin(self):
        self.kept().start()
        for i in (1, 2, 0):
            self.copy(i).start()

    def forward_before(self):
        self.copy(1).wait_recv()
        self.copy(3).start()
        self.copy(4).start()

    def forward_behind(self):
        self.copy(2).wait_recv()
        self.copy(5).start()
        self.copy(6).start()

    def forward_across(self):
        self.copy(3).wait_recv()
        self.copy(7).start()
        self.copy(5).wait_recv()
        self.copy(8).start()

    def sent(self):
        for i in range(9):
            self.copy(i).wait_send()


class PairGather:
    def __init__(self, at, own, out, send, recv, here, base, pieces):
        self.at, self.out, self.send, self.recv, self.base = at, out, send, recv, base
        size = own.shape[0] // pieces
        self.parts = [pl.ds(i * size, size) for i in range(pieces)]
        me = at.yl * 2 + at.core
        self.other = (1 - at.yl) * 2 + at.core
        self.kept = keep(own, out.at[me], here)
        self.far = [
            push(own.at[part], out.at[me, part], send, recv, base + 1 + i, at.partner())
            for i, part in enumerate(self.parts)
        ]
        self.near = [push(own, out.at[me], send, recv, base, at.sibling())]

    def forward(self):
        for i, part in enumerate(self.parts):
            self.far[i].wait_recv()
            view = self.out.at[self.other, part]
            index = self.base + 1 + len(self.parts) + i
            self.near.append(push(view, view, self.send, self.recv, index, self.at.sibling()))

    def finish(self):
        for copy in self.near:
            copy.wait_recv()
        for copy in (*self.far, *self.near):
            copy.wait_send()
        self.kept.wait()


PIECES = 4


class AxisGather:
    def __init__(self, at, axis, view, send, recv, base):
        self.up, self.down = at.along(axis, 1), at.along(axis, 3)
        self.view, self.send, self.recv, self.base = view, send, recv, base

    def go(self, i, view, device):
        return push(view, view, self.send, self.recv, self.base + i, device)

    def begin(self):
        self.first = [
            self.go(0, self.view(0, "all"), self.up), self.go(1, self.view(0, "all"), self.down),
        ]

    def forward(self):
        self.first[0].wait_recv()
        self.far = [self.go(2, self.view(3, "low"), self.up)]
        self.first[1].wait_recv()
        self.far.append(self.go(3, self.view(1, "high"), self.down))

    def finish(self):
        for copy in self.far:
            copy.wait_recv()
        for copy in (*self.first, *self.far):
            copy.wait_send()


def halves_of(ref, first, size):
    spans = {"all": (0, size), "low": (0, size // 2), "high": (size // 2, size // 2)}
    return lambda part: ref.at[pl.ds(first + spans[part][0], spans[part][1])]


class SpreadOut:
    COPIES = 8

    def __init__(self, at, rings, send, recv, here, base=0, through=None):
        self.send, self.recv, self.here, self.base = send, recv, here, base
        self.through = through
        self.own = [(own, slot(0)) for _, own, slot, _ in rings]
        self.plan = []
        for axis, own, slot, _ in rings:
            self.plan.append((own, slot(0), at.along(axis, 1)))
            self.plan.append((own, slot(0), at.along(axis, 3)))
        for axis, _, slot, half in rings:
            low, high = (slot(3).at[pl.ds(0, half)], slot(1).at[pl.ds(half, half)])
            self.plan.append((low, low, at.along(axis, 1)))
            self.plan.append((high, high, at.along(axis, 3)))

    def copy(self, i):
        src, dst, device = self.plan[i]
        return remote(src, dst, self.send, self.recv, self.base + i, device)

    def loaded(self, i):
        return pltpu.make_async_copy(self.own[i][0], self.through.at[i], self.here.at[i])

    def kept(self, i):
        src, dst = self.own[i]
        src = src if self.through is None else self.through.at[i]
        return pltpu.make_async_copy(src, dst, self.here.at[2 + i])

    def begin(self):
        for i in range(4):
            self.copy(i).start()
        for i in range(2):
            (self.kept(i) if self.through is None else self.loaded(i)).start()

    def forward(self):
        for i in range(4):
            self.copy(i).wait_recv()
            self.copy(4 + i).start()
        if self.through is not None:
            for i in range(2):
                self.loaded(i).wait()
                self.kept(i).start()

    def finish(self):
        for i in range(4, 8):
            self.copy(i).wait_recv()
        for i in range(8):
            self.copy(i).wait_send()
        for i in range(2):
            self.kept(i).wait()


def ring_slots(out, place):
    return lambda k: out.at[lax.rem(place + k, 4)]


def first_gather(at, own_a, own_b, over_z, over_x, *sems):
    rings = (
        ("z", own_a, ring_slots(over_z, at.z), 1), ("x", own_b, ring_slots(over_x, at.x), 1),
    )
    return SpreadOut(at, rings, *sems)


def second_gather(at, number, over_z, over_x, quad_a, quad_b, *sems):
    rings = (
        ("x", over_z.at[:, :, number], ring_slots(quad_a, at.x), 2),
        ("z", over_x.at[:, :, number], ring_slots(quad_b, at.z), 2),
    )
    return SpreadOut(at, rings, *sems)


SHARE_SHAPE = jax.ShapeDtypeStruct((2, STEPS, 3, 2, 32, FF), BF)
BLOCK_SHAPE = (4, 2, 3, 2, 32, FF)
LINE_SHAPE = jax.ShapeDtypeStruct((4, 2, STEPS, 3, 2, 32, FF), BF)
QUAD_SHAPE = jax.ShapeDtypeStruct((4, 4, 2, 3, 2, 32, FF), BF)
GRADS_SHAPE = jax.ShapeDtypeStruct((4, 4, 2, STEPS, 3, 2, 32, FF), BF)
SUMS_SHAPE = jax.ShapeDtypeStruct((4, 2, STEPS, 3, 2, 32, FF), BF)


class RingSum:
    COPIES = 6

    def __init__(self, at, axis, part_of, scratch, send, recv, load, base=0, first=0):
        half_a, half_b, up, down, to_up, to_down, own = scratch
        self.half_a, self.half_b, self.up, self.down = half_a, half_b, up, down
        self.to_up, self.to_down, self.own = to_up, to_down, own
        self.send, self.recv, self.base = send, recv, base
        size = half_a.shape[0]
        lo, hi = pl.ds(0, size), pl.ds(size, size)
        place = {"x": at.x, "z": at.z}[axis]
        here, above, across, below = (part_of(lax.rem(place + k, 4)) for k in range(4))
        upper, lower = at.along(axis, 1), at.along(axis, 3)
        self.plan = [
            (across.at[lo], half_a, upper),
            (across.at[hi], half_b, lower),
            (above.at[hi], up.at[hi], upper),
            (below.at[lo], down.at[lo], lower),
            (to_up, up.at[lo], upper),
            (to_down, down.at[hi], lower),
        ]
        self.loads = [
            pltpu.make_async_copy(src, dst, load.at[first + i])
            for i, (src, dst) in enumerate(
                ((above.at[lo], to_up), (below.at[hi], to_down), (here, own))
            )
        ]

    def copy(self, i):
        src, dst, device = self.plan[i]
        return remote(src, dst, self.send, self.recv, self.base + i, device)

    def begin(self):
        for i in range(2):
            self.copy(i).start()
        for load in self.loads:
            load.start()

    def direct(self):
        for i in (2, 3):
            self.copy(i).start()

    def middle(self):
        for i, (total, landed) in enumerate(
            ((self.to_up, self.half_a), (self.to_down, self.half_b))
        ):
            self.loads[i].wait()
            self.copy(i).wait_recv()

            def add(i, carry, total=total, landed=landed):
                total[i] = (total[i].astype(F32) + landed[i].astype(F32)).astype(BF)
                return carry

            lax.fori_loop(0, total.shape[0], add, 0)
            self.copy(4 + i).start()

    def finish(self, out):
        self.loads[2].wait()
        for i in range(2, 6):
            self.copy(i).wait_recv()

        def add(i, carry):
            total = self.own[i].astype(F32) + self.up[i].astype(F32)
            out[i] = (total + self.down[i].astype(F32)).astype(out.dtype)
            return carry

        lax.fori_loop(0, out.shape[0], add, 0)
        for i in range(6):
            self.copy(i).wait_send()


def sum_scratch(block):
    half, whole = pltpu.VMEM((block[0] // 2, *block[1:]), BF), pltpu.VMEM(block, BF)
    return [half, half, whole, whole, half, half, whole]


def startup_kernel(
    hidden, segment_rows, query, key, value, output, router, gains, gate, up, down,
    hidden_all, segment_all, small_all, share_a, share_b, small, segment, send, recv, here,
):
    at = Place()
    greet(
        [
            at.sibling(), at.partner(), at.diagonal(), at.opposite(),
            at.along("x", 1), at.along("x", 3), at.along("z", 1), at.along("z", 3),
        ]
    )
    small[:, 0:256] = query[...]
    small[:, 256:384] = key[...]
    small[:, 384:512] = value[...]
    small[:, 512:768] = output[...]
    columns = jnp.broadcast_to(gains[...].astype(F32)[:, None, :], (2, 8, 32))
    columns = [columns[i].T[:, 0:1].astype(BF) for i in range(2)]
    blank = jnp.zeros((32, 94), BF)
    small[:, 768:896] = jnp.concatenate([router[...], *columns, blank], axis=1)
    segment[0:2, :] = segment_rows[...]
    segment[2:8, :] = jnp.zeros((6, 128), jnp.int32)
    rank = at.yl * 2 + at.core
    mine = small_all.at[(at.x * 4 + at.z) * 2 + at.yh]
    small_kept = keep(small, mine, here.at[0])
    copies = [push(small, mine, send, recv, 0, at.opposite())]
    swaps, swaps_kept = [], []
    base = 13 + 2 * PIECES
    for i, share in enumerate((gate, up, down)):
        for j, out in enumerate((share_a, share_b)):
            dst, two = out.at[at.yh, :, i], pl.ds(2 * j, 2)
            theirs = share.at[pl.ds((1 - at.yh) * STEPS, STEPS), two]
            index = 2 * i + j
            swaps.append(push(theirs, dst, send, recv, base + index, at.opposite()))
            own = share.at[pl.ds(at.yh * STEPS, STEPS), two]
            swaps_kept.append(keep(own, dst, here.at[3 + index]))
    copies.extend(
        push(segment, segment_all.at[rank], send, recv, 1 + i, device)
        for i, device in enumerate((at.sibling(), at.partner(), at.diagonal()))
    )
    pair = PairGather(at, hidden, hidden_all, send, recv, here.at[1], 12, PIECES)
    seg_here = keep(segment, segment_all.at[rank], here.at[2])
    over_z = AxisGather(
        at, "z",
        lambda k, part: halves_of(small_all, (at.x * 4 + lax.rem(at.z + k, 4)) * 2, 2)(part),
        send, recv, 4,
    )
    over_x = AxisGather(
        at, "x", lambda k, part: halves_of(small_all, lax.rem(at.x + k, 4) * 8, 8)(part),
        send, recv, 8,
    )
    small_kept.wait()
    copies[0].wait_recv()
    over_z.begin()
    over_z.forward()
    over_z.finish()
    over_x.begin()
    pair.forward()
    for swap, own in zip(swaps, swaps_kept):
        swap.wait_recv()
        own.wait()
    over_x.forward()
    pair.finish()
    seg_here.wait()
    for copy in copies[1:]:
        copy.wait_recv()
    over_x.finish()
    for copy in (*copies, *swaps):
        copy.wait_send()


def startup(hidden, segment, smalls, shares, ident):
    hbm = pl.BlockSpec(memory_space=pl.ANY)
    vmem = pl.BlockSpec(memory_space=pltpu.VMEM)
    sems = 13 + 2 * PIECES + 6
    shares = [share.reshape(2 * STEPS, QUAD, 32, FF) for share in shares]
    hidden_all, segment_all, small_all, share_a, share_b = pl.pallas_call(
        startup_kernel,
        in_specs=[vmem] * 8 + [hbm] * 3,
        out_specs=[hbm] * 3 + [vmem] * 2,
        out_shape=[
            jax.ShapeDtypeStruct((4, *hidden.shape), hidden.dtype),
            jax.ShapeDtypeStruct((4, 8, 128), segment.dtype),
            jax.ShapeDtypeStruct((32, 32, SMALL), BF),
            SHARE_SHAPE,
            SHARE_SHAPE,
        ],
        scratch_shapes=[
            pltpu.VMEM((32, SMALL), BF),
            pltpu.VMEM((8, 128), jnp.int32),
            pltpu.SemaphoreType.DMA((sems,)),
            pltpu.SemaphoreType.DMA((sems,)),
            pltpu.SemaphoreType.DMA((9,)),
        ],
        compiler_params=pltpu.CompilerParams(collective_id=ident, has_side_effects=True),
        name="startup",
    )(hidden, segment, *smalls, *shares)
    hidden_all, small_all = hidden_all.reshape(SEQ, D), small_all.reshape(D, SMALL)
    return hidden_all, segment_all, small_all, share_a, share_b


class RingScatter:
    def __init__(self, at, part, scratch, send, recv, base=0):
        self.at, self.part, self.send, self.recv, self.base = at, part, send, recv, base
        near, half_a, half_b, self.full_up, self.full_down = scratch[:5]
        to_far, to_up, to_down = scratch[5:] or [
            part.at[at.chip(k) * 2 + at.core] for k in (2, 1, 3)
        ]
        self.near, self.half_a, self.half_b = near, half_a, half_b
        self.to_far, self.to_up, self.to_down = to_far, to_up, to_down
        self.half = half_a.shape[0]
        self.lo, self.hi = pl.ds(0, self.half), pl.ds(self.half, self.half)
        up, down = at.ring(1), at.ring(3)
        self.plan = {
            k: (part.at[at.chip(k) * 2 + 1 - at.core], near.at[k], at.sibling()) for k in range(4)
        }
        self.plan[4] = (to_far.at[self.lo], half_a, up)
        self.plan[5] = (to_far.at[self.hi], half_b, down)
        self.plan[6] = (to_up, self.full_up, up)
        self.plan[7] = (to_down, self.full_down, down)

    def copy(self, i):
        src, dst, device = self.plan[i]
        return remote(src, dst, self.send, self.recv, self.base + i, device)

    def chip_sum(self, k):
        self.copy(k).wait_recv()
        own = self.part[self.at.chip(k) * 2 + self.at.core]
        return own.astype(F32) + self.near[k].astype(F32)

    def far(self):
        self.to_far[...] = self.chip_sum(2).astype(BF)
        self.copy(4).start()
        self.copy(5).start()

    def up_side(self):
        total = self.chip_sum(1)
        self.copy(4).wait_recv()
        self.to_up[self.lo, :] = (total[: self.half] + self.half_a[...].astype(F32)).astype(BF)
        self.to_up[self.hi, :] = total[self.half :].astype(BF)
        self.copy(6).start()

    def down_side(self):
        total = self.chip_sum(3)
        self.copy(5).wait_recv()
        self.to_down[self.lo, :] = total[: self.half].astype(BF)
        self.to_down[self.hi, :] = (total[self.half :] + self.half_b[...].astype(F32)).astype(BF)
        self.copy(7).start()

    def finish(self, out):
        out[...] = self.chip_sum(0)
        self.copy(6).wait_recv()
        out[...] += self.full_up[...].astype(F32)
        self.copy(7).wait_recv()
        out[...] += self.full_down[...].astype(F32)
        for i in range(8):
            self.copy(i).wait_send()


def ring_scratch(rows, columns, own_sends=True):
    block, half = pltpu.VMEM((rows, columns), BF), pltpu.VMEM((rows // 2, columns), BF)
    scratch = [pltpu.VMEM((4, rows, columns), BF), half, half, block, block]
    return scratch + [block] * 3 if own_sends else scratch


class PairScatter:
    def __init__(self, at, part, scratch, send, recv, base=0):
        self.at, self.part, self.send, self.recv, self.base = at, part, send, recv, base
        self.near, self.far_rows, self.to_far = scratch
        size = self.to_far.shape[0] // PIECES
        self.parts = [pl.ds(i * size, size) for i in range(PIECES)]
        self.other, self.own = (1 - at.yl) * 2, at.yl * 2

    def go(self, i, src, dst, device):
        return push(src, dst, self.send, self.recv, self.base + i, device)

    def begin_far(self):
        slot = self.other + 1 - self.at.core
        self.first = [
            self.go(i, self.part.at[slot, rows], self.near.at[1, rows], self.at.sibling())
            for i, rows in enumerate(self.parts)
        ]

    def begin_own(self):
        slot = self.own + 1 - self.at.core
        self.second = self.go(PIECES, self.part.at[slot], self.near.at[0], self.at.sibling())

    def forward(self):
        self.sent = []
        for i, rows in enumerate(self.parts):
            self.first[i].wait_recv()
            own = self.part[self.other + self.at.core, rows, :].astype(F32)
            self.to_far[rows, :] = (own + self.near[1, rows, :].astype(F32)).astype(BF)
            far = self.far_rows.at[rows]
            self.sent.append(self.go(PIECES + 1 + i, self.to_far.at[rows], far, self.at.partner()))

    def finish(self, out):
        self.second.wait_recv()
        out[...] = self.part[self.own + self.at.core].astype(F32) + self.near[0].astype(F32)
        for i, rows in enumerate(self.parts):
            self.sent[i].wait_recv()
            out[rows, :] += self.far_rows[rows, :].astype(F32)
        for copy in (*self.first, self.second, *self.sent):
            copy.wait_send()


def pair_scratch(rows, columns):
    block = pltpu.VMEM((rows, columns), BF)
    return [pltpu.VMEM((2, rows, columns), BF), block, block]


SPLIT = 384


def final_kernel(
    part, grads, weights, sum_a, sum_b, dn1, attention, rest, gate, up, down,
    sum_1a, sum_1b, sum_2a, sum_2b, over_y, from_opposite, share, shares, *refs,
):
    at = Place()
    greet(
        [
            at.sibling(), at.partner(), at.diagonal(), at.opposite(),
            at.along("x", 1), at.along("x", 3), at.along("z", 1), at.along("z", 3),
        ]
    )
    pair_refs = refs[:3]
    groups = [refs[3 + 7 * i : 10 + 7 * i] for i in range(6)]
    total_a, total_b, land_a, land_b = refs[45:49]
    send, recv, load = refs[49:]
    base = 1 + 2 * PIECES
    width = grads.shape[-1]
    a, b = pl.ds(0, SPLIT), pl.ds(SPLIT, width - SPLIT)

    def ring_sum(i, axis, part_of):
        return RingSum(
            at, axis, part_of, groups[i], send, recv, load, base + 6 + RingSum.COPIES * i, 3 * i
        )

    first_a = ring_sum(0, "x", lambda k: grads.at[k, :, :, :, a])
    first_b = ring_sum(1, "z", lambda k: grads.at[:, k, :, :, b])
    second_a = ring_sum(2, "z", lambda k: sum_1a.at[k])
    second_b = ring_sum(3, "x", lambda k: sum_1b.at[k])
    sums = [
        ring_sum(4, "z", lambda k: sum_a.at[k]), ring_sum(5, "x", lambda k: sum_b.at[k]),
    ]
    for each in (first_a, first_b):
        each.begin()
        each.direct()
    for each in sums:
        each.begin()
    pair = PairScatter(at, part, pair_refs, send, recv)
    pair.begin_far()
    pair.begin_own()
    pair.forward()
    first_a.middle()
    first_b.middle()
    for each in sums:
        each.direct()
        each.middle()
    first_a.finish(sum_1a)
    second_a.begin()
    second_a.direct()
    first_b.finish(sum_1b)
    second_b.begin()
    second_b.direct()
    second_a.middle()
    second_b.middle()
    second_a.finish(sum_2a)
    second_b.finish(sum_2b)
    over_y[:, a] = sum_2a[...].reshape(64, SPLIT)
    over_y[:, b] = sum_2b[...].reshape(64, width - SPLIT)
    theirs = pl.ds(pl.multiple_of((1 - at.yh) * 32, 32), 32)
    own = pl.ds(pl.multiple_of(at.yh * 32, 32), 32)
    swap = push(over_y.at[theirs], from_opposite, send, recv, base, at.opposite())
    lands = []
    for i, (each, out, land) in enumerate(
        zip(sums, (total_a, total_b), (land_a, land_b))
    ):
        each.finish(out)
        lands.append(
            push(out.at[1 - at.yh], land, send, recv, base + 1 + i, at.opposite())
        )
    swap.wait_recv()
    total = over_y[own, :].astype(F32) + from_opposite[...].astype(F32)
    attention[...] = total[:, :768]
    gain_part = jnp.sum(total[:, :512] * weights[...].astype(F32), axis=1, keepdims=True)
    lane = lax.broadcasted_iota(jnp.int32, (32, 128), 1)
    share[...] = jnp.where(lane == 33, gain_part, total[:, 768:])
    copies = [
        push(share, shares.at[i], send, recv, base + 3 + i, device)
        for i, device in enumerate((at.sibling(), at.partner(), at.diagonal()))
    ]
    pair.finish(dn1)
    mine, theirs = pl.ds(at.yh * STEPS, STEPS), pl.ds((1 - at.yh) * STEPS, STEPS)
    for j, value in enumerate((total_a, total_b)):
        for i, out in enumerate((gate, up, down)):
            out[mine, 2 * j : 2 * j + 2] = value[at.yh, :, i].astype(F32)
    rest[...] = share[...]
    for i, copy in enumerate(copies):
        copy.wait_recv()
        rest[...] += shares[i]
    for j, (copy, land) in enumerate(zip(lands, (land_a, land_b))):
        copy.wait_recv()
        for i, out in enumerate((gate, up, down)):
            out[theirs, 2 * j : 2 * j + 2] = land[:, i].astype(F32)
    for copy in (swap, *copies, *lands):
        copy.wait_send()


def final(part, grads, weights, sums, ident):
    vmem = pl.BlockSpec(memory_space=pltpu.VMEM)
    hbm = pl.BlockSpec(memory_space=pl.ANY)
    width = grads.shape[1]
    sems = 1 + 2 * PIECES + 6 + 6 * RingSum.COPIES
    block = SUMS_SHAPE.shape[1:]
    narrow_a, narrow_b = (2, 32, SPLIT), (2, 32, width - SPLIT)
    return pl.pallas_call(
        final_kernel,
        in_specs=[vmem] * 3 + [hbm] * 2,
        out_specs=[vmem] * 6,
        out_shape=[
            jax.ShapeDtypeStruct((LOCAL, D), F32),
            jax.ShapeDtypeStruct((32, 768), F32),
            jax.ShapeDtypeStruct((32, 128), F32),
            *[jax.ShapeDtypeStruct((2 * STEPS, QUAD, 32, FF), F32)] * 3,
        ],
        scratch_shapes=[
            pltpu.VMEM((4, 2, 32, SPLIT), BF),
            pltpu.VMEM((4, 2, 32, width - SPLIT), BF),
            pltpu.VMEM(narrow_a, BF),
            pltpu.VMEM(narrow_b, BF),
            pltpu.VMEM((64, width), BF),
            pltpu.VMEM((32, width), BF),
            pltpu.VMEM((32, 128), F32),
            pltpu.VMEM((3, 32, 128), F32),
            *pair_scratch(LOCAL, D),
            *sum_scratch((4, 2, 32, SPLIT)),
            *sum_scratch((4, 2, 32, width - SPLIT)),
            *sum_scratch(narrow_a),
            *sum_scratch(narrow_b),
            *sum_scratch(block),
            *sum_scratch(block),
            *[pltpu.VMEM(block, BF)] * 2,
            *[pltpu.VMEM(block[1:], BF)] * 2,
            pltpu.SemaphoreType.DMA((sems,)),
            pltpu.SemaphoreType.DMA((sems,)),
            pltpu.SemaphoreType.DMA((18,)),
        ],
        compiler_params=pltpu.CompilerParams(
            collective_id=ident, has_side_effects=True, vmem_limit_bytes=48 * MIB
        ),
        name="final",
    )(part.reshape(4, LOCAL, D), grads.reshape(4, 4, 2, 32, width), weights, *sums)


def rotary_tables():
    half = HD // 2
    inverse = (10000.0 ** (-(np.arange(half, dtype=np.float64) * 2.0) / HD)).astype(np.float32)
    angles = np.arange(SEQ, dtype=np.float32)[:, None] * inverse[None, :]
    cosine, sine = np.cos(angles), np.sin(angles)
    wide_cosine = np.concatenate([cosine] * 4, axis=1)
    wide_sine = np.concatenate([-sine, sine] * 2, axis=1)
    return wide_cosine.astype(np.float32), wide_sine.astype(np.float32)


def swapped(values):
    lane = lax.broadcasted_iota(jnp.int32, values.shape, 1)
    low = (lane % HD) < HD // 2
    return jnp.where(low, pltpu.roll(values, 96, 1), pltpu.roll(values, 32, 1))


def rotated(values, cosine, sine):
    return values * cosine + swapped(values) * sine


def bias_block(key_segment, query_segment, first, rows):
    key_at = lax.broadcasted_iota(jnp.int32, (rows, BLOCK), 0)
    query_at = lax.broadcasted_iota(jnp.int32, (rows, BLOCK), 1) + first
    allowed = (key_segment == query_segment) & (key_at <= query_at)
    return jnp.where(allowed, 0.0, MASKED)


def segment_row(segments):
    return jnp.concatenate(
        [segments[rank, i : i + 1, :] for rank in range(4) for i in range(2)], axis=1
    ).astype(F32)


def gain_rows(small):
    return small[:, 768:896].astype(F32).T[32:40, :]


def column_of(row):
    return jnp.broadcast_to(row, (8, row.shape[1])).T[:, 0:1]


def front_kernel(
    hidden, weights, cosine, sine, segments, own_hidden, ids, out_grad, share_a, share_b,
    normed, query, key, value, context_t, log_total, middle, normed_moe, gating,
    over_z, over_x, quad_a, quad_b, out_grad_all, bias, part, context, through, *refs,
):
    pair_refs = refs[:3]
    send, recv, here = refs[3:]
    at = Place()
    greet(
        [
            at.sibling(), at.partner(), at.ring(1), at.ring(3),
            at.along("x", 1), at.along("x", 3), at.along("z", 1), at.along("z", 3),
        ]
    )
    ring = RingGather(at, out_grad, out_grad_all, send, recv, here.at[0], 0)
    lines = first_gather(
        at, share_a, share_b, over_z, over_x, send, recv, here.at[pl.ds(1, 4)], 9
    )
    quad = second_gather(
        at, 0, over_z, over_x, quad_a, quad_b, send, recv, here.at[pl.ds(5, 4)],
        9 + SpreadOut.COPIES, through,
    )
    scatter = PairScatter(at, part, pair_refs, send, recv, 9 + 2 * SpreadOut.COPIES)
    lines.begin()
    ring.begin()

    gains = gain_rows(weights)
    seg_row = segment_row(segments)
    seg_column = column_of(seg_row)
    for block in range(SEQ // BLOCK):
        rows = slice(block * BLOCK, (block + 1) * BLOCK)
        values = hidden[rows, :].astype(F32)
        scale = lax.rsqrt(jnp.mean(values * values, axis=-1, keepdims=True) + EPS)
        normed[rows, :] = (values * scale * gains[0:1, :]).astype(BF)
    for half in range(2):
        columns = slice(half * 128, half * 128 + 128)
        pre = mm(normed[...], weights[:, columns])
        query[:, columns] = (rotated(pre, cosine[...], sine[...]) * 0.125).astype(BF)
    key_pre = mm(normed[...], weights[:, 256:384])
    key[...] = rotated(key_pre, cosine[...], sine[...]).astype(BF)
    value_pre = mm(normed[...], weights[:, 384:512])
    value[...] = value_pre.astype(BF)
    value_t = value_pre.T.astype(BF)
    lines.forward()
    for block in range(SEQ // BLOCK):
        first, end = block * BLOCK, (block + 1) * BLOCK
        bias[:end, :] = bias_block(seg_column[:end, :], seg_row[:, first:end], first, end)
        for head in range(HEADS):
            kv = slice((head // 2) * HD, (head // 2) * HD + HD)
            own = slice(head * HD, head * HD + HD)
            scores = mm_last(key[:end, kv], query[first:end, own]) + bias[:end, :]
            top = jnp.max(scores, axis=0, keepdims=True)
            powers = jnp.exp(scores - top)
            total = jnp.sum(powers, axis=0, keepdims=True)
            share = (powers * (1.0 / total)).astype(BF)
            context_t[own, first:end] = mm(value_t[kv, :end], share).astype(BF)
            log_total[head : head + 1, first:end] = top + jnp.log(total)
        if block == 1:
            lines.finish()
            quad.begin()
        if block == 2:
            ring.forward_before()
            ring.forward_behind()
    context[...] = context_t[...].T

    def project(slot):
        rows = pl.ds(pl.multiple_of(slot * LOCAL, LOCAL), LOCAL)
        part[slot] = mm_last(context[rows, :], weights[:, 512:768]).astype(BF)

    project(scatter.other + 1 - at.core)
    scatter.begin_far()
    project(scatter.other + at.core)
    project(scatter.own + 1 - at.core)
    scatter.begin_own()
    project(scatter.own + at.core)
    scatter.forward()
    quad.forward()
    ring.forward_across()
    scatter.finish(middle)
    values = middle[...] + own_hidden[...].astype(F32)
    middle[...] = values
    scale = lax.rsqrt(jnp.mean(values * values, axis=-1, keepdims=True) + EPS)
    normed_moe[...] = (values * scale * gains[1:2, :]).astype(BF)
    lane = lax.broadcasted_iota(jnp.int32, (LOCAL, 128), 1)
    chosen = lane == ids[:, 0:1]
    for i in range(1, TOPK):
        chosen = chosen | (lane == ids[:, i : i + 1])
    logits = jnp.where(chosen, mm(normed_moe[...], weights[:, 768:896]), MASKED)
    powers = jnp.where(chosen, jnp.exp(logits - jnp.max(logits, axis=-1, keepdims=True)), 0.0)
    gating[...] = powers / jnp.sum(powers, axis=-1, keepdims=True)
    for i in (0, 4, 6, 7, 8):
        ring.copy(i).wait_recv()
    ring.sent()
    ring.kept().wait()
    quad.finish()


def front(hidden, weights, tables, segments, own_hidden, ids, out_grad, shares, ident):
    vmem = pl.BlockSpec(memory_space=pltpu.VMEM)
    hbm = pl.BlockSpec(memory_space=pl.ANY)
    sems = 9 + 2 * SpreadOut.COPIES + 1 + 2 * PIECES
    return pl.pallas_call(
        front_kernel,
        in_specs=[vmem] * 10,
        out_specs=[vmem] * 9 + [hbm] * 5,
        out_shape=[
            jax.ShapeDtypeStruct((SEQ, D), BF),
            jax.ShapeDtypeStruct((SEQ, HEADS * HD), BF),
            jax.ShapeDtypeStruct((SEQ, 128), BF),
            jax.ShapeDtypeStruct((SEQ, 128), BF),
            jax.ShapeDtypeStruct((HEADS * HD, SEQ), BF),
            jax.ShapeDtypeStruct((8, SEQ), F32),
            jax.ShapeDtypeStruct((LOCAL, D), F32),
            jax.ShapeDtypeStruct((LOCAL, D), BF),
            jax.ShapeDtypeStruct((LOCAL, 128), F32),
            *[LINE_SHAPE] * 2,
            *[QUAD_SHAPE] * 2,
            jax.ShapeDtypeStruct((8, LOCAL, D), BF),
        ],
        scratch_shapes=[
            pltpu.VMEM((SEQ, BLOCK), F32),
            pltpu.VMEM((4, LOCAL, D), BF),
            pltpu.VMEM((SEQ, HEADS * HD), BF),
            pltpu.VMEM((2, *BLOCK_SHAPE), BF),
            *pair_scratch(LOCAL, D),
            pltpu.SemaphoreType.DMA((sems,)),
            pltpu.SemaphoreType.DMA((sems,)),
            pltpu.SemaphoreType.DMA((9,)),
        ],
        compiler_params=pltpu.CompilerParams(
            collective_id=ident, has_side_effects=True, vmem_limit_bytes=56 * MIB
        ),
        name="front",
    )(hidden, weights, *tables, segments, own_hidden, ids, out_grad, *shares)


def back_kernel(
    dx, dgate, gating, middle, normed_moe, out_grad, y_part,
    normed, weights, cosine, sine, segments, query, key, value, context_t, log_total,
    expert_a, expert_b, dmiddle, dn1, grads, block_out, sum_a, sum_b,
    bias, dcontext, dquery_t, dkey, dvalue, dall, dall_t, dattn_own, dattn_all, y_sum, *refs,
):
    ring_refs = refs[:8]
    send, recv, here, load = refs[22:]
    at = Place()
    greet(
        [
            at.sibling(), at.partner(), at.ring(1), at.ring(3),
            at.along("x", 1), at.along("x", 3), at.along("z", 1), at.along("z", 3),
        ]
    )
    base = 9 + 2 * PIECES
    sums = [
        RingSum(at, "x", lambda k: expert_a.at[k], refs[8:15], send, recv, load, base),
        RingSum(
            at, "z", lambda k: expert_b.at[k], refs[15:22], send, recv, load,
            base + RingSum.COPIES, 3,
        ),
    ]
    for each in sums:
        each.begin()
    gain = gain_rows(weights)[1:2, :]
    chosen = gating[...]
    dchosen = chosen * (dgate[...] - jnp.sum(chosen * dgate[...], axis=-1, keepdims=True))
    dlogits = dchosen.astype(BF)
    dnormed = dx[...] + mm_last(dlogits, weights[:, 768:896])
    values = middle[...]
    scale = lax.rsqrt(jnp.mean(values * values, axis=-1, keepdims=True) + EPS)
    unit = values * scale
    weighted = dnormed * gain
    inner = jnp.mean(weighted * unit, axis=-1, keepdims=True)
    total = out_grad[...].astype(F32) + scale * (weighted - unit * inner)
    dmiddle[...] = total
    dattn_own[...] = total.astype(BF)
    gather = PairGather(at, dattn_own, dattn_all, send, recv, here, 8, PIECES)
    scatter = RingScatter(at, y_part, ring_refs, send, recv)
    for k in (2, 1, 3, 0):
        scatter.copy(k).start()
    router_part = mm(normed_moe[...].T, dlogits)
    gain_part = column_of(jnp.sum(dnormed * unit, axis=0, keepdims=True))
    lane = lax.broadcasted_iota(jnp.int32, (D, 128), 1)
    grads[:, 768:] = jnp.where(lane == 32, gain_part, router_part).astype(BF)
    seg_row = segment_row(segments)
    seg_column = column_of(seg_row)
    gather.forward()
    scatter.far()
    for each in sums:
        each.middle()
        each.direct()
    gather.finish()
    dattn = dattn_all[...].reshape(SEQ, D)
    dcontext[...] = mm(dattn, weights[:, 512:768]).astype(BF)
    output_grad_t = mm(context_t[...], dattn)
    grads[:, 512:768] = output_grad_t.T.astype(BF)
    key_t = key[...].astype(F32).T.astype(BF)
    dkey[...] = jnp.zeros_like(dkey)
    dvalue[...] = jnp.zeros_like(dvalue)
    for block in range(SEQ // BLOCK):
        first, end = block * BLOCK, (block + 1) * BLOCK
        bias[:end, :] = bias_block(seg_column[:end, :], seg_row[:, first:end], first, end)
        for head in range(HEADS):
            kv = slice((head // 2) * HD, (head // 2) * HD + HD)
            own = slice(head * HD, head * HD + HD)
            query_block = query[first:end, own]
            dcontext_block = dcontext[first:end, own]
            scores = mm_last(key[:end, kv], query_block) + bias[:end, :]
            share = jnp.exp(scores - log_total[head : head + 1, first:end])
            dshare = mm_last(value[:end, kv], dcontext_block)
            centre = jnp.sum(share * dshare, axis=0, keepdims=True)
            dscore = (share * (dshare - centre)).astype(BF)
            dquery_t[own, first:end] = mm(key_t[kv, :end], dscore) * 0.125
            dkey[:end, kv] += mm(dscore, query_block)
            dvalue[:end, kv] += mm(share.astype(BF), dcontext_block)
        if block == 0:
            scatter.up_side()
            scatter.down_side()
    turn = -sine[...]
    for half in range(2):
        rows = slice(half * 128, half * 128 + 128)
        piece = rotated(dquery_t[rows, :].T, cosine[...], turn)
        dall[:, rows] = piece.astype(BF)
        dall_t[rows, :] = piece.T.astype(BF)
    piece = rotated(dkey[...], cosine[...], turn)
    dall[:, 256:384] = piece.astype(BF)
    dall_t[256:384, :] = piece.T.astype(BF)
    dall[:, 384:512] = dvalue[...].astype(BF)
    dall_t[384:512, :] = dvalue[...].T.astype(BF)
    grads[:, 0:512] = mm(dall_t[...], normed[...]).T.astype(BF)
    for block in range(SEQ // BLOCK):
        rows = slice(block * BLOCK, (block + 1) * BLOCK)
        dn1[rows, :] = mm_last(dall[rows, :], weights[:, 0:512]).astype(BF)
    scatter.finish(y_sum)
    block_out[...] = (y_sum[...] + middle[...]).astype(BF)
    for each, out in zip(sums, (sum_a, sum_b)):
        each.finish(out)


def back(
    dx, dgate, gating, middle, normed_moe, out_grad, y_part,
    normed, weights, tables, segments, kept, expert_grads, ident,
):
    vmem = pl.BlockSpec(memory_space=pltpu.VMEM)
    hbm = pl.BlockSpec(memory_space=pl.ANY)
    sems = 9 + 2 * PIECES + 2 * RingSum.COPIES
    return pl.pallas_call(
        back_kernel,
        in_specs=[vmem] * 17 + [hbm] * 2,
        out_specs=[vmem] * 6,
        out_shape=[
            jax.ShapeDtypeStruct((LOCAL, D), F32),
            jax.ShapeDtypeStruct((SEQ, D), BF),
            jax.ShapeDtypeStruct((D, SMALL), BF),
            jax.ShapeDtypeStruct((LOCAL, D), BF),
            SUMS_SHAPE,
            SUMS_SHAPE,
        ],
        scratch_shapes=[
            pltpu.VMEM((SEQ, BLOCK), F32),
            pltpu.VMEM((SEQ, HEADS * HD), BF),
            pltpu.VMEM((HEADS * HD, SEQ), F32),
            pltpu.VMEM((SEQ, 128), F32),
            pltpu.VMEM((SEQ, 128), F32),
            pltpu.VMEM((SEQ, 512), BF),
            pltpu.VMEM((512, SEQ), BF),
            pltpu.VMEM((LOCAL, D), BF),
            pltpu.VMEM((4, LOCAL, D), BF),
            pltpu.VMEM((LOCAL, D), F32),
            *ring_scratch(LOCAL, D),
            *sum_scratch(SUMS_SHAPE.shape),
            *sum_scratch(SUMS_SHAPE.shape),
            pltpu.SemaphoreType.DMA((sems,)),
            pltpu.SemaphoreType.DMA((sems,)),
            pltpu.SemaphoreType.DMA,
            pltpu.SemaphoreType.DMA((6,)),
        ],
        compiler_params=pltpu.CompilerParams(
            collective_id=ident, has_side_effects=True, vmem_limit_bytes=62 * MIB
        ),
        name="back",
    )(
        dx, dgate, gating, middle, normed_moe, out_grad, y_part,
        normed, weights, *tables, segments, *kept, *expert_grads,
    )


def experts_kernel(
    x_in, gate_in, d_in, over_z, over_x, quad_0a, quad_0b, y_out, dx_out, dgate_out,
    grads_a, grads_b, quad_1a, quad_1b, quad_2a, quad_2b, quad_3a, quad_3b,
    x, d, xt, dt, y, dx, gating, dgate, dgate_part, hidden, w, *refs,
):
    dx_scratch, dgate_scratch = refs[:5], refs[5:10]
    send, recv, here, load, store, fetch = refs[10:16]
    at = Place()
    step = pl.program_id(0)
    opening, closing = step == 0, step == STEPS - 1
    rows_at_once = 2 * LOCAL
    lane = lax.broadcasted_iota(jnp.int32, (LOCAL, 128), 1)
    own_first = at.yh * 16 + step * QUAD
    x_gather = RingGather(at, x_in, x, send, recv, here.at[0], 0)
    gate_gather = RingGather(at, gate_in, gating, send, recv, here.at[1], 9)
    gathers = (x_gather, gate_gather)
    scatters = (
        RingScatter(at, d, dx_scratch, send, recv, 18),
        RingScatter(at, dgate_part, dgate_scratch, send, recv, 26),
    )

    later = ((quad_1a, quad_1b), (quad_2a, quad_2b), (quad_3a, quad_3b))
    quads = [
        second_gather(
            at, 1 + i, over_z, over_x, *quad, *refs[16:18], refs[18].at[pl.ds(4 * i, 4)],
            SpreadOut.COPIES * i, refs[19],
        )
        for i, quad in enumerate(later)
    ]

    def ride(condition, what):
        for i, quad in enumerate(quads):

            @pl.when(condition & (step == i))
            def _():
                what(quad)

    def fetches(quad_a, quad_b):
        copies = []
        for g in range(3):
            for i in range(QUAD):
                columns = pl.ds((g * QUAD + i) * FF, FF)
                if i < 2:
                    parts = [(quad_a.at[:, :, :, g, i], w.at[:, :, :, :, columns])]
                else:
                    parts = [
                        (quad_b.at[:, x_at, :, g, i - 2], w.at[x_at, :, :, :, columns])
                        for x_at in range(4)
                    ]
                for part in parts:
                    copies.append(pltpu.make_async_copy(*part, fetch.at[len(copies)]))
        return copies

    def d_load(chip):
        two = pl.ds(chip * 2, 2)
        return pltpu.make_async_copy(d_in.at[two], d.at[two], load.at[chip])

    def y_store(chip):
        two = pl.ds(chip * 2, 2)
        return pltpu.make_async_copy(x.at[two], y_out.at[two], store.at[chip])

    @pl.when(opening)
    def _():
        greet(
            [
                at.sibling(), at.ring(1), at.ring(3),
                at.along("x", 1), at.along("x", 3), at.along("z", 1), at.along("z", 3),
            ]
        )
        for gather in gathers:
            gather.begin()
        for copy in fetches(quad_0a, quad_0b):
            copy.start()
        for chip in range(4):
            d_load(chip).start()

    for copy in fetches(quad_0a, quad_0b):
        copy.wait()

    ride(step < STEPS, lambda quad: quad.begin())

    def arrive(turn):
        @pl.when(turn == 0)
        def _():
            for gather in gathers:
                gather.kept().wait()
                gather.copy(0).wait_recv()

        @pl.when(turn == 1)
        def _():
            for gather in gathers:
                gather.forward_before()
                gather.forward_behind()
            for gather in gathers:
                gather.copy(4).wait_recv()

        @pl.when(turn == 2)
        def _():
            for gather in gathers:
                gather.forward_across()
            for gather in gathers:
                gather.copy(6).wait_recv()

        @pl.when(turn == 3)
        def _():
            for gather in gathers:
                gather.copy(7).wait_recv()
                gather.copy(8).wait_recv()

    def leave(turn):
        @pl.when(turn == 0)
        def _():
            for scatter in scatters:
                scatter.copy(2).start()

        @pl.when(turn == 1)
        def _():
            for scatter in scatters:
                scatter.copy(1).start()
                scatter.far()

        @pl.when(turn == 2)
        def _():
            for scatter in scatters:
                scatter.copy(3).start()
                scatter.up_side()

        @pl.when(turn == 3)
        def _():
            for scatter in scatters:
                scatter.copy(0).start()
                scatter.down_side()

    def tokens_block(turn, carry):
        inward = jnp.where(turn == 0, 0, jnp.where(turn == 1, 3, turn - 1))
        outward = jnp.where(turn == 0, 2, jnp.where(turn == 3, 0, turn * 2 - 1))
        chip = at.chip(jnp.where(closing, outward, inward))
        two = pl.ds(chip * 2, 2)
        rows = pl.ds(pl.multiple_of(chip * rows_at_once, rows_at_once), rows_at_once)

        @pl.when(opening)
        def _():
            arrive(turn)
            d_load(chip).wait()
            xt[:, rows] = x[two].reshape(rows_at_once, D).T
            dt[:, rows] = d[two].reshape(rows_at_once, D).T
            y[rows, :] = jnp.zeros((rows_at_once, D), F32)
            dx[rows, :] = jnp.zeros((rows_at_once, D), F32)
            dgate[rows, :] = jnp.zeros((rows_at_once, 128), F32)

        ride(turn == 3, lambda quad: quad.forward())
        gate_up = w[:, :, :, :, 0 : 2 * F].reshape(D, 2 * F)
        down = w[:, :, :, :, 2 * F :].reshape(D, F)
        for core in range(2):
            slot = chip * 2 + core
            part = pl.ds(pl.multiple_of(slot * LOCAL, LOCAL), LOCAL)
            both = mm(x[slot], gate_up)
            gate, up = both[:, :F], both[:, F:]
            dact = mm(d[slot], down)
            turned = pltpu.roll(gating[slot], lax.rem(128 - own_first, 128), 1)
            factor = jnp.concatenate(
                [jnp.broadcast_to(turned[:, i : i + 1], (LOCAL, FF)) for i in range(QUAD)],
                axis=1,
            )
            q = 1.0 / (1.0 + jnp.exp(-gate))
            silu = gate * q
            act = silu * up
            product = act * dact
            sums = dgate[part, :]
            for i in range(QUAD):
                own = jnp.sum(product[:, i * FF : (i + 1) * FF], axis=1, keepdims=True)
                sums = jnp.where(lane == own_first + i, own, sums)
            dgate[part, :] = sums
            dact = dact * factor
            hidden[part, 0:F] = (dact * up * (q + silu * (1.0 - q))).astype(BF)
            hidden[part, F : 2 * F] = (dact * silu).astype(BF)
            hidden[part, 2 * F :] = (act * factor).astype(BF)
        y[rows, :] += mm_last(hidden[rows, 2 * F :], down)
        dx[rows, :] += mm_last(hidden[rows, 0 : 2 * F], gate_up)

        @pl.when(closing)
        def _():
            x[two] = y[rows, :].astype(BF).reshape(2, LOCAL, D)
            d[two] = dx[rows, :].astype(BF).reshape(2, LOCAL, D)
            dgate_part[two] = dgate[rows, :].astype(BF).reshape(2, LOCAL, 128)
            y_store(chip).start()
            leave(turn)

        return carry

    lax.fori_loop(0, 4, tokens_block, 0)

    @pl.when(opening)
    def _():
        for gather in gathers:
            gather.sent()

    def grads_block(block, carry):
        rows = pl.ds(pl.multiple_of(block * 512, 512), 512)

        def put(g, value):
            value = value.astype(BF).reshape(2, 4, 2, 32, value.shape[1])
            for j in range(value.shape[-1] // FF):
                piece = value[..., j * FF : (j + 1) * FF]
                group, i = g + j // QUAD, j % QUAD
                for x_at in range(2):
                    if i < 2:
                        grads_a[block * 2 + x_at, :, :, 0, group, i] = piece[x_at]
                    else:
                        grads_b[:, block * 2 + x_at, :, 0, group, i - 2] = piece[x_at]

        ride(block == 1, lambda quad: quad.finish())
        for number, quad in enumerate(later):

            @pl.when((block == 1) & (step == number))
            def _():
                for copy in fetches(*quad):
                    copy.start()

        put(0, mm(xt[rows, :], hidden[:, 0 : 2 * F]))
        put(2, mm(dt[rows, :], hidden[:, 2 * F :]))
        return carry

    lax.fori_loop(0, D // 512, grads_block, 0)

    @pl.when(closing)
    def _():
        scatters[0].finish(dx_out)
        scatters[1].finish(dgate_out)
        for chip in range(4):
            y_store(chip).wait()


def experts(x, gating, d, lines, quad, ident):
    hbm = pl.BlockSpec(memory_space=pl.ANY)

    def whole(rows, columns):
        return pl.BlockSpec((rows, columns), lambda step: (0, 0), pipeline_mode=pl.Buffered(1))

    each_step = pl.BlockSpec(
        (4, 4, 2, 1, 3, 2, 32, FF),
        lambda step: (0, 0, 0, step, 0, 0, 0, 0),
        pipeline_mode=pl.Buffered(1),
    )
    return pl.pallas_call(
        experts_kernel,
        grid=(STEPS,),
        in_specs=[hbm] * 7,
        out_specs=[
            hbm,
            whole(LOCAL, D),
            whole(LOCAL, 128),
            each_step,
            each_step,
            *[hbm] * 6,
        ],
        out_shape=[
            jax.ShapeDtypeStruct((8, LOCAL, D), BF),
            jax.ShapeDtypeStruct((LOCAL, D), F32),
            jax.ShapeDtypeStruct((LOCAL, 128), F32),
            GRADS_SHAPE,
            GRADS_SHAPE,
            *[QUAD_SHAPE] * 6,
        ],
        scratch_shapes=[
            pltpu.VMEM((8, LOCAL, D), BF),
            pltpu.VMEM((8, LOCAL, D), BF),
            pltpu.VMEM((D, TOKENS), BF),
            pltpu.VMEM((D, TOKENS), BF),
            pltpu.VMEM((TOKENS, D), F32),
            pltpu.VMEM((TOKENS, D), F32),
            pltpu.VMEM((8, LOCAL, 128), F32),
            pltpu.VMEM((TOKENS, 128), F32),
            pltpu.VMEM((8, LOCAL, 128), BF),
            pltpu.VMEM((TOKENS, 3 * F), BF),
            pltpu.VMEM((4, 4, 2, 32, 3 * F), BF),
            *ring_scratch(LOCAL, D, False),
            *ring_scratch(LOCAL, 128, False),
            pltpu.SemaphoreType.DMA((34,)),
            pltpu.SemaphoreType.DMA((34,)),
            pltpu.SemaphoreType.DMA((2,)),
            pltpu.SemaphoreType.DMA((4,)),
            pltpu.SemaphoreType.DMA((4,)),
            pltpu.SemaphoreType.DMA((30,)),
            pltpu.SemaphoreType.DMA((3 * SpreadOut.COPIES,)),
            pltpu.SemaphoreType.DMA((3 * SpreadOut.COPIES,)),
            pltpu.SemaphoreType.DMA((12,)),
            pltpu.VMEM((2, *BLOCK_SHAPE), BF),
        ],
        compiler_params=pltpu.CompilerParams(
            collective_id=ident, has_side_effects=True, vmem_limit_bytes=63 * MIB
        ),
        name="experts",
    )(x, gating, d, *lines, *quad)[:5]


def norm_scale(values):
    return lax.rsqrt(jnp.mean(values * values, axis=-1, keepdims=True) + EPS)


def norm_grad(values, gain, dnormed):
    scale = norm_scale(values)
    unit = values * scale
    weighted = dnormed * gain
    dvalues = scale * (weighted - unit * jnp.mean(weighted * unit, axis=-1, keepdims=True))
    return dvalues


def on_device(
    hidden_in, out_grad, attn_gain, query_weight, key_weight, value_weight, output_weight,
    moe_gain, router_weight, expert_gate, expert_up, expert_down, expert_ids, segment_ids,
):
    gains = jnp.stack([attn_gain, moe_gain])
    smalls = (query_weight, key_weight, value_weight, output_weight, router_weight, gains)
    own_shares = (expert_gate, expert_up, expert_down)
    hidden_all, segments, small, *shares = startup(
        hidden_in, segment_ids.reshape(2, 128), smalls, own_shares, 0
    )
    tables = tuple(jnp.asarray(t) for t in rotary_tables())
    normed, *more, d = front(
        hidden_all, small, tables, segments, hidden_in, expert_ids, out_grad, shares, 1
    )
    kept, (middle, normed_moe, gating), lines, quad = more[:5], more[5:8], more[8:10], more[10:]
    y, dx, dgate, *expert_grads = experts(normed_moe, gating, d, lines, quad, 3)
    dmiddle, dn1, grads, block_out, *sums = back(
        dx, dgate, gating, middle, normed_moe, out_grad, y,
        normed, small, tables, segments, kept, expert_grads, 5,
    )
    weights = jnp.concatenate([query_weight, key_weight, value_weight], axis=1)
    dn1, attention_grads, rest, *expert_grads = final(dn1, grads, weights, sums, 6)
    hidden = hidden_in.astype(F32)
    dhidden = norm_grad(hidden, small[:, 800].astype(F32), dn1)
    hidden_grad = dmiddle + dhidden
    expert_grads = [share.reshape(E, 32, FF) for share in expert_grads]
    return (
        block_out,
        hidden_grad,
        rest[:, 33] / attn_gain.astype(F32),
        attention_grads[:, 0:256],
        attention_grads[:, 256:384],
        attention_grads[:, 384:512],
        attention_grads[:, 512:768],
        rest[:, 32],
        rest[:, :32],
        *expert_grads,
    )


def solution(mesh):
    fine = Mesh(np.asarray(mesh.devices).reshape(4, 4, 2, 2, 2), ALL)
    return jax.shard_map(
        on_device,
        mesh=fine,
        in_specs=(
            P(ALL, None),
            P(ALL, None),
            P(DP),
            P(DP, TENSOR),
            P(DP, TENSOR),
            P(DP, TENSOR),
            P(DP, TENSOR),
            P(DP),
            P(DP, None),
            P(None, DP, TENSOR),
            P(None, DP, TENSOR),
            P(None, DP, TENSOR),
            P(ALL, None),
            P(ALL),
        ),
        out_specs=(
            P(ALL, None),
            P(ALL, None),
            P(DP),
            P(DP, TENSOR),
            P(DP, TENSOR),
            P(DP, TENSOR),
            P(DP, TENSOR),
            P(DP),
            P(DP, None),
            P(None, DP, TENSOR),
            P(None, DP, TENSOR),
            P(None, DP, TENSOR),
        ),
        check_vma=False,
    )
```

```python
import jax
import jax.numpy as jnp
import numpy as np
from jax import lax
from jax.experimental import pallas as pl
from jax.experimental.pallas import tpu as pltpu
from jax.sharding import Mesh
from jax.sharding import PartitionSpec as P

D = 1024
HD = 64
E = 32
SEQ = 1024
LOCAL = 256
HEADS = 4
QUAD = 4
FF = 128
F = QUAD * FF
EPS = 1e-06
TOPK = 8
MASKED = -1e30
BLOCK = 256
TOKENS = 2048
STEPS = 4

DP = ("x", "z", "yh")
TENSOR = ("yl", "core")
RING = ("yh", "yl", "core")
PLANE = ("x", "z")
ALL = ("x", "z", "yh", "yl", "core")

F32 = jnp.float32
BF = jnp.bfloat16
LAST = (((1,), (1,)), ((), ()))
MIB = 1024 * 1024
MESH = pl.DeviceIdType.MESH
SMALL = 896


def mm(a, b):
    return jnp.dot(a, b, preferred_element_type=F32)


def mm_last(a, b):
    return lax.dot_general(a, b, LAST, preferred_element_type=F32)


class Place:
    def __init__(self):
        self.x = lax.axis_index("x")
        self.z = lax.axis_index("z")
        self.yh = lax.axis_index("yh")
        self.yl = lax.axis_index("yl")
        self.core = lax.axis_index("core")
        self.y = self.yh * 2 + self.yl

    def chip(self, k):
        return lax.rem(self.y + k, 4)

    def ring(self, k):
        chip = self.chip(k)
        return {"yh": chip // 2, "yl": lax.rem(chip, 2)}

    def along(self, axis, k):
        return {axis: lax.rem(getattr(self, axis) + k, 4)}

    def sibling(self):
        return {"core": 1 - self.core}

    def partner(self):
        return {"yl": 1 - self.yl}

    def diagonal(self):
        return {"yl": 1 - self.yl, "core": 1 - self.core}

    def opposite(self):
        return {"yh": 1 - self.yh}


def greet(devices):
    barrier = pltpu.get_barrier_semaphore()
    for device in devices:
        pl.semaphore_signal(barrier, inc=1, device_id=device, device_id_type=MESH)
    pl.semaphore_wait(barrier, len(devices))


def remote(src, dst, send, recv, i, device):
    return pltpu.make_async_remote_copy(
        src_ref=src, dst_ref=dst, send_sem=send.at[i], recv_sem=recv.at[i],
        device_id=device, device_id_type=MESH,
    )


def push(src, dst, send, recv, i, device):
    copy = remote(src, dst, send, recv, i, device)
    copy.start()
    return copy


def keep(src, dst, sem):
    copy = pltpu.make_async_copy(src, dst, sem)
    copy.start()
    return copy


class RingGather:
    def __init__(self, at, own, out, send, recv, here, base=0):
        self.at, self.own, self.out, self.base = at, own, out, base
        self.send, self.recv, self.here = send, recv, here
        half = own.shape[0] // 2
        lo, hi = pl.ds(0, half), pl.ds(half, half)
        me, before, behind, across = (out.at[self.slot(k)] for k in (0, 3, 1, 2))
        near, up, down = at.sibling(), at.ring(1), at.ring(3)
        self.plan = [
            (own, me, near),
            (own, me, up),
            (own, me, down),
            (before.at[lo], before.at[lo], up),
            (before, before, near),
            (behind.at[hi], behind.at[hi], down),
            (behind, behind, near),
            (across.at[lo], across.at[lo], near),
            (across.at[hi], across.at[hi], near),
        ]

    def slot(self, k):
        return self.at.chip(k) * 2 + self.at.core

    def copy(self, i):
        src, dst, device = self.plan[i]
        return remote(src, dst, self.send, self.recv, self.base + i, device)

    def kept(self):
        return pltpu.make_async_copy(self.own, self.out.at[self.slot(0)], self.here)

    def begin(self):
        self.kept().start()
        for i in (1, 2, 0):
            self.copy(i).start()

    def forward_before(self):
        self.copy(1).wait_recv()
        self.copy(3).start()
        self.copy(4).start()

    def forward_behind(self):
        self.copy(2).wait_recv()
        self.copy(5).start()
        self.copy(6).start()

    def forward_across(self):
        self.copy(3).wait_recv()
        self.copy(7).start()
        self.copy(5).wait_recv()
        self.copy(8).start()

    def sent(self):
        for i in range(9):
            self.copy(i).wait_send()


class PairGather:
    def __init__(self, at, own, out, send, recv, here, base, pieces):
        self.at, self.out, self.send, self.recv, self.base = at, out, send, recv, base
        size = own.shape[0] // pieces
        self.parts = [pl.ds(i * size, size) for i in range(pieces)]
        me = at.yl * 2 + at.core
        self.other = (1 - at.yl) * 2 + at.core
        self.kept = keep(own, out.at[me], here)
        self.far = [
            push(own.at[part], out.at[me, part], send, recv, base + 1 + i, at.partner())
            for i, part in enumerate(self.parts)
        ]
        self.near = [push(own, out.at[me], send, recv, base, at.sibling())]

    def forward(self):
        for i, part in enumerate(self.parts):
            self.far[i].wait_recv()
            view = self.out.at[self.other, part]
            index = self.base + 1 + len(self.parts) + i
            self.near.append(push(view, view, self.send, self.recv, index, self.at.sibling()))

    def finish(self):
        for copy in self.near:
            copy.wait_recv()
        for copy in (*self.far, *self.near):
            copy.wait_send()
        self.kept.wait()


PIECES = 4


class AxisGather:
    def __init__(self, at, axis, view, send, recv, base):
        self.up, self.down = at.along(axis, 1), at.along(axis, 3)
        self.view, self.send, self.recv, self.base = view, send, recv, base

    def go(self, i, view, device):
        return push(view, view, self.send, self.recv, self.base + i, device)

    def begin(self):
        self.first = [
            self.go(0, self.view(0, "all"), self.up), self.go(1, self.view(0, "all"), self.down),
        ]

    def forward(self):
        self.first[0].wait_recv()
        self.far = [self.go(2, self.view(3, "low"), self.up)]
        self.first[1].wait_recv()
        self.far.append(self.go(3, self.view(1, "high"), self.down))

    def finish(self):
        for copy in self.far:
            copy.wait_recv()
        for copy in (*self.first, *self.far):
            copy.wait_send()


def halves_of(ref, first, size):
    spans = {"all": (0, size), "low": (0, size // 2), "high": (size // 2, size // 2)}
    return lambda part: ref.at[pl.ds(first + spans[part][0], spans[part][1])]


class SpreadOut:
    COPIES = 8

    def __init__(self, at, rings, send, recv, here, base=0, through=None):
        self.send, self.recv, self.here, self.base = send, recv, here, base
        self.through = through
        self.own = [(own, slot(0)) for _, own, slot, _ in rings]
        self.plan = []
        for axis, own, slot, _ in rings:
            self.plan.append((own, slot(0), at.along(axis, 1)))
            self.plan.append((own, slot(0), at.along(axis, 3)))
        for axis, _, slot, half in rings:
            low, high = (slot(3).at[pl.ds(0, half)], slot(1).at[pl.ds(half, half)])
            self.plan.append((low, low, at.along(axis, 1)))
            self.plan.append((high, high, at.along(axis, 3)))

    def copy(self, i):
        src, dst, device = self.plan[i]
        return remote(src, dst, self.send, self.recv, self.base + i, device)

    def loaded(self, i):
        return pltpu.make_async_copy(self.own[i][0], self.through.at[i], self.here.at[i])

    def kept(self, i):
        src, dst = self.own[i]
        src = src if self.through is None else self.through.at[i]
        return pltpu.make_async_copy(src, dst, self.here.at[2 + i])

    def begin(self):
        for i in range(4):
            self.copy(i).start()
        for i in range(2):
            (self.kept(i) if self.through is None else self.loaded(i)).start()

    def forward(self):
        for i in range(4):
            self.copy(i).wait_recv()
            self.copy(4 + i).start()
        if self.through is not None:
            for i in range(2):
                self.loaded(i).wait()
                self.kept(i).start()

    def finish(self):
        for i in range(4, 8):
            self.copy(i).wait_recv()
        for i in range(8):
            self.copy(i).wait_send()
        for i in range(2):
            self.kept(i).wait()


def ring_slots(out, place):
    return lambda k: out.at[lax.rem(place + k, 4)]


def first_gather(at, own_a, own_b, over_z, over_x, *sems):
    rings = (
        ("z", own_a, ring_slots(over_z, at.z), 1), ("x", own_b, ring_slots(over_x, at.x), 1),
    )
    return SpreadOut(at, rings, *sems)


def second_gather(at, number, over_z, over_x, quad_a, quad_b, *sems):
    rings = (
        ("x", over_z.at[:, :, number], ring_slots(quad_a, at.x), 2),
        ("z", over_x.at[:, :, number], ring_slots(quad_b, at.z), 2),
    )
    return SpreadOut(at, rings, *sems)


SHARE_SHAPE = jax.ShapeDtypeStruct((2, STEPS, 3, 2, 32, FF), BF)
BLOCK_SHAPE = (4, 2, 3, 2, 32, FF)
LINE_SHAPE = jax.ShapeDtypeStruct((4, 2, STEPS, 3, 2, 32, FF), BF)
QUAD_SHAPE = jax.ShapeDtypeStruct((4, 4, 2, 3, 2, 32, FF), BF)
GRADS_SHAPE = jax.ShapeDtypeStruct((4, 4, 2, STEPS, 3, 2, 32, FF), BF)
SUMS_SHAPE = jax.ShapeDtypeStruct((4, 2, STEPS, 3, 2, 32, FF), BF)


class RingSum:
    COPIES = 6

    def __init__(self, at, axis, part_of, scratch, send, recv, load, base=0, first=0):
        half_a, half_b, up, down, to_up, to_down, own = scratch
        self.half_a, self.half_b, self.up, self.down = half_a, half_b, up, down
        self.to_up, self.to_down, self.own = to_up, to_down, own
        self.send, self.recv, self.base = send, recv, base
        size = half_a.shape[0]
        lo, hi = pl.ds(0, size), pl.ds(size, size)
        place = {"x": at.x, "z": at.z}[axis]
        here, above, across, below = (part_of(lax.rem(place + k, 4)) for k in range(4))
        upper, lower = at.along(axis, 1), at.along(axis, 3)
        self.plan = [
            (across.at[lo], half_a, upper),
            (across.at[hi], half_b, lower),
            (above.at[hi], up.at[hi], upper),
            (below.at[lo], down.at[lo], lower),
            (to_up, up.at[lo], upper),
            (to_down, down.at[hi], lower),
        ]
        self.loads = [
            pltpu.make_async_copy(src, dst, load.at[first + i])
            for i, (src, dst) in enumerate(
                ((above.at[lo], to_up), (below.at[hi], to_down), (here, own))
            )
        ]

    def copy(self, i):
        src, dst, device = self.plan[i]
        return remote(src, dst, self.send, self.recv, self.base + i, device)

    def begin(self):
        for i in range(2):
            self.copy(i).start()
        for load in self.loads:
            load.start()

    def direct(self):
        for i in (2, 3):
            self.copy(i).start()

    def middle(self):
        for i, (total, landed) in enumerate(
            ((self.to_up, self.half_a), (self.to_down, self.half_b))
        ):
            self.loads[i].wait()
            self.copy(i).wait_recv()

            def add(i, carry, total=total, landed=landed):
                total[i] = (total[i].astype(F32) + landed[i].astype(F32)).astype(BF)
                return carry

            lax.fori_loop(0, total.shape[0], add, 0)
            self.copy(4 + i).start()

    def finish(self, out):
        self.loads[2].wait()
        for i in range(2, 6):
            self.copy(i).wait_recv()

        def add(i, carry):
            total = self.own[i].astype(F32) + self.up[i].astype(F32)
            out[i] = (total + self.down[i].astype(F32)).astype(out.dtype)
            return carry

        lax.fori_loop(0, out.shape[0], add, 0)
        for i in range(6):
            self.copy(i).wait_send()


def sum_scratch(block):
    half, whole = pltpu.VMEM((block[0] // 2, *block[1:]), BF), pltpu.VMEM(block, BF)
    return [half, half, whole, whole, half, half, whole]


def startup_kernel(
    hidden, segment_rows, query, key, value, output, router, gains, gate, up, down,
    hidden_all, segment_all, small_all, share_a, share_b, small, segment, send, recv, here,
):
    at = Place()
    greet(
        [
            at.sibling(), at.partner(), at.diagonal(), at.opposite(),
            at.along("x", 1), at.along("x", 3), at.along("z", 1), at.along("z", 3),
        ]
    )
    small[:, 0:256] = query[...]
    small[:, 256:384] = key[...]
    small[:, 384:512] = value[...]
    small[:, 512:768] = output[...]
    columns = jnp.broadcast_to(gains[...].astype(F32)[:, None, :], (2, 8, 32))
    columns = [columns[i].T[:, 0:1].astype(BF) for i in range(2)]
    blank = jnp.zeros((32, 94), BF)
    small[:, 768:896] = jnp.concatenate([router[...], *columns, blank], axis=1)
    segment[0:2, :] = segment_rows[...]
    segment[2:8, :] = jnp.zeros((6, 128), jnp.int32)
    rank = at.yl * 2 + at.core
    mine = small_all.at[(at.x * 4 + at.z) * 2 + at.yh]
    small_kept = keep(small, mine, here.at[0])
    copies = [push(small, mine, send, recv, 0, at.opposite())]
    swaps, swaps_kept = [], []
    base = 13 + 2 * PIECES
    for i, share in enumerate((gate, up, down)):
        for j, out in enumerate((share_a, share_b)):
            dst, two = out.at[at.yh, :, i], pl.ds(2 * j, 2)
            theirs = share.at[pl.ds((1 - at.yh) * STEPS, STEPS), two]
            index = 2 * i + j
            swaps.append(push(theirs, dst, send, recv, base + index, at.opposite()))
            own = share.at[pl.ds(at.yh * STEPS, STEPS), two]
            swaps_kept.append(keep(own, dst, here.at[3 + index]))
    copies.extend(
        push(segment, segment_all.at[rank], send, recv, 1 + i, device)
        for i, device in enumerate((at.sibling(), at.partner(), at.diagonal()))
    )
    pair = PairGather(at, hidden, hidden_all, send, recv, here.at[1], 12, PIECES)
    seg_here = keep(segment, segment_all.at[rank], here.at[2])
    over_z = AxisGather(
        at, "z",
        lambda k, part: halves_of(small_all, (at.x * 4 + lax.rem(at.z + k, 4)) * 2, 2)(part),
        send, recv, 4,
    )
    over_x = AxisGather(
        at, "x", lambda k, part: halves_of(small_all, lax.rem(at.x + k, 4) * 8, 8)(part),
        send, recv, 8,
    )
    small_kept.wait()
    copies[0].wait_recv()
    over_z.begin()
    over_z.forward()
    over_z.finish()
    over_x.begin()
    pair.forward()
    for swap, own in zip(swaps, swaps_kept):
        swap.wait_recv()
        own.wait()
    over_x.forward()
    pair.finish()
    seg_here.wait()
    for copy in copies[1:]:
        copy.wait_recv()
    over_x.finish()
    for copy in (*copies, *swaps):
        copy.wait_send()


def startup(hidden, segment, smalls, shares, ident):
    hbm = pl.BlockSpec(memory_space=pl.ANY)
    vmem = pl.BlockSpec(memory_space=pltpu.VMEM)
    sems = 13 + 2 * PIECES + 6
    shares = [share.reshape(2 * STEPS, QUAD, 32, FF) for share in shares]
    hidden_all, segment_all, small_all, share_a, share_b = pl.pallas_call(
        startup_kernel,
        in_specs=[vmem] * 8 + [hbm] * 3,
        out_specs=[hbm] * 3 + [vmem] * 2,
        out_shape=[
            jax.ShapeDtypeStruct((4, *hidden.shape), hidden.dtype),
            jax.ShapeDtypeStruct((4, 8, 128), segment.dtype),
            jax.ShapeDtypeStruct((32, 32, SMALL), BF),
            SHARE_SHAPE,
            SHARE_SHAPE,
        ],
        scratch_shapes=[
            pltpu.VMEM((32, SMALL), BF),
            pltpu.VMEM((8, 128), jnp.int32),
            pltpu.SemaphoreType.DMA((sems,)),
            pltpu.SemaphoreType.DMA((sems,)),
            pltpu.SemaphoreType.DMA((9,)),
        ],
        compiler_params=pltpu.CompilerParams(collective_id=ident, has_side_effects=True),
        name="startup",
    )(hidden, segment, *smalls, *shares)
    hidden_all, small_all = hidden_all.reshape(SEQ, D), small_all.reshape(D, SMALL)
    return hidden_all, segment_all, small_all, share_a, share_b


SPLIT = 384


class RingScatter:
    def __init__(self, at, part, scratch, send, recv, base=0):
        self.at, self.part, self.send, self.recv, self.base = at, part, send, recv, base
        near, half_a, half_b, self.full_up, self.full_down = scratch[:5]
        to_far, to_up, to_down = scratch[5:] or [
            part.at[at.chip(k) * 2 + at.core] for k in (2, 1, 3)
        ]
        self.near, self.half_a, self.half_b = near, half_a, half_b
        self.to_far, self.to_up, self.to_down = to_far, to_up, to_down
        self.half = half_a.shape[0]
        self.lo, self.hi = pl.ds(0, self.half), pl.ds(self.half, self.half)
        up, down = at.ring(1), at.ring(3)
        self.plan = {
            k: (part.at[at.chip(k) * 2 + 1 - at.core], near.at[k], at.sibling()) for k in range(4)
        }
        self.plan[4] = (to_far.at[self.lo], half_a, up)
        self.plan[5] = (to_far.at[self.hi], half_b, down)
        self.plan[6] = (to_up, self.full_up, up)
        self.plan[7] = (to_down, self.full_down, down)

    def copy(self, i):
        src, dst, device = self.plan[i]
        return remote(src, dst, self.send, self.recv, self.base + i, device)

    def chip_sum(self, k):
        self.copy(k).wait_recv()
        own = self.part[self.at.chip(k) * 2 + self.at.core]
        return own.astype(F32) + self.near[k].astype(F32)

    def far(self):
        self.to_far[...] = self.chip_sum(2).astype(BF)
        self.copy(4).start()
        self.copy(5).start()

    def up_side(self):
        total = self.chip_sum(1)
        self.copy(4).wait_recv()
        self.to_up[self.lo, :] = (total[: self.half] + self.half_a[...].astype(F32)).astype(BF)
        self.to_up[self.hi, :] = total[self.half :].astype(BF)
        self.copy(6).start()

    def down_side(self):
        total = self.chip_sum(3)
        self.copy(5).wait_recv()
        self.to_down[self.lo, :] = total[: self.half].astype(BF)
        self.to_down[self.hi, :] = (total[self.half :] + self.half_b[...].astype(F32)).astype(BF)
        self.copy(7).start()

    def finish(self, out):
        out[...] = self.chip_sum(0)
        self.copy(6).wait_recv()
        out[...] += self.full_up[...].astype(F32)
        self.copy(7).wait_recv()
        out[...] += self.full_down[...].astype(F32)
        for i in range(8):
            self.copy(i).wait_send()


def ring_scratch(rows, columns, own_sends=True):
    block, half = pltpu.VMEM((rows, columns), BF), pltpu.VMEM((rows // 2, columns), BF)
    scratch = [pltpu.VMEM((4, rows, columns), BF), half, half, block, block]
    return scratch + [block] * 3 if own_sends else scratch


class PairScatter:
    def __init__(self, at, part, scratch, send, recv, base=0):
        self.at, self.part, self.send, self.recv, self.base = at, part, send, recv, base
        self.near, self.far_rows, self.to_far = scratch
        size = self.to_far.shape[0] // PIECES
        self.parts = [pl.ds(i * size, size) for i in range(PIECES)]
        self.other, self.own = (1 - at.yl) * 2, at.yl * 2

    def go(self, i, src, dst, device):
        return push(src, dst, self.send, self.recv, self.base + i, device)

    def begin_far(self):
        slot = self.other + 1 - self.at.core
        self.first = [
            self.go(i, self.part.at[slot, rows], self.near.at[1, rows], self.at.sibling())
            for i, rows in enumerate(self.parts)
        ]

    def begin_own(self):
        slot = self.own + 1 - self.at.core
        self.second = self.go(PIECES, self.part.at[slot], self.near.at[0], self.at.sibling())

    def forward(self):
        self.sent = []
        for i, rows in enumerate(self.parts):
            self.first[i].wait_recv()
            own = self.part[self.other + self.at.core, rows, :].astype(F32)
            self.to_far[rows, :] = (own + self.near[1, rows, :].astype(F32)).astype(BF)
            far = self.far_rows.at[rows]
            self.sent.append(self.go(PIECES + 1 + i, self.to_far.at[rows], far, self.at.partner()))

    def finish(self, out):
        self.second.wait_recv()
        out[...] = self.part[self.own + self.at.core].astype(F32) + self.near[0].astype(F32)
        for i, rows in enumerate(self.parts):
            self.sent[i].wait_recv()
            out[rows, :] += self.far_rows[rows, :].astype(F32)
        for copy in (*self.first, self.second, *self.sent):
            copy.wait_send()


def pair_scratch(rows, columns):
    block = pltpu.VMEM((rows, columns), BF)
    return [pltpu.VMEM((2, rows, columns), BF), block, block]


SPLIT = 384


def rotary_tables():
    half = HD // 2
    inverse = (10000.0 ** (-(np.arange(half, dtype=np.float64) * 2.0) / HD)).astype(np.float32)
    angles = np.arange(SEQ, dtype=np.float32)[:, None] * inverse[None, :]
    cosine, sine = np.cos(angles), np.sin(angles)
    wide_cosine = np.concatenate([cosine] * 4, axis=1)
    wide_sine = np.concatenate([-sine, sine] * 2, axis=1)
    return wide_cosine.astype(np.float32), wide_sine.astype(np.float32)


def swapped(values):
    lane = lax.broadcasted_iota(jnp.int32, values.shape, 1)
    low = (lane % HD) < HD // 2
    return jnp.where(low, pltpu.roll(values, 96, 1), pltpu.roll(values, 32, 1))


def rotated(values, cosine, sine):
    return values * cosine + swapped(values) * sine


def bias_block(key_segment, query_segment, first, rows):
    key_at = lax.broadcasted_iota(jnp.int32, (rows, BLOCK), 0)
    query_at = lax.broadcasted_iota(jnp.int32, (rows, BLOCK), 1) + first
    allowed = (key_segment == query_segment) & (key_at <= query_at)
    return jnp.where(allowed, 0.0, MASKED)


def segment_row(segments):
    return jnp.concatenate(
        [segments[rank, i : i + 1, :] for rank in range(4) for i in range(2)], axis=1
    ).astype(F32)


def gain_rows(small):
    return small[:, 768:896].astype(F32).T[32:40, :]


def column_of(row):
    return jnp.broadcast_to(row, (8, row.shape[1])).T[:, 0:1]


def front_kernel(
    hidden, weights, cosine, sine, segments, own_hidden, ids, out_grad, share_a, share_b,
    normed, query, key, value, context_t, log_total, middle, normed_moe, gating,
    over_z, over_x, quad_a, quad_b, out_grad_all, bias, part, context, through, *refs,
):
    pair_refs = refs[:3]
    send, recv, here = refs[3:]
    at = Place()
    greet(
        [
            at.sibling(), at.partner(), at.ring(1), at.ring(3),
            at.along("x", 1), at.along("x", 3), at.along("z", 1), at.along("z", 3),
        ]
    )
    ring = RingGather(at, out_grad, out_grad_all, send, recv, here.at[0], 0)
    lines = first_gather(
        at, share_a, share_b, over_z, over_x, send, recv, here.at[pl.ds(1, 4)], 9
    )
    quad = second_gather(
        at, 0, over_z, over_x, quad_a, quad_b, send, recv, here.at[pl.ds(5, 4)],
        9 + SpreadOut.COPIES, through,
    )
    scatter = PairScatter(at, part, pair_refs, send, recv, 9 + 2 * SpreadOut.COPIES)
    lines.begin()
    ring.begin()

    gains = gain_rows(weights)
    seg_row = segment_row(segments)
    seg_column = column_of(seg_row)
    for block in range(SEQ // BLOCK):
        rows = slice(block * BLOCK, (block + 1) * BLOCK)
        values = hidden[rows, :].astype(F32)
        scale = lax.rsqrt(jnp.mean(values * values, axis=-1, keepdims=True) + EPS)
        normed[rows, :] = (values * scale * gains[0:1, :]).astype(BF)
    for half in range(2):
        columns = slice(half * 128, half * 128 + 128)
        pre = mm(normed[...], weights[:, columns])
        query[:, columns] = (rotated(pre, cosine[...], sine[...]) * 0.125).astype(BF)
    key_pre = mm(normed[...], weights[:, 256:384])
    key[...] = rotated(key_pre, cosine[...], sine[...]).astype(BF)
    value_pre = mm(normed[...], weights[:, 384:512])
    value[...] = value_pre.astype(BF)
    value_t = value_pre.T.astype(BF)
    lines.forward()
    for block in range(SEQ // BLOCK):
        first, end = block * BLOCK, (block + 1) * BLOCK
        bias[:end, :] = bias_block(seg_column[:end, :], seg_row[:, first:end], first, end)
        for head in range(HEADS):
            kv = slice((head // 2) * HD, (head // 2) * HD + HD)
            own = slice(head * HD, head * HD + HD)
            scores = mm_last(key[:end, kv], query[first:end, own]) + bias[:end, :]
            top = jnp.max(scores, axis=0, keepdims=True)
            powers = jnp.exp(scores - top)
            total = jnp.sum(powers, axis=0, keepdims=True)
            share = (powers * (1.0 / total)).astype(BF)
            context_t[own, first:end] = mm(value_t[kv, :end], share).astype(BF)
            log_total[head : head + 1, first:end] = top + jnp.log(total)
        if block == 1:
            lines.finish()
            quad.begin()
        if block == 2:
            ring.forward_before()
            ring.forward_behind()
    context[...] = context_t[...].T

    def project(slot):
        rows = pl.ds(pl.multiple_of(slot * LOCAL, LOCAL), LOCAL)
        part[slot] = mm_last(context[rows, :], weights[:, 512:768]).astype(BF)

    project(scatter.other + 1 - at.core)
    scatter.begin_far()
    project(scatter.other + at.core)
    project(scatter.own + 1 - at.core)
    scatter.begin_own()
    project(scatter.own + at.core)
    scatter.forward()
    quad.forward()
    ring.forward_across()
    scatter.finish(middle)
    values = middle[...] + own_hidden[...].astype(F32)
    middle[...] = values
    scale = lax.rsqrt(jnp.mean(values * values, axis=-1, keepdims=True) + EPS)
    normed_moe[...] = (values * scale * gains[1:2, :]).astype(BF)
    lane = lax.broadcasted_iota(jnp.int32, (LOCAL, 128), 1)
    chosen = lane == ids[:, 0:1]
    for i in range(1, TOPK):
        chosen = chosen | (lane == ids[:, i : i + 1])
    logits = jnp.where(chosen, mm(normed_moe[...], weights[:, 768:896]), MASKED)
    powers = jnp.where(chosen, jnp.exp(logits - jnp.max(logits, axis=-1, keepdims=True)), 0.0)
    gating[...] = powers / jnp.sum(powers, axis=-1, keepdims=True)
    for i in (0, 4, 6, 7, 8):
        ring.copy(i).wait_recv()
    ring.sent()
    ring.kept().wait()
    quad.finish()


def front(hidden, weights, tables, segments, own_hidden, ids, out_grad, shares, ident):
    vmem = pl.BlockSpec(memory_space=pltpu.VMEM)
    hbm = pl.BlockSpec(memory_space=pl.ANY)
    sems = 9 + 2 * SpreadOut.COPIES + 1 + 2 * PIECES
    return pl.pallas_call(
        front_kernel,
        in_specs=[vmem] * 10,
        out_specs=[vmem] * 9 + [hbm] * 5,
        out_shape=[
            jax.ShapeDtypeStruct((SEQ, D), BF),
            jax.ShapeDtypeStruct((SEQ, HEADS * HD), BF),
            jax.ShapeDtypeStruct((SEQ, 128), BF),
            jax.ShapeDtypeStruct((SEQ, 128), BF),
            jax.ShapeDtypeStruct((HEADS * HD, SEQ), BF),
            jax.ShapeDtypeStruct((8, SEQ), F32),
            jax.ShapeDtypeStruct((LOCAL, D), F32),
            jax.ShapeDtypeStruct((LOCAL, D), BF),
            jax.ShapeDtypeStruct((LOCAL, 128), F32),
            *[LINE_SHAPE] * 2,
            *[QUAD_SHAPE] * 2,
            jax.ShapeDtypeStruct((8, LOCAL, D), BF),
        ],
        scratch_shapes=[
            pltpu.VMEM((SEQ, BLOCK), F32),
            pltpu.VMEM((4, LOCAL, D), BF),
            pltpu.VMEM((SEQ, HEADS * HD), BF),
            pltpu.VMEM((2, *BLOCK_SHAPE), BF),
            *pair_scratch(LOCAL, D),
            pltpu.SemaphoreType.DMA((sems,)),
            pltpu.SemaphoreType.DMA((sems,)),
            pltpu.SemaphoreType.DMA((9,)),
        ],
        compiler_params=pltpu.CompilerParams(
            collective_id=ident, has_side_effects=True, vmem_limit_bytes=56 * MIB
        ),
        name="front",
    )(hidden, weights, *tables, segments, own_hidden, ids, out_grad, *shares)


def by_owner(value):
    return value.astype(BF).reshape(4, 4, 2, 32, value.shape[1])


def back_kernel(
    dx, dgate, gating, middle, normed_moe, out_grad, y_part,
    normed, weights, cosine, sine, segments, query, key, value, context_t, log_total,
    own_weights, expert_a, expert_b,
    dmiddle, block_out, dn1, attention, rest, gate, up, down,
    bias, dcontext, dquery_t, dkey, dvalue, dall, dall_t, dattn_own, dattn_all, y_sum,
    grads, sum_1a, sum_1b, sum_2a, sum_2b, over_y, from_opposite, share_sum, shares,
    total_a, total_b, land_a, land_b, *refs,
):
    ring_refs, pair_refs = refs[:8], refs[8:11]
    first_refs = (refs[11:18], refs[18:25])
    groups = [refs[25 + 7 * i : 32 + 7 * i] for i in range(4)]
    landings = (refs[53:57], refs[57:61])
    send, recv, here, load = refs[61:]
    at = Place()
    greet(
        [
            at.sibling(), at.partner(), at.diagonal(), at.opposite(), at.ring(1), at.ring(3),
            at.along("x", 1), at.along("x", 3), at.along("z", 1), at.along("z", 3),
        ]
    )
    base = 9 + 2 * PIECES
    sums = [
        RingSum(at, "x", lambda k: expert_a.at[k], first_refs[0], send, recv, load, base),
        RingSum(
            at, "z", lambda k: expert_b.at[k], first_refs[1], send, recv, load,
            base + RingSum.COPIES, 3,
        ),
    ]
    for each in sums:
        each.begin()
    gain = gain_rows(weights)[1:2, :]
    chosen = gating[...]
    dchosen = chosen * (dgate[...] - jnp.sum(chosen * dgate[...], axis=-1, keepdims=True))
    dlogits = dchosen.astype(BF)
    dnormed = dx[...] + mm_last(dlogits, weights[:, 768:896])
    values = middle[...]
    scale = lax.rsqrt(jnp.mean(values * values, axis=-1, keepdims=True) + EPS)
    unit = values * scale
    weighted = dnormed * gain
    inner = jnp.mean(weighted * unit, axis=-1, keepdims=True)
    total = out_grad[...].astype(F32) + scale * (weighted - unit * inner)
    dmiddle[...] = total
    dattn_own[...] = total.astype(BF)
    gather = PairGather(at, dattn_own, dattn_all, send, recv, here, 8, PIECES)
    scatter = RingScatter(at, y_part, ring_refs, send, recv)
    for k in (2, 1, 3, 0):
        scatter.copy(k).start()
    router_part = mm(normed_moe[...].T, dlogits)
    gain_part = column_of(jnp.sum(dnormed * unit, axis=0, keepdims=True))
    lane = lax.broadcasted_iota(jnp.int32, (D, 128), 1)
    grads[..., 768:] = by_owner(jnp.where(lane == 32, gain_part, router_part))
    seg_row = segment_row(segments)
    seg_column = column_of(seg_row)
    gather.forward()
    scatter.far()
    for each in sums:
        each.middle()
        each.direct()
    gather.finish()
    dattn = dattn_all[...].reshape(SEQ, D)
    dcontext[...] = mm(dattn, weights[:, 512:768]).astype(BF)
    output_grad_t = mm(context_t[...], dattn)
    grads[..., 512:768] = by_owner(output_grad_t.T)
    key_t = key[...].astype(F32).T.astype(BF)
    dkey[...] = jnp.zeros_like(dkey)
    dvalue[...] = jnp.zeros_like(dvalue)
    for block in range(SEQ // BLOCK):
        first, end = block * BLOCK, (block + 1) * BLOCK
        bias[:end, :] = bias_block(seg_column[:end, :], seg_row[:, first:end], first, end)
        for head in range(HEADS):
            kv = slice((head // 2) * HD, (head // 2) * HD + HD)
            own = slice(head * HD, head * HD + HD)
            query_block = query[first:end, own]
            dcontext_block = dcontext[first:end, own]
            scores = mm_last(key[:end, kv], query_block) + bias[:end, :]
            share = jnp.exp(scores - log_total[head : head + 1, first:end])
            dshare = mm_last(value[:end, kv], dcontext_block)
            centre = jnp.sum(share * dshare, axis=0, keepdims=True)
            dscore = (share * (dshare - centre)).astype(BF)
            dquery_t[own, first:end] = mm(key_t[kv, :end], dscore) * 0.125
            dkey[:end, kv] += mm(dscore, query_block)
            dvalue[:end, kv] += mm(share.astype(BF), dcontext_block)
        if block == 0:
            scatter.up_side()
            scatter.down_side()
    turn = -sine[...]
    for half in range(2):
        rows = slice(half * 128, half * 128 + 128)
        piece = rotated(dquery_t[rows, :].T, cosine[...], turn)
        dall[:, rows] = piece.astype(BF)
        dall_t[rows, :] = piece.T.astype(BF)
    piece = rotated(dkey[...], cosine[...], turn)
    dall[:, 256:384] = piece.astype(BF)
    dall_t[256:384, :] = piece.T.astype(BF)
    dall[:, 384:512] = dvalue[...].astype(BF)
    dall_t[384:512, :] = dvalue[...].T.astype(BF)
    grads[..., 0:512] = by_owner(mm(dall_t[...], normed[...]).T)
    after = base + 2 * RingSum.COPIES
    width = grads.shape[-1]
    a, b = pl.ds(0, SPLIT), pl.ds(SPLIT, width - SPLIT)

    def ring_sum(i, axis, part_of, scratch):
        return RingSum(
            at, axis, part_of, scratch, send, recv, load, after + RingSum.COPIES * i, 6 + 3 * i
        )

    first_a = ring_sum(0, "x", lambda k: grads.at[k, :, :, :, a], groups[0])
    first_b = ring_sum(1, "z", lambda k: grads.at[:, k, :, :, b], groups[1])
    second_a = ring_sum(2, "z", lambda k: sum_1a.at[k], groups[2])
    second_b = ring_sum(3, "x", lambda k: sum_1b.at[k], groups[3])
    for each in (first_a, first_b):
        each.begin()
        each.direct()
    after = after + 4 * RingSum.COPIES
    pair = PairScatter(at, dattn_all, pair_refs, send, recv, after)
    after = after + 1 + 2 * PIECES

    def project(slot):
        rows = pl.ds(pl.multiple_of(slot * LOCAL, LOCAL), LOCAL)
        dattn_all[slot] = mm_last(dall[rows, :], weights[:, 0:512]).astype(BF)

    project(pair.other + 1 - at.core)
    pair.begin_far()
    project(pair.other + at.core)
    project(pair.own + 1 - at.core)
    pair.begin_own()
    project(pair.own + at.core)
    pair.forward()
    first_a.middle()
    first_b.middle()
    scatter.finish(y_sum)
    block_out[...] = (y_sum[...] + middle[...]).astype(BF)

    final_sums = []
    for i, (each, axis, refs_of, landing) in enumerate(
        zip(sums, ("z", "x"), first_refs, landings)
    ):
        each.finish(each.own)
        to_up, to_down, own = refs_of[4].at[0, pl.ds(0, 1)], refs_of[5].at[0, pl.ds(0, 1)], refs_of[2].at[0]
        final_sums.append(
            RingSum(
                at, axis, lambda k, own=each.own: own.at[k], (*landing, to_up, to_down, own),
                send, recv, load, after + RingSum.COPIES * i, 18 + 3 * i,
            )
        )
        final_sums[i].begin()
        final_sums[i].direct()
    after = after + 2 * RingSum.COPIES
    first_a.finish(sum_1a)
    second_a.begin()
    second_a.direct()
    first_b.finish(sum_1b)
    second_b.begin()
    second_b.direct()
    for each in final_sums:
        each.middle()
    second_a.middle()
    second_b.middle()
    second_a.finish(sum_2a)
    second_b.finish(sum_2b)
    over_y[:, a] = sum_2a[...].reshape(64, SPLIT)
    over_y[:, b] = sum_2b[...].reshape(64, width - SPLIT)
    theirs = pl.ds(pl.multiple_of((1 - at.yh) * 32, 32), 32)
    own = pl.ds(pl.multiple_of(at.yh * 32, 32), 32)
    swap = push(over_y.at[theirs], from_opposite, send, recv, after, at.opposite())
    lands = []
    for i, (each, out, land) in enumerate(
        zip(final_sums, (total_a, total_b), (land_a, land_b))
    ):
        each.finish(out)
        lands.append(push(out.at[1 - at.yh], land, send, recv, after + 1 + i, at.opposite()))
    pair.finish(dn1)
    swap.wait_recv()
    total = over_y[own, :].astype(F32) + from_opposite[...].astype(F32)
    attention[...] = total[:, :768]
    gain_part = jnp.sum(total[:, :512] * own_weights[...].astype(F32), axis=1, keepdims=True)
    lane = lax.broadcasted_iota(jnp.int32, (32, 128), 1)
    share_sum[...] = jnp.where(lane == 33, gain_part, total[:, 768:])
    copies = [
        push(share_sum, shares.at[i], send, recv, after + 3 + i, device)
        for i, device in enumerate((at.sibling(), at.partner(), at.diagonal()))
    ]
    mine, theirs = pl.ds(at.yh * STEPS, STEPS), pl.ds((1 - at.yh) * STEPS, STEPS)
    for j, value in enumerate((total_a, total_b)):
        for i, out in enumerate((gate, up, down)):
            out[mine, 2 * j : 2 * j + 2] = value[at.yh, :, i].astype(F32)
    rest[...] = share_sum[...]
    for i, copy in enumerate(copies):
        copy.wait_recv()
        rest[...] += shares[i]
    for j, (copy, land) in enumerate(zip(lands, (land_a, land_b))):
        copy.wait_recv()
        for i, out in enumerate((gate, up, down)):
            out[theirs, 2 * j : 2 * j + 2] = land[:, i].astype(F32)
    for copy in (swap, *copies, *lands):
        copy.wait_send()


def back(
    dx, dgate, gating, middle, normed_moe, out_grad, y_part,
    normed, weights, tables, segments, kept, own_weights, expert_grads, ident,
):
    vmem = pl.BlockSpec(memory_space=pltpu.VMEM)
    hbm = pl.BlockSpec(memory_space=pl.ANY)
    sems = 2 * (9 + 2 * PIECES) + 8 * RingSum.COPIES + 6
    block = SUMS_SHAPE.shape[1:]
    half = (block[0] // 2, *block[1:])
    first_a, first_b = (4, 2, 32, SPLIT), (4, 2, 32, SMALL - SPLIT)
    landing = [pltpu.VMEM(half, BF)] * 2 + [pltpu.VMEM(block, BF)] * 2
    return pl.pallas_call(
        back_kernel,
        in_specs=[vmem] * 18 + [hbm] * 2,
        out_specs=[vmem] * 8,
        out_shape=[
            jax.ShapeDtypeStruct((LOCAL, D), F32),
            jax.ShapeDtypeStruct((LOCAL, D), BF),
            jax.ShapeDtypeStruct((LOCAL, D), F32),
            jax.ShapeDtypeStruct((32, 768), F32),
            jax.ShapeDtypeStruct((32, 128), F32),
            *[jax.ShapeDtypeStruct((2 * STEPS, QUAD, 32, FF), F32)] * 3,
        ],
        scratch_shapes=[
            pltpu.VMEM((SEQ, BLOCK), F32),
            pltpu.VMEM((SEQ, HEADS * HD), BF),
            pltpu.VMEM((HEADS * HD, SEQ), F32),
            pltpu.VMEM((SEQ, 128), F32),
            pltpu.VMEM((SEQ, 128), F32),
            pltpu.VMEM((SEQ, 512), BF),
            pltpu.VMEM((512, SEQ), BF),
            pltpu.VMEM((LOCAL, D), BF),
            pltpu.VMEM((4, LOCAL, D), BF),
            pltpu.VMEM((LOCAL, D), F32),
            pltpu.VMEM((4, 4, 2, 32, SMALL), BF),
            pltpu.VMEM(first_a, BF),
            pltpu.VMEM(first_b, BF),
            pltpu.VMEM(first_a[1:], BF),
            pltpu.VMEM(first_b[1:], BF),
            pltpu.VMEM((64, SMALL), BF),
            pltpu.VMEM((32, SMALL), BF),
            pltpu.VMEM((32, 128), F32),
            pltpu.VMEM((3, 32, 128), F32),
            *[pltpu.VMEM(block, BF)] * 2,
            *[pltpu.VMEM(block[1:], BF)] * 2,
            *ring_scratch(LOCAL, D),
            *pair_scratch(LOCAL, D),
            *sum_scratch(SUMS_SHAPE.shape),
            *sum_scratch(SUMS_SHAPE.shape),
            *sum_scratch(first_a),
            *sum_scratch(first_b),
            *sum_scratch(first_a[1:]),
            *sum_scratch(first_b[1:]),
            *landing,
            *landing,
            pltpu.SemaphoreType.DMA((sems,)),
            pltpu.SemaphoreType.DMA((sems,)),
            pltpu.SemaphoreType.DMA,
            pltpu.SemaphoreType.DMA((24,)),
        ],
        compiler_params=pltpu.CompilerParams(
            collective_id=ident, has_side_effects=True, vmem_limit_bytes=63 * MIB
        ),
        name="back",
    )(
        dx, dgate, gating, middle, normed_moe, out_grad, y_part,
        normed, weights, *tables, segments, *kept, own_weights, *expert_grads,
    )


def experts_kernel(
    x_in, gate_in, d_in, over_z, over_x, quad_0a, quad_0b, y_out, dx_out, dgate_out,
    grads_a, grads_b, quad_1a, quad_1b, quad_2a, quad_2b, quad_3a, quad_3b,
    x, d, xt, dt, y, dx, gating, dgate, dgate_part, hidden, w, *refs,
):
    dx_scratch, dgate_scratch = refs[:5], refs[5:10]
    send, recv, here, load, store, fetch = refs[10:16]
    at = Place()
    step = pl.program_id(0)
    opening, closing = step == 0, step == STEPS - 1
    rows_at_once = 2 * LOCAL
    lane = lax.broadcasted_iota(jnp.int32, (LOCAL, 128), 1)
    own_first = at.yh * 16 + step * QUAD
    x_gather = RingGather(at, x_in, x, send, recv, here.at[0], 0)
    gate_gather = RingGather(at, gate_in, gating, send, recv, here.at[1], 9)
    gathers = (x_gather, gate_gather)
    scatters = (
        RingScatter(at, d, dx_scratch, send, recv, 18),
        RingScatter(at, dgate_part, dgate_scratch, send, recv, 26),
    )

    later = ((quad_1a, quad_1b), (quad_2a, quad_2b), (quad_3a, quad_3b))
    quads = [
        second_gather(
            at, 1 + i, over_z, over_x, *quad, *refs[16:18], refs[18].at[pl.ds(4 * i, 4)],
            SpreadOut.COPIES * i, refs[19],
        )
        for i, quad in enumerate(later)
    ]

    def ride(condition, what):
        for i, quad in enumerate(quads):

            @pl.when(condition & (step == i))
            def _():
                what(quad)

    def fetches(quad_a, quad_b):
        copies = []
        for g in range(3):
            for i in range(QUAD):
                columns = pl.ds((g * QUAD + i) * FF, FF)
                if i < 2:
                    parts = [(quad_a.at[:, :, :, g, i], w.at[:, :, :, :, columns])]
                else:
                    parts = [
                        (quad_b.at[:, x_at, :, g, i - 2], w.at[x_at, :, :, :, columns])
                        for x_at in range(4)
                    ]
                for part in parts:
                    copies.append(pltpu.make_async_copy(*part, fetch.at[len(copies)]))
        return copies

    def d_load(chip):
        two = pl.ds(chip * 2, 2)
        return pltpu.make_async_copy(d_in.at[two], d.at[two], load.at[chip])

    def y_store(chip):
        two = pl.ds(chip * 2, 2)
        return pltpu.make_async_copy(x.at[two], y_out.at[two], store.at[chip])

    @pl.when(opening)
    def _():
        greet(
            [
                at.sibling(), at.ring(1), at.ring(3),
                at.along("x", 1), at.along("x", 3), at.along("z", 1), at.along("z", 3),
            ]
        )
        for gather in gathers:
            gather.begin()
        for copy in fetches(quad_0a, quad_0b):
            copy.start()
        for chip in range(4):
            d_load(chip).start()

    for copy in fetches(quad_0a, quad_0b):
        copy.wait()

    ride(step < STEPS, lambda quad: quad.begin())

    def arrive(turn):
        @pl.when(turn == 0)
        def _():
            for gather in gathers:
                gather.kept().wait()
                gather.copy(0).wait_recv()

        @pl.when(turn == 1)
        def _():
            for gather in gathers:
                gather.forward_before()
                gather.forward_behind()
            for gather in gathers:
                gather.copy(4).wait_recv()

        @pl.when(turn == 2)
        def _():
            for gather in gathers:
                gather.forward_across()
            for gather in gathers:
                gather.copy(6).wait_recv()

        @pl.when(turn == 3)
        def _():
            for gather in gathers:
                gather.copy(7).wait_recv()
                gather.copy(8).wait_recv()

    def leave(turn):
        @pl.when(turn == 0)
        def _():
            for scatter in scatters:
                scatter.copy(2).start()

        @pl.when(turn == 1)
        def _():
            for scatter in scatters:
                scatter.copy(1).start()
                scatter.far()

        @pl.when(turn == 2)
        def _():
            for scatter in scatters:
                scatter.copy(3).start()
                scatter.up_side()

        @pl.when(turn == 3)
        def _():
            for scatter in scatters:
                scatter.copy(0).start()
                scatter.down_side()

    def tokens_block(turn, carry):
        inward = jnp.where(turn == 0, 0, jnp.where(turn == 1, 3, turn - 1))
        outward = jnp.where(turn == 0, 2, jnp.where(turn == 3, 0, turn * 2 - 1))
        chip = at.chip(jnp.where(closing, outward, inward))
        two = pl.ds(chip * 2, 2)
        rows = pl.ds(pl.multiple_of(chip * rows_at_once, rows_at_once), rows_at_once)

        @pl.when(opening)
        def _():
            arrive(turn)
            d_load(chip).wait()
            xt[:, rows] = x[two].reshape(rows_at_once, D).T
            dt[:, rows] = d[two].reshape(rows_at_once, D).T
            y[rows, :] = jnp.zeros((rows_at_once, D), F32)
            dx[rows, :] = jnp.zeros((rows_at_once, D), F32)
            dgate[rows, :] = jnp.zeros((rows_at_once, 128), F32)

        ride(turn == 3, lambda quad: quad.forward())
        gate_up = w[:, :, :, :, 0 : 2 * F].reshape(D, 2 * F)
        down = w[:, :, :, :, 2 * F :].reshape(D, F)
        for core in range(2):
            slot = chip * 2 + core
            part = pl.ds(pl.multiple_of(slot * LOCAL, LOCAL), LOCAL)
            both = mm(x[slot], gate_up)
            gate, up = both[:, :F], both[:, F:]
            dact = mm(d[slot], down)
            turned = pltpu.roll(gating[slot], lax.rem(128 - own_first, 128), 1)
            factor = jnp.concatenate(
                [jnp.broadcast_to(turned[:, i : i + 1], (LOCAL, FF)) for i in range(QUAD)],
                axis=1,
            )
            q = 1.0 / (1.0 + jnp.exp(-gate))
            silu = gate * q
            act = silu * up
            product = act * dact
            sums = dgate[part, :]
            for i in range(QUAD):
                own = jnp.sum(product[:, i * FF : (i + 1) * FF], axis=1, keepdims=True)
                sums = jnp.where(lane == own_first + i, own, sums)
            dgate[part, :] = sums
            dact = dact * factor
            hidden[part, 0:F] = (dact * up * (q + silu * (1.0 - q))).astype(BF)
            hidden[part, F : 2 * F] = (dact * silu).astype(BF)
            hidden[part, 2 * F :] = (act * factor).astype(BF)
        y[rows, :] += mm_last(hidden[rows, 2 * F :], down)
        dx[rows, :] += mm_last(hidden[rows, 0 : 2 * F], gate_up)

        @pl.when(closing)
        def _():
            x[two] = y[rows, :].astype(BF).reshape(2, LOCAL, D)
            d[two] = dx[rows, :].astype(BF).reshape(2, LOCAL, D)
            dgate_part[two] = dgate[rows, :].astype(BF).reshape(2, LOCAL, 128)
            y_store(chip).start()
            leave(turn)

        return carry

    lax.fori_loop(0, 4, tokens_block, 0)

    @pl.when(opening)
    def _():
        for gather in gathers:
            gather.sent()

    def grads_block(block, carry):
        rows = pl.ds(pl.multiple_of(block * 512, 512), 512)

        def put(g, value):
            value = value.astype(BF).reshape(2, 4, 2, 32, value.shape[1])
            for j in range(value.shape[-1] // FF):
                piece = value[..., j * FF : (j + 1) * FF]
                group, i = g + j // QUAD, j % QUAD
                for x_at in range(2):
                    if i < 2:
                        grads_a[block * 2 + x_at, :, :, 0, group, i] = piece[x_at]
                    else:
                        grads_b[:, block * 2 + x_at, :, 0, group, i - 2] = piece[x_at]

        ride(block == 1, lambda quad: quad.finish())
        for number, quad in enumerate(later):

            @pl.when((block == 1) & (step == number))
            def _():
                for copy in fetches(*quad):
                    copy.start()

        put(0, mm(xt[rows, :], hidden[:, 0 : 2 * F]))
        put(2, mm(dt[rows, :], hidden[:, 2 * F :]))
        return carry

    lax.fori_loop(0, D // 512, grads_block, 0)

    @pl.when(closing)
    def _():
        scatters[0].finish(dx_out)
        scatters[1].finish(dgate_out)
        for chip in range(4):
            y_store(chip).wait()


def experts(x, gating, d, lines, quad, ident):
    hbm = pl.BlockSpec(memory_space=pl.ANY)

    def whole(rows, columns):
        return pl.BlockSpec((rows, columns), lambda step: (0, 0), pipeline_mode=pl.Buffered(1))

    each_step = pl.BlockSpec(
        (4, 4, 2, 1, 3, 2, 32, FF),
        lambda step: (0, 0, 0, step, 0, 0, 0, 0),
        pipeline_mode=pl.Buffered(1),
    )
    return pl.pallas_call(
        experts_kernel,
        grid=(STEPS,),
        in_specs=[hbm] * 7,
        out_specs=[
            hbm,
            whole(LOCAL, D),
            whole(LOCAL, 128),
            each_step,
            each_step,
            *[hbm] * 6,
        ],
        out_shape=[
            jax.ShapeDtypeStruct((8, LOCAL, D), BF),
            jax.ShapeDtypeStruct((LOCAL, D), F32),
            jax.ShapeDtypeStruct((LOCAL, 128), F32),
            GRADS_SHAPE,
            GRADS_SHAPE,
            *[QUAD_SHAPE] * 6,
        ],
        scratch_shapes=[
            pltpu.VMEM((8, LOCAL, D), BF),
            pltpu.VMEM((8, LOCAL, D), BF),
            pltpu.VMEM((D, TOKENS), BF),
            pltpu.VMEM((D, TOKENS), BF),
            pltpu.VMEM((TOKENS, D), F32),
            pltpu.VMEM((TOKENS, D), F32),
            pltpu.VMEM((8, LOCAL, 128), F32),
            pltpu.VMEM((TOKENS, 128), F32),
            pltpu.VMEM((8, LOCAL, 128), BF),
            pltpu.VMEM((TOKENS, 3 * F), BF),
            pltpu.VMEM((4, 4, 2, 32, 3 * F), BF),
            *ring_scratch(LOCAL, D, False),
            *ring_scratch(LOCAL, 128, False),
            pltpu.SemaphoreType.DMA((34,)),
            pltpu.SemaphoreType.DMA((34,)),
            pltpu.SemaphoreType.DMA((2,)),
            pltpu.SemaphoreType.DMA((4,)),
            pltpu.SemaphoreType.DMA((4,)),
            pltpu.SemaphoreType.DMA((30,)),
            pltpu.SemaphoreType.DMA((3 * SpreadOut.COPIES,)),
            pltpu.SemaphoreType.DMA((3 * SpreadOut.COPIES,)),
            pltpu.SemaphoreType.DMA((12,)),
            pltpu.VMEM((2, *BLOCK_SHAPE), BF),
        ],
        compiler_params=pltpu.CompilerParams(
            collective_id=ident, has_side_effects=True, vmem_limit_bytes=63 * MIB
        ),
        name="experts",
    )(x, gating, d, *lines, *quad)[:5]


def norm_scale(values):
    return lax.rsqrt(jnp.mean(values * values, axis=-1, keepdims=True) + EPS)


def norm_grad(values, gain, dnormed):
    scale = norm_scale(values)
    unit = values * scale
    weighted = dnormed * gain
    dvalues = scale * (weighted - unit * jnp.mean(weighted * unit, axis=-1, keepdims=True))
    return dvalues


def on_device(
    hidden_in, out_grad, attn_gain, query_weight, key_weight, value_weight, output_weight,
    moe_gain, router_weight, expert_gate, expert_up, expert_down, expert_ids, segment_ids,
):
    gains = jnp.stack([attn_gain, moe_gain])
    smalls = (query_weight, key_weight, value_weight, output_weight, router_weight, gains)
    own_shares = (expert_gate, expert_up, expert_down)
    hidden_all, segments, small, *shares = startup(
        hidden_in, segment_ids.reshape(2, 128), smalls, own_shares, 0
    )
    tables = tuple(jnp.asarray(t) for t in rotary_tables())
    normed, *more, d = front(
        hidden_all, small, tables, segments, hidden_in, expert_ids, out_grad, shares, 1
    )
    kept, (middle, normed_moe, gating), lines, quad = more[:5], more[5:8], more[8:10], more[10:]
    y, dx, dgate, *expert_grads = experts(normed_moe, gating, d, lines, quad, 3)
    own_weights = jnp.concatenate([query_weight, key_weight, value_weight], axis=1)
    dmiddle, block_out, dn1, attention_grads, rest, *expert_grads = back(
        dx, dgate, gating, middle, normed_moe, out_grad, y,
        normed, small, tables, segments, kept, own_weights, expert_grads, 5,
    )
    hidden = hidden_in.astype(F32)
    dhidden = norm_grad(hidden, small[:, 800].astype(F32), dn1)
    hidden_grad = dmiddle + dhidden
    expert_grads = [share.reshape(E, 32, FF) for share in expert_grads]
    return (
        block_out,
        hidden_grad,
        rest[:, 33] / attn_gain.astype(F32),
        attention_grads[:, 0:256],
        attention_grads[:, 256:384],
        attention_grads[:, 384:512],
        attention_grads[:, 512:768],
        rest[:, 32],
        rest[:, :32],
        *expert_grads,
    )


def solution(mesh):
    fine = Mesh(np.asarray(mesh.devices).reshape(4, 4, 2, 2, 2), ALL)
    return jax.shard_map(
        on_device,
        mesh=fine,
        in_specs=(
            P(ALL, None),
            P(ALL, None),
            P(DP),
            P(DP, TENSOR),
            P(DP, TENSOR),
            P(DP, TENSOR),
            P(DP, TENSOR),
            P(DP),
            P(DP, None),
            P(None, DP, TENSOR),
            P(None, DP, TENSOR),
            P(None, DP, TENSOR),
            P(ALL, None),
            P(ALL),
        ),
        out_specs=(
            P(ALL, None),
            P(ALL, None),
            P(DP),
            P(DP, TENSOR),
            P(DP, TENSOR),
            P(DP, TENSOR),
            P(DP, TENSOR),
            P(DP),
            P(DP, None),
            P(None, DP, TENSOR),
            P(None, DP, TENSOR),
            P(None, DP, TENSOR),
        ),
        check_vma=False,
    )
```

```python
import jax
import jax.numpy as jnp
import numpy as np
from jax import lax
from jax.experimental import pallas as pl
from jax.experimental.pallas import tpu as pltpu
from jax.sharding import Mesh
from jax.sharding import PartitionSpec as P

D = 1024
HD = 64
E = 32
SEQ = 1024
LOCAL = 256
HEADS = 4
QUAD = 4
FF = 128
F = QUAD * FF
EPS = 1e-06
TOPK = 8
MASKED = -1e30
BLOCK = 256
TOKENS = 2048
STEPS = 4

DP = ("x", "z", "yh")
TENSOR = ("yl", "core")
RING = ("yh", "yl", "core")
PLANE = ("x", "z")
ALL = ("x", "z", "yh", "yl", "core")

F32 = jnp.float32
BF = jnp.bfloat16
LAST = (((1,), (1,)), ((), ()))
MIB = 1024 * 1024
MESH = pl.DeviceIdType.MESH
SMALL = 896


def mm(a, b):
    return jnp.dot(a, b, preferred_element_type=F32)


def mm_last(a, b):
    return lax.dot_general(a, b, LAST, preferred_element_type=F32)


class Place:
    def __init__(self):
        self.x = lax.axis_index("x")
        self.z = lax.axis_index("z")
        self.yh = lax.axis_index("yh")
        self.yl = lax.axis_index("yl")
        self.core = lax.axis_index("core")
        self.y = self.yh * 2 + self.yl

    def chip(self, k):
        return lax.rem(self.y + k, 4)

    def ring(self, k):
        chip = self.chip(k)
        return {"yh": chip // 2, "yl": lax.rem(chip, 2)}

    def along(self, axis, k):
        return {axis: lax.rem(getattr(self, axis) + k, 4)}

    def sibling(self):
        return {"core": 1 - self.core}

    def partner(self):
        return {"yl": 1 - self.yl}

    def diagonal(self):
        return {"yl": 1 - self.yl, "core": 1 - self.core}

    def opposite(self):
        return {"yh": 1 - self.yh}


def greet(devices):
    barrier = pltpu.get_barrier_semaphore()
    for device in devices:
        pl.semaphore_signal(barrier, inc=1, device_id=device, device_id_type=MESH)
    pl.semaphore_wait(barrier, len(devices))


def remote(src, dst, send, recv, i, device):
    return pltpu.make_async_remote_copy(
        src_ref=src, dst_ref=dst, send_sem=send.at[i], recv_sem=recv.at[i],
        device_id=device, device_id_type=MESH,
    )


def push(src, dst, send, recv, i, device):
    copy = remote(src, dst, send, recv, i, device)
    copy.start()
    return copy


def keep(src, dst, sem):
    copy = pltpu.make_async_copy(src, dst, sem)
    copy.start()
    return copy


class RingGather:
    def __init__(self, at, own, out, send, recv, here, base=0):
        self.at, self.own, self.out, self.base = at, own, out, base
        self.send, self.recv, self.here = send, recv, here
        half = own.shape[0] // 2
        lo, hi = pl.ds(0, half), pl.ds(half, half)
        me, before, behind, across = (out.at[self.slot(k)] for k in (0, 3, 1, 2))
        near, up, down = at.sibling(), at.ring(1), at.ring(3)
        self.plan = [
            (own, me, near),
            (own, me, up),
            (own, me, down),
            (before.at[lo], before.at[lo], up),
            (before, before, near),
            (behind.at[hi], behind.at[hi], down),
            (behind, behind, near),
            (across.at[lo], across.at[lo], near),
            (across.at[hi], across.at[hi], near),
        ]

    def slot(self, k):
        return self.at.chip(k) * 2 + self.at.core

    def copy(self, i):
        src, dst, device = self.plan[i]
        return remote(src, dst, self.send, self.recv, self.base + i, device)

    def kept(self):
        return pltpu.make_async_copy(self.own, self.out.at[self.slot(0)], self.here)

    def begin(self):
        self.kept().start()
        for i in (1, 2, 0):
            self.copy(i).start()

    def forward_before(self):
        self.copy(1).wait_recv()
        self.copy(3).start()
        self.copy(4).start()

    def forward_behind(self):
        self.copy(2).wait_recv()
        self.copy(5).start()
        self.copy(6).start()

    def forward_across(self):
        self.copy(3).wait_recv()
        self.copy(7).start()
        self.copy(5).wait_recv()
        self.copy(8).start()

    def sent(self):
        for i in range(9):
            self.copy(i).wait_send()


class PairGather:
    def __init__(self, at, own, out, send, recv, here, base, pieces):
        self.at, self.out, self.send, self.recv, self.base = at, out, send, recv, base
        size = own.shape[0] // pieces
        self.parts = [pl.ds(i * size, size) for i in range(pieces)]
        me = at.yl * 2 + at.core
        self.other = (1 - at.yl) * 2 + at.core
        self.kept = keep(own, out.at[me], here)
        self.far = [
            push(own.at[part], out.at[me, part], send, recv, base + 1 + i, at.partner())
            for i, part in enumerate(self.parts)
        ]
        self.near = [push(own, out.at[me], send, recv, base, at.sibling())]

    def forward(self):
        for i, part in enumerate(self.parts):
            self.far[i].wait_recv()
            view = self.out.at[self.other, part]
            index = self.base + 1 + len(self.parts) + i
            self.near.append(push(view, view, self.send, self.recv, index, self.at.sibling()))

    def finish(self):
        for copy in self.near:
            copy.wait_recv()
        for copy in (*self.far, *self.near):
            copy.wait_send()
        self.kept.wait()


PIECES = 4


class AxisGather:
    def __init__(self, at, axis, view, send, recv, base):
        self.up, self.down = at.along(axis, 1), at.along(axis, 3)
        self.view, self.send, self.recv, self.base = view, send, recv, base

    def go(self, i, view, device):
        return push(view, view, self.send, self.recv, self.base + i, device)

    def begin(self):
        self.first = [
            self.go(0, self.view(0, "all"), self.up), self.go(1, self.view(0, "all"), self.down),
        ]

    def forward(self):
        self.first[0].wait_recv()
        self.far = [self.go(2, self.view(3, "low"), self.up)]
        self.first[1].wait_recv()
        self.far.append(self.go(3, self.view(1, "high"), self.down))

    def finish(self):
        for copy in self.far:
            copy.wait_recv()
        for copy in (*self.first, *self.far):
            copy.wait_send()


def halves_of(ref, first, size):
    spans = {"all": (0, size), "low": (0, size // 2), "high": (size // 2, size // 2)}
    return lambda part: ref.at[pl.ds(first + spans[part][0], spans[part][1])]


class SpreadOut:
    COPIES = 8

    def __init__(self, at, rings, send, recv, here, base=0, through=None):
        self.send, self.recv, self.here, self.base = send, recv, here, base
        self.through = through
        self.own = [(own, slot(0)) for _, own, slot, _ in rings]
        self.plan = []
        for axis, own, slot, _ in rings:
            self.plan.append((own, slot(0), at.along(axis, 1)))
            self.plan.append((own, slot(0), at.along(axis, 3)))
        for axis, _, slot, half in rings:
            low, high = (slot(3).at[pl.ds(0, half)], slot(1).at[pl.ds(half, half)])
            self.plan.append((low, low, at.along(axis, 1)))
            self.plan.append((high, high, at.along(axis, 3)))

    def copy(self, i):
        src, dst, device = self.plan[i]
        return remote(src, dst, self.send, self.recv, self.base + i, device)

    def loaded(self, i):
        return pltpu.make_async_copy(self.own[i][0], self.through.at[i], self.here.at[i])

    def kept(self, i):
        src, dst = self.own[i]
        src = src if self.through is None else self.through.at[i]
        return pltpu.make_async_copy(src, dst, self.here.at[2 + i])

    def begin(self):
        for i in range(4):
            self.copy(i).start()
        for i in range(2):
            (self.kept(i) if self.through is None else self.loaded(i)).start()

    def forward(self):
        for i in range(4):
            self.copy(i).wait_recv()
            self.copy(4 + i).start()
        if self.through is not None:
            for i in range(2):
                self.loaded(i).wait()
                self.kept(i).start()

    def finish(self):
        for i in range(4, 8):
            self.copy(i).wait_recv()
        for i in range(8):
            self.copy(i).wait_send()
        for i in range(2):
            self.kept(i).wait()


def ring_slots(out, place):
    return lambda k: out.at[lax.rem(place + k, 4)]


def first_gather(at, own_a, own_b, over_z, over_x, *sems):
    rings = (
        ("z", own_a, ring_slots(over_z, at.z), 1), ("x", own_b, ring_slots(over_x, at.x), 1),
    )
    return SpreadOut(at, rings, *sems)


def second_gather(at, number, over_z, over_x, quad_a, quad_b, *sems):
    rings = (
        ("x", over_z.at[:, :, number], ring_slots(quad_a, at.x), 2),
        ("z", over_x.at[:, :, number], ring_slots(quad_b, at.z), 2),
    )
    return SpreadOut(at, rings, *sems)


SHARE_SHAPE = jax.ShapeDtypeStruct((2, STEPS, 3, 2, 32, FF), BF)
BLOCK_SHAPE = (4, 2, 3, 2, 32, FF)
LINE_SHAPE = jax.ShapeDtypeStruct((4, 2, STEPS, 3, 2, 32, FF), BF)
QUAD_SHAPE = jax.ShapeDtypeStruct((4, 4, 2, 3, 2, 32, FF), BF)
GRADS_SHAPE = jax.ShapeDtypeStruct((4, 4, 2, STEPS, 3, 2, 32, FF), BF)
LAND_SHAPE = jax.ShapeDtypeStruct((2, 2, STEPS, 3, 2, 32, FF), BF)
SUMS_SHAPE = jax.ShapeDtypeStruct((4, 2, STEPS, 3, 2, 32, FF), BF)


class RingSum:
    COPIES = 6

    def __init__(
        self, at, axis, part_of, scratch, send, recv, load, base=0, first=0, arrived=None
    ):
        half_a, half_b, up, down, to_up, to_down, own = scratch
        self.half_a, self.half_b, self.up, self.down = half_a, half_b, up, down
        self.to_up, self.to_down, self.own = to_up, to_down, own
        self.send, self.recv, self.base = send, recv, base
        size = half_a.shape[0]
        lo, hi = pl.ds(0, size), pl.ds(size, size)
        place = {"x": at.x, "z": at.z}[axis]
        here, above, across, below = (part_of(lax.rem(place + k, 4)) for k in range(4))
        upper, lower = at.along(axis, 1), at.along(axis, 3)
        self.plan = [
            (across.at[lo], half_a, upper),
            (across.at[hi], half_b, lower),
            (above.at[hi], up.at[hi], upper),
            (below.at[lo], down.at[lo], lower),
            (to_up, up.at[lo], upper),
            (to_down, down.at[hi], lower),
        ]
        pieces = [(above.at[lo], to_up), (below.at[hi], to_down), (here, own)]
        self.arrived = arrived is not None
        if self.arrived:
            pieces += zip(arrived, (half_a, half_b, up.at[hi], down.at[lo]))
        self.loads = [
            pltpu.make_async_copy(src, dst, load.at[first + i])
            for i, (src, dst) in enumerate(pieces)
        ]

    def copy(self, i):
        src, dst, device = self.plan[i]
        return remote(src, dst, self.send, self.recv, self.base + i, device)

    def begin(self):
        if not self.arrived:
            for i in range(2):
                self.copy(i).start()
        for load in self.loads:
            load.start()

    def direct(self):
        for i in (2, 3):
            self.copy(i).start()

    def landed(self, i):
        if self.arrived and i < 4:
            self.loads[3 + i].wait()
        else:
            self.copy(i).wait_recv()

    def middle(self):
        for i, (total, landed) in enumerate(
            ((self.to_up, self.half_a), (self.to_down, self.half_b))
        ):
            self.loads[i].wait()
            self.landed(i)

            def add(i, carry, total=total, landed=landed):
                total[i] = (total[i].astype(F32) + landed[i].astype(F32)).astype(BF)
                return carry

            lax.fori_loop(0, total.shape[0], add, 0)
            self.copy(4 + i).start()

    def finish(self, out):
        self.loads[2].wait()
        for i in range(2, 6):
            self.landed(i)

        def add(i, carry):
            total = self.own[i].astype(F32) + self.up[i].astype(F32)
            out[i] = (total + self.down[i].astype(F32)).astype(out.dtype)
            return carry

        lax.fori_loop(0, out.shape[0], add, 0)
        for i in range(4 if self.arrived else 0, 6):
            self.copy(i).wait_send()


def sum_scratch(block):
    half, whole = pltpu.VMEM((block[0] // 2, *block[1:]), BF), pltpu.VMEM(block, BF)
    return [half, half, whole, whole, half, half, whole]


def startup_kernel(
    hidden, segment_rows, query, key, value, output, router, gains, gate, up, down,
    hidden_all, segment_all, small_all, share_a, share_b, small, segment, send, recv, here,
):
    at = Place()
    greet(
        [
            at.sibling(), at.partner(), at.diagonal(), at.opposite(),
            at.along("x", 1), at.along("x", 3), at.along("z", 1), at.along("z", 3),
        ]
    )
    small[:, 0:256] = query[...]
    small[:, 256:384] = key[...]
    small[:, 384:512] = value[...]
    small[:, 512:768] = output[...]
    columns = jnp.broadcast_to(gains[...].astype(F32)[:, None, :], (2, 8, 32))
    columns = [columns[i].T[:, 0:1].astype(BF) for i in range(2)]
    blank = jnp.zeros((32, 94), BF)
    small[:, 768:896] = jnp.concatenate([router[...], *columns, blank], axis=1)
    segment[0:2, :] = segment_rows[...]
    segment[2:8, :] = jnp.zeros((6, 128), jnp.int32)
    rank = at.yl * 2 + at.core
    mine = small_all.at[(at.x * 4 + at.z) * 2 + at.yh]
    small_kept = keep(small, mine, here.at[0])
    copies = [push(small, mine, send, recv, 0, at.opposite())]
    swaps, swaps_kept = [], []
    base = 13 + 2 * PIECES
    for i, share in enumerate((gate, up, down)):
        for j, out in enumerate((share_a, share_b)):
            dst, two = out.at[at.yh, :, i], pl.ds(2 * j, 2)
            theirs = share.at[pl.ds((1 - at.yh) * STEPS, STEPS), two]
            index = 2 * i + j
            swaps.append(push(theirs, dst, send, recv, base + index, at.opposite()))
            own = share.at[pl.ds(at.yh * STEPS, STEPS), two]
            swaps_kept.append(keep(own, dst, here.at[3 + index]))
    copies.extend(
        push(segment, segment_all.at[rank], send, recv, 1 + i, device)
        for i, device in enumerate((at.sibling(), at.partner(), at.diagonal()))
    )
    pair = PairGather(at, hidden, hidden_all, send, recv, here.at[1], 12, PIECES)
    seg_here = keep(segment, segment_all.at[rank], here.at[2])
    over_z = AxisGather(
        at, "z",
        lambda k, part: halves_of(small_all, (at.x * 4 + lax.rem(at.z + k, 4)) * 2, 2)(part),
        send, recv, 4,
    )
    over_x = AxisGather(
        at, "x", lambda k, part: halves_of(small_all, lax.rem(at.x + k, 4) * 8, 8)(part),
        send, recv, 8,
    )
    small_kept.wait()
    copies[0].wait_recv()
    over_z.begin()
    over_z.forward()
    over_z.finish()
    over_x.begin()
    pair.forward()
    for swap, own in zip(swaps, swaps_kept):
        swap.wait_recv()
        own.wait()
    over_x.forward()
    pair.finish()
    seg_here.wait()
    for copy in copies[1:]:
        copy.wait_recv()
    over_x.finish()
    for copy in (*copies, *swaps):
        copy.wait_send()


def startup(hidden, segment, smalls, shares, ident):
    hbm = pl.BlockSpec(memory_space=pl.ANY)
    vmem = pl.BlockSpec(memory_space=pltpu.VMEM)
    sems = 13 + 2 * PIECES + 6
    shares = [share.reshape(2 * STEPS, QUAD, 32, FF) for share in shares]
    hidden_all, segment_all, small_all, share_a, share_b = pl.pallas_call(
        startup_kernel,
        in_specs=[vmem] * 8 + [hbm] * 3,
        out_specs=[hbm] * 3 + [vmem] * 2,
        out_shape=[
            jax.ShapeDtypeStruct((4, *hidden.shape), hidden.dtype),
            jax.ShapeDtypeStruct((4, 8, 128), segment.dtype),
            jax.ShapeDtypeStruct((32, 32, SMALL), BF),
            SHARE_SHAPE,
            SHARE_SHAPE,
        ],
        scratch_shapes=[
            pltpu.VMEM((32, SMALL), BF),
            pltpu.VMEM((8, 128), jnp.int32),
            pltpu.SemaphoreType.DMA((sems,)),
            pltpu.SemaphoreType.DMA((sems,)),
            pltpu.SemaphoreType.DMA((9,)),
        ],
        compiler_params=pltpu.CompilerParams(collective_id=ident, has_side_effects=True),
        name="startup",
    )(hidden, segment, *smalls, *shares)
    hidden_all, small_all = hidden_all.reshape(SEQ, D), small_all.reshape(D, SMALL)
    return hidden_all, segment_all, small_all, share_a, share_b


SPLIT = 384


class RingScatter:
    def __init__(self, at, part, scratch, send, recv, base=0):
        self.at, self.part, self.send, self.recv, self.base = at, part, send, recv, base
        near, half_a, half_b, self.full_up, self.full_down = scratch[:5]
        to_far, to_up, to_down = scratch[5:] or [
            part.at[at.chip(k) * 2 + at.core] for k in (2, 1, 3)
        ]
        self.near, self.half_a, self.half_b = near, half_a, half_b
        self.to_far, self.to_up, self.to_down = to_far, to_up, to_down
        self.half = half_a.shape[0]
        self.lo, self.hi = pl.ds(0, self.half), pl.ds(self.half, self.half)
        up, down = at.ring(1), at.ring(3)
        self.plan = {
            k: (part.at[at.chip(k) * 2 + 1 - at.core], near.at[k], at.sibling()) for k in range(4)
        }
        self.plan[4] = (to_far.at[self.lo], half_a, up)
        self.plan[5] = (to_far.at[self.hi], half_b, down)
        self.plan[6] = (to_up, self.full_up, up)
        self.plan[7] = (to_down, self.full_down, down)

    def copy(self, i):
        src, dst, device = self.plan[i]
        return remote(src, dst, self.send, self.recv, self.base + i, device)

    def chip_sum(self, k):
        self.copy(k).wait_recv()
        own = self.part[self.at.chip(k) * 2 + self.at.core]
        return own.astype(F32) + self.near[k].astype(F32)

    def far(self):
        self.to_far[...] = self.chip_sum(2).astype(BF)
        self.copy(4).start()
        self.copy(5).start()

    def up_side(self):
        total = self.chip_sum(1)
        self.copy(4).wait_recv()
        self.to_up[self.lo, :] = (total[: self.half] + self.half_a[...].astype(F32)).astype(BF)
        self.to_up[self.hi, :] = total[self.half :].astype(BF)
        self.copy(6).start()

    def down_side(self):
        total = self.chip_sum(3)
        self.copy(5).wait_recv()
        self.to_down[self.lo, :] = total[: self.half].astype(BF)
        self.to_down[self.hi, :] = (total[self.half :] + self.half_b[...].astype(F32)).astype(BF)
        self.copy(7).start()

    def finish(self, out):
        out[...] = self.chip_sum(0)
        self.copy(6).wait_recv()
        out[...] += self.full_up[...].astype(F32)
        self.copy(7).wait_recv()
        out[...] += self.full_down[...].astype(F32)
        for i in range(8):
            self.copy(i).wait_send()


def ring_scratch(rows, columns, own_sends=True):
    block, half = pltpu.VMEM((rows, columns), BF), pltpu.VMEM((rows // 2, columns), BF)
    scratch = [pltpu.VMEM((4, rows, columns), BF), half, half, block, block]
    return scratch + [block] * 3 if own_sends else scratch


class PairScatter:
    def __init__(self, at, part, scratch, send, recv, base=0):
        self.at, self.part, self.send, self.recv, self.base = at, part, send, recv, base
        self.near, self.far_rows, self.to_far = scratch
        size = self.to_far.shape[0] // PIECES
        self.parts = [pl.ds(i * size, size) for i in range(PIECES)]
        self.other, self.own = (1 - at.yl) * 2, at.yl * 2

    def go(self, i, src, dst, device):
        return push(src, dst, self.send, self.recv, self.base + i, device)

    def begin_far(self):
        slot = self.other + 1 - self.at.core
        self.first = [
            self.go(i, self.part.at[slot, rows], self.near.at[1, rows], self.at.sibling())
            for i, rows in enumerate(self.parts)
        ]

    def begin_own(self):
        slot = self.own + 1 - self.at.core
        self.second = self.go(PIECES, self.part.at[slot], self.near.at[0], self.at.sibling())

    def forward(self):
        self.sent = []
        for i, rows in enumerate(self.parts):
            self.first[i].wait_recv()
            own = self.part[self.other + self.at.core, rows, :].astype(F32)
            self.to_far[rows, :] = (own + self.near[1, rows, :].astype(F32)).astype(BF)
            far = self.far_rows.at[rows]
            self.sent.append(self.go(PIECES + 1 + i, self.to_far.at[rows], far, self.at.partner()))

    def finish(self, out):
        self.second.wait_recv()
        out[...] = self.part[self.own + self.at.core].astype(F32) + self.near[0].astype(F32)
        for i, rows in enumerate(self.parts):
            self.sent[i].wait_recv()
            out[rows, :] += self.far_rows[rows, :].astype(F32)
        for copy in (*self.first, self.second, *self.sent):
            copy.wait_send()


def pair_scratch(rows, columns):
    block = pltpu.VMEM((rows, columns), BF)
    return [pltpu.VMEM((2, rows, columns), BF), block, block]


SPLIT = 384


def rotary_tables():
    half = HD // 2
    inverse = (10000.0 ** (-(np.arange(half, dtype=np.float64) * 2.0) / HD)).astype(np.float32)
    angles = np.arange(SEQ, dtype=np.float32)[:, None] * inverse[None, :]
    cosine, sine = np.cos(angles), np.sin(angles)
    wide_cosine = np.concatenate([cosine] * 4, axis=1)
    wide_sine = np.concatenate([-sine, sine] * 2, axis=1)
    return wide_cosine.astype(np.float32), wide_sine.astype(np.float32)


def swapped(values):
    lane = lax.broadcasted_iota(jnp.int32, values.shape, 1)
    low = (lane % HD) < HD // 2
    return jnp.where(low, pltpu.roll(values, 96, 1), pltpu.roll(values, 32, 1))


def rotated(values, cosine, sine):
    return values * cosine + swapped(values) * sine


def bias_block(key_segment, query_segment, first, rows):
    key_at = lax.broadcasted_iota(jnp.int32, (rows, BLOCK), 0)
    query_at = lax.broadcasted_iota(jnp.int32, (rows, BLOCK), 1) + first
    allowed = (key_segment == query_segment) & (key_at <= query_at)
    return jnp.where(allowed, 0.0, MASKED)


def segment_row(segments):
    return jnp.concatenate(
        [segments[rank, i : i + 1, :] for rank in range(4) for i in range(2)], axis=1
    ).astype(F32)


def gain_rows(small):
    return small[:, 768:896].astype(F32).T[32:40, :]


def column_of(row):
    return jnp.broadcast_to(row, (8, row.shape[1])).T[:, 0:1]


def front_kernel(
    hidden, weights, cosine, sine, segments, own_hidden, ids, out_grad, share_a, share_b,
    normed, query, key, value, context_t, log_total, middle, normed_moe, gating,
    over_z, over_x, quad_a, quad_b, out_grad_all, bias, part, context, through, *refs,
):
    pair_refs = refs[:3]
    send, recv, here = refs[3:]
    at = Place()
    greet(
        [
            at.sibling(), at.partner(), at.ring(1), at.ring(3),
            at.along("x", 1), at.along("x", 3), at.along("z", 1), at.along("z", 3),
        ]
    )
    ring = RingGather(at, out_grad, out_grad_all, send, recv, here.at[0], 0)
    lines = first_gather(
        at, share_a, share_b, over_z, over_x, send, recv, here.at[pl.ds(1, 4)], 9
    )
    quad = second_gather(
        at, 0, over_z, over_x, quad_a, quad_b, send, recv, here.at[pl.ds(5, 4)],
        9 + SpreadOut.COPIES, through,
    )
    scatter = PairScatter(at, part, pair_refs, send, recv, 9 + 2 * SpreadOut.COPIES)
    lines.begin()
    ring.begin()

    gains = gain_rows(weights)
    seg_row = segment_row(segments)
    seg_column = column_of(seg_row)
    for block in range(SEQ // BLOCK):
        rows = slice(block * BLOCK, (block + 1) * BLOCK)
        values = hidden[rows, :].astype(F32)
        scale = lax.rsqrt(jnp.mean(values * values, axis=-1, keepdims=True) + EPS)
        normed[rows, :] = (values * scale * gains[0:1, :]).astype(BF)
    for half in range(2):
        columns = slice(half * 128, half * 128 + 128)
        pre = mm(normed[...], weights[:, columns])
        query[:, columns] = (rotated(pre, cosine[...], sine[...]) * 0.125).astype(BF)
    key_pre = mm(normed[...], weights[:, 256:384])
    key[...] = rotated(key_pre, cosine[...], sine[...]).astype(BF)
    value_pre = mm(normed[...], weights[:, 384:512])
    value[...] = value_pre.astype(BF)
    value_t = value_pre.T.astype(BF)
    lines.forward()
    for block in range(SEQ // BLOCK):
        first, end = block * BLOCK, (block + 1) * BLOCK
        bias[:end, :] = bias_block(seg_column[:end, :], seg_row[:, first:end], first, end)
        for head in range(HEADS):
            kv = slice((head // 2) * HD, (head // 2) * HD + HD)
            own = slice(head * HD, head * HD + HD)
            scores = mm_last(key[:end, kv], query[first:end, own]) + bias[:end, :]
            top = jnp.max(scores, axis=0, keepdims=True)
            powers = jnp.exp(scores - top)
            total = jnp.sum(powers, axis=0, keepdims=True)
            share = (powers * (1.0 / total)).astype(BF)
            context_t[own, first:end] = mm(value_t[kv, :end], share).astype(BF)
            log_total[head : head + 1, first:end] = top + jnp.log(total)
        if block == 1:
            lines.finish()
            quad.begin()
        if block == 2:
            ring.forward_before()
            ring.forward_behind()
    context[...] = context_t[...].T

    def project(slot):
        rows = pl.ds(pl.multiple_of(slot * LOCAL, LOCAL), LOCAL)
        part[slot] = mm_last(context[rows, :], weights[:, 512:768]).astype(BF)

    project(scatter.other + 1 - at.core)
    scatter.begin_far()
    project(scatter.other + at.core)
    project(scatter.own + 1 - at.core)
    scatter.begin_own()
    project(scatter.own + at.core)
    scatter.forward()
    quad.forward()
    ring.forward_across()
    scatter.finish(middle)
    values = middle[...] + own_hidden[...].astype(F32)
    middle[...] = values
    scale = lax.rsqrt(jnp.mean(values * values, axis=-1, keepdims=True) + EPS)
    normed_moe[...] = (values * scale * gains[1:2, :]).astype(BF)
    lane = lax.broadcasted_iota(jnp.int32, (LOCAL, 128), 1)
    chosen = lane == ids[:, 0:1]
    for i in range(1, TOPK):
        chosen = chosen | (lane == ids[:, i : i + 1])
    logits = jnp.where(chosen, mm(normed_moe[...], weights[:, 768:896]), MASKED)
    powers = jnp.where(chosen, jnp.exp(logits - jnp.max(logits, axis=-1, keepdims=True)), 0.0)
    gating[...] = powers / jnp.sum(powers, axis=-1, keepdims=True)
    for i in (0, 4, 6, 7, 8):
        ring.copy(i).wait_recv()
    ring.sent()
    ring.kept().wait()
    quad.finish()


def front(hidden, weights, tables, segments, own_hidden, ids, out_grad, shares, ident):
    vmem = pl.BlockSpec(memory_space=pltpu.VMEM)
    hbm = pl.BlockSpec(memory_space=pl.ANY)
    sems = 9 + 2 * SpreadOut.COPIES + 1 + 2 * PIECES
    return pl.pallas_call(
        front_kernel,
        in_specs=[vmem] * 10,
        out_specs=[vmem] * 9 + [hbm] * 5,
        out_shape=[
            jax.ShapeDtypeStruct((SEQ, D), BF),
            jax.ShapeDtypeStruct((SEQ, HEADS * HD), BF),
            jax.ShapeDtypeStruct((SEQ, 128), BF),
            jax.ShapeDtypeStruct((SEQ, 128), BF),
            jax.ShapeDtypeStruct((HEADS * HD, SEQ), BF),
            jax.ShapeDtypeStruct((8, SEQ), F32),
            jax.ShapeDtypeStruct((LOCAL, D), F32),
            jax.ShapeDtypeStruct((LOCAL, D), BF),
            jax.ShapeDtypeStruct((LOCAL, 128), F32),
            *[LINE_SHAPE] * 2,
            *[QUAD_SHAPE] * 2,
            jax.ShapeDtypeStruct((8, LOCAL, D), BF),
        ],
        scratch_shapes=[
            pltpu.VMEM((SEQ, BLOCK), F32),
            pltpu.VMEM((4, LOCAL, D), BF),
            pltpu.VMEM((SEQ, HEADS * HD), BF),
            pltpu.VMEM((2, *BLOCK_SHAPE), BF),
            *pair_scratch(LOCAL, D),
            pltpu.SemaphoreType.DMA((sems,)),
            pltpu.SemaphoreType.DMA((sems,)),
            pltpu.SemaphoreType.DMA((9,)),
        ],
        compiler_params=pltpu.CompilerParams(
            collective_id=ident, has_side_effects=True, vmem_limit_bytes=56 * MIB
        ),
        name="front",
    )(hidden, weights, *tables, segments, own_hidden, ids, out_grad, *shares)


def by_owner(value):
    return value.astype(BF).reshape(4, 4, 2, 32, value.shape[1])


def back_kernel(
    dx, dgate, gating, middle, normed_moe, out_grad, y_part,
    normed, weights, cosine, sine, segments, query, key, value, context_t, log_total,
    own_weights, expert_a, expert_b,
    land_0, land_1, land_2, land_3, land_4, land_5, land_6, land_7,
    dmiddle, block_out, dn1, attention, rest, gate, up, down,
    bias, dcontext, dquery_t, dkey, dvalue, dall, dall_t, dattn_own, dattn_all, y_sum,
    grads, sum_1a, sum_1b, sum_2a, sum_2b, over_y, from_opposite, share_sum, shares,
    total_a, total_b, land_a, land_b, *refs,
):
    ring_refs, pair_refs = refs[:8], refs[8:11]
    first_refs = (refs[11:18], refs[18:25])
    groups = [refs[25 + 7 * i : 32 + 7 * i] for i in range(4)]
    landings = (refs[53:57], refs[57:61])
    send, recv, here, load = refs[61:]
    at = Place()
    greet(
        [
            at.sibling(), at.partner(), at.diagonal(), at.opposite(), at.ring(1), at.ring(3),
            at.along("x", 1), at.along("x", 3), at.along("z", 1), at.along("z", 3),
        ]
    )
    base = 9 + 2 * PIECES
    sums = [
        RingSum(
            at, "x", lambda k: expert_a.at[k], first_refs[0], send, recv, load, base, 0,
            (land_0, land_1, land_2, land_3),
        ),
        RingSum(
            at, "z", lambda k: expert_b.at[k], first_refs[1], send, recv, load,
            base + RingSum.COPIES, 7, (land_4, land_5, land_6, land_7),
        ),
    ]
    for each in sums:
        each.begin()
    gain = gain_rows(weights)[1:2, :]
    chosen = gating[...]
    dchosen = chosen * (dgate[...] - jnp.sum(chosen * dgate[...], axis=-1, keepdims=True))
    dlogits = dchosen.astype(BF)
    dnormed = dx[...] + mm_last(dlogits, weights[:, 768:896])
    values = middle[...]
    scale = lax.rsqrt(jnp.mean(values * values, axis=-1, keepdims=True) + EPS)
    unit = values * scale
    weighted = dnormed * gain
    inner = jnp.mean(weighted * unit, axis=-1, keepdims=True)
    total = out_grad[...].astype(F32) + scale * (weighted - unit * inner)
    dmiddle[...] = total
    dattn_own[...] = total.astype(BF)
    gather = PairGather(at, dattn_own, dattn_all, send, recv, here, 8, PIECES)
    scatter = RingScatter(at, y_part, ring_refs, send, recv)
    for k in (2, 1, 3, 0):
        scatter.copy(k).start()
    router_part = mm(normed_moe[...].T, dlogits)
    gain_part = column_of(jnp.sum(dnormed * unit, axis=0, keepdims=True))
    lane = lax.broadcasted_iota(jnp.int32, (D, 128), 1)
    grads[..., 768:] = by_owner(jnp.where(lane == 32, gain_part, router_part))
    seg_row = segment_row(segments)
    seg_column = column_of(seg_row)
    gather.forward()
    scatter.far()
    for each in sums:
        each.middle()
    gather.finish()
    dattn = dattn_all[...].reshape(SEQ, D)
    dcontext[...] = mm(dattn, weights[:, 512:768]).astype(BF)
    output_grad_t = mm(context_t[...], dattn)
    grads[..., 512:768] = by_owner(output_grad_t.T)
    key_t = key[...].astype(F32).T.astype(BF)
    dkey[...] = jnp.zeros_like(dkey)
    dvalue[...] = jnp.zeros_like(dvalue)
    for block in range(SEQ // BLOCK):
        first, end = block * BLOCK, (block + 1) * BLOCK
        bias[:end, :] = bias_block(seg_column[:end, :], seg_row[:, first:end], first, end)
        for head in range(HEADS):
            kv = slice((head // 2) * HD, (head // 2) * HD + HD)
            own = slice(head * HD, head * HD + HD)
            query_block = query[first:end, own]
            dcontext_block = dcontext[first:end, own]
            scores = mm_last(key[:end, kv], query_block) + bias[:end, :]
            share = jnp.exp(scores - log_total[head : head + 1, first:end])
            dshare = mm_last(value[:end, kv], dcontext_block)
            centre = jnp.sum(share * dshare, axis=0, keepdims=True)
            dscore = (share * (dshare - centre)).astype(BF)
            dquery_t[own, first:end] = mm(key_t[kv, :end], dscore) * 0.125
            dkey[:end, kv] += mm(dscore, query_block)
            dvalue[:end, kv] += mm(share.astype(BF), dcontext_block)
        if block == 0:
            scatter.up_side()
            scatter.down_side()
        if block == 2:
            last = base + 6 * RingSum.COPIES + 1 + 2 * PIECES
            final_sums = []
            for i, (each, axis, refs_of, landing) in enumerate(
                zip(sums, ("z", "x"), first_refs, landings)
            ):
                each.finish(each.own)
                to_up, to_down, own = refs_of[4].at[0, pl.ds(0, 1)], refs_of[5].at[0, pl.ds(0, 1)], refs_of[2].at[0]
                final_sums.append(
                    RingSum(
                        at, axis, lambda k, own=each.own: own.at[k], (*landing, to_up, to_down, own),
                        send, recv, load, last + RingSum.COPIES * i, 26 + 3 * i,
                    )
                )
                final_sums[i].begin()
                final_sums[i].direct()
        if block == 3:
            for each in final_sums:
                each.middle()
    turn = -sine[...]
    for half in range(2):
        rows = slice(half * 128, half * 128 + 128)
        piece = rotated(dquery_t[rows, :].T, cosine[...], turn)
        dall[:, rows] = piece.astype(BF)
        dall_t[rows, :] = piece.T.astype(BF)
    piece = rotated(dkey[...], cosine[...], turn)
    dall[:, 256:384] = piece.astype(BF)
    dall_t[256:384, :] = piece.T.astype(BF)
    dall[:, 384:512] = dvalue[...].astype(BF)
    dall_t[384:512, :] = dvalue[...].T.astype(BF)
    grads[..., 0:512] = by_owner(mm(dall_t[...], normed[...]).T)
    after = base + 2 * RingSum.COPIES
    width = grads.shape[-1]
    a, b = pl.ds(0, SPLIT), pl.ds(SPLIT, width - SPLIT)

    def ring_sum(i, axis, part_of, scratch):
        return RingSum(
            at, axis, part_of, scratch, send, recv, load, after + RingSum.COPIES * i, 14 + 3 * i
        )

    first_a = ring_sum(0, "x", lambda k: grads.at[k, :, :, :, a], groups[0])
    first_b = ring_sum(1, "z", lambda k: grads.at[:, k, :, :, b], groups[1])
    second_a = ring_sum(2, "z", lambda k: sum_1a.at[k], groups[2])
    second_b = ring_sum(3, "x", lambda k: sum_1b.at[k], groups[3])
    for each in (first_a, first_b):
        each.begin()
        each.direct()
    after = after + 4 * RingSum.COPIES
    pair = PairScatter(at, dattn_all, pair_refs, send, recv, after)
    after = after + 1 + 2 * PIECES + 2 * RingSum.COPIES

    def project(slot):
        rows = pl.ds(pl.multiple_of(slot * LOCAL, LOCAL), LOCAL)
        dattn_all[slot] = mm_last(dall[rows, :], weights[:, 0:512]).astype(BF)

    project(pair.other + 1 - at.core)
    pair.begin_far()
    project(pair.other + at.core)
    project(pair.own + 1 - at.core)
    pair.begin_own()
    project(pair.own + at.core)
    pair.forward()
    first_a.middle()
    first_b.middle()
    lands = []
    for i, (each, out, land) in enumerate(
        zip(final_sums, (total_a, total_b), (land_a, land_b))
    ):
        each.finish(out)
        lands.append(push(out.at[1 - at.yh], land, send, recv, after + 1 + i, at.opposite()))
    scatter.finish(y_sum)
    block_out[...] = (y_sum[...] + middle[...]).astype(BF)

    first_a.finish(sum_1a)
    second_a.begin()
    second_a.direct()
    first_b.finish(sum_1b)
    second_b.begin()
    second_b.direct()
    second_a.middle()
    second_b.middle()
    second_a.finish(sum_2a)
    second_b.finish(sum_2b)
    over_y[:, a] = sum_2a[...].reshape(64, SPLIT)
    over_y[:, b] = sum_2b[...].reshape(64, width - SPLIT)
    theirs = pl.ds(pl.multiple_of((1 - at.yh) * 32, 32), 32)
    own = pl.ds(pl.multiple_of(at.yh * 32, 32), 32)
    swap = push(over_y.at[theirs], from_opposite, send, recv, after, at.opposite())
    pair.finish(dn1)
    swap.wait_recv()
    total = over_y[own, :].astype(F32) + from_opposite[...].astype(F32)
    attention[...] = total[:, :768]
    gain_part = jnp.sum(total[:, :512] * own_weights[...].astype(F32), axis=1, keepdims=True)
    lane = lax.broadcasted_iota(jnp.int32, (32, 128), 1)
    share_sum[...] = jnp.where(lane == 33, gain_part, total[:, 768:])
    copies = [
        push(share_sum, shares.at[i], send, recv, after + 3 + i, device)
        for i, device in enumerate((at.sibling(), at.partner(), at.diagonal()))
    ]
    mine, theirs = pl.ds(at.yh * STEPS, STEPS), pl.ds((1 - at.yh) * STEPS, STEPS)
    for j, value in enumerate((total_a, total_b)):
        for i, out in enumerate((gate, up, down)):
            out[mine, 2 * j : 2 * j + 2] = value[at.yh, :, i].astype(F32)
    rest[...] = share_sum[...]
    for i, copy in enumerate(copies):
        copy.wait_recv()
        rest[...] += shares[i]
    for j, (copy, land) in enumerate(zip(lands, (land_a, land_b))):
        copy.wait_recv()
        for i, out in enumerate((gate, up, down)):
            out[theirs, 2 * j : 2 * j + 2] = land[:, i].astype(F32)
    for copy in (swap, *copies, *lands):
        copy.wait_send()


def back(
    dx, dgate, gating, middle, normed_moe, out_grad, y_part,
    normed, weights, tables, segments, kept, own_weights, expert_grads, ident,
):
    vmem = pl.BlockSpec(memory_space=pltpu.VMEM)
    hbm = pl.BlockSpec(memory_space=pl.ANY)
    sems = 2 * (9 + 2 * PIECES) + 8 * RingSum.COPIES + 6
    block = SUMS_SHAPE.shape[1:]
    half = (block[0] // 2, *block[1:])
    first_a, first_b = (4, 2, 32, SPLIT), (4, 2, 32, SMALL - SPLIT)
    landing = [pltpu.VMEM(half, BF)] * 2 + [pltpu.VMEM(block, BF)] * 2
    return pl.pallas_call(
        back_kernel,
        in_specs=[vmem] * 18 + [hbm] * 10,
        out_specs=[vmem] * 8,
        out_shape=[
            jax.ShapeDtypeStruct((LOCAL, D), F32),
            jax.ShapeDtypeStruct((LOCAL, D), BF),
            jax.ShapeDtypeStruct((LOCAL, D), F32),
            jax.ShapeDtypeStruct((32, 768), F32),
            jax.ShapeDtypeStruct((32, 128), F32),
            *[jax.ShapeDtypeStruct((2 * STEPS, QUAD, 32, FF), F32)] * 3,
        ],
        scratch_shapes=[
            pltpu.VMEM((SEQ, BLOCK), F32),
            pltpu.VMEM((SEQ, HEADS * HD), BF),
            pltpu.VMEM((HEADS * HD, SEQ), F32),
            pltpu.VMEM((SEQ, 128), F32),
            pltpu.VMEM((SEQ, 128), F32),
            pltpu.VMEM((SEQ, 512), BF),
            pltpu.VMEM((512, SEQ), BF),
            pltpu.VMEM((LOCAL, D), BF),
            pltpu.VMEM((4, LOCAL, D), BF),
            pltpu.VMEM((LOCAL, D), F32),
            pltpu.VMEM((4, 4, 2, 32, SMALL), BF),
            pltpu.VMEM(first_a, BF),
            pltpu.VMEM(first_b, BF),
            pltpu.VMEM(first_a[1:], BF),
            pltpu.VMEM(first_b[1:], BF),
            pltpu.VMEM((64, SMALL), BF),
            pltpu.VMEM((32, SMALL), BF),
            pltpu.VMEM((32, 128), F32),
            pltpu.VMEM((3, 32, 128), F32),
            *[pltpu.VMEM(block, BF)] * 2,
            *[pltpu.VMEM(block[1:], BF)] * 2,
            *ring_scratch(LOCAL, D),
            *pair_scratch(LOCAL, D),
            *sum_scratch(SUMS_SHAPE.shape),
            *sum_scratch(SUMS_SHAPE.shape),
            *sum_scratch(first_a),
            *sum_scratch(first_b),
            *sum_scratch(first_a[1:]),
            *sum_scratch(first_b[1:]),
            *landing,
            *landing,
            pltpu.SemaphoreType.DMA((sems,)),
            pltpu.SemaphoreType.DMA((sems,)),
            pltpu.SemaphoreType.DMA,
            pltpu.SemaphoreType.DMA((32,)),
        ],
        compiler_params=pltpu.CompilerParams(
            collective_id=ident, has_side_effects=True, vmem_limit_bytes=63 * MIB
        ),
        name="back",
    )(
        dx, dgate, gating, middle, normed_moe, out_grad, y_part,
        normed, weights, *tables, segments, *kept, own_weights, *expert_grads,
    )


def experts_kernel(
    x_in, gate_in, d_in, over_z, over_x, quad_0a, quad_0b, y_out, dx_out, dgate_out,
    all_a, all_b, land_0, land_1, land_2, land_3, land_4, land_5, land_6, land_7,
    quad_1a, quad_1b, quad_2a, quad_2b, quad_3a, quad_3b,
    x, d, xt, dt, y, dx, gating, dgate, dgate_part, hidden, w, *refs,
):
    dx_scratch, dgate_scratch = refs[:5], refs[5:10]
    send, recv, here, load, store, fetch = refs[10:16]
    at = Place()
    step = pl.program_id(0)
    opening, closing = step == 0, step == STEPS - 1
    rows_at_once = 2 * LOCAL
    lane = lax.broadcasted_iota(jnp.int32, (LOCAL, 128), 1)
    own_first = at.yh * 16 + step * QUAD
    x_gather = RingGather(at, x_in, x, send, recv, here.at[0], 0)
    gate_gather = RingGather(at, gate_in, gating, send, recv, here.at[1], 9)
    gathers = (x_gather, gate_gather)
    scatters = (
        RingScatter(at, d, dx_scratch, send, recv, 18),
        RingScatter(at, dgate_part, dgate_scratch, send, recv, 26),
    )

    later = ((quad_1a, quad_1b), (quad_2a, quad_2b), (quad_3a, quad_3b))
    quads = [
        second_gather(
            at, 1 + i, over_z, over_x, *quad, *refs[16:18], refs[18].at[pl.ds(4 * i, 4)],
            SpreadOut.COPIES * i, refs[19],
        )
        for i, quad in enumerate(later)
    ]

    def ride(condition, what):
        for i, quad in enumerate(quads):

            @pl.when(condition & (step == i))
            def _():
                what(quad)

    grads_a, grads_b, ship_send, ship_recv, keep_sems = refs[20:]

    def shipments(number):
        lo, hi = pl.ds(0, 2), pl.ds(2, 2)
        plan = []
        for part, place, axis, lands in (
            (grads_a, at.x, "x", (land_0, land_1, land_2, land_3)),
            (grads_b, at.z, "z", (land_4, land_5, land_6, land_7)),
        ):
            above, across, below = (part.at[lax.rem(place + k, 4)] for k in (1, 2, 3))
            upper, lower = at.along(axis, 1), at.along(axis, 3)
            plan += [
                (across.at[lo], lands[0], upper), (across.at[hi], lands[1], lower),
                (above.at[hi], lands[2], upper), (below.at[lo], lands[3], lower),
            ]
        return [
            remote(src, land.at[:, :, number], ship_send, ship_recv, 8 * number + i, device)
            for i, (src, land, device) in enumerate(plan)
        ]

    def keeps(number):
        return [
            pltpu.make_async_copy(part, out.at[:, :, :, number], keep_sems.at[i])
            for i, (part, out) in enumerate(((grads_a, all_a), (grads_b, all_b)))
        ]

    def shipped(number):
        for copy in shipments(number):
            copy.wait_send()
        for copy in keeps(number):
            copy.wait()

    def fetches(quad_a, quad_b):
        copies = []
        for g in range(3):
            for i in range(QUAD):
                columns = pl.ds((g * QUAD + i) * FF, FF)
                if i < 2:
                    parts = [(quad_a.at[:, :, :, g, i], w.at[:, :, :, :, columns])]
                else:
                    parts = [
                        (quad_b.at[:, x_at, :, g, i - 2], w.at[x_at, :, :, :, columns])
                        for x_at in range(4)
                    ]
                for part in parts:
                    copies.append(pltpu.make_async_copy(*part, fetch.at[len(copies)]))
        return copies

    def d_load(chip):
        two = pl.ds(chip * 2, 2)
        return pltpu.make_async_copy(d_in.at[two], d.at[two], load.at[chip])

    def y_store(chip):
        two = pl.ds(chip * 2, 2)
        return pltpu.make_async_copy(x.at[two], y_out.at[two], store.at[chip])

    @pl.when(opening)
    def _():
        greet(
            [
                at.sibling(), at.ring(1), at.ring(3),
                at.along("x", 1), at.along("x", 3), at.along("z", 1), at.along("z", 3),
            ]
        )
        for gather in gathers:
            gather.begin()
        for copy in fetches(quad_0a, quad_0b):
            copy.start()
        for chip in range(4):
            d_load(chip).start()

    for copy in fetches(quad_0a, quad_0b):
        copy.wait()

    ride(step < STEPS, lambda quad: quad.begin())

    def arrive(turn):
        @pl.when(turn == 0)
        def _():
            for gather in gathers:
                gather.kept().wait()
                gather.copy(0).wait_recv()

        @pl.when(turn == 1)
        def _():
            for gather in gathers:
                gather.forward_before()
                gather.forward_behind()
            for gather in gathers:
                gather.copy(4).wait_recv()

        @pl.when(turn == 2)
        def _():
            for gather in gathers:
                gather.forward_across()
            for gather in gathers:
                gather.copy(6).wait_recv()

        @pl.when(turn == 3)
        def _():
            for gather in gathers:
                gather.copy(7).wait_recv()
                gather.copy(8).wait_recv()

    def leave(turn):
        @pl.when(turn == 0)
        def _():
            for scatter in scatters:
                scatter.copy(2).start()

        @pl.when(turn == 1)
        def _():
            for scatter in scatters:
                scatter.copy(1).start()
                scatter.far()

        @pl.when(turn == 2)
        def _():
            for scatter in scatters:
                scatter.copy(3).start()
                scatter.up_side()

        @pl.when(turn == 3)
        def _():
            for scatter in scatters:
                scatter.copy(0).start()
                scatter.down_side()

    def tokens_block(turn, carry):
        inward = jnp.where(turn == 0, 0, jnp.where(turn == 1, 3, turn - 1))
        outward = jnp.where(turn == 0, 2, jnp.where(turn == 3, 0, turn * 2 - 1))
        chip = at.chip(jnp.where(closing, outward, inward))
        two = pl.ds(chip * 2, 2)
        rows = pl.ds(pl.multiple_of(chip * rows_at_once, rows_at_once), rows_at_once)

        @pl.when(opening)
        def _():
            arrive(turn)
            d_load(chip).wait()
            xt[:, rows] = x[two].reshape(rows_at_once, D).T
            dt[:, rows] = d[two].reshape(rows_at_once, D).T
            y[rows, :] = jnp.zeros((rows_at_once, D), F32)
            dx[rows, :] = jnp.zeros((rows_at_once, D), F32)
            dgate[rows, :] = jnp.zeros((rows_at_once, 128), F32)

        ride(turn == 3, lambda quad: quad.forward())
        gate_up = w[:, :, :, :, 0 : 2 * F].reshape(D, 2 * F)
        down = w[:, :, :, :, 2 * F :].reshape(D, F)
        for core in range(2):
            slot = chip * 2 + core
            part = pl.ds(pl.multiple_of(slot * LOCAL, LOCAL), LOCAL)
            both = mm(x[slot], gate_up)
            gate, up = both[:, :F], both[:, F:]
            dact = mm(d[slot], down)
            turned = pltpu.roll(gating[slot], lax.rem(128 - own_first, 128), 1)
            factor = jnp.concatenate(
                [jnp.broadcast_to(turned[:, i : i + 1], (LOCAL, FF)) for i in range(QUAD)],
                axis=1,
            )
            q = 1.0 / (1.0 + jnp.exp(-gate))
            silu = gate * q
            act = silu * up
            product = act * dact
            sums = dgate[part, :]
            for i in range(QUAD):
                own = jnp.sum(product[:, i * FF : (i + 1) * FF], axis=1, keepdims=True)
                sums = jnp.where(lane == own_first + i, own, sums)
            dgate[part, :] = sums
            dact = dact * factor
            hidden[part, 0:F] = (dact * up * (q + silu * (1.0 - q))).astype(BF)
            hidden[part, F : 2 * F] = (dact * silu).astype(BF)
            hidden[part, 2 * F :] = (act * factor).astype(BF)
        y[rows, :] += mm_last(hidden[rows, 2 * F :], down)
        dx[rows, :] += mm_last(hidden[rows, 0 : 2 * F], gate_up)

        @pl.when(closing)
        def _():
            x[two] = y[rows, :].astype(BF).reshape(2, LOCAL, D)
            d[two] = dx[rows, :].astype(BF).reshape(2, LOCAL, D)
            dgate_part[two] = dgate[rows, :].astype(BF).reshape(2, LOCAL, 128)
            y_store(chip).start()
            leave(turn)

        return carry

    lax.fori_loop(0, 4, tokens_block, 0)

    @pl.when(opening)
    def _():
        for gather in gathers:
            gather.sent()

    @pl.when(step > 0)
    def _():
        shipped(step - 1)

    def grads_block(block, carry):
        rows = pl.ds(pl.multiple_of(block * 512, 512), 512)

        def put(g, value):
            value = value.astype(BF).reshape(2, 4, 2, 32, value.shape[1])
            for j in range(value.shape[-1] // FF):
                piece = value[..., j * FF : (j + 1) * FF]
                group, i = g + j // QUAD, j % QUAD
                for x_at in range(2):
                    if i < 2:
                        grads_a[block * 2 + x_at, :, :, group, i] = piece[x_at]
                    else:
                        grads_b[:, block * 2 + x_at, :, group, i - 2] = piece[x_at]

        ride(block == 1, lambda quad: quad.finish())
        for number, quad in enumerate(later):

            @pl.when((block == 1) & (step == number))
            def _():
                for copy in fetches(*quad):
                    copy.start()

        put(0, mm(xt[rows, :], hidden[:, 0 : 2 * F]))
        put(2, mm(dt[rows, :], hidden[:, 2 * F :]))
        return carry

    lax.fori_loop(0, D // 512, grads_block, 0)
    for copy in (*shipments(step), *keeps(step)):
        copy.start()

    @pl.when(closing)
    def _():
        scatters[0].finish(dx_out)
        scatters[1].finish(dgate_out)
        for chip in range(4):
            y_store(chip).wait()
        shipped(step)
        for number in range(STEPS):
            for copy in shipments(number):
                copy.wait_recv()


def experts(x, gating, d, lines, quad, ident):
    hbm = pl.BlockSpec(memory_space=pl.ANY)

    def whole(rows, columns):
        return pl.BlockSpec((rows, columns), lambda step: (0, 0), pipeline_mode=pl.Buffered(1))

    return pl.pallas_call(
        experts_kernel,
        grid=(STEPS,),
        in_specs=[hbm] * 7,
        out_specs=[
            hbm,
            whole(LOCAL, D),
            whole(LOCAL, 128),
            *[hbm] * 10,
            *[hbm] * 6,
        ],
        out_shape=[
            jax.ShapeDtypeStruct((8, LOCAL, D), BF),
            jax.ShapeDtypeStruct((LOCAL, D), F32),
            jax.ShapeDtypeStruct((LOCAL, 128), F32),
            *[GRADS_SHAPE] * 2,
            *[LAND_SHAPE] * 8,
            *[QUAD_SHAPE] * 6,
        ],
        scratch_shapes=[
            pltpu.VMEM((8, LOCAL, D), BF),
            pltpu.VMEM((8, LOCAL, D), BF),
            pltpu.VMEM((D, TOKENS), BF),
            pltpu.VMEM((D, TOKENS), BF),
            pltpu.VMEM((TOKENS, D), F32),
            pltpu.VMEM((TOKENS, D), F32),
            pltpu.VMEM((8, LOCAL, 128), F32),
            pltpu.VMEM((TOKENS, 128), F32),
            pltpu.VMEM((8, LOCAL, 128), BF),
            pltpu.VMEM((TOKENS, 3 * F), BF),
            pltpu.VMEM((4, 4, 2, 32, 3 * F), BF),
            *ring_scratch(LOCAL, D, False),
            *ring_scratch(LOCAL, 128, False),
            pltpu.SemaphoreType.DMA((34,)),
            pltpu.SemaphoreType.DMA((34,)),
            pltpu.SemaphoreType.DMA((2,)),
            pltpu.SemaphoreType.DMA((4,)),
            pltpu.SemaphoreType.DMA((4,)),
            pltpu.SemaphoreType.DMA((30,)),
            pltpu.SemaphoreType.DMA((3 * SpreadOut.COPIES,)),
            pltpu.SemaphoreType.DMA((3 * SpreadOut.COPIES,)),
            pltpu.SemaphoreType.DMA((12,)),
            pltpu.VMEM((2, *BLOCK_SHAPE), BF),
            *[pltpu.VMEM((4, 4, 2, 3, 2, 32, FF), BF)] * 2,
            pltpu.SemaphoreType.DMA((8 * STEPS,)),
            pltpu.SemaphoreType.DMA((8 * STEPS,)),
            pltpu.SemaphoreType.DMA((2,)),
        ],
        compiler_params=pltpu.CompilerParams(
            collective_id=ident, has_side_effects=True, vmem_limit_bytes=63 * MIB
        ),
        name="experts",
    )(x, gating, d, *lines, *quad)[:13]


def norm_scale(values):
    return lax.rsqrt(jnp.mean(values * values, axis=-1, keepdims=True) + EPS)


def norm_grad(values, gain, dnormed):
    scale = norm_scale(values)
    unit = values * scale
    weighted = dnormed * gain
    dvalues = scale * (weighted - unit * jnp.mean(weighted * unit, axis=-1, keepdims=True))
    return dvalues


def on_device(
    hidden_in, out_grad, attn_gain, query_weight, key_weight, value_weight, output_weight,
    moe_gain, router_weight, expert_gate, expert_up, expert_down, expert_ids, segment_ids,
):
    gains = jnp.stack([attn_gain, moe_gain])
    smalls = (query_weight, key_weight, value_weight, output_weight, router_weight, gains)
    own_shares = (expert_gate, expert_up, expert_down)
    hidden_all, segments, small, *shares = startup(
        hidden_in, segment_ids.reshape(2, 128), smalls, own_shares, 0
    )
    tables = tuple(jnp.asarray(t) for t in rotary_tables())
    normed, *more, d = front(
        hidden_all, small, tables, segments, hidden_in, expert_ids, out_grad, shares, 1
    )
    kept, (middle, normed_moe, gating), lines, quad = more[:5], more[5:8], more[8:10], more[10:]
    y, dx, dgate, *expert_grads = experts(normed_moe, gating, d, lines, quad, 3)
    own_weights = jnp.concatenate([query_weight, key_weight, value_weight], axis=1)
    dmiddle, block_out, dn1, attention_grads, rest, *expert_grads = back(
        dx, dgate, gating, middle, normed_moe, out_grad, y,
        normed, small, tables, segments, kept, own_weights, expert_grads, 5,
    )
    hidden = hidden_in.astype(F32)
    dhidden = norm_grad(hidden, small[:, 800].astype(F32), dn1)
    hidden_grad = dmiddle + dhidden
    expert_grads = [share.reshape(E, 32, FF) for share in expert_grads]
    return (
        block_out,
        hidden_grad,
        rest[:, 33] / attn_gain.astype(F32),
        attention_grads[:, 0:256],
        attention_grads[:, 256:384],
        attention_grads[:, 384:512],
        attention_grads[:, 512:768],
        rest[:, 32],
        rest[:, :32],
        *expert_grads,
    )


def solution(mesh):
    fine = Mesh(np.asarray(mesh.devices).reshape(4, 4, 2, 2, 2), ALL)
    return jax.shard_map(
        on_device,
        mesh=fine,
        in_specs=(
            P(ALL, None),
            P(ALL, None),
            P(DP),
            P(DP, TENSOR),
            P(DP, TENSOR),
            P(DP, TENSOR),
            P(DP, TENSOR),
            P(DP),
            P(DP, None),
            P(None, DP, TENSOR),
            P(None, DP, TENSOR),
            P(None, DP, TENSOR),
            P(ALL, None),
            P(ALL),
        ),
        out_specs=(
            P(ALL, None),
            P(ALL, None),
            P(DP),
            P(DP, TENSOR),
            P(DP, TENSOR),
            P(DP, TENSOR),
            P(DP, TENSOR),
            P(DP),
            P(DP, None),
            P(None, DP, TENSOR),
            P(None, DP, TENSOR),
            P(None, DP, TENSOR),
        ),
        check_vma=False,
    )
```

```python
import jax
import jax.numpy as jnp
import numpy as np
from jax import lax
from jax.experimental import pallas as pl
from jax.experimental.pallas import tpu as pltpu
from jax.sharding import Mesh
from jax.sharding import PartitionSpec as P

D = 1024
HD = 64
E = 32
SEQ = 1024
LOCAL = 256
HEADS = 4
QUAD = 4
FF = 128
F = QUAD * FF
EPS = 1e-06
TOPK = 8
MASKED = -1e30
BLOCK = 256
TOKENS = 2048
STEPS = 4

DP = ("x", "z", "yh")
TENSOR = ("yl", "core")
RING = ("yh", "yl", "core")
PLANE = ("x", "z")
ALL = ("x", "z", "yh", "yl", "core")

F32 = jnp.float32
BF = jnp.bfloat16
LAST = (((1,), (1,)), ((), ()))
MIB = 1024 * 1024
MESH = pl.DeviceIdType.MESH
SMALL = 896


def mm(a, b):
    return jnp.dot(a, b, preferred_element_type=F32)


def mm_last(a, b):
    return lax.dot_general(a, b, LAST, preferred_element_type=F32)


class Place:
    def __init__(self):
        self.x = lax.axis_index("x")
        self.z = lax.axis_index("z")
        self.yh = lax.axis_index("yh")
        self.yl = lax.axis_index("yl")
        self.core = lax.axis_index("core")
        self.y = self.yh * 2 + self.yl

    def chip(self, k):
        return lax.rem(self.y + k, 4)

    def ring(self, k):
        chip = self.chip(k)
        return {"yh": chip // 2, "yl": lax.rem(chip, 2)}

    def along(self, axis, k):
        return {axis: lax.rem(getattr(self, axis) + k, 4)}

    def sibling(self):
        return {"core": 1 - self.core}

    def partner(self):
        return {"yl": 1 - self.yl}

    def diagonal(self):
        return {"yl": 1 - self.yl, "core": 1 - self.core}

    def opposite(self):
        return {"yh": 1 - self.yh}


def greet(devices):
    barrier = pltpu.get_barrier_semaphore()
    for device in devices:
        pl.semaphore_signal(barrier, inc=1, device_id=device, device_id_type=MESH)
    pl.semaphore_wait(barrier, len(devices))


def remote(src, dst, send, recv, i, device):
    return pltpu.make_async_remote_copy(
        src_ref=src, dst_ref=dst, send_sem=send.at[i], recv_sem=recv.at[i],
        device_id=device, device_id_type=MESH,
    )


def push(src, dst, send, recv, i, device):
    copy = remote(src, dst, send, recv, i, device)
    copy.start()
    return copy


def keep(src, dst, sem):
    copy = pltpu.make_async_copy(src, dst, sem)
    copy.start()
    return copy


class RingGather:
    def __init__(self, at, own, out, send, recv, here, base=0):
        self.at, self.own, self.out, self.base = at, own, out, base
        self.send, self.recv, self.here = send, recv, here
        half = own.shape[0] // 2
        lo, hi = pl.ds(0, half), pl.ds(half, half)
        me, before, behind, across = (out.at[self.slot(k)] for k in (0, 3, 1, 2))
        near, up, down = at.sibling(), at.ring(1), at.ring(3)
        self.plan = [
            (own, me, near),
            (own, me, up),
            (own, me, down),
            (before.at[lo], before.at[lo], up),
            (before, before, near),
            (behind.at[hi], behind.at[hi], down),
            (behind, behind, near),
            (across.at[lo], across.at[lo], near),
            (across.at[hi], across.at[hi], near),
        ]

    def slot(self, k):
        return self.at.chip(k) * 2 + self.at.core

    def copy(self, i):
        src, dst, device = self.plan[i]
        return remote(src, dst, self.send, self.recv, self.base + i, device)

    def kept(self):
        return pltpu.make_async_copy(self.own, self.out.at[self.slot(0)], self.here)

    def begin(self):
        self.kept().start()
        for i in (1, 2, 0):
            self.copy(i).start()

    def forward_before(self):
        self.copy(1).wait_recv()
        self.copy(3).start()
        self.copy(4).start()

    def forward_behind(self):
        self.copy(2).wait_recv()
        self.copy(5).start()
        self.copy(6).start()

    def forward_across(self):
        self.copy(3).wait_recv()
        self.copy(7).start()
        self.copy(5).wait_recv()
        self.copy(8).start()

    def sent(self):
        for i in range(9):
            self.copy(i).wait_send()


class PairGather:
    def __init__(self, at, own, out, send, recv, here, base, pieces):
        self.at, self.out, self.send, self.recv, self.base = at, out, send, recv, base
        size = own.shape[0] // pieces
        self.parts = [pl.ds(i * size, size) for i in range(pieces)]
        me = at.yl * 2 + at.core
        self.other = (1 - at.yl) * 2 + at.core
        self.kept = keep(own, out.at[me], here)
        self.far = [
            push(own.at[part], out.at[me, part], send, recv, base + 1 + i, at.partner())
            for i, part in enumerate(self.parts)
        ]
        self.near = [push(own, out.at[me], send, recv, base, at.sibling())]

    def forward(self):
        for i, part in enumerate(self.parts):
            self.far[i].wait_recv()
            view = self.out.at[self.other, part]
            index = self.base + 1 + len(self.parts) + i
            self.near.append(push(view, view, self.send, self.recv, index, self.at.sibling()))

    def finish(self):
        for copy in self.near:
            copy.wait_recv()
        for copy in (*self.far, *self.near):
            copy.wait_send()
        self.kept.wait()


PIECES = 4


class AxisGather:
    def __init__(self, at, axis, view, send, recv, base):
        self.up, self.down = at.along(axis, 1), at.along(axis, 3)
        self.view, self.send, self.recv, self.base = view, send, recv, base

    def go(self, i, view, device):
        return push(view, view, self.send, self.recv, self.base + i, device)

    def begin(self):
        self.first = [
            self.go(0, self.view(0, "all"), self.up), self.go(1, self.view(0, "all"), self.down),
        ]

    def forward(self):
        self.first[0].wait_recv()
        self.far = [self.go(2, self.view(3, "low"), self.up)]
        self.first[1].wait_recv()
        self.far.append(self.go(3, self.view(1, "high"), self.down))

    def finish(self):
        for copy in self.far:
            copy.wait_recv()
        for copy in (*self.first, *self.far):
            copy.wait_send()


def halves_of(ref, first, size):
    spans = {"all": (0, size), "low": (0, size // 2), "high": (size // 2, size // 2)}
    return lambda part: ref.at[pl.ds(first + spans[part][0], spans[part][1])]


class SpreadOut:
    COPIES = 8

    def __init__(self, at, rings, send, recv, here, base=0, through=None):
        self.send, self.recv, self.here, self.base = send, recv, here, base
        self.through = through
        self.own = [(own, slot(0)) for _, own, slot, _ in rings]
        self.plan = []
        for axis, own, slot, _ in rings:
            self.plan.append((own, slot(0), at.along(axis, 1)))
            self.plan.append((own, slot(0), at.along(axis, 3)))
        for axis, _, slot, half in rings:
            low, high = (slot(3).at[pl.ds(0, half)], slot(1).at[pl.ds(half, half)])
            self.plan.append((low, low, at.along(axis, 1)))
            self.plan.append((high, high, at.along(axis, 3)))

    def copy(self, i):
        src, dst, device = self.plan[i]
        return remote(src, dst, self.send, self.recv, self.base + i, device)

    def loaded(self, i):
        return pltpu.make_async_copy(self.own[i][0], self.through.at[i], self.here.at[i])

    def kept(self, i):
        src, dst = self.own[i]
        src = src if self.through is None else self.through.at[i]
        return pltpu.make_async_copy(src, dst, self.here.at[2 + i])

    def begin(self):
        for i in range(4):
            self.copy(i).start()
        for i in range(2):
            (self.kept(i) if self.through is None else self.loaded(i)).start()

    def forward(self):
        for i in range(4):
            self.copy(i).wait_recv()
            self.copy(4 + i).start()
        if self.through is not None:
            for i in range(2):
                self.loaded(i).wait()
                self.kept(i).start()

    def finish(self):
        for i in range(4, 8):
            self.copy(i).wait_recv()
        for i in range(8):
            self.copy(i).wait_send()
        for i in range(2):
            self.kept(i).wait()


def ring_slots(out, place):
    return lambda k: out.at[lax.rem(place + k, 4)]


def first_gather(at, own_a, own_b, over_z, over_x, *sems):
    rings = (
        ("z", own_a, ring_slots(over_z, at.z), 1), ("x", own_b, ring_slots(over_x, at.x), 1),
    )
    return SpreadOut(at, rings, *sems)


def second_gather(at, number, over_z, over_x, quad_a, quad_b, *sems):
    rings = (
        ("x", over_z.at[:, :, number], ring_slots(quad_a, at.x), 2),
        ("z", over_x.at[:, :, number], ring_slots(quad_b, at.z), 2),
    )
    return SpreadOut(at, rings, *sems)


SHARE_SHAPE = jax.ShapeDtypeStruct((2, STEPS, 3, 2, 32, FF), BF)
BLOCK_SHAPE = (4, 2, 3, 2, 32, FF)
LINE_SHAPE = jax.ShapeDtypeStruct((4, 2, STEPS, 3, 2, 32, FF), BF)
QUAD_SHAPE = jax.ShapeDtypeStruct((4, 4, 2, 3, 2, 32, FF), BF)
GRADS_SHAPE = jax.ShapeDtypeStruct((4, 4, 2, STEPS, 3, 2, 32, FF), BF)
LAND_SHAPE = jax.ShapeDtypeStruct((2, 2, STEPS - 1, 3, 2, 32, FF), BF)
SUMS_SHAPE = jax.ShapeDtypeStruct((4, 2, STEPS, 3, 2, 32, FF), BF)


class RingSum:
    COPIES = 6

    def __init__(
        self, at, axis, part_of, scratch, send, recv, load, base=0, first=0, arrived=None
    ):
        half_a, half_b, up, down, to_up, to_down, own = scratch
        self.half_a, self.half_b, self.up, self.down = half_a, half_b, up, down
        self.to_up, self.to_down, self.own = to_up, to_down, own
        self.send, self.recv, self.base = send, recv, base
        size = half_a.shape[0]
        lo, hi = pl.ds(0, size), pl.ds(size, size)
        place = {"x": at.x, "z": at.z}[axis]
        here, above, across, below = (part_of(lax.rem(place + k, 4)) for k in range(4))
        upper, lower = at.along(axis, 1), at.along(axis, 3)
        self.plan = [
            (across.at[lo], half_a, upper),
            (across.at[hi], half_b, lower),
            (above.at[hi], up.at[hi], upper),
            (below.at[lo], down.at[lo], lower),
            (to_up, up.at[lo], upper),
            (to_down, down.at[hi], lower),
        ]
        pieces = [(above.at[lo], to_up), (below.at[hi], to_down), (here, own)]
        self.arrived = arrived is not None
        if self.arrived:
            done, last = pl.ds(0, STEPS - 1), pl.ds(STEPS - 1, 1)
            for i, here_from in enumerate(arrived):
                src, dst, device = self.plan[i]
                pieces.append((here_from, dst.at[:, :, done]))
                self.plan[i] = (src.at[:, :, last], dst.at[:, :, last], device)
        self.loads = [
            pltpu.make_async_copy(src, dst, load.at[first + i])
            for i, (src, dst) in enumerate(pieces)
        ]

    def copy(self, i):
        src, dst, device = self.plan[i]
        return remote(src, dst, self.send, self.recv, self.base + i, device)

    def begin(self):
        for i in range(2):
            self.copy(i).start()
        for load in self.loads:
            load.start()

    def direct(self):
        for i in (2, 3):
            self.copy(i).start()

    def landed(self, i):
        if self.arrived and i < 4:
            self.loads[3 + i].wait()
        self.copy(i).wait_recv()

    def middle(self):
        for i, (total, landed) in enumerate(
            ((self.to_up, self.half_a), (self.to_down, self.half_b))
        ):
            self.loads[i].wait()
            self.landed(i)

            def add(i, carry, total=total, landed=landed):
                total[i] = (total[i].astype(F32) + landed[i].astype(F32)).astype(BF)
                return carry

            lax.fori_loop(0, total.shape[0], add, 0)
            self.copy(4 + i).start()

    def finish(self, out):
        self.loads[2].wait()
        for i in range(2, 6):
            self.landed(i)

        def add(i, carry):
            total = self.own[i].astype(F32) + self.up[i].astype(F32)
            out[i] = (total + self.down[i].astype(F32)).astype(out.dtype)
            return carry

        lax.fori_loop(0, out.shape[0], add, 0)
        for i in range(6):
            self.copy(i).wait_send()


def sum_scratch(block):
    half, whole = pltpu.VMEM((block[0] // 2, *block[1:]), BF), pltpu.VMEM(block, BF)
    return [half, half, whole, whole, half, half, whole]


def startup_kernel(
    hidden, segment_rows, query, key, value, output, router, gains, gate, up, down,
    hidden_all, segment_all, small_all, share_a, share_b, small, segment, send, recv, here,
):
    at = Place()
    greet(
        [
            at.sibling(), at.partner(), at.diagonal(), at.opposite(),
            at.along("x", 1), at.along("x", 3), at.along("z", 1), at.along("z", 3),
        ]
    )
    small[:, 0:256] = query[...]
    small[:, 256:384] = key[...]
    small[:, 384:512] = value[...]
    small[:, 512:768] = output[...]
    columns = jnp.broadcast_to(gains[...].astype(F32)[:, None, :], (2, 8, 32))
    columns = [columns[i].T[:, 0:1].astype(BF) for i in range(2)]
    blank = jnp.zeros((32, 94), BF)
    small[:, 768:896] = jnp.concatenate([router[...], *columns, blank], axis=1)
    segment[0:2, :] = segment_rows[...]
    segment[2:8, :] = jnp.zeros((6, 128), jnp.int32)
    rank = at.yl * 2 + at.core
    mine = small_all.at[(at.x * 4 + at.z) * 2 + at.yh]
    small_kept = keep(small, mine, here.at[0])
    copies = [push(small, mine, send, recv, 0, at.opposite())]
    swaps, swaps_kept = [], []
    base = 13 + 2 * PIECES
    for i, share in enumerate((gate, up, down)):
        for j, out in enumerate((share_a, share_b)):
            dst, two = out.at[at.yh, :, i], pl.ds(2 * j, 2)
            theirs = share.at[pl.ds((1 - at.yh) * STEPS, STEPS), two]
            index = 2 * i + j
            swaps.append(push(theirs, dst, send, recv, base + index, at.opposite()))
            own = share.at[pl.ds(at.yh * STEPS, STEPS), two]
            swaps_kept.append(keep(own, dst, here.at[3 + index]))
    copies.extend(
        push(segment, segment_all.at[rank], send, recv, 1 + i, device)
        for i, device in enumerate((at.sibling(), at.partner(), at.diagonal()))
    )
    pair = PairGather(at, hidden, hidden_all, send, recv, here.at[1], 12, PIECES)
    seg_here = keep(segment, segment_all.at[rank], here.at[2])
    over_z = AxisGather(
        at, "z",
        lambda k, part: halves_of(small_all, (at.x * 4 + lax.rem(at.z + k, 4)) * 2, 2)(part),
        send, recv, 4,
    )
    over_x = AxisGather(
        at, "x", lambda k, part: halves_of(small_all, lax.rem(at.x + k, 4) * 8, 8)(part),
        send, recv, 8,
    )
    small_kept.wait()
    copies[0].wait_recv()
    over_z.begin()
    over_z.forward()
    over_z.finish()
    over_x.begin()
    pair.forward()
    for swap, own in zip(swaps, swaps_kept):
        swap.wait_recv()
        own.wait()
    over_x.forward()
    pair.finish()
    seg_here.wait()
    for copy in copies[1:]:
        copy.wait_recv()
    over_x.finish()
    for copy in (*copies, *swaps):
        copy.wait_send()


def startup(hidden, segment, smalls, shares, ident):
    hbm = pl.BlockSpec(memory_space=pl.ANY)
    vmem = pl.BlockSpec(memory_space=pltpu.VMEM)
    sems = 13 + 2 * PIECES + 6
    shares = [share.reshape(2 * STEPS, QUAD, 32, FF) for share in shares]
    hidden_all, segment_all, small_all, share_a, share_b = pl.pallas_call(
        startup_kernel,
        in_specs=[vmem] * 8 + [hbm] * 3,
        out_specs=[hbm] * 3 + [vmem] * 2,
        out_shape=[
            jax.ShapeDtypeStruct((4, *hidden.shape), hidden.dtype),
            jax.ShapeDtypeStruct((4, 8, 128), segment.dtype),
            jax.ShapeDtypeStruct((32, 32, SMALL), BF),
            SHARE_SHAPE,
            SHARE_SHAPE,
        ],
        scratch_shapes=[
            pltpu.VMEM((32, SMALL), BF),
            pltpu.VMEM((8, 128), jnp.int32),
            pltpu.SemaphoreType.DMA((sems,)),
            pltpu.SemaphoreType.DMA((sems,)),
            pltpu.SemaphoreType.DMA((9,)),
        ],
        compiler_params=pltpu.CompilerParams(collective_id=ident, has_side_effects=True),
        name="startup",
    )(hidden, segment, *smalls, *shares)
    hidden_all, small_all = hidden_all.reshape(SEQ, D), small_all.reshape(D, SMALL)
    return hidden_all, segment_all, small_all, share_a, share_b


SPLIT = 384


class RingScatter:
    def __init__(self, at, part, scratch, send, recv, base=0):
        self.at, self.part, self.send, self.recv, self.base = at, part, send, recv, base
        near, half_a, half_b, self.full_up, self.full_down = scratch[:5]
        to_far, to_up, to_down = scratch[5:] or [
            part.at[at.chip(k) * 2 + at.core] for k in (2, 1, 3)
        ]
        self.near, self.half_a, self.half_b = near, half_a, half_b
        self.to_far, self.to_up, self.to_down = to_far, to_up, to_down
        self.half = half_a.shape[0]
        self.lo, self.hi = pl.ds(0, self.half), pl.ds(self.half, self.half)
        up, down = at.ring(1), at.ring(3)
        self.plan = {
            k: (part.at[at.chip(k) * 2 + 1 - at.core], near.at[k], at.sibling()) for k in range(4)
        }
        self.plan[4] = (to_far.at[self.lo], half_a, up)
        self.plan[5] = (to_far.at[self.hi], half_b, down)
        self.plan[6] = (to_up, self.full_up, up)
        self.plan[7] = (to_down, self.full_down, down)

    def copy(self, i):
        src, dst, device = self.plan[i]
        return remote(src, dst, self.send, self.recv, self.base + i, device)

    def chip_sum(self, k):
        self.copy(k).wait_recv()
        own = self.part[self.at.chip(k) * 2 + self.at.core]
        return own.astype(F32) + self.near[k].astype(F32)

    def far(self):
        self.to_far[...] = self.chip_sum(2).astype(BF)
        self.copy(4).start()
        self.copy(5).start()

    def up_side(self):
        total = self.chip_sum(1)
        self.copy(4).wait_recv()
        self.to_up[self.lo, :] = (total[: self.half] + self.half_a[...].astype(F32)).astype(BF)
        self.to_up[self.hi, :] = total[self.half :].astype(BF)
        self.copy(6).start()

    def down_side(self):
        total = self.chip_sum(3)
        self.copy(5).wait_recv()
        self.to_down[self.lo, :] = total[: self.half].astype(BF)
        self.to_down[self.hi, :] = (total[self.half :] + self.half_b[...].astype(F32)).astype(BF)
        self.copy(7).start()

    def finish(self, out):
        out[...] = self.chip_sum(0)
        self.copy(6).wait_recv()
        out[...] += self.full_up[...].astype(F32)
        self.copy(7).wait_recv()
        out[...] += self.full_down[...].astype(F32)
        for i in range(8):
            self.copy(i).wait_send()


def ring_scratch(rows, columns, own_sends=True):
    block, half = pltpu.VMEM((rows, columns), BF), pltpu.VMEM((rows // 2, columns), BF)
    scratch = [pltpu.VMEM((4, rows, columns), BF), half, half, block, block]
    return scratch + [block] * 3 if own_sends else scratch


class PairScatter:
    def __init__(self, at, part, scratch, send, recv, base=0):
        self.at, self.part, self.send, self.recv, self.base = at, part, send, recv, base
        self.near, self.far_rows, self.to_far = scratch
        size = self.to_far.shape[0] // PIECES
        self.parts = [pl.ds(i * size, size) for i in range(PIECES)]
        self.other, self.own = (1 - at.yl) * 2, at.yl * 2

    def go(self, i, src, dst, device):
        return push(src, dst, self.send, self.recv, self.base + i, device)

    def begin_far(self):
        slot = self.other + 1 - self.at.core
        self.first = [
            self.go(i, self.part.at[slot, rows], self.near.at[1, rows], self.at.sibling())
            for i, rows in enumerate(self.parts)
        ]

    def begin_own(self):
        slot = self.own + 1 - self.at.core
        self.second = self.go(PIECES, self.part.at[slot], self.near.at[0], self.at.sibling())

    def forward(self):
        self.sent = []
        for i, rows in enumerate(self.parts):
            self.first[i].wait_recv()
            own = self.part[self.other + self.at.core, rows, :].astype(F32)
            self.to_far[rows, :] = (own + self.near[1, rows, :].astype(F32)).astype(BF)
            far = self.far_rows.at[rows]
            self.sent.append(self.go(PIECES + 1 + i, self.to_far.at[rows], far, self.at.partner()))

    def finish(self, out):
        self.second.wait_recv()
        out[...] = self.part[self.own + self.at.core].astype(F32) + self.near[0].astype(F32)
        for i, rows in enumerate(self.parts):
            self.sent[i].wait_recv()
            out[rows, :] += self.far_rows[rows, :].astype(F32)
        for copy in (*self.first, self.second, *self.sent):
            copy.wait_send()


def pair_scratch(rows, columns):
    block = pltpu.VMEM((rows, columns), BF)
    return [pltpu.VMEM((2, rows, columns), BF), block, block]


SPLIT = 384


def rotary_tables():
    half = HD // 2
    inverse = (10000.0 ** (-(np.arange(half, dtype=np.float64) * 2.0) / HD)).astype(np.float32)
    angles = np.arange(SEQ, dtype=np.float32)[:, None] * inverse[None, :]
    cosine, sine = np.cos(angles), np.sin(angles)
    wide_cosine = np.concatenate([cosine] * 4, axis=1)
    wide_sine = np.concatenate([-sine, sine] * 2, axis=1)
    return wide_cosine.astype(np.float32), wide_sine.astype(np.float32)


def swapped(values):
    lane = lax.broadcasted_iota(jnp.int32, values.shape, 1)
    low = (lane % HD) < HD // 2
    return jnp.where(low, pltpu.roll(values, 96, 1), pltpu.roll(values, 32, 1))


def rotated(values, cosine, sine):
    return values * cosine + swapped(values) * sine


def bias_block(key_segment, query_segment, first, rows):
    key_at = lax.broadcasted_iota(jnp.int32, (rows, BLOCK), 0)
    query_at = lax.broadcasted_iota(jnp.int32, (rows, BLOCK), 1) + first
    allowed = (key_segment == query_segment) & (key_at <= query_at)
    return jnp.where(allowed, 0.0, MASKED)


def segment_row(segments):
    return jnp.concatenate(
        [segments[rank, i : i + 1, :] for rank in range(4) for i in range(2)], axis=1
    ).astype(F32)


def gain_rows(small):
    return small[:, 768:896].astype(F32).T[32:40, :]


def column_of(row):
    return jnp.broadcast_to(row, (8, row.shape[1])).T[:, 0:1]


def front_kernel(
    hidden, weights, cosine, sine, segments, own_hidden, ids, out_grad, share_a, share_b,
    normed, query, key, value, context_t, log_total, middle, normed_moe, gating,
    over_z, over_x, quad_a, quad_b, out_grad_all, bias, part, context, through, *refs,
):
    pair_refs = refs[:3]
    send, recv, here = refs[3:]
    at = Place()
    greet(
        [
            at.sibling(), at.partner(), at.ring(1), at.ring(3),
            at.along("x", 1), at.along("x", 3), at.along("z", 1), at.along("z", 3),
        ]
    )
    ring = RingGather(at, out_grad, out_grad_all, send, recv, here.at[0], 0)
    lines = first_gather(
        at, share_a, share_b, over_z, over_x, send, recv, here.at[pl.ds(1, 4)], 9
    )
    quad = second_gather(
        at, 0, over_z, over_x, quad_a, quad_b, send, recv, here.at[pl.ds(5, 4)],
        9 + SpreadOut.COPIES, through,
    )
    scatter = PairScatter(at, part, pair_refs, send, recv, 9 + 2 * SpreadOut.COPIES)
    lines.begin()
    ring.begin()

    gains = gain_rows(weights)
    seg_row = segment_row(segments)
    seg_column = column_of(seg_row)
    for block in range(SEQ // BLOCK):
        rows = slice(block * BLOCK, (block + 1) * BLOCK)
        values = hidden[rows, :].astype(F32)
        scale = lax.rsqrt(jnp.mean(values * values, axis=-1, keepdims=True) + EPS)
        normed[rows, :] = (values * scale * gains[0:1, :]).astype(BF)
    for half in range(2):
        columns = slice(half * 128, half * 128 + 128)
        pre = mm(normed[...], weights[:, columns])
        query[:, columns] = (rotated(pre, cosine[...], sine[...]) * 0.125).astype(BF)
    key_pre = mm(normed[...], weights[:, 256:384])
    key[...] = rotated(key_pre, cosine[...], sine[...]).astype(BF)
    value_pre = mm(normed[...], weights[:, 384:512])
    value[...] = value_pre.astype(BF)
    value_t = value_pre.T.astype(BF)
    lines.forward()
    for block in range(SEQ // BLOCK):
        first, end = block * BLOCK, (block + 1) * BLOCK
        bias[:end, :] = bias_block(seg_column[:end, :], seg_row[:, first:end], first, end)
        for head in range(HEADS):
            kv = slice((head // 2) * HD, (head // 2) * HD + HD)
            own = slice(head * HD, head * HD + HD)
            scores = mm_last(key[:end, kv], query[first:end, own]) + bias[:end, :]
            top = jnp.max(scores, axis=0, keepdims=True)
            powers = jnp.exp(scores - top)
            total = jnp.sum(powers, axis=0, keepdims=True)
            share = (powers * (1.0 / total)).astype(BF)
            context_t[own, first:end] = mm(value_t[kv, :end], share).astype(BF)
            log_total[head : head + 1, first:end] = top + jnp.log(total)
        if block == 2:
            ring.forward_before()
            ring.forward_behind()
    lines.finish()
    quad.begin()
    context[...] = context_t[...].T

    def project(slot):
        rows = pl.ds(pl.multiple_of(slot * LOCAL, LOCAL), LOCAL)
        part[slot] = mm_last(context[rows, :], weights[:, 512:768]).astype(BF)

    project(scatter.other + 1 - at.core)
    scatter.begin_far()
    project(scatter.other + at.core)
    project(scatter.own + 1 - at.core)
    scatter.begin_own()
    project(scatter.own + at.core)
    scatter.forward()
    quad.forward()
    ring.forward_across()
    scatter.finish(middle)
    values = middle[...] + own_hidden[...].astype(F32)
    middle[...] = values
    scale = lax.rsqrt(jnp.mean(values * values, axis=-1, keepdims=True) + EPS)
    normed_moe[...] = (values * scale * gains[1:2, :]).astype(BF)
    lane = lax.broadcasted_iota(jnp.int32, (LOCAL, 128), 1)
    chosen = lane == ids[:, 0:1]
    for i in range(1, TOPK):
        chosen = chosen | (lane == ids[:, i : i + 1])
    logits = jnp.where(chosen, mm(normed_moe[...], weights[:, 768:896]), MASKED)
    powers = jnp.where(chosen, jnp.exp(logits - jnp.max(logits, axis=-1, keepdims=True)), 0.0)
    gating[...] = powers / jnp.sum(powers, axis=-1, keepdims=True)
    for i in (0, 4, 6, 7, 8):
        ring.copy(i).wait_recv()
    ring.sent()
    ring.kept().wait()
    quad.finish()


def front(hidden, weights, tables, segments, own_hidden, ids, out_grad, shares, ident):
    vmem = pl.BlockSpec(memory_space=pltpu.VMEM)
    hbm = pl.BlockSpec(memory_space=pl.ANY)
    sems = 9 + 2 * SpreadOut.COPIES + 1 + 2 * PIECES
    return pl.pallas_call(
        front_kernel,
        in_specs=[vmem] * 10,
        out_specs=[vmem] * 9 + [hbm] * 5,
        out_shape=[
            jax.ShapeDtypeStruct((SEQ, D), BF),
            jax.ShapeDtypeStruct((SEQ, HEADS * HD), BF),
            jax.ShapeDtypeStruct((SEQ, 128), BF),
            jax.ShapeDtypeStruct((SEQ, 128), BF),
            jax.ShapeDtypeStruct((HEADS * HD, SEQ), BF),
            jax.ShapeDtypeStruct((8, SEQ), F32),
            jax.ShapeDtypeStruct((LOCAL, D), F32),
            jax.ShapeDtypeStruct((LOCAL, D), BF),
            jax.ShapeDtypeStruct((LOCAL, 128), F32),
            *[LINE_SHAPE] * 2,
            *[QUAD_SHAPE] * 2,
            jax.ShapeDtypeStruct((8, LOCAL, D), BF),
        ],
        scratch_shapes=[
            pltpu.VMEM((SEQ, BLOCK), F32),
            pltpu.VMEM((4, LOCAL, D), BF),
            pltpu.VMEM((SEQ, HEADS * HD), BF),
            pltpu.VMEM((2, *BLOCK_SHAPE), BF),
            *pair_scratch(LOCAL, D),
            pltpu.SemaphoreType.DMA((sems,)),
            pltpu.SemaphoreType.DMA((sems,)),
            pltpu.SemaphoreType.DMA((9,)),
        ],
        compiler_params=pltpu.CompilerParams(
            collective_id=ident, has_side_effects=True, vmem_limit_bytes=56 * MIB
        ),
        name="front",
    )(hidden, weights, *tables, segments, own_hidden, ids, out_grad, *shares)


def by_owner(value):
    return value.astype(BF).reshape(4, 4, 2, 32, value.shape[1])


def back_kernel(
    dx, dgate, gating, middle, normed_moe, out_grad, y_part,
    normed, weights, cosine, sine, segments, query, key, value, context_t, log_total,
    own_weights, own_hidden, expert_a, expert_b,
    land_0, land_1, land_2, land_3, land_4, land_5, land_6, land_7,
    hidden_grad, block_out, attention, rest, gate, up, down,
    bias, dcontext, dquery_t, dkey, dvalue, dall, dall_t, dattn_own, dattn_all, y_sum,
    grads, sum_1a, sum_1b, sum_2a, sum_2b, over_y, from_opposite, share_sum, shares,
    total_a, total_b, land_a, land_b, *refs,
):
    ring_refs, pair_refs = refs[:8], refs[8:11]
    first_refs = (refs[11:18], refs[18:25])
    groups = [refs[25 + 7 * i : 32 + 7 * i] for i in range(4)]
    landings = (refs[53:57], refs[57:61])
    send, recv, here, load = refs[61:]
    at = Place()
    greet(
        [
            at.sibling(), at.partner(), at.diagonal(), at.opposite(), at.ring(1), at.ring(3),
            at.along("x", 1), at.along("x", 3), at.along("z", 1), at.along("z", 3),
        ]
    )
    base = 9 + 2 * PIECES
    sums = [
        RingSum(
            at, "x", lambda k: expert_a.at[k], first_refs[0], send, recv, load, base, 0,
            (land_0, land_1, land_2, land_3),
        ),
        RingSum(
            at, "z", lambda k: expert_b.at[k], first_refs[1], send, recv, load,
            base + RingSum.COPIES, 7, (land_4, land_5, land_6, land_7),
        ),
    ]
    for each in sums:
        each.begin()
        each.direct()
    gain = gain_rows(weights)[1:2, :]
    chosen = gating[...]
    dchosen = chosen * (dgate[...] - jnp.sum(chosen * dgate[...], axis=-1, keepdims=True))
    dlogits = dchosen.astype(BF)
    dnormed = dx[...] + mm_last(dlogits, weights[:, 768:896])
    values = middle[...]
    scale = lax.rsqrt(jnp.mean(values * values, axis=-1, keepdims=True) + EPS)
    unit = values * scale
    weighted = dnormed * gain
    inner = jnp.mean(weighted * unit, axis=-1, keepdims=True)
    total = out_grad[...].astype(F32) + scale * (weighted - unit * inner)
    hidden_grad[...] = total
    dattn_own[...] = total.astype(BF)
    gather = PairGather(at, dattn_own, dattn_all, send, recv, here, 8, PIECES)
    scatter = RingScatter(at, y_part, ring_refs, send, recv)
    for k in (2, 1, 3, 0):
        scatter.copy(k).start()
    router_part = mm(normed_moe[...].T, dlogits)
    gain_part = column_of(jnp.sum(dnormed * unit, axis=0, keepdims=True))
    lane = lax.broadcasted_iota(jnp.int32, (D, 128), 1)
    grads[..., 768:] = by_owner(jnp.where(lane == 32, gain_part, router_part))
    seg_row = segment_row(segments)
    seg_column = column_of(seg_row)
    gather.forward()
    scatter.far()
    for each in sums:
        each.middle()
    gather.finish()
    dattn = dattn_all[...].reshape(SEQ, D)
    dcontext[...] = mm(dattn, weights[:, 512:768]).astype(BF)
    output_grad_t = mm(context_t[...], dattn)
    grads[..., 512:768] = by_owner(output_grad_t.T)
    key_t = key[...].astype(F32).T.astype(BF)
    dkey[...] = jnp.zeros_like(dkey)
    dvalue[...] = jnp.zeros_like(dvalue)
    for block in range(SEQ // BLOCK):
        first, end = block * BLOCK, (block + 1) * BLOCK
        bias[:end, :] = bias_block(seg_column[:end, :], seg_row[:, first:end], first, end)
        for head in range(HEADS):
            kv = slice((head // 2) * HD, (head // 2) * HD + HD)
            own = slice(head * HD, head * HD + HD)
            query_block = query[first:end, own]
            dcontext_block = dcontext[first:end, own]
            scores = mm_last(key[:end, kv], query_block) + bias[:end, :]
            share = jnp.exp(scores - log_total[head : head + 1, first:end])
            dshare = mm_last(value[:end, kv], dcontext_block)
            centre = jnp.sum(share * dshare, axis=0, keepdims=True)
            dscore = (share * (dshare - centre)).astype(BF)
            dquery_t[own, first:end] = mm(key_t[kv, :end], dscore) * 0.125
            dkey[:end, kv] += mm(dscore, query_block)
            dvalue[:end, kv] += mm(share.astype(BF), dcontext_block)
        if block == 0:
            scatter.up_side()
            scatter.down_side()
        if block == 2:
            last = base + 6 * RingSum.COPIES + 1 + 2 * PIECES
            final_sums = []
            for i, (each, axis, refs_of, landing) in enumerate(
                zip(sums, ("z", "x"), first_refs, landings)
            ):
                each.finish(each.own)
                to_up, to_down, own = refs_of[4].at[0, pl.ds(0, 1)], refs_of[5].at[0, pl.ds(0, 1)], refs_of[2].at[0]
                final_sums.append(
                    RingSum(
                        at, axis, lambda k, own=each.own: own.at[k], (*landing, to_up, to_down, own),
                        send, recv, load, last + RingSum.COPIES * i, 26 + 3 * i,
                    )
                )
                final_sums[i].begin()
                final_sums[i].direct()
        if block == 3:
            for each in final_sums:
                each.middle()
    turn = -sine[...]
    for half in range(2):
        rows = slice(half * 128, half * 128 + 128)
        piece = rotated(dquery_t[rows, :].T, cosine[...], turn)
        dall[:, rows] = piece.astype(BF)
        dall_t[rows, :] = piece.T.astype(BF)
    piece = rotated(dkey[...], cosine[...], turn)
    dall[:, 256:384] = piece.astype(BF)
    dall_t[256:384, :] = piece.T.astype(BF)
    dall[:, 384:512] = dvalue[...].astype(BF)
    dall_t[384:512, :] = dvalue[...].T.astype(BF)
    grads[..., 0:512] = by_owner(mm(dall_t[...], normed[...]).T)
    after = base + 2 * RingSum.COPIES
    width = grads.shape[-1]
    a, b = pl.ds(0, SPLIT), pl.ds(SPLIT, width - SPLIT)

    def ring_sum(i, axis, part_of, scratch):
        return RingSum(
            at, axis, part_of, scratch, send, recv, load, after + RingSum.COPIES * i, 14 + 3 * i
        )

    first_a = ring_sum(0, "x", lambda k: grads.at[k, :, :, :, a], groups[0])
    first_b = ring_sum(1, "z", lambda k: grads.at[:, k, :, :, b], groups[1])
    second_a = ring_sum(2, "z", lambda k: sum_1a.at[k], groups[2])
    second_b = ring_sum(3, "x", lambda k: sum_1b.at[k], groups[3])
    for each in (first_a, first_b):
        each.begin()
        each.direct()
    after = after + 4 * RingSum.COPIES
    pair = PairScatter(at, dattn_all, pair_refs, send, recv, after)
    after = after + 1 + 2 * PIECES + 2 * RingSum.COPIES

    def project(slot):
        rows = pl.ds(pl.multiple_of(slot * LOCAL, LOCAL), LOCAL)
        dattn_all[slot] = mm_last(dall[rows, :], weights[:, 0:512]).astype(BF)

    project(pair.other + 1 - at.core)
    pair.begin_far()
    project(pair.other + at.core)
    project(pair.own + 1 - at.core)
    pair.begin_own()
    project(pair.own + at.core)
    pair.forward()
    first_a.middle()
    first_b.middle()
    lands = []
    for i, (each, out, land) in enumerate(
        zip(final_sums, (total_a, total_b), (land_a, land_b))
    ):
        each.finish(out)
        lands.append(push(out.at[1 - at.yh], land, send, recv, after + 1 + i, at.opposite()))
    scatter.finish(y_sum)
    block_out[...] = (y_sum[...] + middle[...]).astype(BF)

    first_a.finish(sum_1a)
    second_a.begin()
    second_a.direct()
    first_b.finish(sum_1b)
    second_b.begin()
    second_b.direct()
    second_a.middle()
    second_b.middle()
    second_a.finish(sum_2a)
    second_b.finish(sum_2b)
    over_y[:, a] = sum_2a[...].reshape(64, SPLIT)
    over_y[:, b] = sum_2b[...].reshape(64, width - SPLIT)
    theirs = pl.ds(pl.multiple_of((1 - at.yh) * 32, 32), 32)
    own = pl.ds(pl.multiple_of(at.yh * 32, 32), 32)
    swap = push(over_y.at[theirs], from_opposite, send, recv, after, at.opposite())
    dn1 = y_sum
    pair.finish(dn1)
    hidden = own_hidden[...].astype(F32)
    scale = lax.rsqrt(jnp.mean(hidden * hidden, axis=-1, keepdims=True) + EPS)
    unit = hidden * scale
    weighted = dn1[...] * gain_rows(weights)[0:1, :]
    inner = jnp.mean(weighted * unit, axis=-1, keepdims=True)
    hidden_grad[...] += scale * (weighted - unit * inner)
    swap.wait_recv()
    total = over_y[own, :].astype(F32) + from_opposite[...].astype(F32)
    attention[...] = total[:, :768]
    gain_part = jnp.sum(total[:, :512] * own_weights[...].astype(F32), axis=1, keepdims=True)
    lane = lax.broadcasted_iota(jnp.int32, (32, 128), 1)
    share_sum[...] = jnp.where(lane == 33, gain_part, total[:, 768:])
    copies = [
        push(share_sum, shares.at[i], send, recv, after + 3 + i, device)
        for i, device in enumerate((at.sibling(), at.partner(), at.diagonal()))
    ]
    mine, theirs = pl.ds(at.yh * STEPS, STEPS), pl.ds((1 - at.yh) * STEPS, STEPS)
    for j, value in enumerate((total_a, total_b)):
        for i, out in enumerate((gate, up, down)):
            out[mine, 2 * j : 2 * j + 2] = value[at.yh, :, i].astype(F32)
    rest[...] = share_sum[...]
    for i, copy in enumerate(copies):
        copy.wait_recv()
        rest[...] += shares[i]
    for j, (copy, land) in enumerate(zip(lands, (land_a, land_b))):
        copy.wait_recv()
        for i, out in enumerate((gate, up, down)):
            out[theirs, 2 * j : 2 * j + 2] = land[:, i].astype(F32)
    for copy in (swap, *copies, *lands):
        copy.wait_send()


def back(
    dx, dgate, gating, middle, normed_moe, out_grad, y_part,
    normed, weights, tables, segments, kept, own_weights, own_hidden, expert_grads, ident,
):
    vmem = pl.BlockSpec(memory_space=pltpu.VMEM)
    hbm = pl.BlockSpec(memory_space=pl.ANY)
    sems = 2 * (9 + 2 * PIECES) + 8 * RingSum.COPIES + 6
    block = SUMS_SHAPE.shape[1:]
    half = (block[0] // 2, *block[1:])
    first_a, first_b = (4, 2, 32, SPLIT), (4, 2, 32, SMALL - SPLIT)
    landing = [pltpu.VMEM(half, BF)] * 2 + [pltpu.VMEM(block, BF)] * 2
    return pl.pallas_call(
        back_kernel,
        in_specs=[vmem] * 19 + [hbm] * 10,
        out_specs=[vmem] * 7,
        out_shape=[
            jax.ShapeDtypeStruct((LOCAL, D), F32),
            jax.ShapeDtypeStruct((LOCAL, D), BF),
            jax.ShapeDtypeStruct((32, 768), F32),
            jax.ShapeDtypeStruct((32, 128), F32),
            *[jax.ShapeDtypeStruct((2 * STEPS, QUAD, 32, FF), F32)] * 3,
        ],
        scratch_shapes=[
            pltpu.VMEM((SEQ, BLOCK), F32),
            pltpu.VMEM((SEQ, HEADS * HD), BF),
            pltpu.VMEM((HEADS * HD, SEQ), F32),
            pltpu.VMEM((SEQ, 128), F32),
            pltpu.VMEM((SEQ, 128), F32),
            pltpu.VMEM((SEQ, 512), BF),
            pltpu.VMEM((512, SEQ), BF),
            pltpu.VMEM((LOCAL, D), BF),
            pltpu.VMEM((4, LOCAL, D), BF),
            pltpu.VMEM((LOCAL, D), F32),
            pltpu.VMEM((4, 4, 2, 32, SMALL), BF),
            pltpu.VMEM(first_a, BF),
            pltpu.VMEM(first_b, BF),
            pltpu.VMEM(first_a[1:], BF),
            pltpu.VMEM(first_b[1:], BF),
            pltpu.VMEM((64, SMALL), BF),
            pltpu.VMEM((32, SMALL), BF),
            pltpu.VMEM((32, 128), F32),
            pltpu.VMEM((3, 32, 128), F32),
            *[pltpu.VMEM(block, BF)] * 2,
            *[pltpu.VMEM(block[1:], BF)] * 2,
            *ring_scratch(LOCAL, D),
            *pair_scratch(LOCAL, D),
            *sum_scratch(SUMS_SHAPE.shape),
            *sum_scratch(SUMS_SHAPE.shape),
            *sum_scratch(first_a),
            *sum_scratch(first_b),
            *sum_scratch(first_a[1:]),
            *sum_scratch(first_b[1:]),
            *landing,
            *landing,
            pltpu.SemaphoreType.DMA((sems,)),
            pltpu.SemaphoreType.DMA((sems,)),
            pltpu.SemaphoreType.DMA,
            pltpu.SemaphoreType.DMA((32,)),
        ],
        compiler_params=pltpu.CompilerParams(
            collective_id=ident, has_side_effects=True, vmem_limit_bytes=63 * MIB
        ),
        name="back",
    )(
        dx, dgate, gating, middle, normed_moe, out_grad, y_part,
        normed, weights, *tables, segments, *kept, own_weights, own_hidden, *expert_grads,
    )


def experts_kernel(
    x_in, gate_in, d_in, over_z, over_x, quad_0a, quad_0b, y_out, dx_out, dgate_out,
    all_a, all_b, land_0, land_1, land_2, land_3, land_4, land_5, land_6, land_7,
    quad_1a, quad_1b, quad_2a, quad_2b, quad_3a, quad_3b,
    x, d, xt, dt, y, dx, gating, dgate, dgate_part, hidden, w, *refs,
):
    dx_scratch, dgate_scratch = refs[:5], refs[5:10]
    send, recv, here, load, store, fetch = refs[10:16]
    at = Place()
    step = pl.program_id(0)
    opening, closing = step == 0, step == STEPS - 1
    rows_at_once = 2 * LOCAL
    lane = lax.broadcasted_iota(jnp.int32, (LOCAL, 128), 1)
    own_first = at.yh * 16 + step * QUAD
    x_gather = RingGather(at, x_in, x, send, recv, here.at[0], 0)
    gate_gather = RingGather(at, gate_in, gating, send, recv, here.at[1], 9)
    gathers = (x_gather, gate_gather)
    scatters = (
        RingScatter(at, d, dx_scratch, send, recv, 18),
        RingScatter(at, dgate_part, dgate_scratch, send, recv, 26),
    )

    later = ((quad_1a, quad_1b), (quad_2a, quad_2b), (quad_3a, quad_3b))
    quads = [
        second_gather(
            at, 1 + i, over_z, over_x, *quad, *refs[16:18], refs[18].at[pl.ds(4 * i, 4)],
            SpreadOut.COPIES * i, refs[19],
        )
        for i, quad in enumerate(later)
    ]

    def ride(condition, what):
        for i, quad in enumerate(quads):

            @pl.when(condition & (step == i))
            def _():
                what(quad)

    grads_a, grads_b, ship_send, ship_recv, keep_sems = refs[20:]

    def shipments(number):
        lo, hi = pl.ds(0, 2), pl.ds(2, 2)
        plan = []
        for part, place, axis, lands in (
            (grads_a, at.x, "x", (land_0, land_1, land_2, land_3)),
            (grads_b, at.z, "z", (land_4, land_5, land_6, land_7)),
        ):
            above, across, below = (part.at[lax.rem(place + k, 4)] for k in (1, 2, 3))
            upper, lower = at.along(axis, 1), at.along(axis, 3)
            plan += [
                (across.at[lo], lands[0], upper), (across.at[hi], lands[1], lower),
                (above.at[hi], lands[2], upper), (below.at[lo], lands[3], lower),
            ]
        return [
            remote(src, land.at[:, :, number], ship_send, ship_recv, 8 * number + i, device)
            for i, (src, land, device) in enumerate(plan)
        ]

    def keeps(number):
        return [
            pltpu.make_async_copy(part, out.at[:, :, :, number], keep_sems.at[i])
            for i, (part, out) in enumerate(((grads_a, all_a), (grads_b, all_b)))
        ]

    def shipped(number):
        for copy in shipments(number):
            copy.wait_send()
        for copy in keeps(number):
            copy.wait()

    def begin_shipping():
        for copy in shipments(step):
            copy.start()

    def fetches(quad_a, quad_b):
        copies = []
        for g in range(3):
            for i in range(QUAD):
                columns = pl.ds((g * QUAD + i) * FF, FF)
                if i < 2:
                    parts = [(quad_a.at[:, :, :, g, i], w.at[:, :, :, :, columns])]
                else:
                    parts = [
                        (quad_b.at[:, x_at, :, g, i - 2], w.at[x_at, :, :, :, columns])
                        for x_at in range(4)
                    ]
                for part in parts:
                    copies.append(pltpu.make_async_copy(*part, fetch.at[len(copies)]))
        return copies

    def d_load(chip):
        two = pl.ds(chip * 2, 2)
        return pltpu.make_async_copy(d_in.at[two], d.at[two], load.at[chip])

    def y_store(chip):
        two = pl.ds(chip * 2, 2)
        return pltpu.make_async_copy(x.at[two], y_out.at[two], store.at[chip])

    @pl.when(opening)
    def _():
        greet(
            [
                at.sibling(), at.ring(1), at.ring(3),
                at.along("x", 1), at.along("x", 3), at.along("z", 1), at.along("z", 3),
            ]
        )
        for gather in gathers:
            gather.begin()
        for copy in fetches(quad_0a, quad_0b):
            copy.start()
        for chip in range(4):
            d_load(chip).start()

    for copy in fetches(quad_0a, quad_0b):
        copy.wait()

    ride(step < STEPS, lambda quad: quad.begin())

    def arrive(turn):
        @pl.when(turn == 0)
        def _():
            for gather in gathers:
                gather.kept().wait()
                gather.copy(0).wait_recv()

        @pl.when(turn == 1)
        def _():
            for gather in gathers:
                gather.forward_before()
                gather.forward_behind()
            for gather in gathers:
                gather.copy(4).wait_recv()

        @pl.when(turn == 2)
        def _():
            for gather in gathers:
                gather.forward_across()
            for gather in gathers:
                gather.copy(6).wait_recv()

        @pl.when(turn == 3)
        def _():
            for gather in gathers:
                gather.copy(7).wait_recv()
                gather.copy(8).wait_recv()

    def leave(turn):
        @pl.when(turn == 0)
        def _():
            for scatter in scatters:
                scatter.copy(2).start()

        @pl.when(turn == 1)
        def _():
            for scatter in scatters:
                scatter.copy(1).start()
                scatter.far()

        @pl.when(turn == 2)
        def _():
            for scatter in scatters:
                scatter.copy(3).start()
                scatter.up_side()

        @pl.when(turn == 3)
        def _():
            for scatter in scatters:
                scatter.copy(0).start()
                scatter.down_side()

    def tokens_block(turn, carry):
        inward = jnp.where(turn == 0, 0, jnp.where(turn == 1, 3, turn - 1))
        outward = jnp.where(turn == 0, 2, jnp.where(turn == 3, 0, turn * 2 - 1))
        chip = at.chip(jnp.where(closing, outward, inward))
        two = pl.ds(chip * 2, 2)
        rows = pl.ds(pl.multiple_of(chip * rows_at_once, rows_at_once), rows_at_once)

        @pl.when(opening)
        def _():
            arrive(turn)
            d_load(chip).wait()
            xt[:, rows] = x[two].reshape(rows_at_once, D).T
            dt[:, rows] = d[two].reshape(rows_at_once, D).T
            y[rows, :] = jnp.zeros((rows_at_once, D), F32)
            dx[rows, :] = jnp.zeros((rows_at_once, D), F32)
            dgate[rows, :] = jnp.zeros((rows_at_once, 128), F32)

        ride(turn == 3, lambda quad: quad.forward())
        gate_up = w[:, :, :, :, 0 : 2 * F].reshape(D, 2 * F)
        down = w[:, :, :, :, 2 * F :].reshape(D, F)
        for core in range(2):
            slot = chip * 2 + core
            part = pl.ds(pl.multiple_of(slot * LOCAL, LOCAL), LOCAL)
            both = mm(x[slot], gate_up)
            gate, up = both[:, :F], both[:, F:]
            dact = mm(d[slot], down)
            turned = pltpu.roll(gating[slot], lax.rem(128 - own_first, 128), 1)
            factor = jnp.concatenate(
                [jnp.broadcast_to(turned[:, i : i + 1], (LOCAL, FF)) for i in range(QUAD)],
                axis=1,
            )
            q = 1.0 / (1.0 + jnp.exp(-gate))
            silu = gate * q
            act = silu * up
            product = act * dact
            sums = dgate[part, :]
            for i in range(QUAD):
                own = jnp.sum(product[:, i * FF : (i + 1) * FF], axis=1, keepdims=True)
                sums = jnp.where(lane == own_first + i, own, sums)
            dgate[part, :] = sums
            dact = dact * factor
            hidden[part, 0:F] = (dact * up * (q + silu * (1.0 - q))).astype(BF)
            hidden[part, F : 2 * F] = (dact * silu).astype(BF)
            hidden[part, 2 * F :] = (act * factor).astype(BF)
        y[rows, :] += mm_last(hidden[rows, 2 * F :], down)
        dx[rows, :] += mm_last(hidden[rows, 0 : 2 * F], gate_up)

        @pl.when(closing)
        def _():
            x[two] = y[rows, :].astype(BF).reshape(2, LOCAL, D)
            d[two] = dx[rows, :].astype(BF).reshape(2, LOCAL, D)
            dgate_part[two] = dgate[rows, :].astype(BF).reshape(2, LOCAL, 128)
            y_store(chip).start()
            leave(turn)

        return carry

    lax.fori_loop(0, 4, tokens_block, 0)

    @pl.when(opening)
    def _():
        for gather in gathers:
            gather.sent()

    @pl.when(step > 0)
    def _():
        shipped(step - 1)

    def grads_block(block, carry):
        rows = pl.ds(pl.multiple_of(block * 512, 512), 512)

        def put(g, value):
            value = value.astype(BF).reshape(2, 4, 2, 32, value.shape[1])
            for j in range(value.shape[-1] // FF):
                piece = value[..., j * FF : (j + 1) * FF]
                group, i = g + j // QUAD, j % QUAD
                for x_at in range(2):
                    if i < 2:
                        grads_a[block * 2 + x_at, :, :, group, i] = piece[x_at]
                    else:
                        grads_b[:, block * 2 + x_at, :, group, i - 2] = piece[x_at]

        ride(block == 1, lambda quad: quad.finish())
        for number, quad in enumerate(later):

            @pl.when((block == 1) & (step == number))
            def _():
                for copy in fetches(*quad):
                    copy.start()

        put(0, mm(xt[rows, :], hidden[:, 0 : 2 * F]))
        put(2, mm(dt[rows, :], hidden[:, 2 * F :]))
        return carry

    lax.fori_loop(0, D // 512, grads_block, 0)
    for copy in keeps(step):
        copy.start()
    pl.when(step < STEPS - 1)(begin_shipping)

    @pl.when(closing)
    def _():
        scatters[0].finish(dx_out)
        scatters[1].finish(dgate_out)
        for chip in range(4):
            y_store(chip).wait()
        for copy in keeps(step):
            copy.wait()
        for number in range(STEPS - 1):
            for copy in shipments(number):
                copy.wait_recv()


def experts(x, gating, d, lines, quad, ident):
    hbm = pl.BlockSpec(memory_space=pl.ANY)

    def whole(rows, columns):
        return pl.BlockSpec((rows, columns), lambda step: (0, 0), pipeline_mode=pl.Buffered(1))

    return pl.pallas_call(
        experts_kernel,
        grid=(STEPS,),
        in_specs=[hbm] * 7,
        out_specs=[
            hbm,
            whole(LOCAL, D),
            whole(LOCAL, 128),
            *[hbm] * 10,
            *[hbm] * 6,
        ],
        out_shape=[
            jax.ShapeDtypeStruct((8, LOCAL, D), BF),
            jax.ShapeDtypeStruct((LOCAL, D), F32),
            jax.ShapeDtypeStruct((LOCAL, 128), F32),
            *[GRADS_SHAPE] * 2,
            *[LAND_SHAPE] * 8,
            *[QUAD_SHAPE] * 6,
        ],
        scratch_shapes=[
            pltpu.VMEM((8, LOCAL, D), BF),
            pltpu.VMEM((8, LOCAL, D), BF),
            pltpu.VMEM((D, TOKENS), BF),
            pltpu.VMEM((D, TOKENS), BF),
            pltpu.VMEM((TOKENS, D), F32),
            pltpu.VMEM((TOKENS, D), F32),
            pltpu.VMEM((8, LOCAL, 128), F32),
            pltpu.VMEM((TOKENS, 128), F32),
            pltpu.VMEM((8, LOCAL, 128), BF),
            pltpu.VMEM((TOKENS, 3 * F), BF),
            pltpu.VMEM((4, 4, 2, 32, 3 * F), BF),
            *ring_scratch(LOCAL, D, False),
            *ring_scratch(LOCAL, 128, False),
            pltpu.SemaphoreType.DMA((34,)),
            pltpu.SemaphoreType.DMA((34,)),
            pltpu.SemaphoreType.DMA((2,)),
            pltpu.SemaphoreType.DMA((4,)),
            pltpu.SemaphoreType.DMA((4,)),
            pltpu.SemaphoreType.DMA((30,)),
            pltpu.SemaphoreType.DMA((3 * SpreadOut.COPIES,)),
            pltpu.SemaphoreType.DMA((3 * SpreadOut.COPIES,)),
            pltpu.SemaphoreType.DMA((12,)),
            pltpu.VMEM((2, *BLOCK_SHAPE), BF),
            *[pltpu.VMEM((4, 4, 2, 3, 2, 32, FF), BF)] * 2,
            pltpu.SemaphoreType.DMA((8 * STEPS - 8,)),
            pltpu.SemaphoreType.DMA((8 * STEPS - 8,)),
            pltpu.SemaphoreType.DMA((2,)),
        ],
        compiler_params=pltpu.CompilerParams(
            collective_id=ident, has_side_effects=True, vmem_limit_bytes=63 * MIB
        ),
        name="experts",
    )(x, gating, d, *lines, *quad)[:13]


def on_device(
    hidden_in, out_grad, attn_gain, query_weight, key_weight, value_weight, output_weight,
    moe_gain, router_weight, expert_gate, expert_up, expert_down, expert_ids, segment_ids,
):
    gains = jnp.stack([attn_gain, moe_gain])
    smalls = (query_weight, key_weight, value_weight, output_weight, router_weight, gains)
    own_shares = (expert_gate, expert_up, expert_down)
    hidden_all, segments, small, *shares = startup(
        hidden_in, segment_ids.reshape(2, 128), smalls, own_shares, 0
    )
    tables = tuple(jnp.asarray(t) for t in rotary_tables())
    normed, *more, d = front(
        hidden_all, small, tables, segments, hidden_in, expert_ids, out_grad, shares, 1
    )
    kept, (middle, normed_moe, gating), lines, quad = more[:5], more[5:8], more[8:10], more[10:]
    y, dx, dgate, *expert_grads = experts(normed_moe, gating, d, lines, quad, 3)
    own_weights = jnp.concatenate([query_weight, key_weight, value_weight], axis=1)
    hidden_grad, block_out, attention_grads, rest, *expert_grads = back(
        dx, dgate, gating, middle, normed_moe, out_grad, y,
        normed, small, tables, segments, kept, own_weights, hidden_in, expert_grads, 5,
    )
    expert_grads = [share.reshape(E, 32, FF) for share in expert_grads]
    return (
        block_out,
        hidden_grad,
        rest[:, 33] / attn_gain.astype(F32),
        attention_grads[:, 0:256],
        attention_grads[:, 256:384],
        attention_grads[:, 384:512],
        attention_grads[:, 512:768],
        rest[:, 32],
        rest[:, :32],
        *expert_grads,
    )


def solution(mesh):
    fine = Mesh(np.asarray(mesh.devices).reshape(4, 4, 2, 2, 2), ALL)
    return jax.shard_map(
        on_device,
        mesh=fine,
        in_specs=(
            P(ALL, None),
            P(ALL, None),
            P(DP),
            P(DP, TENSOR),
            P(DP, TENSOR),
            P(DP, TENSOR),
            P(DP, TENSOR),
            P(DP),
            P(DP, None),
            P(None, DP, TENSOR),
            P(None, DP, TENSOR),
            P(None, DP, TENSOR),
            P(ALL, None),
            P(ALL),
        ),
        out_specs=(
            P(ALL, None),
            P(ALL, None),
            P(DP),
            P(DP, TENSOR),
            P(DP, TENSOR),
            P(DP, TENSOR),
            P(DP, TENSOR),
            P(DP),
            P(DP, None),
            P(None, DP, TENSOR),
            P(None, DP, TENSOR),
            P(None, DP, TENSOR),
        ),
        check_vma=False,
    )
```

```python
import jax
import jax.numpy as jnp
import numpy as np
from jax import lax
from jax.experimental import pallas as pl
from jax.experimental.pallas import tpu as pltpu
from jax.sharding import Mesh
from jax.sharding import PartitionSpec as P

D = 1024
HD = 64
E = 32
SEQ = 1024
LOCAL = 256
HEADS = 4
QUAD = 4
FF = 128
F = QUAD * FF
EPS = 1e-06
TOPK = 8
MASKED = -1e30
BLOCK = 256
TOKENS = 2048
STEPS = 4

DP = ("x", "z", "yh")
TENSOR = ("yl", "core")
RING = ("yh", "yl", "core")
PLANE = ("x", "z")
ALL = ("x", "z", "yh", "yl", "core")

F32 = jnp.float32
BF = jnp.bfloat16
LAST = (((1,), (1,)), ((), ()))
MIB = 1024 * 1024
MESH = pl.DeviceIdType.MESH
SMALL = 896


def mm(a, b):
    return jnp.dot(a, b, preferred_element_type=F32)


def mm_last(a, b):
    return lax.dot_general(a, b, LAST, preferred_element_type=F32)


class Place:
    def __init__(self):
        self.x = lax.axis_index("x")
        self.z = lax.axis_index("z")
        self.yh = lax.axis_index("yh")
        self.yl = lax.axis_index("yl")
        self.core = lax.axis_index("core")
        self.y = self.yh * 2 + self.yl

    def chip(self, k):
        return lax.rem(self.y + k, 4)

    def ring(self, k):
        chip = self.chip(k)
        return {"yh": chip // 2, "yl": lax.rem(chip, 2)}

    def along(self, axis, k):
        return {axis: lax.rem(getattr(self, axis) + k, 4)}

    def sibling(self):
        return {"core": 1 - self.core}

    def partner(self):
        return {"yl": 1 - self.yl}

    def diagonal(self):
        return {"yl": 1 - self.yl, "core": 1 - self.core}

    def opposite(self):
        return {"yh": 1 - self.yh}


def greet(devices):
    barrier = pltpu.get_barrier_semaphore()
    for device in devices:
        pl.semaphore_signal(barrier, inc=1, device_id=device, device_id_type=MESH)
    pl.semaphore_wait(barrier, len(devices))


def remote(src, dst, send, recv, i, device):
    return pltpu.make_async_remote_copy(
        src_ref=src, dst_ref=dst, send_sem=send.at[i], recv_sem=recv.at[i],
        device_id=device, device_id_type=MESH,
    )


def push(src, dst, send, recv, i, device):
    copy = remote(src, dst, send, recv, i, device)
    copy.start()
    return copy


def keep(src, dst, sem):
    copy = pltpu.make_async_copy(src, dst, sem)
    copy.start()
    return copy


class RingGather:
    def __init__(self, at, own, out, send, recv, here, base=0):
        self.at, self.own, self.out, self.base = at, own, out, base
        self.send, self.recv, self.here = send, recv, here
        half = own.shape[0] // 2
        lo, hi = pl.ds(0, half), pl.ds(half, half)
        me, before, behind, across = (out.at[self.slot(k)] for k in (0, 3, 1, 2))
        near, up, down = at.sibling(), at.ring(1), at.ring(3)
        self.plan = [
            (own, me, near),
            (own, me, up),
            (own, me, down),
            (before.at[lo], before.at[lo], up),
            (before, before, near),
            (behind.at[hi], behind.at[hi], down),
            (behind, behind, near),
            (across.at[lo], across.at[lo], near),
            (across.at[hi], across.at[hi], near),
        ]

    def slot(self, k):
        return self.at.chip(k) * 2 + self.at.core

    def copy(self, i):
        src, dst, device = self.plan[i]
        return remote(src, dst, self.send, self.recv, self.base + i, device)

    def kept(self):
        return pltpu.make_async_copy(self.own, self.out.at[self.slot(0)], self.here)

    def begin(self):
        self.kept().start()
        for i in (1, 2, 0):
            self.copy(i).start()

    def forward_before(self):
        self.copy(1).wait_recv()
        self.copy(3).start()
        self.copy(4).start()

    def forward_behind(self):
        self.copy(2).wait_recv()
        self.copy(5).start()
        self.copy(6).start()

    def forward_across(self):
        self.copy(3).wait_recv()
        self.copy(7).start()
        self.copy(5).wait_recv()
        self.copy(8).start()

    def sent(self):
        for i in range(9):
            self.copy(i).wait_send()


class PairGather:
    def __init__(self, at, own, out, send, recv, here, base, pieces):
        self.at, self.out, self.send, self.recv, self.base = at, out, send, recv, base
        size = own.shape[0] // pieces
        self.parts = [pl.ds(i * size, size) for i in range(pieces)]
        me = at.yl * 2 + at.core
        self.other = (1 - at.yl) * 2 + at.core
        self.kept = keep(own, out.at[me], here)
        self.far = [
            push(own.at[part], out.at[me, part], send, recv, base + 1 + i, at.partner())
            for i, part in enumerate(self.parts)
        ]
        self.near = [push(own, out.at[me], send, recv, base, at.sibling())]

    def forward(self):
        for i, part in enumerate(self.parts):
            self.far[i].wait_recv()
            view = self.out.at[self.other, part]
            index = self.base + 1 + len(self.parts) + i
            self.near.append(push(view, view, self.send, self.recv, index, self.at.sibling()))

    def finish(self):
        for copy in self.near:
            copy.wait_recv()
        for copy in (*self.far, *self.near):
            copy.wait_send()
        self.kept.wait()


PIECES = 4


class AxisGather:
    def __init__(self, at, axis, view, send, recv, base):
        self.up, self.down = at.along(axis, 1), at.along(axis, 3)
        self.view, self.send, self.recv, self.base = view, send, recv, base

    def go(self, i, view, device):
        return push(view, view, self.send, self.recv, self.base + i, device)

    def begin(self):
        self.first = [
            self.go(0, self.view(0, "all"), self.up), self.go(1, self.view(0, "all"), self.down),
        ]

    def forward(self):
        self.first[0].wait_recv()
        self.far = [self.go(2, self.view(3, "low"), self.up)]
        self.first[1].wait_recv()
        self.far.append(self.go(3, self.view(1, "high"), self.down))

    def finish(self):
        for copy in self.far:
            copy.wait_recv()
        for copy in (*self.first, *self.far):
            copy.wait_send()


def halves_of(ref, first, size):
    spans = {"all": (0, size), "low": (0, size // 2), "high": (size // 2, size // 2)}
    return lambda part: ref.at[pl.ds(first + spans[part][0], spans[part][1])]


class SpreadOut:
    COPIES = 8

    def __init__(self, at, rings, send, recv, here, base=0, through=None):
        self.send, self.recv, self.here, self.base = send, recv, here, base
        self.through = through
        self.own = [(own, slot(0)) for _, own, slot, _ in rings]
        self.plan = []
        for axis, own, slot, _ in rings:
            self.plan.append((own, slot(0), at.along(axis, 1)))
            self.plan.append((own, slot(0), at.along(axis, 3)))
        for axis, _, slot, half in rings:
            low, high = (slot(3).at[pl.ds(0, half)], slot(1).at[pl.ds(half, half)])
            self.plan.append((low, low, at.along(axis, 1)))
            self.plan.append((high, high, at.along(axis, 3)))

    def copy(self, i):
        src, dst, device = self.plan[i]
        return remote(src, dst, self.send, self.recv, self.base + i, device)

    def loaded(self, i):
        return pltpu.make_async_copy(self.own[i][0], self.through.at[i], self.here.at[i])

    def kept(self, i):
        src, dst = self.own[i]
        src = src if self.through is None else self.through.at[i]
        return pltpu.make_async_copy(src, dst, self.here.at[2 + i])

    def begin(self):
        for i in range(4):
            self.copy(i).start()
        for i in range(2):
            (self.kept(i) if self.through is None else self.loaded(i)).start()

    def forward(self):
        for i in range(4):
            self.copy(i).wait_recv()
            self.copy(4 + i).start()
        if self.through is not None:
            for i in range(2):
                self.loaded(i).wait()
                self.kept(i).start()

    def finish(self):
        for i in range(4, 8):
            self.copy(i).wait_recv()
        for i in range(8):
            self.copy(i).wait_send()
        for i in range(2):
            self.kept(i).wait()


def ring_slots(out, place):
    return lambda k: out.at[lax.rem(place + k, 4)]


def first_gather(at, own_a, own_b, over_z, over_x, *sems):
    rings = (
        ("z", own_a, ring_slots(over_z, at.z), 1), ("x", own_b, ring_slots(over_x, at.x), 1),
    )
    return SpreadOut(at, rings, *sems)


def second_gather(at, number, over_z, over_x, quad_a, quad_b, *sems):
    rings = (
        ("x", over_z.at[:, :, number], ring_slots(quad_a, at.x), 2),
        ("z", over_x.at[:, :, number], ring_slots(quad_b, at.z), 2),
    )
    return SpreadOut(at, rings, *sems)


SHARE_SHAPE = jax.ShapeDtypeStruct((2, STEPS, 3, 2, 32, FF), BF)
BLOCK_SHAPE = (4, 2, 3, 2, 32, FF)
LINE_SHAPE = jax.ShapeDtypeStruct((4, 2, STEPS, 3, 2, 32, FF), BF)
QUAD_SHAPE = jax.ShapeDtypeStruct((4, 4, 2, 3, 2, 32, FF), BF)
GRADS_SHAPE = jax.ShapeDtypeStruct((4, 4, 2, STEPS, 3, 2, 32, FF), BF)
LAND_SHAPE = jax.ShapeDtypeStruct((2, 2, STEPS - 1, 3, 2, 32, FF), BF)
SUMS_SHAPE = jax.ShapeDtypeStruct((4, 2, STEPS, 3, 2, 32, FF), BF)


class RingSum:
    COPIES = 6

    def __init__(
        self, at, axis, part_of, scratch, send, recv, load, base=0, first=0, arrived=None
    ):
        half_a, half_b, up, down, to_up, to_down, own = scratch
        self.half_a, self.half_b, self.up, self.down = half_a, half_b, up, down
        self.to_up, self.to_down, self.own = to_up, to_down, own
        self.send, self.recv, self.base = send, recv, base
        size = half_a.shape[0]
        lo, hi = pl.ds(0, size), pl.ds(size, size)
        place = {"x": at.x, "z": at.z}[axis]
        here, above, across, below = (part_of(lax.rem(place + k, 4)) for k in range(4))
        upper, lower = at.along(axis, 1), at.along(axis, 3)
        self.plan = [
            (across.at[lo], half_a, upper),
            (across.at[hi], half_b, lower),
            (above.at[hi], up.at[hi], upper),
            (below.at[lo], down.at[lo], lower),
            (to_up, up.at[lo], upper),
            (to_down, down.at[hi], lower),
        ]
        pieces = [(above.at[lo], to_up), (below.at[hi], to_down), (here, own)]
        self.arrived = arrived is not None
        if self.arrived:
            done, last = pl.ds(0, STEPS - 1), pl.ds(STEPS - 1, 1)
            for i, here_from in enumerate(arrived):
                src, dst, device = self.plan[i]
                pieces.append((here_from, dst.at[:, :, done]))
                self.plan[i] = (src.at[:, :, last], dst.at[:, :, last], device)
        self.loads = [
            pltpu.make_async_copy(src, dst, load.at[first + i])
            for i, (src, dst) in enumerate(pieces)
        ]

    def copy(self, i):
        src, dst, device = self.plan[i]
        return remote(src, dst, self.send, self.recv, self.base + i, device)

    def begin(self):
        for i in range(2):
            self.copy(i).start()
        for load in self.loads:
            load.start()

    def direct(self):
        for i in (2, 3):
            self.copy(i).start()

    def landed(self, i):
        if self.arrived and i < 4:
            self.loads[3 + i].wait()
        self.copy(i).wait_recv()

    def middle(self):
        for i, (total, landed) in enumerate(
            ((self.to_up, self.half_a), (self.to_down, self.half_b))
        ):
            self.loads[i].wait()
            self.landed(i)

            def add(i, carry, total=total, landed=landed):
                total[i] = (total[i].astype(F32) + landed[i].astype(F32)).astype(BF)
                return carry

            lax.fori_loop(0, total.shape[0], add, 0)
            self.copy(4 + i).start()

    def finish(self, out):
        self.loads[2].wait()
        for i in range(2, 6):
            self.landed(i)

        def add(i, carry):
            total = self.own[i].astype(F32) + self.up[i].astype(F32)
            out[i] = (total + self.down[i].astype(F32)).astype(out.dtype)
            return carry

        lax.fori_loop(0, out.shape[0], add, 0)
        for i in range(6):
            self.copy(i).wait_send()


def sum_scratch(block):
    half, whole = pltpu.VMEM((block[0] // 2, *block[1:]), BF), pltpu.VMEM(block, BF)
    return [half, half, whole, whole, half, half, whole]


def startup_kernel(
    hidden, segment_rows, query, key, value, output, router, gains, gate, up, down,
    hidden_all, segment_all, small_all, share_a, share_b, small, segment, send, recv, here,
):
    at = Place()
    greet(
        [
            at.sibling(), at.partner(), at.diagonal(), at.opposite(),
            at.along("x", 1), at.along("x", 3), at.along("z", 1), at.along("z", 3),
        ]
    )
    small[:, 0:256] = query[...]
    small[:, 256:384] = key[...]
    small[:, 384:512] = value[...]
    small[:, 512:768] = output[...]
    columns = jnp.broadcast_to(gains[...].astype(F32)[:, None, :], (2, 8, 32))
    columns = [columns[i].T[:, 0:1].astype(BF) for i in range(2)]
    blank = jnp.zeros((32, 94), BF)
    small[:, 768:896] = jnp.concatenate([router[...], *columns, blank], axis=1)
    segment[0:2, :] = segment_rows[...]
    segment[2:8, :] = jnp.zeros((6, 128), jnp.int32)
    rank = at.yl * 2 + at.core
    mine = small_all.at[(at.x * 4 + at.z) * 2 + at.yh]
    small_kept = keep(small, mine, here.at[0])
    copies = [push(small, mine, send, recv, 0, at.opposite())]
    swaps, swaps_kept = [], []
    base = 13 + 2 * PIECES
    for i, share in enumerate((gate, up, down)):
        for j, out in enumerate((share_a, share_b)):
            dst, two = out.at[at.yh, :, i], pl.ds(2 * j, 2)
            theirs = share.at[pl.ds((1 - at.yh) * STEPS, STEPS), two]
            index = 2 * i + j
            swaps.append(push(theirs, dst, send, recv, base + index, at.opposite()))
            own = share.at[pl.ds(at.yh * STEPS, STEPS), two]
            swaps_kept.append(keep(own, dst, here.at[3 + index]))
    copies.extend(
        push(segment, segment_all.at[rank], send, recv, 1 + i, device)
        for i, device in enumerate((at.sibling(), at.partner(), at.diagonal()))
    )
    pair = PairGather(at, hidden, hidden_all, send, recv, here.at[1], 12, PIECES)
    seg_here = keep(segment, segment_all.at[rank], here.at[2])
    over_z = AxisGather(
        at, "z",
        lambda k, part: halves_of(small_all, (at.x * 4 + lax.rem(at.z + k, 4)) * 2, 2)(part),
        send, recv, 4,
    )
    over_x = AxisGather(
        at, "x", lambda k, part: halves_of(small_all, lax.rem(at.x + k, 4) * 8, 8)(part),
        send, recv, 8,
    )
    small_kept.wait()
    copies[0].wait_recv()
    over_z.begin()
    over_z.forward()
    over_z.finish()
    over_x.begin()
    pair.forward()
    for swap, own in zip(swaps, swaps_kept):
        swap.wait_recv()
        own.wait()
    over_x.forward()
    pair.finish()
    seg_here.wait()
    for copy in copies[1:]:
        copy.wait_recv()
    over_x.finish()
    for copy in (*copies, *swaps):
        copy.wait_send()


def startup(hidden, segment, smalls, shares, ident):
    hbm = pl.BlockSpec(memory_space=pl.ANY)
    vmem = pl.BlockSpec(memory_space=pltpu.VMEM)
    sems = 13 + 2 * PIECES + 6
    shares = [share.reshape(2 * STEPS, QUAD, 32, FF) for share in shares]
    hidden_all, segment_all, small_all, share_a, share_b = pl.pallas_call(
        startup_kernel,
        in_specs=[vmem] * 8 + [hbm] * 3,
        out_specs=[hbm] * 3 + [vmem] * 2,
        out_shape=[
            jax.ShapeDtypeStruct((4, *hidden.shape), hidden.dtype),
            jax.ShapeDtypeStruct((4, 8, 128), segment.dtype),
            jax.ShapeDtypeStruct((32, 32, SMALL), BF),
            SHARE_SHAPE,
            SHARE_SHAPE,
        ],
        scratch_shapes=[
            pltpu.VMEM((32, SMALL), BF),
            pltpu.VMEM((8, 128), jnp.int32),
            pltpu.SemaphoreType.DMA((sems,)),
            pltpu.SemaphoreType.DMA((sems,)),
            pltpu.SemaphoreType.DMA((9,)),
        ],
        compiler_params=pltpu.CompilerParams(collective_id=ident, has_side_effects=True),
        name="startup",
    )(hidden, segment, *smalls, *shares)
    hidden_all, small_all = hidden_all.reshape(SEQ, D), small_all.reshape(D, SMALL)
    return hidden_all, segment_all, small_all, share_a, share_b


SPLIT = 384


class RingScatter:
    def __init__(self, at, part, scratch, send, recv, base=0):
        self.at, self.part, self.send, self.recv, self.base = at, part, send, recv, base
        near, half_a, half_b, self.full_up, self.full_down = scratch[:5]
        to_far, to_up, to_down = scratch[5:] or [
            part.at[at.chip(k) * 2 + at.core] for k in (2, 1, 3)
        ]
        self.near, self.half_a, self.half_b = near, half_a, half_b
        self.to_far, self.to_up, self.to_down = to_far, to_up, to_down
        self.half = half_a.shape[0]
        self.lo, self.hi = pl.ds(0, self.half), pl.ds(self.half, self.half)
        up, down = at.ring(1), at.ring(3)
        self.plan = {
            k: (part.at[at.chip(k) * 2 + 1 - at.core], near.at[k], at.sibling()) for k in range(4)
        }
        self.plan[4] = (to_far.at[self.lo], half_a, up)
        self.plan[5] = (to_far.at[self.hi], half_b, down)
        self.plan[6] = (to_up, self.full_up, up)
        self.plan[7] = (to_down, self.full_down, down)

    def copy(self, i):
        src, dst, device = self.plan[i]
        return remote(src, dst, self.send, self.recv, self.base + i, device)

    def chip_sum(self, k):
        self.copy(k).wait_recv()
        own = self.part[self.at.chip(k) * 2 + self.at.core]
        return own.astype(F32) + self.near[k].astype(F32)

    def far(self):
        self.to_far[...] = self.chip_sum(2).astype(BF)
        self.copy(4).start()
        self.copy(5).start()

    def up_side(self):
        total = self.chip_sum(1)
        self.copy(4).wait_recv()
        self.to_up[self.lo, :] = (total[: self.half] + self.half_a[...].astype(F32)).astype(BF)
        self.to_up[self.hi, :] = total[self.half :].astype(BF)
        self.copy(6).start()

    def down_side(self):
        total = self.chip_sum(3)
        self.copy(5).wait_recv()
        self.to_down[self.lo, :] = total[: self.half].astype(BF)
        self.to_down[self.hi, :] = (total[self.half :] + self.half_b[...].astype(F32)).astype(BF)
        self.copy(7).start()

    def finish(self, out):
        out[...] = self.chip_sum(0)
        self.copy(6).wait_recv()
        out[...] += self.full_up[...].astype(F32)
        self.copy(7).wait_recv()
        out[...] += self.full_down[...].astype(F32)
        for i in range(8):
            self.copy(i).wait_send()


def ring_scratch(rows, columns, own_sends=True):
    block, half = pltpu.VMEM((rows, columns), BF), pltpu.VMEM((rows // 2, columns), BF)
    scratch = [pltpu.VMEM((4, rows, columns), BF), half, half, block, block]
    return scratch + [block] * 3 if own_sends else scratch


class PairScatter:
    def __init__(self, at, part, scratch, send, recv, base=0):
        self.at, self.part, self.send, self.recv, self.base = at, part, send, recv, base
        self.near, self.far_rows, self.to_far = scratch
        size = self.to_far.shape[0] // PIECES
        self.parts = [pl.ds(i * size, size) for i in range(PIECES)]
        self.other, self.own = (1 - at.yl) * 2, at.yl * 2

    def go(self, i, src, dst, device):
        return push(src, dst, self.send, self.recv, self.base + i, device)

    def begin_far(self):
        slot = self.other + 1 - self.at.core
        self.first = [
            self.go(i, self.part.at[slot, rows], self.near.at[1, rows], self.at.sibling())
            for i, rows in enumerate(self.parts)
        ]

    def begin_own(self):
        slot = self.own + 1 - self.at.core
        self.second = self.go(PIECES, self.part.at[slot], self.near.at[0], self.at.sibling())

    def forward(self):
        self.sent = []
        for i, rows in enumerate(self.parts):
            self.first[i].wait_recv()
            own = self.part[self.other + self.at.core, rows, :].astype(F32)
            self.to_far[rows, :] = (own + self.near[1, rows, :].astype(F32)).astype(BF)
            far = self.far_rows.at[rows]
            self.sent.append(self.go(PIECES + 1 + i, self.to_far.at[rows], far, self.at.partner()))

    def finish(self, out):
        self.second.wait_recv()
        out[...] = self.part[self.own + self.at.core].astype(F32) + self.near[0].astype(F32)
        for i, rows in enumerate(self.parts):
            self.sent[i].wait_recv()
            out[rows, :] += self.far_rows[rows, :].astype(F32)
        for copy in (*self.first, self.second, *self.sent):
            copy.wait_send()


def pair_scratch(rows, columns):
    block = pltpu.VMEM((rows, columns), BF)
    return [pltpu.VMEM((2, rows, columns), BF), block, block]


SPLIT = 384


def rotary_tables():
    half = HD // 2
    inverse = (10000.0 ** (-(np.arange(half, dtype=np.float64) * 2.0) / HD)).astype(np.float32)
    angles = np.arange(SEQ, dtype=np.float32)[:, None] * inverse[None, :]
    cosine, sine = np.cos(angles), np.sin(angles)
    wide_cosine = np.concatenate([cosine] * 4, axis=1)
    wide_sine = np.concatenate([-sine, sine] * 2, axis=1)
    return wide_cosine.astype(np.float32), wide_sine.astype(np.float32)


def swapped(values):
    lane = lax.broadcasted_iota(jnp.int32, values.shape, 1)
    low = (lane % HD) < HD // 2
    return jnp.where(low, pltpu.roll(values, 96, 1), pltpu.roll(values, 32, 1))


def rotated(values, cosine, sine):
    return values * cosine + swapped(values) * sine


def bias_block(key_segment, query_segment, first, rows):
    key_at = lax.broadcasted_iota(jnp.int32, (rows, BLOCK), 0)
    query_at = lax.broadcasted_iota(jnp.int32, (rows, BLOCK), 1) + first
    allowed = (key_segment == query_segment) & (key_at <= query_at)
    return jnp.where(allowed, 0.0, MASKED)


def segment_row(segments):
    return jnp.concatenate(
        [segments[rank, i : i + 1, :] for rank in range(4) for i in range(2)], axis=1
    ).astype(F32)


def gain_rows(small):
    return small[:, 768:896].astype(F32).T[32:40, :]


def column_of(row):
    return jnp.broadcast_to(row, (8, row.shape[1])).T[:, 0:1]


def front_kernel(
    hidden, weights, cosine, sine, segments, own_hidden, ids, out_grad, share_a, share_b,
    normed, query, key, value, context_t, log_total, middle, normed_moe, gating,
    over_z, over_x, quad_a, quad_b, out_grad_all, bias, part, context, through, *refs,
):
    pair_refs = refs[:3]
    send, recv, here = refs[3:]
    at = Place()
    greet(
        [
            at.sibling(), at.partner(), at.ring(1), at.ring(3),
            at.along("x", 1), at.along("x", 3), at.along("z", 1), at.along("z", 3),
        ]
    )
    ring = RingGather(at, out_grad, out_grad_all, send, recv, here.at[0], 0)
    lines = first_gather(
        at, share_a, share_b, over_z, over_x, send, recv, here.at[pl.ds(1, 4)], 9
    )
    quad = second_gather(
        at, 0, over_z, over_x, quad_a, quad_b, send, recv, here.at[pl.ds(5, 4)],
        9 + SpreadOut.COPIES, through,
    )
    scatter = PairScatter(at, part, pair_refs, send, recv, 9 + 2 * SpreadOut.COPIES)
    lines.begin()
    ring.begin()

    gains = gain_rows(weights)
    seg_row = segment_row(segments)
    seg_column = column_of(seg_row)
    for block in range(SEQ // BLOCK):
        rows = slice(block * BLOCK, (block + 1) * BLOCK)
        values = hidden[rows, :].astype(F32)
        scale = lax.rsqrt(jnp.mean(values * values, axis=-1, keepdims=True) + EPS)
        normed[rows, :] = (values * scale * gains[0:1, :]).astype(BF)
    for half in range(2):
        columns = slice(half * 128, half * 128 + 128)
        pre = mm(normed[...], weights[:, columns])
        query[:, columns] = (rotated(pre, cosine[...], sine[...]) * 0.125).astype(BF)
    key_pre = mm(normed[...], weights[:, 256:384])
    key[...] = rotated(key_pre, cosine[...], sine[...]).astype(BF)
    value_pre = mm(normed[...], weights[:, 384:512])
    value[...] = value_pre.astype(BF)
    value_t = value_pre.T.astype(BF)
    lines.forward()
    for block in range(SEQ // BLOCK):
        first, end = block * BLOCK, (block + 1) * BLOCK
        bias[:end, :] = bias_block(seg_column[:end, :], seg_row[:, first:end], first, end)
        for head in range(HEADS):
            kv = slice((head // 2) * HD, (head // 2) * HD + HD)
            own = slice(head * HD, head * HD + HD)
            scores = mm_last(key[:end, kv], query[first:end, own]) + bias[:end, :]
            top = jnp.max(scores, axis=0, keepdims=True)
            powers = jnp.exp(scores - top)
            total = jnp.sum(powers, axis=0, keepdims=True)
            share = (powers * (1.0 / total)).astype(BF)
            context_t[own, first:end] = mm(value_t[kv, :end], share).astype(BF)
            log_total[head : head + 1, first:end] = top + jnp.log(total)
        if block == 2:
            ring.forward_before()
            ring.forward_behind()
    lines.finish()
    quad.begin()
    context[...] = context_t[...].T

    def project(slot):
        rows = pl.ds(pl.multiple_of(slot * LOCAL, LOCAL), LOCAL)
        part[slot] = mm_last(context[rows, :], weights[:, 512:768]).astype(BF)

    project(scatter.other + 1 - at.core)
    scatter.begin_far()
    project(scatter.other + at.core)
    project(scatter.own + 1 - at.core)
    scatter.begin_own()
    project(scatter.own + at.core)
    scatter.forward()
    quad.forward()
    ring.forward_across()
    scatter.finish(middle)
    values = middle[...] + own_hidden[...].astype(F32)
    middle[...] = values
    scale = lax.rsqrt(jnp.mean(values * values, axis=-1, keepdims=True) + EPS)
    normed_moe[...] = (values * scale * gains[1:2, :]).astype(BF)
    lane = lax.broadcasted_iota(jnp.int32, (LOCAL, 128), 1)
    chosen = lane == ids[:, 0:1]
    for i in range(1, TOPK):
        chosen = chosen | (lane == ids[:, i : i + 1])
    logits = jnp.where(chosen, mm(normed_moe[...], weights[:, 768:896]), MASKED)
    powers = jnp.where(chosen, jnp.exp(logits - jnp.max(logits, axis=-1, keepdims=True)), 0.0)
    gating[...] = powers / jnp.sum(powers, axis=-1, keepdims=True)
    for i in (0, 4, 6, 7, 8):
        ring.copy(i).wait_recv()
    ring.sent()
    ring.kept().wait()
    quad.finish()


def front(hidden, weights, tables, segments, own_hidden, ids, out_grad, shares, ident):
    vmem = pl.BlockSpec(memory_space=pltpu.VMEM)
    hbm = pl.BlockSpec(memory_space=pl.ANY)
    sems = 9 + 2 * SpreadOut.COPIES + 1 + 2 * PIECES
    return pl.pallas_call(
        front_kernel,
        in_specs=[vmem] * 10,
        out_specs=[vmem] * 9 + [hbm] * 5,
        out_shape=[
            jax.ShapeDtypeStruct((SEQ, D), BF),
            jax.ShapeDtypeStruct((SEQ, HEADS * HD), BF),
            jax.ShapeDtypeStruct((SEQ, 128), BF),
            jax.ShapeDtypeStruct((SEQ, 128), BF),
            jax.ShapeDtypeStruct((HEADS * HD, SEQ), BF),
            jax.ShapeDtypeStruct((8, SEQ), F32),
            jax.ShapeDtypeStruct((LOCAL, D), F32),
            jax.ShapeDtypeStruct((LOCAL, D), BF),
            jax.ShapeDtypeStruct((LOCAL, 128), F32),
            *[LINE_SHAPE] * 2,
            *[QUAD_SHAPE] * 2,
            jax.ShapeDtypeStruct((8, LOCAL, D), BF),
        ],
        scratch_shapes=[
            pltpu.VMEM((SEQ, BLOCK), F32),
            pltpu.VMEM((4, LOCAL, D), BF),
            pltpu.VMEM((SEQ, HEADS * HD), BF),
            pltpu.VMEM((2, *BLOCK_SHAPE), BF),
            *pair_scratch(LOCAL, D),
            pltpu.SemaphoreType.DMA((sems,)),
            pltpu.SemaphoreType.DMA((sems,)),
            pltpu.SemaphoreType.DMA((9,)),
        ],
        compiler_params=pltpu.CompilerParams(
            collective_id=ident, has_side_effects=True, vmem_limit_bytes=56 * MIB
        ),
        name="front",
    )(hidden, weights, *tables, segments, own_hidden, ids, out_grad, *shares)


def by_owner(value):
    return value.astype(BF).reshape(4, 4, 2, 32, value.shape[1])


def back_kernel(
    dx, dgate, gating, middle, normed_moe, out_grad, y_part,
    normed, weights, cosine, sine, segments, query, key, value, context_t, log_total,
    own_weights, own_hidden, expert_a, expert_b,
    land_0, land_1, land_2, land_3, land_4, land_5, land_6, land_7,
    hidden_grad, block_out, query_grad, key_grad, value_grad, output_grad, rest, gate, up, down,
    bias, dcontext, dquery_t, dkey, dvalue, dall, dall_t, dattn_own, dattn_all, y_sum,
    grads, sum_1a, sum_1b, sum_2a, sum_2b, over_y, from_opposite, share_sum, shares,
    total_a, total_b, land_a, land_b, *refs,
):
    ring_refs, pair_refs = refs[:8], refs[8:11]
    first_refs = (refs[11:18], refs[18:25])
    groups = [refs[25 + 7 * i : 32 + 7 * i] for i in range(4)]
    landings = (refs[53:57], refs[57:61])
    send, recv, here, load = refs[61:]
    at = Place()
    greet(
        [
            at.sibling(), at.partner(), at.diagonal(), at.opposite(), at.ring(1), at.ring(3),
            at.along("x", 1), at.along("x", 3), at.along("z", 1), at.along("z", 3),
        ]
    )
    base = 9 + 2 * PIECES
    sums = [
        RingSum(
            at, "x", lambda k: expert_a.at[k], first_refs[0], send, recv, load, base, 0,
            (land_0, land_1, land_2, land_3),
        ),
        RingSum(
            at, "z", lambda k: expert_b.at[k], first_refs[1], send, recv, load,
            base + RingSum.COPIES, 7, (land_4, land_5, land_6, land_7),
        ),
    ]
    for each in sums:
        each.begin()
        each.direct()
    gain = gain_rows(weights)[1:2, :]
    chosen = gating[...]
    dchosen = chosen * (dgate[...] - jnp.sum(chosen * dgate[...], axis=-1, keepdims=True))
    dlogits = dchosen.astype(BF)
    dnormed = dx[...] + mm_last(dlogits, weights[:, 768:896])
    values = middle[...]
    scale = lax.rsqrt(jnp.mean(values * values, axis=-1, keepdims=True) + EPS)
    unit = values * scale
    weighted = dnormed * gain
    inner = jnp.mean(weighted * unit, axis=-1, keepdims=True)
    total = out_grad[...].astype(F32) + scale * (weighted - unit * inner)
    hidden_grad[...] = total
    dattn_own[...] = total.astype(BF)
    gather = PairGather(at, dattn_own, dattn_all, send, recv, here, 8, PIECES)
    scatter = RingScatter(at, y_part, ring_refs, send, recv)
    for k in (2, 1, 3, 0):
        scatter.copy(k).start()
    router_part = mm(normed_moe[...].T, dlogits)
    gain_part = column_of(jnp.sum(dnormed * unit, axis=0, keepdims=True))
    lane = lax.broadcasted_iota(jnp.int32, (D, 128), 1)
    grads[..., 768:] = by_owner(jnp.where(lane == 32, gain_part, router_part))
    seg_row = segment_row(segments)
    seg_column = column_of(seg_row)
    gather.forward()
    scatter.far()
    for each in sums:
        each.middle()
    gather.finish()
    dattn = dattn_all[...].reshape(SEQ, D)
    dcontext[...] = mm(dattn, weights[:, 512:768]).astype(BF)
    output_grad_t = mm(context_t[...], dattn)
    grads[..., 512:768] = by_owner(output_grad_t.T)
    key_t = key[...].astype(F32).T.astype(BF)
    dkey[...] = jnp.zeros_like(dkey)
    dvalue[...] = jnp.zeros_like(dvalue)
    for block in range(SEQ // BLOCK):
        first, end = block * BLOCK, (block + 1) * BLOCK
        bias[:end, :] = bias_block(seg_column[:end, :], seg_row[:, first:end], first, end)
        for head in range(HEADS):
            kv = slice((head // 2) * HD, (head // 2) * HD + HD)
            own = slice(head * HD, head * HD + HD)
            query_block = query[first:end, own]
            dcontext_block = dcontext[first:end, own]
            scores = mm_last(key[:end, kv], query_block) + bias[:end, :]
            share = jnp.exp(scores - log_total[head : head + 1, first:end])
            dshare = mm_last(value[:end, kv], dcontext_block)
            centre = jnp.sum(share * dshare, axis=0, keepdims=True)
            dscore = (share * (dshare - centre)).astype(BF)
            dquery_t[own, first:end] = mm(key_t[kv, :end], dscore) * 0.125
            dkey[:end, kv] += mm(dscore, query_block)
            dvalue[:end, kv] += mm(share.astype(BF), dcontext_block)
        if block == 0:
            scatter.up_side()
            scatter.down_side()
        if block == 2:
            last = base + 6 * RingSum.COPIES + 1 + 2 * PIECES
            final_sums = []
            for i, (each, axis, refs_of, landing) in enumerate(
                zip(sums, ("z", "x"), first_refs, landings)
            ):
                each.finish(each.own)
                to_up, to_down, own = refs_of[4].at[0, pl.ds(0, 1)], refs_of[5].at[0, pl.ds(0, 1)], refs_of[2].at[0]
                final_sums.append(
                    RingSum(
                        at, axis, lambda k, own=each.own: own.at[k], (*landing, to_up, to_down, own),
                        send, recv, load, last + RingSum.COPIES * i, 26 + 3 * i,
                    )
                )
                final_sums[i].begin()
                final_sums[i].direct()
        if block == 3:
            for each in final_sums:
                each.middle()
    turn = -sine[...]
    for half in range(2):
        rows = slice(half * 128, half * 128 + 128)
        piece = rotated(dquery_t[rows, :].T, cosine[...], turn)
        dall[:, rows] = piece.astype(BF)
        dall_t[rows, :] = piece.T.astype(BF)
    piece = rotated(dkey[...], cosine[...], turn)
    dall[:, 256:384] = piece.astype(BF)
    dall_t[256:384, :] = piece.T.astype(BF)
    dall[:, 384:512] = dvalue[...].astype(BF)
    dall_t[384:512, :] = dvalue[...].T.astype(BF)
    grads[..., 0:512] = by_owner(mm(dall_t[...], normed[...]).T)
    after = base + 2 * RingSum.COPIES
    width = grads.shape[-1]
    a, b = pl.ds(0, SPLIT), pl.ds(SPLIT, width - SPLIT)

    def ring_sum(i, axis, part_of, scratch):
        return RingSum(
            at, axis, part_of, scratch, send, recv, load, after + RingSum.COPIES * i, 14 + 3 * i
        )

    first_a = ring_sum(0, "x", lambda k: grads.at[k, :, :, :, a], groups[0])
    first_b = ring_sum(1, "z", lambda k: grads.at[:, k, :, :, b], groups[1])
    second_a = ring_sum(2, "z", lambda k: sum_1a.at[k], groups[2])
    second_b = ring_sum(3, "x", lambda k: sum_1b.at[k], groups[3])
    for each in (first_a, first_b):
        each.begin()
        each.direct()
    after = after + 4 * RingSum.COPIES
    pair = PairScatter(at, dattn_all, pair_refs, send, recv, after)
    after = after + 1 + 2 * PIECES + 2 * RingSum.COPIES

    def project(slot):
        rows = pl.ds(pl.multiple_of(slot * LOCAL, LOCAL), LOCAL)
        dattn_all[slot] = mm_last(dall[rows, :], weights[:, 0:512]).astype(BF)

    project(pair.other + 1 - at.core)
    pair.begin_far()
    project(pair.other + at.core)
    project(pair.own + 1 - at.core)
    pair.begin_own()
    project(pair.own + at.core)
    pair.forward()
    first_a.middle()
    first_b.middle()
    lands = []
    for i, (each, out, land) in enumerate(
        zip(final_sums, (total_a, total_b), (land_a, land_b))
    ):
        each.finish(out)
        lands.append(push(out.at[1 - at.yh], land, send, recv, after + 1 + i, at.opposite()))
    scatter.finish(y_sum)
    block_out[...] = (y_sum[...] + middle[...]).astype(BF)

    first_a.finish(sum_1a)
    second_a.begin()
    second_a.direct()
    first_b.finish(sum_1b)
    second_b.begin()
    second_b.direct()
    second_a.middle()
    second_b.middle()
    second_a.finish(sum_2a)
    second_b.finish(sum_2b)
    over_y[:, a] = sum_2a[...].reshape(64, SPLIT)
    over_y[:, b] = sum_2b[...].reshape(64, width - SPLIT)
    theirs = pl.ds(pl.multiple_of((1 - at.yh) * 32, 32), 32)
    own = pl.ds(pl.multiple_of(at.yh * 32, 32), 32)
    swap = push(over_y.at[theirs], from_opposite, send, recv, after, at.opposite())
    dn1 = y_sum
    pair.finish(dn1)
    hidden = own_hidden[...].astype(F32)
    scale = lax.rsqrt(jnp.mean(hidden * hidden, axis=-1, keepdims=True) + EPS)
    unit = hidden * scale
    weighted = dn1[...] * gain_rows(weights)[0:1, :]
    inner = jnp.mean(weighted * unit, axis=-1, keepdims=True)
    hidden_grad[...] += scale * (weighted - unit * inner)
    swap.wait_recv()
    total = over_y[own, :].astype(F32) + from_opposite[...].astype(F32)
    query_grad[...] = total[:, :256]
    key_grad[...] = total[:, 256:384]
    value_grad[...] = total[:, 384:512]
    output_grad[...] = total[:, 512:768]
    gain_part = jnp.sum(total[:, :512] * own_weights[...].astype(F32), axis=1, keepdims=True)
    lane = lax.broadcasted_iota(jnp.int32, (32, 128), 1)
    share_sum[...] = jnp.where(lane == 33, gain_part, total[:, 768:])
    copies = [
        push(share_sum, shares.at[i], send, recv, after + 3 + i, device)
        for i, device in enumerate((at.sibling(), at.partner(), at.diagonal()))
    ]
    mine, theirs = pl.ds(at.yh * STEPS, STEPS), pl.ds((1 - at.yh) * STEPS, STEPS)
    for j, value in enumerate((total_a, total_b)):
        for i, out in enumerate((gate, up, down)):
            out[mine, 2 * j : 2 * j + 2] = value[at.yh, :, i].astype(F32)
    rest[...] = share_sum[...]
    for i, copy in enumerate(copies):
        copy.wait_recv()
        rest[...] += shares[i]
    for j, (copy, land) in enumerate(zip(lands, (land_a, land_b))):
        copy.wait_recv()
        for i, out in enumerate((gate, up, down)):
            out[theirs, 2 * j : 2 * j + 2] = land[:, i].astype(F32)
    for copy in (swap, *copies, *lands):
        copy.wait_send()


def back(
    dx, dgate, gating, middle, normed_moe, out_grad, y_part,
    normed, weights, tables, segments, kept, own_weights, own_hidden, expert_grads, ident,
):
    vmem = pl.BlockSpec(memory_space=pltpu.VMEM)
    hbm = pl.BlockSpec(memory_space=pl.ANY)
    sems = 2 * (9 + 2 * PIECES) + 8 * RingSum.COPIES + 6
    block = SUMS_SHAPE.shape[1:]
    half = (block[0] // 2, *block[1:])
    first_a, first_b = (4, 2, 32, SPLIT), (4, 2, 32, SMALL - SPLIT)
    landing = [pltpu.VMEM(half, BF)] * 2 + [pltpu.VMEM(block, BF)] * 2
    return pl.pallas_call(
        back_kernel,
        in_specs=[vmem] * 19 + [hbm] * 10,
        out_specs=[vmem] * 10,
        out_shape=[
            jax.ShapeDtypeStruct((LOCAL, D), F32),
            jax.ShapeDtypeStruct((LOCAL, D), BF),
            *[jax.ShapeDtypeStruct((32, columns), F32) for columns in (256, 128, 128, 256)],
            jax.ShapeDtypeStruct((32, 128), F32),
            *[jax.ShapeDtypeStruct((2 * STEPS, QUAD, 32, FF), F32)] * 3,
        ],
        scratch_shapes=[
            pltpu.VMEM((SEQ, BLOCK), F32),
            pltpu.VMEM((SEQ, HEADS * HD), BF),
            pltpu.VMEM((HEADS * HD, SEQ), F32),
            pltpu.VMEM((SEQ, 128), F32),
            pltpu.VMEM((SEQ, 128), F32),
            pltpu.VMEM((SEQ, 512), BF),
            pltpu.VMEM((512, SEQ), BF),
            pltpu.VMEM((LOCAL, D), BF),
            pltpu.VMEM((4, LOCAL, D), BF),
            pltpu.VMEM((LOCAL, D), F32),
            pltpu.VMEM((4, 4, 2, 32, SMALL), BF),
            pltpu.VMEM(first_a, BF),
            pltpu.VMEM(first_b, BF),
            pltpu.VMEM(first_a[1:], BF),
            pltpu.VMEM(first_b[1:], BF),
            pltpu.VMEM((64, SMALL), BF),
            pltpu.VMEM((32, SMALL), BF),
            pltpu.VMEM((32, 128), F32),
            pltpu.VMEM((3, 32, 128), F32),
            *[pltpu.VMEM(block, BF)] * 2,
            *[pltpu.VMEM(block[1:], BF)] * 2,
            *ring_scratch(LOCAL, D),
            *pair_scratch(LOCAL, D),
            *sum_scratch(SUMS_SHAPE.shape),
            *sum_scratch(SUMS_SHAPE.shape),
            *sum_scratch(first_a),
            *sum_scratch(first_b),
            *sum_scratch(first_a[1:]),
            *sum_scratch(first_b[1:]),
            *landing,
            *landing,
            pltpu.SemaphoreType.DMA((sems,)),
            pltpu.SemaphoreType.DMA((sems,)),
            pltpu.SemaphoreType.DMA,
            pltpu.SemaphoreType.DMA((32,)),
        ],
        compiler_params=pltpu.CompilerParams(
            collective_id=ident, has_side_effects=True, vmem_limit_bytes=63 * MIB
        ),
        name="back",
    )(
        dx, dgate, gating, middle, normed_moe, out_grad, y_part,
        normed, weights, *tables, segments, *kept, own_weights, own_hidden, *expert_grads,
    )


def experts_kernel(
    x_in, gate_in, d_in, over_z, over_x, quad_0a, quad_0b, y_out, dx_out, dgate_out,
    all_a, all_b, land_0, land_1, land_2, land_3, land_4, land_5, land_6, land_7,
    quad_1a, quad_1b, quad_2a, quad_2b, quad_3a, quad_3b,
    x, d, xt, dt, y, dx, gating, dgate, dgate_part, hidden, w, *refs,
):
    dx_scratch, dgate_scratch = refs[:5], refs[5:10]
    send, recv, here, load, store, fetch = refs[10:16]
    at = Place()
    step = pl.program_id(0)
    opening, closing = step == 0, step == STEPS - 1
    rows_at_once = 2 * LOCAL
    lane = lax.broadcasted_iota(jnp.int32, (LOCAL, 128), 1)
    own_first = at.yh * 16 + step * QUAD
    x_gather = RingGather(at, x_in, x, send, recv, here.at[0], 0)
    gate_gather = RingGather(at, gate_in, gating, send, recv, here.at[1], 9)
    gathers = (x_gather, gate_gather)
    scatters = (
        RingScatter(at, d, dx_scratch, send, recv, 18),
        RingScatter(at, dgate_part, dgate_scratch, send, recv, 26),
    )

    later = ((quad_1a, quad_1b), (quad_2a, quad_2b), (quad_3a, quad_3b))
    quads = [
        second_gather(
            at, 1 + i, over_z, over_x, *quad, *refs[16:18], refs[18].at[pl.ds(4 * i, 4)],
            SpreadOut.COPIES * i, refs[19],
        )
        for i, quad in enumerate(later)
    ]

    def ride(condition, what):
        for i, quad in enumerate(quads):

            @pl.when(condition & (step == i))
            def _():
                what(quad)

    grads_a, grads_b, ship_send, ship_recv, keep_sems = refs[20:]

    def shipments(number):
        lo, hi = pl.ds(0, 2), pl.ds(2, 2)
        plan = []
        for part, place, axis, lands in (
            (grads_a, at.x, "x", (land_0, land_1, land_2, land_3)),
            (grads_b, at.z, "z", (land_4, land_5, land_6, land_7)),
        ):
            above, across, below = (part.at[lax.rem(place + k, 4)] for k in (1, 2, 3))
            upper, lower = at.along(axis, 1), at.along(axis, 3)
            plan += [
                (across.at[lo], lands[0], upper), (across.at[hi], lands[1], lower),
                (above.at[hi], lands[2], upper), (below.at[lo], lands[3], lower),
            ]
        return [
            remote(src, land.at[:, :, number], ship_send, ship_recv, 8 * number + i, device)
            for i, (src, land, device) in enumerate(plan)
        ]

    def keeps(number):
        return [
            pltpu.make_async_copy(part, out.at[:, :, :, number], keep_sems.at[i])
            for i, (part, out) in enumerate(((grads_a, all_a), (grads_b, all_b)))
        ]

    def shipped(number):
        for copy in shipments(number):
            copy.wait_send()
        for copy in keeps(number):
            copy.wait()

    def begin_shipping():
        for copy in shipments(step - 1):
            copy.start()

    def fetches(quad_a, quad_b):
        copies = []
        for g in range(3):
            for i in range(QUAD):
                columns = pl.ds((g * QUAD + i) * FF, FF)
                if i < 2:
                    parts = [(quad_a.at[:, :, :, g, i], w.at[:, :, :, :, columns])]
                else:
                    parts = [
                        (quad_b.at[:, x_at, :, g, i - 2], w.at[x_at, :, :, :, columns])
                        for x_at in range(4)
                    ]
                for part in parts:
                    copies.append(pltpu.make_async_copy(*part, fetch.at[len(copies)]))
        return copies

    def d_load(chip):
        two = pl.ds(chip * 2, 2)
        return pltpu.make_async_copy(d_in.at[two], d.at[two], load.at[chip])

    def y_store(chip):
        two = pl.ds(chip * 2, 2)
        return pltpu.make_async_copy(x.at[two], y_out.at[two], store.at[chip])

    @pl.when(opening)
    def _():
        greet(
            [
                at.sibling(), at.ring(1), at.ring(3),
                at.along("x", 1), at.along("x", 3), at.along("z", 1), at.along("z", 3),
            ]
        )
        for gather in gathers:
            gather.begin()
        for copy in fetches(quad_0a, quad_0b):
            copy.start()
        for chip in range(4):
            d_load(chip).start()

    for copy in fetches(quad_0a, quad_0b):
        copy.wait()

    ride(step < STEPS, lambda quad: quad.begin())

    def arrive(turn):
        @pl.when(turn == 0)
        def _():
            for gather in gathers:
                gather.kept().wait()
                gather.copy(0).wait_recv()

        @pl.when(turn == 1)
        def _():
            for gather in gathers:
                gather.forward_before()
                gather.forward_behind()
            for gather in gathers:
                gather.copy(4).wait_recv()

        @pl.when(turn == 2)
        def _():
            for gather in gathers:
                gather.forward_across()
            for gather in gathers:
                gather.copy(6).wait_recv()

        @pl.when(turn == 3)
        def _():
            for gather in gathers:
                gather.copy(7).wait_recv()
                gather.copy(8).wait_recv()

    def leave(turn):
        @pl.when(turn == 0)
        def _():
            for scatter in scatters:
                scatter.copy(2).start()

        @pl.when(turn == 1)
        def _():
            for scatter in scatters:
                scatter.copy(1).start()
                scatter.far()

        @pl.when(turn == 2)
        def _():
            for scatter in scatters:
                scatter.copy(3).start()
                scatter.up_side()

        @pl.when(turn == 3)
        def _():
            for scatter in scatters:
                scatter.copy(0).start()
                scatter.down_side()

    def tokens_block(turn, carry):
        inward = jnp.where(turn == 0, 0, jnp.where(turn == 1, 3, turn - 1))
        outward = jnp.where(turn == 0, 2, jnp.where(turn == 3, 0, turn * 2 - 1))
        chip = at.chip(jnp.where(closing, outward, inward))
        two = pl.ds(chip * 2, 2)
        rows = pl.ds(pl.multiple_of(chip * rows_at_once, rows_at_once), rows_at_once)

        @pl.when(opening)
        def _():
            arrive(turn)
            d_load(chip).wait()
            xt[:, rows] = x[two].reshape(rows_at_once, D).T
            dt[:, rows] = d[two].reshape(rows_at_once, D).T
            y[rows, :] = jnp.zeros((rows_at_once, D), F32)
            dx[rows, :] = jnp.zeros((rows_at_once, D), F32)
            dgate[rows, :] = jnp.zeros((rows_at_once, 128), F32)

        ride(turn == 3, lambda quad: quad.forward())
        pl.when((turn == 1) & (step > 0))(begin_shipping)
        gate_up = w[:, :, :, :, 0 : 2 * F].reshape(D, 2 * F)
        down = w[:, :, :, :, 2 * F :].reshape(D, F)
        for core in range(2):
            slot = chip * 2 + core
            part = pl.ds(pl.multiple_of(slot * LOCAL, LOCAL), LOCAL)
            both = mm(x[slot], gate_up)
            gate, up = both[:, :F], both[:, F:]
            dact = mm(d[slot], down)
            turned = pltpu.roll(gating[slot], lax.rem(128 - own_first, 128), 1)
            factor = jnp.concatenate(
                [jnp.broadcast_to(turned[:, i : i + 1], (LOCAL, FF)) for i in range(QUAD)],
                axis=1,
            )
            q = 1.0 / (1.0 + jnp.exp(-gate))
            silu = gate * q
            act = silu * up
            product = act * dact
            sums = dgate[part, :]
            for i in range(QUAD):
                own = jnp.sum(product[:, i * FF : (i + 1) * FF], axis=1, keepdims=True)
                sums = jnp.where(lane == own_first + i, own, sums)
            dgate[part, :] = sums
            dact = dact * factor
            hidden[part, 0:F] = (dact * up * (q + silu * (1.0 - q))).astype(BF)
            hidden[part, F : 2 * F] = (dact * silu).astype(BF)
            hidden[part, 2 * F :] = (act * factor).astype(BF)
        y[rows, :] += mm_last(hidden[rows, 2 * F :], down)
        dx[rows, :] += mm_last(hidden[rows, 0 : 2 * F], gate_up)

        @pl.when(closing)
        def _():
            x[two] = y[rows, :].astype(BF).reshape(2, LOCAL, D)
            d[two] = dx[rows, :].astype(BF).reshape(2, LOCAL, D)
            dgate_part[two] = dgate[rows, :].astype(BF).reshape(2, LOCAL, 128)
            y_store(chip).start()
            leave(turn)

        return carry

    lax.fori_loop(0, 4, tokens_block, 0)

    @pl.when(opening)
    def _():
        for gather in gathers:
            gather.sent()

    @pl.when(step > 0)
    def _():
        shipped(step - 1)

    def grads_block(block, carry):
        rows = pl.ds(pl.multiple_of(block * 512, 512), 512)

        def put(g, value):
            value = value.astype(BF).reshape(2, 4, 2, 32, value.shape[1])
            for j in range(value.shape[-1] // FF):
                piece = value[..., j * FF : (j + 1) * FF]
                group, i = g + j // QUAD, j % QUAD
                for x_at in range(2):
                    if i < 2:
                        grads_a[block * 2 + x_at, :, :, group, i] = piece[x_at]
                    else:
                        grads_b[:, block * 2 + x_at, :, group, i - 2] = piece[x_at]

        ride(block == 1, lambda quad: quad.finish())
        for number, quad in enumerate(later):

            @pl.when((block == 1) & (step == number))
            def _():
                for copy in fetches(*quad):
                    copy.start()

        put(0, mm(xt[rows, :], hidden[:, 0 : 2 * F]))
        put(2, mm(dt[rows, :], hidden[:, 2 * F :]))
        return carry

    lax.fori_loop(0, D // 512, grads_block, 0)
    for copy in keeps(step):
        copy.start()

    @pl.when(closing)
    def _():
        scatters[0].finish(dx_out)
        scatters[1].finish(dgate_out)
        for chip in range(4):
            y_store(chip).wait()
        for copy in keeps(step):
            copy.wait()
        for number in range(STEPS - 1):
            for copy in shipments(number):
                copy.wait_recv()


def experts(x, gating, d, lines, quad, ident):
    hbm = pl.BlockSpec(memory_space=pl.ANY)

    def whole(rows, columns):
        return pl.BlockSpec((rows, columns), lambda step: (0, 0), pipeline_mode=pl.Buffered(1))

    return pl.pallas_call(
        experts_kernel,
        grid=(STEPS,),
        in_specs=[hbm] * 7,
        out_specs=[
            hbm,
            whole(LOCAL, D),
            whole(LOCAL, 128),
            *[hbm] * 10,
            *[hbm] * 6,
        ],
        out_shape=[
            jax.ShapeDtypeStruct((8, LOCAL, D), BF),
            jax.ShapeDtypeStruct((LOCAL, D), F32),
            jax.ShapeDtypeStruct((LOCAL, 128), F32),
            *[GRADS_SHAPE] * 2,
            *[LAND_SHAPE] * 8,
            *[QUAD_SHAPE] * 6,
        ],
        scratch_shapes=[
            pltpu.VMEM((8, LOCAL, D), BF),
            pltpu.VMEM((8, LOCAL, D), BF),
            pltpu.VMEM((D, TOKENS), BF),
            pltpu.VMEM((D, TOKENS), BF),
            pltpu.VMEM((TOKENS, D), F32),
            pltpu.VMEM((TOKENS, D), F32),
            pltpu.VMEM((8, LOCAL, 128), F32),
            pltpu.VMEM((TOKENS, 128), F32),
            pltpu.VMEM((8, LOCAL, 128), BF),
            pltpu.VMEM((TOKENS, 3 * F), BF),
            pltpu.VMEM((4, 4, 2, 32, 3 * F), BF),
            *ring_scratch(LOCAL, D, False),
            *ring_scratch(LOCAL, 128, False),
            pltpu.SemaphoreType.DMA((34,)),
            pltpu.SemaphoreType.DMA((34,)),
            pltpu.SemaphoreType.DMA((2,)),
            pltpu.SemaphoreType.DMA((4,)),
            pltpu.SemaphoreType.DMA((4,)),
            pltpu.SemaphoreType.DMA((30,)),
            pltpu.SemaphoreType.DMA((3 * SpreadOut.COPIES,)),
            pltpu.SemaphoreType.DMA((3 * SpreadOut.COPIES,)),
            pltpu.SemaphoreType.DMA((12,)),
            pltpu.VMEM((2, *BLOCK_SHAPE), BF),
            *[pltpu.VMEM((4, 4, 2, 3, 2, 32, FF), BF)] * 2,
            pltpu.SemaphoreType.DMA((8 * STEPS - 8,)),
            pltpu.SemaphoreType.DMA((8 * STEPS - 8,)),
            pltpu.SemaphoreType.DMA((2,)),
        ],
        compiler_params=pltpu.CompilerParams(
            collective_id=ident, has_side_effects=True, vmem_limit_bytes=63 * MIB
        ),
        name="experts",
    )(x, gating, d, *lines, *quad)[:13]


def on_device(
    hidden_in, out_grad, attn_gain, query_weight, key_weight, value_weight, output_weight,
    moe_gain, router_weight, expert_gate, expert_up, expert_down, expert_ids, segment_ids,
):
    gains = jnp.stack([attn_gain, moe_gain])
    smalls = (query_weight, key_weight, value_weight, output_weight, router_weight, gains)
    own_shares = (expert_gate, expert_up, expert_down)
    hidden_all, segments, small, *shares = startup(
        hidden_in, segment_ids.reshape(2, 128), smalls, own_shares, 0
    )
    tables = tuple(jnp.asarray(t) for t in rotary_tables())
    normed, *more, d = front(
        hidden_all, small, tables, segments, hidden_in, expert_ids, out_grad, shares, 1
    )
    kept, (middle, normed_moe, gating), lines, quad = more[:5], more[5:8], more[8:10], more[10:]
    y, dx, dgate, *expert_grads = experts(normed_moe, gating, d, lines, quad, 3)
    own_weights = jnp.concatenate([query_weight, key_weight, value_weight], axis=1)
    hidden_grad, block_out, *attention_grads, rest, gate, up, down = back(
        dx, dgate, gating, middle, normed_moe, out_grad, y,
        normed, small, tables, segments, kept, own_weights, hidden_in, expert_grads, 5,
    )
    expert_grads = [share.reshape(E, 32, FF) for share in (gate, up, down)]
    return (
        block_out,
        hidden_grad,
        rest[:, 33] / attn_gain.astype(F32),
        *attention_grads,
        rest[:, 32],
        rest[:, :32],
        *expert_grads,
    )


def solution(mesh):
    fine = Mesh(np.asarray(mesh.devices).reshape(4, 4, 2, 2, 2), ALL)
    return jax.shard_map(
        on_device,
        mesh=fine,
        in_specs=(
            P(ALL, None),
            P(ALL, None),
            P(DP),
            P(DP, TENSOR),
            P(DP, TENSOR),
            P(DP, TENSOR),
            P(DP, TENSOR),
            P(DP),
            P(DP, None),
            P(None, DP, TENSOR),
            P(None, DP, TENSOR),
            P(None, DP, TENSOR),
            P(ALL, None),
            P(ALL),
        ),
        out_specs=(
            P(ALL, None),
            P(ALL, None),
            P(DP),
            P(DP, TENSOR),
            P(DP, TENSOR),
            P(DP, TENSOR),
            P(DP, TENSOR),
            P(DP),
            P(DP, None),
            P(None, DP, TENSOR),
            P(None, DP, TENSOR),
            P(None, DP, TENSOR),
        ),
        check_vma=False,
    )
```

```python
import jax
import jax.numpy as jnp
import numpy as np
from jax import lax
from jax.experimental import pallas as pl
from jax.experimental.pallas import tpu as pltpu
from jax.sharding import Mesh
from jax.sharding import PartitionSpec as P

D = 1024
HD = 64
E = 32
SEQ = 1024
LOCAL = 256
HEADS = 4
QUAD = 4
FF = 128
F = QUAD * FF
EPS = 1e-06
TOPK = 8
MASKED = -1e30
BLOCK = 256
TOKENS = 2048
STEPS = 4

DP = ("x", "z", "yh")
TENSOR = ("yl", "core")
RING = ("yh", "yl", "core")
PLANE = ("x", "z")
ALL = ("x", "z", "yh", "yl", "core")

F32 = jnp.float32
BF = jnp.bfloat16
LAST = (((1,), (1,)), ((), ()))
MIB = 1024 * 1024
MESH = pl.DeviceIdType.MESH
SMALL = 896


def mm(a, b):
    return jnp.dot(a, b, preferred_element_type=F32)


def mm_last(a, b):
    return lax.dot_general(a, b, LAST, preferred_element_type=F32)


class Place:
    def __init__(self):
        self.x = lax.axis_index("x")
        self.z = lax.axis_index("z")
        self.yh = lax.axis_index("yh")
        self.yl = lax.axis_index("yl")
        self.core = lax.axis_index("core")
        self.y = self.yh * 2 + self.yl

    def chip(self, k):
        return lax.rem(self.y + k, 4)

    def ring(self, k):
        chip = self.chip(k)
        return {"yh": chip // 2, "yl": lax.rem(chip, 2)}

    def along(self, axis, k):
        return {axis: lax.rem(getattr(self, axis) + k, 4)}

    def sibling(self):
        return {"core": 1 - self.core}

    def partner(self):
        return {"yl": 1 - self.yl}

    def diagonal(self):
        return {"yl": 1 - self.yl, "core": 1 - self.core}

    def opposite(self):
        return {"yh": 1 - self.yh}


def greet(devices):
    barrier = pltpu.get_barrier_semaphore()
    for device in devices:
        pl.semaphore_signal(barrier, inc=1, device_id=device, device_id_type=MESH)
    pl.semaphore_wait(barrier, len(devices))


def remote(src, dst, send, recv, i, device):
    return pltpu.make_async_remote_copy(
        src_ref=src, dst_ref=dst, send_sem=send.at[i], recv_sem=recv.at[i],
        device_id=device, device_id_type=MESH,
    )


def push(src, dst, send, recv, i, device):
    copy = remote(src, dst, send, recv, i, device)
    copy.start()
    return copy


def keep(src, dst, sem):
    copy = pltpu.make_async_copy(src, dst, sem)
    copy.start()
    return copy


class RingGather:
    def __init__(self, at, own, out, send, recv, here, base=0):
        self.at, self.own, self.out, self.base = at, own, out, base
        self.send, self.recv, self.here = send, recv, here
        half = own.shape[0] // 2
        lo, hi = pl.ds(0, half), pl.ds(half, half)
        me, before, behind, across = (out.at[self.slot(k)] for k in (0, 3, 1, 2))
        near, up, down = at.sibling(), at.ring(1), at.ring(3)
        self.plan = [
            (own, me, near),
            (own, me, up),
            (own, me, down),
            (before.at[lo], before.at[lo], up),
            (before, before, near),
            (behind.at[hi], behind.at[hi], down),
            (behind, behind, near),
            (across.at[lo], across.at[lo], near),
            (across.at[hi], across.at[hi], near),
        ]

    def slot(self, k):
        return self.at.chip(k) * 2 + self.at.core

    def copy(self, i):
        src, dst, device = self.plan[i]
        return remote(src, dst, self.send, self.recv, self.base + i, device)

    def kept(self):
        return pltpu.make_async_copy(self.own, self.out.at[self.slot(0)], self.here)

    def begin(self):
        self.kept().start()
        for i in (1, 2, 0):
            self.copy(i).start()

    def forward_before(self):
        self.copy(1).wait_recv()
        self.copy(3).start()
        self.copy(4).start()

    def forward_behind(self):
        self.copy(2).wait_recv()
        self.copy(5).start()
        self.copy(6).start()

    def forward_across(self):
        self.copy(3).wait_recv()
        self.copy(7).start()
        self.copy(5).wait_recv()
        self.copy(8).start()

    def sent(self):
        for i in range(9):
            self.copy(i).wait_send()


class PairGather:
    def __init__(self, at, own, out, send, recv, here, base, pieces):
        self.at, self.out, self.send, self.recv, self.base = at, out, send, recv, base
        size = own.shape[0] // pieces
        self.parts = [pl.ds(i * size, size) for i in range(pieces)]
        me = at.yl * 2 + at.core
        self.other = (1 - at.yl) * 2 + at.core
        self.kept = keep(own, out.at[me], here)
        self.far = [
            push(own.at[part], out.at[me, part], send, recv, base + 1 + i, at.partner())
            for i, part in enumerate(self.parts)
        ]
        self.near = [push(own, out.at[me], send, recv, base, at.sibling())]

    def forward(self):
        for i, part in enumerate(self.parts):
            self.far[i].wait_recv()
            view = self.out.at[self.other, part]
            index = self.base + 1 + len(self.parts) + i
            self.near.append(push(view, view, self.send, self.recv, index, self.at.sibling()))

    def finish(self):
        for copy in self.near:
            copy.wait_recv()
        for copy in (*self.far, *self.near):
            copy.wait_send()
        self.kept.wait()


PIECES = 4


class AxisGather:
    def __init__(self, at, axis, view, send, recv, base):
        self.up, self.down = at.along(axis, 1), at.along(axis, 3)
        self.view, self.send, self.recv, self.base = view, send, recv, base

    def go(self, i, view, device):
        return push(view, view, self.send, self.recv, self.base + i, device)

    def begin(self):
        self.first = [
            self.go(0, self.view(0, "all"), self.up), self.go(1, self.view(0, "all"), self.down),
        ]

    def forward(self):
        self.first[0].wait_recv()
        self.far = [self.go(2, self.view(3, "low"), self.up)]
        self.first[1].wait_recv()
        self.far.append(self.go(3, self.view(1, "high"), self.down))

    def finish(self):
        for copy in self.far:
            copy.wait_recv()
        for copy in (*self.first, *self.far):
            copy.wait_send()


def halves_of(ref, first, size):
    spans = {"all": (0, size), "low": (0, size // 2), "high": (size // 2, size // 2)}
    return lambda part: ref.at[pl.ds(first + spans[part][0], spans[part][1])]


class SpreadOut:
    COPIES = 8

    def __init__(self, at, rings, send, recv, here, base=0, through=None):
        self.send, self.recv, self.here, self.base = send, recv, here, base
        self.through = through
        self.own = [(own, slot(0)) for _, own, slot, _ in rings]
        self.plan = []
        for axis, own, slot, _ in rings:
            self.plan.append((own, slot(0), at.along(axis, 1)))
            self.plan.append((own, slot(0), at.along(axis, 3)))
        for axis, _, slot, half in rings:
            low, high = (slot(3).at[pl.ds(0, half)], slot(1).at[pl.ds(half, half)])
            self.plan.append((low, low, at.along(axis, 1)))
            self.plan.append((high, high, at.along(axis, 3)))

    def copy(self, i):
        src, dst, device = self.plan[i]
        return remote(src, dst, self.send, self.recv, self.base + i, device)

    def loaded(self, i):
        return pltpu.make_async_copy(self.own[i][0], self.through.at[i], self.here.at[i])

    def kept(self, i):
        src, dst = self.own[i]
        src = src if self.through is None else self.through.at[i]
        return pltpu.make_async_copy(src, dst, self.here.at[2 + i])

    def begin(self):
        for i in range(4):
            self.copy(i).start()
        for i in range(2):
            (self.kept(i) if self.through is None else self.loaded(i)).start()

    def forward(self):
        for i in range(4):
            self.copy(i).wait_recv()
            self.copy(4 + i).start()
        if self.through is not None:
            for i in range(2):
                self.loaded(i).wait()
                self.kept(i).start()

    def finish(self):
        for i in range(4, 8):
            self.copy(i).wait_recv()
        for i in range(8):
            self.copy(i).wait_send()
        for i in range(2):
            self.kept(i).wait()


def ring_slots(out, place):
    return lambda k: out.at[lax.rem(place + k, 4)]


def first_gather(at, own_a, own_b, over_z, over_x, *sems):
    rings = (
        ("z", own_a, ring_slots(over_z, at.z), 1), ("x", own_b, ring_slots(over_x, at.x), 1),
    )
    return SpreadOut(at, rings, *sems)


def second_gather(at, number, over_z, over_x, quad_a, quad_b, *sems):
    rings = (
        ("x", over_z.at[:, :, number], ring_slots(quad_a, at.x), 2),
        ("z", over_x.at[:, :, number], ring_slots(quad_b, at.z), 2),
    )
    return SpreadOut(at, rings, *sems)


SHARE_SHAPE = jax.ShapeDtypeStruct((2, STEPS, 3, 2, 32, FF), BF)
BLOCK_SHAPE = (4, 2, 3, 2, 32, FF)
LINE_SHAPE = jax.ShapeDtypeStruct((4, 2, STEPS, 3, 2, 32, FF), BF)
QUAD_SHAPE = jax.ShapeDtypeStruct((4, 4, 2, 3, 2, 32, FF), BF)
GRADS_SHAPE = jax.ShapeDtypeStruct((4, 4, 2, STEPS, 3, 2, 32, FF), BF)
LAND_SHAPE = jax.ShapeDtypeStruct((2, 2, STEPS - 1, 3, 2, 32, FF), BF)
SUMS_SHAPE = jax.ShapeDtypeStruct((4, 2, STEPS, 3, 2, 32, FF), BF)


class RingSum:
    COPIES = 6

    def __init__(
        self, at, axis, part_of, scratch, send, recv, load, base=0, first=0, arrived=None
    ):
        half_a, half_b, up, down, to_up, to_down, own = scratch
        self.half_a, self.half_b, self.up, self.down = half_a, half_b, up, down
        self.to_up, self.to_down, self.own = to_up, to_down, own
        self.send, self.recv, self.base = send, recv, base
        size = half_a.shape[0]
        lo, hi = pl.ds(0, size), pl.ds(size, size)
        place = {"x": at.x, "z": at.z}[axis]
        here, above, across, below = (part_of(lax.rem(place + k, 4)) for k in range(4))
        upper, lower = at.along(axis, 1), at.along(axis, 3)
        self.plan = [
            (across.at[lo], half_a, upper),
            (across.at[hi], half_b, lower),
            (above.at[hi], up.at[hi], upper),
            (below.at[lo], down.at[lo], lower),
            (to_up, up.at[lo], upper),
            (to_down, down.at[hi], lower),
        ]
        pieces = [(above.at[lo], to_up), (below.at[hi], to_down), (here, own)]
        self.arrived = arrived is not None
        if self.arrived:
            done, last = pl.ds(0, STEPS - 1), pl.ds(STEPS - 1, 1)
            for i, here_from in enumerate(arrived):
                src, dst, device = self.plan[i]
                pieces.append((here_from, dst.at[:, :, done]))
                self.plan[i] = (src.at[:, :, last], dst.at[:, :, last], device)
        self.loads = [
            pltpu.make_async_copy(src, dst, load.at[first + i])
            for i, (src, dst) in enumerate(pieces)
        ]

    def copy(self, i):
        src, dst, device = self.plan[i]
        return remote(src, dst, self.send, self.recv, self.base + i, device)

    def begin(self):
        for i in range(2):
            self.copy(i).start()
        for load in self.loads:
            load.start()

    def direct(self):
        for i in (2, 3):
            self.copy(i).start()

    def landed(self, i):
        if self.arrived and i < 4:
            self.loads[3 + i].wait()
        self.copy(i).wait_recv()

    def middle(self):
        for i, (total, landed) in enumerate(
            ((self.to_up, self.half_a), (self.to_down, self.half_b))
        ):
            self.loads[i].wait()
            self.landed(i)

            def add(i, carry, total=total, landed=landed):
                total[i] = (total[i].astype(F32) + landed[i].astype(F32)).astype(BF)
                return carry

            lax.fori_loop(0, total.shape[0], add, 0)
            self.copy(4 + i).start()

    def finish(self, out):
        self.loads[2].wait()
        for i in range(2, 6):
            self.landed(i)

        def add(i, carry):
            total = self.own[i].astype(F32) + self.up[i].astype(F32)
            out[i] = (total + self.down[i].astype(F32)).astype(out.dtype)
            return carry

        lax.fori_loop(0, out.shape[0], add, 0)
        for i in range(6):
            self.copy(i).wait_send()


def sum_scratch(block):
    half, whole = pltpu.VMEM((block[0] // 2, *block[1:]), BF), pltpu.VMEM(block, BF)
    return [half, half, whole, whole, half, half, whole]


def startup_kernel(
    hidden, segment_rows, query, key, value, output, router, gains, gate, up, down,
    hidden_all, segment_all, small_all, share_a, share_b, small, segment, send, recv, here,
):
    at = Place()
    greet(
        [
            at.sibling(), at.partner(), at.diagonal(), at.opposite(),
            at.along("x", 1), at.along("x", 3), at.along("z", 1), at.along("z", 3),
        ]
    )
    small[:, 0:256] = query[...]
    small[:, 256:384] = key[...]
    small[:, 384:512] = value[...]
    small[:, 512:768] = output[...]
    columns = jnp.broadcast_to(gains[...].astype(F32)[:, None, :], (2, 8, 32))
    columns = [columns[i].T[:, 0:1].astype(BF) for i in range(2)]
    blank = jnp.zeros((32, 94), BF)
    small[:, 768:896] = jnp.concatenate([router[...], *columns, blank], axis=1)
    segment[0:2, :] = segment_rows[...]
    segment[2:8, :] = jnp.zeros((6, 128), jnp.int32)
    rank = at.yl * 2 + at.core
    mine = small_all.at[(at.x * 4 + at.z) * 2 + at.yh]
    small_kept = keep(small, mine, here.at[0])
    copies = [push(small, mine, send, recv, 0, at.opposite())]
    swaps, swaps_kept = [], []
    base = 13 + 2 * PIECES
    for i, share in enumerate((gate, up, down)):
        for j, out in enumerate((share_a, share_b)):
            dst, two = out.at[at.yh, :, i], pl.ds(2 * j, 2)
            theirs = share.at[pl.ds((1 - at.yh) * STEPS, STEPS), two]
            index = 2 * i + j
            swaps.append(push(theirs, dst, send, recv, base + index, at.opposite()))
            own = share.at[pl.ds(at.yh * STEPS, STEPS), two]
            swaps_kept.append(keep(own, dst, here.at[3 + index]))
    copies.extend(
        push(segment, segment_all.at[rank], send, recv, 1 + i, device)
        for i, device in enumerate((at.sibling(), at.partner(), at.diagonal()))
    )
    pair = PairGather(at, hidden, hidden_all, send, recv, here.at[1], 12, PIECES)
    seg_here = keep(segment, segment_all.at[rank], here.at[2])
    over_z = AxisGather(
        at, "z",
        lambda k, part: halves_of(small_all, (at.x * 4 + lax.rem(at.z + k, 4)) * 2, 2)(part),
        send, recv, 4,
    )
    over_x = AxisGather(
        at, "x", lambda k, part: halves_of(small_all, lax.rem(at.x + k, 4) * 8, 8)(part),
        send, recv, 8,
    )
    small_kept.wait()
    copies[0].wait_recv()
    over_z.begin()
    over_z.forward()
    over_z.finish()
    over_x.begin()
    pair.forward()
    over_x.forward()
    pair.finish()
    seg_here.wait()
    for copy in copies[1:]:
        copy.wait_recv()
    for swap, own in zip(swaps, swaps_kept):
        swap.wait_recv()
        own.wait()
    over_x.finish()
    for copy in (*copies, *swaps):
        copy.wait_send()


def startup(hidden, segment, smalls, shares, ident):
    hbm = pl.BlockSpec(memory_space=pl.ANY)
    vmem = pl.BlockSpec(memory_space=pltpu.VMEM)
    sems = 13 + 2 * PIECES + 6
    shares = [share.reshape(2 * STEPS, QUAD, 32, FF) for share in shares]
    hidden_all, segment_all, small_all, share_a, share_b = pl.pallas_call(
        startup_kernel,
        in_specs=[vmem] * 8 + [hbm] * 3,
        out_specs=[hbm] * 3 + [vmem] * 2,
        out_shape=[
            jax.ShapeDtypeStruct((4, *hidden.shape), hidden.dtype),
            jax.ShapeDtypeStruct((4, 8, 128), segment.dtype),
            jax.ShapeDtypeStruct((32, 32, SMALL), BF),
            SHARE_SHAPE,
            SHARE_SHAPE,
        ],
        scratch_shapes=[
            pltpu.VMEM((32, SMALL), BF),
            pltpu.VMEM((8, 128), jnp.int32),
            pltpu.SemaphoreType.DMA((sems,)),
            pltpu.SemaphoreType.DMA((sems,)),
            pltpu.SemaphoreType.DMA((9,)),
        ],
        compiler_params=pltpu.CompilerParams(collective_id=ident, has_side_effects=True),
        name="startup",
    )(hidden, segment, *smalls, *shares)
    hidden_all, small_all = hidden_all.reshape(SEQ, D), small_all.reshape(D, SMALL)
    return hidden_all, segment_all, small_all, share_a, share_b


SPLIT = 384


class RingScatter:
    def __init__(self, at, part, scratch, send, recv, base=0):
        self.at, self.part, self.send, self.recv, self.base = at, part, send, recv, base
        near, half_a, half_b, self.full_up, self.full_down = scratch[:5]
        to_far, to_up, to_down = scratch[5:] or [
            part.at[at.chip(k) * 2 + at.core] for k in (2, 1, 3)
        ]
        self.near, self.half_a, self.half_b = near, half_a, half_b
        self.to_far, self.to_up, self.to_down = to_far, to_up, to_down
        self.half = half_a.shape[0]
        self.lo, self.hi = pl.ds(0, self.half), pl.ds(self.half, self.half)
        up, down = at.ring(1), at.ring(3)
        self.plan = {
            k: (part.at[at.chip(k) * 2 + 1 - at.core], near.at[k], at.sibling()) for k in range(4)
        }
        self.plan[4] = (to_far.at[self.lo], half_a, up)
        self.plan[5] = (to_far.at[self.hi], half_b, down)
        self.plan[6] = (to_up, self.full_up, up)
        self.plan[7] = (to_down, self.full_down, down)

    def copy(self, i):
        src, dst, device = self.plan[i]
        return remote(src, dst, self.send, self.recv, self.base + i, device)

    def chip_sum(self, k):
        self.copy(k).wait_recv()
        own = self.part[self.at.chip(k) * 2 + self.at.core]
        return own.astype(F32) + self.near[k].astype(F32)

    def far(self):
        self.to_far[...] = self.chip_sum(2).astype(BF)
        self.copy(4).start()
        self.copy(5).start()

    def up_side(self):
        total = self.chip_sum(1)
        self.copy(4).wait_recv()
        self.to_up[self.lo, :] = (total[: self.half] + self.half_a[...].astype(F32)).astype(BF)
        self.to_up[self.hi, :] = total[self.half :].astype(BF)
        self.copy(6).start()

    def down_side(self):
        total = self.chip_sum(3)
        self.copy(5).wait_recv()
        self.to_down[self.lo, :] = total[: self.half].astype(BF)
        self.to_down[self.hi, :] = (total[self.half :] + self.half_b[...].astype(F32)).astype(BF)
        self.copy(7).start()

    def finish(self, out):
        out[...] = self.chip_sum(0)
        self.copy(6).wait_recv()
        out[...] += self.full_up[...].astype(F32)
        self.copy(7).wait_recv()
        out[...] += self.full_down[...].astype(F32)
        for i in range(8):
            self.copy(i).wait_send()


def ring_scratch(rows, columns, own_sends=True):
    block, half = pltpu.VMEM((rows, columns), BF), pltpu.VMEM((rows // 2, columns), BF)
    scratch = [pltpu.VMEM((4, rows, columns), BF), half, half, block, block]
    return scratch + [block] * 3 if own_sends else scratch


class PairScatter:
    def __init__(self, at, part, scratch, send, recv, base=0):
        self.at, self.part, self.send, self.recv, self.base = at, part, send, recv, base
        self.near, self.far_rows, self.to_far = scratch
        size = self.to_far.shape[0] // PIECES
        self.parts = [pl.ds(i * size, size) for i in range(PIECES)]
        self.other, self.own = (1 - at.yl) * 2, at.yl * 2

    def go(self, i, src, dst, device):
        return push(src, dst, self.send, self.recv, self.base + i, device)

    def begin_far(self):
        slot = self.other + 1 - self.at.core
        self.first = [
            self.go(i, self.part.at[slot, rows], self.near.at[1, rows], self.at.sibling())
            for i, rows in enumerate(self.parts)
        ]

    def begin_own(self):
        slot = self.own + 1 - self.at.core
        self.second = self.go(PIECES, self.part.at[slot], self.near.at[0], self.at.sibling())

    def forward(self):
        self.sent = []
        for i, rows in enumerate(self.parts):
            self.first[i].wait_recv()
            own = self.part[self.other + self.at.core, rows, :].astype(F32)
            self.to_far[rows, :] = (own + self.near[1, rows, :].astype(F32)).astype(BF)
            far = self.far_rows.at[rows]
            self.sent.append(self.go(PIECES + 1 + i, self.to_far.at[rows], far, self.at.partner()))

    def finish(self, out):
        self.second.wait_recv()
        out[...] = self.part[self.own + self.at.core].astype(F32) + self.near[0].astype(F32)
        for i, rows in enumerate(self.parts):
            self.sent[i].wait_recv()
            out[rows, :] += self.far_rows[rows, :].astype(F32)
        for copy in (*self.first, self.second, *self.sent):
            copy.wait_send()


def pair_scratch(rows, columns):
    block = pltpu.VMEM((rows, columns), BF)
    return [pltpu.VMEM((2, rows, columns), BF), block, block]


SPLIT = 384


def rotary_tables():
    half = HD // 2
    inverse = (10000.0 ** (-(np.arange(half, dtype=np.float64) * 2.0) / HD)).astype(np.float32)
    angles = np.arange(SEQ, dtype=np.float32)[:, None] * inverse[None, :]
    cosine, sine = np.cos(angles), np.sin(angles)
    wide_cosine = np.concatenate([cosine] * 4, axis=1)
    wide_sine = np.concatenate([-sine, sine] * 2, axis=1)
    return wide_cosine.astype(np.float32), wide_sine.astype(np.float32)


def swapped(values):
    lane = lax.broadcasted_iota(jnp.int32, values.shape, 1)
    low = (lane % HD) < HD // 2
    return jnp.where(low, pltpu.roll(values, 96, 1), pltpu.roll(values, 32, 1))


def rotated(values, cosine, sine):
    return values * cosine + swapped(values) * sine


def bias_block(key_segment, query_segment, first, rows):
    key_at = lax.broadcasted_iota(jnp.int32, (rows, BLOCK), 0)
    query_at = lax.broadcasted_iota(jnp.int32, (rows, BLOCK), 1) + first
    allowed = (key_segment == query_segment) & (key_at <= query_at)
    return jnp.where(allowed, 0.0, MASKED)


def segment_row(segments):
    return jnp.concatenate(
        [segments[rank, i : i + 1, :] for rank in range(4) for i in range(2)], axis=1
    ).astype(F32)


def gain_rows(small):
    return small[:, 768:896].astype(F32).T[32:40, :]


def column_of(row):
    return jnp.broadcast_to(row, (8, row.shape[1])).T[:, 0:1]


def front_kernel(
    hidden, weights, cosine, sine, segments, own_hidden, ids, out_grad, share_a, share_b,
    normed, query, key, value, context_t, log_total, middle, normed_moe, gating,
    over_z, over_x, quad_a, quad_b, out_grad_all, bias, part, context, through, *refs,
):
    pair_refs = refs[:3]
    send, recv, here = refs[3:]
    at = Place()
    greet(
        [
            at.sibling(), at.partner(), at.ring(1), at.ring(3),
            at.along("x", 1), at.along("x", 3), at.along("z", 1), at.along("z", 3),
        ]
    )
    ring = RingGather(at, out_grad, out_grad_all, send, recv, here.at[0], 0)
    lines = first_gather(
        at, share_a, share_b, over_z, over_x, send, recv, here.at[pl.ds(1, 4)], 9
    )
    quad = second_gather(
        at, 0, over_z, over_x, quad_a, quad_b, send, recv, here.at[pl.ds(5, 4)],
        9 + SpreadOut.COPIES, through,
    )
    scatter = PairScatter(at, part, pair_refs, send, recv, 9 + 2 * SpreadOut.COPIES)
    lines.begin()
    ring.begin()

    gains = gain_rows(weights)
    seg_row = segment_row(segments)
    seg_column = column_of(seg_row)
    for block in range(SEQ // BLOCK):
        rows = slice(block * BLOCK, (block + 1) * BLOCK)
        values = hidden[rows, :].astype(F32)
        scale = lax.rsqrt(jnp.mean(values * values, axis=-1, keepdims=True) + EPS)
        normed[rows, :] = (values * scale * gains[0:1, :]).astype(BF)
    for half in range(2):
        columns = slice(half * 128, half * 128 + 128)
        pre = mm(normed[...], weights[:, columns])
        query[:, columns] = (rotated(pre, cosine[...], sine[...]) * 0.125).astype(BF)
    key_pre = mm(normed[...], weights[:, 256:384])
    key[...] = rotated(key_pre, cosine[...], sine[...]).astype(BF)
    value_pre = mm(normed[...], weights[:, 384:512])
    value[...] = value_pre.astype(BF)
    value_t = value_pre.T.astype(BF)
    lines.forward()
    for block in range(SEQ // BLOCK):
        first, end = block * BLOCK, (block + 1) * BLOCK
        bias[:end, :] = bias_block(seg_column[:end, :], seg_row[:, first:end], first, end)
        for head in range(HEADS):
            kv = slice((head // 2) * HD, (head // 2) * HD + HD)
            own = slice(head * HD, head * HD + HD)
            scores = mm_last(key[:end, kv], query[first:end, own]) + bias[:end, :]
            top = jnp.max(scores, axis=0, keepdims=True)
            powers = jnp.exp(scores - top)
            total = jnp.sum(powers, axis=0, keepdims=True)
            share = (powers * (1.0 / total)).astype(BF)
            context_t[own, first:end] = mm(value_t[kv, :end], share).astype(BF)
            log_total[head : head + 1, first:end] = top + jnp.log(total)
        if block == 2:
            ring.forward_before()
            ring.forward_behind()
    lines.finish()
    quad.begin()
    context[...] = context_t[...].T

    def project(slot):
        rows = pl.ds(pl.multiple_of(slot * LOCAL, LOCAL), LOCAL)
        part[slot] = mm_last(context[rows, :], weights[:, 512:768]).astype(BF)

    project(scatter.other + 1 - at.core)
    scatter.begin_far()
    project(scatter.other + at.core)
    project(scatter.own + 1 - at.core)
    scatter.begin_own()
    project(scatter.own + at.core)
    scatter.forward()
    quad.forward()
    ring.forward_across()
    scatter.finish(middle)
    values = middle[...] + own_hidden[...].astype(F32)
    middle[...] = values
    scale = lax.rsqrt(jnp.mean(values * values, axis=-1, keepdims=True) + EPS)
    normed_moe[...] = (values * scale * gains[1:2, :]).astype(BF)
    lane = lax.broadcasted_iota(jnp.int32, (LOCAL, 128), 1)
    chosen = lane == ids[:, 0:1]
    for i in range(1, TOPK):
        chosen = chosen | (lane == ids[:, i : i + 1])
    logits = jnp.where(chosen, mm(normed_moe[...], weights[:, 768:896]), MASKED)
    powers = jnp.where(chosen, jnp.exp(logits - jnp.max(logits, axis=-1, keepdims=True)), 0.0)
    gating[...] = powers / jnp.sum(powers, axis=-1, keepdims=True)
    for i in (0, 4, 6, 7, 8):
        ring.copy(i).wait_recv()
    ring.sent()
    ring.kept().wait()
    quad.finish()


def front(hidden, weights, tables, segments, own_hidden, ids, out_grad, shares, ident):
    vmem = pl.BlockSpec(memory_space=pltpu.VMEM)
    hbm = pl.BlockSpec(memory_space=pl.ANY)
    sems = 9 + 2 * SpreadOut.COPIES + 1 + 2 * PIECES
    return pl.pallas_call(
        front_kernel,
        in_specs=[vmem] * 10,
        out_specs=[vmem] * 9 + [hbm] * 5,
        out_shape=[
            jax.ShapeDtypeStruct((SEQ, D), BF),
            jax.ShapeDtypeStruct((SEQ, HEADS * HD), BF),
            jax.ShapeDtypeStruct((SEQ, 128), BF),
            jax.ShapeDtypeStruct((SEQ, 128), BF),
            jax.ShapeDtypeStruct((HEADS * HD, SEQ), BF),
            jax.ShapeDtypeStruct((8, SEQ), F32),
            jax.ShapeDtypeStruct((LOCAL, D), F32),
            jax.ShapeDtypeStruct((LOCAL, D), BF),
            jax.ShapeDtypeStruct((LOCAL, 128), F32),
            *[LINE_SHAPE] * 2,
            *[QUAD_SHAPE] * 2,
            jax.ShapeDtypeStruct((8, LOCAL, D), BF),
        ],
        scratch_shapes=[
            pltpu.VMEM((SEQ, BLOCK), F32),
            pltpu.VMEM((4, LOCAL, D), BF),
            pltpu.VMEM((SEQ, HEADS * HD), BF),
            pltpu.VMEM((2, *BLOCK_SHAPE), BF),
            *pair_scratch(LOCAL, D),
            pltpu.SemaphoreType.DMA((sems,)),
            pltpu.SemaphoreType.DMA((sems,)),
            pltpu.SemaphoreType.DMA((9,)),
        ],
        compiler_params=pltpu.CompilerParams(
            collective_id=ident, has_side_effects=True, vmem_limit_bytes=56 * MIB
        ),
        name="front",
    )(hidden, weights, *tables, segments, own_hidden, ids, out_grad, *shares)


def by_owner(value):
    return value.astype(BF).reshape(4, 4, 2, 32, value.shape[1])


def back_kernel(
    dx, dgate, gating, middle, normed_moe, out_grad, y_part,
    normed, weights, cosine, sine, segments, query, key, value, context_t, log_total,
    own_weights, own_hidden, expert_a, expert_b,
    land_0, land_1, land_2, land_3, land_4, land_5, land_6, land_7,
    hidden_grad, block_out, query_grad, key_grad, value_grad, output_grad, rest, gate, up, down,
    bias, dcontext, dquery_t, dkey, dvalue, dall, dall_t, dattn_own, dattn_all, y_sum,
    grads, sum_1a, sum_1b, sum_2a, sum_2b, over_y, from_opposite, share_sum, shares,
    total_a, total_b, land_a, land_b, *refs,
):
    ring_refs, pair_refs = refs[:8], refs[8:11]
    first_refs = (refs[11:18], refs[18:25])
    groups = [refs[25 + 7 * i : 32 + 7 * i] for i in range(4)]
    landings = (refs[53:57], refs[57:61])
    send, recv, here, load = refs[61:]
    at = Place()
    greet(
        [
            at.sibling(), at.partner(), at.diagonal(), at.opposite(), at.ring(1), at.ring(3),
            at.along("x", 1), at.along("x", 3), at.along("z", 1), at.along("z", 3),
        ]
    )
    base = 9 + 2 * PIECES
    sums = [
        RingSum(
            at, "x", lambda k: expert_a.at[k], first_refs[0], send, recv, load, base, 0,
            (land_0, land_1, land_2, land_3),
        ),
        RingSum(
            at, "z", lambda k: expert_b.at[k], first_refs[1], send, recv, load,
            base + RingSum.COPIES, 7, (land_4, land_5, land_6, land_7),
        ),
    ]
    for each in sums:
        each.begin()
        each.direct()
    gain = gain_rows(weights)[1:2, :]
    chosen = gating[...]
    dchosen = chosen * (dgate[...] - jnp.sum(chosen * dgate[...], axis=-1, keepdims=True))
    dlogits = dchosen.astype(BF)
    dnormed = dx[...] + mm_last(dlogits, weights[:, 768:896])
    values = middle[...]
    scale = lax.rsqrt(jnp.mean(values * values, axis=-1, keepdims=True) + EPS)
    unit = values * scale
    weighted = dnormed * gain
    inner = jnp.mean(weighted * unit, axis=-1, keepdims=True)
    total = out_grad[...].astype(F32) + scale * (weighted - unit * inner)
    hidden_grad[...] = total
    dattn_own[...] = total.astype(BF)
    gather = PairGather(at, dattn_own, dattn_all, send, recv, here, 8, PIECES)
    scatter = RingScatter(at, y_part, ring_refs, send, recv)
    for k in (2, 1, 3, 0):
        scatter.copy(k).start()
    router_part = mm(normed_moe[...].T, dlogits)
    gain_part = column_of(jnp.sum(dnormed * unit, axis=0, keepdims=True))
    lane = lax.broadcasted_iota(jnp.int32, (D, 128), 1)
    grads[..., 768:] = by_owner(jnp.where(lane == 32, gain_part, router_part))
    seg_row = segment_row(segments)
    seg_column = column_of(seg_row)
    gather.forward()
    scatter.far()
    for each in sums:
        each.middle()
    gather.finish()
    dattn = dattn_all[...].reshape(SEQ, D)
    dcontext[...] = mm(dattn, weights[:, 512:768]).astype(BF)
    output_grad_t = mm(context_t[...], dattn)
    grads[..., 512:768] = by_owner(output_grad_t.T)
    key_t = key[...].astype(F32).T.astype(BF)
    dkey[...] = jnp.zeros_like(dkey)
    dvalue[...] = jnp.zeros_like(dvalue)
    for block in range(SEQ // BLOCK):
        first, end = block * BLOCK, (block + 1) * BLOCK
        bias[:end, :] = bias_block(seg_column[:end, :], seg_row[:, first:end], first, end)
        for head in range(HEADS):
            kv = slice((head // 2) * HD, (head // 2) * HD + HD)
            own = slice(head * HD, head * HD + HD)
            query_block = query[first:end, own]
            dcontext_block = dcontext[first:end, own]
            scores = mm_last(key[:end, kv], query_block) + bias[:end, :]
            share = jnp.exp(scores - log_total[head : head + 1, first:end])
            dshare = mm_last(value[:end, kv], dcontext_block)
            centre = jnp.sum(share * dshare, axis=0, keepdims=True)
            dscore = (share * (dshare - centre)).astype(BF)
            dquery_t[own, first:end] = mm(key_t[kv, :end], dscore) * 0.125
            dkey[:end, kv] += mm(dscore, query_block)
            dvalue[:end, kv] += mm(share.astype(BF), dcontext_block)
        if block == 0:
            scatter.up_side()
            scatter.down_side()
        if block == 2:
            last = base + 6 * RingSum.COPIES + 1 + 2 * PIECES
            final_sums = []
            for i, (each, axis, refs_of, landing) in enumerate(
                zip(sums, ("z", "x"), first_refs, landings)
            ):
                each.finish(each.own)
                to_up, to_down, own = refs_of[4].at[0, pl.ds(0, 1)], refs_of[5].at[0, pl.ds(0, 1)], refs_of[2].at[0]
                final_sums.append(
                    RingSum(
                        at, axis, lambda k, own=each.own: own.at[k], (*landing, to_up, to_down, own),
                        send, recv, load, last + RingSum.COPIES * i, 26 + 3 * i,
                    )
                )
                final_sums[i].begin()
                final_sums[i].direct()
        if block == 3:
            for each in final_sums:
                each.middle()
    turn = -sine[...]
    for half in range(2):
        rows = slice(half * 128, half * 128 + 128)
        piece = rotated(dquery_t[rows, :].T, cosine[...], turn)
        dall[:, rows] = piece.astype(BF)
        dall_t[rows, :] = piece.T.astype(BF)
    piece = rotated(dkey[...], cosine[...], turn)
    dall[:, 256:384] = piece.astype(BF)
    dall_t[256:384, :] = piece.T.astype(BF)
    dall[:, 384:512] = dvalue[...].astype(BF)
    dall_t[384:512, :] = dvalue[...].T.astype(BF)
    grads[..., 0:512] = by_owner(mm(dall_t[...], normed[...]).T)
    after = base + 2 * RingSum.COPIES
    width = grads.shape[-1]
    a, b = pl.ds(0, SPLIT), pl.ds(SPLIT, width - SPLIT)

    def ring_sum(i, axis, part_of, scratch):
        return RingSum(
            at, axis, part_of, scratch, send, recv, load, after + RingSum.COPIES * i, 14 + 3 * i
        )

    first_a = ring_sum(0, "x", lambda k: grads.at[k, :, :, :, a], groups[0])
    first_b = ring_sum(1, "z", lambda k: grads.at[:, k, :, :, b], groups[1])
    second_a = ring_sum(2, "z", lambda k: sum_1a.at[k], groups[2])
    second_b = ring_sum(3, "x", lambda k: sum_1b.at[k], groups[3])
    for each in (first_a, first_b):
        each.begin()
        each.direct()
    after = after + 4 * RingSum.COPIES
    pair = PairScatter(at, dattn_all, pair_refs, send, recv, after)
    after = after + 1 + 2 * PIECES + 2 * RingSum.COPIES

    def project(slot):
        rows = pl.ds(pl.multiple_of(slot * LOCAL, LOCAL), LOCAL)
        dattn_all[slot] = mm_last(dall[rows, :], weights[:, 0:512]).astype(BF)

    project(pair.other + 1 - at.core)
    pair.begin_far()
    project(pair.other + at.core)
    project(pair.own + 1 - at.core)
    pair.begin_own()
    project(pair.own + at.core)
    pair.forward()
    first_a.middle()
    first_b.middle()
    lands = []
    for i, (each, out, land) in enumerate(
        zip(final_sums, (total_a, total_b), (land_a, land_b))
    ):
        each.finish(out)
        lands.append(push(out.at[1 - at.yh], land, send, recv, after + 1 + i, at.opposite()))
    scatter.finish(y_sum)
    block_out[...] = (y_sum[...] + middle[...]).astype(BF)

    first_a.finish(sum_1a)
    second_a.begin()
    second_a.direct()
    first_b.finish(sum_1b)
    second_b.begin()
    second_b.direct()
    second_a.middle()
    second_b.middle()
    second_a.finish(sum_2a)
    second_b.finish(sum_2b)
    over_y[:, a] = sum_2a[...].reshape(64, SPLIT)
    over_y[:, b] = sum_2b[...].reshape(64, width - SPLIT)
    theirs = pl.ds(pl.multiple_of((1 - at.yh) * 32, 32), 32)
    own = pl.ds(pl.multiple_of(at.yh * 32, 32), 32)
    swap = push(over_y.at[theirs], from_opposite, send, recv, after, at.opposite())
    dn1 = y_sum
    pair.finish(dn1)
    hidden = own_hidden[...].astype(F32)
    scale = lax.rsqrt(jnp.mean(hidden * hidden, axis=-1, keepdims=True) + EPS)
    unit = hidden * scale
    weighted = dn1[...] * gain_rows(weights)[0:1, :]
    inner = jnp.mean(weighted * unit, axis=-1, keepdims=True)
    hidden_grad[...] += scale * (weighted - unit * inner)
    swap.wait_recv()
    total = over_y[own, :].astype(F32) + from_opposite[...].astype(F32)
    query_grad[...] = total[:, :256]
    key_grad[...] = total[:, 256:384]
    value_grad[...] = total[:, 384:512]
    output_grad[...] = total[:, 512:768]
    gain_part = jnp.sum(total[:, :512] * own_weights[...].astype(F32), axis=1, keepdims=True)
    lane = lax.broadcasted_iota(jnp.int32, (32, 128), 1)
    share_sum[...] = jnp.where(lane == 33, gain_part, total[:, 768:])
    copies = [
        push(share_sum, shares.at[i], send, recv, after + 3 + i, device)
        for i, device in enumerate((at.sibling(), at.partner(), at.diagonal()))
    ]
    mine, theirs = pl.ds(at.yh * STEPS, STEPS), pl.ds((1 - at.yh) * STEPS, STEPS)
    for j, value in enumerate((total_a, total_b)):
        for i, out in enumerate((gate, up, down)):
            out[mine, 2 * j : 2 * j + 2] = value[at.yh, :, i].astype(F32)
    rest[...] = share_sum[...]
    for i, copy in enumerate(copies):
        copy.wait_recv()
        rest[...] += shares[i]
    for j, (copy, land) in enumerate(zip(lands, (land_a, land_b))):
        copy.wait_recv()
        for i, out in enumerate((gate, up, down)):
            out[theirs, 2 * j : 2 * j + 2] = land[:, i].astype(F32)
    for copy in (swap, *copies, *lands):
        copy.wait_send()


def back(
    dx, dgate, gating, middle, normed_moe, out_grad, y_part,
    normed, weights, tables, segments, kept, own_weights, own_hidden, expert_grads, ident,
):
    vmem = pl.BlockSpec(memory_space=pltpu.VMEM)
    hbm = pl.BlockSpec(memory_space=pl.ANY)
    sems = 2 * (9 + 2 * PIECES) + 8 * RingSum.COPIES + 6
    block = SUMS_SHAPE.shape[1:]
    half = (block[0] // 2, *block[1:])
    first_a, first_b = (4, 2, 32, SPLIT), (4, 2, 32, SMALL - SPLIT)
    landing = [pltpu.VMEM(half, BF)] * 2 + [pltpu.VMEM(block, BF)] * 2
    return pl.pallas_call(
        back_kernel,
        in_specs=[vmem] * 19 + [hbm] * 10,
        out_specs=[vmem] * 10,
        out_shape=[
            jax.ShapeDtypeStruct((LOCAL, D), F32),
            jax.ShapeDtypeStruct((LOCAL, D), BF),
            *[jax.ShapeDtypeStruct((32, columns), F32) for columns in (256, 128, 128, 256)],
            jax.ShapeDtypeStruct((32, 128), F32),
            *[jax.ShapeDtypeStruct((2 * STEPS, QUAD, 32, FF), F32)] * 3,
        ],
        scratch_shapes=[
            pltpu.VMEM((SEQ, BLOCK), F32),
            pltpu.VMEM((SEQ, HEADS * HD), BF),
            pltpu.VMEM((HEADS * HD, SEQ), F32),
            pltpu.VMEM((SEQ, 128), F32),
            pltpu.VMEM((SEQ, 128), F32),
            pltpu.VMEM((SEQ, 512), BF),
            pltpu.VMEM((512, SEQ), BF),
            pltpu.VMEM((LOCAL, D), BF),
            pltpu.VMEM((4, LOCAL, D), BF),
            pltpu.VMEM((LOCAL, D), F32),
            pltpu.VMEM((4, 4, 2, 32, SMALL), BF),
            pltpu.VMEM(first_a, BF),
            pltpu.VMEM(first_b, BF),
            pltpu.VMEM(first_a[1:], BF),
            pltpu.VMEM(first_b[1:], BF),
            pltpu.VMEM((64, SMALL), BF),
            pltpu.VMEM((32, SMALL), BF),
            pltpu.VMEM((32, 128), F32),
            pltpu.VMEM((3, 32, 128), F32),
            *[pltpu.VMEM(block, BF)] * 2,
            *[pltpu.VMEM(block[1:], BF)] * 2,
            *ring_scratch(LOCAL, D),
            *pair_scratch(LOCAL, D),
            *sum_scratch(SUMS_SHAPE.shape),
            *sum_scratch(SUMS_SHAPE.shape),
            *sum_scratch(first_a),
            *sum_scratch(first_b),
            *sum_scratch(first_a[1:]),
            *sum_scratch(first_b[1:]),
            *landing,
            *landing,
            pltpu.SemaphoreType.DMA((sems,)),
            pltpu.SemaphoreType.DMA((sems,)),
            pltpu.SemaphoreType.DMA,
            pltpu.SemaphoreType.DMA((32,)),
        ],
        compiler_params=pltpu.CompilerParams(
            collective_id=ident, has_side_effects=True, vmem_limit_bytes=63 * MIB
        ),
        name="back",
    )(
        dx, dgate, gating, middle, normed_moe, out_grad, y_part,
        normed, weights, *tables, segments, *kept, own_weights, own_hidden, *expert_grads,
    )


def experts_kernel(
    x_in, gate_in, d_in, over_z, over_x, quad_0a, quad_0b, y_out, dx_out, dgate_out,
    all_a, all_b, land_0, land_1, land_2, land_3, land_4, land_5, land_6, land_7,
    quad_1a, quad_1b, quad_2a, quad_2b, quad_3a, quad_3b,
    x, d, xt, dt, y, dx, gating, dgate, dgate_part, hidden, w, *refs,
):
    dx_scratch, dgate_scratch = refs[:5], refs[5:10]
    send, recv, here, load, store, fetch = refs[10:16]
    at = Place()
    step = pl.program_id(0)
    opening, closing = step == 0, step == STEPS - 1
    rows_at_once = 2 * LOCAL
    lane = lax.broadcasted_iota(jnp.int32, (LOCAL, 128), 1)
    own_first = at.yh * 16 + step * QUAD
    x_gather = RingGather(at, x_in, x, send, recv, here.at[0], 0)
    gate_gather = RingGather(at, gate_in, gating, send, recv, here.at[1], 9)
    gathers = (x_gather, gate_gather)
    scatters = (
        RingScatter(at, d, dx_scratch, send, recv, 18),
        RingScatter(at, dgate_part, dgate_scratch, send, recv, 26),
    )

    later = ((quad_1a, quad_1b), (quad_2a, quad_2b), (quad_3a, quad_3b))
    quads = [
        second_gather(
            at, 1 + i, over_z, over_x, *quad, *refs[16:18], refs[18].at[pl.ds(4 * i, 4)],
            SpreadOut.COPIES * i, refs[19],
        )
        for i, quad in enumerate(later)
    ]

    def ride(condition, what):
        for i, quad in enumerate(quads):

            @pl.when(condition & (step == i))
            def _():
                what(quad)

    grads_a, grads_b, ship_send, ship_recv, keep_sems = refs[20:]

    def shipments(number):
        lo, hi = pl.ds(0, 2), pl.ds(2, 2)
        plan = []
        for part, place, axis, lands in (
            (grads_a, at.x, "x", (land_0, land_1, land_2, land_3)),
            (grads_b, at.z, "z", (land_4, land_5, land_6, land_7)),
        ):
            above, across, below = (part.at[lax.rem(place + k, 4)] for k in (1, 2, 3))
            upper, lower = at.along(axis, 1), at.along(axis, 3)
            plan += [
                (across.at[lo], lands[0], upper), (across.at[hi], lands[1], lower),
                (above.at[hi], lands[2], upper), (below.at[lo], lands[3], lower),
            ]
        return [
            remote(src, land.at[:, :, number], ship_send, ship_recv, 8 * number + i, device)
            for i, (src, land, device) in enumerate(plan)
        ]

    def keeps(number):
        return [
            pltpu.make_async_copy(part, out.at[:, :, :, number], keep_sems.at[i])
            for i, (part, out) in enumerate(((grads_a, all_a), (grads_b, all_b)))
        ]

    def shipped(number):
        for copy in shipments(number):
            copy.wait_send()
        for copy in keeps(number):
            copy.wait()

    def begin_shipping():
        for copy in shipments(step - 1):
            copy.start()

    def fetches(quad_a, quad_b):
        copies = []
        for g in range(3):
            for i in range(QUAD):
                columns = pl.ds((g * QUAD + i) * FF, FF)
                if i < 2:
                    parts = [(quad_a.at[:, :, :, g, i], w.at[:, :, :, :, columns])]
                else:
                    parts = [
                        (quad_b.at[:, x_at, :, g, i - 2], w.at[x_at, :, :, :, columns])
                        for x_at in range(4)
                    ]
                for part in parts:
                    copies.append(pltpu.make_async_copy(*part, fetch.at[len(copies)]))
        return copies

    def d_load(chip):
        two = pl.ds(chip * 2, 2)
        return pltpu.make_async_copy(d_in.at[two], d.at[two], load.at[chip])

    def y_store(chip):
        two = pl.ds(chip * 2, 2)
        return pltpu.make_async_copy(x.at[two], y_out.at[two], store.at[chip])

    @pl.when(opening)
    def _():
        greet(
            [
                at.sibling(), at.ring(1), at.ring(3),
                at.along("x", 1), at.along("x", 3), at.along("z", 1), at.along("z", 3),
            ]
        )
        for gather in gathers:
            gather.begin()
        for copy in fetches(quad_0a, quad_0b):
            copy.start()
        for chip in range(4):
            d_load(chip).start()

    for copy in fetches(quad_0a, quad_0b):
        copy.wait()

    ride(step < STEPS, lambda quad: quad.begin())

    def arrive(turn):
        @pl.when(turn == 0)
        def _():
            for gather in gathers:
                gather.kept().wait()
                gather.copy(0).wait_recv()

        @pl.when(turn == 1)
        def _():
            for gather in gathers:
                gather.forward_before()
                gather.forward_behind()
            for gather in gathers:
                gather.copy(4).wait_recv()

        @pl.when(turn == 2)
        def _():
            for gather in gathers:
                gather.forward_across()
            for gather in gathers:
                gather.copy(6).wait_recv()

        @pl.when(turn == 3)
        def _():
            for gather in gathers:
                gather.copy(7).wait_recv()
                gather.copy(8).wait_recv()

    def leave(turn):
        @pl.when(turn == 0)
        def _():
            for scatter in scatters:
                scatter.copy(2).start()

        @pl.when(turn == 1)
        def _():
            for scatter in scatters:
                scatter.copy(1).start()
                scatter.far()

        @pl.when(turn == 2)
        def _():
            for scatter in scatters:
                scatter.copy(3).start()
                scatter.up_side()

        @pl.when(turn == 3)
        def _():
            for scatter in scatters:
                scatter.copy(0).start()
                scatter.down_side()

    def tokens_block(turn, carry):
        inward = jnp.where(turn == 0, 0, jnp.where(turn == 1, 3, turn - 1))
        outward = jnp.where(turn == 0, 2, jnp.where(turn == 3, 0, turn * 2 - 1))
        chip = at.chip(jnp.where(closing, outward, inward))
        two = pl.ds(chip * 2, 2)
        rows = pl.ds(pl.multiple_of(chip * rows_at_once, rows_at_once), rows_at_once)

        @pl.when(opening)
        def _():
            arrive(turn)
            d_load(chip).wait()
            xt[:, rows] = x[two].reshape(rows_at_once, D).T
            dt[:, rows] = d[two].reshape(rows_at_once, D).T
            y[rows, :] = jnp.zeros((rows_at_once, D), F32)
            dx[rows, :] = jnp.zeros((rows_at_once, D), F32)
            dgate[rows, :] = jnp.zeros((rows_at_once, 128), F32)

        ride(turn == 3, lambda quad: quad.forward())
        pl.when((turn == 1) & (step > 0))(begin_shipping)
        gate_up = w[:, :, :, :, 0 : 2 * F].reshape(D, 2 * F)
        down = w[:, :, :, :, 2 * F :].reshape(D, F)
        for core in range(2):
            slot = chip * 2 + core
            part = pl.ds(pl.multiple_of(slot * LOCAL, LOCAL), LOCAL)
            both = mm(x[slot], gate_up)
            gate, up = both[:, :F], both[:, F:]
            dact = mm(d[slot], down)
            turned = pltpu.roll(gating[slot], lax.rem(128 - own_first, 128), 1)
            factor = jnp.concatenate(
                [jnp.broadcast_to(turned[:, i : i + 1], (LOCAL, FF)) for i in range(QUAD)],
                axis=1,
            )
            q = 1.0 / (1.0 + jnp.exp(-gate))
            silu = gate * q
            act = silu * up
            product = act * dact
            sums = dgate[part, :]
            for i in range(QUAD):
                own = jnp.sum(product[:, i * FF : (i + 1) * FF], axis=1, keepdims=True)
                sums = jnp.where(lane == own_first + i, own, sums)
            dgate[part, :] = sums
            dact = dact * factor
            hidden[part, 0:F] = (dact * up * (q + silu * (1.0 - q))).astype(BF)
            hidden[part, F : 2 * F] = (dact * silu).astype(BF)
            hidden[part, 2 * F :] = (act * factor).astype(BF)
        y[rows, :] += mm_last(hidden[rows, 2 * F :], down)
        dx[rows, :] += mm_last(hidden[rows, 0 : 2 * F], gate_up)

        @pl.when(closing)
        def _():
            x[two] = y[rows, :].astype(BF).reshape(2, LOCAL, D)
            d[two] = dx[rows, :].astype(BF).reshape(2, LOCAL, D)
            dgate_part[two] = dgate[rows, :].astype(BF).reshape(2, LOCAL, 128)
            y_store(chip).start()
            leave(turn)

        return carry

    lax.fori_loop(0, 4, tokens_block, 0)

    @pl.when(opening)
    def _():
        for gather in gathers:
            gather.sent()

    @pl.when(step > 0)
    def _():
        shipped(step - 1)

    def grads_block(block, carry):
        rows = pl.ds(pl.multiple_of(block * 512, 512), 512)

        def put(g, value):
            value = value.astype(BF).reshape(2, 4, 2, 32, value.shape[1])
            for j in range(value.shape[-1] // FF):
                piece = value[..., j * FF : (j + 1) * FF]
                group, i = g + j // QUAD, j % QUAD
                for x_at in range(2):
                    if i < 2:
                        grads_a[block * 2 + x_at, :, :, group, i] = piece[x_at]
                    else:
                        grads_b[:, block * 2 + x_at, :, group, i - 2] = piece[x_at]

        ride(block == 1, lambda quad: quad.finish())
        for number, quad in enumerate(later):

            @pl.when((block == 1) & (step == number))
            def _():
                for copy in fetches(*quad):
                    copy.start()

        put(0, mm(xt[rows, :], hidden[:, 0 : 2 * F]))
        put(2, mm(dt[rows, :], hidden[:, 2 * F :]))
        return carry

    lax.fori_loop(0, D // 512, grads_block, 0)
    for copy in keeps(step):
        copy.start()

    @pl.when(closing)
    def _():
        scatters[0].finish(dx_out)
        scatters[1].finish(dgate_out)
        for chip in range(4):
            y_store(chip).wait()
        for copy in keeps(step):
            copy.wait()
        for number in range(STEPS - 1):
            for copy in shipments(number):
                copy.wait_recv()


def experts(x, gating, d, lines, quad, ident):
    hbm = pl.BlockSpec(memory_space=pl.ANY)

    def whole(rows, columns):
        return pl.BlockSpec((rows, columns), lambda step: (0, 0), pipeline_mode=pl.Buffered(1))

    return pl.pallas_call(
        experts_kernel,
        grid=(STEPS,),
        in_specs=[hbm] * 7,
        out_specs=[
            hbm,
            whole(LOCAL, D),
            whole(LOCAL, 128),
            *[hbm] * 10,
            *[hbm] * 6,
        ],
        out_shape=[
            jax.ShapeDtypeStruct((8, LOCAL, D), BF),
            jax.ShapeDtypeStruct((LOCAL, D), F32),
            jax.ShapeDtypeStruct((LOCAL, 128), F32),
            *[GRADS_SHAPE] * 2,
            *[LAND_SHAPE] * 8,
            *[QUAD_SHAPE] * 6,
        ],
        scratch_shapes=[
            pltpu.VMEM((8, LOCAL, D), BF),
            pltpu.VMEM((8, LOCAL, D), BF),
            pltpu.VMEM((D, TOKENS), BF),
            pltpu.VMEM((D, TOKENS), BF),
            pltpu.VMEM((TOKENS, D), F32),
            pltpu.VMEM((TOKENS, D), F32),
            pltpu.VMEM((8, LOCAL, 128), F32),
            pltpu.VMEM((TOKENS, 128), F32),
            pltpu.VMEM((8, LOCAL, 128), BF),
            pltpu.VMEM((TOKENS, 3 * F), BF),
            pltpu.VMEM((4, 4, 2, 32, 3 * F), BF),
            *ring_scratch(LOCAL, D, False),
            *ring_scratch(LOCAL, 128, False),
            pltpu.SemaphoreType.DMA((34,)),
            pltpu.SemaphoreType.DMA((34,)),
            pltpu.SemaphoreType.DMA((2,)),
            pltpu.SemaphoreType.DMA((4,)),
            pltpu.SemaphoreType.DMA((4,)),
            pltpu.SemaphoreType.DMA((30,)),
            pltpu.SemaphoreType.DMA((3 * SpreadOut.COPIES,)),
            pltpu.SemaphoreType.DMA((3 * SpreadOut.COPIES,)),
            pltpu.SemaphoreType.DMA((12,)),
            pltpu.VMEM((2, *BLOCK_SHAPE), BF),
            *[pltpu.VMEM((4, 4, 2, 3, 2, 32, FF), BF)] * 2,
            pltpu.SemaphoreType.DMA((8 * STEPS - 8,)),
            pltpu.SemaphoreType.DMA((8 * STEPS - 8,)),
            pltpu.SemaphoreType.DMA((2,)),
        ],
        compiler_params=pltpu.CompilerParams(
            collective_id=ident, has_side_effects=True, vmem_limit_bytes=63 * MIB
        ),
        name="experts",
    )(x, gating, d, *lines, *quad)[:13]


def on_device(
    hidden_in, out_grad, attn_gain, query_weight, key_weight, value_weight, output_weight,
    moe_gain, router_weight, expert_gate, expert_up, expert_down, expert_ids, segment_ids,
):
    gains = jnp.stack([attn_gain, moe_gain])
    smalls = (query_weight, key_weight, value_weight, output_weight, router_weight, gains)
    own_shares = (expert_gate, expert_up, expert_down)
    hidden_all, segments, small, *shares = startup(
        hidden_in, segment_ids.reshape(2, 128), smalls, own_shares, 0
    )
    tables = tuple(jnp.asarray(t) for t in rotary_tables())
    normed, *more, d = front(
        hidden_all, small, tables, segments, hidden_in, expert_ids, out_grad, shares, 1
    )
    kept, (middle, normed_moe, gating), lines, quad = more[:5], more[5:8], more[8:10], more[10:]
    y, dx, dgate, *expert_grads = experts(normed_moe, gating, d, lines, quad, 3)
    own_weights = jnp.concatenate([query_weight, key_weight, value_weight], axis=1)
    hidden_grad, block_out, *attention_grads, rest, gate, up, down = back(
        dx, dgate, gating, middle, normed_moe, out_grad, y,
        normed, small, tables, segments, kept, own_weights, hidden_in, expert_grads, 5,
    )
    expert_grads = [share.reshape(E, 32, FF) for share in (gate, up, down)]
    return (
        block_out,
        hidden_grad,
        rest[:, 33] / attn_gain.astype(F32),
        *attention_grads,
        rest[:, 32],
        rest[:, :32],
        *expert_grads,
    )


def solution(mesh):
    fine = Mesh(np.asarray(mesh.devices).reshape(4, 4, 2, 2, 2), ALL)
    return jax.shard_map(
        on_device,
        mesh=fine,
        in_specs=(
            P(ALL, None),
            P(ALL, None),
            P(DP),
            P(DP, TENSOR),
            P(DP, TENSOR),
            P(DP, TENSOR),
            P(DP, TENSOR),
            P(DP),
            P(DP, None),
            P(None, DP, TENSOR),
            P(None, DP, TENSOR),
            P(None, DP, TENSOR),
            P(ALL, None),
            P(ALL),
        ),
        out_specs=(
            P(ALL, None),
            P(ALL, None),
            P(DP),
            P(DP, TENSOR),
            P(DP, TENSOR),
            P(DP, TENSOR),
            P(DP, TENSOR),
            P(DP),
            P(DP, None),
            P(None, DP, TENSOR),
            P(None, DP, TENSOR),
            P(None, DP, TENSOR),
        ),
        check_vma=False,
    )
```
